32 devices in a mesh: bucket: 8 (over z, core), tok: 4 (over y, x).
Axes of the slice: x: 2, y: 2, z: 4, core: 2. Of those that a mesh axis runs over, the one named last changes fastest.
Arguments:
- tokens: bfloat16 [16, 1024, 1152], P('bucket', 'tok'), may hold values from -6 to 6
- cotangent: bfloat16 [16, 1024, 1152], P('bucket', 'tok'), may hold values from -6 to 6
- timesteps: int32 [16], P('bucket'), may hold values from 0 to 999, as said below
- bucket_ids: int32 [8], P('bucket'), may hold values from 0 to 7
- head_masks: int32 [8, 16], replicated, may hold values 0 or 1
- channel_masks: int32 [8, 36], replicated, may hold values 0 or 1
- skip_rows: int32 [16, 256], P('bucket'), may hold values from 0 to 1023, as said below
- w_qkv: bfloat16 [1152, 3456], replicated, may hold values from -0.1875 to 0.1875
- q_bias: bfloat16 [1152], replicated, may hold values from -6 to 6
- v_bias: bfloat16 [1152], replicated, may hold values from -0.75 to 0.75
- w_proj: bfloat16 [1152, 1152], replicated, may hold values from -2 to 2
- proj_bias: bfloat16 [1152], replicated, may hold values from -4 to 4
- w_fc1: bfloat16 [1152, 4608], replicated, may hold values from -0.1875 to 0.1875
- fc1_bias: bfloat16 [4608], replicated, may hold values from -4 to 4
- w_fc2: bfloat16 [4608, 1152], replicated, may hold values from -0.1875 to 0.1875
- fc2_bias: bfloat16 [1152], replicated, may hold values from -4 to 4
- ada_weight: bfloat16 [1152, 6912], P(None, 'tok'), may hold values from -0.25 to 0.25
- ada_bias: bfloat16 [6912], P('tok'), may hold values from -4 to 4
Outputs:
- output: bfloat16 [16, 1024, 1152], P('bucket', 'tok')
- grad_tokens: float32 [16, 1024, 1152], P('bucket', 'tok')
- grad_w_qkv: float32 [1152, 3456], P('bucket', 'tok')
- grad_q_bias: float32 [1152], P(('bucket', 'tok'))
- grad_v_bias: float32 [1152], P(('bucket', 'tok'))
- grad_w_proj: float32 [1152, 1152], P('bucket', 'tok')
- grad_proj_bias: float32 [1152], P(('bucket', 'tok'))
- grad_w_fc1: float32 [1152, 4608], P('bucket', 'tok')
- grad_fc1_bias: float32 [4608], P(('bucket', 'tok'))
- grad_w_fc2: float32 [4608, 1152], P('bucket', 'tok')
- grad_fc2_bias: float32 [1152], P(('bucket', 'tok'))
- grad_ada_weight: float32 [1152, 6912], P('bucket', 'tok')
- grad_ada_bias: float32 [6912], P('bucket')
The draws below stay inside these ranges and needn't reach their ends.
Inputs may be any that keep to these rules, and one draw needn't show every extreme that they name: The timesteps of the items of group b lie from bucket_ids[b] * 125 to (bucket_ids[b] + 1) * 125 - 1. `skip_rows`: the entries of a row are distinct.
All inputs are finite; a program needn't handle non-finite values.
Results may differ from the reference program's by a relative error of at most 0.015.
The reference program's roundings to bfloat16 on the way count: a program that leaves them out, or rounds other values in their place, can miss the bound.
Values may be sent and summed in bfloat16 or wider, within the bound.
A program may use at most 320 MiB of HBM per device.

```python
import math
import jax
import jax.numpy as jnp
from jax import lax

D = 1152
HEADS = 16
FF = 4608
SEQ = 1024
ITEMS = 2
GROUP_W = 128
NBK = 8
STEP_SPAN = 125
SKIP = 256
ITEMS_ALL = 16
N_BUCKET = 8


def bucket_layout(key):
    bucket_draw = jax.random.randint(key, (N_BUCKET,), 0, NBK)
    last_group = jax.random.randint(jax.random.fold_in(key, 1), (), 0, N_BUCKET)
    first_group = (last_group + 1 + jax.random.randint(jax.random.fold_in(key, 2), (), 0, N_BUCKET - 1)) % N_BUCKET
    bucket_draw = bucket_draw.at[last_group].set(NBK - 1).at[first_group].set(0)
    return (bucket_draw, last_group, first_group)


def draw_bucket_ids(key, part):
    layout = bucket_layout(key)
    return layout[0].astype(jnp.int32)


def draw_timesteps(key, part):
    layout = bucket_layout(key)
    key = jax.random.fold_in(key, 23)
    offsets = jax.random.randint(key, (ITEMS_ALL,), 0, STEP_SPAN)
    offsets = offsets.at[layout[1] * ITEMS].set(STEP_SPAN - 1).at[layout[2] * ITEMS].set(0)
    group_index = jnp.arange(ITEMS_ALL) // ITEMS
    return (layout[0][group_index] * STEP_SPAN + offsets).astype(jnp.int32)


def move_to_slot(order, target, slot):
    located = jnp.argmax(order == target)
    present = order[slot]
    return order.at[located].set(present).at[slot].set(target)


def row_order(row_key):
    return jax.random.permutation(row_key, SEQ)


def draw_skip_rows(key, part):
    key = jax.random.fold_in(key, 37)
    row_keys = jax.random.split(key, ITEMS_ALL)
    orders = jax.vmap(row_order)(row_keys)
    chosen = jax.random.randint(jax.random.fold_in(key, 5), (), 0, ITEMS_ALL)
    special = move_to_slot(move_to_slot(orders[chosen], SEQ - 1, 0), 0, 1)
    orders = orders.at[chosen].set(special)
    return orders[:, :SKIP].astype(jnp.int32)


def touch_ends(drawn, own_key, least, top_value):
    longest = drawn.shape.index(max(drawn.shape))
    spots = []
    for shift in (0, 1):
        where = [jax.random.randint(jax.random.fold_in(own_key, axis), (), 0, length) for axis, length in enumerate(drawn.shape)]
        where[longest] = (where[longest] + shift) % drawn.shape[longest]
        spots.append(tuple(where))
    return drawn.at[spots[0]].set(least).at[spots[1]].set(top_value)


def block_scale(own_key, dims, cuts, low, largest):
    level, own = 1.0, jax.random.fold_in(own_key, 6)
    for position, parts in cuts:
        steps = jnp.exp(jax.random.uniform(jax.random.fold_in(own, position), (parts,), jnp.float32, low / len(cuts), largest / len(cuts)))
        level = level * jnp.repeat(steps, dims[position] // parts).reshape([-1 if axis == position else 1 for axis in range(len(dims))])
    return level


def normal_values(stream_key, shape, deviation, bound, pieces=(), kind=jnp.bfloat16):
    values = jax.random.normal(stream_key, shape, jnp.float32) * deviation
    if len(pieces) > 0:
        values = block_scale(stream_key, shape, pieces, -0.22, 0.18) * values
    return jnp.clip(values, min=-bound, max=bound).astype(kind)


def setup_inputs(seed: int = 0) -> dict:
    streams_of = jax.random.split(jax.random.key(seed), 19)
    return {
        "tokens": normal_values(streams_of[0], (ITEMS_ALL, SEQ, D), 1.0, 6.0, ((0, 8), (1, 4))),
        "cotangent": normal_values(streams_of[1], (ITEMS_ALL, SEQ, D), 1.0, 6.0, ((0, 8), (1, 4))),
        "timesteps": draw_timesteps(jax.random.fold_in(streams_of[18], 71), 0),
        "bucket_ids": draw_bucket_ids(jax.random.fold_in(streams_of[18], 71), 0),
        "head_masks": touch_ends((jax.random.randint(streams_of[4], (NBK, HEADS), 0, 4) < 3).astype(jnp.int32), jax.random.fold_in(streams_of[4], 1), 0, 1),
        "channel_masks": touch_ends((jax.random.randint(streams_of[5], (NBK, FF // GROUP_W), 0, 4) < 3).astype(jnp.int32), jax.random.fold_in(streams_of[5], 1), 0, 1),
        "skip_rows": draw_skip_rows(jax.random.fold_in(streams_of[18], 71), 0),
        "w_qkv": normal_values(streams_of[7], (D, 3 * D), D ** -0.5, 0.1875),
        "q_bias": normal_values(streams_of[8], (D,), 1.0, 6.0),
        "v_bias": normal_values(streams_of[9], (D,), 0.05, 0.75),
        "w_proj": normal_values(streams_of[10], (D, D), (D // 128) ** -0.5, 2.0),
        "proj_bias": normal_values(streams_of[11], (D,), 0.3, 4.0),
        "w_fc1": normal_values(streams_of[12], (D, FF), D ** -0.5, 0.1875),
        "fc1_bias": normal_values(streams_of[13], (FF,), 0.3, 4.0),
        "w_fc2": normal_values(streams_of[14], (FF, D), (FF // 4) ** -0.5, 0.1875),
        "fc2_bias": normal_values(streams_of[15], (D,), 0.3, 4.0),
        "ada_weight": normal_values(streams_of[16], (D, 6 * D), (D // 2) ** -0.5, 0.25, ((1, 4),)),
        "ada_bias": normal_values(streams_of[17], (6 * D,), 0.3, 4.0, ((0, 4),)),
    }


EPSILON = 1e-06
HIGHEST = lax.Precision.HIGHEST

@jax.custom_vjp
def low(v):
    return lax.optimization_barrier(v.astype(jnp.bfloat16)).astype(jnp.float32)

@jax.custom_vjp
def low_back(v):
    return v

def low_keep(v):
    return (low(v), None)

def low_pass(kept, grad):
    return (grad,)

def back_keep(v):
    return (v, None)

def back_low(kept, grad):
    return (low(grad),)
low.defvjp(low_keep, low_pass)
low_back.defvjp(back_keep, back_low)

def step_embedding(timesteps, model_width):
    half_width = model_width // 2
    frequency = jnp.exp(-math.log(10000.0) * jnp.arange(half_width, dtype=jnp.float32) / half_width)
    angles = timesteps.astype(jnp.float32)[:, None] * frequency[None, :]
    return jnp.concatenate([jnp.cos(angles), jnp.sin(angles)], axis=1)

def layer_norm(values):
    centred = values - lax.optimization_barrier(jnp.mean(values, axis=-1, keepdims=True))
    return centred * lax.rsqrt(lax.optimization_barrier(jnp.mean(centred * centred, axis=-1, keepdims=True)) + EPSILON)

def matmul(left, right):
    return jnp.dot(left, right, precision=HIGHEST)

def item_forward(params, inputs, modulation, head_on, channel_on, kept_rows):
    w_qkv, q_bias, v_bias, w_proj, proj_bias, w_fc1, fc1_bias, w_fc2, fc2_bias = params
    item_count, length, model_width = inputs.shape
    head_dim = model_width // HEADS
    score_scale = 1.0 / math.sqrt(head_dim)
    shift_a = modulation[:, 0, None, :]
    scale_a = modulation[:, 1, None, :]
    gate_a = modulation[:, 2, None, :]
    shift_m = modulation[:, 3, None, :]
    scale_m = modulation[:, 4, None, :]
    gate_m = modulation[:, 5, None, :]
    shifted = low(layer_norm(inputs) * (1.0 + scale_a) + shift_a)
    qkv_bias = jnp.concatenate([q_bias, jnp.zeros_like(q_bias), v_bias])
    projected = low_back(low(matmul(shifted, w_qkv) + qkv_bias))
    queries = projected[:, :, :model_width].reshape(item_count, length, HEADS, head_dim)
    key_rows = projected[:, :, model_width:2 * model_width].reshape(item_count, length, HEADS, head_dim)
    value_rows = projected[:, :, 2 * model_width:].reshape(item_count, length, HEADS, head_dim)
    scores = low_back(jnp.einsum('nqhe,nkhe->nhqk', queries, key_rows, precision=HIGHEST) * score_scale)
    top_score = lax.optimization_barrier(jnp.max(scores, axis=-1, keepdims=True))
    expanded = jnp.exp(scores - top_score)
    probs = expanded / lax.optimization_barrier(jnp.sum(expanded, axis=-1, keepdims=True))
    head_out = jnp.einsum('nhqk,nkhe->nqhe', low(probs), value_rows, precision=HIGHEST) * head_on[:, None]
    mixed = low_back(low(head_out.reshape(item_count, length, model_width)))
    attn = low_back(matmul(mixed, w_proj) + proj_bias)
    resid = inputs + gate_a * attn
    shifted2 = low(layer_norm(resid) * (1.0 + scale_m) + shift_m)
    pre = low_back(matmul(shifted2, w_fc1) + fc1_bias)
    hidden = low(jax.nn.gelu(pre, approximate=True) * channel_on)
    branch = low_back(matmul(hidden, w_fc2) + fc2_bias)
    return resid + kept_rows[:, :, None] * gate_m * branch

def reference(tokens, cotangent, timesteps, bucket_ids, head_masks, channel_masks, skip_rows, w_qkv, q_bias, v_bias, w_proj, proj_bias, w_fc1, fc1_bias, w_fc2, fc2_bias, ada_weight, ada_bias):
    item_total, length, model_width = tokens.shape
    condition = low(jax.nn.silu(step_embedding(timesteps, model_width)))
    head_on = jnp.repeat(head_masks[bucket_ids].astype(jnp.float32), ITEMS, axis=0)
    channel_on = jnp.repeat(jnp.repeat(channel_masks[bucket_ids].astype(jnp.float32), GROUP_W, axis=1), ITEMS, axis=0)
    positions = jnp.arange(length, dtype=jnp.int32)
    skipped = jnp.any(skip_rows[:, :, None] == positions[None, None, :], axis=1)
    kept_rows = (1.0 - skipped.astype(jnp.float32)).reshape(item_total, 1, length)
    inputs = tokens.astype(jnp.float32)
    params = (w_qkv.astype(jnp.float32), q_bias.astype(jnp.float32), v_bias.astype(jnp.float32), w_proj.astype(jnp.float32), proj_bias.astype(jnp.float32), w_fc1.astype(jnp.float32), fc1_bias.astype(jnp.float32), w_fc2.astype(jnp.float32), fc2_bias.astype(jnp.float32))
    ada_weight_f = ada_weight.astype(jnp.float32)
    ada_bias_f = ada_bias.astype(jnp.float32)

    def whole(inputs_all, weights, ada_w_all, ada_b_all):
        modulation = (matmul(condition, ada_w_all) + ada_b_all).reshape(item_total, 1, 6, model_width)

        def one_item(packed):
            inputs_item, modulation_item, head_item, channel_item, kept_item = packed
            return item_forward(weights, inputs_item, modulation_item, head_item, channel_item, kept_item)
        grouped = inputs_all.reshape(item_total, 1, length, model_width)
        return lax.map(jax.checkpoint(one_item), (grouped, modulation, head_on, channel_on, kept_rows))
    result, pull = jax.vjp(whole, inputs, params, ada_weight_f, ada_bias_f)
    grad_inputs, grad_params, grad_ada_w, grad_ada_b = pull(cotangent.astype(jnp.float32).reshape(result.shape))
    return (result.reshape(tokens.shape).astype(jnp.bfloat16), grad_inputs.reshape(tokens.shape), grad_params[0], grad_params[1], grad_params[2], grad_params[3], grad_params[4], grad_params[5], grad_params[6], grad_params[7], grad_params[8], grad_ada_w, grad_ada_b)
```

```python
import functools
import math

import jax
import jax.numpy as jnp
from jax import lax
from jax.experimental import pallas as pl
from jax.experimental.pallas import tpu as pltpu
from jax.sharding import PartitionSpec as P

HEADS = 16
EPSILON = 1e-06
LOG2E = 1.4426950408889634
GELU_K = math.sqrt(2.0 / math.pi)
GELU_C = 0.044715
LANES = 128
BOTH = ("bucket", "tok")
bf16, f32 = jnp.bfloat16, jnp.float32


def dot_nn(a, b):
    return lax.dot_general(a, b, (((1,), (0,)), ((), ())), preferred_element_type=f32)


def dot_nt(a, b):
    return lax.dot_general(a, b, (((1,), (1,)), ((), ())), preferred_element_type=f32)


def dot_tn(a, b):
    return lax.dot_general(a, b, (((0,), (0,)), ((), ())), preferred_element_type=f32)


def step_embedding(timesteps, model_width):
    half_width = model_width // 2
    frequency = jnp.exp(-math.log(10000.0) * jnp.arange(half_width, dtype=jnp.float32) / half_width)
    angles = timesteps.astype(jnp.float32)[:, None] * frequency[None, :]
    return jnp.concatenate([jnp.cos(angles), jnp.sin(angles)], axis=1)


def normalize(values):
    centred = values - jnp.mean(values, axis=-1, keepdims=True)
    inverse = lax.rsqrt(jnp.mean(centred * centred, axis=-1, keepdims=True) + EPSILON)
    return (centred * inverse, inverse)


def normalize_back(incoming, normed, inverse):
    return inverse * (
        incoming
        - jnp.mean(incoming, axis=-1, keepdims=True)
        - normed * jnp.mean(incoming * normed, axis=-1, keepdims=True)
    )


D = 1152
DC, DZ, TD = D // 8, D // 4, D // 4
HD = D // HEADS
HC = HEADS // 2
WC = D // 2
FF = 4608
NF = 3
FB = FF // 2 // NF
FZ = FB // 4
L = 1024
LH = L // 2
LB = L // 4
G1R = 3 * DC
G2R = 2 * FZ + FZ // 4
PR = 2 * DC + DC // 3
QR = 7 * DC + 16
QA = QR // 2 + 176
QB_ROWS = QR - QA
VMEM_LIMIT = 58 * 1024 * 1024


def call(kernel, name, out_shape, args, grid=None, in_specs=None, out_specs=None, scratch=(), grid_spec=None,
         flops=0, nbytes=0):
    whole = pl.BlockSpec(memory_space=pltpu.VMEM)
    kwargs = {}
    if grid_spec is not None:
        kwargs["grid_spec"] = grid_spec
    else:
        kwargs["in_specs"] = in_specs if in_specs is not None else [whole] * len(args)
        kwargs["out_specs"] = out_specs if out_specs is not None else jax.tree.map(lambda _: whole, out_shape)
        kwargs["scratch_shapes"] = list(scratch)
        if grid is not None:
            kwargs["grid"] = grid
    return pl.pallas_call(
        kernel,
        out_shape=out_shape,
        compiler_params=pltpu.CompilerParams(vmem_limit_bytes=VMEM_LIMIT),
        cost_estimate=pl.CostEstimate(flops=int(flops), bytes_accessed=int(nbytes), transcendentals=0),
        name=name,
        **kwargs,
    )(*args)


SMEM = pl.BlockSpec(memory_space=pltpu.SMEM)


def full(shape):
    return pl.BlockSpec(shape, lambda *_: (0,) * len(shape))


def rows(block, width):
    return pl.BlockSpec((block, width), lambda i: (i, 0))


def prow(block, width):
    return pl.BlockSpec((block, width), lambda i, s: (i, 0))


def prep_kernel(sc, wq, w1, wq_o, w1_o):
    for core in range(2):

        @pl.when(sc[1] == core)
        def _():
            for k in range(12):
                wq_o[:, DC * k : DC * (k + 1)] = wq[:, DZ * k + DC * core : DZ * k + DC * (core + 1)]
            for f in range(NF):
                for k in range(4):
                    start = 4 * DZ * k + FF // 8 * core + FZ * f
                    w1_o[f, :, FZ * k : FZ * (k + 1)] = w1[:, start : start + FZ]


def qkv_kernel(tok, mod, w, bias, shifted_o, qkv_o):
    normed, _ = normalize(tok[...].astype(f32))
    shifted = (normed * (1.0 + mod[1:2, :]) + mod[0:1, :]).astype(bf16)
    shifted_o[...] = shifted
    qkv_o[...] = (dot_nn(shifted, w[...]) + bias[...]).astype(bf16)


def attn_kernel(step, qkv, head_on, out, qs, ks, vs):
    scale = LOG2E / math.sqrt(HD)
    for h in range(HC):
        qs[...] = qkv[:, h * HD : (h + 1) * HD]
        ks[...] = qkv[:, WC + h * HD : WC + (h + 1) * HD]
        vs[...] = qkv[:, 2 * WC + h * HD : 2 * WC + (h + 1) * HD]
        on = head_on[h]

        def body(i, carry):
            part = pl.ds(pl.multiple_of(i * step, step), step)
            s = dot_nt(qs[part, :], ks[...])
            top = jnp.max(s, axis=1, keepdims=True)
            p = jnp.exp2((s - top) * scale)
            total = jnp.sum(p, axis=1, keepdims=True)
            o = dot_nn(p.astype(bf16), vs[...])
            out[part, h * HD : (h + 1) * HD] = (o * (on / total)).astype(bf16)
            return carry

        lax.fori_loop(0, L // step, body, 0)


def proj_kernel(mine, other, w_mine, w_other, bias, tok, mod, shifted2_o, attn_o):
    attn = (
        dot_nn(mine[...], w_mine[...].reshape(WC, D))
        + dot_nn(other[...], w_other[...].reshape(WC, D))
        + bias[...]
    )

    @pl.when(pl.program_id(0) < 2)
    def _():
        attn_o[...] = attn

    resid = tok[...].astype(f32) + mod[2:3, :] * attn
    normed, _ = normalize(resid)
    shifted2_o[...] = (normed * (1.0 + mod[4:5, :]) + mod[3:4, :]).astype(bf16)


def mlp_kernel(steps, sc, sh2, g, kept, mod, w1, b1, chan, w2,
               g1k, g1s, g2k, g2s, branch_o, ds2_o, sum1_o, sum2_o, acc1, acc2, t1, t2):
    i = pl.program_id(0)
    z, c, y, x = sc[0], sc[1], sc[2], sc[3]
    w1v = w1[0]
    w2v = w2[...].reshape(FB, D)
    db = (g[...].astype(f32) * mod[5:6, :] * kept[...]).astype(bf16)
    v = dot_nn(sh2[...], w1v) + b1[0]
    v2 = v * v
    th = jnp.tanh(GELU_K * v * (1.0 + GELU_C * v2))
    half = 0.5 * (1.0 + th)
    on = chan[0]
    hidden = (v * half * on).astype(bf16)
    slope = (half + (0.5 * GELU_K) * v * (1.0 - th * th) * (1.0 + (3.0 * GELU_C) * v2)) * on
    branch_o[...] = dot_nn(hidden, w2v).astype(bf16)
    d_pre = (dot_nt(db, w2v) * slope).astype(bf16)
    ds2_o[...] = dot_nt(d_pre, w1v).astype(bf16)
    p2 = dot_tn(hidden, db)
    p1 = dot_tn(sh2[...], d_pre)
    s1 = jnp.sum(d_pre.astype(f32), axis=0, keepdims=True)
    s2 = jnp.sum(db.astype(f32), axis=0, keepdims=True)

    @pl.when(i == 0)
    def _():
        acc1[...] = p1
        acc2[...] = p2
        sum1_o[...] = s1
        sum2_o[...] = s2

    @pl.when(i > 0)
    def _():
        acc1[...] += p1
        acc2[...] += p2
        sum1_o[...] += s1
        sum2_o[...] += s2

    @pl.when(i == steps - 1)
    def _():
        for t in range(4):
            t1[t] = acc1[:, FZ * t : FZ * (t + 1)].astype(bf16)
            t2[t] = acc2[:, TD * t : TD * (t + 1)].astype(bf16)
        for rz in range(4):
            zz = rz ^ z
            for ry in range(2):
                for rx in range(2):
                    tt = (ry ^ y) * 2 + (rx ^ x)
                    o1 = (g1k, g1s)[rx]
                    tails = []
                    for rc in range(2):
                        start = pl.multiple_of(zz * DZ + (rc ^ c) * DC, 16)
                        part = t1[tt, pl.ds(start, DC), :]
                        o1[ry, rz, rc * DC : (rc + 1) * DC, :] = part[:, :LANES]
                        tails.append(part[:, LANES:])
                    o1[ry, rz, 2 * DC : 3 * DC, :] = jnp.concatenate(tails, axis=1)
                    o2 = (g2k, g2s)[ry]
                    part = t2[tt, pl.ds(pl.multiple_of(zz * FZ, 16), FZ), :]
                    o2[rx, rz, :FZ, :] = part[:, :LANES]
                    o2[rx, rz, FZ : 2 * FZ, :] = part[:, LANES : 2 * LANES]
                    q = FZ // 4
                    o2[rx, rz, 2 * FZ :, :] = jnp.concatenate(
                        [part[q * k : q * (k + 1), 2 * LANES :] for k in range(4)], axis=1
                    )


def mid_kernel(ds_a, ds_b, ds_c, ds_r, br_a, br_b, br_c, br_r, attn, tok, g, kept, mod, bias2,
               d_resid_o, d_attn_o, out_o, sums_o):
    i = pl.program_id(0)
    tokf, gf, at = tok[...].astype(f32), g[...].astype(f32), attn[...]
    resid = tokf + mod[2:3, :] * at
    normed2, inverse2 = normalize(resid)
    ds2 = ds_a[...].astype(f32) + ds_b[...].astype(f32) + ds_c[...].astype(f32) + ds_r[...].astype(f32)
    branch = (
        br_a[...].astype(f32) + br_b[...].astype(f32) + br_c[...].astype(f32) + br_r[...].astype(f32) + bias2[...]
    )
    kb = kept[...] * branch
    out_o[...] = (resid + mod[5:6, :] * kb).astype(bf16)
    d_resid = gf + normalize_back(ds2 * (1.0 + mod[4:5, :]), normed2, inverse2)
    d_resid_o[...] = d_resid
    d_attn_o[...] = (mod[2:3, :] * d_resid).astype(bf16)
    parts = [at * d_resid, ds2, ds2 * normed2, kb * gf]
    sums = [jnp.sum(p, axis=0, keepdims=True) for p in parts]
    sums = jnp.concatenate(sums + [jnp.zeros((4, D), f32)], axis=0)

    @pl.when(i == 0)
    def _():
        sums_o[...] = sums

    @pl.when(i > 0)
    def _():
        sums_o[...] += sums


def heads_kernel(sc, da_mine, da_other, mixed, w, dh_o, pk, ps, sum_o, t1):
    z, c, y, x = sc[0], sc[1], sc[2], sc[3]
    wv = w[...].reshape(WC, D)
    dh_o[:LH, :] = dot_nt(da_mine[...], wv).astype(bf16)
    dh_o[LH:, :] = dot_nt(da_other[...], wv).astype(bf16)
    grad = dot_tn(mixed[:LH, :], da_mine[...]) + dot_tn(mixed[LH:, :], da_other[...])
    sum_o[...] = jnp.sum(da_mine[...].astype(f32), axis=0, keepdims=True) + jnp.sum(
        da_other[...].astype(f32), axis=0, keepdims=True
    )
    for t in range(4):
        t1[t] = grad[:, TD * t : TD * (t + 1)].astype(bf16)
    for rz in range(4):
        zz = rz ^ z
        for ry in range(2):
            for rx in range(2):
                tt = (ry ^ y) * 2 + (rx ^ x)
                o = (pk, ps)[ry]
                part = t1[tt, pl.ds(pl.multiple_of(zz * DC, 16), DC), :]
                o[rx, rz, :DC, :] = part[:, :LANES]
                o[rx, rz, DC : 2 * DC, :] = part[:, LANES : 2 * LANES]
                q = DC // 3
                tails = [part[q * k : q * (k + 1), 2 * LANES :] for k in range(3)]
                tails.append(jnp.zeros((q, 32), bf16))
                o[rx, rz, 2 * DC :, :] = jnp.concatenate(tails, axis=1)


def attn_back_kernel(step, qkv, dh, head_on, out, qs, ks, vs, dos, dq, dk, dv):
    scale = LOG2E / math.sqrt(HD)
    for h in range(HC):
        qs[...] = qkv[:, h * HD : (h + 1) * HD]
        ks[...] = qkv[:, WC + h * HD : WC + (h + 1) * HD]
        vs[...] = qkv[:, 2 * WC + h * HD : 2 * WC + (h + 1) * HD]
        dos[...] = (dh[:, h * HD : (h + 1) * HD].astype(f32) * head_on[h]).astype(bf16)
        dk[...] = jnp.zeros_like(dk)
        dv[...] = jnp.zeros_like(dv)

        def body(i, carry):
            part = pl.ds(pl.multiple_of(i * step, step), step)
            q, do = qs[part, :], dos[part, :]
            s = dot_nt(ks[...], q)
            top = jnp.max(s, axis=0, keepdims=True)
            p = jnp.exp2((s - top) * scale)
            p = p * (1.0 / jnp.sum(p, axis=0, keepdims=True))
            dp = dot_nt(vs[...], do)
            row_dot = jnp.sum(p * dp, axis=0, keepdims=True)
            ds = (p * (dp - row_dot)).astype(bf16)
            dv[...] += dot_nn(p.astype(bf16), do)
            dk[...] += dot_nn(ds, q)
            dq[part, :] = dot_tn(ds, ks[...])
            return carry

        lax.fori_loop(0, L // step, body, 0)
        out[:, h * HD : (h + 1) * HD] = (dq[...] * (1.0 / math.sqrt(HD))).astype(bf16)
        out[:, WC + h * HD : WC + (h + 1) * HD] = (dk[...] * (1.0 / math.sqrt(HD))).astype(bf16)
        out[:, 2 * WC + h * HD : 2 * WC + (h + 1) * HD] = dv[...].astype(bf16)


def qkv_grad_kernel(sc, shifted, dqkv, extra, ak, as_, bk, bs, t1):
    z, c, y, x = sc[0], sc[1], sc[2], sc[3]
    for k in range(4):
        grad = dot_tn(shifted[:, DZ * k : DZ * (k + 1)], dqkv[...])
        for t in range(4):
            t1[t, DZ * k : DZ * (k + 1), :] = grad[:, 3 * DC * t : 3 * DC * (t + 1)].astype(bf16)
    ones = jnp.ones((16, L), bf16)
    sums = dot_nn(ones, dqkv[...])[0:1, :]
    for zs in range(4):
        for ts in range(4):
            piece = DC * zs + DC // 4 * ts
            qsum = sums[:, piece : piece + DC // 4]
            vsum = sums[:, 2 * WC + piece : 2 * WC + piece + DC // 4]
            row1 = jnp.concatenate([jnp.zeros((1, 88), f32), qsum, jnp.zeros((1, 4), f32)], axis=1)
            row2 = jnp.concatenate([vsum, jnp.zeros((1, LANES - DC // 4), f32)], axis=1)
            add = jnp.concatenate([jnp.zeros((1, LANES), f32), row1, row2, jnp.zeros((13, LANES), f32)], axis=0)
            rz, ry, rx = zs ^ z, (ts // 2) ^ y, (ts % 2) ^ x
            block = (extra[zs, ts] + add).astype(bf16)

            @pl.when(ry == 0)
            def _():
                bk[rx, rz, QB_ROWS - 16 :, :] = block

            @pl.when(ry == 1)
            def _():
                bs[rx, rz, QB_ROWS - 16 :, :] = block

    for rz in range(4):
        zz = rz ^ z
        for ry in range(2):
            for rx in range(2):
                tt = (ry ^ y) * 2 + (rx ^ x)
                a, b = (ak, as_)[rx], (bk, bs)[ry]
                parts = [
                    t1[tt, pl.ds(pl.multiple_of(zz * DZ + (rc ^ c) * DC, 16), DC), :] for rc in range(2)
                ]
                for rc in range(2):
                    for k in range(2):
                        first = (2 * k + rc) * DC
                        a[ry, rz, first : first + DC, :] = parts[rc][:, LANES * k : LANES * (k + 1)]
                third = [part[:, 2 * LANES : 3 * LANES] for part in parts]
                cut = QA - 4 * DC
                a[ry, rz, 4 * DC : QA, :] = third[0][:cut, :]
                b[rx, rz, : DC - cut, :] = third[0][cut:, :]
                b[rx, rz, DC - cut : 2 * DC - cut, :] = third[1]
                gap = jnp.zeros((DC, 16), bf16)
                b[rx, rz, 2 * DC - cut : 3 * DC - cut, :] = jnp.concatenate(
                    [parts[0][:, 3 * LANES :], gap, parts[1][:, 3 * LANES :], gap], axis=1
                )


def back_kernel(dqkv, w, out):
    out[...] = dot_nt(dqkv[...], w[...]).astype(bf16)


def last_kernel(mine, other, d_resid, tok, mod, grad_o, sums_o):
    i = pl.program_id(0)
    d_shifted = mine[...].astype(f32) + other[...].astype(f32)
    normed, inverse = normalize(tok[...].astype(f32))
    grad = d_resid[...] + normalize_back(d_shifted * (1.0 + mod[1:2, :]), normed, inverse)
    grad_o[...] = grad.astype(bf16)
    sums = [jnp.sum(p, axis=0, keepdims=True) for p in (d_shifted, d_shifted * normed)]
    sums = jnp.concatenate(sums + [jnp.zeros((6, D), f32)], axis=0)

    @pl.when(i == 0)
    def _():
        sums_o[...] = sums

    @pl.when(i > 0)
    def _():
        sums_o[...] += sums


def finish_kernel(sc, f0, f1, f2, fp, fq, s0, s1, s2, sq, gq_o, gp_o, g1_o, g2_o):
    own = fq[...]
    sib = sq[...].astype(f32)
    mine = jnp.concatenate(
        [own[0:DC], own[2 * DC : 3 * DC], own[4 * DC : 5 * DC], own[6 * DC : 7 * DC, : DC // 3]], axis=1
    )
    theirs = jnp.concatenate(
        [sib[DC : 2 * DC], sib[3 * DC : 4 * DC], sib[5 * DC : 6 * DC], sib[6 * DC : 7 * DC, 64 : 64 + DC // 3]],
        axis=1,
    )
    first = [f[...] for f in (f0, f1, f2)]
    second = [s[...].astype(f32) for s in (s0, s1, s2)]
    for core in range(2):

        @pl.when(sc[1] == core)
        def _():
            for k in range(3):
                a, b = DZ * k + DC * core, DZ * k + DC * (1 - core)
                gq_o[:, a : a + DC] = mine[:, DC * k : DC * (k + 1)]
                gq_o[:, b : b + DC] = theirs[:, DC * k : DC * (k + 1)]
            for f in range(NF):
                a, b = FF // 8 * core + FZ * f, FF // 8 * (1 - core) + FZ * f
                g1_o[:, a : a + FZ] = jnp.concatenate(
                    [first[f][:DC], first[f][2 * DC : 3 * DC, : FZ - LANES]], axis=1
                )
                g1_o[:, b : b + FZ] = jnp.concatenate(
                    [second[f][DC : 2 * DC], second[f][2 * DC : 3 * DC, FZ - LANES :]], axis=1
                )

    for f in range(NF):
        part = first[f][G1R:]
        tail = part[2 * FZ :]
        tail = jnp.concatenate([tail[:, 32 * k : 32 * (k + 1)] for k in range(4)], axis=0)
        g2_o[FZ * f : FZ * (f + 1), :] = jnp.concatenate([part[:FZ], part[FZ : 2 * FZ], tail], axis=1)
    part = fp[...]
    tail = part[2 * DC :]
    tail = jnp.concatenate([tail[:, 32 * k : 32 * (k + 1)] for k in range(3)], axis=0)
    gp_o[...] = jnp.concatenate([part[:DC], part[DC : 2 * DC], tail], axis=1)


def make_perm(move):
    pairs = []
    for b in range(8):
        for t in range(4):
            z, c, y, x = move(b // 2, b % 2, t // 2, t % 2)
            pairs.append((b * 4 + t, (z * 2 + c) * 4 + y * 2 + x))
    return pairs


PERM_X = make_perm(lambda z, c, y, x: (z, c, y, 1 - x))
PERM_Y = make_perm(lambda z, c, y, x: (z, c, 1 - y, x))
PERM_XY = make_perm(lambda z, c, y, x: (z, c, 1 - y, 1 - x))
PERM_C = make_perm(lambda z, c, y, x: (z, 1 - c, y, x))
PERM_Z = [None] + [make_perm(lambda z, c, y, x, j=j: (z ^ j, c, y, x)) for j in (1, 2, 3)]
PERM_T = [make_perm(lambda z, c, y, x, j=j: (z, y, c, x ^ j)) for j in (0, 1)]


def send(value, perm):
    return lax.ppermute(value, BOTH, perm)


def reduce_streams(streams):
    halves = []
    for kept, sent, first, second in streams:
        got = send(sent, first)
        onward = (kept[1].astype(f32) + got[1].astype(f32)).astype(bf16)
        halves.append((kept[0], got[0], send(onward, second)))
    sums = [[a[k].astype(f32) + b[k].astype(f32) + c[k].astype(f32) for a, b, c in halves] for k in range(4)]
    total = jnp.concatenate(sums[0], axis=0)
    for k in (1, 2, 3):
        total = total + send(jnp.concatenate([s.astype(bf16) for s in sums[k]], axis=0), PERM_Z[k]).astype(f32)
    return total


def one_item_per_chip(
    tokens, cotangent, timesteps, bucket_ids, head_masks, channel_masks, skip_rows,
    w_qkv, q_bias, v_bias, w_proj, proj_bias, w_fc1, fc1_bias, w_fc2, fc2_bias, ada_weight, ada_bias,
):
    b, t = lax.axis_index("bucket"), lax.axis_index("tok")
    z, c, y, x = b // 2, b % 2, t // 2, t % 2
    sc = jnp.stack([z, c, y, x]).astype(jnp.int32)
    sds = jax.ShapeDtypeStruct

    def gather(values):
        here = lax.dynamic_index_in_dim(values, x, 0, keepdims=False)
        there = lax.dynamic_index_in_dim(values, 1 - x, 0, keepdims=False)
        mine = jnp.concatenate([send(here, PERM_T[0]), send(there, PERM_T[1])], axis=0)
        return jnp.concatenate([mine, send(mine, PERM_C)], axis=0)

    def scatter(values):
        here, there = send(values[:LB], PERM_T[0]), send(values[LB:], PERM_T[1])
        return jnp.where(x == 0, jnp.stack([here, there]), jnp.stack([there, here]))

    tok = gather(tokens)
    ints = jnp.concatenate([timesteps, bucket_ids, jnp.zeros((13,), jnp.int32), skip_rows.reshape(-1)])
    ints_other = send(ints, PERM_C)
    every_step = lax.all_gather(timesteps, "bucket", axis=0, tiled=True)
    g_all = gather(cotangent)

    steps4 = jnp.where(c == 0, jnp.concatenate([ints[:2], ints_other[:2]]), jnp.concatenate([ints_other[:2], ints[:2]]))
    group_ints = jnp.where(c == y, ints, ints_other)
    bucket = group_ints[2]
    skip = lax.dynamic_slice_in_dim(group_ints, 16 + skip_rows.shape[1] * x, skip_rows.shape[1], 0)
    blocks = jnp.stack([2 * c + x, 2 * c + 1 - x, 2 * (1 - c) + x, 2 * (1 - c) + 1 - x])
    positions = (blocks[:, None] * LB + jnp.arange(LB)[None, :]).reshape(L, 1)
    kept = 1.0 - jnp.any(positions == skip[None, :], axis=1, keepdims=True).astype(f32)
    kept = kept.reshape(L, 1)

    condition = jax.nn.silu(step_embedding(steps4, D)).astype(bf16)
    mod4 = jnp.dot(condition, ada_weight, preferred_element_type=f32) + ada_bias.astype(f32)
    pick = lambda k: lax.dynamic_index_in_dim(mod4, t ^ k, 0, keepdims=False)
    shares = jnp.stack([pick(0), send(pick(1), PERM_X), send(pick(2), PERM_Y), send(pick(3), PERM_XY)])
    mod = jnp.take(shares, jnp.arange(4) ^ t, axis=0).reshape(6, D)
    mod = jnp.concatenate([mod, jnp.zeros((2, D), f32)], axis=0)

    def core_half(v, *dims):
        return lax.dynamic_index_in_dim(v.reshape(dims), c, 1, keepdims=False)

    head_on = core_half(lax.dynamic_index_in_dim(head_masks, bucket, 0, keepdims=False).astype(f32), 4, 2, 2).reshape(HC)
    group_on = lax.dynamic_index_in_dim(channel_masks, bucket, 0, keepdims=False).astype(f32)
    channel_on = jnp.repeat(group_on, FF // group_on.shape[0])

    def hidden_order(v):
        return core_half(v, 4, 2, NF, FZ).transpose(1, 0, 2).reshape(NF, 1, FB)

    chan = hidden_order(channel_on)
    b1 = hidden_order(fc1_bias.astype(f32))
    qkv_bias = jnp.concatenate([q_bias, jnp.zeros_like(q_bias), v_bias]).astype(f32)
    qkv_bias = core_half(qkv_bias, 12, 2, DC).reshape(1, 3 * WC)

    wq, w1 = call(
        prep_kernel, "prep",
        (sds((D, 3 * WC), bf16), sds((NF, D, FB), bf16)), (sc, w_qkv, w_fc1),
        grid=(8,),
        in_specs=[SMEM, rows(DC, 3 * D), rows(DC, FF)],
        out_specs=(rows(DC, 3 * WC), pl.BlockSpec((NF, DC, FB), lambda i: (0, i, 0))),
        nbytes=28e6,
    )
    w2 = w_fc2.reshape(4, 2, NF, FZ, D)
    wp = w_proj.reshape(4, 2, DC, D)
    wp_mine = lax.dynamic_index_in_dim(wp, c, 1, keepdims=False).reshape(WC, D)
    wp_other = lax.dynamic_index_in_dim(wp, 1 - c, 1, keepdims=False).reshape(WC, D)

    shifted, qkv = call(
        qkv_kernel, "ln_qkv",
        (sds((L, D), bf16), sds((L, 3 * WC), bf16)), (tok, mod, wq, qkv_bias),
        grid=(4,),
        in_specs=[rows(LB, D), full((8, D)), full((D, 3 * WC)), full((1, 3 * WC))],
        out_specs=(rows(LB, D), rows(LB, 3 * WC)),
        flops=2 * L * D * 3 * WC, nbytes=12e6,
    )
    mixed = call(
        functools.partial(attn_kernel, 256), "attn",
        sds((L, WC), bf16), (qkv, head_on),
        in_specs=[pl.BlockSpec(memory_space=pltpu.VMEM), SMEM],
        scratch=[pltpu.VMEM((L, HD), bf16)] * 3,
        flops=16e9, nbytes=5e6,
    )
    mixed_other = send(mixed, PERM_C)
    shifted2, attn = call(
        proj_kernel, "proj_ln",
        (sds((L, D), bf16), sds((LH, D), f32)),
        (mixed, mixed_other, wp_mine, wp_other, proj_bias.astype(f32).reshape(1, D), tok, mod),
        grid=(4,),
        in_specs=[rows(LB, WC), pl.BlockSpec((LB, WC), lambda i: ((i + 2) % 4, 0)), full((WC, D)), full((WC, D)),
                  full((1, D)), rows(LB, D), full((8, D))],
        out_specs=(rows(LB, D), pl.BlockSpec((LB, D), lambda i: (jnp.minimum(i, 1), 0))),
        flops=2 * L * D * D, nbytes=12e6,
    )

    mlp_steps = 2
    block = L // mlp_steps
    finals, branches, ds2s, sums1 = [], [], [], []
    for f in range(NF):
        slot1, slot2 = sds((2, 4, G1R, LANES), bf16), sds((2, 4, G2R, LANES), bf16)
        g1k, g1s, g2k, g2s, branch_f, ds2_f, sum1, sum2 = call(
            functools.partial(mlp_kernel, mlp_steps), f"mlp{f}",
            (slot1, slot1, slot2, slot2, sds((L, D), bf16), sds((L, D), bf16), sds((1, FB), f32), sds((1, D), f32)),
            (sc, shifted2, g_all, kept, mod, w1, b1, chan, w2),
            grid_spec=pltpu.PrefetchScalarGridSpec(
                num_scalar_prefetch=1,
                grid=(mlp_steps,),
                in_specs=[
                    prow(block, D), prow(block, D), prow(block, 1), full((8, D)),
                    pl.BlockSpec((1, D, FB), lambda i, s, f=f: (f, 0, 0)),
                    pl.BlockSpec((1, 1, FB), lambda i, s, f=f: (f, 0, 0)),
                    pl.BlockSpec((1, 1, FB), lambda i, s, f=f: (f, 0, 0)),
                    pl.BlockSpec((4, 1, 1, FZ, D), lambda i, s, f=f: (0, s[1], f, 0, 0)),
                ],
                out_specs=(full(slot1.shape), full(slot1.shape), full(slot2.shape), full(slot2.shape),
                           prow(block, D), prow(block, D), full((1, FB)), full((1, D))),
                scratch_shapes=[pltpu.VMEM((D, FB), f32), pltpu.VMEM((FB, D), f32),
                                pltpu.VMEM((4, D, FZ), bf16), pltpu.VMEM((4, FB, TD), bf16)],
            ),
            flops=12 * L * D * FB, nbytes=20e6,
        )
        finals.append(reduce_streams([(g1k, g1s, PERM_X, PERM_Y), (g2k, g2s, PERM_Y, PERM_X)]))
        branches.append(branch_f)
        ds2s.append(ds2_f)
        sums1.append(sum1)

    def far_half(parts):
        return sum(p[LH:].astype(f32) for p in parts).astype(bf16)

    ds2_r = send(far_half(ds2s), PERM_C)
    branch_r = send(far_half(branches), PERM_C)
    row = rows(LB, D)
    d_resid, d_attn, out_rows, sums_mid = call(
        mid_kernel, "mid",
        (sds((LH, D), f32), sds((LH, D), bf16), sds((LH, D), bf16), sds((8, D), f32)),
        (*ds2s, ds2_r, *branches, branch_r, attn, tok, g_all, kept, mod, fc2_bias.astype(f32).reshape(1, D)),
        grid=(2,),
        in_specs=[row] * 8 + [row, row, row, rows(LB, 1), full((8, D)), full((1, D))],
        out_specs=(row, row, row, full((8, D))),
        nbytes=20e6,
    )
    output = scatter(out_rows)
    d_attn_other = send(d_attn, PERM_C)
    slotp = sds((2, 4, PR, LANES), bf16)
    dh, pk, ps, sum_attn = call(
        heads_kernel, "heads_back",
        (sds((L, WC), bf16), slotp, slotp, sds((1, D), f32)),
        (sc, d_attn, d_attn_other, mixed, wp_mine),
        in_specs=[SMEM] + [pl.BlockSpec(memory_space=pltpu.VMEM)] * 4,
        scratch=[pltpu.VMEM((4, WC, TD), bf16)],
        flops=4 * L * D * WC, nbytes=10e6,
    )
    final_p = reduce_streams([(pk, ps, PERM_Y, PERM_X)])
    dqkv = call(
        functools.partial(attn_back_kernel, 512), "attn_back",
        sds((L, 3 * WC), bf16), (qkv, dh, head_on),
        in_specs=[pl.BlockSpec(memory_space=pltpu.VMEM)] * 2 + [SMEM],
        scratch=[pltpu.VMEM((L, HD), bf16)] * 4 + [pltpu.VMEM((L, HD), f32)] * 3,
        flops=30e9, nbytes=9e6,
    )
    sum_fc1 = jnp.concatenate(sums1, axis=0).reshape(NF, 4, FZ).transpose(1, 0, 2).reshape(4, 4, FF // 32)
    own = lambda v: core_half(v, 4, 2, 4, D // 32)
    sum_fc2, sum_attn = own(sum2), own(sum_attn)
    line = jnp.concatenate(
        [sum_fc1, sum_fc2, sum_attn, jnp.zeros((4, 4, 3 * LANES - FF // 32 - D // 16), f32)], axis=2
    ).reshape(4, 4, 3, LANES)
    extra = jnp.concatenate([line, jnp.zeros((4, 4, 13, LANES), f32)], axis=2)
    slota, slotb = sds((2, 4, QA, LANES), bf16), sds((2, 4, QB_ROWS, LANES), bf16)
    ak, as_, bk, bs = call(
        qkv_grad_kernel, "qkv_grad",
        (slota, slota, slotb, slotb), (sc, shifted, dqkv, extra),
        in_specs=[SMEM] + [pl.BlockSpec(memory_space=pltpu.VMEM)] * 3,
        scratch=[pltpu.VMEM((4, D, 3 * DC), bf16)],
        flops=2 * L * D * 3 * WC, nbytes=12e6,
    )
    final_q = reduce_streams([(ak, as_, PERM_X, PERM_Y), (bk, bs, PERM_Y, PERM_X)])
    d_shifted = call(
        back_kernel, "qkv_back",
        sds((L, D), bf16), (dqkv, wq),
        grid=(2,),
        in_specs=[rows(LH, 3 * WC), full((D, 3 * WC))],
        out_specs=rows(LH, D),
        flops=2 * L * D * 3 * WC, nbytes=12e6,
    )
    d_shifted_r = send(d_shifted[LH:], PERM_C)
    grad_rows, sums_last = call(
        last_kernel, "last",
        (sds((LH, D), bf16), sds((8, D), f32)),
        (d_shifted, d_shifted_r, d_resid, tok, mod),
        grid=(2,),
        in_specs=[row, row, row, row, full((8, D))],
        out_specs=(row, full((8, D))),
        nbytes=10e6,
    )
    grad_tokens = scatter(grad_rows).astype(f32)

    mine = jnp.concatenate([sums_last[:2], sums_mid[:4]], axis=0).reshape(1, 6 * D)
    every = lax.all_gather(mine, BOTH, axis=0, tiled=True)
    every = every.reshape(4, 2, 4, 6 * D).sum(axis=1).reshape(16, 6 * D)
    ada_cols = ada_weight.shape[1]
    cond_all = jax.nn.silu(step_embedding(every_step, D)).astype(bf16).astype(f32)
    cond_rows = lax.dynamic_slice_in_dim(cond_all, b * DC, DC, 1)
    columns = lax.dynamic_slice_in_dim(every, t * ada_cols, ada_cols, 1)
    grad_ada_weight = lax.dot_general(
        cond_rows, columns, (((0,), (0,)), ((), ())), precision=lax.Precision.HIGHEST
    )
    bias_cols = 6 * D // 8
    grad_ada_bias = jnp.sum(lax.dynamic_slice_in_dim(every, b * bias_cols, bias_cols, 1), axis=0)

    other = send(jnp.concatenate([f[:G1R].astype(bf16) for f in finals] + [final_q[: 7 * DC].astype(bf16)], axis=0), PERM_C)
    others = [other[G1R * f : G1R * (f + 1)] for f in range(NF)]
    gq, gp, g1, g2 = call(
        finish_kernel, "finish",
        (sds((DC, 3 * TD), f32), sds((DC, TD), f32), sds((DC, FF // 4), f32), sds((FF // 8, TD), f32)),
        (sc, *finals, final_p, final_q, *others, other[NF * G1R :]),
        in_specs=[SMEM] + [pl.BlockSpec(memory_space=pltpu.VMEM)] * 9,
        nbytes=6e6,
    )
    line = final_q[7 * DC :].reshape(-1)
    n1, n = FF // 32, D // 32
    b_fc1, b_fc2, b_proj = line[:n1], line[n1 : n1 + n], line[n1 + n : n1 + 2 * n]
    b_q, b_v = line[n1 + 2 * n : n1 + 3 * n], line[2 * LANES : 2 * LANES + n]
    return (output, grad_tokens, gq, b_q, b_v, gp, b_proj, g1, b_fc1, g2, b_fc2, grad_ada_weight, grad_ada_bias)


def gelu_tanh(values):
    return jax.nn.gelu(values, approximate=True)


def split_heads(key_value, model_width, head_dim):
    item_count, length = (key_value.shape[0], key_value.shape[1])
    key_rows = key_value[:, :, :model_width].reshape(
        item_count, length, model_width // head_dim, head_dim
    )
    value_rows = key_value[:, :, model_width:].reshape(
        item_count, length, model_width // head_dim, head_dim
    )
    return (key_rows, value_rows)


def scores_of(queries, key_rows, score_scale):
    return (
        jnp.einsum("nqhe,nkhe->nhqk", queries, key_rows, preferred_element_type=jnp.float32)
        * score_scale
    )


def to_blocks(values, per_step):
    return values.reshape((values.shape[0] // per_step, per_step) + values.shape[1:])


def from_blocks(values):
    return values.reshape((values.shape[0] * values.shape[1],) + values.shape[2:])


def on_device(
    tokens,
    cotangent,
    timesteps,
    bucket_ids,
    head_masks,
    channel_masks,
    skip_rows,
    w_qkv,
    q_bias,
    v_bias,
    w_proj,
    proj_bias,
    w_fc1,
    fc1_bias,
    w_fc2,
    fc2_bias,
    ada_weight,
    ada_bias,
):
    item_count, local_len, model_width = tokens.shape
    row_count = item_count * local_len
    head_dim = model_width // HEADS
    score_scale = 1.0 / math.sqrt(head_dim)
    hidden_width = w_fc1.shape[1]
    ada_cols = ada_weight.shape[1]
    tok_index = lax.axis_index("tok")
    per_step = 1
    for candidate in range(1, item_count + 1):
        per_step = candidate
    condition = jax.nn.silu(step_embedding(timesteps, model_width)).astype(jnp.bfloat16)
    mod_local = jnp.dot(
        condition, ada_weight, preferred_element_type=jnp.float32
    ) + ada_bias.astype(jnp.float32)
    modulation = lax.all_gather(mod_local, "tok", axis=1, tiled=True)
    pieces = modulation.reshape(item_count, 6, 1, model_width)
    shift_a = pieces[:, 0]
    scale_a = pieces[:, 1]
    gate_a = pieces[:, 2]
    shift_m = pieces[:, 3]
    scale_m = pieces[:, 4]
    gate_m = pieces[:, 5]
    chosen = (jnp.arange(head_masks.shape[0], dtype=jnp.int32) == bucket_ids[0]).astype(jnp.float32)
    head_on = jnp.sum(chosen[:, None] * head_masks.astype(jnp.float32), axis=0)
    group_on = jnp.sum(chosen[:, None] * channel_masks.astype(jnp.float32), axis=0)
    channel_on = jnp.repeat(group_on, hidden_width // group_on.shape[0])
    positions = tok_index * local_len + jnp.arange(local_len, dtype=jnp.int32)
    skipped = jnp.any(skip_rows[:, :, None] == positions[None, None, :], axis=1)
    kept_rows = 1.0 - skipped.astype(jnp.float32)
    inputs = tokens.astype(jnp.float32)
    normed, inverse = normalize(inputs)
    shifted = (
        (normed * (1.0 + scale_a) + shift_a).astype(jnp.bfloat16).reshape(row_count, model_width)
    )
    qkv_bias = jnp.concatenate([q_bias, jnp.zeros_like(q_bias), v_bias]).astype(jnp.float32)
    projected = (jnp.dot(shifted, w_qkv, preferred_element_type=jnp.float32) + qkv_bias).astype(
        jnp.bfloat16
    )
    projected = projected.reshape(item_count, local_len, 3 * model_width)
    queries = projected[:, :, :model_width].reshape(item_count, local_len, HEADS, head_dim)
    key_value = projected[:, :, model_width:]
    all_kv = lax.all_gather(key_value, "tok", axis=1, tiled=True)

    def forward_block(packed):
        query_block, kv_block = packed
        key_rows, value_rows = split_heads(kv_block, model_width, head_dim)
        scores = scores_of(query_block, key_rows, score_scale)
        top_score = jnp.max(scores, axis=-1, keepdims=True)
        expanded = jnp.exp(scores - top_score)
        totals = jnp.sum(expanded, axis=-1, keepdims=True)
        weights_low = (expanded / totals).astype(jnp.bfloat16)
        head_out = (
            jnp.einsum(
                "nhqk,nkhe->nqhe", weights_low, value_rows, preferred_element_type=jnp.float32
            )
            * head_on[:, None]
        )
        return (head_out.astype(jnp.bfloat16), top_score + jnp.log(totals))

    mixed_heads, log_total = lax.map(
        forward_block, (to_blocks(queries, per_step), to_blocks(all_kv, per_step))
    )
    log_total = from_blocks(log_total)
    mixed = from_blocks(mixed_heads).reshape(row_count, model_width)
    attn = (
        jnp.dot(mixed, w_proj, preferred_element_type=jnp.float32) + proj_bias.astype(jnp.float32)
    ).reshape(item_count, local_len, model_width)
    resid = inputs + gate_a * attn
    normed2, inverse2 = normalize(resid)
    shifted2 = (
        (normed2 * (1.0 + scale_m) + shift_m).astype(jnp.bfloat16).reshape(row_count, model_width)
    )
    pre = jnp.dot(shifted2, w_fc1, preferred_element_type=jnp.float32) + fc1_bias.astype(
        jnp.float32
    )
    activated, gelu_pull = jax.vjp(gelu_tanh, pre)
    hidden = (activated * channel_on).astype(jnp.bfloat16)
    branch = (
        jnp.dot(hidden, w_fc2, preferred_element_type=jnp.float32) + fc2_bias.astype(jnp.float32)
    ).reshape(item_count, local_len, model_width)
    gated = kept_rows[:, :, None] * gate_m
    output = (resid + gated * branch).astype(jnp.bfloat16)
    incoming = cotangent.astype(jnp.float32)
    d_gate_m = jnp.sum(kept_rows[:, :, None] * branch * incoming, axis=1)
    d_branch = (gated * incoming).astype(jnp.bfloat16).reshape(row_count, model_width)
    grad_w_fc2 = jnp.dot(hidden.T, d_branch, preferred_element_type=jnp.float32)
    grad_fc2_bias = jnp.sum(d_branch.astype(jnp.float32), axis=0)
    d_hidden = jnp.dot(d_branch, w_fc2.T, preferred_element_type=jnp.float32)
    d_pre = gelu_pull(d_hidden * channel_on)[0].astype(jnp.bfloat16)
    grad_w_fc1 = jnp.dot(shifted2.T, d_pre, preferred_element_type=jnp.float32)
    grad_fc1_bias = jnp.sum(d_pre.astype(jnp.float32), axis=0)
    d_shifted2 = jnp.dot(d_pre, w_fc1.T, preferred_element_type=jnp.float32).reshape(
        item_count, local_len, model_width
    )
    d_shift_m = jnp.sum(d_shifted2, axis=1)
    d_scale_m = jnp.sum(d_shifted2 * normed2, axis=1)
    d_resid = incoming + normalize_back(d_shifted2 * (1.0 + scale_m), normed2, inverse2)
    d_gate_a = jnp.sum(attn * d_resid, axis=1)
    d_attn = (gate_a * d_resid).astype(jnp.bfloat16).reshape(row_count, model_width)
    grad_w_proj = jnp.dot(mixed.T, d_attn, preferred_element_type=jnp.float32)
    grad_proj_bias = jnp.sum(d_attn.astype(jnp.float32), axis=0)
    d_mixed = jnp.dot(d_attn, w_proj.T, preferred_element_type=jnp.float32).astype(jnp.bfloat16)
    d_heads = d_mixed.reshape(item_count, local_len, HEADS, head_dim) * head_on[:, None].astype(
        jnp.bfloat16
    )
    again_kv = lax.all_gather(key_value, "tok", axis=1, tiled=True)

    def backward_block(packed):
        query_block, kv_block, head_grads, totals_log = packed
        key_rows, value_rows = split_heads(kv_block, model_width, head_dim)
        scores = scores_of(query_block, key_rows, score_scale)
        probs = jnp.exp(scores - totals_log)
        d_probs = jnp.einsum(
            "nqhe,nkhe->nhqk", head_grads, value_rows, preferred_element_type=jnp.float32
        )
        row_dot = jnp.sum(probs * d_probs, axis=-1, keepdims=True)
        d_scores = (probs * (d_probs - row_dot)).astype(jnp.bfloat16)
        d_queries = (
            jnp.einsum("nhqk,nkhe->nqhe", d_scores, key_rows, preferred_element_type=jnp.float32)
            * score_scale
        )
        return (d_queries, row_dot)

    mapped = lax.map(
        backward_block,
        (
            to_blocks(queries, per_step),
            to_blocks(again_kv, per_step),
            to_blocks(d_heads, per_step),
            to_blocks(log_total, per_step),
        ),
    )
    d_queries = from_blocks(mapped[0])
    row_dot = from_blocks(mapped[1])
    queries_all, head_grads_all = (
        lax.all_gather(queries, "tok", axis=1, tiled=True),
        lax.all_gather(d_heads, "tok", axis=1, tiled=True),
    )
    totals_all, row_dot_all = (
        lax.all_gather(log_total, "tok", axis=2, tiled=True),
        lax.all_gather(row_dot, "tok", axis=2, tiled=True),
    )

    def key_block(packed):
        kv_block, query_block, head_grads, totals_log, dots = packed
        key_rows, value_rows = split_heads(kv_block, model_width, head_dim)
        scores = (
            jnp.einsum("nkhe,nqhe->nhkq", key_rows, query_block, preferred_element_type=jnp.float32)
            * score_scale
        )
        probs = jnp.exp(scores - totals_log[:, :, None, :, 0])
        d_probs = jnp.einsum(
            "nkhe,nqhe->nhkq", value_rows, head_grads, preferred_element_type=jnp.float32
        )
        d_scores = (probs * (d_probs - dots[:, :, None, :, 0])).astype(jnp.bfloat16)
        d_keys = (
            jnp.einsum("nhkq,nqhe->nkhe", d_scores, query_block, preferred_element_type=jnp.float32)
            * score_scale
        )
        d_values = jnp.einsum(
            "nhkq,nqhe->nkhe",
            probs.astype(jnp.bfloat16),
            head_grads,
            preferred_element_type=jnp.float32,
        )
        return jnp.concatenate(
            [
                d_keys.reshape(d_keys.shape[0], local_len, model_width),
                d_values.reshape(d_values.shape[0], local_len, model_width),
            ],
            axis=2,
        )

    d_kv = from_blocks(
        lax.map(
            key_block,
            (
                to_blocks(key_value, per_step),
                to_blocks(queries_all, per_step),
                to_blocks(head_grads_all, per_step),
                to_blocks(totals_all, per_step),
                to_blocks(row_dot_all, per_step),
            ),
        )
    )
    d_qkv = jnp.concatenate([d_queries.reshape(item_count, local_len, model_width), d_kv], axis=2)
    d_qkv = d_qkv.astype(jnp.bfloat16).reshape(row_count, 3 * model_width)
    grad_w_qkv = jnp.dot(shifted.T, d_qkv, preferred_element_type=jnp.float32)
    qkv_sums = jnp.sum(d_qkv.astype(jnp.float32), axis=0)
    grad_q_bias = qkv_sums[:model_width]
    grad_v_bias = qkv_sums[2 * model_width :]
    d_shifted = jnp.dot(d_qkv, w_qkv.T, preferred_element_type=jnp.float32).reshape(
        item_count, local_len, model_width
    )
    d_shift_a = jnp.sum(d_shifted, axis=1)
    d_scale_a = jnp.sum(d_shifted * normed, axis=1)
    grad_tokens = d_resid + normalize_back(d_shifted * (1.0 + scale_a), normed, inverse)
    d_modulation = jnp.concatenate(
        [d_shift_a, d_scale_a, d_gate_a, d_shift_m, d_scale_m, d_gate_m], axis=1
    )
    d_modulation = lax.psum(d_modulation, "tok")
    mod_columns = lax.dynamic_slice_in_dim(d_modulation, tok_index * ada_cols, ada_cols, 1)
    grad_ada_weight = jnp.dot(
        condition.astype(jnp.float32).T, mod_columns, precision=lax.Precision.HIGHEST
    )
    grad_ada_bias = jnp.sum(d_modulation, axis=0)
    bucket_done = (
        lax.psum_scatter(grad_w_qkv, "bucket", scatter_dimension=0, tiled=True),
        lax.psum_scatter(grad_w_proj, "bucket", scatter_dimension=0, tiled=True),
        lax.psum_scatter(grad_w_fc1, "bucket", scatter_dimension=0, tiled=True),
        lax.psum_scatter(grad_w_fc2, "bucket", scatter_dimension=0, tiled=True),
        lax.psum_scatter(grad_q_bias, "bucket", scatter_dimension=0, tiled=True),
        lax.psum_scatter(grad_v_bias, "bucket", scatter_dimension=0, tiled=True),
        lax.psum_scatter(grad_proj_bias, "bucket", scatter_dimension=0, tiled=True),
        lax.psum_scatter(grad_fc1_bias, "bucket", scatter_dimension=0, tiled=True),
        lax.psum_scatter(grad_fc2_bias, "bucket", scatter_dimension=0, tiled=True),
        lax.psum_scatter(grad_ada_weight, "bucket", scatter_dimension=0, tiled=True),
        lax.psum_scatter(grad_ada_bias, "bucket", scatter_dimension=0, tiled=True),
    )
    token_done = (
        lax.psum_scatter(bucket_done[0], "tok", scatter_dimension=1, tiled=True),
        lax.psum_scatter(bucket_done[1], "tok", scatter_dimension=1, tiled=True),
        lax.psum_scatter(bucket_done[2], "tok", scatter_dimension=1, tiled=True),
        lax.psum_scatter(bucket_done[3], "tok", scatter_dimension=1, tiled=True),
        lax.psum_scatter(bucket_done[4].reshape(1, -1), "tok", scatter_dimension=1, tiled=True),
        lax.psum_scatter(bucket_done[5].reshape(1, -1), "tok", scatter_dimension=1, tiled=True),
        lax.psum_scatter(bucket_done[6].reshape(1, -1), "tok", scatter_dimension=1, tiled=True),
        lax.psum_scatter(bucket_done[7].reshape(1, -1), "tok", scatter_dimension=1, tiled=True),
        lax.psum_scatter(bucket_done[8].reshape(1, -1), "tok", scatter_dimension=1, tiled=True),
    )
    finished = (
        token_done[0],
        token_done[1],
        token_done[2],
        token_done[3],
        token_done[4],
        token_done[5],
        token_done[6],
        token_done[7],
        token_done[8],
        bucket_done[9],
        bucket_done[10],
    )
    return (
        output,
        grad_tokens,
        finished[0],
        finished[4].reshape(-1),
        finished[5].reshape(-1),
        finished[1],
        finished[6].reshape(-1),
        finished[2],
        finished[7].reshape(-1),
        finished[3],
        finished[8].reshape(-1),
        finished[9],
        finished[10],
    )


def solution(mesh):
    planned = mesh.shape["tok"] == 4 and mesh.shape["bucket"] == 8
    return jax.shard_map(
        one_item_per_chip if planned else on_device,
        mesh=mesh,
        in_specs=(
            P("bucket", "tok", None),
            P("bucket", "tok", None),
            P("bucket"),
            P("bucket"),
            P(),
            P(),
            P("bucket", None),
            P(),
            P(),
            P(),
            P(),
            P(),
            P(),
            P(),
            P(),
            P(),
            P(None, "tok"),
            P("tok"),
        ),
        out_specs=(
            P("bucket", "tok", None),
            P("bucket", "tok", None),
            P("bucket", "tok"),
            P(("bucket", "tok")),
            P(("bucket", "tok")),
            P("bucket", "tok"),
            P(("bucket", "tok")),
            P("bucket", "tok"),
            P(("bucket", "tok")),
            P("bucket", "tok"),
            P(("bucket", "tok")),
            P("bucket", "tok"),
            P("bucket"),
        ),
        check_vma=False,
    )
```

```python
import functools
import math

import jax
import jax.numpy as jnp
from jax import lax
from jax.experimental import pallas as pl
from jax.experimental.pallas import tpu as pltpu
from jax.sharding import PartitionSpec as P

HEADS = 16
EPSILON = 1e-06
LOG2E = 1.4426950408889634
GELU_K = math.sqrt(2.0 / math.pi)
GELU_C = 0.044715
LANES = 128
BOTH = ("bucket", "tok")
bf16, f32 = jnp.bfloat16, jnp.float32


def dot_nn(a, b):
    return lax.dot_general(a, b, (((1,), (0,)), ((), ())), preferred_element_type=f32)


def dot_nt(a, b):
    return lax.dot_general(a, b, (((1,), (1,)), ((), ())), preferred_element_type=f32)


def dot_tn(a, b):
    return lax.dot_general(a, b, (((0,), (0,)), ((), ())), preferred_element_type=f32)


def step_embedding(timesteps, model_width):
    half_width = model_width // 2
    frequency = jnp.exp(-math.log(10000.0) * jnp.arange(half_width, dtype=jnp.float32) / half_width)
    angles = timesteps.astype(jnp.float32)[:, None] * frequency[None, :]
    return jnp.concatenate([jnp.cos(angles), jnp.sin(angles)], axis=1)


def normalize(values):
    centred = values - jnp.mean(values, axis=-1, keepdims=True)
    inverse = lax.rsqrt(jnp.mean(centred * centred, axis=-1, keepdims=True) + EPSILON)
    return (centred * inverse, inverse)


def normalize_back(incoming, normed, inverse):
    return inverse * (
        incoming
        - jnp.mean(incoming, axis=-1, keepdims=True)
        - normed * jnp.mean(incoming * normed, axis=-1, keepdims=True)
    )


D = 1152
DC, DZ, TD = D // 8, D // 4, D // 4
HD = D // HEADS
HC = HEADS // 2
WC = D // 2
FF = 4608
NF = 3
FB = FF // 2 // NF
FZ = FB // 4
L = 1024
LH = L // 2
LB = L // 4
G1R = 3 * DC
G2R = 2 * FZ + FZ // 4
PR = 2 * DC + DC // 3
PA = 176
QR = 7 * DC + 16
QA = QR // 2
VMEM_LIMIT = 58 * 1024 * 1024


ANY = pl.BlockSpec(memory_space=pl.ANY)
MESH = pl.DeviceIdType.MESH


def place():
    b, t = lax.axis_index("bucket"), lax.axis_index("tok")
    return b // 2, b % 2, t // 2, t % 2


def flip(value, other):
    return (value // 2 + other // 2) % 2 * 2 + (value % 2 + other % 2) % 2


def peer(name):
    z, c, y, x = place()
    if name == "x":
        x = 1 - x
    elif name == "y":
        y = 1 - y
    elif name == "xy":
        x, y = 1 - x, 1 - y
    elif name == "c":
        c = 1 - c
    elif name in ("t0", "t1"):
        c, y, x = y, c, x if name == "t0" else 1 - x
    else:
        z = flip(z, int(name[1]))
    return (z * 2 + c, y * 2 + x)


def meet(names):
    sem = pltpu.get_barrier_semaphore()
    others = [name for name in names if name != "t0"]
    for name in others:
        pl.semaphore_signal(sem, inc=1, device_id=peer(name), device_id_type=MESH)
    wanted = len(others)
    if "t0" in names:
        _, c, y, _ = place()
        wanted = wanted + (c + y) % 2

        @pl.when(c != y)
        def _():
            pl.semaphore_signal(sem, inc=1, device_id=peer("t0"), device_id_type=MESH)

    pl.semaphore_wait(sem, wanted)


def remote(src, dst, sems, k, name):
    return pltpu.make_async_remote_copy(
        src_ref=src, dst_ref=dst, send_sem=sems.at[0, k], recv_sem=sems.at[1, k],
        device_id=peer(name), device_id_type=MESH,
    )


def vm(*shape, dtype=bf16):
    return pltpu.VMEM(shape, dtype)


class FirstSum:
    peers = ("x", "y")

    def __init__(self, keep_a, sent_a, keep_b, sent_b):
        self.ins = [keep_a, sent_a, keep_b, sent_b]
        shapes = [keep.shape[1:] for keep in (keep_a, keep_b)]
        self.outs = [jax.ShapeDtypeStruct(s, bf16) for s in shapes for _ in range(2)]
        self.scratch = [vm(*s) for s in shapes for _ in range(3)]
        self.scratch += [pltpu.SemaphoreType.DMA((2, 4)), pltpu.SemaphoreType.DMA((4,))]

    def plan(self, ins, outs, scratch):
        ka, sa, kb, sb = ins
        _, qa, _, qb = outs
        kav, rav, _, kbv, rbv, _, sems, local = scratch
        far = [
            remote(sa.at[1], rav, sems, 0, "x"),
            remote(sb.at[1], rbv, sems, 1, "y"),
            remote(sa.at[0], qa, sems, 2, "x"),
            remote(sb.at[0], qb, sems, 3, "y"),
        ]
        near = [
            pltpu.make_async_copy(ka.at[1], kav, local.at[0]),
            pltpu.make_async_copy(kb.at[1], kbv, local.at[1]),
        ]
        return far, near

    def finish(self, ins, outs, scratch):
        kav, rav, oav, kbv, rbv, obv, _, local = scratch
        oav[...] = (kav[...].astype(f32) + rav[...].astype(f32)).astype(bf16)
        obv[...] = (kbv[...].astype(f32) + rbv[...].astype(f32)).astype(bf16)
        return [
            pltpu.make_async_copy(oav, outs[0], local.at[2]),
            pltpu.make_async_copy(obv, outs[2], local.at[3]),
        ]


class SecondSum:
    peers = ("x", "y")

    def __init__(self, on_a, q_a, on_b, q_b, keep_a, keep_b):
        self.ins = [on_a, q_a, on_b, q_b, keep_a, keep_b]
        self.rows = [on_a.shape[1], on_b.shape[1]]
        total = sum(self.rows)
        self.outs = [jax.ShapeDtypeStruct((3, total, LANES), bf16), jax.ShapeDtypeStruct((total, LANES), f32)]
        self.scratch = [vm(4, r, LANES) for r in self.rows for _ in range(3)]
        self.scratch += [vm(3, total, LANES), vm(total, LANES, dtype=f32)]
        self.scratch += [pltpu.SemaphoreType.DMA((2, 2)), pltpu.SemaphoreType.DMA((6,))]

    def plan(self, ins, outs, scratch):
        oa, qa, ob, qb, ka, kb = ins
        kav, qav, rav, kbv, qbv, rbv, _, _, sems, local = scratch
        far = [remote(oa, rav, sems, 0, "y"), remote(ob, rbv, sems, 1, "x")]
        pairs = [(ka.at[0], kav), (qa, qav), (kb.at[0], kbv), (qb, qbv)]
        return far, [pltpu.make_async_copy(a, b, local.at[k]) for k, (a, b) in enumerate(pairs)]

    def finish(self, ins, outs, scratch):
        zs, zk, local = scratch[6], scratch[7], scratch[9]
        start = 0
        for k, r in enumerate(self.rows):
            kv, qv, rv = scratch[3 * k : 3 * k + 3]
            for j in range(4):
                total = kv[j].astype(f32) + qv[j].astype(f32) + rv[j].astype(f32)
                if j == 0:
                    zk[start : start + r, :] = total
                else:
                    zs[j - 1, start : start + r, :] = total.astype(bf16)
            start += r
        return [
            pltpu.make_async_copy(zs, outs[0], local.at[4]),
            pltpu.make_async_copy(zk, outs[1], local.at[5]),
        ]


class ThirdSum:
    peers = ("z1", "z2", "z3")

    def __init__(self, sent, kept):
        self.ins = [sent, kept]
        self.outs = [jax.ShapeDtypeStruct(kept.shape, f32)]
        self.scratch = [vm(*sent.shape), vm(*kept.shape, dtype=f32)]
        self.scratch += [pltpu.SemaphoreType.DMA((2, 3)), pltpu.SemaphoreType.DMA((2,))]

    def plan(self, ins, outs, scratch):
        got, kept, sems, local = scratch
        far = [remote(ins[0].at[k], got.at[k], sems, k, f"z{k + 1}") for k in (2, 1, 0)]
        return far, [pltpu.make_async_copy(ins[1], kept, local.at[0])]

    def finish(self, ins, outs, scratch):
        got, kept, _, local = scratch
        kept[...] = kept[...] + got[0].astype(f32) + got[1].astype(f32) + got[2].astype(f32)
        return [pltpu.make_async_copy(kept, outs[0], local.at[1])]


def call(kernel, name, out_shape, args, in_specs=None, out_specs=None, scratch=(), grid=None,
         peers=(), jobs=(), cid=None, flops=0, nbytes=0):
    whole = pl.BlockSpec(memory_space=pltpu.VMEM)
    single = not isinstance(out_shape, (tuple, list))
    out_shape = [out_shape] if single else list(out_shape)
    in_specs = list(in_specs) if in_specs is not None else [whole] * len(args)
    out_specs = [whole] * len(out_shape) if out_specs is None else [out_specs] if single else list(out_specs)
    counts = [len(args), sum(len(j.ins) for j in jobs), len(out_shape), sum(len(j.outs) for j in jobs), len(scratch)]
    names = sorted(set(peers).union(*[j.peers for j in jobs]))

    def run(*refs):
        groups, at = [], 0
        for n in counts:
            groups.append(refs[at : at + n])
            at += n
        bound, ai, ao, asc = [], 0, 0, at
        for j in jobs:
            bound.append((
                j, groups[1][ai : ai + len(j.ins)], groups[3][ao : ao + len(j.outs)], refs[asc : asc + len(j.scratch)]
            ))
            ai, ao, asc = ai + len(j.ins), ao + len(j.outs), asc + len(j.scratch)

        def begin():
            if names:
                meet(names)
            for j, *r in bound:
                for group in j.plan(*r):
                    for copy in group:
                        copy.start()

        def end():
            last = []
            for j, *r in bound:
                far, near = j.plan(*r)
                for copy in far:
                    copy.wait()
                for copy in near:
                    copy.wait()
                copies = j.finish(*r)
                for copy in copies:
                    copy.start()
                last += copies
            for copy in last:
                copy.wait()

        if grid is None:
            begin()
            kernel(*groups[0], *groups[2], *groups[4])
            end()
        else:
            pl.when(pl.program_id(0) == 0)(begin)
            kernel(*groups[0], *groups[2], *groups[4])
            pl.when(pl.program_id(0) == grid[0] - 1)(end)

    extra = {} if grid is None else {"grid": grid}
    params = {"collective_id": cid, "has_side_effects": True} if names else {}
    outs = pl.pallas_call(
        run,
        out_shape=out_shape + [o for j in jobs for o in j.outs],
        in_specs=in_specs + [ANY] * counts[1],
        out_specs=out_specs + [ANY] * counts[3],
        scratch_shapes=list(scratch) + [q for j in jobs for q in j.scratch],
        compiler_params=pltpu.CompilerParams(vmem_limit_bytes=VMEM_LIMIT, **params),
        cost_estimate=pl.CostEstimate(flops=int(flops), bytes_accessed=int(nbytes), transcendentals=0),
        name=name,
        **extra,
    )(*args, *[a for j in jobs for a in j.ins])
    own, rest, given = outs[: len(out_shape)], outs[len(out_shape) :], []
    for j in jobs:
        given.append(rest[: len(j.outs)])
        rest = rest[len(j.outs) :]
    return (own[0] if single else own), given


SMEM = pl.BlockSpec(memory_space=pltpu.SMEM)


def full(shape):
    return pl.BlockSpec(shape, lambda *_: (0,) * len(shape))


def once(*shape):
    return pl.BlockSpec(shape, lambda *_: (0,) * len(shape), pipeline_mode=pl.Buffered(1))


def rows(block, width):
    return pl.BlockSpec((block, width), lambda i: (i, 0))


def prep_kernel(wq, w1, wq_o, w1_o):
    c = place()[1]
    for core in range(2):

        @pl.when(c == core)
        def _():
            for k in range(12):
                wq_o[:, DC * k : DC * (k + 1)] = wq[:, DZ * k + DC * core : DZ * k + DC * (core + 1)]
            for f in range(NF):
                for k in range(4):
                    start = 4 * DZ * k + FF // 8 * core + FZ * f
                    w1_o[f, :, FZ * k : FZ * (k + 1)] = w1[:, start : start + FZ]


def qkv_kernel(tok, mod, w, bias, shifted_o, qkv_o):
    normed, _ = normalize(tok[...].astype(f32))
    shifted = (normed * (1.0 + mod[1:2, :]) + mod[0:1, :]).astype(bf16)
    shifted_o[...] = shifted
    qkv_o[...] = (dot_nn(shifted, w[...]) + bias[...]).astype(bf16)


def attn_kernel(step, qkv, head_on, out, qs, ks, vs):
    scale = LOG2E / math.sqrt(HD)
    for h in range(HC):
        qs[...] = qkv[:, h * HD : (h + 1) * HD]
        ks[...] = qkv[:, WC + h * HD : WC + (h + 1) * HD]
        vs[...] = qkv[:, 2 * WC + h * HD : 2 * WC + (h + 1) * HD]
        on = head_on[h]

        def body(i, carry):
            part = pl.ds(pl.multiple_of(i * step, step), step)
            s = dot_nt(qs[part, :], ks[...])
            top = jnp.max(s, axis=1, keepdims=True)
            p = jnp.exp2((s - top) * scale)
            total = jnp.sum(p, axis=1, keepdims=True)
            o = dot_nn(p.astype(bf16), vs[...])
            out[part, h * HD : (h + 1) * HD] = (o * (on / total)).astype(bf16)
            return carry

        lax.fori_loop(0, L // step, body, 0)


def proj_kernel(mine, other, w_mine, w_other, bias, tok, mod, shifted2_o, attn_o):
    attn = (
        dot_nn(mine[...], w_mine[...].reshape(WC, D))
        + dot_nn(other[...], w_other[...].reshape(WC, D))
        + bias[...]
    )

    @pl.when(pl.program_id(0) < 2)
    def _():
        attn_o[...] = attn

    resid = tok[...].astype(f32) + mod[2:3, :] * attn
    normed, _ = normalize(resid)
    shifted2_o[...] = (normed * (1.0 + mod[4:5, :]) + mod[3:4, :]).astype(bf16)


def pack_hidden(block1, block2, o1, o2, ry, rx, rz):
    o1[ry, rz, : 2 * DC, :] = block1[:, :LANES]
    o1[ry, rz, 2 * DC :, :] = jnp.concatenate([block1[:DC, LANES:], block1[DC:, LANES:]], axis=1)
    o2[rx, rz, :FZ, :] = block2[:, :LANES]
    o2[rx, rz, FZ : 2 * FZ, :] = block2[:, LANES : 2 * LANES]
    q = FZ // 4
    o2[rx, rz, 2 * FZ :, :] = jnp.concatenate([block2[q * k : q * (k + 1), 2 * LANES :] for k in range(4)], axis=1)


def mlp_kernel(f, *refs):
    last = f == NF - 1
    refs = list(refs)
    sh2, g, kept, mod, w1, b1, chan, w2 = refs[:8]
    del refs[:8]
    before = None
    if f > 0:
        before = refs[:2]
        del refs[:2]
    slots, branch_o, ds2_o, sum1_o, sum2_o = refs[:4], refs[4], refs[5], refs[6], refs[7]
    del refs[:8]
    if last:
        got = refs[:2]
        del refs[:2]
    hid, dpre, dbs, w2v, t1, t2, s1k, s1s, s2k, s2s, sems = refs[:11]
    if last:
        far, csems = refs[11:]
        crossing = [remote(far.at[k], got[k], csems, k, "c") for k in range(2)]
    stages = (s1k, s1s, s2k, s2s)
    i = pl.program_id(0)
    z, c, y, x = place()

    @pl.when(i == 0)
    def _():
        copy = pltpu.make_async_copy(w2.at[:, c, f], w2v, sems.at[4])
        copy.start()
        copy.wait()

    part = pl.ds(pl.multiple_of((1 - i) * LH, LH), LH)
    w1v = w1[0]
    w2f = w2v[...].reshape(FB, D)
    db = (g[...].astype(f32) * mod[5:6, :] * kept[...]).astype(bf16)
    dbs[part, :] = db
    v = dot_nn(sh2[part, :], w1v) + b1[0]
    v2 = v * v
    th = jnp.tanh(GELU_K * v * (1.0 + GELU_C * v2))
    half = 0.5 * (1.0 + th)
    on = chan[0]
    hidden = (v * half * on).astype(bf16)
    hid[part, :] = hidden
    slope = (half + (0.5 * GELU_K) * v * (1.0 - th * th) * (1.0 + (3.0 * GELU_C) * v2)) * on
    d_pre = (dot_nt(db, w2f) * slope).astype(bf16)
    dpre[part, :] = d_pre
    branch, ds2 = dot_nn(hidden, w2f), dot_nt(d_pre, w1v)
    if before is not None:
        branch = branch + before[0][...].astype(f32)
        ds2 = ds2 + before[1][...].astype(f32)
    branch, ds2 = branch.astype(bf16), ds2.astype(bf16)
    if last:

        @pl.when(i == 0)
        def _():
            far[0] = branch
            far[1] = ds2
            for copy in crossing:
                copy.start()

        @pl.when(i == 1)
        def _():
            branch_o[...] = branch
            ds2_o[...] = ds2
    else:
        branch_o[...] = branch
        ds2_o[...] = ds2
    s1 = jnp.sum(d_pre.astype(f32), axis=0, keepdims=True)
    s2 = jnp.sum(db.astype(f32), axis=0, keepdims=True)

    @pl.when(i == 0)
    def _():
        sum1_o[...] = s1
        sum2_o[...] = s2

    @pl.when(i == 1)
    def _():
        sum1_o[...] += s1
        sum2_o[...] += s2
        for m in range(3):
            cut = slice(m * D // 3, (m + 1) * D // 3)
            p = dot_tn(sh2[:, cut], dpre[...]).astype(bf16)
            for t in range(4):
                t1[t, cut, :] = p[:, FZ * t : FZ * (t + 1)]
        for m in range(3):
            cut = slice(m * FB // 3, (m + 1) * FB // 3)
            p = dot_tn(hid[:, cut], dbs[...]).astype(bf16)
            for t in range(4):
                t2[t, cut, :] = p[:, TD * t : TD * (t + 1)]
        for rz in range(4):
            zz = flip(z, rz)
            for ry in range(2):
                for rx in range(2):
                    tt = (ry + y) % 2 * 2 + (rx + x) % 2
                    one = [
                        t1[tt, pl.ds(pl.multiple_of(zz * DZ + (rc + c) % 2 * DC, 16), DC), :] for rc in range(2)
                    ]
                    two = t2[tt, pl.ds(pl.multiple_of(zz * FZ, 16), FZ), :]
                    pack_hidden(jnp.concatenate(one, axis=0), two, (s1k, s1s)[rx], (s2k, s2s)[ry], ry, rx, rz)
        copies = [pltpu.make_async_copy(a, b, sems.at[k]) for k, (a, b) in enumerate(zip(stages, slots))]
        for copy in copies:
            copy.start()
        for copy in copies:
            copy.wait()
        if last:
            for copy in crossing:
                copy.wait()


def middle_kernel(ds, ds_r, br, br_r, attn, tok, g, kept, mod, bias2, mixed, w,
                  d_resid_o, out, dh_o, pka, psa, pkb, psb, sums_o, sum_o, da, ob, t1, csems, tsems, lsem):
    i = pl.program_id(0)
    n = LH // 4
    z, c, y, x = place()
    part = pl.ds(pl.multiple_of(i * n, n), n)
    gf, at = g[...].astype(f32), attn[...]
    resid = tok[...].astype(f32) + mod[2:3, :] * at
    normed2, inverse2 = normalize(resid)
    ds2 = ds[...].astype(f32) + ds_r[...].astype(f32)
    kb = kept[...] * (br[...].astype(f32) + br_r[...].astype(f32) + bias2[...])
    ob[part, :] = (resid + mod[5:6, :] * kb).astype(bf16)
    d_resid = gf + normalize_back(ds2 * (1.0 + mod[4:5, :]), normed2, inverse2)
    d_resid_o[...] = d_resid
    da[part, :] = (mod[2:3, :] * d_resid).astype(bf16)
    sums = [jnp.sum(p, axis=0, keepdims=True) for p in (at * d_resid, ds2, ds2 * normed2, kb * gf)]
    sums = jnp.concatenate(sums + [jnp.zeros((4, D), f32)], axis=0)

    @pl.when(i == 0)
    def _():
        sums_o[...] = sums

    @pl.when(i > 0)
    def _():
        sums_o[...] += sums

    crossing = [
        remote(da.at[pl.ds(n * k, n)], da.at[pl.ds(LH + n * k, n)], csems, k, "c") for k in range(4)
    ]
    home0 = remote(ob.at[pl.ds(0, LB)], out.at[x], tsems, 0, "t0")
    stay0 = pltpu.make_async_copy(ob.at[pl.ds(0, LB)], out.at[x], lsem)
    home1 = remote(ob.at[pl.ds(LB, LB)], out.at[x], tsems, 1, "t1")
    for k in range(4):

        @pl.when(i == k)
        def _():
            crossing[k].start()
            if k == 1:
                pl.when(c != y)(home0.start)
                pl.when(c == y)(stay0.start)
            if k == 3:
                home1.start()

    @pl.when(i == 3)
    def _():
        for copy in crossing:
            copy.wait()
        wv = w[...].reshape(WC, D)
        dh_o[...] = dot_nt(da[...], wv).astype(bf16)
        sum_o[...] = dot_nn(jnp.ones((16, L), bf16), da[...])[:8]
        grad = dot_tn(mixed[...], da[...]).astype(bf16)
        for t in range(4):
            t1[t] = grad[:, TD * t : TD * (t + 1)]
        for rz in range(4):
            zz = flip(z, rz)
            for ry in range(2):
                for rx in range(2):
                    tt = (ry + y) % 2 * 2 + (rx + x) % 2
                    a, b = (pka, psa)[rx], (pkb, psb)[ry]
                    block = t1[tt, pl.ds(pl.multiple_of(zz * DC, 16), DC), :]
                    a[ry, rz, :DC, :] = block[:, :LANES]
                    a[ry, rz, DC:, :] = block[: PA - DC, LANES : 2 * LANES]
                    b[rx, rz, : 2 * DC - PA, :] = block[PA - DC :, LANES : 2 * LANES]
                    q = DC // 3
                    tails = [block[q * k : q * (k + 1), 2 * LANES :] for k in range(3)]
                    tails.append(jnp.zeros((q, 32), bf16))
                    b[rx, rz, 2 * DC - PA :, :] = jnp.concatenate(tails, axis=1)
        pl.when(c != y)(home0.wait)
        pl.when(c == y)(stay0.wait)
        home1.wait()


def attn_back_kernel(step, qkv, dh, head_on, out, qs, ks, vs, dos, dq, dk, dv):
    scale = LOG2E / math.sqrt(HD)
    for h in range(HC):
        qs[...] = qkv[:, h * HD : (h + 1) * HD]
        ks[...] = qkv[:, WC + h * HD : WC + (h + 1) * HD]
        vs[...] = qkv[:, 2 * WC + h * HD : 2 * WC + (h + 1) * HD]
        dos[...] = (dh[:, h * HD : (h + 1) * HD].astype(f32) * head_on[h]).astype(bf16)
        dk[...] = jnp.zeros_like(dk)
        dv[...] = jnp.zeros_like(dv)

        def body(i, carry):
            part = pl.ds(pl.multiple_of(i * step, step), step)
            q, do = qs[part, :], dos[part, :]
            s = dot_nt(ks[...], q)
            top = jnp.max(s, axis=0, keepdims=True)
            p = jnp.exp2((s - top) * scale)
            p = p * (1.0 / jnp.sum(p, axis=0, keepdims=True))
            dp = dot_nt(vs[...], do)
            row_dot = jnp.sum(p * dp, axis=0, keepdims=True)
            ds = (p * (dp - row_dot)).astype(bf16)
            dv[...] += dot_nn(p.astype(bf16), do)
            dk[...] += dot_nn(ds, q)
            dq[part, :] = dot_tn(ds, ks[...])
            return carry

        lax.fori_loop(0, L // step, body, 0)
        out[:, h * HD : (h + 1) * HD] = (dq[...] * (1.0 / math.sqrt(HD))).astype(bf16)
        out[:, WC + h * HD : WC + (h + 1) * HD] = (dk[...] * (1.0 / math.sqrt(HD))).astype(bf16)
        out[:, 2 * WC + h * HD : 2 * WC + (h + 1) * HD] = dv[...].astype(bf16)


def qkv_grad_kernel(shifted, dqkv, extra, ka, sa, kb, sb, t1):
    z, c, y, x = place()
    for k in range(4):
        grad = dot_tn(shifted[:, DZ * k : DZ * (k + 1)], dqkv[...]).astype(bf16)
        for t in range(4):
            t1[t, DZ * k : DZ * (k + 1), :] = grad[:, 3 * DC * t : 3 * DC * (t + 1)]
    sums = dot_nn(jnp.ones((16, L), bf16), dqkv[...])[0:1, :]
    for zs in range(4):
        for ts in range(4):
            piece = DC * zs + DC // 4 * ts
            qsum = sums[:, piece : piece + DC // 4]
            vsum = sums[:, 2 * WC + piece : 2 * WC + piece + DC // 4]
            row1 = jnp.concatenate([jnp.zeros((1, 88), f32), qsum, jnp.zeros((1, 4), f32)], axis=1)
            row2 = jnp.concatenate([vsum, jnp.zeros((1, LANES - DC // 4), f32)], axis=1)
            add = jnp.concatenate([jnp.zeros((1, LANES), f32), row1, row2, jnp.zeros((13, LANES), f32)], axis=0)
            rz, ry, rx = flip(z, zs), (ts // 2 + y) % 2, (ts % 2 + x) % 2
            block = (extra[zs, ts] + add).astype(bf16)

            @pl.when(ry == 0)
            def _():
                kb[rx, rz, QA - 16 :, :] = block

            @pl.when(ry == 1)
            def _():
                sb[rx, rz, QA - 16 :, :] = block

    for rz in range(4):
        zz = flip(z, rz)
        for ry in range(2):
            for rx in range(2):
                tt = (ry + y) % 2 * 2 + (rx + x) % 2
                a, b = (ka, sa)[rx], (kb, sb)[ry]
                parts = [
                    t1[tt, pl.ds(pl.multiple_of(zz * DZ + (rc + c) % 2 * DC, 16), DC), :] for rc in range(2)
                ]
                strips = [p[:, LANES * k : LANES * (k + 1)] for k in range(3) for p in parts]
                gap = jnp.zeros((DC, 16), bf16)
                strips.append(jnp.concatenate([parts[0][:, 3 * LANES :], gap, parts[1][:, 3 * LANES :], gap], axis=1))
                for k, strip in enumerate(strips):
                    first = DC * k
                    if first + DC <= QA:
                        a[ry, rz, first : first + DC, :] = strip
                    elif first >= QA:
                        b[rx, rz, first - QA : first - QA + DC, :] = strip
                    else:
                        a[ry, rz, first:, :] = strip[: QA - first]
                        b[rx, rz, : first + DC - QA, :] = strip[QA - first :]


def tail_kernel(dqkv, w, d_resid, tok, mod, sums_mid, grad, item_o, got, far, gb, other, csems, tsems, lsem):
    i = pl.program_id(0)
    c, y, x = place()[1:]
    d_shifted = dot_nt(dqkv[...], w[...])
    crossing = [remote(far.at[k], got.at[k], csems, k, "c") for k in range(2)]
    sums_over = remote(item_o, other, csems, 2, "c")
    home0 = remote(gb.at[0], grad.at[x], tsems, 0, "t0")
    stay0 = pltpu.make_async_copy(gb.at[0], grad.at[x], lsem)
    home1 = remote(gb.at[1], grad.at[x], tsems, 1, "t1")
    for k in range(2):

        @pl.when(i == k)
        def _():
            far[k] = d_shifted.astype(bf16)
            crossing[k].start()

        @pl.when(i == k + 2)
        def _():
            crossing[k].wait()
            total = d_shifted + got[k].astype(f32)
            normed, inverse = normalize(tok[...].astype(f32))
            back = d_resid[...] + normalize_back(total * (1.0 + mod[1:2, :]), normed, inverse)
            gb[k] = back.astype(bf16)
            sums = [jnp.sum(p, axis=0, keepdims=True) for p in (total, total * normed)]
            if k == 0:
                pl.when(c != y)(home0.start)
                pl.when(c == y)(stay0.start)
                item_o[...] = jnp.concatenate(sums + [sums_mid[0:4, :], jnp.zeros((2, D), f32)], axis=0)
            else:
                home1.start()
                item_o[0:2, :] += jnp.concatenate(sums, axis=0)
                sums_over.start()
                sums_over.wait()
                item_o[...] += other[...]
                pl.when(c != y)(home0.wait)
                pl.when(c == y)(stay0.wait)
                home1.wait()


def square_kernel(item, square, sems, lsem):
    t = lax.axis_index("tok")
    here = pltpu.make_async_copy(item, square.at[t], lsem)
    copies = [remote(item, square.at[t], sems, k, name) for k, name in enumerate(("x", "y", "xy"))]
    here.start()
    for copy in copies:
        copy.start()
    here.wait()
    for copy in copies:
        copy.wait()


def every_kernel(square, every, sems, lsem):
    z = place()[0]
    here = pltpu.make_async_copy(square, every.at[z], lsem)
    copies = [remote(square, every.at[z], sems, k, f"z{k + 1}") for k in range(3)]
    here.start()
    for copy in copies:
        copy.start()
    here.wait()
    for copy in copies:
        copy.wait()


def finish_kernel(f0, f1, f2, fp, fq, gq_o, gp_o, g1_o, g2_o, mine, theirs, sems):
    c = place()[1]
    for f, ref in enumerate((f0, f1, f2)):
        mine[G1R * f : G1R * (f + 1), :] = ref[:G1R, :].astype(bf16)
    mine[NF * G1R :, :] = fq[: 7 * DC, :].astype(bf16)
    copy = remote(mine, theirs, sems, 0, "c")
    copy.start()

    def place_columns(own, q, first):
        columns = jnp.concatenate(q, axis=1)
        for core in range(2):

            @pl.when(c == core)
            def _():
                at = core if own else 1 - core
                for k in range(3):
                    gq_o[:, DZ * k + DC * at : DZ * k + DC * (at + 1)] = columns[:, DC * k : DC * (k + 1)]
                for f in range(NF):
                    start = FF // 8 * at + FZ * f
                    g1_o[:, start : start + FZ] = jnp.concatenate(first[f], axis=1)

    q = fq[...]
    place_columns(
        True,
        [q[0:DC], q[2 * DC : 3 * DC], q[4 * DC : 5 * DC], q[6 * DC : 7 * DC, : DC // 3]],
        [[f[:DC, :], f[2 * DC : 3 * DC, : FZ - LANES]] for f in (f0, f1, f2)],
    )
    for f, ref in enumerate((f0, f1, f2)):
        part = ref[G1R:, :]
        tail = part[2 * FZ :]
        tail = jnp.concatenate([tail[:, 32 * k : 32 * (k + 1)] for k in range(4)], axis=0)
        g2_o[FZ * f : FZ * (f + 1), :] = jnp.concatenate([part[:FZ], part[FZ : 2 * FZ], tail], axis=1)
    part = fp[...]
    tail = part[2 * DC :]
    tail = jnp.concatenate([tail[:, 32 * k : 32 * (k + 1)] for k in range(3)], axis=0)
    gp_o[...] = jnp.concatenate([part[:DC], part[DC : 2 * DC], tail], axis=1)
    copy.wait()
    got = theirs[...].astype(f32)
    q = got[NF * G1R :]
    place_columns(
        False,
        [q[DC : 2 * DC], q[3 * DC : 4 * DC], q[5 * DC : 6 * DC], q[6 * DC :, 64 : 64 + DC // 3]],
        [
            [got[G1R * f + DC : G1R * f + 2 * DC], got[G1R * f + 2 * DC : G1R * (f + 1), FZ - LANES :]]
            for f in range(NF)
        ],
    )


def make_perm(move):
    pairs = []
    for b in range(8):
        for t in range(4):
            z, c, y, x = move(b // 2, b % 2, t // 2, t % 2)
            pairs.append((b * 4 + t, (z * 2 + c) * 4 + y * 2 + x))
    return pairs


PERM_X = make_perm(lambda z, c, y, x: (z, c, y, 1 - x))
PERM_Y = make_perm(lambda z, c, y, x: (z, c, 1 - y, x))
PERM_XY = make_perm(lambda z, c, y, x: (z, c, 1 - y, 1 - x))
PERM_C = make_perm(lambda z, c, y, x: (z, 1 - c, y, x))
PERM_Z = [None] + [make_perm(lambda z, c, y, x, j=j: (z ^ j, c, y, x)) for j in (1, 2, 3)]
PERM_T = [make_perm(lambda z, c, y, x, j=j: (z, y, c, x ^ j)) for j in (0, 1)]


def send(value, perm):
    return lax.ppermute(value, BOTH, perm)


def one_item_per_chip(
    tokens, cotangent, timesteps, bucket_ids, head_masks, channel_masks, skip_rows,
    w_qkv, q_bias, v_bias, w_proj, proj_bias, w_fc1, fc1_bias, w_fc2, fc2_bias, ada_weight, ada_bias,
):
    b, t = lax.axis_index("bucket"), lax.axis_index("tok")
    z, c, y, x = b // 2, b % 2, t // 2, t % 2
    sds = jax.ShapeDtypeStruct

    def gather(values):
        here = lax.dynamic_index_in_dim(values, x, 0, keepdims=False)
        there = lax.dynamic_index_in_dim(values, 1 - x, 0, keepdims=False)
        mine = jnp.concatenate([send(here, PERM_T[0]), send(there, PERM_T[1])], axis=0)
        return jnp.concatenate([mine, send(mine, PERM_C)], axis=0)

    tok = gather(tokens)
    ints = jnp.concatenate([timesteps, bucket_ids, jnp.zeros((13,), jnp.int32), skip_rows.reshape(-1)])
    ints_other = send(ints, PERM_C)
    every_step = lax.all_gather(timesteps, "bucket", axis=0, tiled=True)
    g_all = gather(cotangent)

    steps4 = jnp.where(c == 0, jnp.concatenate([ints[:2], ints_other[:2]]), jnp.concatenate([ints_other[:2], ints[:2]]))
    group_ints = jnp.where(c == y, ints, ints_other)
    bucket = group_ints[2]
    skip = lax.dynamic_slice_in_dim(group_ints, 16 + skip_rows.shape[1] * x, skip_rows.shape[1], 0)
    blocks = jnp.stack([2 * c + x, 2 * c + 1 - x, 2 * (1 - c) + x, 2 * (1 - c) + 1 - x])
    positions = (blocks[:, None] * LB + jnp.arange(LB)[None, :]).reshape(L, 1)
    kept = 1.0 - jnp.any(positions == skip[None, :], axis=1, keepdims=True).astype(f32)
    kept = kept.reshape(L, 1)

    condition = jax.nn.silu(step_embedding(steps4, D)).astype(bf16)
    mod4 = jnp.dot(condition, ada_weight, preferred_element_type=f32) + ada_bias.astype(f32)
    pick = lambda k: lax.dynamic_index_in_dim(mod4, t ^ k, 0, keepdims=False)
    shares = jnp.stack([pick(0), send(pick(1), PERM_X), send(pick(2), PERM_Y), send(pick(3), PERM_XY)])
    mod = jnp.take(shares, jnp.arange(4) ^ t, axis=0).reshape(6, D)
    mod = jnp.concatenate([mod, jnp.zeros((2, D), f32)], axis=0)

    def core_half(v, *dims):
        return lax.dynamic_index_in_dim(v.reshape(dims), c, 1, keepdims=False)

    head_on = core_half(lax.dynamic_index_in_dim(head_masks, bucket, 0, keepdims=False).astype(f32), 4, 2, 2).reshape(HC)
    group_on = lax.dynamic_index_in_dim(channel_masks, bucket, 0, keepdims=False).astype(f32)
    channel_on = jnp.repeat(group_on, FF // group_on.shape[0])

    def hidden_order(v):
        return core_half(v, 4, 2, NF, FZ).transpose(1, 0, 2).reshape(NF, 1, FB)

    chan = hidden_order(channel_on)
    b1 = hidden_order(fc1_bias.astype(f32))
    qkv_bias = jnp.concatenate([q_bias, jnp.zeros_like(q_bias), v_bias]).astype(f32)
    qkv_bias = core_half(qkv_bias, 12, 2, DC).reshape(1, 3 * WC)

    (wq, w1), _ = call(
        prep_kernel, "prep",
        (sds((D, 3 * WC), bf16), sds((NF, D, FB), bf16)), (w_qkv, w_fc1),
        grid=(8,),
        in_specs=[rows(DC, 3 * D), rows(DC, FF)],
        out_specs=(rows(DC, 3 * WC), pl.BlockSpec((NF, DC, FB), lambda i: (0, i, 0))),
        nbytes=28e6,
    )
    w2 = w_fc2.reshape(4, 2, NF, FZ, D)
    wp = w_proj.reshape(4, 2, DC, D)
    wp_mine = lax.dynamic_index_in_dim(wp, c, 1, keepdims=False).reshape(WC, D)
    wp_other = lax.dynamic_index_in_dim(wp, 1 - c, 1, keepdims=False).reshape(WC, D)

    (shifted, qkv), _ = call(
        qkv_kernel, "ln_qkv",
        (sds((L, D), bf16), sds((L, 3 * WC), bf16)), (tok, mod, wq, qkv_bias),
        grid=(4,),
        in_specs=[rows(LB, D), full((8, D)), full((D, 3 * WC)), full((1, 3 * WC))],
        out_specs=(rows(LB, D), rows(LB, 3 * WC)),
        flops=2 * L * D * 3 * WC, nbytes=12e6,
    )
    vmem = pl.BlockSpec(memory_space=pltpu.VMEM)
    mixed, _ = call(
        functools.partial(attn_kernel, 256), "attn",
        sds((L, WC), bf16), (qkv, head_on),
        in_specs=[vmem, SMEM],
        scratch=[vm(L, HD)] * 3,
        flops=16e9, nbytes=5e6,
    )
    mixed_other = send(mixed, PERM_C)
    (shifted2, attn), _ = call(
        proj_kernel, "proj_ln",
        (sds((L, D), bf16), sds((LH, D), f32)),
        (mixed, mixed_other, wp_mine, wp_other, proj_bias.astype(f32).reshape(1, D), tok, mod),
        grid=(4,),
        in_specs=[rows(LB, WC), pl.BlockSpec((LB, WC), lambda i: ((i + 2) % 4, 0)), full((WC, D)), full((WC, D)),
                  full((1, D)), rows(LB, D), full((8, D))],
        out_specs=(rows(LB, D), pl.BlockSpec((LB, D), lambda i: (jnp.minimum(i, 1), 0))),
        flops=2 * L * D * D, nbytes=12e6,
    )

    firsts, kepts, sums1, results, before = [], [], [], [], []
    half = pl.BlockSpec((LH, D), lambda i: (1 - i, 0))
    slot1, slot2 = sds((2, 4, G1R, LANES), bf16), sds((2, 4, G2R, LANES), bf16)
    for f in range(NF):
        jobs = []
        if f > 0:
            jobs.append(FirstSum(*slots))
        if f > 1:
            jobs.append(SecondSum(*firsts[f - 2], *kepts[f - 2]))
        last = f == NF - 1
        pick = lambda i, f=f: (f, 0, 0)
        out_shape = [slot1, slot1, slot2, slot2] + [sds((LH if last else L, D), bf16)] * 2
        out_shape += [sds((1, FB), f32), sds((1, D), f32)] + [sds((LH, D), bf16)] * (2 * last)
        own, given = call(
            functools.partial(mlp_kernel, f), f"mlp{f}",
            out_shape, (shifted2, g_all, kept, mod, w1, b1, chan, w2, *before),
            grid=(2,),
            in_specs=[once(L, D), half, pl.BlockSpec((LH, 1), lambda i: (1 - i, 0)), full((8, D)),
                      pl.BlockSpec((1, D, FB), pick, pipeline_mode=pl.Buffered(1)),
                      pl.BlockSpec((1, 1, FB), pick), pl.BlockSpec((1, 1, FB), pick), ANY] + [half] * len(before),
            out_specs=[ANY] * 4 + [full((LH, D)) if last else half] * 2 + [full((1, FB)), full((1, D))]
            + [ANY] * (2 * last),
            scratch=[vm(L, FB), vm(L, FB), vm(L, D), vm(4, FZ, D), vm(4, D, FZ), vm(4, FB, TD)]
            + [vm(*s.shape) for s in (slot1, slot1, slot2, slot2)] + [pltpu.SemaphoreType.DMA((5,))]
            + ([vm(2, LH, D), pltpu.SemaphoreType.DMA((2, 2))] if last else []),
            peers=("c",) if last else (), jobs=jobs, cid=f,
            flops=12 * L * D * FB, nbytes=20e6,
        )
        slots, before = own[:4], own[4:6]
        kepts.append((slots[0], slots[2]))
        sums1.append(own[6])
        if f > 0:
            firsts.append(given[0])
        if f > 1:
            results.append(given[1])
    sum2 = own[7]
    branch_r, ds2_r = own[8:]

    n = LH // 4
    row = rows(n, D)
    slot_a, slot_b = sds((2, 4, PA, LANES), bf16), sds((2, 4, PR - PA, LANES), bf16)
    own, given = call(
        middle_kernel, "middle",
        (sds((LH, D), f32), sds((2, LB, D), bf16), sds((L, WC), bf16), slot_a, slot_a, slot_b, slot_b,
         sds((8, D), f32), sds((8, D), f32)),
        (before[1], ds2_r, before[0], branch_r, attn, tok, g_all, kept, mod, fc2_bias.astype(f32).reshape(1, D),
         mixed, wp_mine),
        grid=(4,),
        in_specs=[row] * 7 + [rows(n, 1), full((8, D)), full((1, D)), once(L, WC), once(WC, D)],
        out_specs=(row, ANY, full((L, WC)), full(slot_a.shape), full(slot_a.shape), full(slot_b.shape),
                   full(slot_b.shape), full((8, D)), full((8, D))),
        scratch=[vm(L, D), vm(LH, D), vm(4, WC, TD), pltpu.SemaphoreType.DMA((2, 4)), pltpu.SemaphoreType.DMA((2, 2)),
                 pltpu.SemaphoreType.DMA],
        peers=("c", "t0", "t1"), cid=3,
        jobs=[FirstSum(*slots), SecondSum(*firsts[1], *kepts[1]), ThirdSum(*results[0])],
        flops=4 * L * D * WC, nbytes=20e6,
    )
    d_resid, output, dh, *slots_p, sums_mid, sum_attn = own
    firsts.append(given[0])
    results.append(given[1])
    finals = [given[2][0]]
    dqkv, given = call(
        functools.partial(attn_back_kernel, 512), "attn_back",
        sds((L, 3 * WC), bf16), (qkv, dh, head_on),
        in_specs=[vmem, vmem, SMEM],
        scratch=[vm(L, HD)] * 4 + [vm(L, HD, dtype=f32)] * 3,
        cid=4, jobs=[FirstSum(*slots_p), SecondSum(*firsts[2], *kepts[2]), ThirdSum(*results[1])],
        flops=30e9, nbytes=9e6,
    )
    first_p = given[0]
    results.append(given[1])
    finals.append(given[2][0])
    sum_fc1 = jnp.concatenate(sums1, axis=0).reshape(NF, 4, FZ).transpose(1, 0, 2).reshape(4, 4, FF // 32)
    own_part = lambda v: core_half(v, 4, 2, 4, D // 32)
    line = jnp.concatenate(
        [sum_fc1, own_part(sum2), own_part(sum_attn[0]), jnp.zeros((4, 4, 3 * LANES - FF // 32 - D // 16), f32)], axis=2
    ).reshape(4, 4, 3, LANES)
    extra = jnp.concatenate([line, jnp.zeros((4, 4, 13, LANES), f32)], axis=2)
    slot_q = sds((2, 4, QA, LANES), bf16)
    slots_q, given = call(
        qkv_grad_kernel, "qkv_grad",
        (slot_q,) * 4, (shifted, dqkv, extra),
        scratch=[vm(4, D, 3 * DC)],
        cid=5, jobs=[SecondSum(*first_p, slots_p[0], slots_p[2]), ThirdSum(*results[2])],
        flops=2 * L * D * 3 * WC, nbytes=12e6,
    )
    result_p = given[0]
    finals.append(given[1][0])
    near = pl.BlockSpec((LB, D), lambda i: (jnp.maximum(i - 2, 0), 0))
    (grad_rows, item), given = call(
        tail_kernel, "tail",
        (sds((2, LB, D), bf16), sds((8, D), f32)),
        (dqkv, wq, d_resid, tok, mod, sums_mid),
        grid=(4,),
        in_specs=[pl.BlockSpec((LB, 3 * WC), lambda i: ((i + 2) % 4, 0)), once(D, 3 * WC), near, near, full((8, D)),
                  full((8, D))],
        out_specs=(ANY, full((8, D))),
        scratch=[vm(2, LB, D), vm(2, LB, D), vm(2, LB, D), vm(8, D, dtype=f32), pltpu.SemaphoreType.DMA((2, 3)),
                 pltpu.SemaphoreType.DMA((2, 2)), pltpu.SemaphoreType.DMA],
        peers=("c", "t0", "t1"), cid=6, jobs=[FirstSum(*slots_q), ThirdSum(*result_p)],
        flops=2 * L * D * 3 * WC, nbytes=12e6,
    )
    first_q, final_p = given[0], given[1][0]
    grad_tokens = grad_rows.astype(f32)
    square, given = call(
        square_kernel, "square", sds((4, 8, D), f32), (item,),
        scratch=[pltpu.SemaphoreType.DMA((2, 3)), pltpu.SemaphoreType.DMA],
        peers=("x", "y", "xy"), cid=7, jobs=[SecondSum(*first_q, slots_q[0], slots_q[2])],
    )
    every, given = call(
        every_kernel, "every", sds((4, 4, 8, D), f32), (square,),
        scratch=[pltpu.SemaphoreType.DMA((2, 3)), pltpu.SemaphoreType.DMA],
        peers=("z1", "z2", "z3"), cid=8, jobs=[ThirdSum(*given[0])],
    )
    final_q = given[0][0]

    every = every.reshape(16, 8, D)[:, :6].reshape(16, 6 * D)
    ada_cols = ada_weight.shape[1]
    cond_all = jax.nn.silu(step_embedding(every_step, D)).astype(bf16).astype(f32)
    cond_rows = lax.dynamic_slice_in_dim(cond_all, b * DC, DC, 1)
    columns = lax.dynamic_slice_in_dim(every, t * ada_cols, ada_cols, 1)
    grad_ada_weight = lax.dot_general(
        cond_rows, columns, (((0,), (0,)), ((), ())), precision=lax.Precision.HIGHEST
    )
    bias_cols = 6 * D // 8
    grad_ada_bias = jnp.sum(lax.dynamic_slice_in_dim(every, b * bias_cols, bias_cols, 1), axis=0)

    (gq, gp, g1, g2), _ = call(
        finish_kernel, "finish",
        (sds((DC, 3 * TD), f32), sds((DC, TD), f32), sds((DC, FF // 4), f32), sds((FF // 8, TD), f32)),
        (*finals, final_p, final_q),
        scratch=[vm(NF * G1R + 7 * DC, LANES), vm(NF * G1R + 7 * DC, LANES), pltpu.SemaphoreType.DMA((2, 1))],
        peers=("c",), cid=9, nbytes=6e6,
    )
    line = final_q[7 * DC :].reshape(-1)
    n1, n = FF // 32, D // 32
    b_fc1, b_fc2, b_proj = line[:n1], line[n1 : n1 + n], line[n1 + n : n1 + 2 * n]
    b_q, b_v = line[n1 + 2 * n : n1 + 3 * n], line[2 * LANES : 2 * LANES + n]
    return (output, grad_tokens, gq, b_q, b_v, gp, b_proj, g1, b_fc1, g2, b_fc2, grad_ada_weight, grad_ada_bias)


def gelu_tanh(values):
    return jax.nn.gelu(values, approximate=True)


def split_heads(key_value, model_width, head_dim):
    item_count, length = (key_value.shape[0], key_value.shape[1])
    key_rows = key_value[:, :, :model_width].reshape(
        item_count, length, model_width // head_dim, head_dim
    )
    value_rows = key_value[:, :, model_width:].reshape(
        item_count, length, model_width // head_dim, head_dim
    )
    return (key_rows, value_rows)


def scores_of(queries, key_rows, score_scale):
    return (
        jnp.einsum("nqhe,nkhe->nhqk", queries, key_rows, preferred_element_type=jnp.float32)
        * score_scale
    )


def to_blocks(values, per_step):
    return values.reshape((values.shape[0] // per_step, per_step) + values.shape[1:])


def from_blocks(values):
    return values.reshape((values.shape[0] * values.shape[1],) + values.shape[2:])


def on_device(
    tokens,
    cotangent,
    timesteps,
    bucket_ids,
    head_masks,
    channel_masks,
    skip_rows,
    w_qkv,
    q_bias,
    v_bias,
    w_proj,
    proj_bias,
    w_fc1,
    fc1_bias,
    w_fc2,
    fc2_bias,
    ada_weight,
    ada_bias,
):
    item_count, local_len, model_width = tokens.shape
    row_count = item_count * local_len
    head_dim = model_width // HEADS
    score_scale = 1.0 / math.sqrt(head_dim)
    hidden_width = w_fc1.shape[1]
    ada_cols = ada_weight.shape[1]
    tok_index = lax.axis_index("tok")
    per_step = 1
    for candidate in range(1, item_count + 1):
        per_step = candidate
    condition = jax.nn.silu(step_embedding(timesteps, model_width)).astype(jnp.bfloat16)
    mod_local = jnp.dot(
        condition, ada_weight, preferred_element_type=jnp.float32
    ) + ada_bias.astype(jnp.float32)
    modulation = lax.all_gather(mod_local, "tok", axis=1, tiled=True)
    pieces = modulation.reshape(item_count, 6, 1, model_width)
    shift_a = pieces[:, 0]
    scale_a = pieces[:, 1]
    gate_a = pieces[:, 2]
    shift_m = pieces[:, 3]
    scale_m = pieces[:, 4]
    gate_m = pieces[:, 5]
    chosen = (jnp.arange(head_masks.shape[0], dtype=jnp.int32) == bucket_ids[0]).astype(jnp.float32)
    head_on = jnp.sum(chosen[:, None] * head_masks.astype(jnp.float32), axis=0)
    group_on = jnp.sum(chosen[:, None] * channel_masks.astype(jnp.float32), axis=0)
    channel_on = jnp.repeat(group_on, hidden_width // group_on.shape[0])
    positions = tok_index * local_len + jnp.arange(local_len, dtype=jnp.int32)
    skipped = jnp.any(skip_rows[:, :, None] == positions[None, None, :], axis=1)
    kept_rows = 1.0 - skipped.astype(jnp.float32)
    inputs = tokens.astype(jnp.float32)
    normed, inverse = normalize(inputs)
    shifted = (
        (normed * (1.0 + scale_a) + shift_a).astype(jnp.bfloat16).reshape(row_count, model_width)
    )
    qkv_bias = jnp.concatenate([q_bias, jnp.zeros_like(q_bias), v_bias]).astype(jnp.float32)
    projected = (jnp.dot(shifted, w_qkv, preferred_element_type=jnp.float32) + qkv_bias).astype(
        jnp.bfloat16
    )
    projected = projected.reshape(item_count, local_len, 3 * model_width)
    queries = projected[:, :, :model_width].reshape(item_count, local_len, HEADS, head_dim)
    key_value = projected[:, :, model_width:]
    all_kv = lax.all_gather(key_value, "tok", axis=1, tiled=True)

    def forward_block(packed):
        query_block, kv_block = packed
        key_rows, value_rows = split_heads(kv_block, model_width, head_dim)
        scores = scores_of(query_block, key_rows, score_scale)
        top_score = jnp.max(scores, axis=-1, keepdims=True)
        expanded = jnp.exp(scores - top_score)
        totals = jnp.sum(expanded, axis=-1, keepdims=True)
        weights_low = (expanded / totals).astype(jnp.bfloat16)
        head_out = (
            jnp.einsum(
                "nhqk,nkhe->nqhe", weights_low, value_rows, preferred_element_type=jnp.float32
            )
            * head_on[:, None]
        )
        return (head_out.astype(jnp.bfloat16), top_score + jnp.log(totals))

    mixed_heads, log_total = lax.map(
        forward_block, (to_blocks(queries, per_step), to_blocks(all_kv, per_step))
    )
    log_total = from_blocks(log_total)
    mixed = from_blocks(mixed_heads).reshape(row_count, model_width)
    attn = (
        jnp.dot(mixed, w_proj, preferred_element_type=jnp.float32) + proj_bias.astype(jnp.float32)
    ).reshape(item_count, local_len, model_width)
    resid = inputs + gate_a * attn
    normed2, inverse2 = normalize(resid)
    shifted2 = (
        (normed2 * (1.0 + scale_m) + shift_m).astype(jnp.bfloat16).reshape(row_count, model_width)
    )
    pre = jnp.dot(shifted2, w_fc1, preferred_element_type=jnp.float32) + fc1_bias.astype(
        jnp.float32
    )
    activated, gelu_pull = jax.vjp(gelu_tanh, pre)
    hidden = (activated * channel_on).astype(jnp.bfloat16)
    branch = (
        jnp.dot(hidden, w_fc2, preferred_element_type=jnp.float32) + fc2_bias.astype(jnp.float32)
    ).reshape(item_count, local_len, model_width)
    gated = kept_rows[:, :, None] * gate_m
    output = (resid + gated * branch).astype(jnp.bfloat16)
    incoming = cotangent.astype(jnp.float32)
    d_gate_m = jnp.sum(kept_rows[:, :, None] * branch * incoming, axis=1)
    d_branch = (gated * incoming).astype(jnp.bfloat16).reshape(row_count, model_width)
    grad_w_fc2 = jnp.dot(hidden.T, d_branch, preferred_element_type=jnp.float32)
    grad_fc2_bias = jnp.sum(d_branch.astype(jnp.float32), axis=0)
    d_hidden = jnp.dot(d_branch, w_fc2.T, preferred_element_type=jnp.float32)
    d_pre = gelu_pull(d_hidden * channel_on)[0].astype(jnp.bfloat16)
    grad_w_fc1 = jnp.dot(shifted2.T, d_pre, preferred_element_type=jnp.float32)
    grad_fc1_bias = jnp.sum(d_pre.astype(jnp.float32), axis=0)
    d_shifted2 = jnp.dot(d_pre, w_fc1.T, preferred_element_type=jnp.float32).reshape(
        item_count, local_len, model_width
    )
    d_shift_m = jnp.sum(d_shifted2, axis=1)
    d_scale_m = jnp.sum(d_shifted2 * normed2, axis=1)
    d_resid = incoming + normalize_back(d_shifted2 * (1.0 + scale_m), normed2, inverse2)
    d_gate_a = jnp.sum(attn * d_resid, axis=1)
    d_attn = (gate_a * d_resid).astype(jnp.bfloat16).reshape(row_count, model_width)
    grad_w_proj = jnp.dot(mixed.T, d_attn, preferred_element_type=jnp.float32)
    grad_proj_bias = jnp.sum(d_attn.astype(jnp.float32), axis=0)
    d_mixed = jnp.dot(d_attn, w_proj.T, preferred_element_type=jnp.float32).astype(jnp.bfloat16)
    d_heads = d_mixed.reshape(item_count, local_len, HEADS, head_dim) * head_on[:, None].astype(
        jnp.bfloat16
    )
    again_kv = lax.all_gather(key_value, "tok", axis=1, tiled=True)

    def backward_block(packed):
        query_block, kv_block, head_grads, totals_log = packed
        key_rows, value_rows = split_heads(kv_block, model_width, head_dim)
        scores = scores_of(query_block, key_rows, score_scale)
        probs = jnp.exp(scores - totals_log)
        d_probs = jnp.einsum(
            "nqhe,nkhe->nhqk", head_grads, value_rows, preferred_element_type=jnp.float32
        )
        row_dot = jnp.sum(probs * d_probs, axis=-1, keepdims=True)
        d_scores = (probs * (d_probs - row_dot)).astype(jnp.bfloat16)
        d_queries = (
            jnp.einsum("nhqk,nkhe->nqhe", d_scores, key_rows, preferred_element_type=jnp.float32)
            * score_scale
        )
        return (d_queries, row_dot)

    mapped = lax.map(
        backward_block,
        (
            to_blocks(queries, per_step),
            to_blocks(again_kv, per_step),
            to_blocks(d_heads, per_step),
            to_blocks(log_total, per_step),
        ),
    )
    d_queries = from_blocks(mapped[0])
    row_dot = from_blocks(mapped[1])
    queries_all, head_grads_all = (
        lax.all_gather(queries, "tok", axis=1, tiled=True),
        lax.all_gather(d_heads, "tok", axis=1, tiled=True),
    )
    totals_all, row_dot_all = (
        lax.all_gather(log_total, "tok", axis=2, tiled=True),
        lax.all_gather(row_dot, "tok", axis=2, tiled=True),
    )

    def key_block(packed):
        kv_block, query_block, head_grads, totals_log, dots = packed
        key_rows, value_rows = split_heads(kv_block, model_width, head_dim)
        scores = (
            jnp.einsum("nkhe,nqhe->nhkq", key_rows, query_block, preferred_element_type=jnp.float32)
            * score_scale
        )
        probs = jnp.exp(scores - totals_log[:, :, None, :, 0])
        d_probs = jnp.einsum(
            "nkhe,nqhe->nhkq", value_rows, head_grads, preferred_element_type=jnp.float32
        )
        d_scores = (probs * (d_probs - dots[:, :, None, :, 0])).astype(jnp.bfloat16)
        d_keys = (
            jnp.einsum("nhkq,nqhe->nkhe", d_scores, query_block, preferred_element_type=jnp.float32)
            * score_scale
        )
        d_values = jnp.einsum(
            "nhkq,nqhe->nkhe",
            probs.astype(jnp.bfloat16),
            head_grads,
            preferred_element_type=jnp.float32,
        )
        return jnp.concatenate(
            [
                d_keys.reshape(d_keys.shape[0], local_len, model_width),
                d_values.reshape(d_values.shape[0], local_len, model_width),
            ],
            axis=2,
        )

    d_kv = from_blocks(
        lax.map(
            key_block,
            (
                to_blocks(key_value, per_step),
                to_blocks(queries_all, per_step),
                to_blocks(head_grads_all, per_step),
                to_blocks(totals_all, per_step),
                to_blocks(row_dot_all, per_step),
            ),
        )
    )
    d_qkv = jnp.concatenate([d_queries.reshape(item_count, local_len, model_width), d_kv], axis=2)
    d_qkv = d_qkv.astype(jnp.bfloat16).reshape(row_count, 3 * model_width)
    grad_w_qkv = jnp.dot(shifted.T, d_qkv, preferred_element_type=jnp.float32)
    qkv_sums = jnp.sum(d_qkv.astype(jnp.float32), axis=0)
    grad_q_bias = qkv_sums[:model_width]
    grad_v_bias = qkv_sums[2 * model_width :]
    d_shifted = jnp.dot(d_qkv, w_qkv.T, preferred_element_type=jnp.float32).reshape(
        item_count, local_len, model_width
    )
    d_shift_a = jnp.sum(d_shifted, axis=1)
    d_scale_a = jnp.sum(d_shifted * normed, axis=1)
    grad_tokens = d_resid + normalize_back(d_shifted * (1.0 + scale_a), normed, inverse)
    d_modulation = jnp.concatenate(
        [d_shift_a, d_scale_a, d_gate_a, d_shift_m, d_scale_m, d_gate_m], axis=1
    )
    d_modulation = lax.psum(d_modulation, "tok")
    mod_columns = lax.dynamic_slice_in_dim(d_modulation, tok_index * ada_cols, ada_cols, 1)
    grad_ada_weight = jnp.dot(
        condition.astype(jnp.float32).T, mod_columns, precision=lax.Precision.HIGHEST
    )
    grad_ada_bias = jnp.sum(d_modulation, axis=0)
    bucket_done = (
        lax.psum_scatter(grad_w_qkv, "bucket", scatter_dimension=0, tiled=True),
        lax.psum_scatter(grad_w_proj, "bucket", scatter_dimension=0, tiled=True),
        lax.psum_scatter(grad_w_fc1, "bucket", scatter_dimension=0, tiled=True),
        lax.psum_scatter(grad_w_fc2, "bucket", scatter_dimension=0, tiled=True),
        lax.psum_scatter(grad_q_bias, "bucket", scatter_dimension=0, tiled=True),
        lax.psum_scatter(grad_v_bias, "bucket", scatter_dimension=0, tiled=True),
        lax.psum_scatter(grad_proj_bias, "bucket", scatter_dimension=0, tiled=True),
        lax.psum_scatter(grad_fc1_bias, "bucket", scatter_dimension=0, tiled=True),
        lax.psum_scatter(grad_fc2_bias, "bucket", scatter_dimension=0, tiled=True),
        lax.psum_scatter(grad_ada_weight, "bucket", scatter_dimension=0, tiled=True),
        lax.psum_scatter(grad_ada_bias, "bucket", scatter_dimension=0, tiled=True),
    )
    token_done = (
        lax.psum_scatter(bucket_done[0], "tok", scatter_dimension=1, tiled=True),
        lax.psum_scatter(bucket_done[1], "tok", scatter_dimension=1, tiled=True),
        lax.psum_scatter(bucket_done[2], "tok", scatter_dimension=1, tiled=True),
        lax.psum_scatter(bucket_done[3], "tok", scatter_dimension=1, tiled=True),
        lax.psum_scatter(bucket_done[4].reshape(1, -1), "tok", scatter_dimension=1, tiled=True),
        lax.psum_scatter(bucket_done[5].reshape(1, -1), "tok", scatter_dimension=1, tiled=True),
        lax.psum_scatter(bucket_done[6].reshape(1, -1), "tok", scatter_dimension=1, tiled=True),
        lax.psum_scatter(bucket_done[7].reshape(1, -1), "tok", scatter_dimension=1, tiled=True),
        lax.psum_scatter(bucket_done[8].reshape(1, -1), "tok", scatter_dimension=1, tiled=True),
    )
    finished = (
        token_done[0],
        token_done[1],
        token_done[2],
        token_done[3],
        token_done[4],
        token_done[5],
        token_done[6],
        token_done[7],
        token_done[8],
        bucket_done[9],
        bucket_done[10],
    )
    return (
        output,
        grad_tokens,
        finished[0],
        finished[4].reshape(-1),
        finished[5].reshape(-1),
        finished[1],
        finished[6].reshape(-1),
        finished[2],
        finished[7].reshape(-1),
        finished[3],
        finished[8].reshape(-1),
        finished[9],
        finished[10],
    )


def solution(mesh):
    planned = mesh.shape["tok"] == 4 and mesh.shape["bucket"] == 8
    return jax.shard_map(
        one_item_per_chip if planned else on_device,
        mesh=mesh,
        in_specs=(
            P("bucket", "tok", None),
            P("bucket", "tok", None),
            P("bucket"),
            P("bucket"),
            P(),
            P(),
            P("bucket", None),
            P(),
            P(),
            P(),
            P(),
            P(),
            P(),
            P(),
            P(),
            P(),
            P(None, "tok"),
            P("tok"),
        ),
        out_specs=(
            P("bucket", "tok", None),
            P("bucket", "tok", None),
            P("bucket", "tok"),
            P(("bucket", "tok")),
            P(("bucket", "tok")),
            P("bucket", "tok"),
            P(("bucket", "tok")),
            P("bucket", "tok"),
            P(("bucket", "tok")),
            P("bucket", "tok"),
            P(("bucket", "tok")),
            P("bucket", "tok"),
            P("bucket"),
        ),
        check_vma=False,
    )
```

```python
import functools
import math

import jax
import jax.numpy as jnp
from jax import lax
from jax.experimental import pallas as pl
from jax.experimental.pallas import tpu as pltpu
from jax.sharding import PartitionSpec as P

HEADS = 16
EPSILON = 1e-06
LOG2E = 1.4426950408889634
GELU_K = math.sqrt(2.0 / math.pi)
GELU_C = 0.044715
LANES = 128
bf16, f32 = jnp.bfloat16, jnp.float32


def dot_nn(a, b):
    return lax.dot_general(a, b, (((1,), (0,)), ((), ())), preferred_element_type=f32)


def dot_nt(a, b):
    return lax.dot_general(a, b, (((1,), (1,)), ((), ())), preferred_element_type=f32)


def dot_tn(a, b):
    return lax.dot_general(a, b, (((0,), (0,)), ((), ())), preferred_element_type=f32)


def step_embedding(timesteps, model_width):
    half_width = model_width // 2
    frequency = jnp.exp(-math.log(10000.0) * jnp.arange(half_width, dtype=jnp.float32) / half_width)
    angles = timesteps.astype(jnp.float32)[:, None] * frequency[None, :]
    return jnp.concatenate([jnp.cos(angles), jnp.sin(angles)], axis=1)


def normalize(values):
    centred = values - jnp.mean(values, axis=-1, keepdims=True)
    inverse = lax.rsqrt(jnp.mean(centred * centred, axis=-1, keepdims=True) + EPSILON)
    return (centred * inverse, inverse)


def normalize_back(incoming, normed, inverse):
    return inverse * (
        incoming
        - jnp.mean(incoming, axis=-1, keepdims=True)
        - normed * jnp.mean(incoming * normed, axis=-1, keepdims=True)
    )


D = 1152
DC, DZ, TD = D // 8, D // 4, D // 4
HD = D // HEADS
HC = HEADS // 2
WC = D // 2
FF = 4608
NF = 3
FB = FF // 2 // NF
FZ = FB // 4
L = 1024
LH = L // 2
LB = L // 4
G1R = 3 * DC
G2R = 2 * FZ + FZ // 4
PR = 2 * DC + DC // 3
PA = 176
QR = 7 * DC + 16
QA = QR // 2
VMEM_LIMIT = 58 * 1024 * 1024


ANY = pl.BlockSpec(memory_space=pl.ANY)
MESH = pl.DeviceIdType.MESH


def place():
    b, t = lax.axis_index("bucket"), lax.axis_index("tok")
    return b // 2, b % 2, t // 2, t % 2


def flip(value, other):
    return (value // 2 + other // 2) % 2 * 2 + (value % 2 + other % 2) % 2


def peer(name):
    z, c, y, x = place()
    if name == "x":
        x = 1 - x
    elif name == "y":
        y = 1 - y
    elif name == "xy":
        x, y = 1 - x, 1 - y
    elif name == "c":
        c = 1 - c
    elif name in ("t0", "t1"):
        c, y, x = y, c, x if name == "t0" else 1 - x
    else:
        z = flip(z, int(name[1]))
    return (z * 2 + c, y * 2 + x)


def meet(names):
    sem = pltpu.get_barrier_semaphore()
    others = [name for name in names if name != "t0"]
    for name in others:
        pl.semaphore_signal(sem, inc=1, device_id=peer(name), device_id_type=MESH)
    wanted = len(others)
    if "t0" in names:
        _, c, y, _ = place()
        wanted = wanted + (c + y) % 2

        @pl.when(c != y)
        def _():
            pl.semaphore_signal(sem, inc=1, device_id=peer("t0"), device_id_type=MESH)

    pl.semaphore_wait(sem, wanted)


def remote(src, dst, sems, k, name):
    return pltpu.make_async_remote_copy(
        src_ref=src, dst_ref=dst, send_sem=sems.at[0, k], recv_sem=sems.at[1, k],
        device_id=peer(name), device_id_type=MESH,
    )


def vm(*shape, dtype=bf16):
    return pltpu.VMEM(shape, dtype)


class FirstSum:
    peers = ("x", "y")

    def __init__(self, keep_a, sent_a, keep_b, sent_b):
        self.ins = [keep_a, sent_a, keep_b, sent_b]
        shapes = [keep.shape[1:] for keep in (keep_a, keep_b)]
        self.outs = [jax.ShapeDtypeStruct(s, bf16) for s in shapes for _ in range(2)]
        self.scratch = [vm(*s) for s in shapes for _ in range(3)]
        self.scratch += [pltpu.SemaphoreType.DMA((2, 4)), pltpu.SemaphoreType.DMA((4,))]

    def plan(self, ins, outs, scratch):
        ka, sa, kb, sb = ins
        _, qa, _, qb = outs
        kav, rav, _, kbv, rbv, _, sems, local = scratch
        far = [
            remote(sa.at[1], rav, sems, 0, "x"),
            remote(sb.at[1], rbv, sems, 1, "y"),
            remote(sa.at[0], qa, sems, 2, "x"),
            remote(sb.at[0], qb, sems, 3, "y"),
        ]
        near = [
            pltpu.make_async_copy(ka.at[1], kav, local.at[0]),
            pltpu.make_async_copy(kb.at[1], kbv, local.at[1]),
        ]
        return far, near

    def finish(self, ins, outs, scratch):
        kav, rav, oav, kbv, rbv, obv, _, local = scratch
        oav[...] = (kav[...].astype(f32) + rav[...].astype(f32)).astype(bf16)
        obv[...] = (kbv[...].astype(f32) + rbv[...].astype(f32)).astype(bf16)
        return [
            pltpu.make_async_copy(oav, outs[0], local.at[2]),
            pltpu.make_async_copy(obv, outs[2], local.at[3]),
        ]


class SecondSum:
    peers = ("x", "y")

    def __init__(self, on_a, q_a, on_b, q_b, keep_a, keep_b):
        self.ins = [on_a, q_a, on_b, q_b, keep_a, keep_b]
        self.rows = [on_a.shape[1], on_b.shape[1]]
        total = sum(self.rows)
        self.outs = [jax.ShapeDtypeStruct((3, total, LANES), bf16), jax.ShapeDtypeStruct((total, LANES), f32)]
        self.scratch = [vm(4, r, LANES) for r in self.rows for _ in range(3)]
        self.scratch += [vm(3, total, LANES), vm(total, LANES, dtype=f32)]
        self.scratch += [pltpu.SemaphoreType.DMA((2, 2)), pltpu.SemaphoreType.DMA((6,))]

    def plan(self, ins, outs, scratch):
        oa, qa, ob, qb, ka, kb = ins
        kav, qav, rav, kbv, qbv, rbv, _, _, sems, local = scratch
        far = [remote(oa, rav, sems, 0, "y"), remote(ob, rbv, sems, 1, "x")]
        pairs = [(ka.at[0], kav), (qa, qav), (kb.at[0], kbv), (qb, qbv)]
        return far, [pltpu.make_async_copy(a, b, local.at[k]) for k, (a, b) in enumerate(pairs)]

    def finish(self, ins, outs, scratch):
        zs, zk, local = scratch[6], scratch[7], scratch[9]
        start = 0
        for k, r in enumerate(self.rows):
            kv, qv, rv = scratch[3 * k : 3 * k + 3]
            for j in range(4):
                total = kv[j].astype(f32) + qv[j].astype(f32) + rv[j].astype(f32)
                if j == 0:
                    zk[start : start + r, :] = total
                else:
                    zs[j - 1, start : start + r, :] = total.astype(bf16)
            start += r
        return [
            pltpu.make_async_copy(zs, outs[0], local.at[4]),
            pltpu.make_async_copy(zk, outs[1], local.at[5]),
        ]


class ThirdSum:
    peers = ("z1", "z2", "z3")

    def __init__(self, sent, kept):
        self.ins = [sent, kept]
        self.outs = [jax.ShapeDtypeStruct(kept.shape, f32)]
        self.scratch = [vm(*sent.shape), vm(*kept.shape, dtype=f32)]
        self.scratch += [pltpu.SemaphoreType.DMA((2, 3)), pltpu.SemaphoreType.DMA((2,))]

    def plan(self, ins, outs, scratch):
        got, kept, sems, local = scratch
        far = [remote(ins[0].at[k], got.at[k], sems, k, f"z{k + 1}") for k in (2, 1, 0)]
        return far, [pltpu.make_async_copy(ins[1], kept, local.at[0])]

    def finish(self, ins, outs, scratch):
        got, kept, _, local = scratch
        kept[...] = kept[...] + got[0].astype(f32) + got[1].astype(f32) + got[2].astype(f32)
        return [pltpu.make_async_copy(kept, outs[0], local.at[1])]


def call(kernel, name, out_shape, args, in_specs=None, out_specs=None, scratch=(), grid=None,
         peers=(), jobs=(), cid=None, flops=0, nbytes=0):
    whole = pl.BlockSpec(memory_space=pltpu.VMEM)
    single = not isinstance(out_shape, (tuple, list))
    out_shape = [out_shape] if single else list(out_shape)
    in_specs = list(in_specs) if in_specs is not None else [whole] * len(args)
    out_specs = [whole] * len(out_shape) if out_specs is None else [out_specs] if single else list(out_specs)
    counts = [len(args), sum(len(j.ins) for j in jobs), len(out_shape), sum(len(j.outs) for j in jobs), len(scratch)]
    names = sorted(set(peers).union(*[j.peers for j in jobs]))

    def run(*refs):
        groups, at = [], 0
        for n in counts:
            groups.append(refs[at : at + n])
            at += n
        bound, ai, ao, asc = [], 0, 0, at
        for j in jobs:
            bound.append((
                j, groups[1][ai : ai + len(j.ins)], groups[3][ao : ao + len(j.outs)], refs[asc : asc + len(j.scratch)]
            ))
            ai, ao, asc = ai + len(j.ins), ao + len(j.outs), asc + len(j.scratch)

        def begin():
            if names:
                meet(names)
            for j, *r in bound:
                for group in j.plan(*r):
                    for copy in group:
                        copy.start()

        def end():
            last = []
            for j, *r in bound:
                far, near = j.plan(*r)
                for copy in far:
                    copy.wait()
                for copy in near:
                    copy.wait()
                copies = j.finish(*r)
                for copy in copies:
                    copy.start()
                last += copies
            for copy in last:
                copy.wait()

        if grid is None:
            begin()
            kernel(*groups[0], *groups[2], *groups[4])
            end()
        else:
            pl.when(pl.program_id(0) == 0)(begin)
            kernel(*groups[0], *groups[2], *groups[4])
            pl.when(pl.program_id(0) == grid[0] - 1)(end)

    extra = {} if grid is None else {"grid": grid}
    params = {"collective_id": cid, "has_side_effects": True} if names else {}
    outs = pl.pallas_call(
        run,
        out_shape=out_shape + [o for j in jobs for o in j.outs],
        in_specs=in_specs + [ANY] * counts[1],
        out_specs=out_specs + [ANY] * counts[3],
        scratch_shapes=list(scratch) + [q for j in jobs for q in j.scratch],
        compiler_params=pltpu.CompilerParams(vmem_limit_bytes=VMEM_LIMIT, **params),
        cost_estimate=pl.CostEstimate(flops=int(flops), bytes_accessed=int(nbytes), transcendentals=0),
        name=name,
        **extra,
    )(*args, *[a for j in jobs for a in j.ins])
    own, rest, given = outs[: len(out_shape)], outs[len(out_shape) :], []
    for j in jobs:
        given.append(rest[: len(j.outs)])
        rest = rest[len(j.outs) :]
    return (own[0] if single else own), given


def full(shape):
    return pl.BlockSpec(shape, lambda *_: (0,) * len(shape))


def once(*shape):
    return pl.BlockSpec(shape, lambda *_: (0,) * len(shape), pipeline_mode=pl.Buffered(1))


def rows(block, width):
    return pl.BlockSpec((block, width), lambda i: (i, 0))


def column(n):
    return lax.broadcasted_iota(jnp.int32, (n, 1), 0)


def front_kernel(tokens, cotangent, ints, ada_w, ada_b, freq, heads_t, channels_t, w_qkv, w_fc1, q_bias, v_bias, b1,
                 tok_o, cot_o, shifted_o, qkv_o, wq_o, w1_o, mod_o, kept_o, hmask_o, chan_o, b1_o,
                 tk, ck, wqv, wqc, w1v, w1c, adav, ints_other, m4, to_send, shares, csems, tsems, ssems, lsems):
    z, c, y, x = place()
    t = 2 * y + x
    loads = [
        pltpu.make_async_copy(a, b, lsems.at[k])
        for k, (a, b) in enumerate(((ada_w, adav), (w_qkv, wqv), (w_fc1, w1v)))
    ]

    def arrivals(src, dst, k):
        block = [dst.at[pl.ds(LB * j, LB)] for j in range(4)]
        first = remote(src.at[x], block[0], tsems, k, "t0")
        stay = pltpu.make_async_copy(src.at[x], block[0], lsems.at[3 + k])
        second = remote(src.at[1 - x], block[1], tsems, 2 + k, "t1")
        onward = [remote(block[j], block[2 + j], csems, 2 * k + j, "c") for j in range(2)]
        return first, stay, second, onward

    def leave(first, stay, second, onward):
        pl.when(c != y)(first.start)
        pl.when(c == y)(stay.start)
        second.start()

    def pass_on(first, stay, second, onward):
        pl.when(c != y)(first.wait_recv)
        pl.when(c == y)(stay.wait)
        onward[0].start()
        second.wait_recv()
        onward[1].start()

    def settle(first, stay, second, onward):
        pl.when(c != y)(first.wait_send)
        second.wait_send()
        for copy in onward:
            copy.wait_send()

    tok_moves, cot_moves = arrivals(tokens, tk, 0), arrivals(cotangent, ck, 1)
    leave(*tok_moves)
    swap = remote(ints, ints_other, csems, 4, "c")
    swap.start()
    for load in loads:
        load.start()
    swap.wait()

    mine, other = ints[...], ints_other[...]
    mine_t, other_t = mine[4:5, :].astype(f32), other[4:5, :].astype(f32)
    r = column(8)
    steps = jnp.zeros((8, 1), f32)
    for k in range(2):
        steps = jnp.where(r == 2 * c + k, mine_t[:, k : k + 1], steps)
        steps = jnp.where(r == 2 * (1 - c) + k, other_t[:, k : k + 1], steps)
    angles = steps * freq[...]
    condition = jax.nn.silu(jnp.concatenate([jnp.cos(angles), jnp.sin(angles)], axis=1))
    condition = jnp.concatenate([condition, jnp.zeros_like(condition)], axis=0).astype(bf16)
    loads[0].wait()
    m4[...] = dot_nn(condition, adav[...])[:8] + ada_b[...].astype(f32)
    moves = []
    for k in range(4):
        to = (y + k // 2) % 2 * 2 + (x + k) % 2
        row = jnp.broadcast_to(m4[pl.ds(to, 1), :], to_send.shape[1:])
        if k == 0:
            shares[t] = row
        else:
            to_send[k - 1] = row
            moves.append(remote(to_send.at[k - 1], shares.at[t], ssems, k - 1, ("x", "y", "xy")[k - 1]))
            moves[-1].start()

    group = jnp.where(c == y, mine, other)
    bucket = group[4:5, 2:3]
    skip = jnp.where(x == 0, group[0:2], group[2:4])
    for j in range(4):
        block = 2 * ((c + j // 2) % 2) + (x + j) % 2
        position = column(LB) + LB * block
        hit = jnp.where((position == skip[0:1, :]) | (position == skip[1:2, :]), 1.0, 0.0)
        kept_o[LB * j : LB * (j + 1), :] = 1.0 - jnp.max(hit, axis=1, keepdims=True)

    def chosen(masks):
        lane = lax.broadcasted_iota(jnp.int32, masks.shape, 1)
        return jnp.sum(jnp.where(lane == bucket, masks[...].astype(f32), 0.0), axis=1, keepdims=True)

    def spread(on, low, width):
        first = width * lax.broadcasted_iota(jnp.int32, (on.shape[0], low.shape[1]), 0)
        return jnp.sum(jnp.where((low >= first) & (low < first + width), on, 0.0), axis=0, keepdims=True)

    lane = lax.broadcasted_iota(jnp.int32, (1, WC), 1)
    share = sum(jnp.where(lane >= DC * k, 1, 0) for k in range(1, 4))
    hmask_o[...] = spread(chosen(heads_t), lane + DC * (share + c), HD)
    channels = chosen(channels_t)
    lane = lax.broadcasted_iota(jnp.int32, (1, FB), 1)
    share = sum(jnp.where(lane >= FZ * k, 1, 0) for k in range(1, 4))
    for f in range(NF):
        low = lane + (4 * DZ - FZ) * share + FF // 8 * c + FZ * f
        chan_o[f] = spread(channels, low, FF // channels.shape[0])

    def half(v, k, width):
        v = v[:, 2 * width * k : 2 * width * (k + 1)].astype(f32)
        return jnp.where(c == 0, v[:, :width], v[:, width:])

    bias = [half(q_bias[...], k, DC) for k in range(4)]
    bias += [jnp.zeros((1, WC), f32)] + [half(v_bias[...], k, DC) for k in range(4)]
    bias = jnp.concatenate(bias, axis=1)
    b1v = [half(b1[...], k, FF // 8) for k in range(4)]
    for f in range(NF):
        b1_o[f] = jnp.concatenate([v[:, FZ * f : FZ * (f + 1)] for v in b1v], axis=1)
    loads[1].wait()
    loads[2].wait()
    for core in range(2):

        @pl.when(c == core)
        def _():
            for k in range(12):
                wqc[:, DC * k : DC * (k + 1)] = wqv[:, DZ * k + DC * core : DZ * k + DC * (core + 1)]
            for f in range(NF):
                for k in range(4):
                    start = 4 * DZ * k + FF // 8 * core + FZ * f
                    w1c[f, :, FZ * k : FZ * (k + 1)] = w1v[:, start : start + FZ]

    stores = [
        pltpu.make_async_copy(a, b, lsems.at[k]) for k, (a, b) in enumerate(((wqc, wq_o), (w1c, w1_o)))
    ]
    for store in stores:
        store.start()
    pass_on(*tok_moves)
    leave(*cot_moves)
    for copy in moves:
        copy.wait()
    share_rows = [shares[k][0:1, :] for k in range(4)]
    n, m = D // 2, 3 * D // 2
    mod = [share_rows[0][:, :D], jnp.concatenate([share_rows[0][:, D:], share_rows[1][:, :n]], axis=1),
           share_rows[1][:, n:], share_rows[2][:, :D],
           jnp.concatenate([share_rows[2][:, D:], share_rows[3][:, :n]], axis=1), share_rows[3][:, n:]]
    own_step = 0.5 * jnp.sum(jnp.where(r == t, steps, 0.0), axis=0, keepdims=True)
    mod += [jnp.broadcast_to(own_step, (1, D)), jnp.zeros((1, D), f32)]
    mod_o[...] = jnp.concatenate(mod, axis=0)
    for j in range(4):
        if j >= 2:
            tok_moves[3][j - 2].wait_recv()
        part = slice(LB * j, LB * (j + 1))
        normed, _ = normalize(tk[part, :].astype(f32))
        shifted = (normed * (1.0 + mod[1]) + mod[0]).astype(bf16)
        shifted_o[part, :] = shifted
        qkv_o[part, :] = (dot_nn(shifted, wqc[...]) + bias).astype(bf16)
    keep = pltpu.make_async_copy(tk, tok_o, lsems.at[2])
    keep.start()
    pass_on(*cot_moves)
    for copy in cot_moves[3]:
        copy.wait_recv()
    keep_cot = pltpu.make_async_copy(ck, cot_o, lsems.at[5])
    keep_cot.start()
    settle(*tok_moves)
    settle(*cot_moves)
    for store in stores:
        store.wait()
    keep.wait()
    keep_cot.wait()


def attn_kernel(step, qkv, hmask, wp, bias, tok, mod, mixed_o, shifted2_o, attn_o,
                qh, kh, vh, mx, mo, wpv, tkv, csems, lsems):
    c = place()[1]
    loads = [
        pltpu.make_async_copy(wp.at[:, c], wpv.at[0], lsems.at[0]),
        pltpu.make_async_copy(wp.at[:, 1 - c], wpv.at[1], lsems.at[1]),
        pltpu.make_async_copy(tok, tkv, lsems.at[2]),
    ]
    for load in loads:
        load.start()
    scale = LOG2E / math.sqrt(HD)
    for h in range(HC):
        for k, ref in enumerate((qh, kh, vh)):
            ref[h] = qkv[:, WC * k + HD * h : WC * k + HD * (h + 1)]

    def crossing(i):
        src = mx.at[pl.ds(pl.multiple_of(i * step, step), step)]
        dst = mo.at[pl.ds(pl.multiple_of((i * step + LH) % L, step), step)]
        return remote(src, dst, csems, i, "c")

    def body(i, carry):
        part = pl.ds(pl.multiple_of(i * step, step), step)
        outs = []
        for h in range(HC):
            s = dot_nt(qh[h, part, :], kh[h])
            top = jnp.max(s, axis=1, keepdims=True)
            p = jnp.exp2((s - top) * scale)
            total = jnp.sum(p, axis=1, keepdims=True)
            outs.append(dot_nn(p.astype(bf16), vh[h]) * (1.0 / total))
        mx[part, :] = (jnp.concatenate(outs, axis=1) * hmask[...]).astype(bf16)
        crossing(i).start()
        return carry

    lax.fori_loop(0, L // step, body, 0)
    keep = pltpu.make_async_copy(mx, mixed_o, lsems.at[3])
    keep.start()
    for load in loads:
        load.wait()
    for i in range(L // step):
        crossing(i).wait()
    w_mine, w_other = wpv[0].reshape(WC, D), wpv[1].reshape(WC, D)
    for j in range(4):
        part = slice(LB * j, LB * (j + 1))
        attn = dot_nn(mx[part, :], w_mine) + dot_nn(mo[part, :], w_other) + bias[...]
        if j < 2:
            attn_o[part, :] = attn
        normed, _ = normalize(tkv[part, :].astype(f32) + mod[2:3, :] * attn)
        shifted2_o[part, :] = (normed * (1.0 + mod[4:5, :]) + mod[3:4, :]).astype(bf16)
    keep.wait()


def pack_hidden(block1, block2, o1, o2, ry, rx, rz):
    o1[ry, rz, : 2 * DC, :] = block1[:, :LANES]
    o1[ry, rz, 2 * DC :, :] = jnp.concatenate([block1[:DC, LANES:], block1[DC:, LANES:]], axis=1)
    o2[rx, rz, :FZ, :] = block2[:, :LANES]
    o2[rx, rz, FZ : 2 * FZ, :] = block2[:, LANES : 2 * LANES]
    q = FZ // 4
    o2[rx, rz, 2 * FZ :, :] = jnp.concatenate([block2[q * k : q * (k + 1), 2 * LANES :] for k in range(4)], axis=1)


def mlp_kernel(f, *refs):
    last = f == NF - 1
    refs = list(refs)
    sh2, g, kept, mod, w1, b1, chan, w2 = refs[:8]
    del refs[:8]
    before = None
    if f > 0:
        before = refs[:2]
        del refs[:2]
    slots, branch_o, ds2_o, sum1_o, sum2_o = refs[:4], refs[4], refs[5], refs[6], refs[7]
    del refs[:8]
    if last:
        got = refs[:2]
        del refs[:2]
    hid, dpre, dbs, w2v, t1, t2, s1k, s1s, s2k, s2s, sems = refs[:11]
    if last:
        far, csems = refs[11:]
        crossing = [remote(far.at[k], got[k], csems, k, "c") for k in range(2)]
    stages = (s1k, s1s, s2k, s2s)
    i = pl.program_id(0)
    z, c, y, x = place()

    @pl.when(i == 0)
    def _():
        copy = pltpu.make_async_copy(w2.at[:, c, f], w2v, sems.at[4])
        copy.start()
        copy.wait()

    part = pl.ds(pl.multiple_of((1 - i) * LH, LH), LH)
    w1v = w1[0]
    w2f = w2v[...].reshape(FB, D)
    db = (g[...].astype(f32) * mod[5:6, :] * kept[...]).astype(bf16)
    dbs[part, :] = db
    v = dot_nn(sh2[part, :], w1v) + b1[0]
    v2 = v * v
    th = jnp.tanh(GELU_K * v * (1.0 + GELU_C * v2))
    half = 0.5 * (1.0 + th)
    on = chan[0]
    hidden = (v * half * on).astype(bf16)
    hid[part, :] = hidden
    slope = (half + (0.5 * GELU_K) * v * (1.0 - th * th) * (1.0 + (3.0 * GELU_C) * v2)) * on
    d_pre = (dot_nt(db, w2f) * slope).astype(bf16)
    dpre[part, :] = d_pre
    branch, ds2 = dot_nn(hidden, w2f), dot_nt(d_pre, w1v)
    if before is not None:
        branch = branch + before[0][...].astype(f32)
        ds2 = ds2 + before[1][...].astype(f32)
    branch, ds2 = branch.astype(bf16), ds2.astype(bf16)
    if last:

        @pl.when(i == 0)
        def _():
            far[0] = branch
            far[1] = ds2
            for copy in crossing:
                copy.start()

        @pl.when(i == 1)
        def _():
            branch_o[...] = branch
            ds2_o[...] = ds2
    else:
        branch_o[...] = branch
        ds2_o[...] = ds2
    s1 = jnp.sum(d_pre.astype(f32), axis=0, keepdims=True)
    s2 = jnp.sum(db.astype(f32), axis=0, keepdims=True)

    @pl.when(i == 0)
    def _():
        sum1_o[...] = s1
        sum2_o[...] = s2

    @pl.when(i == 1)
    def _():
        sum1_o[...] += s1
        sum2_o[...] += s2
        for m in range(3):
            cut = slice(m * D // 3, (m + 1) * D // 3)
            p = dot_tn(sh2[:, cut], dpre[...]).astype(bf16)
            for t in range(4):
                t1[t, cut, :] = p[:, FZ * t : FZ * (t + 1)]
        for m in range(3):
            cut = slice(m * FB // 3, (m + 1) * FB // 3)
            p = dot_tn(hid[:, cut], dbs[...]).astype(bf16)
            for t in range(4):
                t2[t, cut, :] = p[:, TD * t : TD * (t + 1)]
        for rz in range(4):
            zz = flip(z, rz)
            for ry in range(2):
                for rx in range(2):
                    tt = (ry + y) % 2 * 2 + (rx + x) % 2
                    one = [
                        t1[tt, pl.ds(pl.multiple_of(zz * DZ + (rc + c) % 2 * DC, 16), DC), :] for rc in range(2)
                    ]
                    two = t2[tt, pl.ds(pl.multiple_of(zz * FZ, 16), FZ), :]
                    pack_hidden(jnp.concatenate(one, axis=0), two, (s1k, s1s)[rx], (s2k, s2s)[ry], ry, rx, rz)
        copies = [pltpu.make_async_copy(a, b, sems.at[k]) for k, (a, b) in enumerate(zip(stages, slots))]
        for copy in copies:
            copy.start()
        for copy in copies:
            copy.wait()
        if last:
            for copy in crossing:
                copy.wait()


def middle_kernel(ds, ds_r, br, br_r, attn, tok, g, kept, mod, bias2, mixed, wp,
                  d_resid_o, out, dh_o, pka, psa, pkb, psb, sums_o, sum_o, da, ob, t1, wpv, csems, tsems, lsems):
    i = pl.program_id(0)
    n = LH // 4
    z, c, y, x = place()
    part = pl.ds(pl.multiple_of(i * n, n), n)
    gf, at = g[...].astype(f32), attn[...]
    resid = tok[...].astype(f32) + mod[2:3, :] * at
    normed2, inverse2 = normalize(resid)
    ds2 = ds[...].astype(f32) + ds_r[...].astype(f32)
    kb = kept[...] * (br[...].astype(f32) + br_r[...].astype(f32) + bias2[...])
    ob[part, :] = (resid + mod[5:6, :] * kb).astype(bf16)
    d_resid = gf + normalize_back(ds2 * (1.0 + mod[4:5, :]), normed2, inverse2)
    d_resid_o[...] = d_resid
    da[part, :] = (mod[2:3, :] * d_resid).astype(bf16)
    sums = [jnp.sum(p, axis=0, keepdims=True) for p in (at * d_resid, ds2, ds2 * normed2, kb * gf)]
    sums = jnp.concatenate(sums + [jnp.zeros((4, D), f32)], axis=0)

    @pl.when(i == 0)
    def _():
        sums_o[...] = sums

    @pl.when(i > 0)
    def _():
        sums_o[...] += sums

    crossing = [
        remote(da.at[pl.ds(n * k, n)], da.at[pl.ds(LH + n * k, n)], csems, k, "c") for k in range(4)
    ]
    home0 = remote(ob.at[pl.ds(0, LB)], out.at[x], tsems, 0, "t0")
    stay0 = pltpu.make_async_copy(ob.at[pl.ds(0, LB)], out.at[x], lsems.at[0])
    load = pltpu.make_async_copy(wp.at[:, c], wpv, lsems.at[1])
    pl.when(i == 0)(load.start)
    home1 = remote(ob.at[pl.ds(LB, LB)], out.at[x], tsems, 1, "t1")
    for k in range(4):

        @pl.when(i == k)
        def _():
            crossing[k].start()
            if k == 1:
                pl.when(c != y)(home0.start)
                pl.when(c == y)(stay0.start)
            if k == 3:
                home1.start()

    @pl.when(i == 3)
    def _():
        for copy in crossing:
            copy.wait()
        load.wait()
        wv = wpv[...].reshape(WC, D)
        dh_o[...] = dot_nt(da[...], wv).astype(bf16)
        sum_o[...] = dot_nn(jnp.ones((16, L), bf16), da[...])[:8]
        grad = dot_tn(mixed[...], da[...]).astype(bf16)
        for t in range(4):
            t1[t] = grad[:, TD * t : TD * (t + 1)]
        for rz in range(4):
            zz = flip(z, rz)
            for ry in range(2):
                for rx in range(2):
                    tt = (ry + y) % 2 * 2 + (rx + x) % 2
                    a, b = (pka, psa)[rx], (pkb, psb)[ry]
                    block = t1[tt, pl.ds(pl.multiple_of(zz * DC, 16), DC), :]
                    a[ry, rz, :DC, :] = block[:, :LANES]
                    a[ry, rz, DC:, :] = block[: PA - DC, LANES : 2 * LANES]
                    b[rx, rz, : 2 * DC - PA, :] = block[PA - DC :, LANES : 2 * LANES]
                    q = DC // 3
                    tails = [block[q * k : q * (k + 1), 2 * LANES :] for k in range(3)]
                    tails.append(jnp.zeros((q, 32), bf16))
                    b[rx, rz, 2 * DC - PA :, :] = jnp.concatenate(tails, axis=1)
        pl.when(c != y)(home0.wait)
        pl.when(c == y)(stay0.wait)
        home1.wait()


def attn_back_kernel(step, qkv, dh, hmask, out, qh, kh, vh, doh, dk, dv):
    scale = LOG2E / math.sqrt(HD)
    for h in range(HC):
        for k, ref in enumerate((qh, kh, vh)):
            ref[h] = qkv[:, WC * k + HD * h : WC * k + HD * (h + 1)]
        cut = slice(HD * h, HD * (h + 1))
        doh[h] = (dh[:, cut].astype(f32) * hmask[:, cut]).astype(bf16)
    dk[...] = jnp.zeros_like(dk)
    dv[...] = jnp.zeros_like(dv)

    def body(i, carry):
        part = pl.ds(pl.multiple_of(i * step, step), step)
        outs = []
        for h in range(HC):
            q, do = qh[h, part, :], doh[h, part, :]
            s = dot_nt(kh[h], q)
            top = jnp.max(s, axis=0, keepdims=True)
            p = jnp.exp2((s - top) * scale)
            p = p * (1.0 / jnp.sum(p, axis=0, keepdims=True))
            dp = dot_nt(vh[h], do)
            row_dot = jnp.sum(p * dp, axis=0, keepdims=True)
            ds = (p * (dp - row_dot)).astype(bf16)
            dv[h] += dot_nn(p.astype(bf16), do)
            dk[h] += dot_nn(ds, q)
            outs.append(dot_tn(ds, kh[h]))
        out[part, :WC] = (jnp.concatenate(outs, axis=1) * (1.0 / math.sqrt(HD))).astype(bf16)
        return carry

    lax.fori_loop(0, L // step, body, 0)
    for h in range(HC):
        out[:, WC + HD * h : WC + HD * (h + 1)] = (dk[h] * (1.0 / math.sqrt(HD))).astype(bf16)
        out[:, 2 * WC + HD * h : 2 * WC + HD * (h + 1)] = dv[h].astype(bf16)


def qkv_grad_kernel(shifted, dqkv, extra, ka, sa, kb, sb, t1):
    z, c, y, x = place()
    for k in range(4):
        grad = dot_tn(shifted[:, DZ * k : DZ * (k + 1)], dqkv[...]).astype(bf16)
        for t in range(4):
            t1[t, DZ * k : DZ * (k + 1), :] = grad[:, 3 * DC * t : 3 * DC * (t + 1)]
    sums = dot_nn(jnp.ones((16, L), bf16), dqkv[...])[0:1, :]
    for zs in range(4):
        for ts in range(4):
            piece = DC * zs + DC // 4 * ts
            qsum = sums[:, piece : piece + DC // 4]
            vsum = sums[:, 2 * WC + piece : 2 * WC + piece + DC // 4]
            row1 = jnp.concatenate([jnp.zeros((1, 88), f32), qsum, jnp.zeros((1, 4), f32)], axis=1)
            row2 = jnp.concatenate([vsum, jnp.zeros((1, LANES - DC // 4), f32)], axis=1)
            add = jnp.concatenate([jnp.zeros((1, LANES), f32), row1, row2, jnp.zeros((13, LANES), f32)], axis=0)
            rz, ry, rx = flip(z, zs), (ts // 2 + y) % 2, (ts % 2 + x) % 2
            block = (extra[zs, ts] + add).astype(bf16)

            @pl.when(ry == 0)
            def _():
                kb[rx, rz, QA - 16 :, :] = block

            @pl.when(ry == 1)
            def _():
                sb[rx, rz, QA - 16 :, :] = block

    for rz in range(4):
        zz = flip(z, rz)
        for ry in range(2):
            for rx in range(2):
                tt = (ry + y) % 2 * 2 + (rx + x) % 2
                a, b = (ka, sa)[rx], (kb, sb)[ry]
                parts = [
                    t1[tt, pl.ds(pl.multiple_of(zz * DZ + (rc + c) % 2 * DC, 16), DC), :] for rc in range(2)
                ]
                strips = [p[:, LANES * k : LANES * (k + 1)] for k in range(3) for p in parts]
                gap = jnp.zeros((DC, 16), bf16)
                strips.append(jnp.concatenate([parts[0][:, 3 * LANES :], gap, parts[1][:, 3 * LANES :], gap], axis=1))
                for k, strip in enumerate(strips):
                    first = DC * k
                    if first + DC <= QA:
                        a[ry, rz, first : first + DC, :] = strip
                    elif first >= QA:
                        b[rx, rz, first - QA : first - QA + DC, :] = strip
                    else:
                        a[ry, rz, first:, :] = strip[: QA - first]
                        b[rx, rz, : first + DC - QA, :] = strip[QA - first :]


def tail_kernel(dqkv, w, d_resid, tok, mod, sums_mid, grad, item_o, got, far, gb, other, csems, tsems, lsem):
    i = pl.program_id(0)
    c, y, x = place()[1:]
    d_shifted = dot_nt(dqkv[...], w[...])
    crossing = [remote(far.at[k], got.at[k], csems, k, "c") for k in range(2)]
    sums_over = remote(item_o, other, csems, 2, "c")
    home0 = remote(gb.at[0], grad.at[x], tsems, 0, "t0")
    stay0 = pltpu.make_async_copy(gb.at[0], grad.at[x], lsem)
    home1 = remote(gb.at[1], grad.at[x], tsems, 1, "t1")
    for k in range(2):

        @pl.when(i == k)
        def _():
            far[k] = d_shifted.astype(bf16)
            crossing[k].start()

        @pl.when(i == k + 2)
        def _():
            crossing[k].wait()
            total = d_shifted + got[k].astype(f32)
            normed, inverse = normalize(tok[...].astype(f32))
            back = d_resid[...] + normalize_back(total * (1.0 + mod[1:2, :]), normed, inverse)
            gb[k] = back.astype(bf16)
            sums = [jnp.sum(p, axis=0, keepdims=True) for p in (total, total * normed)]
            if k == 0:
                pl.when(c != y)(home0.start)
                pl.when(c == y)(stay0.start)
                item_o[...] = jnp.concatenate(sums + [sums_mid[0:4, :], mod[6:8, :]], axis=0)
            else:
                home1.start()
                item_o[0:2, :] += jnp.concatenate(sums, axis=0)
                sums_over.start()
                sums_over.wait()
                item_o[...] += other[...]
                pl.when(c != y)(home0.wait)
                pl.when(c == y)(stay0.wait)
                home1.wait()


def square_kernel(item, square, sems, lsem):
    t = lax.axis_index("tok")
    here = pltpu.make_async_copy(item, square.at[t], lsem)
    copies = [remote(item, square.at[t], sems, k, name) for k, name in enumerate(("x", "y", "xy"))]
    here.start()
    for copy in copies:
        copy.start()
    here.wait()
    for copy in copies:
        copy.wait()


def every_kernel(square, every, sems, lsem):
    z = place()[0]
    here = pltpu.make_async_copy(square, every.at[z], lsem)
    copies = [remote(square, every.at[z], sems, k, f"z{k + 1}") for k in range(3)]
    here.start()
    for copy in copies:
        copy.start()
    here.wait()
    for copy in copies:
        copy.wait()


def finish_kernel(f0, f1, f2, fp, fq, gq_o, gp_o, g1_o, g2_o, mine, theirs, sems):
    c = place()[1]
    for f, ref in enumerate((f0, f1, f2)):
        mine[G1R * f : G1R * (f + 1), :] = ref[:G1R, :].astype(bf16)
    mine[NF * G1R :, :] = fq[: 7 * DC, :].astype(bf16)
    copy = remote(mine, theirs, sems, 0, "c")
    copy.start()

    def place_columns(own, q, first):
        columns = jnp.concatenate(q, axis=1)
        for core in range(2):

            @pl.when(c == core)
            def _():
                at = core if own else 1 - core
                for k in range(3):
                    gq_o[:, DZ * k + DC * at : DZ * k + DC * (at + 1)] = columns[:, DC * k : DC * (k + 1)]
                for f in range(NF):
                    start = FF // 8 * at + FZ * f
                    g1_o[:, start : start + FZ] = jnp.concatenate(first[f], axis=1)

    q = fq[...]
    place_columns(
        True,
        [q[0:DC], q[2 * DC : 3 * DC], q[4 * DC : 5 * DC], q[6 * DC : 7 * DC, : DC // 3]],
        [[f[:DC, :], f[2 * DC : 3 * DC, : FZ - LANES]] for f in (f0, f1, f2)],
    )
    for f, ref in enumerate((f0, f1, f2)):
        part = ref[G1R:, :]
        tail = part[2 * FZ :]
        tail = jnp.concatenate([tail[:, 32 * k : 32 * (k + 1)] for k in range(4)], axis=0)
        g2_o[FZ * f : FZ * (f + 1), :] = jnp.concatenate([part[:FZ], part[FZ : 2 * FZ], tail], axis=1)
    part = fp[...]
    tail = part[2 * DC :]
    tail = jnp.concatenate([tail[:, 32 * k : 32 * (k + 1)] for k in range(3)], axis=0)
    gp_o[...] = jnp.concatenate([part[:DC], part[DC : 2 * DC], tail], axis=1)
    copy.wait()
    got = theirs[...].astype(f32)
    q = got[NF * G1R :]
    place_columns(
        False,
        [q[DC : 2 * DC], q[3 * DC : 4 * DC], q[5 * DC : 6 * DC], q[6 * DC :, 64 : 64 + DC // 3]],
        [
            [got[G1R * f + DC : G1R * f + 2 * DC], got[G1R * f + 2 * DC : G1R * (f + 1), FZ - LANES :]]
            for f in range(NF)
        ],
    )


def one_item_per_chip(
    tokens, cotangent, timesteps, bucket_ids, head_masks, channel_masks, skip_rows,
    w_qkv, q_bias, v_bias, w_proj, proj_bias, w_fc1, fc1_bias, w_fc2, fc2_bias, ada_weight, ada_bias,
):
    b, t = lax.axis_index("bucket"), lax.axis_index("tok")
    z, c, y, x = b // 2, b % 2, t // 2, t % 2
    sds = jax.ShapeDtypeStruct

    def core_half(v, *dims):
        return lax.dynamic_index_in_dim(v.reshape(dims), c, 1, keepdims=False)

    vmem = pl.BlockSpec(memory_space=pltpu.VMEM)
    skips = skip_rows.reshape(-1, LANES)
    ints = jnp.concatenate([timesteps, bucket_ids, jnp.zeros((LANES - 3,), jnp.int32)]).reshape(1, LANES)
    ints = jnp.concatenate([skips, ints, jnp.zeros((7 - skips.shape[0], LANES), jnp.int32)], axis=0)
    freq = jnp.exp(-math.log(10000.0) * jnp.arange(D // 2, dtype=f32) / (D // 2)).reshape(1, D // 2)
    ada_cols = ada_weight.shape[1]
    front, _ = call(
        front_kernel, "front",
        (sds((L, D), bf16), sds((L, D), bf16), sds((L, D), bf16), sds((L, 3 * WC), bf16), sds((D, 3 * WC), bf16),
         sds((NF, D, FB), bf16), sds((8, D), f32), sds((L, 1), f32), sds((1, WC), f32), sds((NF, 1, FB), f32),
         sds((NF, 1, FB), f32)),
        (tokens, cotangent, ints, ada_weight, ada_bias.reshape(1, ada_cols), freq, head_masks.T, channel_masks.T,
         w_qkv, w_fc1, q_bias.reshape(1, D), v_bias.reshape(1, D), fc1_bias.reshape(1, FF)),
        in_specs=[ANY, ANY, vmem, ANY, vmem, vmem, vmem, vmem, ANY, ANY, vmem, vmem, vmem],
        out_specs=[ANY, ANY, vmem, vmem, ANY, ANY] + [vmem] * 5,
        scratch=[vm(L, D), vm(L, D), vm(D, 3 * D), vm(D, 3 * WC), vm(D, FF), vm(NF, D, FB), vm(D, ada_cols),
                 vm(8, LANES, dtype=jnp.int32), vm(8, ada_cols, dtype=f32), vm(3, 8, ada_cols, dtype=f32),
                 vm(4, 8, ada_cols, dtype=f32), pltpu.SemaphoreType.DMA((2, 5)), pltpu.SemaphoreType.DMA((2, 4)),
                 pltpu.SemaphoreType.DMA((2, 3)), pltpu.SemaphoreType.DMA((6,))],
        peers=("c", "t0", "t1", "x", "y", "xy"), cid=10, flops=2 * L * D * 3 * WC, nbytes=50e6,
    )
    tok, g_all, shifted, qkv, wq, w1, mod, kept, hmask, chan, b1 = front
    w2 = w_fc2.reshape(4, 2, NF, FZ, D)
    wp = w_proj.reshape(4, 2, DC, D)
    (mixed, shifted2, attn), _ = call(
        functools.partial(attn_kernel, 256), "attn",
        (sds((L, WC), bf16), sds((L, D), bf16), sds((LH, D), f32)),
        (qkv, hmask, wp, proj_bias.astype(f32).reshape(1, D), tok, mod),
        in_specs=[vmem, vmem, ANY, vmem, ANY, vmem],
        out_specs=[ANY, vmem, vmem],
        scratch=[vm(HC, L, HD)] * 3 + [vm(L, WC), vm(L, WC), vm(2, 4, DC, D), vm(L, D),
                 pltpu.SemaphoreType.DMA((2, 4)), pltpu.SemaphoreType.DMA((4,))],
        peers=("c",), cid=11, flops=16e9, nbytes=5e6,
    )

    firsts, kepts, sums1, results, before = [], [], [], [], []
    half = pl.BlockSpec((LH, D), lambda i: (1 - i, 0))
    slot1, slot2 = sds((2, 4, G1R, LANES), bf16), sds((2, 4, G2R, LANES), bf16)
    for f in range(NF):
        jobs = []
        if f > 0:
            jobs.append(FirstSum(*slots))
        if f > 1:
            jobs.append(SecondSum(*firsts[f - 2], *kepts[f - 2]))
        last = f == NF - 1
        pick = lambda i, f=f: (f, 0, 0)
        out_shape = [slot1, slot1, slot2, slot2] + [sds((LH if last else L, D), bf16)] * 2
        out_shape += [sds((1, FB), f32), sds((1, D), f32)] + [sds((LH, D), bf16)] * (2 * last)
        own, given = call(
            functools.partial(mlp_kernel, f), f"mlp{f}",
            out_shape, (shifted2, g_all, kept, mod, w1, b1, chan, w2, *before),
            grid=(2,),
            in_specs=[once(L, D), half, pl.BlockSpec((LH, 1), lambda i: (1 - i, 0)), full((8, D)),
                      pl.BlockSpec((1, D, FB), pick, pipeline_mode=pl.Buffered(1)),
                      pl.BlockSpec((1, 1, FB), pick), pl.BlockSpec((1, 1, FB), pick), ANY] + [half] * len(before),
            out_specs=[ANY] * 4 + [full((LH, D)) if last else half] * 2 + [full((1, FB)), full((1, D))]
            + [ANY] * (2 * last),
            scratch=[vm(L, FB), vm(L, FB), vm(L, D), vm(4, FZ, D), vm(4, D, FZ), vm(4, FB, TD)]
            + [vm(*s.shape) for s in (slot1, slot1, slot2, slot2)] + [pltpu.SemaphoreType.DMA((5,))]
            + ([vm(2, LH, D), pltpu.SemaphoreType.DMA((2, 2))] if last else []),
            peers=("c",) if last else (), jobs=jobs, cid=f,
            flops=12 * L * D * FB, nbytes=20e6,
        )
        slots, before = own[:4], own[4:6]
        kepts.append((slots[0], slots[2]))
        sums1.append(own[6])
        if f > 0:
            firsts.append(given[0])
        if f > 1:
            results.append(given[1])
    sum2 = own[7]
    branch_r, ds2_r = own[8:]

    n = LH // 4
    row = rows(n, D)
    slot_a, slot_b = sds((2, 4, PA, LANES), bf16), sds((2, 4, PR - PA, LANES), bf16)
    own, given = call(
        middle_kernel, "middle",
        (sds((LH, D), f32), sds((2, LB, D), bf16), sds((L, WC), bf16), slot_a, slot_a, slot_b, slot_b,
         sds((8, D), f32), sds((8, D), f32)),
        (before[1], ds2_r, before[0], branch_r, attn, tok, g_all, kept, mod, fc2_bias.astype(f32).reshape(1, D),
         mixed, wp),
        grid=(4,),
        in_specs=[row] * 7 + [rows(n, 1), full((8, D)), full((1, D)), once(L, WC), ANY],
        out_specs=(row, ANY, full((L, WC)), full(slot_a.shape), full(slot_a.shape), full(slot_b.shape),
                   full(slot_b.shape), full((8, D)), full((8, D))),
        scratch=[vm(L, D), vm(LH, D), vm(4, WC, TD), vm(4, DC, D), pltpu.SemaphoreType.DMA((2, 4)),
                 pltpu.SemaphoreType.DMA((2, 2)), pltpu.SemaphoreType.DMA((2,))],
        peers=("c", "t0", "t1"), cid=3,
        jobs=[FirstSum(*slots), SecondSum(*firsts[1], *kepts[1]), ThirdSum(*results[0])],
        flops=4 * L * D * WC, nbytes=20e6,
    )
    d_resid, output, dh, *slots_p, sums_mid, sum_attn = own
    firsts.append(given[0])
    results.append(given[1])
    finals = [given[2][0]]
    dqkv, given = call(
        functools.partial(attn_back_kernel, 512), "attn_back",
        sds((L, 3 * WC), bf16), (qkv, dh, hmask),
        scratch=[vm(HC, L, HD)] * 4 + [vm(HC, L, HD, dtype=f32)] * 2,
        cid=4, jobs=[FirstSum(*slots_p), SecondSum(*firsts[2], *kepts[2]), ThirdSum(*results[1])],
        flops=30e9, nbytes=9e6,
    )
    first_p = given[0]
    results.append(given[1])
    finals.append(given[2][0])
    sum_fc1 = jnp.concatenate(sums1, axis=0).reshape(NF, 4, FZ).transpose(1, 0, 2).reshape(4, 4, FF // 32)
    own_part = lambda v: core_half(v, 4, 2, 4, D // 32)
    line = jnp.concatenate(
        [sum_fc1, own_part(sum2), own_part(sum_attn[0]), jnp.zeros((4, 4, 3 * LANES - FF // 32 - D // 16), f32)], axis=2
    ).reshape(4, 4, 3, LANES)
    extra = jnp.concatenate([line, jnp.zeros((4, 4, 13, LANES), f32)], axis=2)
    slot_q = sds((2, 4, QA, LANES), bf16)
    slots_q, given = call(
        qkv_grad_kernel, "qkv_grad",
        (slot_q,) * 4, (shifted, dqkv, extra),
        scratch=[vm(4, D, 3 * DC)],
        cid=5, jobs=[SecondSum(*first_p, slots_p[0], slots_p[2]), ThirdSum(*results[2])],
        flops=2 * L * D * 3 * WC, nbytes=12e6,
    )
    result_p = given[0]
    finals.append(given[1][0])
    near = pl.BlockSpec((LB, D), lambda i: (jnp.maximum(i - 2, 0), 0))
    (grad_rows, item), given = call(
        tail_kernel, "tail",
        (sds((2, LB, D), bf16), sds((8, D), f32)),
        (dqkv, wq, d_resid, tok, mod, sums_mid),
        grid=(4,),
        in_specs=[pl.BlockSpec((LB, 3 * WC), lambda i: ((i + 2) % 4, 0)), once(D, 3 * WC), near, near, full((8, D)),
                  full((8, D))],
        out_specs=(ANY, full((8, D))),
        scratch=[vm(2, LB, D), vm(2, LB, D), vm(2, LB, D), vm(8, D, dtype=f32), pltpu.SemaphoreType.DMA((2, 3)),
                 pltpu.SemaphoreType.DMA((2, 2)), pltpu.SemaphoreType.DMA],
        peers=("c", "t0", "t1"), cid=6, jobs=[FirstSum(*slots_q), ThirdSum(*result_p)],
        flops=2 * L * D * 3 * WC, nbytes=12e6,
    )
    first_q, final_p = given[0], given[1][0]
    grad_tokens = grad_rows.astype(f32)
    square, given = call(
        square_kernel, "square", sds((4, 8, D), f32), (item,),
        scratch=[pltpu.SemaphoreType.DMA((2, 3)), pltpu.SemaphoreType.DMA],
        peers=("x", "y", "xy"), cid=7, jobs=[SecondSum(*first_q, slots_q[0], slots_q[2])],
    )
    every, given = call(
        every_kernel, "every", sds((4, 4, 8, D), f32), (square,),
        scratch=[pltpu.SemaphoreType.DMA((2, 3)), pltpu.SemaphoreType.DMA],
        peers=("z1", "z2", "z3"), cid=8, jobs=[ThirdSum(*given[0])],
    )
    final_q = given[0][0]

    every = every.reshape(16, 8, D)
    cond_all = jax.nn.silu(step_embedding(every[:, 6, 0], D)).astype(bf16).astype(f32)
    every = every[:, :6].reshape(16, 6 * D)
    cond_rows = lax.dynamic_slice_in_dim(cond_all, b * DC, DC, 1)
    columns = lax.dynamic_slice_in_dim(every, t * ada_cols, ada_cols, 1)
    grad_ada_weight = lax.dot_general(
        cond_rows, columns, (((0,), (0,)), ((), ())), precision=lax.Precision.HIGHEST
    )
    bias_cols = 6 * D // 8
    grad_ada_bias = jnp.sum(lax.dynamic_slice_in_dim(every, b * bias_cols, bias_cols, 1), axis=0)

    (gq, gp, g1, g2), _ = call(
        finish_kernel, "finish",
        (sds((DC, 3 * TD), f32), sds((DC, TD), f32), sds((DC, FF // 4), f32), sds((FF // 8, TD), f32)),
        (*finals, final_p, final_q),
        scratch=[vm(NF * G1R + 7 * DC, LANES), vm(NF * G1R + 7 * DC, LANES), pltpu.SemaphoreType.DMA((2, 1))],
        peers=("c",), cid=9, nbytes=6e6,
    )
    line = final_q[7 * DC :].reshape(-1)
    n1, n = FF // 32, D // 32
    b_fc1, b_fc2, b_proj = line[:n1], line[n1 : n1 + n], line[n1 + n : n1 + 2 * n]
    b_q, b_v = line[n1 + 2 * n : n1 + 3 * n], line[2 * LANES : 2 * LANES + n]
    return (output, grad_tokens, gq, b_q, b_v, gp, b_proj, g1, b_fc1, g2, b_fc2, grad_ada_weight, grad_ada_bias)


def gelu_tanh(values):
    return jax.nn.gelu(values, approximate=True)


def split_heads(key_value, model_width, head_dim):
    item_count, length = (key_value.shape[0], key_value.shape[1])
    key_rows = key_value[:, :, :model_width].reshape(
        item_count, length, model_width // head_dim, head_dim
    )
    value_rows = key_value[:, :, model_width:].reshape(
        item_count, length, model_width // head_dim, head_dim
    )
    return (key_rows, value_rows)


def scores_of(queries, key_rows, score_scale):
    return (
        jnp.einsum("nqhe,nkhe->nhqk", queries, key_rows, preferred_element_type=jnp.float32)
        * score_scale
    )


def to_blocks(values, per_step):
    return values.reshape((values.shape[0] // per_step, per_step) + values.shape[1:])


def from_blocks(values):
    return values.reshape((values.shape[0] * values.shape[1],) + values.shape[2:])


def on_device(
    tokens,
    cotangent,
    timesteps,
    bucket_ids,
    head_masks,
    channel_masks,
    skip_rows,
    w_qkv,
    q_bias,
    v_bias,
    w_proj,
    proj_bias,
    w_fc1,
    fc1_bias,
    w_fc2,
    fc2_bias,
    ada_weight,
    ada_bias,
):
    item_count, local_len, model_width = tokens.shape
    row_count = item_count * local_len
    head_dim = model_width // HEADS
    score_scale = 1.0 / math.sqrt(head_dim)
    hidden_width = w_fc1.shape[1]
    ada_cols = ada_weight.shape[1]
    tok_index = lax.axis_index("tok")
    per_step = 1
    for candidate in range(1, item_count + 1):
        per_step = candidate
    condition = jax.nn.silu(step_embedding(timesteps, model_width)).astype(jnp.bfloat16)
    mod_local = jnp.dot(
        condition, ada_weight, preferred_element_type=jnp.float32
    ) + ada_bias.astype(jnp.float32)
    modulation = lax.all_gather(mod_local, "tok", axis=1, tiled=True)
    pieces = modulation.reshape(item_count, 6, 1, model_width)
    shift_a = pieces[:, 0]
    scale_a = pieces[:, 1]
    gate_a = pieces[:, 2]
    shift_m = pieces[:, 3]
    scale_m = pieces[:, 4]
    gate_m = pieces[:, 5]
    chosen = (jnp.arange(head_masks.shape[0], dtype=jnp.int32) == bucket_ids[0]).astype(jnp.float32)
    head_on = jnp.sum(chosen[:, None] * head_masks.astype(jnp.float32), axis=0)
    group_on = jnp.sum(chosen[:, None] * channel_masks.astype(jnp.float32), axis=0)
    channel_on = jnp.repeat(group_on, hidden_width // group_on.shape[0])
    positions = tok_index * local_len + jnp.arange(local_len, dtype=jnp.int32)
    skipped = jnp.any(skip_rows[:, :, None] == positions[None, None, :], axis=1)
    kept_rows = 1.0 - skipped.astype(jnp.float32)
    inputs = tokens.astype(jnp.float32)
    normed, inverse = normalize(inputs)
    shifted = (
        (normed * (1.0 + scale_a) + shift_a).astype(jnp.bfloat16).reshape(row_count, model_width)
    )
    qkv_bias = jnp.concatenate([q_bias, jnp.zeros_like(q_bias), v_bias]).astype(jnp.float32)
    projected = (jnp.dot(shifted, w_qkv, preferred_element_type=jnp.float32) + qkv_bias).astype(
        jnp.bfloat16
    )
    projected = projected.reshape(item_count, local_len, 3 * model_width)
    queries = projected[:, :, :model_width].reshape(item_count, local_len, HEADS, head_dim)
    key_value = projected[:, :, model_width:]
    all_kv = lax.all_gather(key_value, "tok", axis=1, tiled=True)

    def forward_block(packed):
        query_block, kv_block = packed
        key_rows, value_rows = split_heads(kv_block, model_width, head_dim)
        scores = scores_of(query_block, key_rows, score_scale)
        top_score = jnp.max(scores, axis=-1, keepdims=True)
        expanded = jnp.exp(scores - top_score)
        totals = jnp.sum(expanded, axis=-1, keepdims=True)
        weights_low = (expanded / totals).astype(jnp.bfloat16)
        head_out = (
            jnp.einsum(
                "nhqk,nkhe->nqhe", weights_low, value_rows, preferred_element_type=jnp.float32
            )
            * head_on[:, None]
        )
        return (head_out.astype(jnp.bfloat16), top_score + jnp.log(totals))

    mixed_heads, log_total = lax.map(
        forward_block, (to_blocks(queries, per_step), to_blocks(all_kv, per_step))
    )
    log_total = from_blocks(log_total)
    mixed = from_blocks(mixed_heads).reshape(row_count, model_width)
    attn = (
        jnp.dot(mixed, w_proj, preferred_element_type=jnp.float32) + proj_bias.astype(jnp.float32)
    ).reshape(item_count, local_len, model_width)
    resid = inputs + gate_a * attn
    normed2, inverse2 = normalize(resid)
    shifted2 = (
        (normed2 * (1.0 + scale_m) + shift_m).astype(jnp.bfloat16).reshape(row_count, model_width)
    )
    pre = jnp.dot(shifted2, w_fc1, preferred_element_type=jnp.float32) + fc1_bias.astype(
        jnp.float32
    )
    activated, gelu_pull = jax.vjp(gelu_tanh, pre)
    hidden = (activated * channel_on).astype(jnp.bfloat16)
    branch = (
        jnp.dot(hidden, w_fc2, preferred_element_type=jnp.float32) + fc2_bias.astype(jnp.float32)
    ).reshape(item_count, local_len, model_width)
    gated = kept_rows[:, :, None] * gate_m
    output = (resid + gated * branch).astype(jnp.bfloat16)
    incoming = cotangent.astype(jnp.float32)
    d_gate_m = jnp.sum(kept_rows[:, :, None] * branch * incoming, axis=1)
    d_branch = (gated * incoming).astype(jnp.bfloat16).reshape(row_count, model_width)
    grad_w_fc2 = jnp.dot(hidden.T, d_branch, preferred_element_type=jnp.float32)
    grad_fc2_bias = jnp.sum(d_branch.astype(jnp.float32), axis=0)
    d_hidden = jnp.dot(d_branch, w_fc2.T, preferred_element_type=jnp.float32)
    d_pre = gelu_pull(d_hidden * channel_on)[0].astype(jnp.bfloat16)
    grad_w_fc1 = jnp.dot(shifted2.T, d_pre, preferred_element_type=jnp.float32)
    grad_fc1_bias = jnp.sum(d_pre.astype(jnp.float32), axis=0)
    d_shifted2 = jnp.dot(d_pre, w_fc1.T, preferred_element_type=jnp.float32).reshape(
        item_count, local_len, model_width
    )
    d_shift_m = jnp.sum(d_shifted2, axis=1)
    d_scale_m = jnp.sum(d_shifted2 * normed2, axis=1)
    d_resid = incoming + normalize_back(d_shifted2 * (1.0 + scale_m), normed2, inverse2)
    d_gate_a = jnp.sum(attn * d_resid, axis=1)
    d_attn = (gate_a * d_resid).astype(jnp.bfloat16).reshape(row_count, model_width)
    grad_w_proj = jnp.dot(mixed.T, d_attn, preferred_element_type=jnp.float32)
    grad_proj_bias = jnp.sum(d_attn.astype(jnp.float32), axis=0)
    d_mixed = jnp.dot(d_attn, w_proj.T, preferred_element_type=jnp.float32).astype(jnp.bfloat16)
    d_heads = d_mixed.reshape(item_count, local_len, HEADS, head_dim) * head_on[:, None].astype(
        jnp.bfloat16
    )
    again_kv = lax.all_gather(key_value, "tok", axis=1, tiled=True)

    def backward_block(packed):
        query_block, kv_block, head_grads, totals_log = packed
        key_rows, value_rows = split_heads(kv_block, model_width, head_dim)
        scores = scores_of(query_block, key_rows, score_scale)
        probs = jnp.exp(scores - totals_log)
        d_probs = jnp.einsum(
            "nqhe,nkhe->nhqk", head_grads, value_rows, preferred_element_type=jnp.float32
        )
        row_dot = jnp.sum(probs * d_probs, axis=-1, keepdims=True)
        d_scores = (probs * (d_probs - row_dot)).astype(jnp.bfloat16)
        d_queries = (
            jnp.einsum("nhqk,nkhe->nqhe", d_scores, key_rows, preferred_element_type=jnp.float32)
            * score_scale
        )
        return (d_queries, row_dot)

    mapped = lax.map(
        backward_block,
        (
            to_blocks(queries, per_step),
            to_blocks(again_kv, per_step),
            to_blocks(d_heads, per_step),
            to_blocks(log_total, per_step),
        ),
    )
    d_queries = from_blocks(mapped[0])
    row_dot = from_blocks(mapped[1])
    queries_all, head_grads_all = (
        lax.all_gather(queries, "tok", axis=1, tiled=True),
        lax.all_gather(d_heads, "tok", axis=1, tiled=True),
    )
    totals_all, row_dot_all = (
        lax.all_gather(log_total, "tok", axis=2, tiled=True),
        lax.all_gather(row_dot, "tok", axis=2, tiled=True),
    )

    def key_block(packed):
        kv_block, query_block, head_grads, totals_log, dots = packed
        key_rows, value_rows = split_heads(kv_block, model_width, head_dim)
        scores = (
            jnp.einsum("nkhe,nqhe->nhkq", key_rows, query_block, preferred_element_type=jnp.float32)
            * score_scale
        )
        probs = jnp.exp(scores - totals_log[:, :, None, :, 0])
        d_probs = jnp.einsum(
            "nkhe,nqhe->nhkq", value_rows, head_grads, preferred_element_type=jnp.float32
        )
        d_scores = (probs * (d_probs - dots[:, :, None, :, 0])).astype(jnp.bfloat16)
        d_keys = (
            jnp.einsum("nhkq,nqhe->nkhe", d_scores, query_block, preferred_element_type=jnp.float32)
            * score_scale
        )
        d_values = jnp.einsum(
            "nhkq,nqhe->nkhe",
            probs.astype(jnp.bfloat16),
            head_grads,
            preferred_element_type=jnp.float32,
        )
        return jnp.concatenate(
            [
                d_keys.reshape(d_keys.shape[0], local_len, model_width),
                d_values.reshape(d_values.shape[0], local_len, model_width),
            ],
            axis=2,
        )

    d_kv = from_blocks(
        lax.map(
            key_block,
            (
                to_blocks(key_value, per_step),
                to_blocks(queries_all, per_step),
                to_blocks(head_grads_all, per_step),
                to_blocks(totals_all, per_step),
                to_blocks(row_dot_all, per_step),
            ),
        )
    )
    d_qkv = jnp.concatenate([d_queries.reshape(item_count, local_len, model_width), d_kv], axis=2)
    d_qkv = d_qkv.astype(jnp.bfloat16).reshape(row_count, 3 * model_width)
    grad_w_qkv = jnp.dot(shifted.T, d_qkv, preferred_element_type=jnp.float32)
    qkv_sums = jnp.sum(d_qkv.astype(jnp.float32), axis=0)
    grad_q_bias = qkv_sums[:model_width]
    grad_v_bias = qkv_sums[2 * model_width :]
    d_shifted = jnp.dot(d_qkv, w_qkv.T, preferred_element_type=jnp.float32).reshape(
        item_count, local_len, model_width
    )
    d_shift_a = jnp.sum(d_shifted, axis=1)
    d_scale_a = jnp.sum(d_shifted * normed, axis=1)
    grad_tokens = d_resid + normalize_back(d_shifted * (1.0 + scale_a), normed, inverse)
    d_modulation = jnp.concatenate(
        [d_shift_a, d_scale_a, d_gate_a, d_shift_m, d_scale_m, d_gate_m], axis=1
    )
    d_modulation = lax.psum(d_modulation, "tok")
    mod_columns = lax.dynamic_slice_in_dim(d_modulation, tok_index * ada_cols, ada_cols, 1)
    grad_ada_weight = jnp.dot(
        condition.astype(jnp.float32).T, mod_columns, precision=lax.Precision.HIGHEST
    )
    grad_ada_bias = jnp.sum(d_modulation, axis=0)
    bucket_done = (
        lax.psum_scatter(grad_w_qkv, "bucket", scatter_dimension=0, tiled=True),
        lax.psum_scatter(grad_w_proj, "bucket", scatter_dimension=0, tiled=True),
        lax.psum_scatter(grad_w_fc1, "bucket", scatter_dimension=0, tiled=True),
        lax.psum_scatter(grad_w_fc2, "bucket", scatter_dimension=0, tiled=True),
        lax.psum_scatter(grad_q_bias, "bucket", scatter_dimension=0, tiled=True),
        lax.psum_scatter(grad_v_bias, "bucket", scatter_dimension=0, tiled=True),
        lax.psum_scatter(grad_proj_bias, "bucket", scatter_dimension=0, tiled=True),
        lax.psum_scatter(grad_fc1_bias, "bucket", scatter_dimension=0, tiled=True),
        lax.psum_scatter(grad_fc2_bias, "bucket", scatter_dimension=0, tiled=True),
        lax.psum_scatter(grad_ada_weight, "bucket", scatter_dimension=0, tiled=True),
        lax.psum_scatter(grad_ada_bias, "bucket", scatter_dimension=0, tiled=True),
    )
    token_done = (
        lax.psum_scatter(bucket_done[0], "tok", scatter_dimension=1, tiled=True),
        lax.psum_scatter(bucket_done[1], "tok", scatter_dimension=1, tiled=True),
        lax.psum_scatter(bucket_done[2], "tok", scatter_dimension=1, tiled=True),
        lax.psum_scatter(bucket_done[3], "tok", scatter_dimension=1, tiled=True),
        lax.psum_scatter(bucket_done[4].reshape(1, -1), "tok", scatter_dimension=1, tiled=True),
        lax.psum_scatter(bucket_done[5].reshape(1, -1), "tok", scatter_dimension=1, tiled=True),
        lax.psum_scatter(bucket_done[6].reshape(1, -1), "tok", scatter_dimension=1, tiled=True),
        lax.psum_scatter(bucket_done[7].reshape(1, -1), "tok", scatter_dimension=1, tiled=True),
        lax.psum_scatter(bucket_done[8].reshape(1, -1), "tok", scatter_dimension=1, tiled=True),
    )
    finished = (
        token_done[0],
        token_done[1],
        token_done[2],
        token_done[3],
        token_done[4],
        token_done[5],
        token_done[6],
        token_done[7],
        token_done[8],
        bucket_done[9],
        bucket_done[10],
    )
    return (
        output,
        grad_tokens,
        finished[0],
        finished[4].reshape(-1),
        finished[5].reshape(-1),
        finished[1],
        finished[6].reshape(-1),
        finished[2],
        finished[7].reshape(-1),
        finished[3],
        finished[8].reshape(-1),
        finished[9],
        finished[10],
    )


def solution(mesh):
    planned = mesh.shape["tok"] == 4 and mesh.shape["bucket"] == 8
    return jax.shard_map(
        one_item_per_chip if planned else on_device,
        mesh=mesh,
        in_specs=(
            P("bucket", "tok", None),
            P("bucket", "tok", None),
            P("bucket"),
            P("bucket"),
            P(),
            P(),
            P("bucket", None),
            P(),
            P(),
            P(),
            P(),
            P(),
            P(),
            P(),
            P(),
            P(),
            P(None, "tok"),
            P("tok"),
        ),
        out_specs=(
            P("bucket", "tok", None),
            P("bucket", "tok", None),
            P("bucket", "tok"),
            P(("bucket", "tok")),
            P(("bucket", "tok")),
            P("bucket", "tok"),
            P(("bucket", "tok")),
            P("bucket", "tok"),
            P(("bucket", "tok")),
            P("bucket", "tok"),
            P(("bucket", "tok")),
            P("bucket", "tok"),
            P("bucket"),
        ),
        check_vma=False,
    )
```

```python
import functools
import math

import jax
import jax.numpy as jnp
from jax import lax
from jax.experimental import pallas as pl
from jax.experimental.pallas import tpu as pltpu
from jax.sharding import PartitionSpec as P

HEADS = 16
EPSILON = 1e-06
LOG2E = 1.4426950408889634
GELU_K = math.sqrt(2.0 / math.pi)
GELU_C = 0.044715
LANES = 128
bf16, f32 = jnp.bfloat16, jnp.float32


def dot_nn(a, b):
    return lax.dot_general(a, b, (((1,), (0,)), ((), ())), preferred_element_type=f32)


def dot_nt(a, b):
    return lax.dot_general(a, b, (((1,), (1,)), ((), ())), preferred_element_type=f32)


def dot_tn(a, b):
    return lax.dot_general(a, b, (((0,), (0,)), ((), ())), preferred_element_type=f32)


def step_embedding(timesteps, model_width):
    half_width = model_width // 2
    frequency = jnp.exp(-math.log(10000.0) * jnp.arange(half_width, dtype=jnp.float32) / half_width)
    angles = timesteps.astype(jnp.float32)[:, None] * frequency[None, :]
    return jnp.concatenate([jnp.cos(angles), jnp.sin(angles)], axis=1)


def normalize(values):
    centred = values - jnp.mean(values, axis=-1, keepdims=True)
    inverse = lax.rsqrt(jnp.mean(centred * centred, axis=-1, keepdims=True) + EPSILON)
    return (centred * inverse, inverse)


def normalize_back(incoming, normed, inverse):
    return inverse * (
        incoming
        - jnp.mean(incoming, axis=-1, keepdims=True)
        - normed * jnp.mean(incoming * normed, axis=-1, keepdims=True)
    )


D = 1152
DC, DZ, TD = D // 8, D // 4, D // 4
HD = D // HEADS
HC = HEADS // 2
WC = D // 2
FF = 4608
NF = 3
FB = FF // 2 // NF
FZ = FB // 4
L = 1024
LH = L // 2
LB = L // 4
G1R = 3 * DC
G2R = 2 * FZ + FZ // 4
PR = 2 * DC + DC // 3
PA = 176
QR = 7 * DC + 16
QA = QR // 2
VMEM_LIMIT = 58 * 1024 * 1024


ANY = pl.BlockSpec(memory_space=pl.ANY)
MESH = pl.DeviceIdType.MESH


def place():
    b, t = lax.axis_index("bucket"), lax.axis_index("tok")
    return b // 2, b % 2, t // 2, t % 2


def flip(value, other):
    return (value // 2 + other // 2) % 2 * 2 + (value % 2 + other % 2) % 2


def peer(name):
    z, c, y, x = place()
    if name == "x":
        x = 1 - x
    elif name == "y":
        y = 1 - y
    elif name == "xy":
        x, y = 1 - x, 1 - y
    elif name == "c":
        c = 1 - c
    elif name in ("t0", "t1"):
        c, y, x = y, c, x if name == "t0" else 1 - x
    else:
        z = flip(z, int(name[1]))
    return (z * 2 + c, y * 2 + x)


def meet(names):
    sem = pltpu.get_barrier_semaphore()
    others = [name for name in names if name != "t0"]
    for name in others:
        pl.semaphore_signal(sem, inc=1, device_id=peer(name), device_id_type=MESH)
    wanted = len(others)
    if "t0" in names:
        _, c, y, _ = place()
        wanted = wanted + (c + y) % 2

        @pl.when(c != y)
        def _():
            pl.semaphore_signal(sem, inc=1, device_id=peer("t0"), device_id_type=MESH)

    pl.semaphore_wait(sem, wanted)


def remote(src, dst, sems, k, name):
    return pltpu.make_async_remote_copy(
        src_ref=src, dst_ref=dst, send_sem=sems.at[0, k], recv_sem=sems.at[1, k],
        device_id=peer(name), device_id_type=MESH,
    )


def vm(*shape, dtype=bf16):
    return pltpu.VMEM(shape, dtype)


class FirstSum:
    peers = ("x", "y")

    def __init__(self, keep_a, sent_a, keep_b, sent_b):
        self.ins = [keep_a, sent_a, keep_b, sent_b]
        shapes = [keep.shape[1:] for keep in (keep_a, keep_b)]
        self.outs = [jax.ShapeDtypeStruct(s, bf16) for s in shapes for _ in range(2)]
        self.scratch = [vm(*s) for s in shapes for _ in range(3)]
        self.scratch += [pltpu.SemaphoreType.DMA((2, 4)), pltpu.SemaphoreType.DMA((4,))]

    def plan(self, ins, outs, scratch):
        ka, sa, kb, sb = ins
        _, qa, _, qb = outs
        kav, rav, _, kbv, rbv, _, sems, local = scratch
        far = [
            remote(sa.at[1], rav, sems, 0, "x"),
            remote(sb.at[1], rbv, sems, 1, "y"),
            remote(sa.at[0], qa, sems, 2, "x"),
            remote(sb.at[0], qb, sems, 3, "y"),
        ]
        near = [
            pltpu.make_async_copy(ka.at[1], kav, local.at[0]),
            pltpu.make_async_copy(kb.at[1], kbv, local.at[1]),
        ]
        return far, near

    def finish(self, ins, outs, scratch):
        kav, rav, oav, kbv, rbv, obv, _, local = scratch
        oav[...] = (kav[...].astype(f32) + rav[...].astype(f32)).astype(bf16)
        obv[...] = (kbv[...].astype(f32) + rbv[...].astype(f32)).astype(bf16)
        return [
            pltpu.make_async_copy(oav, outs[0], local.at[2]),
            pltpu.make_async_copy(obv, outs[2], local.at[3]),
        ]


class SecondSum:
    peers = ("x", "y")

    def __init__(self, on_a, q_a, on_b, q_b, keep_a, keep_b):
        self.ins = [on_a, q_a, on_b, q_b, keep_a, keep_b]
        self.rows = [on_a.shape[1], on_b.shape[1]]
        total = sum(self.rows)
        self.outs = [jax.ShapeDtypeStruct((3, total, LANES), bf16), jax.ShapeDtypeStruct((total, LANES), f32)]
        self.scratch = [vm(4, r, LANES) for r in self.rows for _ in range(3)]
        self.scratch += [vm(3, total, LANES), vm(total, LANES, dtype=f32)]
        self.scratch += [pltpu.SemaphoreType.DMA((2, 2)), pltpu.SemaphoreType.DMA((6,))]

    def plan(self, ins, outs, scratch):
        oa, qa, ob, qb, ka, kb = ins
        kav, qav, rav, kbv, qbv, rbv, _, _, sems, local = scratch
        far = [remote(oa, rav, sems, 0, "y"), remote(ob, rbv, sems, 1, "x")]
        pairs = [(ka.at[0], kav), (qa, qav), (kb.at[0], kbv), (qb, qbv)]
        return far, [pltpu.make_async_copy(a, b, local.at[k]) for k, (a, b) in enumerate(pairs)]

    def finish(self, ins, outs, scratch):
        zs, zk, local = scratch[6], scratch[7], scratch[9]
        layer_sums([scratch[0:3], scratch[3:6]], zs, zk)
        return [
            pltpu.make_async_copy(zs, outs[0], local.at[4]),
            pltpu.make_async_copy(zk, outs[1], local.at[5]),
        ]


class ThirdSum:
    peers = ("z1", "z2", "z3")

    def __init__(self, sent, kept):
        self.ins = [sent, kept]
        self.outs = [jax.ShapeDtypeStruct(kept.shape, f32)]
        self.scratch = [vm(*sent.shape), vm(*kept.shape, dtype=f32)]
        self.scratch += [pltpu.SemaphoreType.DMA((2, 3)), pltpu.SemaphoreType.DMA((2,))]

    def plan(self, ins, outs, scratch):
        got, kept, sems, local = scratch
        far = [remote(ins[0].at[k], got.at[k], sems, k, f"z{k + 1}") for k in (2, 1, 0)]
        return far, [pltpu.make_async_copy(ins[1], kept, local.at[0])]

    def finish(self, ins, outs, scratch):
        got, kept, _, local = scratch
        kept[...] = kept[...] + got[0].astype(f32) + got[1].astype(f32) + got[2].astype(f32)
        return [pltpu.make_async_copy(kept, outs[0], local.at[1])]


def layer_sums(streams, zs, zk):
    start = 0
    for kv, qv, rv in streams:
        rows_ = rv.shape[1]
        for j in range(4):
            total = kv[j].astype(f32) + qv[j].astype(f32) + rv[j].astype(f32)
            if j == 0:
                zk[start : start + rows_, :] = total
            else:
                zs[j - 1, start : start + rows_, :] = total.astype(bf16)
        start += rows_


class SecondThird(SecondSum):
    peers = ("x", "y", "z1", "z2", "z3")

    def __init__(self, *args):
        super().__init__(*args)
        total = sum(self.rows)
        self.outs = [jax.ShapeDtypeStruct((total, LANES), f32)]
        self.scratch += [vm(3, total, LANES), pltpu.SemaphoreType.DMA((2, 3))]

    def third(self, scratch):
        zs, got, sems = scratch[6], scratch[10], scratch[11]
        return [remote(zs.at[k], got.at[k], sems, k, f"z{k + 1}") for k in (2, 1, 0)]

    def tick(self, ins, outs, scratch):
        for group in super().plan(ins, outs, scratch[:10]):
            for copy in group:
                copy.wait()
        layer_sums([scratch[0:3], scratch[3:6]], scratch[6], scratch[7])
        for copy in self.third(scratch):
            copy.start()

    def plan(self, ins, outs, scratch):
        return super().plan(ins, outs, scratch[:10])

    def settle(self, ins, outs, scratch):
        return self.third(scratch)

    def finish(self, ins, outs, scratch):
        kept, local, got = scratch[7], scratch[9], scratch[10]
        kept[...] = kept[...] + got[0].astype(f32) + got[1].astype(f32) + got[2].astype(f32)
        return [pltpu.make_async_copy(kept, outs[0], local.at[5])]


class FirstSecond:
    peers = ("x", "y")

    def __init__(self, keep_a, sent_a, keep_b, sent_b):
        self.ins = [keep_a, sent_a, keep_b, sent_b]
        self.rows = [keep_a.shape[2], keep_b.shape[2]]
        total = sum(self.rows)
        self.outs = [jax.ShapeDtypeStruct((3, total, LANES), bf16), jax.ShapeDtypeStruct((total, LANES), f32)]
        self.scratch = []
        for r in self.rows:
            self.scratch += [vm(2, 4, r, LANES), vm(2, 4, r, LANES), vm(4, r, LANES), vm(4, r, LANES)]
        self.scratch += [vm(3, total, LANES), vm(total, LANES, dtype=f32)]
        self.scratch += [pltpu.SemaphoreType.DMA((2, 6)), pltpu.SemaphoreType.DMA((4,))]

    def plan(self, ins, outs, scratch):
        ka, sa, kb, sb = ins
        sems, local = scratch[10:]
        far = [
            remote(sa.at[1], scratch[1].at[1], sems, 0, "x"),
            remote(sb.at[1], scratch[5].at[1], sems, 1, "y"),
            remote(sa.at[0], scratch[1].at[0], sems, 2, "x"),
            remote(sb.at[0], scratch[5].at[0], sems, 3, "y"),
        ]
        near = [pltpu.make_async_copy(k, scratch[4 * j], local.at[j]) for j, k in enumerate((ka, kb))]
        return far, near

    def second(self, scratch):
        sems = scratch[10]
        return [remote(scratch[4 * j + 2], scratch[4 * j + 3], sems, 4 + j, name) for j, name in enumerate("yx")]

    def tick(self, ins, outs, scratch):
        for group in self.plan(ins, outs, scratch):
            for copy in group:
                copy.wait()
        for j in range(2):
            kv, rv, on = scratch[4 * j : 4 * j + 3]
            on[...] = (kv[1].astype(f32) + rv[1].astype(f32)).astype(bf16)
        for copy in self.second(scratch):
            copy.start()

    def settle(self, ins, outs, scratch):
        return self.second(scratch)

    def finish(self, ins, outs, scratch):
        zs, zk, local = scratch[8], scratch[9], scratch[11]
        layer_sums([(scratch[j].at[0], scratch[j + 1].at[0], scratch[j + 3]) for j in (0, 4)], zs, zk)
        return [
            pltpu.make_async_copy(zs, outs[0], local.at[2]),
            pltpu.make_async_copy(zk, outs[1], local.at[3]),
        ]


class GoHome:
    peers = ("t0", "t1")

    def __init__(self, values):
        self.ins = [values]
        self.outs = [jax.ShapeDtypeStruct((2, LB, D), values.dtype)]
        self.scratch = [pltpu.SemaphoreType.DMA((2, 2)), pltpu.SemaphoreType.DMA]

    def plan(self, ins, outs, scratch):
        return [], []

    def tick(self, ins, outs, scratch):
        home_start(*self.copies(ins, outs, scratch))

    def copies(self, ins, outs, scratch):
        return homeward(ins[0].at[pl.ds(0, LB)], ins[0].at[pl.ds(LB, LB)], outs[0], *scratch)

    def settle(self, ins, outs, scratch):
        home_wait(*self.copies(ins, outs, scratch))
        return []

    def finish(self, ins, outs, scratch):
        return []


def homeward(first, second, dst, sems, local):
    x = place()[3]
    return (
        remote(first, dst.at[x], sems, 0, "t0"),
        pltpu.make_async_copy(first, dst.at[x], local),
        remote(second, dst.at[x], sems, 1, "t1"),
    )


def home_start(away, stay, second):
    _, c, y, _ = place()
    pl.when(c != y)(away.start)
    pl.when(c == y)(stay.start)
    second.start()


def home_wait(away, stay, second):
    _, c, y, _ = place()
    pl.when(c != y)(away.wait)
    pl.when(c == y)(stay.wait)
    second.wait()


def call(kernel, name, out_shape, args, in_specs=None, out_specs=None, scratch=(), grid=None,
         peers=(), jobs=(), cid=None, ticks=False, flops=0, nbytes=0):
    whole = pl.BlockSpec(memory_space=pltpu.VMEM)
    single = not isinstance(out_shape, (tuple, list))
    out_shape = [out_shape] if single else list(out_shape)
    in_specs = list(in_specs) if in_specs is not None else [whole] * len(args)
    out_specs = [whole] * len(out_shape) if out_specs is None else [out_specs] if single else list(out_specs)
    counts = [len(args), sum(len(j.ins) for j in jobs), len(out_shape), sum(len(j.outs) for j in jobs), len(scratch)]
    names = sorted(set(peers).union(*[j.peers for j in jobs]))

    def run(*refs):
        groups, at = [], 0
        for n in counts:
            groups.append(refs[at : at + n])
            at += n
        bound, ai, ao, asc = [], 0, 0, at
        for j in jobs:
            bound.append((
                j, groups[1][ai : ai + len(j.ins)], groups[3][ao : ao + len(j.outs)], refs[asc : asc + len(j.scratch)]
            ))
            ai, ao, asc = ai + len(j.ins), ao + len(j.outs), asc + len(j.scratch)

        def begin():
            if names:
                meet(names)
            for j, *r in bound:
                for group in j.plan(*r):
                    for copy in group:
                        copy.start()

        def end():
            last = []
            for j, *r in bound:
                far, near = (j.settle(*r), []) if hasattr(j, "tick") else j.plan(*r)
                for copy in far:
                    copy.wait()
                for copy in near:
                    copy.wait()
                copies = j.finish(*r)
                for copy in copies:
                    copy.start()
                last += copies
            for copy in last:
                copy.wait()

        def tick():
            for j, *r in bound:
                if hasattr(j, "tick"):
                    j.tick(*r)

        if grid is None:
            begin()
            kernel(*groups[0], *groups[2], *groups[4], **({"tick": tick} if ticks else {}))
            end()
        else:
            pl.when(pl.program_id(0) == 0)(begin)
            kernel(*groups[0], *groups[2], *groups[4])
            pl.when(pl.program_id(0) == grid[0] - 1)(end)

    extra = {} if grid is None else {"grid": grid}
    params = {"collective_id": cid, "has_side_effects": True} if names else {}
    outs = pl.pallas_call(
        run,
        out_shape=out_shape + [o for j in jobs for o in j.outs],
        in_specs=in_specs + [ANY] * counts[1],
        out_specs=out_specs + [ANY] * counts[3],
        scratch_shapes=list(scratch) + [q for j in jobs for q in j.scratch],
        compiler_params=pltpu.CompilerParams(vmem_limit_bytes=VMEM_LIMIT, **params),
        cost_estimate=pl.CostEstimate(flops=int(flops), bytes_accessed=int(nbytes), transcendentals=0),
        name=name,
        **extra,
    )(*args, *[a for j in jobs for a in j.ins])
    own, rest, given = outs[: len(out_shape)], outs[len(out_shape) :], []
    for j in jobs:
        given.append(rest[: len(j.outs)])
        rest = rest[len(j.outs) :]
    return (own[0] if single else own), given


def full(shape):
    return pl.BlockSpec(shape, lambda *_: (0,) * len(shape))


def once(*shape):
    return pl.BlockSpec(shape, lambda *_: (0,) * len(shape), pipeline_mode=pl.Buffered(1))


def rows(block, width):
    return pl.BlockSpec((block, width), lambda i: (i, 0))


def column(n):
    return lax.broadcasted_iota(jnp.int32, (n, 1), 0)


def front_kernel(tokens, cotangent, ints, ada_w, ada_b, freq, heads_t, channels_t, w_qkv, w_fc1, q_bias, v_bias, b1,
                 tok_o, cot_o, shifted_o, qkv_o, wq_o, w1_o, mod_o, kept_o, hmask_o, chan_o, b1_o,
                 tk, ck, wqv, wqc, w1v, w1c, adav, ints_other, m4, to_send, shares, csems, tsems, ssems, lsems):
    z, c, y, x = place()
    t = 2 * y + x
    loads = [
        pltpu.make_async_copy(a, b, lsems.at[k])
        for k, (a, b) in enumerate(((ada_w, adav), (w_qkv, wqv), (w_fc1, w1v)))
    ]

    def arrivals(src, dst, k):
        block = [dst.at[pl.ds(LB * j, LB)] for j in range(4)]
        first = remote(src.at[x], block[0], tsems, k, "t0")
        stay = pltpu.make_async_copy(src.at[x], block[0], lsems.at[3 + k])
        second = remote(src.at[1 - x], block[1], tsems, 2 + k, "t1")
        onward = [remote(block[j], block[2 + j], csems, 2 * k + j, "c") for j in range(2)]
        return first, stay, second, onward

    def leave(first, stay, second, onward):
        pl.when(c != y)(first.start)
        pl.when(c == y)(stay.start)
        second.start()

    def pass_on(first, stay, second, onward):
        pl.when(c != y)(first.wait_recv)
        pl.when(c == y)(stay.wait)
        onward[0].start()
        second.wait_recv()
        onward[1].start()

    def settle(first, stay, second, onward):
        pl.when(c != y)(first.wait_send)
        second.wait_send()
        for copy in onward:
            copy.wait_send()

    tok_moves, cot_moves = arrivals(tokens, tk, 0), arrivals(cotangent, ck, 1)
    leave(*tok_moves)
    swap = remote(ints, ints_other, csems, 4, "c")
    swap.start()
    for load in loads:
        load.start()
    swap.wait()

    mine, other = ints[...], ints_other[...]
    mine_t, other_t = mine[4:5, :].astype(f32), other[4:5, :].astype(f32)
    r = column(8)
    steps = jnp.zeros((8, 1), f32)
    for k in range(2):
        steps = jnp.where(r == 2 * c + k, mine_t[:, k : k + 1], steps)
        steps = jnp.where(r == 2 * (1 - c) + k, other_t[:, k : k + 1], steps)
    angles = steps * freq[...]
    condition = jax.nn.silu(jnp.concatenate([jnp.cos(angles), jnp.sin(angles)], axis=1))
    condition = jnp.concatenate([condition, jnp.zeros_like(condition)], axis=0).astype(bf16)
    loads[0].wait()
    m4[...] = dot_nt(condition, adav[...])[:8] + ada_b[...].astype(f32)
    moves = []
    for k in range(4):
        to = (y + k // 2) % 2 * 2 + (x + k) % 2
        row = jnp.broadcast_to(m4[pl.ds(to, 1), :], to_send.shape[1:])
        if k == 0:
            shares[t] = row
        else:
            to_send[k - 1] = row
            moves.append(remote(to_send.at[k - 1], shares.at[t], ssems, k - 1, ("x", "y", "xy")[k - 1]))
            moves[-1].start()

    group = jnp.where(c == y, mine, other)
    bucket = group[4:5, 2:3]
    skip = jnp.where(x == 0, group[0:2], group[2:4])
    for j in range(4):
        block = 2 * ((c + j // 2) % 2) + (x + j) % 2
        position = column(LB) + LB * block
        hit = jnp.where((position == skip[0:1, :]) | (position == skip[1:2, :]), 1.0, 0.0)
        kept_o[LB * j : LB * (j + 1), :] = 1.0 - jnp.max(hit, axis=1, keepdims=True)

    def chosen(masks):
        lane = lax.broadcasted_iota(jnp.int32, masks.shape, 1)
        return jnp.sum(jnp.where(lane == bucket, masks[...].astype(f32), 0.0), axis=1, keepdims=True)

    def spread(on, low, width):
        first = width * lax.broadcasted_iota(jnp.int32, (on.shape[0], low.shape[1]), 0)
        return jnp.sum(jnp.where((low >= first) & (low < first + width), on, 0.0), axis=0, keepdims=True)

    lane = lax.broadcasted_iota(jnp.int32, (1, WC), 1)
    share = sum(jnp.where(lane >= DC * k, 1, 0) for k in range(1, 4))
    hmask_o[...] = spread(chosen(heads_t), lane + DC * (share + c), HD)
    channels = chosen(channels_t)
    lane = lax.broadcasted_iota(jnp.int32, (1, FB), 1)
    share = sum(jnp.where(lane >= FZ * k, 1, 0) for k in range(1, 4))
    for f in range(NF):
        low = lane + (4 * DZ - FZ) * share + FF // 8 * c + FZ * f
        chan_o[f] = spread(channels, low, FF // channels.shape[0])

    def half(v, k, width):
        v = v[:, 2 * width * k : 2 * width * (k + 1)].astype(f32)
        return jnp.where(c == 0, v[:, :width], v[:, width:])

    bias = [half(q_bias[...], k, DC) for k in range(4)]
    bias += [jnp.zeros((1, WC), f32)] + [half(v_bias[...], k, DC) for k in range(4)]
    bias = jnp.concatenate(bias, axis=1)
    b1v = [half(b1[...], k, FF // 8) for k in range(4)]
    for f in range(NF):
        b1_o[f] = jnp.concatenate([v[:, FZ * f : FZ * (f + 1)] for v in b1v], axis=1)
    loads[1].wait()
    loads[2].wait()
    for core in range(2):

        @pl.when(c == core)
        def _():
            for k in range(12):
                wqc[:, DC * k : DC * (k + 1)] = wqv[:, DZ * k + DC * core : DZ * k + DC * (core + 1)]
            for f in range(NF):
                for k in range(4):
                    start = 4 * DZ * k + FF // 8 * core + FZ * f
                    w1c[f, :, FZ * k : FZ * (k + 1)] = w1v[:, start : start + FZ]

    stores = [
        pltpu.make_async_copy(a, b, lsems.at[k]) for k, (a, b) in enumerate(((wqc, wq_o), (w1c, w1_o)))
    ]
    for store in stores:
        store.start()
    pass_on(*tok_moves)
    leave(*cot_moves)
    for copy in moves:
        copy.wait()
    share_rows = [shares[k][0:1, :] for k in range(4)]
    n, m = D // 2, 3 * D // 2
    mod = [share_rows[0][:, :D], jnp.concatenate([share_rows[0][:, D:], share_rows[1][:, :n]], axis=1),
           share_rows[1][:, n:], share_rows[2][:, :D],
           jnp.concatenate([share_rows[2][:, D:], share_rows[3][:, :n]], axis=1), share_rows[3][:, n:]]
    own_step = 0.5 * jnp.sum(jnp.where(r == t, steps, 0.0), axis=0, keepdims=True)
    mod += [jnp.broadcast_to(own_step, (1, D)), jnp.zeros((1, D), f32)]
    mod_o[...] = jnp.concatenate(mod, axis=0)
    for j in range(4):
        if j >= 2:
            tok_moves[3][j - 2].wait_recv()
        part = slice(LB * j, LB * (j + 1))
        normed, _ = normalize(tk[part, :].astype(f32))
        shifted = (normed * (1.0 + mod[1]) + mod[0]).astype(bf16)
        shifted_o[part, :] = shifted
        qkv_o[part, :] = (dot_nn(shifted, wqc[...]) + bias).astype(bf16)
    keep = pltpu.make_async_copy(tk, tok_o, lsems.at[2])
    keep.start()
    pass_on(*cot_moves)
    for copy in cot_moves[3]:
        copy.wait_recv()
    keep_cot = pltpu.make_async_copy(ck, cot_o, lsems.at[5])
    keep_cot.start()
    settle(*tok_moves)
    settle(*cot_moves)
    for store in stores:
        store.wait()
    keep.wait()
    keep_cot.wait()


def attn_kernel(step, qkv, hmask, wp, bias, tok, mod, mixed_o, shifted2_o, attn_o,
                qh, kh, vh, mx, mo, wpv, tkv, csems, lsems):
    c = place()[1]
    loads = [
        pltpu.make_async_copy(wp.at[:, c], wpv.at[0], lsems.at[0]),
        pltpu.make_async_copy(wp.at[:, 1 - c], wpv.at[1], lsems.at[1]),
        pltpu.make_async_copy(tok, tkv, lsems.at[2]),
    ]
    for load in loads:
        load.start()
    scale = LOG2E / math.sqrt(HD)
    for h in range(HC):
        for k, ref in enumerate((qh, kh, vh)):
            ref[h] = qkv[:, WC * k + HD * h : WC * k + HD * (h + 1)]

    def crossing(i):
        src = mx.at[pl.ds(pl.multiple_of(i * step, step), step)]
        dst = mo.at[pl.ds(pl.multiple_of((i * step + LH) % L, step), step)]
        return remote(src, dst, csems, i, "c")

    def body(i, carry):
        part = pl.ds(pl.multiple_of(i * step, step), step)
        outs = []
        for h in range(HC):
            s = dot_nt(qh[h, part, :], kh[h])
            top = jnp.max(s, axis=1, keepdims=True)
            p = jnp.exp2((s - top) * scale)
            total = jnp.sum(p, axis=1, keepdims=True)
            outs.append(dot_nn(p.astype(bf16), vh[h]) * (1.0 / total))
        mx[part, :] = (jnp.concatenate(outs, axis=1) * hmask[...]).astype(bf16)
        crossing(i).start()
        return carry

    lax.fori_loop(0, L // step, body, 0)
    keep = pltpu.make_async_copy(mx, mixed_o, lsems.at[3])
    keep.start()
    for load in loads:
        load.wait()
    for i in range(L // step):
        crossing(i).wait()
    w_mine, w_other = wpv[0].reshape(WC, D), wpv[1].reshape(WC, D)
    for j in range(4):
        part = slice(LB * j, LB * (j + 1))
        attn = dot_nn(mx[part, :], w_mine) + dot_nn(mo[part, :], w_other) + bias[...]
        if j < 2:
            attn_o[part, :] = attn
        normed, _ = normalize(tkv[part, :].astype(f32) + mod[2:3, :] * attn)
        shifted2_o[part, :] = (normed * (1.0 + mod[4:5, :]) + mod[3:4, :]).astype(bf16)
    keep.wait()


def pack_hidden(block1, block2, o1, o2, ry, rx, rz):
    o1[ry, rz, : 2 * DC, :] = block1[:, :LANES]
    o1[ry, rz, 2 * DC :, :] = jnp.concatenate([block1[:DC, LANES:], block1[DC:, LANES:]], axis=1)
    o2[rx, rz, :FZ, :] = block2[:, :LANES]
    o2[rx, rz, FZ : 2 * FZ, :] = block2[:, LANES : 2 * LANES]
    q = FZ // 4
    o2[rx, rz, 2 * FZ :, :] = jnp.concatenate([block2[q * k : q * (k + 1), 2 * LANES :] for k in range(4)], axis=1)


def mlp_kernel(f, *refs):
    last = f == NF - 1
    refs = list(refs)
    sh2, g, kept, mod, w1, b1, chan, w2 = refs[:8]
    del refs[:8]
    before = None
    if f > 0:
        before = refs[:2]
        del refs[:2]
    slots, branch_o, ds2_o, sum1_o, sum2_o = refs[:4], refs[4], refs[5], refs[6], refs[7]
    del refs[:8]
    if last:
        got = refs[:2]
        del refs[:2]
    hid, dpre, dbs, w2v, t1, t2, s1k, s1s, s2k, s2s, sems = refs[:11]
    if last:
        far, csems = refs[11:]
        crossing = [remote(far.at[k], got[k], csems, k, "c") for k in range(2)]
    stages = (s1k, s1s, s2k, s2s)
    i = pl.program_id(0)
    z, c, y, x = place()

    @pl.when(i == 0)
    def _():
        copy = pltpu.make_async_copy(w2.at[:, c, f], w2v, sems.at[4])
        copy.start()
        copy.wait()

    part = pl.ds(pl.multiple_of((1 - i) * LH, LH), LH)
    w1v = w1[0]
    w2f = w2v[...].reshape(FB, D)
    db = (g[...].astype(f32) * mod[5:6, :] * kept[...]).astype(bf16)
    dbs[part, :] = db
    v = dot_nn(sh2[part, :], w1v) + b1[0]
    v2 = v * v
    th = jnp.tanh(GELU_K * v * (1.0 + GELU_C * v2))
    half = 0.5 * (1.0 + th)
    on = chan[0]
    hidden = (v * half * on).astype(bf16)
    hid[part, :] = hidden
    slope = (half + (0.5 * GELU_K) * v * (1.0 - th * th) * (1.0 + (3.0 * GELU_C) * v2)) * on
    d_pre = (dot_nt(db, w2f) * slope).astype(bf16)
    dpre[part, :] = d_pre
    branch, ds2 = dot_nn(hidden, w2f), dot_nt(d_pre, w1v)
    if before is not None:
        branch = branch + before[0][...].astype(f32)
        ds2 = ds2 + before[1][...].astype(f32)
    branch, ds2 = branch.astype(bf16), ds2.astype(bf16)
    if last:

        @pl.when(i == 0)
        def _():
            far[0] = branch
            far[1] = ds2
            for copy in crossing:
                copy.start()

        @pl.when(i == 1)
        def _():
            branch_o[...] = branch
            ds2_o[...] = ds2
    else:
        branch_o[...] = branch
        ds2_o[...] = ds2
    s1 = jnp.sum(d_pre.astype(f32), axis=0, keepdims=True)
    s2 = jnp.sum(db.astype(f32), axis=0, keepdims=True)

    @pl.when(i == 0)
    def _():
        sum1_o[...] = s1
        sum2_o[...] = s2

    @pl.when(i == 1)
    def _():
        sum1_o[...] += s1
        sum2_o[...] += s2
        for m in range(3):
            cut = slice(m * D // 3, (m + 1) * D // 3)
            p = dot_tn(sh2[:, cut], dpre[...]).astype(bf16)
            for t in range(4):
                t1[t, cut, :] = p[:, FZ * t : FZ * (t + 1)]
        for m in range(3):
            cut = slice(m * FB // 3, (m + 1) * FB // 3)
            p = dot_tn(hid[:, cut], dbs[...]).astype(bf16)
            for t in range(4):
                t2[t, cut, :] = p[:, TD * t : TD * (t + 1)]
        for rz in range(4):
            zz = flip(z, rz)
            for ry in range(2):
                for rx in range(2):
                    tt = (ry + y) % 2 * 2 + (rx + x) % 2
                    one = [
                        t1[tt, pl.ds(pl.multiple_of(zz * DZ + (rc + c) % 2 * DC, 16), DC), :] for rc in range(2)
                    ]
                    two = t2[tt, pl.ds(pl.multiple_of(zz * FZ, 16), FZ), :]
                    pack_hidden(jnp.concatenate(one, axis=0), two, (s1k, s1s)[rx], (s2k, s2s)[ry], ry, rx, rz)
        copies = [pltpu.make_async_copy(a, b, sems.at[k]) for k, (a, b) in enumerate(zip(stages, slots))]
        for copy in copies:
            copy.start()
        for copy in copies:
            copy.wait()
        if last:
            for copy in crossing:
                copy.wait()


def middle_kernel(ds, ds_r, br, br_r, attn, tok, g, kept, mod, bias2, mixed, wp,
                  d_resid_o, out_o, dh_o, pka, psa, pkb, psb, sums_o, sum_o, da, t1, wpv, csems, lsem):
    i = pl.program_id(0)
    n = LH // 4
    z, c, y, x = place()
    part = pl.ds(pl.multiple_of(i * n, n), n)
    gf, at = g[...].astype(f32), attn[...]
    resid = tok[...].astype(f32) + mod[2:3, :] * at
    normed2, inverse2 = normalize(resid)
    ds2 = ds[...].astype(f32) + ds_r[...].astype(f32)
    kb = kept[...] * (br[...].astype(f32) + br_r[...].astype(f32) + bias2[...])
    out_o[...] = (resid + mod[5:6, :] * kb).astype(bf16)
    d_resid = gf + normalize_back(ds2 * (1.0 + mod[4:5, :]), normed2, inverse2)
    d_resid_o[...] = d_resid
    da[part, :] = (mod[2:3, :] * d_resid).astype(bf16)
    sums = [jnp.sum(p, axis=0, keepdims=True) for p in (at * d_resid, ds2, ds2 * normed2, kb * gf)]
    sums = jnp.concatenate(sums + [jnp.zeros((4, D), f32)], axis=0)

    @pl.when(i == 0)
    def _():
        sums_o[...] = sums

    @pl.when(i > 0)
    def _():
        sums_o[...] += sums

    crossing = [
        remote(da.at[pl.ds(n * k, n)], da.at[pl.ds(LH + n * k, n)], csems, k, "c") for k in range(4)
    ]
    load = pltpu.make_async_copy(wp.at[:, c], wpv, lsem)
    pl.when(i == 0)(load.start)
    for k in range(4):
        pl.when(i == k)(crossing[k].start)

    @pl.when(i == 3)
    def _():
        for copy in crossing:
            copy.wait()
        load.wait()
        wv = wpv[...].reshape(WC, D)
        dh_o[...] = dot_nt(da[...], wv).astype(bf16)
        sum_o[...] = dot_nn(jnp.ones((16, L), bf16), da[...])[:8]
        grad = dot_tn(mixed[...], da[...]).astype(bf16)
        for t in range(4):
            t1[t] = grad[:, TD * t : TD * (t + 1)]
        for rz in range(4):
            zz = flip(z, rz)
            for ry in range(2):
                for rx in range(2):
                    tt = (ry + y) % 2 * 2 + (rx + x) % 2
                    a, b = (pka, psa)[rx], (pkb, psb)[ry]
                    block = t1[tt, pl.ds(pl.multiple_of(zz * DC, 16), DC), :]
                    a[ry, rz, :DC, :] = block[:, :LANES]
                    a[ry, rz, DC:, :] = block[: PA - DC, LANES : 2 * LANES]
                    b[rx, rz, : 2 * DC - PA, :] = block[PA - DC :, LANES : 2 * LANES]
                    q = DC // 3
                    tails = [block[q * k : q * (k + 1), 2 * LANES :] for k in range(3)]
                    tails.append(jnp.zeros((q, 32), bf16))
                    b[rx, rz, 2 * DC - PA :, :] = jnp.concatenate(tails, axis=1)


def attn_back_kernel(step, qkv, dh, hmask, out, qh, kh, vh, doh, dk, dv, tick):
    scale = LOG2E / math.sqrt(HD)
    for h in range(HC):
        for k, ref in enumerate((qh, kh, vh)):
            ref[h] = qkv[:, WC * k + HD * h : WC * k + HD * (h + 1)]
        cut = slice(HD * h, HD * (h + 1))
        doh[h] = (dh[:, cut].astype(f32) * hmask[:, cut]).astype(bf16)
    dk[...] = jnp.zeros_like(dk)
    dv[...] = jnp.zeros_like(dv)

    def body(i, carry):
        part = pl.ds(pl.multiple_of(i * step, step), step)
        outs = []
        for h in range(HC):
            q, do = qh[h, part, :], doh[h, part, :]
            s = dot_nt(kh[h], q)
            top = jnp.max(s, axis=0, keepdims=True)
            p = jnp.exp2((s - top) * scale)
            p = p * (1.0 / jnp.sum(p, axis=0, keepdims=True))
            dp = dot_nt(vh[h], do)
            row_dot = jnp.sum(p * dp, axis=0, keepdims=True)
            ds = (p * (dp - row_dot)).astype(bf16)
            dv[h] += dot_nn(p.astype(bf16), do)
            dk[h] += dot_nn(ds, q)
            outs.append(dot_tn(ds, kh[h]))
        out[part, :WC] = (jnp.concatenate(outs, axis=1) * (1.0 / math.sqrt(HD))).astype(bf16)
        return carry

    lax.fori_loop(0, L // step // 2, body, 0)
    tick()
    lax.fori_loop(L // step // 2, L // step, body, 0)
    for h in range(HC):
        out[:, WC + HD * h : WC + HD * (h + 1)] = (dk[h] * (1.0 / math.sqrt(HD))).astype(bf16)
        out[:, 2 * WC + HD * h : 2 * WC + HD * (h + 1)] = dv[h].astype(bf16)


def end_kernel(shifted, dqkv, extra, wq, d_resid, tok, mod, sums_mid, f0, f1, f2, sent_p, kept_p, freq,
               grad, gq_o, gp_o, g1_o, g2_o, ada_o, ada_bias_o, line_o,
               t1, ka, sa, kb, sb, ra, rb, ona, onb, r2a, r2b, zs, zk, zr, wqv, dres, tokv, fv, far, got, gb,
               item, item_r, out_shares, square, every, row_out, row_in, mine, theirs, mine_q, theirs_q, pk, pr,
               qsems, csems, tsems, ssems, psems, lsems):
    z, c, y, x = place()
    t, b = 2 * y + x, 2 * z + c
    loads = [
        pltpu.make_async_copy(src, dst, lsems.at[k])
        for k, (src, dst) in enumerate(
            ((wq, wqv), (d_resid, dres), (tok.at[pl.ds(0, LH)], tokv), (f0, fv.at[0]), (f1, fv.at[1]),
             (f2, fv.at[2]), (kept_p, pk))
        )
    ]
    third_p = [remote(sent_p.at[k], pr.at[k], psems, k, f"z{k + 1}") for k in (2, 1, 0)]
    for copy in third_p + loads:
        copy.start()

    for k in range(4):
        p = dot_tn(shifted[:, DZ * k : DZ * (k + 1)], dqkv[...]).astype(bf16)
        for j in range(4):
            t1[j, DZ * k : DZ * (k + 1), :] = p[:, 3 * DC * j : 3 * DC * (j + 1)]
    sums = dot_nn(jnp.ones((16, L), bf16), dqkv[...])[0:1, :]
    for z_ in range(4):
        for t_ in range(4):
            piece = DC * z_ + DC // 4 * t_
            qsum = sums[:, piece : piece + DC // 4]
            vsum = sums[:, 2 * WC + piece : 2 * WC + piece + DC // 4]
            row1 = jnp.concatenate([jnp.zeros((1, 88), f32), qsum, jnp.zeros((1, 4), f32)], axis=1)
            row2 = jnp.concatenate([vsum, jnp.zeros((1, LANES - DC // 4), f32)], axis=1)
            add = jnp.concatenate([jnp.zeros((1, LANES), f32), row1, row2, jnp.zeros((13, LANES), f32)], axis=0)
            rz, ry, rx = flip(z, z_), (t_ // 2 + y) % 2, (t_ % 2 + x) % 2
            block = (extra[z_, t_] + add).astype(bf16)

            @pl.when(ry == 0)
            def _():
                kb[rx, rz, QA - 16 :, :] = block

            @pl.when(ry == 1)
            def _():
                sb[rx, rz, QA - 16 :, :] = block

    for rz in range(4):
        zz = flip(z, rz)
        for ry in range(2):
            for rx in range(2):
                tt = (ry + y) % 2 * 2 + (rx + x) % 2
                one, two = (ka, sa)[rx], (kb, sb)[ry]
                parts = [
                    t1[tt, pl.ds(pl.multiple_of(zz * DZ + (rc + c) % 2 * DC, 16), DC), :] for rc in range(2)
                ]
                strips = [p[:, LANES * k : LANES * (k + 1)] for k in range(3) for p in parts]
                gap = jnp.zeros((DC, 16), bf16)
                strips.append(jnp.concatenate([parts[0][:, 3 * LANES :], gap, parts[1][:, 3 * LANES :], gap], axis=1))
                for k, strip in enumerate(strips):
                    first = DC * k
                    if first + DC <= QA:
                        one[ry, rz, first : first + DC, :] = strip
                    elif first >= QA:
                        two[rx, rz, first - QA : first - QA + DC, :] = strip
                    else:
                        one[ry, rz, first:, :] = strip[: QA - first]
                        two[rx, rz, : first + DC - QA, :] = strip[QA - first :]
    first_q = [
        remote(sa.at[1], ra.at[1], qsems, 0, "x"), remote(sb.at[1], rb.at[1], qsems, 1, "y"),
        remote(sa.at[0], ra.at[0], qsems, 2, "x"), remote(sb.at[0], rb.at[0], qsems, 3, "y"),
    ]
    for copy in first_q:
        copy.start()

    loads[0].wait()
    crossing = [remote(far.at[k], got.at[k], csems, k, "c") for k in range(2)]
    for k in range(2):
        far[k] = dot_nt(dqkv[LH + LB * k : LH + LB * (k + 1), :], wqv[...]).astype(bf16)
        crossing[k].start()
    loads[1].wait()
    loads[2].wait()
    total_sums = sums_mid[0:4, :]
    token_sums = jnp.zeros((2, D), f32)
    for k in range(2):
        part = slice(LB * k, LB * (k + 1))
        mine_rows = dot_nt(dqkv[part, :], wqv[...])
        crossing[k].wait()
        total = mine_rows + got[k].astype(f32)
        normed, inverse = normalize(tokv[part, :].astype(f32))
        back = dres[part, :] + normalize_back(total * (1.0 + mod[1:2, :]), normed, inverse)
        gb[k] = back.astype(bf16)
        token_sums += jnp.concatenate(
            [jnp.sum(v, axis=0, keepdims=True) for v in (total, total * normed)], axis=0
        )
    item[...] = jnp.concatenate([token_sums, total_sums, mod[6:8, :]], axis=0)
    over = remote(item, item_r, csems, 2, "c")
    over.start()

    for k in (3, 4, 5, 6):
        loads[k].wait()
    for f in range(NF):
        mine[G1R * f : G1R * (f + 1), :] = fv[f, :G1R, :].astype(bf16)
    swap = remote(mine, theirs, csems, 3, "c")
    swap.start()
    over.wait()
    v = item[...] + item_r[...]
    n = D // 2
    stamp = v[6:7, :LANES]
    pieces = ([v[0:1], v[1:2, :n]], [v[1:2, n:], v[2:3]], [v[3:4], v[4:5, :n]], [v[4:5, n:], v[5:6]])
    for j in range(4):
        out_shares[j] = jnp.concatenate(pieces[j] + [stamp], axis=1)
    for j in range(4):
        to = (y + j // 2) % 2 * 2 + (x + j) % 2
        if j == 0:
            square[t] = out_shares[t]
    meeting = [
        remote(out_shares.at[(y + j // 2) % 2 * 2 + (x + j) % 2], square.at[t], ssems, j - 1, ("x", "y", "xy")[j - 1])
        for j in (1, 2, 3)
    ]
    for copy in meeting:
        copy.start()

    def own_columns(q, firsts, own):
        columns = jnp.concatenate(q, axis=1) if q else None
        for core in range(2):

            @pl.when(c == core)
            def _():
                at = core if own else 1 - core
                if q:
                    for k in range(3):
                        gq_o[:, DZ * k + DC * at : DZ * k + DC * (at + 1)] = columns[:, DC * k : DC * (k + 1)]
                for f, pair in enumerate(firsts):
                    start = FF // 8 * at + FZ * f
                    g1_o[:, start : start + FZ] = jnp.concatenate(pair, axis=1)

    own_columns(None, [[fv[f, :DC, :], fv[f, 2 * DC : 3 * DC, : FZ - LANES]] for f in range(NF)], True)
    for f in range(NF):
        part = fv[f, G1R:, :]
        tail = part[2 * FZ :]
        tail = jnp.concatenate([tail[:, 32 * k : 32 * (k + 1)] for k in range(4)], axis=0)
        g2_o[FZ * f : FZ * (f + 1), :] = jnp.concatenate([part[:FZ], part[FZ : 2 * FZ], tail], axis=1)

    for copy in first_q:
        copy.wait()
    for kv, rv, on in ((ka, ra, ona), (kb, rb, onb)):
        on[...] = (kv[1].astype(f32) + rv[1].astype(f32)).astype(bf16)
    second_q = [remote(ona, r2a, qsems, 4, "y"), remote(onb, r2b, qsems, 5, "x")]
    for copy in second_q:
        copy.start()
    for copy in third_p + meeting:
        copy.wait()
    spread_z = [remote(square, every.at[z], ssems, 2 + k, f"z{k}") for k in (1, 2, 3)]
    every[z] = square[...]
    for copy in spread_z:
        copy.start()
    part = pk[...] + pr[0].astype(f32) + pr[1].astype(f32) + pr[2].astype(f32)
    tail = part[2 * DC :]
    tail = jnp.concatenate([tail[:, 32 * k : 32 * (k + 1)] for k in range(3)], axis=0)
    gp_o[...] = jnp.concatenate([part[:DC], part[DC : 2 * DC], tail], axis=1)
    swap.wait()
    own_columns(
        None,
        [
            [theirs[G1R * f + DC : G1R * f + 2 * DC, :].astype(f32),
             theirs[G1R * f + 2 * DC : G1R * (f + 1), FZ - LANES :].astype(f32)]
            for f in range(NF)
        ],
        False,
    )

    for copy in second_q:
        copy.wait()
    layer_sums([(ka.at[0], ra.at[0], r2a), (kb.at[0], rb.at[0], r2b)], zs, zk)
    third_q = [remote(zs.at[k], zr.at[k], qsems, 6 + k, f"z{k + 1}") for k in (2, 1, 0)]
    for copy in third_q:
        copy.start()
    home = homeward(gb.at[0], gb.at[1], grad, tsems, lsems.at[7])
    home_start(*home)

    for copy in spread_z:
        copy.wait()
    columns = jnp.concatenate([every[i, j] for i in range(4) for j in range(4)], axis=0)
    width = 3 * D // 2
    angles = columns[:, width : width + 1] * freq[b % 4]
    cond = jax.nn.silu(jnp.where(b < 4, jnp.cos(angles), jnp.sin(angles))).astype(bf16).astype(f32)
    columns = columns[:, :width]
    ada_o[...] = lax.dot_general(
        cond, columns, (((0,), (0,)), ((), ())), precision=lax.Precision.HIGHEST, preferred_element_type=f32
    )
    row = jnp.sum(columns, axis=0, keepdims=True)
    row_out[0] = row
    row_in[t] = row
    rows_ = [remote(row_out.at[0], row_in.at[t], ssems, 6 + j, name) for j, name in enumerate(("x", "y", "xy"))]
    for copy in rows_:
        copy.start()
    for copy in rows_:
        copy.wait()
    row = row_in[z]
    ada_bias_o[...] = jnp.where(c == 0, row[:, : width // 2], row[:, width // 2 :])

    for copy in third_q:
        copy.wait()
    q = zk[...] + zr[0].astype(f32) + zr[1].astype(f32) + zr[2].astype(f32)
    mine_q[...] = q[: 7 * DC].astype(bf16)
    swap = remote(mine_q, theirs_q, csems, 4, "c")
    swap.start()
    line_o[...] = q[7 * DC :]
    own_columns([q[0:DC], q[2 * DC : 3 * DC], q[4 * DC : 5 * DC], q[6 * DC : 7 * DC, : DC // 3]], [], True)
    swap.wait()
    q = theirs_q[...].astype(f32)
    own_columns([q[DC : 2 * DC], q[3 * DC : 4 * DC], q[5 * DC : 6 * DC], q[6 * DC :, 64 : 64 + DC // 3]], [], False)
    home_wait(*home)


def one_item_per_chip(
    tokens, cotangent, timesteps, bucket_ids, head_masks, channel_masks, skip_rows,
    w_qkv, q_bias, v_bias, w_proj, proj_bias, w_fc1, fc1_bias, w_fc2, fc2_bias, ada_weight, ada_bias,
):
    b, t = lax.axis_index("bucket"), lax.axis_index("tok")
    z, c, y, x = b // 2, b % 2, t // 2, t % 2
    sds = jax.ShapeDtypeStruct

    def core_half(v, *dims):
        return lax.dynamic_index_in_dim(v.reshape(dims), c, 1, keepdims=False)

    vmem = pl.BlockSpec(memory_space=pltpu.VMEM)
    skips = skip_rows.reshape(-1, LANES)
    ints = jnp.concatenate([timesteps, bucket_ids, jnp.zeros((LANES - 3,), jnp.int32)]).reshape(1, LANES)
    ints = jnp.concatenate([skips, ints, jnp.zeros((7 - skips.shape[0], LANES), jnp.int32)], axis=0)
    freq = jnp.exp(-math.log(10000.0) * jnp.arange(D // 2, dtype=f32) / (D // 2)).reshape(1, D // 2)
    ada_cols = ada_weight.shape[1]
    front, _ = call(
        front_kernel, "front",
        (sds((L, D), bf16), sds((L, D), bf16), sds((L, D), bf16), sds((L, 3 * WC), bf16), sds((D, 3 * WC), bf16),
         sds((NF, D, FB), bf16), sds((8, D), f32), sds((L, 1), f32), sds((1, WC), f32), sds((NF, 1, FB), f32),
         sds((NF, 1, FB), f32)),
        (tokens, cotangent, ints, ada_weight.T, ada_bias.reshape(1, ada_cols), freq, head_masks.T, channel_masks.T,
         w_qkv, w_fc1, q_bias.reshape(1, D), v_bias.reshape(1, D), fc1_bias.reshape(1, FF)),
        in_specs=[ANY, ANY, vmem, ANY, vmem, vmem, vmem, vmem, ANY, ANY, vmem, vmem, vmem],
        out_specs=[ANY, ANY, vmem, vmem, ANY, ANY] + [vmem] * 5,
        scratch=[vm(L, D), vm(L, D), vm(D, 3 * D), vm(D, 3 * WC), vm(D, FF), vm(NF, D, FB), vm(ada_cols, D),
                 vm(8, LANES, dtype=jnp.int32), vm(8, ada_cols, dtype=f32), vm(3, 8, ada_cols, dtype=f32),
                 vm(4, 8, ada_cols, dtype=f32), pltpu.SemaphoreType.DMA((2, 5)), pltpu.SemaphoreType.DMA((2, 4)),
                 pltpu.SemaphoreType.DMA((2, 3)), pltpu.SemaphoreType.DMA((6,))],
        peers=("c", "t0", "t1", "x", "y", "xy"), cid=10, flops=2 * L * D * 3 * WC, nbytes=50e6,
    )
    tok, g_all, shifted, qkv, wq, w1, mod, kept, hmask, chan, b1 = front
    w2 = w_fc2.reshape(4, 2, NF, FZ, D)
    wp = w_proj.reshape(4, 2, DC, D)
    (mixed, shifted2, attn), _ = call(
        functools.partial(attn_kernel, 256), "attn",
        (sds((L, WC), bf16), sds((L, D), bf16), sds((LH, D), f32)),
        (qkv, hmask, wp, proj_bias.astype(f32).reshape(1, D), tok, mod),
        in_specs=[vmem, vmem, ANY, vmem, ANY, vmem],
        out_specs=[ANY, vmem, vmem],
        scratch=[vm(HC, L, HD)] * 3 + [vm(L, WC), vm(L, WC), vm(2, 4, DC, D), vm(L, D),
                 pltpu.SemaphoreType.DMA((2, 4)), pltpu.SemaphoreType.DMA((4,))],
        peers=("c",), cid=11, flops=16e9, nbytes=5e6,
    )

    firsts, kepts, sums1, results, before = [], [], [], [], []
    half = pl.BlockSpec((LH, D), lambda i: (1 - i, 0))
    slot1, slot2 = sds((2, 4, G1R, LANES), bf16), sds((2, 4, G2R, LANES), bf16)
    for f in range(NF):
        jobs = []
        if f > 0:
            jobs.append(FirstSum(*slots))
        if f > 1:
            jobs.append(SecondSum(*firsts[f - 2], *kepts[f - 2]))
        last = f == NF - 1
        pick = lambda i, f=f: (f, 0, 0)
        out_shape = [slot1, slot1, slot2, slot2] + [sds((LH if last else L, D), bf16)] * 2
        out_shape += [sds((1, FB), f32), sds((1, D), f32)] + [sds((LH, D), bf16)] * (2 * last)
        own, given = call(
            functools.partial(mlp_kernel, f), f"mlp{f}",
            out_shape, (shifted2, g_all, kept, mod, w1, b1, chan, w2, *before),
            grid=(2,),
            in_specs=[once(L, D), half, pl.BlockSpec((LH, 1), lambda i: (1 - i, 0)), full((8, D)),
                      pl.BlockSpec((1, D, FB), pick, pipeline_mode=pl.Buffered(1)),
                      pl.BlockSpec((1, 1, FB), pick), pl.BlockSpec((1, 1, FB), pick), ANY] + [half] * len(before),
            out_specs=[ANY] * 4 + [full((LH, D)) if last else half] * 2 + [full((1, FB)), full((1, D))]
            + [ANY] * (2 * last),
            scratch=[vm(L, FB), vm(L, FB), vm(L, D), vm(4, FZ, D), vm(4, D, FZ), vm(4, FB, TD)]
            + [vm(*s.shape) for s in (slot1, slot1, slot2, slot2)] + [pltpu.SemaphoreType.DMA((5,))]
            + ([vm(2, LH, D), pltpu.SemaphoreType.DMA((2, 2))] if last else []),
            peers=("c",) if last else (), jobs=jobs, cid=f,
            flops=12 * L * D * FB, nbytes=20e6,
        )
        slots, before = own[:4], own[4:6]
        kepts.append((slots[0], slots[2]))
        sums1.append(own[6])
        if f > 0:
            firsts.append(given[0])
        if f > 1:
            results.append(given[1])
    sum2 = own[7]
    branch_r, ds2_r = own[8:]

    n = LH // 4
    row = rows(n, D)
    slot_a, slot_b = sds((2, 4, PA, LANES), bf16), sds((2, 4, PR - PA, LANES), bf16)
    own, given = call(
        middle_kernel, "middle",
        (sds((LH, D), f32), sds((LH, D), bf16), sds((L, WC), bf16), slot_a, slot_a, slot_b, slot_b,
         sds((8, D), f32), sds((8, D), f32)),
        (before[1], ds2_r, before[0], branch_r, attn, tok, g_all, kept, mod, fc2_bias.astype(f32).reshape(1, D),
         mixed, wp),
        grid=(4,),
        in_specs=[row] * 7 + [rows(n, 1), full((8, D)), full((1, D)), once(L, WC), ANY],
        out_specs=(row, row, full((L, WC)), full(slot_a.shape), full(slot_a.shape), full(slot_b.shape),
                   full(slot_b.shape), full((8, D)), full((8, D))),
        scratch=[vm(L, D), vm(4, WC, TD), vm(4, DC, D), pltpu.SemaphoreType.DMA((2, 4)), pltpu.SemaphoreType.DMA],
        peers=("c",), cid=3,
        jobs=[FirstSum(*slots), SecondSum(*firsts[1], *kepts[1]), ThirdSum(*results[0])],
        flops=4 * L * D * WC, nbytes=20e6,
    )
    d_resid, out_rows, dh, *slots_p, sums_mid, sum_attn = own
    firsts.append(given[0])
    results.append(given[1])
    finals = [given[2][0]]
    dqkv, given = call(
        functools.partial(attn_back_kernel, 512), "attn_back",
        sds((L, 3 * WC), bf16), (qkv, dh, hmask),
        scratch=[vm(HC, L, HD)] * 4 + [vm(HC, L, HD, dtype=f32)] * 2,
        cid=4, ticks=True,
        jobs=[SecondThird(*firsts[2], *kepts[2]), FirstSecond(*slots_p), ThirdSum(*results[1]), GoHome(out_rows)],
        flops=30e9, nbytes=9e6,
    )
    finals += [given[2][0], given[0][0]]
    sent_p, kept_p = given[1]
    output = given[3][0]
    sum_fc1 = jnp.concatenate(sums1, axis=0).reshape(NF, 4, FZ).transpose(1, 0, 2).reshape(4, 4, FF // 32)
    own_part = lambda v: core_half(v, 4, 2, 4, D // 32)
    line = jnp.concatenate(
        [sum_fc1, own_part(sum2), own_part(sum_attn[0]), jnp.zeros((4, 4, 3 * LANES - FF // 32 - D // 16), f32)], axis=2
    ).reshape(4, 4, 3, LANES)
    extra = jnp.concatenate([line, jnp.zeros((4, 4, 13, LANES), f32)], axis=2)
    slot_q = vm(2, 4, QA, LANES)
    fourth = vm(4, QA, LANES)
    width = ada_cols + LANES
    dma = pltpu.SemaphoreType.DMA
    (grad_rows, gq, gp, g1, g2, grad_ada_weight, grad_ada_bias, line), _ = call(
        end_kernel, "end",
        (sds((2, LB, D), bf16), sds((DC, 3 * TD), f32), sds((DC, TD), f32), sds((DC, FF // 4), f32),
         sds((FF // 8, TD), f32), sds((DC, ada_cols), f32), sds((1, ada_cols // 2), f32), sds((16, LANES), f32)),
        (shifted, dqkv, extra, wq, d_resid, tok, mod, sums_mid, *finals, sent_p, kept_p, freq.reshape(4, 1, DC)),
        in_specs=[vmem] * 3 + [ANY] * 3 + [vmem] * 2 + [ANY] * 5 + [vmem],
        out_specs=[ANY] + [vmem] * 7,
        scratch=[vm(4, D, 3 * DC)] + [slot_q] * 6 + [fourth] * 4
        + [vm(3, QR, LANES), vm(QR, LANES, dtype=f32), vm(3, QR, LANES), vm(D, 3 * WC), vm(LH, D, dtype=f32),
           vm(LH, D), vm(NF, G1R + G2R, LANES, dtype=f32)] + [vm(2, LB, D)] * 3
        + [vm(8, D, dtype=f32)] * 2 + [vm(4, 1, width, dtype=f32)] * 2
        + [vm(4, 4, 1, width, dtype=f32), vm(1, 1, ada_cols, dtype=f32), vm(4, 1, ada_cols, dtype=f32)]
        + [vm(NF * G1R, LANES)] * 2 + [vm(7 * DC, LANES)] * 2 + [vm(PR, LANES, dtype=f32), vm(3, PR, LANES)]
        + [dma((2, 9)), dma((2, 5)), dma((2, 2)), dma((2, 9)), dma((2, 3)), dma((8,))],
        peers=("c", "t0", "t1", "x", "y", "xy", "z1", "z2", "z3"), cid=5,
        flops=4 * L * D * 3 * WC, nbytes=30e6,
    )
    grad_tokens = grad_rows.astype(f32)
    line = line.reshape(-1)
    n1, n = FF // 32, D // 32
    b_fc1, b_fc2, b_proj = line[:n1], line[n1 : n1 + n], line[n1 + n : n1 + 2 * n]
    b_q, b_v = line[n1 + 2 * n : n1 + 3 * n], line[2 * LANES : 2 * LANES + n]
    return (output, grad_tokens, gq, b_q, b_v, gp, b_proj, g1, b_fc1, g2, b_fc2, grad_ada_weight,
            grad_ada_bias.reshape(-1))


def gelu_tanh(values):
    return jax.nn.gelu(values, approximate=True)


def split_heads(key_value, model_width, head_dim):
    item_count, length = (key_value.shape[0], key_value.shape[1])
    key_rows = key_value[:, :, :model_width].reshape(
        item_count, length, model_width // head_dim, head_dim
    )
    value_rows = key_value[:, :, model_width:].reshape(
        item_count, length, model_width // head_dim, head_dim
    )
    return (key_rows, value_rows)


def scores_of(queries, key_rows, score_scale):
    return (
        jnp.einsum("nqhe,nkhe->nhqk", queries, key_rows, preferred_element_type=jnp.float32)
        * score_scale
    )


def to_blocks(values, per_step):
    return values.reshape((values.shape[0] // per_step, per_step) + values.shape[1:])


def from_blocks(values):
    return values.reshape((values.shape[0] * values.shape[1],) + values.shape[2:])


def on_device(
    tokens,
    cotangent,
    timesteps,
    bucket_ids,
    head_masks,
    channel_masks,
    skip_rows,
    w_qkv,
    q_bias,
    v_bias,
    w_proj,
    proj_bias,
    w_fc1,
    fc1_bias,
    w_fc2,
    fc2_bias,
    ada_weight,
    ada_bias,
):
    item_count, local_len, model_width = tokens.shape
    row_count = item_count * local_len
    head_dim = model_width // HEADS
    score_scale = 1.0 / math.sqrt(head_dim)
    hidden_width = w_fc1.shape[1]
    ada_cols = ada_weight.shape[1]
    tok_index = lax.axis_index("tok")
    per_step = 1
    for candidate in range(1, item_count + 1):
        per_step = candidate
    condition = jax.nn.silu(step_embedding(timesteps, model_width)).astype(jnp.bfloat16)
    mod_local = jnp.dot(
        condition, ada_weight, preferred_element_type=jnp.float32
    ) + ada_bias.astype(jnp.float32)
    modulation = lax.all_gather(mod_local, "tok", axis=1, tiled=True)
    pieces = modulation.reshape(item_count, 6, 1, model_width)
    shift_a = pieces[:, 0]
    scale_a = pieces[:, 1]
    gate_a = pieces[:, 2]
    shift_m = pieces[:, 3]
    scale_m = pieces[:, 4]
    gate_m = pieces[:, 5]
    chosen = (jnp.arange(head_masks.shape[0], dtype=jnp.int32) == bucket_ids[0]).astype(jnp.float32)
    head_on = jnp.sum(chosen[:, None] * head_masks.astype(jnp.float32), axis=0)
    group_on = jnp.sum(chosen[:, None] * channel_masks.astype(jnp.float32), axis=0)
    channel_on = jnp.repeat(group_on, hidden_width // group_on.shape[0])
    positions = tok_index * local_len + jnp.arange(local_len, dtype=jnp.int32)
    skipped = jnp.any(skip_rows[:, :, None] == positions[None, None, :], axis=1)
    kept_rows = 1.0 - skipped.astype(jnp.float32)
    inputs = tokens.astype(jnp.float32)
    normed, inverse = normalize(inputs)
    shifted = (
        (normed * (1.0 + scale_a) + shift_a).astype(jnp.bfloat16).reshape(row_count, model_width)
    )
    qkv_bias = jnp.concatenate([q_bias, jnp.zeros_like(q_bias), v_bias]).astype(jnp.float32)
    projected = (jnp.dot(shifted, w_qkv, preferred_element_type=jnp.float32) + qkv_bias).astype(
        jnp.bfloat16
    )
    projected = projected.reshape(item_count, local_len, 3 * model_width)
    queries = projected[:, :, :model_width].reshape(item_count, local_len, HEADS, head_dim)
    key_value = projected[:, :, model_width:]
    all_kv = lax.all_gather(key_value, "tok", axis=1, tiled=True)

    def forward_block(packed):
        query_block, kv_block = packed
        key_rows, value_rows = split_heads(kv_block, model_width, head_dim)
        scores = scores_of(query_block, key_rows, score_scale)
        top_score = jnp.max(scores, axis=-1, keepdims=True)
        expanded = jnp.exp(scores - top_score)
        totals = jnp.sum(expanded, axis=-1, keepdims=True)
        weights_low = (expanded / totals).astype(jnp.bfloat16)
        head_out = (
            jnp.einsum(
                "nhqk,nkhe->nqhe", weights_low, value_rows, preferred_element_type=jnp.float32
            )
            * head_on[:, None]
        )
        return (head_out.astype(jnp.bfloat16), top_score + jnp.log(totals))

    mixed_heads, log_total = lax.map(
        forward_block, (to_blocks(queries, per_step), to_blocks(all_kv, per_step))
    )
    log_total = from_blocks(log_total)
    mixed = from_blocks(mixed_heads).reshape(row_count, model_width)
    attn = (
        jnp.dot(mixed, w_proj, preferred_element_type=jnp.float32) + proj_bias.astype(jnp.float32)
    ).reshape(item_count, local_len, model_width)
    resid = inputs + gate_a * attn
    normed2, inverse2 = normalize(resid)
    shifted2 = (
        (normed2 * (1.0 + scale_m) + shift_m).astype(jnp.bfloat16).reshape(row_count, model_width)
    )
    pre = jnp.dot(shifted2, w_fc1, preferred_element_type=jnp.float32) + fc1_bias.astype(
        jnp.float32
    )
    activated, gelu_pull = jax.vjp(gelu_tanh, pre)
    hidden = (activated * channel_on).astype(jnp.bfloat16)
    branch = (
        jnp.dot(hidden, w_fc2, preferred_element_type=jnp.float32) + fc2_bias.astype(jnp.float32)
    ).reshape(item_count, local_len, model_width)
    gated = kept_rows[:, :, None] * gate_m
    output = (resid + gated * branch).astype(jnp.bfloat16)
    incoming = cotangent.astype(jnp.float32)
    d_gate_m = jnp.sum(kept_rows[:, :, None] * branch * incoming, axis=1)
    d_branch = (gated * incoming).astype(jnp.bfloat16).reshape(row_count, model_width)
    grad_w_fc2 = jnp.dot(hidden.T, d_branch, preferred_element_type=jnp.float32)
    grad_fc2_bias = jnp.sum(d_branch.astype(jnp.float32), axis=0)
    d_hidden = jnp.dot(d_branch, w_fc2.T, preferred_element_type=jnp.float32)
    d_pre = gelu_pull(d_hidden * channel_on)[0].astype(jnp.bfloat16)
    grad_w_fc1 = jnp.dot(shifted2.T, d_pre, preferred_element_type=jnp.float32)
    grad_fc1_bias = jnp.sum(d_pre.astype(jnp.float32), axis=0)
    d_shifted2 = jnp.dot(d_pre, w_fc1.T, preferred_element_type=jnp.float32).reshape(
        item_count, local_len, model_width
    )
    d_shift_m = jnp.sum(d_shifted2, axis=1)
    d_scale_m = jnp.sum(d_shifted2 * normed2, axis=1)
    d_resid = incoming + normalize_back(d_shifted2 * (1.0 + scale_m), normed2, inverse2)
    d_gate_a = jnp.sum(attn * d_resid, axis=1)
    d_attn = (gate_a * d_resid).astype(jnp.bfloat16).reshape(row_count, model_width)
    grad_w_proj = jnp.dot(mixed.T, d_attn, preferred_element_type=jnp.float32)
    grad_proj_bias = jnp.sum(d_attn.astype(jnp.float32), axis=0)
    d_mixed = jnp.dot(d_attn, w_proj.T, preferred_element_type=jnp.float32).astype(jnp.bfloat16)
    d_heads = d_mixed.reshape(item_count, local_len, HEADS, head_dim) * head_on[:, None].astype(
        jnp.bfloat16
    )
    again_kv = lax.all_gather(key_value, "tok", axis=1, tiled=True)

    def backward_block(packed):
        query_block, kv_block, head_grads, totals_log = packed
        key_rows, value_rows = split_heads(kv_block, model_width, head_dim)
        scores = scores_of(query_block, key_rows, score_scale)
        probs = jnp.exp(scores - totals_log)
        d_probs = jnp.einsum(
            "nqhe,nkhe->nhqk", head_grads, value_rows, preferred_element_type=jnp.float32
        )
        row_dot = jnp.sum(probs * d_probs, axis=-1, keepdims=True)
        d_scores = (probs * (d_probs - row_dot)).astype(jnp.bfloat16)
        d_queries = (
            jnp.einsum("nhqk,nkhe->nqhe", d_scores, key_rows, preferred_element_type=jnp.float32)
            * score_scale
        )
        return (d_queries, row_dot)

    mapped = lax.map(
        backward_block,
        (
            to_blocks(queries, per_step),
            to_blocks(again_kv, per_step),
            to_blocks(d_heads, per_step),
            to_blocks(log_total, per_step),
        ),
    )
    d_queries = from_blocks(mapped[0])
    row_dot = from_blocks(mapped[1])
    queries_all, head_grads_all = (
        lax.all_gather(queries, "tok", axis=1, tiled=True),
        lax.all_gather(d_heads, "tok", axis=1, tiled=True),
    )
    totals_all, row_dot_all = (
        lax.all_gather(log_total, "tok", axis=2, tiled=True),
        lax.all_gather(row_dot, "tok", axis=2, tiled=True),
    )

    def key_block(packed):
        kv_block, query_block, head_grads, totals_log, dots = packed
        key_rows, value_rows = split_heads(kv_block, model_width, head_dim)
        scores = (
            jnp.einsum("nkhe,nqhe->nhkq", key_rows, query_block, preferred_element_type=jnp.float32)
            * score_scale
        )
        probs = jnp.exp(scores - totals_log[:, :, None, :, 0])
        d_probs = jnp.einsum(
            "nkhe,nqhe->nhkq", value_rows, head_grads, preferred_element_type=jnp.float32
        )
        d_scores = (probs * (d_probs - dots[:, :, None, :, 0])).astype(jnp.bfloat16)
        d_keys = (
            jnp.einsum("nhkq,nqhe->nkhe", d_scores, query_block, preferred_element_type=jnp.float32)
            * score_scale
        )
        d_values = jnp.einsum(
            "nhkq,nqhe->nkhe",
            probs.astype(jnp.bfloat16),
            head_grads,
            preferred_element_type=jnp.float32,
        )
        return jnp.concatenate(
            [
                d_keys.reshape(d_keys.shape[0], local_len, model_width),
                d_values.reshape(d_values.shape[0], local_len, model_width),
            ],
            axis=2,
        )

    d_kv = from_blocks(
        lax.map(
            key_block,
            (
                to_blocks(key_value, per_step),
                to_blocks(queries_all, per_step),
                to_blocks(head_grads_all, per_step),
                to_blocks(totals_all, per_step),
                to_blocks(row_dot_all, per_step),
            ),
        )
    )
    d_qkv = jnp.concatenate([d_queries.reshape(item_count, local_len, model_width), d_kv], axis=2)
    d_qkv = d_qkv.astype(jnp.bfloat16).reshape(row_count, 3 * model_width)
    grad_w_qkv = jnp.dot(shifted.T, d_qkv, preferred_element_type=jnp.float32)
    qkv_sums = jnp.sum(d_qkv.astype(jnp.float32), axis=0)
    grad_q_bias = qkv_sums[:model_width]
    grad_v_bias = qkv_sums[2 * model_width :]
    d_shifted = jnp.dot(d_qkv, w_qkv.T, preferred_element_type=jnp.float32).reshape(
        item_count, local_len, model_width
    )
    d_shift_a = jnp.sum(d_shifted, axis=1)
    d_scale_a = jnp.sum(d_shifted * normed, axis=1)
    grad_tokens = d_resid + normalize_back(d_shifted * (1.0 + scale_a), normed, inverse)
    d_modulation = jnp.concatenate(
        [d_shift_a, d_scale_a, d_gate_a, d_shift_m, d_scale_m, d_gate_m], axis=1
    )
    d_modulation = lax.psum(d_modulation, "tok")
    mod_columns = lax.dynamic_slice_in_dim(d_modulation, tok_index * ada_cols, ada_cols, 1)
    grad_ada_weight = jnp.dot(
        condition.astype(jnp.float32).T, mod_columns, precision=lax.Precision.HIGHEST
    )
    grad_ada_bias = jnp.sum(d_modulation, axis=0)
    bucket_done = (
        lax.psum_scatter(grad_w_qkv, "bucket", scatter_dimension=0, tiled=True),
        lax.psum_scatter(grad_w_proj, "bucket", scatter_dimension=0, tiled=True),
        lax.psum_scatter(grad_w_fc1, "bucket", scatter_dimension=0, tiled=True),
        lax.psum_scatter(grad_w_fc2, "bucket", scatter_dimension=0, tiled=True),
        lax.psum_scatter(grad_q_bias, "bucket", scatter_dimension=0, tiled=True),
        lax.psum_scatter(grad_v_bias, "bucket", scatter_dimension=0, tiled=True),
        lax.psum_scatter(grad_proj_bias, "bucket", scatter_dimension=0, tiled=True),
        lax.psum_scatter(grad_fc1_bias, "bucket", scatter_dimension=0, tiled=True),
        lax.psum_scatter(grad_fc2_bias, "bucket", scatter_dimension=0, tiled=True),
        lax.psum_scatter(grad_ada_weight, "bucket", scatter_dimension=0, tiled=True),
        lax.psum_scatter(grad_ada_bias, "bucket", scatter_dimension=0, tiled=True),
    )
    token_done = (
        lax.psum_scatter(bucket_done[0], "tok", scatter_dimension=1, tiled=True),
        lax.psum_scatter(bucket_done[1], "tok", scatter_dimension=1, tiled=True),
        lax.psum_scatter(bucket_done[2], "tok", scatter_dimension=1, tiled=True),
        lax.psum_scatter(bucket_done[3], "tok", scatter_dimension=1, tiled=True),
        lax.psum_scatter(bucket_done[4].reshape(1, -1), "tok", scatter_dimension=1, tiled=True),
        lax.psum_scatter(bucket_done[5].reshape(1, -1), "tok", scatter_dimension=1, tiled=True),
        lax.psum_scatter(bucket_done[6].reshape(1, -1), "tok", scatter_dimension=1, tiled=True),
        lax.psum_scatter(bucket_done[7].reshape(1, -1), "tok", scatter_dimension=1, tiled=True),
        lax.psum_scatter(bucket_done[8].reshape(1, -1), "tok", scatter_dimension=1, tiled=True),
    )
    finished = (
        token_done[0],
        token_done[1],
        token_done[2],
        token_done[3],
        token_done[4],
        token_done[5],
        token_done[6],
        token_done[7],
        token_done[8],
        bucket_done[9],
        bucket_done[10],
    )
    return (
        output,
        grad_tokens,
        finished[0],
        finished[4].reshape(-1),
        finished[5].reshape(-1),
        finished[1],
        finished[6].reshape(-1),
        finished[2],
        finished[7].reshape(-1),
        finished[3],
        finished[8].reshape(-1),
        finished[9],
        finished[10],
    )


def solution(mesh):
    planned = mesh.shape["tok"] == 4 and mesh.shape["bucket"] == 8
    return jax.shard_map(
        one_item_per_chip if planned else on_device,
        mesh=mesh,
        in_specs=(
            P("bucket", "tok", None),
            P("bucket", "tok", None),
            P("bucket"),
            P("bucket"),
            P(),
            P(),
            P("bucket", None),
            P(),
            P(),
            P(),
            P(),
            P(),
            P(),
            P(),
            P(),
            P(),
            P(None, "tok"),
            P("tok"),
        ),
        out_specs=(
            P("bucket", "tok", None),
            P("bucket", "tok", None),
            P("bucket", "tok"),
            P(("bucket", "tok")),
            P(("bucket", "tok")),
            P("bucket", "tok"),
            P(("bucket", "tok")),
            P("bucket", "tok"),
            P(("bucket", "tok")),
            P("bucket", "tok"),
            P(("bucket", "tok")),
            P("bucket", "tok"),
            P("bucket"),
        ),
        check_vma=False,
    )
```

```python
import functools
import math

import jax
import jax.numpy as jnp
import numpy as np
from jax import lax
from jax.experimental import pallas as pl
from jax.experimental.pallas import tpu as pltpu
from jax.sharding import PartitionSpec as P

HEADS = 16
EPSILON = 1e-06
LOG2E = 1.4426950408889634
GELU_K = math.sqrt(2.0 / math.pi)
GELU_C = 0.044715
LANES = 128
bf16, f32 = jnp.bfloat16, jnp.float32


def dot_nn(a, b):
    return lax.dot_general(a, b, (((1,), (0,)), ((), ())), preferred_element_type=f32)


def dot_nt(a, b):
    return lax.dot_general(a, b, (((1,), (1,)), ((), ())), preferred_element_type=f32)


def dot_tn(a, b):
    return lax.dot_general(a, b, (((0,), (0,)), ((), ())), preferred_element_type=f32)


def step_embedding(timesteps, model_width):
    half_width = model_width // 2
    frequency = jnp.exp(-math.log(10000.0) * jnp.arange(half_width, dtype=jnp.float32) / half_width)
    angles = timesteps.astype(jnp.float32)[:, None] * frequency[None, :]
    return jnp.concatenate([jnp.cos(angles), jnp.sin(angles)], axis=1)


def normalize(values):
    centred = values - jnp.mean(values, axis=-1, keepdims=True)
    inverse = lax.rsqrt(jnp.mean(centred * centred, axis=-1, keepdims=True) + EPSILON)
    return (centred * inverse, inverse)


def normalize_back(incoming, normed, inverse):
    return inverse * (
        incoming
        - jnp.mean(incoming, axis=-1, keepdims=True)
        - normed * jnp.mean(incoming * normed, axis=-1, keepdims=True)
    )


D = 1152
DC, DZ, TD = D // 8, D // 4, D // 4
HD = D // HEADS
HC = HEADS // 2
WC = D // 2
FF = 4608
NF = 3
FB = FF // 2 // NF
FZ = FB // 4
L = 1024
LH = L // 2
LB = L // 4
G1R = 3 * DC
G2R = 2 * FZ + FZ // 4
PR = 2 * DC + DC // 3
PA = 176
QR = 7 * DC + 16
QA = QR // 2
VMEM_LIMIT = 58 * 1024 * 1024


ANY = pl.BlockSpec(memory_space=pl.ANY)
MESH = pl.DeviceIdType.MESH


def place():
    b, t = lax.axis_index("bucket"), lax.axis_index("tok")
    return b // 2, b % 2, t // 2, t % 2


def flip(value, other):
    return (value // 2 + other // 2) % 2 * 2 + (value % 2 + other % 2) % 2


def peer(name):
    z, c, y, x = place()
    if name == "x":
        x = 1 - x
    elif name == "y":
        y = 1 - y
    elif name == "xy":
        x, y = 1 - x, 1 - y
    elif name == "c":
        c = 1 - c
    elif name in ("t0", "t1"):
        c, y, x = y, c, x if name == "t0" else 1 - x
    else:
        z = flip(z, int(name[1]))
    return (z * 2 + c, y * 2 + x)


def meet(names):
    sem = pltpu.get_barrier_semaphore()
    others = [name for name in names if name != "t0"]
    for name in others:
        pl.semaphore_signal(sem, inc=1, device_id=peer(name), device_id_type=MESH)
    wanted = len(others)
    if "t0" in names:
        _, c, y, _ = place()
        wanted = wanted + (c + y) % 2

        @pl.when(c != y)
        def _():
            pl.semaphore_signal(sem, inc=1, device_id=peer("t0"), device_id_type=MESH)

    pl.semaphore_wait(sem, wanted)


def remote(src, dst, sems, k, name):
    return pltpu.make_async_remote_copy(
        src_ref=src, dst_ref=dst, send_sem=sems.at[0, k], recv_sem=sems.at[1, k],
        device_id=peer(name), device_id_type=MESH,
    )


def vm(*shape, dtype=bf16):
    return pltpu.VMEM(shape, dtype)


class FirstSum:
    peers = ("x", "y")

    def __init__(self, keep_a, sent_a, keep_b, sent_b):
        self.ins = [keep_a, sent_a, keep_b, sent_b]
        shapes = [keep.shape[1:] for keep in (keep_a, keep_b)]
        self.outs = [jax.ShapeDtypeStruct(s, bf16) for s in shapes for _ in range(2)]
        self.scratch = [vm(*s) for s in shapes for _ in range(3)]
        self.scratch += [pltpu.SemaphoreType.DMA((2, 4)), pltpu.SemaphoreType.DMA((4,))]

    def plan(self, ins, outs, scratch):
        ka, sa, kb, sb = ins
        _, qa, _, qb = outs
        kav, rav, _, kbv, rbv, _, sems, local = scratch
        far = [
            remote(sa.at[1], rav, sems, 0, "x"),
            remote(sb.at[1], rbv, sems, 1, "y"),
            remote(sa.at[0], qa, sems, 2, "x"),
            remote(sb.at[0], qb, sems, 3, "y"),
        ]
        near = [
            pltpu.make_async_copy(ka.at[1], kav, local.at[0]),
            pltpu.make_async_copy(kb.at[1], kbv, local.at[1]),
        ]
        return far, near

    def finish(self, ins, outs, scratch):
        kav, rav, oav, kbv, rbv, obv, _, local = scratch
        oav[...] = (kav[...].astype(f32) + rav[...].astype(f32)).astype(bf16)
        obv[...] = (kbv[...].astype(f32) + rbv[...].astype(f32)).astype(bf16)
        return [
            pltpu.make_async_copy(oav, outs[0], local.at[2]),
            pltpu.make_async_copy(obv, outs[2], local.at[3]),
        ]


class SecondSum:
    peers = ("x", "y")

    def __init__(self, on_a, q_a, on_b, q_b, keep_a, keep_b):
        self.ins = [on_a, q_a, on_b, q_b, keep_a, keep_b]
        self.rows = [on_a.shape[1], on_b.shape[1]]
        total = sum(self.rows)
        self.outs = [jax.ShapeDtypeStruct((3, total, LANES), bf16), jax.ShapeDtypeStruct((total, LANES), f32)]
        self.scratch = [vm(4, r, LANES) for r in self.rows for _ in range(3)]
        self.scratch += [vm(3, total, LANES), vm(total, LANES, dtype=f32)]
        self.scratch += [pltpu.SemaphoreType.DMA((2, 2)), pltpu.SemaphoreType.DMA((6,))]

    def plan(self, ins, outs, scratch):
        oa, qa, ob, qb, ka, kb = ins
        kav, qav, rav, kbv, qbv, rbv, _, _, sems, local = scratch
        far = [remote(oa, rav, sems, 0, "y"), remote(ob, rbv, sems, 1, "x")]
        whole = len(ka.shape) == 4
        pairs = [(ka.at[0] if whole else ka, kav), (qa, qav), (kb.at[0] if whole else kb, kbv), (qb, qbv)]
        return far, [pltpu.make_async_copy(a, b, local.at[k]) for k, (a, b) in enumerate(pairs)]

    def finish(self, ins, outs, scratch):
        zs, zk, local = scratch[6], scratch[7], scratch[9]
        layer_sums([scratch[0:3], scratch[3:6]], zs, zk)
        return [
            pltpu.make_async_copy(zs, outs[0], local.at[4]),
            pltpu.make_async_copy(zk, outs[1], local.at[5]),
        ]


class ThirdSum:
    peers = ("z1", "z2", "z3")

    def __init__(self, sent, kept):
        self.ins = [sent, kept]
        self.outs = [jax.ShapeDtypeStruct(kept.shape, f32)]
        self.scratch = [vm(*sent.shape), vm(*kept.shape, dtype=f32)]
        self.scratch += [pltpu.SemaphoreType.DMA((2, 3)), pltpu.SemaphoreType.DMA((2,))]

    def plan(self, ins, outs, scratch):
        got, kept, sems, local = scratch
        far = [remote(ins[0].at[k], got.at[k], sems, k, f"z{k + 1}") for k in (2, 1, 0)]
        return far, [pltpu.make_async_copy(ins[1], kept, local.at[0])]

    def finish(self, ins, outs, scratch):
        got, kept, _, local = scratch
        kept[...] = kept[...] + got[0].astype(f32) + got[1].astype(f32) + got[2].astype(f32)
        return [pltpu.make_async_copy(kept, outs[0], local.at[1])]


def layer_sums(streams, zs, zk):
    start = 0
    for kv, qv, rv in streams:
        rows_ = rv.shape[1]
        for j in range(4):
            total = kv[j].astype(f32) + qv[j].astype(f32) + rv[j].astype(f32)
            if j == 0:
                zk[start : start + rows_, :] = total
            else:
                zs[j - 1, start : start + rows_, :] = total.astype(bf16)
        start += rows_


class SecondThird(SecondSum):
    peers = ("x", "y", "z1", "z2", "z3")

    def __init__(self, *args):
        super().__init__(*args)
        total = sum(self.rows)
        self.outs = [jax.ShapeDtypeStruct((total, LANES), f32)]
        self.scratch += [vm(3, total, LANES), pltpu.SemaphoreType.DMA((2, 3))]

    def third(self, scratch):
        zs, got, sems = scratch[6], scratch[10], scratch[11]
        return [remote(zs.at[k], got.at[k], sems, k, f"z{k + 1}") for k in (2, 1, 0)]

    def tick(self, ins, outs, scratch):
        for group in super().plan(ins, outs, scratch[:10]):
            for copy in group:
                copy.wait()
        layer_sums([scratch[0:3], scratch[3:6]], scratch[6], scratch[7])
        for copy in self.third(scratch):
            copy.start()

    def plan(self, ins, outs, scratch):
        return super().plan(ins, outs, scratch[:10])

    def settle(self, ins, outs, scratch):
        return self.third(scratch)

    def finish(self, ins, outs, scratch):
        kept, local, got = scratch[7], scratch[9], scratch[10]
        kept[...] = kept[...] + got[0].astype(f32) + got[1].astype(f32) + got[2].astype(f32)
        return [pltpu.make_async_copy(kept, outs[0], local.at[5])]


class FirstSecond:
    peers = ("x", "y")

    def __init__(self, keep_a, sent_a, keep_b, sent_b):
        self.ins = [keep_a, sent_a, keep_b, sent_b]
        self.rows = [keep_a.shape[2], keep_b.shape[2]]
        total = sum(self.rows)
        self.outs = [jax.ShapeDtypeStruct((3, total, LANES), bf16), jax.ShapeDtypeStruct((total, LANES), f32)]
        self.scratch = []
        for r in self.rows:
            self.scratch += [vm(2, 4, r, LANES), vm(2, 4, r, LANES), vm(4, r, LANES), vm(4, r, LANES)]
        self.scratch += [vm(3, total, LANES), vm(total, LANES, dtype=f32)]
        self.scratch += [pltpu.SemaphoreType.DMA((2, 6)), pltpu.SemaphoreType.DMA((4,))]

    def plan(self, ins, outs, scratch):
        ka, sa, kb, sb = ins
        sems, local = scratch[10:]
        far = [
            remote(sa.at[1], scratch[1].at[1], sems, 0, "x"),
            remote(sb.at[1], scratch[5].at[1], sems, 1, "y"),
            remote(sa.at[0], scratch[1].at[0], sems, 2, "x"),
            remote(sb.at[0], scratch[5].at[0], sems, 3, "y"),
        ]
        near = [pltpu.make_async_copy(k, scratch[4 * j], local.at[j]) for j, k in enumerate((ka, kb))]
        return far, near

    def second(self, scratch):
        sems = scratch[10]
        return [remote(scratch[4 * j + 2], scratch[4 * j + 3], sems, 4 + j, name) for j, name in enumerate("yx")]

    def tick(self, ins, outs, scratch):
        for group in self.plan(ins, outs, scratch):
            for copy in group:
                copy.wait()
        for j in range(2):
            kv, rv, on = scratch[4 * j : 4 * j + 3]
            on[...] = (kv[1].astype(f32) + rv[1].astype(f32)).astype(bf16)
        for copy in self.second(scratch):
            copy.start()

    def settle(self, ins, outs, scratch):
        return self.second(scratch)

    def finish(self, ins, outs, scratch):
        zs, zk, local = scratch[8], scratch[9], scratch[11]
        layer_sums([(scratch[j].at[0], scratch[j + 1].at[0], scratch[j + 3]) for j in (0, 4)], zs, zk)
        return [
            pltpu.make_async_copy(zs, outs[0], local.at[2]),
            pltpu.make_async_copy(zk, outs[1], local.at[3]),
        ]


class GoHome:
    peers = ("t0", "t1")

    def __init__(self, values):
        self.ins = [values]
        self.outs = [jax.ShapeDtypeStruct((2, LB, D), values.dtype)]
        self.scratch = [pltpu.SemaphoreType.DMA((2, 2)), pltpu.SemaphoreType.DMA]

    def plan(self, ins, outs, scratch):
        return [], []

    def tick(self, ins, outs, scratch):
        home_start(*self.copies(ins, outs, scratch))

    def copies(self, ins, outs, scratch):
        return homeward(ins[0].at[pl.ds(0, LB)], ins[0].at[pl.ds(LB, LB)], outs[0], *scratch)

    def settle(self, ins, outs, scratch):
        home_wait(*self.copies(ins, outs, scratch))
        return []

    def finish(self, ins, outs, scratch):
        return []


def homeward(first, second, dst, sems, local):
    x = place()[3]
    return (
        remote(first, dst.at[x], sems, 0, "t0"),
        pltpu.make_async_copy(first, dst.at[x], local),
        remote(second, dst.at[x], sems, 1, "t1"),
    )


def home_start(away, stay, second):
    _, c, y, _ = place()
    pl.when(c != y)(away.start)
    pl.when(c == y)(stay.start)
    second.start()


def home_wait(away, stay, second):
    _, c, y, _ = place()
    pl.when(c != y)(away.wait)
    pl.when(c == y)(stay.wait)
    second.wait()


def call(kernel, name, out_shape, args, in_specs=None, out_specs=None, scratch=(), grid=None,
         peers=(), jobs=(), cid=None, ticks=False, flops=0, nbytes=0):
    whole = pl.BlockSpec(memory_space=pltpu.VMEM)
    single = not isinstance(out_shape, (tuple, list))
    out_shape = [out_shape] if single else list(out_shape)
    in_specs = list(in_specs) if in_specs is not None else [whole] * len(args)
    out_specs = [whole] * len(out_shape) if out_specs is None else [out_specs] if single else list(out_specs)
    counts = [len(args), sum(len(j.ins) for j in jobs), len(out_shape), sum(len(j.outs) for j in jobs), len(scratch)]
    names = sorted(set(peers).union(*[j.peers for j in jobs]))

    def run(*refs):
        groups, at = [], 0
        for n in counts:
            groups.append(refs[at : at + n])
            at += n
        bound, ai, ao, asc = [], 0, 0, at
        for j in jobs:
            bound.append((
                j, groups[1][ai : ai + len(j.ins)], groups[3][ao : ao + len(j.outs)], refs[asc : asc + len(j.scratch)]
            ))
            ai, ao, asc = ai + len(j.ins), ao + len(j.outs), asc + len(j.scratch)

        def begin():
            if names:
                meet(names)
            for j, *r in bound:
                for group in j.plan(*r):
                    for copy in group:
                        copy.start()

        def end():
            last = []
            for j, *r in bound:
                far, near = (j.settle(*r), []) if hasattr(j, "tick") else j.plan(*r)
                for copy in far:
                    copy.wait()
                for copy in near:
                    copy.wait()
                copies = j.finish(*r)
                for copy in copies:
                    copy.start()
                last += copies
            for copy in last:
                copy.wait()

        def tick():
            for j, *r in bound:
                if hasattr(j, "tick"):
                    j.tick(*r)

        if grid is None:
            begin()
            kernel(*groups[0], *groups[2], *groups[4], **({"tick": tick} if ticks else {}))
            end()
        else:
            pl.when(pl.program_id(0) == 0)(begin)
            kernel(*groups[0], *groups[2], *groups[4])
            pl.when(pl.program_id(0) == grid[0] - 1)(end)

    extra = {} if grid is None else {"grid": grid}
    params = {"collective_id": cid, "has_side_effects": True} if names else {}
    outs = pl.pallas_call(
        run,
        out_shape=out_shape + [o for j in jobs for o in j.outs],
        in_specs=in_specs + [ANY] * counts[1],
        out_specs=out_specs + [ANY] * counts[3],
        scratch_shapes=list(scratch) + [q for j in jobs for q in j.scratch],
        compiler_params=pltpu.CompilerParams(vmem_limit_bytes=VMEM_LIMIT, **params),
        cost_estimate=pl.CostEstimate(flops=int(flops), bytes_accessed=int(nbytes), transcendentals=0),
        name=name,
        **extra,
    )(*args, *[a for j in jobs for a in j.ins])
    own, rest, given = outs[: len(out_shape)], outs[len(out_shape) :], []
    for j in jobs:
        given.append(rest[: len(j.outs)])
        rest = rest[len(j.outs) :]
    return (own[0] if single else own), given


def full(shape):
    return pl.BlockSpec(shape, lambda *_: (0,) * len(shape))


def once(*shape):
    return pl.BlockSpec(shape, lambda *_: (0,) * len(shape), pipeline_mode=pl.Buffered(1))


def rows(block, width):
    return pl.BlockSpec((block, width), lambda i: (i, 0))


def column(n):
    return lax.broadcasted_iota(jnp.int32, (n, 1), 0)


def front_kernel(tokens, cotangent, timesteps, bucket_ids, skips, ada_w, ada_b, head_masks, channel_masks, w_qkv, w_fc1,
                 q_bias, v_bias, b1, freq, tok_o, cot_o, shifted_o, qkv_o, wq_o, w1_o, mod_o, kept_o, hmask_o, chan_o, b1_o,
                 tk, ck, wqv, wqc, w1v, w1c, adav, ints, ints_other, m4, to_send, shares, csems, tsems, ssems, lsems):
    z, c, y, x = place()
    t = 2 * y + x
    loads = [
        pltpu.make_async_copy(a, b, lsems.at[k])
        for k, (a, b) in enumerate(((ada_w, adav), (w_qkv, wqv), (w_fc1, w1v)))
    ]

    def arrivals(src, dst, k):
        block = [dst.at[pl.ds(LB * j, LB)] for j in range(4)]
        first = remote(src.at[x], block[0], tsems, k, "t0")
        stay = pltpu.make_async_copy(src.at[x], block[0], lsems.at[3 + k])
        second = remote(src.at[1 - x], block[1], tsems, 2 + k, "t1")
        onward = [remote(block[j], block[2 + j], csems, 2 * k + j, "c") for j in range(2)]
        return first, stay, second, onward

    def leave(first, stay, second, onward):
        pl.when(c != y)(first.start)
        pl.when(c == y)(stay.start)
        second.start()

    def pass_on(first, stay, second, onward):
        pl.when(c != y)(first.wait_recv)
        pl.when(c == y)(stay.wait)
        onward[0].start()
        second.wait_recv()
        onward[1].start()

    def settle(first, stay, second, onward):
        pl.when(c != y)(first.wait_send)
        second.wait_send()
        for copy in onward:
            copy.wait_send()

    tok_moves, cot_moves = arrivals(tokens, tk, 0), arrivals(cotangent, ck, 1)
    leave(*tok_moves)
    halves = [skips[:, :LANES], skips[:, LANES:]]
    ints[0:4, :] = jnp.concatenate([halves[0][0:1], halves[1][0:1], halves[0][1:2], halves[1][1:2]], axis=0)
    for k, value in enumerate((timesteps[0], timesteps[1], bucket_ids[0], 0)):
        ints[4 + k : 5 + k, :] = jnp.full((1, LANES), value, jnp.int32)
    swap = remote(ints, ints_other, csems, 4, "c")
    swap.start()
    for load in loads:
        load.start()
    swap.wait()

    mine, other = ints[...], ints_other[...]
    r = column(8)
    steps = jnp.zeros((8, 1), f32)
    for k in range(2):
        steps = jnp.where(r == 2 * c + k, mine[4 + k : 5 + k, 0:1].astype(f32), steps)
        steps = jnp.where(r == 2 * (1 - c) + k, other[4 + k : 5 + k, 0:1].astype(f32), steps)
    angles = steps * freq[...]
    condition = jax.nn.silu(jnp.concatenate([jnp.cos(angles), jnp.sin(angles)], axis=1))
    condition = jnp.concatenate([condition, jnp.zeros_like(condition)], axis=0).astype(bf16)
    loads[0].wait()
    m4[...] = dot_nt(condition, adav[...])[:8] + ada_b[...].astype(f32).reshape(1, -1)
    moves = []
    for k in range(4):
        to = (y + k // 2) % 2 * 2 + (x + k) % 2
        row = jnp.broadcast_to(m4[pl.ds(to, 1), :], to_send.shape[1:])
        if k == 0:
            shares[t] = row
        else:
            to_send[k - 1] = row
            moves.append(remote(to_send.at[k - 1], shares.at[t], ssems, k - 1, ("x", "y", "xy")[k - 1]))
            moves[-1].start()

    group = jnp.where(c == y, mine, other)
    bucket = group[6:7, 0:1]
    skip = jnp.where(x == 0, group[0:2], group[2:4])
    for j in range(4):
        block = 2 * ((c + j // 2) % 2) + (x + j) % 2
        position = column(LB) + LB * block
        hit = jnp.where((position == skip[0:1, :]) | (position == skip[1:2, :]), 1.0, 0.0)
        kept_o[LB * j : LB * (j + 1), :] = 1.0 - jnp.max(hit, axis=1, keepdims=True)

    def chosen(masks):
        line = lax.broadcasted_iota(jnp.int32, masks.shape, 0)
        row = jnp.sum(jnp.where(line == bucket, masks[...].astype(f32), 0.0), axis=0, keepdims=True)
        return jnp.broadcast_to(row, (16, masks.shape[1])).astype(bf16)

    def spread(on, low, width):
        first = width * lax.broadcasted_iota(jnp.int32, (on.shape[1], low.shape[1]), 0)
        return dot_nn(on, jnp.where((low >= first) & (low < first + width), 1.0, 0.0).astype(bf16))[0:1, :]

    lane = lax.broadcasted_iota(jnp.int32, (1, WC), 1)
    share = sum(jnp.where(lane >= DC * k, 1, 0) for k in range(1, 4))
    hmask_o[...] = spread(chosen(head_masks), lane + DC * (share + c), HD)
    channels = chosen(channel_masks)
    lane = lax.broadcasted_iota(jnp.int32, (1, FB), 1)
    share = sum(jnp.where(lane >= FZ * k, 1, 0) for k in range(1, 4))
    for f in range(NF):
        low = lane + (4 * DZ - FZ) * share + FF // 8 * c + FZ * f
        chan_o[f] = spread(channels, low, FF // channels.shape[1])

    def half(v, k, width):
        v = v[:, 2 * width * k : 2 * width * (k + 1)]
        return jnp.where(c == 0, v[:, :width], v[:, width:])

    def line(ref):
        return ref[...].astype(f32).reshape(1, -1)

    bias = [half(line(q_bias), k, DC) for k in range(4)]
    bias += [jnp.zeros((1, WC), f32)] + [half(line(v_bias), k, DC) for k in range(4)]
    bias = jnp.concatenate(bias, axis=1)
    b1v = [half(line(b1), k, FF // 8) for k in range(4)]
    for f in range(NF):
        b1_o[f] = jnp.concatenate([v[:, FZ * f : FZ * (f + 1)] for v in b1v], axis=1)
    loads[1].wait()
    loads[2].wait()
    for core in range(2):

        @pl.when(c == core)
        def _():
            for k in range(12):
                wqc[:, DC * k : DC * (k + 1)] = wqv[:, DZ * k + DC * core : DZ * k + DC * (core + 1)]
            for f in range(NF):
                for k in range(4):
                    start = 4 * DZ * k + FF // 8 * core + FZ * f
                    w1c[f, :, FZ * k : FZ * (k + 1)] = w1v[:, start : start + FZ]

    stores = [
        pltpu.make_async_copy(a, b, lsems.at[k]) for k, (a, b) in enumerate(((wqc, wq_o), (w1c, w1_o)))
    ]
    for store in stores:
        store.start()
    pass_on(*tok_moves)
    leave(*cot_moves)
    for copy in moves:
        copy.wait()
    share_rows = [shares[k][0:1, :] for k in range(4)]
    n, m = D // 2, 3 * D // 2
    mod = [share_rows[0][:, :D], jnp.concatenate([share_rows[0][:, D:], share_rows[1][:, :n]], axis=1),
           share_rows[1][:, n:], share_rows[2][:, :D],
           jnp.concatenate([share_rows[2][:, D:], share_rows[3][:, :n]], axis=1), share_rows[3][:, n:]]
    own_step = 0.5 * jnp.sum(jnp.where(r == t, steps, 0.0), axis=0, keepdims=True)
    mod += [jnp.broadcast_to(own_step, (1, D)), jnp.zeros((1, D), f32)]
    mod_o[...] = jnp.concatenate(mod, axis=0)
    for j in range(4):
        if j >= 2:
            tok_moves[3][j - 2].wait_recv()
        part = slice(LB * j, LB * (j + 1))
        normed, _ = normalize(tk[part, :].astype(f32))
        shifted = (normed * (1.0 + mod[1]) + mod[0]).astype(bf16)
        shifted_o[part, :] = shifted
        qkv_o[part, :] = (dot_nn(shifted, wqc[...]) + bias).astype(bf16)
    keep = pltpu.make_async_copy(tk, tok_o, lsems.at[2])
    keep.start()
    pass_on(*cot_moves)
    for copy in cot_moves[3]:
        copy.wait_recv()
    keep_cot = pltpu.make_async_copy(ck, cot_o, lsems.at[5])
    keep_cot.start()
    settle(*tok_moves)
    settle(*cot_moves)
    for store in stores:
        store.wait()
    keep.wait()
    keep_cot.wait()


def attn_kernel(step, qkv, hmask, wp, bias, tok, mod, mixed_o, shifted2_o, attn_o,
                qh, kh, vh, mx, mo, wpv, tkv, csems, lsems):
    c = place()[1]
    loads = [
        pltpu.make_async_copy(wp.at[:, c], wpv.at[0], lsems.at[0]),
        pltpu.make_async_copy(wp.at[:, 1 - c], wpv.at[1], lsems.at[1]),
        pltpu.make_async_copy(tok, tkv, lsems.at[2]),
    ]
    for load in loads:
        load.start()
    scale = LOG2E / math.sqrt(HD)
    for h in range(HC):
        for k, ref in enumerate((qh, kh, vh)):
            ref[h] = qkv[:, WC * k + HD * h : WC * k + HD * (h + 1)]

    def crossing(i):
        src = mx.at[pl.ds(pl.multiple_of(i * step, step), step)]
        dst = mo.at[pl.ds(pl.multiple_of((i * step + LH) % L, step), step)]
        return remote(src, dst, csems, i, "c")

    def body(i, carry):
        part = pl.ds(pl.multiple_of(i * step, step), step)
        outs = []
        for h in range(HC):
            s = dot_nt(qh[h, part, :], kh[h])
            top = jnp.max(s, axis=1, keepdims=True)
            p = jnp.exp2((s - top) * scale)
            total = jnp.sum(p, axis=1, keepdims=True)
            outs.append(dot_nn(p.astype(bf16), vh[h]) * (1.0 / total))
        mx[part, :] = (jnp.concatenate(outs, axis=1) * hmask[...]).astype(bf16)
        crossing(i).start()
        return carry

    lax.fori_loop(0, L // step, body, 0)
    keep = pltpu.make_async_copy(mx, mixed_o, lsems.at[3])
    keep.start()
    for load in loads:
        load.wait()
    for i in range(L // step):
        crossing(i).wait()
    w_mine, w_other = wpv[0].reshape(WC, D), wpv[1].reshape(WC, D)
    bias_line = bias[...].astype(f32).reshape(1, D)
    for j in range(4):
        part = slice(LB * j, LB * (j + 1))
        attn = dot_nn(mx[part, :], w_mine) + dot_nn(mo[part, :], w_other) + bias_line
        if j < 2:
            attn_o[part, :] = attn
        normed, _ = normalize(tkv[part, :].astype(f32) + mod[2:3, :] * attn)
        shifted2_o[part, :] = (normed * (1.0 + mod[4:5, :]) + mod[3:4, :]).astype(bf16)
    keep.wait()


def mlp_kernel(sh2, g, kept, mod, w1, b1, chan, w2,
               on_a0, q_a0, on_b0, q_b0, keep_a0, keep_b0, on_a1, q_a1, on_b1, q_b1, keep_a1, keep_b1,
               k2a, s2a, k2b, s2b, branch_o, ds2_o, branch_r, ds2_r, sum1_o, sum2_o,
               sh2v, gv, dbs, w1v, w2v, hid, dpre, br, ds, far, tt_, ka, sa, kb, sb, ra, rb, ona, onb,
               fsems, csems, lsems, wsems, osems):
    z, c, y, x = place()
    out0 = (on_a0, q_a0, on_b0, q_b0, keep_a0, keep_b0)
    out1 = (on_a1, q_a1, on_b1, q_b1, keep_a1, keep_b1)
    outs = (out0, out1)

    def weights(f):
        return [
            pltpu.make_async_copy(w1.at[f], w1v.at[f % 2], wsems.at[0, f % 2]),
            pltpu.make_async_copy(w2.at[:, c, f], w2v.at[f % 2], wsems.at[1, f % 2]),
        ]

    def first(f):
        k, out = f % 2, outs[f]
        return [
            remote(sa.at[k, 1], ra.at[k], fsems, 4 * k, "x"), remote(sb.at[k, 1], rb.at[k], fsems, 4 * k + 1, "y"),
            remote(sa.at[k, 0], out[1], fsems, 4 * k + 2, "x"), remote(sb.at[k, 0], out[3], fsems, 4 * k + 3, "y"),
        ]

    def stored(f):
        k = f % 2
        if f == NF - 1:
            pairs = ((ka.at[k], k2a), (sa.at[k], s2a), (kb.at[k], k2b), (sb.at[k], s2b))
        else:
            pairs = ((ka.at[k, 0], outs[f][4]), (kb.at[k, 0], outs[f][5]))
        return [pltpu.make_async_copy(src, dst, osems.at[k, j]) for j, (src, dst) in enumerate(pairs)]

    def onward(f):
        k = f % 2
        for copy in first(f):
            copy.wait()
        for kv, rv, on in ((ka, ra, ona), (kb, rb, onb)):
            on[k] = (kv[k, 1].astype(f32) + rv[k].astype(f32)).astype(bf16)
        copies = [
            pltpu.make_async_copy(src.at[k], dst, osems.at[k, 4 + j])
            for j, (src, dst) in enumerate(((ona, outs[f][0]), (onb, outs[f][2])))
        ]
        for copy in copies:
            copy.start()
        return copies

    loads = [pltpu.make_async_copy(src, dst, lsems.at[k]) for k, (src, dst) in enumerate(((g, gv), (sh2, sh2v)))]
    for copy in loads + weights(0):
        copy.start()
    loads[0].wait()
    sum2 = jnp.zeros((1, D), f32)
    for j in range(4):
        part = slice(LB * j, LB * (j + 1))
        db = (gv[part, :].astype(f32) * mod[5:6, :] * kept[part, :]).astype(bf16)
        dbs[part, :] = db
        sum2 += jnp.sum(db.astype(f32), axis=0, keepdims=True)
    sum2_o[...] = sum2
    loads[1].wait()
    crossing = [remote(far.at[j], dst, csems, j, "c") for j, dst in enumerate((branch_r, ds2_r))]
    waiting = []
    for f in range(NF):
        for copy in weights(f):
            copy.wait()
        if f + 1 < NF:
            for copy in weights(f + 1):
                copy.start()
        w1f, w2f = w1v[f % 2], w2v[f % 2].reshape(FB, D)
        on = chan[f]
        sum1 = jnp.zeros((1, FB), f32)
        for side in (1, 0):
            part = slice(LH * side, LH * (side + 1))
            v = dot_nn(sh2v[part, :], w1f) + b1[f]
            v2 = v * v
            th = jnp.tanh(GELU_K * v * (1.0 + GELU_C * v2))
            half = 0.5 * (1.0 + th)
            hidden = (v * half * on).astype(bf16)
            hid[part, :] = hidden
            slope = (half + (0.5 * GELU_K) * v * (1.0 - th * th) * (1.0 + (3.0 * GELU_C) * v2)) * on
            d_pre = (dot_nt(dbs[part, :], w2f) * slope).astype(bf16)
            dpre[part, :] = d_pre
            sum1 += jnp.sum(d_pre.astype(f32), axis=0, keepdims=True)
            branch, ds2 = dot_nn(hidden, w2f), dot_nt(d_pre, w1f)
            if f > 0:
                branch, ds2 = branch + br[part, :], ds2 + ds[part, :]
            if f < NF - 1:
                br[part, :] = branch
                ds[part, :] = ds2
            elif side == 1:
                far[0] = branch.astype(bf16)
                far[1] = ds2.astype(bf16)
                for copy in crossing:
                    copy.start()
            else:
                branch_o[...] = branch.astype(bf16)
                ds2_o[...] = ds2.astype(bf16)
        sum1_o[f] = sum1
        k = f % 2
        for m in range(3):
            cut = slice(m * D // 3, (m + 1) * D // 3)
            p = dot_tn(sh2v[:, cut], dpre[...]).astype(bf16)
            for t in range(4):
                tt_[t, cut, :FZ] = p[:, FZ * t : FZ * (t + 1)]
        for rz in range(4):
            zz = flip(z, rz)
            for ry in range(2):
                for rx in range(2):
                    tt = (ry + y) % 2 * 2 + (rx + x) % 2
                    o = (ka, sa)[rx]
                    tails = []
                    for rc in range(2):
                        block = tt_[tt, pl.ds(pl.multiple_of(zz * DZ + (rc + c) % 2 * DC, 16), DC), :FZ]
                        o[k, ry, rz, DC * rc : DC * (rc + 1), :] = block[:, :LANES]
                        tails.append(block[:, LANES:])
                    o[k, ry, rz, 2 * DC :, :] = jnp.concatenate(tails, axis=1)
        for m in range(3):
            cut = slice(m * FB // 3, (m + 1) * FB // 3)
            p = dot_tn(hid[:, cut], dbs[...]).astype(bf16)
            for t in range(4):
                tt_[t, cut, :] = p[:, TD * t : TD * (t + 1)]
        for rz in range(4):
            zz = flip(z, rz)
            for ry in range(2):
                for rx in range(2):
                    tt = (ry + y) % 2 * 2 + (rx + x) % 2
                    o = (kb, sb)[ry]
                    block = tt_[tt, pl.ds(pl.multiple_of(zz * FZ, 16), FZ), :]
                    o[k, rx, rz, :FZ, :] = block[:, :LANES]
                    o[k, rx, rz, FZ : 2 * FZ, :] = block[:, LANES : 2 * LANES]
                    q = FZ // 4
                    o[k, rx, rz, 2 * FZ :, :] = jnp.concatenate(
                        [block[q * j : q * (j + 1), 2 * LANES :] for j in range(4)], axis=1
                    )
        if f < NF - 1:
            for copy in first(f):
                copy.start()
        for copy in stored(f):
            copy.start()
        waiting += stored(f)
        if f > 0:
            waiting += onward(f - 1)
        if f == NF - 2:
            for copy in waiting:
                copy.wait()
            waiting = []
    for copy in waiting + crossing:
        copy.wait()


def middle_kernel(ds, ds_r, br, br_r, attn, tok, g, kept, mod, bias2, mixed, wp,
                  d_resid_o, out_o, dh_o, pka, psa, pkb, psb, sums_o, sum_o, da, t1, wpv, csems, lsem):
    i = pl.program_id(0)
    n = LH // 4
    z, c, y, x = place()
    part = pl.ds(pl.multiple_of(i * n, n), n)
    gf, at = g[...].astype(f32), attn[...]
    resid = tok[...].astype(f32) + mod[2:3, :] * at
    normed2, inverse2 = normalize(resid)
    ds2 = ds[...].astype(f32) + ds_r[...].astype(f32)
    kb = kept[...] * (br[...].astype(f32) + br_r[...].astype(f32) + bias2[...].astype(f32).reshape(1, D))
    out_o[...] = (resid + mod[5:6, :] * kb).astype(bf16)
    d_resid = gf + normalize_back(ds2 * (1.0 + mod[4:5, :]), normed2, inverse2)
    d_resid_o[...] = d_resid
    da[part, :] = (mod[2:3, :] * d_resid).astype(bf16)
    sums = [jnp.sum(p, axis=0, keepdims=True) for p in (at * d_resid, ds2, ds2 * normed2, kb * gf)]
    sums = jnp.concatenate(sums + [jnp.zeros((4, D), f32)], axis=0)

    @pl.when(i == 0)
    def _():
        sums_o[...] = sums

    @pl.when(i > 0)
    def _():
        sums_o[...] += sums

    crossing = [
        remote(da.at[pl.ds(n * k, n)], da.at[pl.ds(LH + n * k, n)], csems, k, "c") for k in range(4)
    ]
    load = pltpu.make_async_copy(wp.at[:, c], wpv, lsem)
    pl.when(i == 0)(load.start)
    for k in range(4):
        pl.when(i == k)(crossing[k].start)

    @pl.when(i == 3)
    def _():
        for copy in crossing:
            copy.wait()
        load.wait()
        wv = wpv[...].reshape(WC, D)
        dh_o[...] = dot_nt(da[...], wv).astype(bf16)
        sum_o[...] = dot_nn(jnp.ones((16, L), bf16), da[...])[:8]
        grad = dot_tn(mixed[...], da[...]).astype(bf16)
        for t in range(4):
            t1[t] = grad[:, TD * t : TD * (t + 1)]
        for rz in range(4):
            zz = flip(z, rz)
            for ry in range(2):
                for rx in range(2):
                    tt = (ry + y) % 2 * 2 + (rx + x) % 2
                    a, b = (pka, psa)[rx], (pkb, psb)[ry]
                    block = t1[tt, pl.ds(pl.multiple_of(zz * DC, 16), DC), :]
                    a[ry, rz, :DC, :] = block[:, :LANES]
                    a[ry, rz, DC:, :] = block[: PA - DC, LANES : 2 * LANES]
                    b[rx, rz, : 2 * DC - PA, :] = block[PA - DC :, LANES : 2 * LANES]
                    q = DC // 3
                    tails = [block[q * k : q * (k + 1), 2 * LANES :] for k in range(3)]
                    tails.append(jnp.zeros((q, 32), bf16))
                    b[rx, rz, 2 * DC - PA :, :] = jnp.concatenate(tails, axis=1)


def attn_back_kernel(step, qkv, dh, hmask, out, qh, kh, vh, doh, dk, dv, tick):
    scale = LOG2E / math.sqrt(HD)
    for h in range(HC):
        for k, ref in enumerate((qh, kh, vh)):
            ref[h] = qkv[:, WC * k + HD * h : WC * k + HD * (h + 1)]
        cut = slice(HD * h, HD * (h + 1))
        doh[h] = (dh[:, cut].astype(f32) * hmask[:, cut]).astype(bf16)
    dk[...] = jnp.zeros_like(dk)
    dv[...] = jnp.zeros_like(dv)

    def body(i, carry):
        part = pl.ds(pl.multiple_of(i * step, step), step)
        outs = []
        for h in range(HC):
            q, do = qh[h, part, :], doh[h, part, :]
            s = dot_nt(kh[h], q)
            top = jnp.max(s, axis=0, keepdims=True)
            p = jnp.exp2((s - top) * scale)
            p = p * (1.0 / jnp.sum(p, axis=0, keepdims=True))
            dp = dot_nt(vh[h], do)
            row_dot = jnp.sum(p * dp, axis=0, keepdims=True)
            ds = (p * (dp - row_dot)).astype(bf16)
            dv[h] += dot_nn(p.astype(bf16), do)
            dk[h] += dot_nn(ds, q)
            outs.append(dot_tn(ds, kh[h]))
        out[part, :WC] = (jnp.concatenate(outs, axis=1) * (1.0 / math.sqrt(HD))).astype(bf16)
        return carry

    lax.fori_loop(0, L // step // 2, body, 0)
    tick()
    lax.fori_loop(L // step // 2, L // step, body, 0)
    for h in range(HC):
        out[:, WC + HD * h : WC + HD * (h + 1)] = (dk[h] * (1.0 / math.sqrt(HD))).astype(bf16)
        out[:, 2 * WC + HD * h : 2 * WC + HD * (h + 1)] = dv[h].astype(bf16)


def end_kernel(shifted, dqkv, extra, wq, d_resid, tok, mod, sums_mid, f0, f1, sent_2, kept_2, sent_p, kept_p, freq,
               grad, gq_o, gp_o, g1_o, g2_o, ada_o, ada_bias_o, line_o,
               t1, ka, sa, kb, sb, ra, rb, ona, onb, r2a, r2b, zs, zk, zr, wqv, dres, tokv, fv, far, got, gb,
               item, item_r, out_shares, square, every, row_out, row_in, mine, theirs, mine_q, theirs_q, pk, pr, br,
               qsems, csems, tsems, ssems, psems, lsems):
    z, c, y, x = place()
    t, b = 2 * y + x, 2 * z + c
    loads = [
        pltpu.make_async_copy(src, dst, lsems.at[k])
        for k, (src, dst) in enumerate(
            ((wq, wqv), (d_resid, dres), (tok.at[pl.ds(0, LH)], tokv), (f0, fv.at[0]), (f1, fv.at[1]),
             (kept_2, fv.at[2]), (kept_p, pk))
        )
    ]
    third_p = [remote(sent_2.at[k], br.at[k], psems, 3 + k, f"z{k + 1}") for k in (2, 1, 0)]
    third_p += [remote(sent_p.at[k], pr.at[k], psems, k, f"z{k + 1}") for k in (2, 1, 0)]
    for copy in third_p + loads:
        copy.start()

    for k in range(4):
        p = dot_tn(shifted[:, DZ * k : DZ * (k + 1)], dqkv[...]).astype(bf16)
        for j in range(4):
            t1[j, DZ * k : DZ * (k + 1), :] = p[:, 3 * DC * j : 3 * DC * (j + 1)]
    sums = dot_nn(jnp.ones((16, L), bf16), dqkv[...])[0:1, :]
    for z_ in range(4):
        for t_ in range(4):
            piece = DC * z_ + DC // 4 * t_
            qsum = sums[:, piece : piece + DC // 4]
            vsum = sums[:, 2 * WC + piece : 2 * WC + piece + DC // 4]
            row1 = jnp.concatenate([jnp.zeros((1, 88), f32), qsum, jnp.zeros((1, 4), f32)], axis=1)
            row2 = jnp.concatenate([vsum, jnp.zeros((1, LANES - DC // 4), f32)], axis=1)
            add = jnp.concatenate([jnp.zeros((1, LANES), f32), row1, row2, jnp.zeros((13, LANES), f32)], axis=0)
            rz, ry, rx = flip(z, z_), (t_ // 2 + y) % 2, (t_ % 2 + x) % 2
            block = (extra[z_, t_] + add).astype(bf16)

            @pl.when(ry == 0)
            def _():
                kb[rx, rz, QA - 16 :, :] = block

            @pl.when(ry == 1)
            def _():
                sb[rx, rz, QA - 16 :, :] = block

    for rz in range(4):
        zz = flip(z, rz)
        for ry in range(2):
            for rx in range(2):
                tt = (ry + y) % 2 * 2 + (rx + x) % 2
                one, two = (ka, sa)[rx], (kb, sb)[ry]
                parts = [
                    t1[tt, pl.ds(pl.multiple_of(zz * DZ + (rc + c) % 2 * DC, 16), DC), :] for rc in range(2)
                ]
                strips = [p[:, LANES * k : LANES * (k + 1)] for k in range(3) for p in parts]
                gap = jnp.zeros((DC, 16), bf16)
                strips.append(jnp.concatenate([parts[0][:, 3 * LANES :], gap, parts[1][:, 3 * LANES :], gap], axis=1))
                for k, strip in enumerate(strips):
                    first = DC * k
                    if first + DC <= QA:
                        one[ry, rz, first : first + DC, :] = strip
                    elif first >= QA:
                        two[rx, rz, first - QA : first - QA + DC, :] = strip
                    else:
                        one[ry, rz, first:, :] = strip[: QA - first]
                        two[rx, rz, : first + DC - QA, :] = strip[QA - first :]
    first_q = [
        remote(sa.at[1], ra.at[1], qsems, 0, "x"), remote(sb.at[1], rb.at[1], qsems, 1, "y"),
        remote(sa.at[0], ra.at[0], qsems, 2, "x"), remote(sb.at[0], rb.at[0], qsems, 3, "y"),
    ]
    for copy in first_q:
        copy.start()

    loads[0].wait()
    crossing = [remote(far.at[k], got.at[k], csems, k, "c") for k in range(2)]
    for k in range(2):
        far[k] = dot_nt(dqkv[LH + LB * k : LH + LB * (k + 1), :], wqv[...]).astype(bf16)
        crossing[k].start()
    loads[1].wait()
    loads[2].wait()
    total_sums = sums_mid[0:4, :]
    token_sums = jnp.zeros((2, D), f32)
    for k in range(2):
        part = slice(LB * k, LB * (k + 1))
        mine_rows = dot_nt(dqkv[part, :], wqv[...])
        crossing[k].wait()
        total = mine_rows + got[k].astype(f32)
        normed, inverse = normalize(tokv[part, :].astype(f32))
        back = dres[part, :] + normalize_back(total * (1.0 + mod[1:2, :]), normed, inverse)
        gb[k] = back.astype(bf16)
        token_sums += jnp.concatenate(
            [jnp.sum(v, axis=0, keepdims=True) for v in (total, total * normed)], axis=0
        )
    item[...] = jnp.concatenate([token_sums, total_sums, mod[6:8, :]], axis=0)
    over = remote(item, item_r, csems, 2, "c")
    over.start()

    over.wait()
    v = item[...] + item_r[...]
    n = D // 2
    stamp = v[6:7, :LANES]
    pieces = ([v[0:1], v[1:2, :n]], [v[1:2, n:], v[2:3]], [v[3:4], v[4:5, :n]], [v[4:5, n:], v[5:6]])
    for j in range(4):
        out_shares[j] = jnp.concatenate(pieces[j] + [stamp], axis=1)
    for j in range(4):
        to = (y + j // 2) % 2 * 2 + (x + j) % 2
        if j == 0:
            square[t] = out_shares[t]
    meeting = [
        remote(out_shares.at[(y + j // 2) % 2 * 2 + (x + j) % 2], square.at[t], ssems, j - 1, ("x", "y", "xy")[j - 1])
        for j in (1, 2, 3)
    ]
    for copy in meeting:
        copy.start()

    def own_columns(q, firsts, own):
        columns = jnp.concatenate(q, axis=1) if q else None
        for core in range(2):

            @pl.when(c == core)
            def _():
                at = core if own else 1 - core
                if q:
                    for k in range(3):
                        gq_o[:, DZ * k + DC * at : DZ * k + DC * (at + 1)] = columns[:, DC * k : DC * (k + 1)]
                for f, pair in enumerate(firsts):
                    start = FF // 8 * at + FZ * f
                    g1_o[:, start : start + FZ] = jnp.concatenate(pair, axis=1)

    for copy in first_q:
        copy.wait()
    for kv, rv, on in ((ka, ra, ona), (kb, rb, onb)):
        on[...] = (kv[1].astype(f32) + rv[1].astype(f32)).astype(bf16)
    second_q = [remote(ona, r2a, qsems, 4, "y"), remote(onb, r2b, qsems, 5, "x")]
    for copy in second_q:
        copy.start()
    for copy in meeting:
        copy.wait()
    spread_z = [remote(square, every.at[z], ssems, 2 + k, f"z{k}") for k in (1, 2, 3)]
    every[z] = square[...]
    for copy in spread_z:
        copy.start()

    for k in (3, 4, 5, 6):
        loads[k].wait()
    for copy in third_p:
        copy.wait()
    fv[2] = fv[2] + br[0].astype(f32) + br[1].astype(f32) + br[2].astype(f32)
    for f in range(NF):
        mine[G1R * f : G1R * (f + 1), :] = fv[f, :G1R, :].astype(bf16)
    swap = remote(mine, theirs, csems, 3, "c")
    swap.start()
    own_columns(None, [[fv[f, :DC, :], fv[f, 2 * DC : 3 * DC, : FZ - LANES]] for f in range(NF)], True)
    for f in range(NF):
        part = fv[f, G1R:, :]
        tail = part[2 * FZ :]
        tail = jnp.concatenate([tail[:, 32 * k : 32 * (k + 1)] for k in range(4)], axis=0)
        g2_o[FZ * f : FZ * (f + 1), :] = jnp.concatenate([part[:FZ], part[FZ : 2 * FZ], tail], axis=1)
    part = pk[...] + pr[0].astype(f32) + pr[1].astype(f32) + pr[2].astype(f32)
    tail = part[2 * DC :]
    tail = jnp.concatenate([tail[:, 32 * k : 32 * (k + 1)] for k in range(3)], axis=0)
    gp_o[...] = jnp.concatenate([part[:DC], part[DC : 2 * DC], tail], axis=1)
    swap.wait()
    own_columns(
        None,
        [
            [theirs[G1R * f + DC : G1R * f + 2 * DC, :].astype(f32),
             theirs[G1R * f + 2 * DC : G1R * (f + 1), FZ - LANES :].astype(f32)]
            for f in range(NF)
        ],
        False,
    )

    for copy in second_q:
        copy.wait()
    layer_sums([(ka.at[0], ra.at[0], r2a), (kb.at[0], rb.at[0], r2b)], zs, zk)
    third_q = [remote(zs.at[k], zr.at[k], qsems, 6 + k, f"z{k + 1}") for k in (2, 1, 0)]
    for copy in third_q:
        copy.start()
    home = homeward(gb.at[0], gb.at[1], grad, tsems, lsems.at[7])
    home_start(*home)

    for copy in spread_z:
        copy.wait()
    columns = jnp.concatenate([every[i, j] for i in range(4) for j in range(4)], axis=0)
    width = 3 * D // 2
    angles = columns[:, width : width + 1] * freq[b % 4]
    cond = jax.nn.silu(jnp.where(b < 4, jnp.cos(angles), jnp.sin(angles))).astype(bf16).astype(f32)
    columns = columns[:, :width]
    ada_o[...] = lax.dot_general(
        cond, columns, (((0,), (0,)), ((), ())), precision=lax.Precision.HIGHEST, preferred_element_type=f32
    )
    row = jnp.sum(columns, axis=0, keepdims=True)
    row_out[0] = row
    row_in[t] = row
    rows_ = [remote(row_out.at[0], row_in.at[t], ssems, 6 + j, name) for j, name in enumerate(("x", "y", "xy"))]
    for copy in rows_:
        copy.start()
    for copy in rows_:
        copy.wait()
    row = row_in[z]
    ada_bias_o[...] = jnp.where(c == 0, row[:, : width // 2], row[:, width // 2 :])

    for copy in third_q:
        copy.wait()
    q = zk[...] + zr[0].astype(f32) + zr[1].astype(f32) + zr[2].astype(f32)
    mine_q[...] = q[: 7 * DC].astype(bf16)
    swap = remote(mine_q, theirs_q, csems, 4, "c")
    swap.start()
    line_o[...] = q[7 * DC :]
    own_columns([q[0:DC], q[2 * DC : 3 * DC], q[4 * DC : 5 * DC], q[6 * DC : 7 * DC, : DC // 3]], [], True)
    swap.wait()
    q = theirs_q[...].astype(f32)
    own_columns([q[DC : 2 * DC], q[3 * DC : 4 * DC], q[5 * DC : 6 * DC], q[6 * DC :, 64 : 64 + DC // 3]], [], False)
    home_wait(*home)


def final_kernel(out_rows, grad_rows, gq, gp, g1, g2, ada, ada_bias, line,
                 out, grad, gq_o, gp_o, g1_o, g2_o, ada_o, ada_bias_o, b_fc1, b_fc2, b_proj, b_q, b_v):
    out[...] = out_rows[...]
    grad[...] = grad_rows[...].astype(f32)
    gq_o[...] = gq[...]
    gp_o[...] = gp[...]
    g1_o[...] = g1[...]
    g2_o[...] = jnp.transpose(g2[...])
    ada_o[...] = ada[...]
    ada_bias_o[...] = ada_bias[...]
    n1, n = FF // 32 - LANES, D // 32
    second = line[1:2, :]
    b_fc1[...] = jnp.concatenate([line[0:1, :], second[:, :n1]], axis=1)
    for k, ref in enumerate((b_fc2, b_proj, b_q)):
        ref[...] = second[:, n1 + n * k : n1 + n * (k + 1)]
    b_v[...] = line[2:3, :n]


def one_item_per_chip(
    tokens, cotangent, timesteps, bucket_ids, head_masks, channel_masks, skip_rows,
    w_qkv, q_bias, v_bias, w_proj, proj_bias, w_fc1, fc1_bias, w_fc2, fc2_bias, ada_weight, ada_bias,
):
    b, t = lax.axis_index("bucket"), lax.axis_index("tok")
    z, c, y, x = b // 2, b % 2, t // 2, t % 2
    sds = jax.ShapeDtypeStruct

    def core_half(v, *dims):
        return lax.dynamic_index_in_dim(v.reshape(dims), c, 1, keepdims=False)

    vmem, smem = pl.BlockSpec(memory_space=pltpu.VMEM), pl.BlockSpec(memory_space=pltpu.SMEM)
    steps = -np.float32(math.log(10000.0)) * np.arange(D // 2, dtype=np.float32) / np.float32(D // 2)
    freq = jnp.asarray(np.exp(steps).reshape(1, D // 2))
    ada_cols = ada_weight.shape[1]
    front, _ = call(
        front_kernel, "front",
        (sds((L, D), bf16), sds((L, D), bf16), sds((L, D), bf16), sds((L, 3 * WC), bf16), sds((D, 3 * WC), bf16),
         sds((NF, D, FB), bf16), sds((8, D), f32), sds((L, 1), f32), sds((1, WC), f32), sds((NF, 1, FB), f32),
         sds((NF, 1, FB), f32)),
        (tokens, cotangent, timesteps, bucket_ids, skip_rows, ada_weight.T, ada_bias, head_masks, channel_masks,
         w_qkv, w_fc1, q_bias, v_bias, fc1_bias, freq),
        in_specs=[ANY, ANY, smem, smem, vmem, ANY, vmem, vmem, vmem, ANY, ANY, vmem, vmem, vmem, vmem],
        out_specs=[ANY, ANY, vmem, vmem, ANY, ANY] + [vmem] * 5,
        scratch=[vm(L, D), vm(L, D), vm(D, 3 * D), vm(D, 3 * WC), vm(D, FF), vm(NF, D, FB), vm(ada_cols, D),
                 vm(8, LANES, dtype=jnp.int32), vm(8, LANES, dtype=jnp.int32), vm(8, ada_cols, dtype=f32), vm(3, 8, ada_cols, dtype=f32),
                 vm(4, 8, ada_cols, dtype=f32), pltpu.SemaphoreType.DMA((2, 5)), pltpu.SemaphoreType.DMA((2, 4)),
                 pltpu.SemaphoreType.DMA((2, 3)), pltpu.SemaphoreType.DMA((6,))],
        peers=("c", "t0", "t1", "x", "y", "xy"), cid=10, flops=2 * L * D * 3 * WC, nbytes=50e6,
    )
    tok, g_all, shifted, qkv, wq, w1, mod, kept, hmask, chan, b1 = front
    w2 = w_fc2.reshape(4, 2, NF, FZ, D)
    wp = w_proj.reshape(4, 2, DC, D)
    (mixed, shifted2, attn), _ = call(
        functools.partial(attn_kernel, 256), "attn",
        (sds((L, WC), bf16), sds((L, D), bf16), sds((LH, D), f32)),
        (qkv, hmask, wp, proj_bias, tok, mod),
        in_specs=[vmem, vmem, ANY, vmem, ANY, vmem],
        out_specs=[ANY, vmem, vmem],
        scratch=[vm(HC, L, HD)] * 3 + [vm(L, WC), vm(L, WC), vm(2, 4, DC, D), vm(L, D),
                 pltpu.SemaphoreType.DMA((2, 4)), pltpu.SemaphoreType.DMA((4,))],
        peers=("c",), cid=11, flops=16e9, nbytes=5e6,
    )

    slot1, slot2 = sds((2, 4, G1R, LANES), bf16), sds((2, 4, G2R, LANES), bf16)
    part1, part2 = sds(slot1.shape[1:], bf16), sds(slot2.shape[1:], bf16)
    one = [part1, part1, part2, part2, part1, part2]
    rows_half = sds((LH, D), bf16)
    dma = pltpu.SemaphoreType.DMA
    own, _ = call(
        mlp_kernel, "mlp",
        one + one + [slot1, slot1, slot2, slot2] + [rows_half] * 4 + [sds((NF, 1, FB), f32), sds((1, D), f32)],
        (shifted2, g_all, kept, mod, w1, b1, chan, w2),
        in_specs=[ANY, ANY, vmem, vmem, ANY, vmem, vmem, ANY],
        out_specs=[ANY] * 16 + [vmem, vmem, ANY, ANY, vmem, vmem],
        scratch=[vm(L, D), vm(L, D), vm(L, D), vm(2, D, FB), vm(2, 4, FZ, D), vm(L, FB), vm(L, FB),
                 vm(L, D, dtype=f32), vm(L, D, dtype=f32), vm(2, LH, D), vm(4, D, TD)]
        + [vm(2, *slot1.shape)] * 2 + [vm(2, *slot2.shape)] * 2
        + [vm(2, *p.shape) for p in (part1, part2)] * 2
        + [dma((2, 8)), dma((2, 2)), dma((2,)), dma((2, 2)), dma((2, 6))],
        peers=("c", "x", "y"), cid=0,
        flops=36 * L * D * FB, nbytes=40e6,
    )
    second0, second1, slots = own[:6], own[6:12], own[12:16]
    branch, ds2, branch_r, ds2_r, sum1, sum2 = own[16:]

    n = LH // 4
    row = rows(n, D)
    slot_a, slot_b = sds((2, 4, PA, LANES), bf16), sds((2, 4, PR - PA, LANES), bf16)
    own, given = call(
        middle_kernel, "middle",
        (sds((LH, D), f32), sds((LH, D), bf16), sds((L, WC), bf16), slot_a, slot_a, slot_b, slot_b,
         sds((8, D), f32), sds((8, D), f32)),
        (ds2, ds2_r, branch, branch_r, attn, tok, g_all, kept, mod, fc2_bias,
         mixed, wp),
        grid=(4,),
        in_specs=[row] * 7 + [rows(n, 1), full((8, D)), vmem, once(L, WC), ANY],
        out_specs=(row, row, full((L, WC)), full(slot_a.shape), full(slot_a.shape), full(slot_b.shape),
                   full(slot_b.shape), full((8, D)), full((8, D))),
        scratch=[vm(L, D), vm(4, WC, TD), vm(4, DC, D), pltpu.SemaphoreType.DMA((2, 4)), pltpu.SemaphoreType.DMA],
        peers=("c",), cid=3,
        jobs=[FirstSum(*slots), SecondSum(*second0)],
        flops=4 * L * D * WC, nbytes=20e6,
    )
    d_resid, out_rows, dh, *slots_p, sums_mid, sum_attn = own
    first2, result0 = given
    dqkv, given = call(
        functools.partial(attn_back_kernel, 512), "attn_back",
        sds((L, 3 * WC), bf16), (qkv, dh, hmask),
        scratch=[vm(HC, L, HD)] * 4 + [vm(HC, L, HD, dtype=f32)] * 2,
        cid=4, ticks=True,
        jobs=[SecondThird(*second1), SecondSum(*first2, slots[0], slots[2]), FirstSecond(*slots_p), ThirdSum(*result0),
              GoHome(out_rows)],
        flops=30e9, nbytes=9e6,
    )
    final1, (sent2, kept2), (sent_p, kept_p), final0, output = given[0][0], given[1], given[2], given[3][0], given[4][0]
    sum_fc1 = sum1.reshape(NF, 4, FZ).transpose(1, 0, 2).reshape(4, 4, FF // 32)
    own_part = lambda v: core_half(v, 4, 2, 4, D // 32)
    line = jnp.concatenate(
        [sum_fc1, own_part(sum2), own_part(sum_attn[0]), jnp.zeros((4, 4, 3 * LANES - FF // 32 - D // 16), f32)], axis=2
    ).reshape(4, 4, 3, LANES)
    extra = jnp.concatenate([line, jnp.zeros((4, 4, 13, LANES), f32)], axis=2)
    slot_q = vm(2, 4, QA, LANES)
    fourth = vm(4, QA, LANES)
    width = ada_cols + LANES
    (grad_rows, gq, gp, g1, g2, grad_ada_weight, grad_ada_bias, line), _ = call(
        end_kernel, "end",
        (sds((2, LB, D), bf16), sds((DC, 3 * TD), f32), sds((DC, TD), f32), sds((DC, FF // 4), f32),
         sds((FF // 8, TD), f32), sds((DC, ada_cols), f32), sds((1, ada_cols // 2), f32), sds((16, LANES), f32)),
        (shifted, dqkv, extra, wq, d_resid, tok, mod, sums_mid, final0, final1, sent2, kept2, sent_p, kept_p,
         freq.reshape(4, 1, DC)),
        in_specs=[vmem] * 3 + [ANY] * 3 + [vmem] * 2 + [ANY] * 6 + [vmem],
        out_specs=[ANY] + [vmem] * 7,
        scratch=[vm(4, D, 3 * DC)] + [slot_q] * 6 + [fourth] * 4
        + [vm(3, QR, LANES), vm(QR, LANES, dtype=f32), vm(3, QR, LANES), vm(D, 3 * WC), vm(LH, D, dtype=f32),
           vm(LH, D), vm(NF, G1R + G2R, LANES, dtype=f32)] + [vm(2, LB, D)] * 3
        + [vm(8, D, dtype=f32)] * 2 + [vm(4, 1, width, dtype=f32)] * 2
        + [vm(4, 4, 1, width, dtype=f32), vm(1, 1, ada_cols, dtype=f32), vm(4, 1, ada_cols, dtype=f32)]
        + [vm(NF * G1R, LANES)] * 2 + [vm(7 * DC, LANES)] * 2 + [vm(PR, LANES, dtype=f32), vm(3, PR, LANES),
                                                                      vm(3, G1R + G2R, LANES)]
        + [dma((2, 9)), dma((2, 5)), dma((2, 2)), dma((2, 9)), dma((2, 6)), dma((8,))],
        peers=("c", "t0", "t1", "x", "y", "xy", "z1", "z2", "z3"), cid=5,
        flops=4 * L * D * 3 * WC, nbytes=30e6,
    )
    thin = lambda height, width: pl.BlockSpec((height, width), lambda i: (i, 0))
    tokens_spec = pl.BlockSpec((2, LB // 2, D), lambda i: (0, i, 0))
    ends = [thin(DC // 2, 3 * TD), thin(DC // 2, TD), thin(DC // 2, FF // 4)]
    bias_cols = ada_cols // 2
    finals, _ = call(
        final_kernel, "final",
        (sds((2, LB, D), bf16), sds((2, LB, D), f32), sds((DC, 3 * TD), f32), sds((DC, TD), f32), sds((DC, FF // 4), f32),
         sds((TD, FF // 8), f32), sds((DC, ada_cols), f32), sds((1, bias_cols), f32), sds((1, FF // 32), f32))
        + (sds((1, D // 32), f32),) * 4,
        (output, grad_rows, gq, gp, g1, g2, grad_ada_weight, grad_ada_bias, line),
        grid=(2,),
        in_specs=[tokens_spec, tokens_spec, *ends, full((FF // 8, TD)), thin(DC // 2, ada_cols), full((1, bias_cols)),
                  full((16, LANES))],
        out_specs=[tokens_spec, tokens_spec, *ends, full((TD, FF // 8)), thin(DC // 2, ada_cols), full((1, bias_cols)),
                   full((1, FF // 32))] + [full((1, D // 32))] * 4,
    )
    output, grad_tokens, gq, gp, g1, g2, g_ada, *lines = finals
    ada_b, b_fc1, b_fc2, b_proj, b_q, b_v = [v.reshape(-1) for v in lines]
    return (output, grad_tokens, gq, b_q, b_v, gp, b_proj, g1, b_fc1, g2.T, b_fc2, g_ada, ada_b)


def gelu_tanh(values):
    return jax.nn.gelu(values, approximate=True)


def split_heads(key_value, model_width, head_dim):
    item_count, length = (key_value.shape[0], key_value.shape[1])
    key_rows = key_value[:, :, :model_width].reshape(
        item_count, length, model_width // head_dim, head_dim
    )
    value_rows = key_value[:, :, model_width:].reshape(
        item_count, length, model_width // head_dim, head_dim
    )
    return (key_rows, value_rows)


def scores_of(queries, key_rows, score_scale):
    return (
        jnp.einsum("nqhe,nkhe->nhqk", queries, key_rows, preferred_element_type=jnp.float32)
        * score_scale
    )


def to_blocks(values, per_step):
    return values.reshape((values.shape[0] // per_step, per_step) + values.shape[1:])


def from_blocks(values):
    return values.reshape((values.shape[0] * values.shape[1],) + values.shape[2:])


def on_device(
    tokens,
    cotangent,
    timesteps,
    bucket_ids,
    head_masks,
    channel_masks,
    skip_rows,
    w_qkv,
    q_bias,
    v_bias,
    w_proj,
    proj_bias,
    w_fc1,
    fc1_bias,
    w_fc2,
    fc2_bias,
    ada_weight,
    ada_bias,
):
    item_count, local_len, model_width = tokens.shape
    row_count = item_count * local_len
    head_dim = model_width // HEADS
    score_scale = 1.0 / math.sqrt(head_dim)
    hidden_width = w_fc1.shape[1]
    ada_cols = ada_weight.shape[1]
    tok_index = lax.axis_index("tok")
    per_step = 1
    for candidate in range(1, item_count + 1):
        per_step = candidate
    condition = jax.nn.silu(step_embedding(timesteps, model_width)).astype(jnp.bfloat16)
    mod_local = jnp.dot(
        condition, ada_weight, preferred_element_type=jnp.float32
    ) + ada_bias.astype(jnp.float32)
    modulation = lax.all_gather(mod_local, "tok", axis=1, tiled=True)
    pieces = modulation.reshape(item_count, 6, 1, model_width)
    shift_a = pieces[:, 0]
    scale_a = pieces[:, 1]
    gate_a = pieces[:, 2]
    shift_m = pieces[:, 3]
    scale_m = pieces[:, 4]
    gate_m = pieces[:, 5]
    chosen = (jnp.arange(head_masks.shape[0], dtype=jnp.int32) == bucket_ids[0]).astype(jnp.float32)
    head_on = jnp.sum(chosen[:, None] * head_masks.astype(jnp.float32), axis=0)
    group_on = jnp.sum(chosen[:, None] * channel_masks.astype(jnp.float32), axis=0)
    channel_on = jnp.repeat(group_on, hidden_width // group_on.shape[0])
    positions = tok_index * local_len + jnp.arange(local_len, dtype=jnp.int32)
    skipped = jnp.any(skip_rows[:, :, None] == positions[None, None, :], axis=1)
    kept_rows = 1.0 - skipped.astype(jnp.float32)
    inputs = tokens.astype(jnp.float32)
    normed, inverse = normalize(inputs)
    shifted = (
        (normed * (1.0 + scale_a) + shift_a).astype(jnp.bfloat16).reshape(row_count, model_width)
    )
    qkv_bias = jnp.concatenate([q_bias, jnp.zeros_like(q_bias), v_bias]).astype(jnp.float32)
    projected = (jnp.dot(shifted, w_qkv, preferred_element_type=jnp.float32) + qkv_bias).astype(
        jnp.bfloat16
    )
    projected = projected.reshape(item_count, local_len, 3 * model_width)
    queries = projected[:, :, :model_width].reshape(item_count, local_len, HEADS, head_dim)
    key_value = projected[:, :, model_width:]
    all_kv = lax.all_gather(key_value, "tok", axis=1, tiled=True)

    def forward_block(packed):
        query_block, kv_block = packed
        key_rows, value_rows = split_heads(kv_block, model_width, head_dim)
        scores = scores_of(query_block, key_rows, score_scale)
        top_score = jnp.max(scores, axis=-1, keepdims=True)
        expanded = jnp.exp(scores - top_score)
        totals = jnp.sum(expanded, axis=-1, keepdims=True)
        weights_low = (expanded / totals).astype(jnp.bfloat16)
        head_out = (
            jnp.einsum(
                "nhqk,nkhe->nqhe", weights_low, value_rows, preferred_element_type=jnp.float32
            )
            * head_on[:, None]
        )
        return (head_out.astype(jnp.bfloat16), top_score + jnp.log(totals))

    mixed_heads, log_total = lax.map(
        forward_block, (to_blocks(queries, per_step), to_blocks(all_kv, per_step))
    )
    log_total = from_blocks(log_total)
    mixed = from_blocks(mixed_heads).reshape(row_count, model_width)
    attn = (
        jnp.dot(mixed, w_proj, preferred_element_type=jnp.float32) + proj_bias.astype(jnp.float32)
    ).reshape(item_count, local_len, model_width)
    resid = inputs + gate_a * attn
    normed2, inverse2 = normalize(resid)
    shifted2 = (
        (normed2 * (1.0 + scale_m) + shift_m).astype(jnp.bfloat16).reshape(row_count, model_width)
    )
    pre = jnp.dot(shifted2, w_fc1, preferred_element_type=jnp.float32) + fc1_bias.astype(
        jnp.float32
    )
    activated, gelu_pull = jax.vjp(gelu_tanh, pre)
    hidden = (activated * channel_on).astype(jnp.bfloat16)
    branch = (
        jnp.dot(hidden, w_fc2, preferred_element_type=jnp.float32) + fc2_bias.astype(jnp.float32)
    ).reshape(item_count, local_len, model_width)
    gated = kept_rows[:, :, None] * gate_m
    output = (resid + gated * branch).astype(jnp.bfloat16)
    incoming = cotangent.astype(jnp.float32)
    d_gate_m = jnp.sum(kept_rows[:, :, None] * branch * incoming, axis=1)
    d_branch = (gated * incoming).astype(jnp.bfloat16).reshape(row_count, model_width)
    grad_w_fc2 = jnp.dot(hidden.T, d_branch, preferred_element_type=jnp.float32)
    grad_fc2_bias = jnp.sum(d_branch.astype(jnp.float32), axis=0)
    d_hidden = jnp.dot(d_branch, w_fc2.T, preferred_element_type=jnp.float32)
    d_pre = gelu_pull(d_hidden * channel_on)[0].astype(jnp.bfloat16)
    grad_w_fc1 = jnp.dot(shifted2.T, d_pre, preferred_element_type=jnp.float32)
    grad_fc1_bias = jnp.sum(d_pre.astype(jnp.float32), axis=0)
    d_shifted2 = jnp.dot(d_pre, w_fc1.T, preferred_element_type=jnp.float32).reshape(
        item_count, local_len, model_width
    )
    d_shift_m = jnp.sum(d_shifted2, axis=1)
    d_scale_m = jnp.sum(d_shifted2 * normed2, axis=1)
    d_resid = incoming + normalize_back(d_shifted2 * (1.0 + scale_m), normed2, inverse2)
    d_gate_a = jnp.sum(attn * d_resid, axis=1)
    d_attn = (gate_a * d_resid).astype(jnp.bfloat16).reshape(row_count, model_width)
    grad_w_proj = jnp.dot(mixed.T, d_attn, preferred_element_type=jnp.float32)
    grad_proj_bias = jnp.sum(d_attn.astype(jnp.float32), axis=0)
    d_mixed = jnp.dot(d_attn, w_proj.T, preferred_element_type=jnp.float32).astype(jnp.bfloat16)
    d_heads = d_mixed.reshape(item_count, local_len, HEADS, head_dim) * head_on[:, None].astype(
        jnp.bfloat16
    )
    again_kv = lax.all_gather(key_value, "tok", axis=1, tiled=True)

    def backward_block(packed):
        query_block, kv_block, head_grads, totals_log = packed
        key_rows, value_rows = split_heads(kv_block, model_width, head_dim)
        scores = scores_of(query_block, key_rows, score_scale)
        probs = jnp.exp(scores - totals_log)
        d_probs = jnp.einsum(
            "nqhe,nkhe->nhqk", head_grads, value_rows, preferred_element_type=jnp.float32
        )
        row_dot = jnp.sum(probs * d_probs, axis=-1, keepdims=True)
        d_scores = (probs * (d_probs - row_dot)).astype(jnp.bfloat16)
        d_queries = (
            jnp.einsum("nhqk,nkhe->nqhe", d_scores, key_rows, preferred_element_type=jnp.float32)
            * score_scale
        )
        return (d_queries, row_dot)

    mapped = lax.map(
        backward_block,
        (
            to_blocks(queries, per_step),
            to_blocks(again_kv, per_step),
            to_blocks(d_heads, per_step),
            to_blocks(log_total, per_step),
        ),
    )
    d_queries = from_blocks(mapped[0])
    row_dot = from_blocks(mapped[1])
    queries_all, head_grads_all = (
        lax.all_gather(queries, "tok", axis=1, tiled=True),
        lax.all_gather(d_heads, "tok", axis=1, tiled=True),
    )
    totals_all, row_dot_all = (
        lax.all_gather(log_total, "tok", axis=2, tiled=True),
        lax.all_gather(row_dot, "tok", axis=2, tiled=True),
    )

    def key_block(packed):
        kv_block, query_block, head_grads, totals_log, dots = packed
        key_rows, value_rows = split_heads(kv_block, model_width, head_dim)
        scores = (
            jnp.einsum("nkhe,nqhe->nhkq", key_rows, query_block, preferred_element_type=jnp.float32)
            * score_scale
        )
        probs = jnp.exp(scores - totals_log[:, :, None, :, 0])
        d_probs = jnp.einsum(
            "nkhe,nqhe->nhkq", value_rows, head_grads, preferred_element_type=jnp.float32
        )
        d_scores = (probs * (d_probs - dots[:, :, None, :, 0])).astype(jnp.bfloat16)
        d_keys = (
            jnp.einsum("nhkq,nqhe->nkhe", d_scores, query_block, preferred_element_type=jnp.float32)
            * score_scale
        )
        d_values = jnp.einsum(
            "nhkq,nqhe->nkhe",
            probs.astype(jnp.bfloat16),
            head_grads,
            preferred_element_type=jnp.float32,
        )
        return jnp.concatenate(
            [
                d_keys.reshape(d_keys.shape[0], local_len, model_width),
                d_values.reshape(d_values.shape[0], local_len, model_width),
            ],
            axis=2,
        )

    d_kv = from_blocks(
        lax.map(
            key_block,
            (
                to_blocks(key_value, per_step),
                to_blocks(queries_all, per_step),
                to_blocks(head_grads_all, per_step),
                to_blocks(totals_all, per_step),
                to_blocks(row_dot_all, per_step),
            ),
        )
    )
    d_qkv = jnp.concatenate([d_queries.reshape(item_count, local_len, model_width), d_kv], axis=2)
    d_qkv = d_qkv.astype(jnp.bfloat16).reshape(row_count, 3 * model_width)
    grad_w_qkv = jnp.dot(shifted.T, d_qkv, preferred_element_type=jnp.float32)
    qkv_sums = jnp.sum(d_qkv.astype(jnp.float32), axis=0)
    grad_q_bias = qkv_sums[:model_width]
    grad_v_bias = qkv_sums[2 * model_width :]
    d_shifted = jnp.dot(d_qkv, w_qkv.T, preferred_element_type=jnp.float32).reshape(
        item_count, local_len, model_width
    )
    d_shift_a = jnp.sum(d_shifted, axis=1)
    d_scale_a = jnp.sum(d_shifted * normed, axis=1)
    grad_tokens = d_resid + normalize_back(d_shifted * (1.0 + scale_a), normed, inverse)
    d_modulation = jnp.concatenate(
        [d_shift_a, d_scale_a, d_gate_a, d_shift_m, d_scale_m, d_gate_m], axis=1
    )
    d_modulation = lax.psum(d_modulation, "tok")
    mod_columns = lax.dynamic_slice_in_dim(d_modulation, tok_index * ada_cols, ada_cols, 1)
    grad_ada_weight = jnp.dot(
        condition.astype(jnp.float32).T, mod_columns, precision=lax.Precision.HIGHEST
    )
    grad_ada_bias = jnp.sum(d_modulation, axis=0)
    bucket_done = (
        lax.psum_scatter(grad_w_qkv, "bucket", scatter_dimension=0, tiled=True),
        lax.psum_scatter(grad_w_proj, "bucket", scatter_dimension=0, tiled=True),
        lax.psum_scatter(grad_w_fc1, "bucket", scatter_dimension=0, tiled=True),
        lax.psum_scatter(grad_w_fc2, "bucket", scatter_dimension=0, tiled=True),
        lax.psum_scatter(grad_q_bias, "bucket", scatter_dimension=0, tiled=True),
        lax.psum_scatter(grad_v_bias, "bucket", scatter_dimension=0, tiled=True),
        lax.psum_scatter(grad_proj_bias, "bucket", scatter_dimension=0, tiled=True),
        lax.psum_scatter(grad_fc1_bias, "bucket", scatter_dimension=0, tiled=True),
        lax.psum_scatter(grad_fc2_bias, "bucket", scatter_dimension=0, tiled=True),
        lax.psum_scatter(grad_ada_weight, "bucket", scatter_dimension=0, tiled=True),
        lax.psum_scatter(grad_ada_bias, "bucket", scatter_dimension=0, tiled=True),
    )
    token_done = (
        lax.psum_scatter(bucket_done[0], "tok", scatter_dimension=1, tiled=True),
        lax.psum_scatter(bucket_done[1], "tok", scatter_dimension=1, tiled=True),
        lax.psum_scatter(bucket_done[2], "tok", scatter_dimension=1, tiled=True),
        lax.psum_scatter(bucket_done[3], "tok", scatter_dimension=1, tiled=True),
        lax.psum_scatter(bucket_done[4].reshape(1, -1), "tok", scatter_dimension=1, tiled=True),
        lax.psum_scatter(bucket_done[5].reshape(1, -1), "tok", scatter_dimension=1, tiled=True),
        lax.psum_scatter(bucket_done[6].reshape(1, -1), "tok", scatter_dimension=1, tiled=True),
        lax.psum_scatter(bucket_done[7].reshape(1, -1), "tok", scatter_dimension=1, tiled=True),
        lax.psum_scatter(bucket_done[8].reshape(1, -1), "tok", scatter_dimension=1, tiled=True),
    )
    finished = (
        token_done[0],
        token_done[1],
        token_done[2],
        token_done[3],
        token_done[4],
        token_done[5],
        token_done[6],
        token_done[7],
        token_done[8],
        bucket_done[9],
        bucket_done[10],
    )
    return (
        output,
        grad_tokens,
        finished[0],
        finished[4].reshape(-1),
        finished[5].reshape(-1),
        finished[1],
        finished[6].reshape(-1),
        finished[2],
        finished[7].reshape(-1),
        finished[3],
        finished[8].reshape(-1),
        finished[9],
        finished[10],
    )


def solution(mesh):
    planned = mesh.shape["tok"] == 4 and mesh.shape["bucket"] == 8
    return jax.shard_map(
        one_item_per_chip if planned else on_device,
        mesh=mesh,
        in_specs=(
            P("bucket", "tok", None),
            P("bucket", "tok", None),
            P("bucket"),
            P("bucket"),
            P(),
            P(),
            P("bucket", None),
            P(),
            P(),
            P(),
            P(),
            P(),
            P(),
            P(),
            P(),
            P(),
            P(None, "tok"),
            P("tok"),
        ),
        out_specs=(
            P("bucket", "tok", None),
            P("bucket", "tok", None),
            P("bucket", "tok"),
            P(("bucket", "tok")),
            P(("bucket", "tok")),
            P("bucket", "tok"),
            P(("bucket", "tok")),
            P("bucket", "tok"),
            P(("bucket", "tok")),
            P("bucket", "tok"),
            P(("bucket", "tok")),
            P("bucket", "tok"),
            P("bucket"),
        ),
        check_vma=False,
    )
```

```python
import functools
import math

import jax
import jax.numpy as jnp
import numpy as np
from jax import lax
from jax.experimental import pallas as pl
from jax.experimental.pallas import tpu as pltpu
from jax.sharding import PartitionSpec as P

HEADS = 16
EPSILON = 1e-06
LOG2E = 1.4426950408889634
GELU_K = math.sqrt(2.0 / math.pi)
GELU_C = 0.044715
LANES = 128
bf16, f32 = jnp.bfloat16, jnp.float32


def dot_nn(a, b):
    return lax.dot_general(a, b, (((1,), (0,)), ((), ())), preferred_element_type=f32)


def dot_nt(a, b):
    return lax.dot_general(a, b, (((1,), (1,)), ((), ())), preferred_element_type=f32)


def dot_tn(a, b):
    return lax.dot_general(a, b, (((0,), (0,)), ((), ())), preferred_element_type=f32)


def step_embedding(timesteps, model_width):
    half_width = model_width // 2
    frequency = jnp.exp(-math.log(10000.0) * jnp.arange(half_width, dtype=jnp.float32) / half_width)
    angles = timesteps.astype(jnp.float32)[:, None] * frequency[None, :]
    return jnp.concatenate([jnp.cos(angles), jnp.sin(angles)], axis=1)


def normalize(values):
    centred = values - jnp.mean(values, axis=-1, keepdims=True)
    inverse = lax.rsqrt(jnp.mean(centred * centred, axis=-1, keepdims=True) + EPSILON)
    return (centred * inverse, inverse)


def normalize_back(incoming, normed, inverse):
    return inverse * (
        incoming
        - jnp.mean(incoming, axis=-1, keepdims=True)
        - normed * jnp.mean(incoming * normed, axis=-1, keepdims=True)
    )


D = 1152
DC, DZ, TD = D // 8, D // 4, D // 4
HD = D // HEADS
HC = HEADS // 2
WC = D // 2
FF = 4608
NF = 3
FB = FF // 2 // NF
FZ = FB // 4
L = 1024
LH = L // 2
LB = L // 4
G1R = 3 * DC
G2R = 2 * FZ + FZ // 4
PR = 2 * DC + DC // 3
PA = 176
WQ = 3 * WC // 2
TQ = WQ // 4
QR = 512
QA = QR // 2
VMEM_LIMIT = 58 * 1024 * 1024


ANY = pl.BlockSpec(memory_space=pl.ANY)
MESH = pl.DeviceIdType.MESH


def place():
    b, t = lax.axis_index("bucket"), lax.axis_index("tok")
    return b // 2, b % 2, t // 2, t % 2


def flip(value, other):
    return (value // 2 + other // 2) % 2 * 2 + (value % 2 + other % 2) % 2


def peer(name):
    z, c, y, x = place()
    if name == "x":
        x = 1 - x
    elif name == "y":
        y = 1 - y
    elif name == "xy":
        x, y = 1 - x, 1 - y
    elif name == "c":
        c = 1 - c
    elif name in ("t0", "t1"):
        c, y, x = y, c, x if name == "t0" else 1 - x
    else:
        z = flip(z, int(name[1]))
    return (z * 2 + c, y * 2 + x)


def meet(names):
    sem = pltpu.get_barrier_semaphore()
    others = [name for name in names if name != "t0"]
    for name in others:
        pl.semaphore_signal(sem, inc=1, device_id=peer(name), device_id_type=MESH)
    wanted = len(others)
    if "t0" in names:
        _, c, y, _ = place()
        wanted = wanted + (c + y) % 2

        @pl.when(c != y)
        def _():
            pl.semaphore_signal(sem, inc=1, device_id=peer("t0"), device_id_type=MESH)

    pl.semaphore_wait(sem, wanted)


def remote(src, dst, sems, k, name):
    return pltpu.make_async_remote_copy(
        src_ref=src, dst_ref=dst, send_sem=sems.at[0, k], recv_sem=sems.at[1, k],
        device_id=peer(name), device_id_type=MESH,
    )


def vm(*shape, dtype=bf16):
    return pltpu.VMEM(shape, dtype)


class FirstSum:
    peers = ("x", "y")

    def __init__(self, keep_a, sent_a, keep_b, sent_b):
        self.ins = [keep_a, sent_a, keep_b, sent_b]
        shapes = [keep.shape[1:] for keep in (keep_a, keep_b)]
        self.outs = [jax.ShapeDtypeStruct(s, bf16) for s in shapes for _ in range(2)]
        self.scratch = [vm(*s) for s in shapes for _ in range(3)]
        self.scratch += [pltpu.SemaphoreType.DMA((2, 4)), pltpu.SemaphoreType.DMA((4,))]

    def plan(self, ins, outs, scratch):
        ka, sa, kb, sb = ins
        _, qa, _, qb = outs
        kav, rav, _, kbv, rbv, _, sems, local = scratch
        far = [
            remote(sa.at[1], rav, sems, 0, "x"),
            remote(sb.at[1], rbv, sems, 1, "y"),
            remote(sa.at[0], qa, sems, 2, "x"),
            remote(sb.at[0], qb, sems, 3, "y"),
        ]
        near = [
            pltpu.make_async_copy(ka.at[1], kav, local.at[0]),
            pltpu.make_async_copy(kb.at[1], kbv, local.at[1]),
        ]
        return far, near

    def finish(self, ins, outs, scratch):
        kav, rav, oav, kbv, rbv, obv, _, local = scratch
        oav[...] = (kav[...].astype(f32) + rav[...].astype(f32)).astype(bf16)
        obv[...] = (kbv[...].astype(f32) + rbv[...].astype(f32)).astype(bf16)
        return [
            pltpu.make_async_copy(oav, outs[0], local.at[2]),
            pltpu.make_async_copy(obv, outs[2], local.at[3]),
        ]


class SecondSum:
    peers = ("x", "y")

    def __init__(self, on_a, q_a, on_b, q_b, keep_a, keep_b):
        self.ins = [on_a, q_a, on_b, q_b, keep_a, keep_b]
        self.rows = [on_a.shape[1], on_b.shape[1]]
        total = sum(self.rows)
        self.outs = [jax.ShapeDtypeStruct((3, total, LANES), bf16), jax.ShapeDtypeStruct((total, LANES), f32)]
        self.scratch = [vm(4, r, LANES) for r in self.rows for _ in range(3)]
        self.scratch += [vm(3, total, LANES), vm(total, LANES, dtype=f32)]
        self.scratch += [pltpu.SemaphoreType.DMA((2, 2)), pltpu.SemaphoreType.DMA((6,))]

    def plan(self, ins, outs, scratch):
        oa, qa, ob, qb, ka, kb = ins
        kav, qav, rav, kbv, qbv, rbv, _, _, sems, local = scratch
        far = [remote(oa, rav, sems, 0, "y"), remote(ob, rbv, sems, 1, "x")]
        whole = len(ka.shape) == 4
        pairs = [(ka.at[0] if whole else ka, kav), (qa, qav), (kb.at[0] if whole else kb, kbv), (qb, qbv)]
        return far, [pltpu.make_async_copy(a, b, local.at[k]) for k, (a, b) in enumerate(pairs)]

    def finish(self, ins, outs, scratch):
        zs, zk, local = scratch[6], scratch[7], scratch[9]
        layer_sums([scratch[0:3], scratch[3:6]], zs, zk)
        return [
            pltpu.make_async_copy(zs, outs[0], local.at[4]),
            pltpu.make_async_copy(zk, outs[1], local.at[5]),
        ]


class ThirdSum:
    peers = ("z1", "z2", "z3")

    def __init__(self, sent, kept):
        self.ins = [sent, kept]
        self.outs = [jax.ShapeDtypeStruct(kept.shape, f32)]
        self.scratch = [vm(*sent.shape), vm(*kept.shape, dtype=f32)]
        self.scratch += [pltpu.SemaphoreType.DMA((2, 3)), pltpu.SemaphoreType.DMA((2,))]

    def plan(self, ins, outs, scratch):
        got, kept, sems, local = scratch
        far = [remote(ins[0].at[k], got.at[k], sems, k, f"z{k + 1}") for k in (2, 1, 0)]
        return far, [pltpu.make_async_copy(ins[1], kept, local.at[0])]

    def finish(self, ins, outs, scratch):
        got, kept, _, local = scratch
        kept[...] = kept[...] + got[0].astype(f32) + got[1].astype(f32) + got[2].astype(f32)
        return [pltpu.make_async_copy(kept, outs[0], local.at[1])]


def layer_sums(streams, zs, zk):
    start = 0
    for kv, qv, rv in streams:
        rows_ = rv.shape[1]
        for j in range(4):
            total = kv[j].astype(f32) + qv[j].astype(f32) + rv[j].astype(f32)
            if j == 0:
                zk[start : start + rows_, :] = total
            else:
                zs[j - 1, start : start + rows_, :] = total.astype(bf16)
        start += rows_


class SecondThird(SecondSum):
    peers = ("x", "y", "z1", "z2", "z3")

    def __init__(self, *args, start_at=0, tick_at=1):
        super().__init__(*args)
        self.start_at, self.tick_at = start_at, tick_at
        total = sum(self.rows)
        self.outs = [jax.ShapeDtypeStruct((total, LANES), f32)]
        self.scratch += [vm(3, total, LANES), pltpu.SemaphoreType.DMA((2, 3))]

    def third(self, scratch):
        zs, got, sems = scratch[6], scratch[10], scratch[11]
        return [remote(zs.at[k], got.at[k], sems, k, f"z{k + 1}") for k in (2, 1, 0)]

    def tick(self, ins, outs, scratch):
        for group in super().plan(ins, outs, scratch[:10]):
            for copy in group:
                copy.wait()
        layer_sums([scratch[0:3], scratch[3:6]], scratch[6], scratch[7])
        for copy in self.third(scratch):
            copy.start()

    def plan(self, ins, outs, scratch):
        return super().plan(ins, outs, scratch[:10])

    def settle(self, ins, outs, scratch):
        return self.third(scratch)

    def finish(self, ins, outs, scratch):
        kept, local, got = scratch[7], scratch[9], scratch[10]
        kept[...] = kept[...] + got[0].astype(f32) + got[1].astype(f32) + got[2].astype(f32)
        return [pltpu.make_async_copy(kept, outs[0], local.at[5])]


class FirstSecond:
    peers = ("x", "y")

    def __init__(self, keep_a, sent_a, keep_b, sent_b, start_at=0, tick_at=1):
        self.start_at, self.tick_at = start_at, tick_at
        self.ins = [keep_a, sent_a, keep_b, sent_b]
        self.rows = [keep_a.shape[2], keep_b.shape[2]]
        total = sum(self.rows)
        self.outs = [jax.ShapeDtypeStruct((3, total, LANES), bf16), jax.ShapeDtypeStruct((total, LANES), f32)]
        self.scratch = []
        for r in self.rows:
            self.scratch += [vm(2, 4, r, LANES), vm(2, 4, r, LANES), vm(4, r, LANES), vm(4, r, LANES)]
        self.scratch += [vm(3, total, LANES), vm(total, LANES, dtype=f32)]
        self.scratch += [pltpu.SemaphoreType.DMA((2, 6)), pltpu.SemaphoreType.DMA((4,))]

    def plan(self, ins, outs, scratch):
        ka, sa, kb, sb = ins
        sems, local = scratch[10:]
        far = [
            remote(sa.at[1], scratch[1].at[1], sems, 0, "x"),
            remote(sb.at[1], scratch[5].at[1], sems, 1, "y"),
            remote(sa.at[0], scratch[1].at[0], sems, 2, "x"),
            remote(sb.at[0], scratch[5].at[0], sems, 3, "y"),
        ]
        near = [pltpu.make_async_copy(k, scratch[4 * j], local.at[j]) for j, k in enumerate((ka, kb))]
        return far, near

    def second(self, scratch):
        sems = scratch[10]
        return [remote(scratch[4 * j + 2], scratch[4 * j + 3], sems, 4 + j, name) for j, name in enumerate("yx")]

    def tick(self, ins, outs, scratch):
        for group in self.plan(ins, outs, scratch):
            for copy in group:
                copy.wait()
        for j in range(2):
            kv, rv, on = scratch[4 * j : 4 * j + 3]
            on[...] = (kv[1].astype(f32) + rv[1].astype(f32)).astype(bf16)
        for copy in self.second(scratch):
            copy.start()

    def settle(self, ins, outs, scratch):
        return self.second(scratch)

    def finish(self, ins, outs, scratch):
        zs, zk, local = scratch[8], scratch[9], scratch[11]
        layer_sums([(scratch[j].at[0], scratch[j + 1].at[0], scratch[j + 3]) for j in (0, 4)], zs, zk)
        return [
            pltpu.make_async_copy(zs, outs[0], local.at[2]),
            pltpu.make_async_copy(zk, outs[1], local.at[3]),
        ]


class GoHome:
    peers = ("t0", "t1")

    def __init__(self, values, tick_at=1):
        self.tick_at = tick_at
        self.ins = [values]
        self.outs = [jax.ShapeDtypeStruct((2, LB, D), values.dtype)]
        self.scratch = [pltpu.SemaphoreType.DMA((2, 2)), pltpu.SemaphoreType.DMA]

    def plan(self, ins, outs, scratch):
        return [], []

    def tick(self, ins, outs, scratch):
        home_start(*self.copies(ins, outs, scratch))

    def copies(self, ins, outs, scratch):
        return homeward(ins[0].at[pl.ds(0, LB)], ins[0].at[pl.ds(LB, LB)], outs[0], *scratch)

    def settle(self, ins, outs, scratch):
        home_wait(*self.copies(ins, outs, scratch))
        return []

    def finish(self, ins, outs, scratch):
        return []


def homeward(first, second, dst, sems, local):
    x = place()[3]
    return (
        remote(first, dst.at[x], sems, 0, "t0"),
        pltpu.make_async_copy(first, dst.at[x], local),
        remote(second, dst.at[x], sems, 1, "t1"),
    )


def home_start(away, stay, second):
    _, c, y, _ = place()
    pl.when(c != y)(away.start)
    pl.when(c == y)(stay.start)
    second.start()


def home_wait(away, stay, second):
    _, c, y, _ = place()
    pl.when(c != y)(away.wait)
    pl.when(c == y)(stay.wait)
    second.wait()


def call(kernel, name, out_shape, args, in_specs=None, out_specs=None, scratch=(), grid=None,
         peers=(), jobs=(), cid=None, ticks=False, flops=0, nbytes=0):
    whole = pl.BlockSpec(memory_space=pltpu.VMEM)
    single = not isinstance(out_shape, (tuple, list))
    out_shape = [out_shape] if single else list(out_shape)
    in_specs = list(in_specs) if in_specs is not None else [whole] * len(args)
    out_specs = [whole] * len(out_shape) if out_specs is None else [out_specs] if single else list(out_specs)
    counts = [len(args), sum(len(j.ins) for j in jobs), len(out_shape), sum(len(j.outs) for j in jobs), len(scratch)]
    names = sorted(set(peers).union(*[j.peers for j in jobs]))

    def run(*refs):
        groups, at = [], 0
        for n in counts:
            groups.append(refs[at : at + n])
            at += n
        bound, ai, ao, asc = [], 0, 0, at
        for j in jobs:
            bound.append((
                j, groups[1][ai : ai + len(j.ins)], groups[3][ao : ao + len(j.outs)], refs[asc : asc + len(j.scratch)]
            ))
            ai, ao, asc = ai + len(j.ins), ao + len(j.outs), asc + len(j.scratch)

        def begin():
            if names:
                meet(names)
            for j, *r in bound:
                if not getattr(j, "start_at", 0):
                    j_start(j, r)

        def j_start(j, r):
            for group in j.plan(*r):
                for copy in group:
                    copy.start()

        def tick(k):
            for j, *r in bound:
                if getattr(j, "tick_at", 0) == k:
                    j.tick(*r)
            for j, *r in bound:
                if getattr(j, "start_at", 0) == k:
                    j_start(j, r)

        def end():
            last = []
            for j, *r in bound:
                far, near = (j.settle(*r), []) if hasattr(j, "tick") else j.plan(*r)
                for copy in far:
                    copy.wait()
                for copy in near:
                    copy.wait()
                copies = j.finish(*r)
                for copy in copies:
                    copy.start()
                last += copies
            for copy in last:
                copy.wait()

        if grid is None:
            begin()
            kernel(*groups[0], *groups[2], *groups[4], **({"tick": tick} if ticks else {}))
            end()
        else:
            pl.when(pl.program_id(0) == 0)(begin)
            kernel(*groups[0], *groups[2], *groups[4])
            pl.when(pl.program_id(0) == grid[0] - 1)(end)

    extra = {} if grid is None else {"grid": grid}
    params = {"collective_id": cid, "has_side_effects": True} if names else {}
    outs = pl.pallas_call(
        run,
        out_shape=out_shape + [o for j in jobs for o in j.outs],
        in_specs=in_specs + [ANY] * counts[1],
        out_specs=out_specs + [ANY] * counts[3],
        scratch_shapes=list(scratch) + [q for j in jobs for q in j.scratch],
        compiler_params=pltpu.CompilerParams(vmem_limit_bytes=VMEM_LIMIT, **params),
        cost_estimate=pl.CostEstimate(flops=int(flops), bytes_accessed=int(nbytes), transcendentals=0),
        name=name,
        **extra,
    )(*args, *[a for j in jobs for a in j.ins])
    own, rest, given = outs[: len(out_shape)], outs[len(out_shape) :], []
    for j in jobs:
        given.append(rest[: len(j.outs)])
        rest = rest[len(j.outs) :]
    return (own[0] if single else own), given


def full(shape):
    return pl.BlockSpec(shape, lambda *_: (0,) * len(shape))


def once(*shape):
    return pl.BlockSpec(shape, lambda *_: (0,) * len(shape), pipeline_mode=pl.Buffered(1))


def rows(block, width):
    return pl.BlockSpec((block, width), lambda i: (i, 0))


def column(n):
    return lax.broadcasted_iota(jnp.int32, (n, 1), 0)


def front_kernel(tokens, cotangent, timesteps, bucket_ids, skips, ada_w, ada_b, head_masks, channel_masks, w_qkv, w_fc1,
                 q_bias, v_bias, b1, freq, tok_o, cot_o, shifted_o, qkv_o, wq_o, w1_o, mod_o, kept_o, hmask_o, chan_o, b1_o,
                 tk, ck, wqv, wqc, w1v, w1c, adav, ints, ints_other, m4, to_send, shares, csems, tsems, ssems, lsems):
    z, c, y, x = place()
    t = 2 * y + x
    loads = [
        pltpu.make_async_copy(a, b, lsems.at[k])
        for k, (a, b) in enumerate(((ada_w, adav), (w_qkv, wqv), (w_fc1, w1v)))
    ]

    def arrivals(src, dst, k):
        block = [dst.at[pl.ds(LB * j, LB)] for j in range(4)]
        first = remote(src.at[x], block[0], tsems, k, "t0")
        stay = pltpu.make_async_copy(src.at[x], block[0], lsems.at[3 + k])
        second = remote(src.at[1 - x], block[1], tsems, 2 + k, "t1")
        onward = [remote(block[j], block[2 + j], csems, 2 * k + j, "c") for j in range(2)]
        return first, stay, second, onward

    def leave(first, stay, second, onward):
        pl.when(c != y)(first.start)
        pl.when(c == y)(stay.start)
        second.start()

    def pass_on(first, stay, second, onward):
        pl.when(c != y)(first.wait_recv)
        pl.when(c == y)(stay.wait)
        onward[0].start()
        second.wait_recv()
        onward[1].start()

    def settle(first, stay, second, onward):
        pl.when(c != y)(first.wait_send)
        second.wait_send()
        for copy in onward:
            copy.wait_send()

    tok_moves, cot_moves = arrivals(tokens, tk, 0), arrivals(cotangent, ck, 1)
    leave(*tok_moves)
    halves = [skips[:, :LANES], skips[:, LANES:]]
    ints[0:4, :] = jnp.concatenate([halves[0][0:1], halves[1][0:1], halves[0][1:2], halves[1][1:2]], axis=0)
    for k, value in enumerate((timesteps[0], timesteps[1], bucket_ids[0], 0)):
        ints[4 + k : 5 + k, :] = jnp.full((1, LANES), value, jnp.int32)
    swap = remote(ints, ints_other, csems, 4, "c")
    swap.start()
    for load in loads:
        load.start()
    swap.wait()

    mine, other = ints[...], ints_other[...]
    r = column(8)
    steps = jnp.zeros((8, 1), f32)
    for k in range(2):
        steps = jnp.where(r == 2 * c + k, mine[4 + k : 5 + k, 0:1].astype(f32), steps)
        steps = jnp.where(r == 2 * (1 - c) + k, other[4 + k : 5 + k, 0:1].astype(f32), steps)
    angles = steps * freq[...]
    condition = jax.nn.silu(jnp.concatenate([jnp.cos(angles), jnp.sin(angles)], axis=1))
    condition = jnp.concatenate([condition, jnp.zeros_like(condition)], axis=0).astype(bf16)
    loads[0].wait()
    m4[...] = dot_nt(condition, adav[...])[:8] + ada_b[...].astype(f32).reshape(1, -1)
    moves = []
    for k in range(4):
        to = (y + k // 2) % 2 * 2 + (x + k) % 2
        row = jnp.broadcast_to(m4[pl.ds(to, 1), :], to_send.shape[1:])
        if k == 0:
            shares[t] = row
        else:
            to_send[k - 1] = row
            moves.append(remote(to_send.at[k - 1], shares.at[t], ssems, k - 1, ("x", "y", "xy")[k - 1]))
            moves[-1].start()

    group = jnp.where(c == y, mine, other)
    bucket = group[6:7, 0:1]
    skip = jnp.where(x == 0, group[0:2], group[2:4])
    for j in range(4):
        block = 2 * ((c + j // 2) % 2) + (x + j) % 2
        position = column(LB) + LB * block
        hit = jnp.where((position == skip[0:1, :]) | (position == skip[1:2, :]), 1.0, 0.0)
        kept_o[LB * j : LB * (j + 1), :] = 1.0 - jnp.max(hit, axis=1, keepdims=True)

    def chosen(masks):
        line = lax.broadcasted_iota(jnp.int32, masks.shape, 0)
        row = jnp.sum(jnp.where(line == bucket, masks[...].astype(f32), 0.0), axis=0, keepdims=True)
        return jnp.broadcast_to(row, (16, masks.shape[1])).astype(bf16)

    def spread(on, low, width):
        first = width * lax.broadcasted_iota(jnp.int32, (on.shape[1], low.shape[1]), 0)
        return dot_nn(on, jnp.where((low >= first) & (low < first + width), 1.0, 0.0).astype(bf16))[0:1, :]

    lane = lax.broadcasted_iota(jnp.int32, (1, WC), 1)
    share = sum(jnp.where(lane >= DC * k, 1, 0) for k in range(1, 4))
    hmask_o[...] = spread(chosen(head_masks), lane + DC * (share + c), HD)
    channels = chosen(channel_masks)
    lane = lax.broadcasted_iota(jnp.int32, (1, FB), 1)
    share = sum(jnp.where(lane >= FZ * k, 1, 0) for k in range(1, 4))
    for f in range(NF):
        low = lane + (4 * DZ - FZ) * share + FF // 8 * c + FZ * f
        chan_o[f] = spread(channels, low, FF // channels.shape[1])

    def half(v, k, width):
        v = v[:, 2 * width * k : 2 * width * (k + 1)]
        return jnp.where(c == 0, v[:, :width], v[:, width:])

    def line(ref):
        return ref[...].astype(f32).reshape(1, -1)

    def parity(v, odd):
        return [half(v, k, DC)[:, HD * odd : HD * (odd + 1)] for k in range(4)]

    bias = []
    for odd in range(2):
        bias += parity(line(q_bias), odd) + [jnp.zeros((1, DZ), f32)] + parity(line(v_bias), odd)
    bias = jnp.concatenate(bias, axis=1)
    b1v = [half(line(b1), k, FF // 8) for k in range(4)]
    for f in range(NF):
        b1_o[f] = jnp.concatenate([v[:, FZ * f : FZ * (f + 1)] for v in b1v], axis=1)
    loads[1].wait()
    loads[2].wait()
    for core in range(2):

        @pl.when(c == core)
        def _():
            for odd in range(2):
                for k in range(12):
                    to, start = WQ * odd + HD * k, DZ * k + DC * core + HD * odd
                    wqc[:, to : to + HD] = wqv[:, start : start + HD]
            for f in range(NF):
                for k in range(4):
                    start = 4 * DZ * k + FF // 8 * core + FZ * f
                    w1c[f, :, FZ * k : FZ * (k + 1)] = w1v[:, start : start + FZ]

    stores = [
        pltpu.make_async_copy(a, b, lsems.at[k]) for k, (a, b) in enumerate(((wqc, wq_o), (w1c, w1_o)))
    ]
    for store in stores:
        store.start()
    pass_on(*tok_moves)
    leave(*cot_moves)
    for copy in moves:
        copy.wait()
    share_rows = [shares[k][0:1, :] for k in range(4)]
    n, m = D // 2, 3 * D // 2
    mod = [share_rows[0][:, :D], jnp.concatenate([share_rows[0][:, D:], share_rows[1][:, :n]], axis=1),
           share_rows[1][:, n:], share_rows[2][:, :D],
           jnp.concatenate([share_rows[2][:, D:], share_rows[3][:, :n]], axis=1), share_rows[3][:, n:]]
    own_step = 0.5 * jnp.sum(jnp.where(r == t, steps, 0.0), axis=0, keepdims=True)
    mod += [jnp.broadcast_to(own_step, (1, D)), jnp.zeros((1, D), f32)]
    mod_o[...] = jnp.concatenate(mod, axis=0)
    for j in range(4):
        if j >= 2:
            tok_moves[3][j - 2].wait_recv()
        part = slice(LB * j, LB * (j + 1))
        normed, _ = normalize(tk[part, :].astype(f32))
        shifted = (normed * (1.0 + mod[1]) + mod[0]).astype(bf16)
        shifted_o[part, :] = shifted
        qkv_o[part, :] = (dot_nn(shifted, wqc[...]) + bias).astype(bf16)
    keep = pltpu.make_async_copy(tk, tok_o, lsems.at[2])
    keep.start()
    pass_on(*cot_moves)
    for copy in cot_moves[3]:
        copy.wait_recv()
    keep_cot = pltpu.make_async_copy(ck, cot_o, lsems.at[5])
    keep_cot.start()
    settle(*tok_moves)
    settle(*cot_moves)
    for store in stores:
        store.wait()
    keep.wait()
    keep_cot.wait()


def attn_kernel(step, qkv, hmask, wp, bias, tok, mod, mixed_o, shifted2_o, attn_o,
                qh, kh, vh, mx, mo, wpv, tkv, csems, lsems):
    c = place()[1]
    loads = [
        pltpu.make_async_copy(wp.at[:, c], wpv.at[0], lsems.at[0]),
        pltpu.make_async_copy(wp.at[:, 1 - c], wpv.at[1], lsems.at[1]),
        pltpu.make_async_copy(tok, tkv, lsems.at[2]),
    ]
    for load in loads:
        load.start()
    scale = LOG2E / math.sqrt(HD)
    for h in range(HC):
        for k, ref in enumerate((qh, kh, vh)):
            start = WQ * (h % 2) + DZ * k + HD * (h // 2)
            ref[h] = qkv[:, start : start + HD]

    def crossing(i):
        src = mx.at[pl.ds(pl.multiple_of(i * step, step), step)]
        dst = mo.at[pl.ds(pl.multiple_of((i * step + LH) % L, step), step)]
        return remote(src, dst, csems, i, "c")

    def body(i, carry):
        part = pl.ds(pl.multiple_of(i * step, step), step)
        outs = []
        for h in range(HC):
            s = dot_nt(qh[h, part, :], kh[h])
            top = jnp.max(s, axis=1, keepdims=True)
            p = jnp.exp2((s - top) * scale)
            total = jnp.sum(p, axis=1, keepdims=True)
            outs.append(dot_nn(p.astype(bf16), vh[h]) * (1.0 / total))
        mx[part, :] = (jnp.concatenate(outs, axis=1) * hmask[...]).astype(bf16)
        crossing(i).start()
        return carry

    lax.fori_loop(0, L // step, body, 0)
    keep = pltpu.make_async_copy(mx, mixed_o, lsems.at[3])
    keep.start()
    for load in loads:
        load.wait()
    for i in range(L // step):
        crossing(i).wait()
    w_mine, w_other = wpv[0].reshape(WC, D), wpv[1].reshape(WC, D)
    bias_line = bias[...].astype(f32).reshape(1, D)
    for j in range(4):
        part = slice(LB * j, LB * (j + 1))
        attn = dot_nn(mx[part, :], w_mine) + dot_nn(mo[part, :], w_other) + bias_line
        if j < 2:
            attn_o[part, :] = attn
        normed, _ = normalize(tkv[part, :].astype(f32) + mod[2:3, :] * attn)
        shifted2_o[part, :] = (normed * (1.0 + mod[4:5, :]) + mod[3:4, :]).astype(bf16)
    keep.wait()


def mlp_kernel(sh2, g, kept, mod, w1, b1, chan, w2,
               on_a0, q_a0, on_b0, q_b0, keep_a0, keep_b0, on_a1, q_a1, on_b1, q_b1, keep_a1, keep_b1,
               k2a, s2a, k2b, s2b, branch_o, ds2_o, branch_r, ds2_r, sum1_o, sum2_o,
               sh2v, gv, dbs, w1v, w2v, hid, dpre, br, ds, far, tt_, ka, sa, kb, sb, ra, rb, ona, onb,
               fsems, csems, lsems, wsems, osems):
    z, c, y, x = place()
    out0 = (on_a0, q_a0, on_b0, q_b0, keep_a0, keep_b0)
    out1 = (on_a1, q_a1, on_b1, q_b1, keep_a1, keep_b1)
    outs = (out0, out1)

    def weights(f):
        return [
            pltpu.make_async_copy(w1.at[f], w1v.at[f % 2], wsems.at[0, f % 2]),
            pltpu.make_async_copy(w2.at[:, c, f], w2v.at[f % 2], wsems.at[1, f % 2]),
        ]

    def first(f):
        k, out = f % 2, outs[f]
        return [
            remote(sa.at[k, 1], ra.at[k], fsems, 4 * k, "x"), remote(sb.at[k, 1], rb.at[k], fsems, 4 * k + 1, "y"),
            remote(sa.at[k, 0], out[1], fsems, 4 * k + 2, "x"), remote(sb.at[k, 0], out[3], fsems, 4 * k + 3, "y"),
        ]

    def stored(f):
        k = f % 2
        if f == NF - 1:
            pairs = ((ka.at[k], k2a), (sa.at[k], s2a), (kb.at[k], k2b), (sb.at[k], s2b))
        else:
            pairs = ((ka.at[k, 0], outs[f][4]), (kb.at[k, 0], outs[f][5]))
        return [pltpu.make_async_copy(src, dst, osems.at[k, j]) for j, (src, dst) in enumerate(pairs)]

    def onward(f):
        k = f % 2
        for copy in first(f):
            copy.wait()
        for kv, rv, on in ((ka, ra, ona), (kb, rb, onb)):
            on[k] = (kv[k, 1].astype(f32) + rv[k].astype(f32)).astype(bf16)
        copies = [
            pltpu.make_async_copy(src.at[k], dst, osems.at[k, 4 + j])
            for j, (src, dst) in enumerate(((ona, outs[f][0]), (onb, outs[f][2])))
        ]
        for copy in copies:
            copy.start()
        return copies

    loads = [pltpu.make_async_copy(src, dst, lsems.at[k]) for k, (src, dst) in enumerate(((g, gv), (sh2, sh2v)))]
    for copy in loads + weights(0):
        copy.start()
    loads[0].wait()
    sum2 = jnp.zeros((1, D), f32)
    for j in range(4):
        part = slice(LB * j, LB * (j + 1))
        db = (gv[part, :].astype(f32) * mod[5:6, :] * kept[part, :]).astype(bf16)
        dbs[part, :] = db
        sum2 += jnp.sum(db.astype(f32), axis=0, keepdims=True)
    sum2_o[...] = sum2
    loads[1].wait()
    crossing = [remote(far.at[j], dst, csems, j, "c") for j, dst in enumerate((branch_r, ds2_r))]
    waiting = []
    for f in range(NF):
        for copy in weights(f):
            copy.wait()
        if f + 1 < NF:
            for copy in weights(f + 1):
                copy.start()
        w1f, w2f = w1v[f % 2], w2v[f % 2].reshape(FB, D)
        on = chan[f]
        sum1 = jnp.zeros((1, FB), f32)
        for side in (1, 0):
            part = slice(LH * side, LH * (side + 1))
            v = dot_nn(sh2v[part, :], w1f) + b1[f]
            v2 = v * v
            th = jnp.tanh(GELU_K * v * (1.0 + GELU_C * v2))
            half = 0.5 * (1.0 + th)
            hidden = (v * half * on).astype(bf16)
            hid[part, :] = hidden
            slope = (half + (0.5 * GELU_K) * v * (1.0 - th * th) * (1.0 + (3.0 * GELU_C) * v2)) * on
            d_pre = (dot_nt(dbs[part, :], w2f) * slope).astype(bf16)
            dpre[part, :] = d_pre
            sum1 += jnp.sum(d_pre.astype(f32), axis=0, keepdims=True)
            branch, ds2 = dot_nn(hidden, w2f), dot_nt(d_pre, w1f)
            if f > 0:
                branch, ds2 = branch + br[part, :], ds2 + ds[part, :]
            if f < NF - 1:
                br[part, :] = branch
                ds[part, :] = ds2
            elif side == 1:
                far[0] = branch.astype(bf16)
                far[1] = ds2.astype(bf16)
                for copy in crossing:
                    copy.start()
            else:
                branch_o[...] = branch.astype(bf16)
                ds2_o[...] = ds2.astype(bf16)
        sum1_o[f] = sum1
        k = f % 2
        for m in range(3):
            cut = slice(m * D // 3, (m + 1) * D // 3)
            p = dot_tn(sh2v[:, cut], dpre[...]).astype(bf16)
            for t in range(4):
                tt_[t, cut, :FZ] = p[:, FZ * t : FZ * (t + 1)]
        for rz in range(4):
            zz = flip(z, rz)
            for ry in range(2):
                for rx in range(2):
                    tt = (ry + y) % 2 * 2 + (rx + x) % 2
                    o = (ka, sa)[rx]
                    tails = []
                    for rc in range(2):
                        block = tt_[tt, pl.ds(pl.multiple_of(zz * DZ + (rc + c) % 2 * DC, 16), DC), :FZ]
                        o[k, ry, rz, DC * rc : DC * (rc + 1), :] = block[:, :LANES]
                        tails.append(block[:, LANES:])
                    o[k, ry, rz, 2 * DC :, :] = jnp.concatenate(tails, axis=1)
        for m in range(3):
            cut = slice(m * FB // 3, (m + 1) * FB // 3)
            p = dot_tn(hid[:, cut], dbs[...]).astype(bf16)
            for t in range(4):
                tt_[t, cut, :] = p[:, TD * t : TD * (t + 1)]
        for rz in range(4):
            zz = flip(z, rz)
            for ry in range(2):
                for rx in range(2):
                    tt = (ry + y) % 2 * 2 + (rx + x) % 2
                    o = (kb, sb)[ry]
                    block = tt_[tt, pl.ds(pl.multiple_of(zz * FZ, 16), FZ), :]
                    o[k, rx, rz, :FZ, :] = block[:, :LANES]
                    o[k, rx, rz, FZ : 2 * FZ, :] = block[:, LANES : 2 * LANES]
                    q = FZ // 4
                    o[k, rx, rz, 2 * FZ :, :] = jnp.concatenate(
                        [block[q * j : q * (j + 1), 2 * LANES :] for j in range(4)], axis=1
                    )
        if f < NF - 1:
            for copy in first(f):
                copy.start()
        for copy in stored(f):
            copy.start()
        waiting += stored(f)
        if f > 0:
            waiting += onward(f - 1)
        if f == NF - 2:
            for copy in waiting:
                copy.wait()
            waiting = []
    for copy in waiting + crossing:
        copy.wait()


def middle_kernel(ds, ds_r, br, br_r, attn, tok, g, kept, mod, bias2, mixed, wp,
                  d_resid_o, out_o, dh_o, pka, psa, pkb, psb, sums_o, sum_o,
                  dsv, attnv, tokv, mixv, wpv, da, t1, csems, lsems):
    z, c, y, x = place()
    n = LH // 4
    near = pl.ds(0, LH)
    loads = [
        pltpu.make_async_copy(src, dst, lsems.at[k])
        for k, (src, dst) in enumerate(
            ((tok.at[near], tokv.at[0]), (attn, attnv), (ds, dsv.at[0]), (ds_r, dsv.at[1]), (br, dsv.at[2]),
             (br_r, dsv.at[3]), (g.at[near], tokv.at[1]), (wp.at[:, c], wpv), (mixed, mixv))
        )
    ]
    for load in loads:
        load.start()
    crossing = [remote(da.at[pl.ds(n * k, n)], da.at[pl.ds(LH + n * k, n)], csems, k, "c") for k in range(4)]
    sums = jnp.zeros((4, D), f32)
    bias_line = bias2[...].astype(f32).reshape(1, D)
    for load in loads[:7]:
        load.wait()
    for k in range(4):
        part = slice(n * k, n * (k + 1))
        gf, at = tokv[1, part, :].astype(f32), attnv[part, :]
        resid = tokv[0, part, :].astype(f32) + mod[2:3, :] * at
        normed2, inverse2 = normalize(resid)
        ds2 = dsv[0, part, :].astype(f32) + dsv[1, part, :].astype(f32)
        kb = kept[part, :] * (dsv[2, part, :].astype(f32) + dsv[3, part, :].astype(f32) + bias_line)
        out_o[part, :] = (resid + mod[5:6, :] * kb).astype(bf16)
        d_resid = gf + normalize_back(ds2 * (1.0 + mod[4:5, :]), normed2, inverse2)
        d_resid_o[part, :] = d_resid
        da[part, :] = (mod[2:3, :] * d_resid).astype(bf16)
        crossing[k].start()
        sums += jnp.concatenate(
            [jnp.sum(p, axis=0, keepdims=True) for p in (at * d_resid, ds2, ds2 * normed2, kb * gf)], axis=0
        )
    sums_o[...] = jnp.concatenate([sums, jnp.zeros((4, D), f32)], axis=0)
    for load in loads[7:]:
        load.wait()
    for copy in crossing:
        copy.wait()
    wv = wpv[...].reshape(WC, D)
    dh_o[...] = dot_nt(da[...], wv).astype(bf16)
    sum_o[...] = dot_nn(jnp.ones((16, L), bf16), da[...])[:8]
    grad = dot_tn(mixv[...], da[...]).astype(bf16)
    for t in range(4):
        t1[t] = grad[:, TD * t : TD * (t + 1)]
    for rz in range(4):
        zz = flip(z, rz)
        for ry in range(2):
            for rx in range(2):
                tt = (ry + y) % 2 * 2 + (rx + x) % 2
                a, b = (pka, psa)[rx], (pkb, psb)[ry]
                block = t1[tt, pl.ds(pl.multiple_of(zz * DC, 16), DC), :]
                a[ry, rz, :DC, :] = block[:, :LANES]
                a[ry, rz, DC:, :] = block[: PA - DC, LANES : 2 * LANES]
                b[rx, rz, : 2 * DC - PA, :] = block[PA - DC :, LANES : 2 * LANES]
                q = DC // 3
                tails = [block[q * k : q * (k + 1), 2 * LANES :] for k in range(3)]
                tails.append(jnp.zeros((q, 32), bf16))
                b[rx, rz, 2 * DC - PA :, :] = jnp.concatenate(tails, axis=1)


def qkv_slots(dqkv, shifted, extra, t1, ka, sa, kb, sb):
    z, _, y, x = place()
    grad = dot_tn(dqkv, shifted)
    for t in range(4):
        for zz in range(4):
            t1[t, zz] = grad[TQ * t : TQ * (t + 1), DZ * zz : DZ * (zz + 1)]
    q = TQ // 3
    for rz in range(4):
        zz = flip(z, rz)
        for ry in range(2):
            for rx in range(2):
                tt = (ry + y) % 2 * 2 + (rx + x) % 2
                block = t1[tt, zz]
                tails = [block[q * k : q * (k + 1), 2 * LANES :] for k in range(3)] + [jnp.zeros((q, 32), f32)]
                more = jnp.zeros((8, LANES), f32) if extra is None else extra[zz, tt]
                slot = [block[:, :LANES], block[:, LANES : 2 * LANES], jnp.concatenate(tails, axis=1), more]
                slot = jnp.concatenate(slot, axis=0).astype(bf16)
                (ka, sa)[rx][ry, rz] = slot[:QA]
                (kb, sb)[ry][rx, rz] = slot[QA:]


def column_sums(dqkv):
    return dot_nn(jnp.ones((16, L), bf16), dqkv)[:8]


def attn_back_kernel(step, qkv, dh, shifted, hmask, out, on_a, q_a, on_b, q_b, keep_a, keep_b, sums_o,
                     qkvv, dhv, shv, outv, qh, kh, vh, doh, dk, dv, t1, ka, sa, kb, sb, ra, rb, ona, onb,
                     fsems, lsems, tick):
    loads = [
        pltpu.make_async_copy(a, b, lsems.at[k])
        for k, (a, b) in enumerate(((qkv, qkvv), (dh, dhv), (shifted, shv)))
    ]
    for load in loads:
        load.start()
    for load in loads:
        load.wait()
    scale = LOG2E / math.sqrt(HD)
    first = [
        remote(sa.at[1], ra, fsems, 0, "x"), remote(sb.at[1], rb, fsems, 1, "y"),
        remote(sa.at[0], q_a, fsems, 2, "x"), remote(sb.at[0], q_b, fsems, 3, "y"),
    ]
    stores = [pltpu.make_async_copy(a, b, lsems.at[3 + k]) for k, (a, b) in enumerate(((ka.at[0], keep_a), (kb.at[0], keep_b)))]
    for odd in range(2):
        base = WQ * odd
        for j in range(HC // 2):
            for k, ref in enumerate((qh, kh, vh)):
                start = base + DZ * k + HD * j
                ref[j] = qkvv[:, start : start + HD]
            cut = slice(HD * (2 * j + odd), HD * (2 * j + odd + 1))
            doh[j] = (dhv[:, cut].astype(f32) * hmask[:, cut]).astype(bf16)
        dk[...] = jnp.zeros_like(dk)
        dv[...] = jnp.zeros_like(dv)

        def body(i, carry):
            part = pl.ds(pl.multiple_of(i * step, step), step)
            outs = []
            for j in range(HC // 2):
                q, do = qh[j, part, :], doh[j, part, :]
                s = dot_nt(kh[j], q)
                top = jnp.max(s, axis=0, keepdims=True)
                p = jnp.exp2((s - top) * scale)
                p = p * (1.0 / jnp.sum(p, axis=0, keepdims=True))
                dp = dot_nt(vh[j], do)
                row_dot = jnp.sum(p * dp, axis=0, keepdims=True)
                ds = (p * (dp - row_dot)).astype(bf16)
                dv[j] += dot_nn(p.astype(bf16), do)
                dk[j] += dot_nn(ds, q)
                outs.append(dot_tn(ds, kh[j]))
            outv[part, base : base + DZ] = (jnp.concatenate(outs, axis=1) * (1.0 / math.sqrt(HD))).astype(bf16)
            return carry

        half = L // step // 2
        lax.fori_loop(0, half, body, 0)
        tick(1 + 2 * odd)
        lax.fori_loop(half, 2 * half, body, 0)
        for j in range(HC // 2):
            start = base + DZ + HD * j
            outv[:, start : start + HD] = (dk[j] * (1.0 / math.sqrt(HD))).astype(bf16)
            outv[:, start + DZ : start + DZ + HD] = dv[j].astype(bf16)
        if odd == 0:
            sums_o[...] = column_sums(outv[:, :WQ])
            qkv_slots(outv[:, :WQ], shv[...], None, t1, ka, sa, kb, sb)
            for copy in first + stores:
                copy.start()
            tick(2)
    keep = pltpu.make_async_copy(outv, out, lsems.at[5])
    keep.start()
    for copy in first:
        copy.wait()
    for kv, rv, on in ((ka, ra, ona), (kb, rb, onb)):
        on[...] = (kv[1].astype(f32) + rv[...].astype(f32)).astype(bf16)
    onward = [pltpu.make_async_copy(a, b, lsems.at[6 + k]) for k, (a, b) in enumerate(((ona, on_a), (onb, on_b)))]
    for copy in onward:
        copy.start()
    for copy in stores + onward + [keep]:
        copy.wait()


def end_kernel(dqkv, shifted, even_sums, sum1, sum2, sum_attn, wq, d_resid, tok, mod, sums_mid, f0, f1, f2, sent_p, kept_p, freq,
               on_a, q_a, on_b, q_b, keep_a, keep_b,
               grad, gq_o, gp_o, g1_o, g2_o, ada_o, ada_bias_o, line_o,
               dqv, shv, extra, t1, ka, sa, kb, sb, ra, rb, ona, onb, r2a, r2b, zs, zk, zr,
               eqa, era, eka, eqb, erb, ekb, ezs, ezk, ezr, qt, wqv, dres, tokv, fv, far, got, gb,
               item, item_r, out_shares, square, every, row_out, row_in, mine, theirs, mine_q, theirs_q, pk, pr,
               qsems, esems, csems, tsems, ssems, psems, lsems):
    z, c, y, x = place()
    t, b = 2 * y + x, 2 * z + c
    second_e = [remote(on_a, era, esems, 0, "y"), remote(on_b, erb, esems, 1, "x")]
    third_p = [remote(sent_p.at[k], pr.at[k], psems, k, f"z{k + 1}") for k in (2, 1, 0)]
    pairs = ((dqkv, dqv), (shifted, shv), (wq, wqv), (d_resid, dres), (tok.at[pl.ds(0, LH)], tokv),
             (keep_a, eka), (q_a, eqa), (keep_b, ekb), (q_b, eqb), (f0, fv.at[0]), (f1, fv.at[1]), (f2, fv.at[2]),
             (kept_p, pk))
    loads = [pltpu.make_async_copy(src, dst, lsems.at[k]) for k, (src, dst) in enumerate(pairs)]
    for copy in second_e + third_p + loads:
        copy.start()

    loads[0].wait()
    loads[1].wait()
    odd = dqv[:, WQ:]
    odd_sums = column_sums(odd)
    for zs_ in range(4):
        for ts in range(4):
            start, n = FF // 32 * ts, FF // 32
            pieces = []
            for f in range(NF):
                low, high = max(start, FZ * f), min(start + n, FZ * (f + 1))
                if low < high:
                    pieces.append(sum1[f][:, FZ * zs_ + low - FZ * f : FZ * zs_ + high - FZ * f])
            n = D // 32
            for total in (sum2[...], sum_attn[0:1, :]):
                at = DZ * zs_ + n * ts
                pieces.append(jnp.where(c == 0, total[:, at : at + n], total[:, at + DC : at + DC + n]))
            total = (even_sums, odd_sums)[ts // 2][0:1, :]
            at = HD * zs_ + n * (ts % 2)
            pieces += [total[:, at : at + n], total[:, 2 * DZ + at : 2 * DZ + at + n]]
            flat = jnp.concatenate(pieces + [jnp.zeros((1, 3 * LANES - DZ), f32)], axis=1)
            lines = [flat[:, LANES * k : LANES * (k + 1)] for k in range(3)] + [jnp.zeros((5, LANES), f32)]
            extra[zs_, ts] = jnp.concatenate(lines, axis=0)
    qkv_slots(odd, shv[...], extra, t1, ka, sa, kb, sb)
    first_q = [
        remote(sa.at[1], ra.at[1], qsems, 0, "x"), remote(sb.at[1], rb.at[1], qsems, 1, "y"),
        remote(sa.at[0], ra.at[0], qsems, 2, "x"), remote(sb.at[0], rb.at[0], qsems, 3, "y"),
    ]
    for copy in first_q:
        copy.start()

    loads[2].wait()
    crossing = [remote(far.at[k], got.at[k], csems, k, "c") for k in range(2)]
    d_far = dot_nt(dqv[LH:, :], wqv[...])
    for k in range(2):
        far[k] = d_far[LB * k : LB * (k + 1)].astype(bf16)
        crossing[k].start()

    for copy in second_e:
        copy.wait()
    for k in (5, 6, 7, 8):
        loads[k].wait()
    layer_sums([(eka, eqa, era), (ekb, eqb, erb)], ezs, ezk)
    third_e = [remote(ezs.at[k], ezr.at[k], esems, 2 + k, f"z{k + 1}") for k in (2, 1, 0)]
    for copy in third_e:
        copy.start()
    d_near = dot_nt(dqv[:LH, :], wqv[...])
    loads[3].wait()
    loads[4].wait()
    token_sums = jnp.zeros((2, D), f32)
    for k in range(2):
        part = slice(LB * k, LB * (k + 1))
        crossing[k].wait()
        total = d_near[part] + got[k].astype(f32)
        normed, inverse = normalize(tokv[part, :].astype(f32))
        back = dres[part, :] + normalize_back(total * (1.0 + mod[1:2, :]), normed, inverse)
        gb[k] = back.astype(bf16)
        token_sums += jnp.concatenate(
            [jnp.sum(v, axis=0, keepdims=True) for v in (total, total * normed)], axis=0
        )
    item[...] = jnp.concatenate([token_sums, sums_mid[0:4, :], mod[6:8, :]], axis=0)
    over = remote(item, item_r, csems, 2, "c")
    over.start()

    for copy in first_q:
        copy.wait()
    for kv, rv, on in ((ka, ra, ona), (kb, rb, onb)):
        on[...] = (kv[1].astype(f32) + rv[1].astype(f32)).astype(bf16)
    second_q = [remote(ona, r2a, qsems, 4, "y"), remote(onb, r2b, qsems, 5, "x")]
    for copy in second_q:
        copy.start()
    over.wait()
    v = item[...] + item_r[...]
    n = D // 2
    stamp = v[6:7, :LANES]
    pieces = ([v[0:1], v[1:2, :n]], [v[1:2, n:], v[2:3]], [v[3:4], v[4:5, :n]], [v[4:5, n:], v[5:6]])
    for j in range(4):
        out_shares[j] = jnp.concatenate(pieces[j] + [stamp], axis=1)
    square[t] = out_shares[t]
    meeting = [
        remote(out_shares.at[(y + j // 2) % 2 * 2 + (x + j) % 2], square.at[t], ssems, j - 1, ("x", "y", "xy")[j - 1])
        for j in (1, 2, 3)
    ]
    for copy in meeting:
        copy.start()

    def first_columns(pairs, own):
        for core in range(2):

            @pl.when(c == core)
            def _():
                for f, pair in enumerate(pairs):
                    start = FF // 8 * (core if own else 1 - core) + FZ * f
                    g1_o[:, start : start + FZ] = jnp.concatenate(pair, axis=1)

    for k in (9, 10, 11, 12):
        loads[k].wait()
    for f in range(NF):
        mine[G1R * f : G1R * (f + 1), :] = fv[f, :G1R, :].astype(bf16)
    swap = remote(mine, theirs, csems, 3, "c")
    swap.start()
    first_columns([[fv[f, :DC, :], fv[f, 2 * DC : 3 * DC, : FZ - LANES]] for f in range(NF)], True)
    for copy in second_q:
        copy.wait()
    layer_sums([(ka.at[0], ra.at[0], r2a), (kb.at[0], rb.at[0], r2b)], zs, zk)
    third_q = [remote(zs.at[k], zr.at[k], qsems, 6 + k, f"z{k + 1}") for k in (2, 1, 0)]
    for copy in third_q:
        copy.start()
    home = homeward(gb.at[0], gb.at[1], grad, tsems, lsems.at[len(pairs)])
    home_start(*home)
    for copy in meeting:
        copy.wait()
    spread_z = [remote(square, every.at[z], ssems, 2 + k, f"z{k}") for k in (1, 2, 3)]
    every[z] = square[...]
    for copy in spread_z:
        copy.start()
    for f in range(NF):
        part = fv[f, G1R:, :]
        tail = part[2 * FZ :]
        tail = jnp.concatenate([tail[:, 32 * k : 32 * (k + 1)] for k in range(4)], axis=0)
        g2_o[FZ * f : FZ * (f + 1), :] = jnp.concatenate([part[:FZ], part[FZ : 2 * FZ], tail], axis=1)
    for copy in third_p:
        copy.wait()
    part = pk[...] + pr[0].astype(f32) + pr[1].astype(f32) + pr[2].astype(f32)
    tail = part[2 * DC :]
    tail = jnp.concatenate([tail[:, 32 * k : 32 * (k + 1)] for k in range(3)], axis=0)
    gp_o[...] = jnp.concatenate([part[:DC], part[DC : 2 * DC], tail], axis=1)
    swap.wait()
    first_columns(
        [
            [theirs[G1R * f + DC : G1R * f + 2 * DC, :].astype(f32),
             theirs[G1R * f + 2 * DC : G1R * (f + 1), FZ - LANES :].astype(f32)]
            for f in range(NF)
        ],
        False,
    )

    for copy in spread_z:
        copy.wait()
    columns = jnp.concatenate([every[i, j] for i in range(4) for j in range(4)], axis=0)
    width = 3 * D // 2
    angles = columns[:, width : width + 1] * freq[b % 4]
    cond = jax.nn.silu(jnp.where(b < 4, jnp.cos(angles), jnp.sin(angles))).astype(bf16).astype(f32)
    columns = columns[:, :width]
    ada_o[...] = lax.dot_general(
        cond, columns, (((0,), (0,)), ((), ())), precision=lax.Precision.HIGHEST, preferred_element_type=f32
    )
    row = jnp.sum(columns, axis=0, keepdims=True)
    row_out[0] = row
    row_in[t] = row
    rows_ = [remote(row_out.at[0], row_in.at[t], ssems, 6 + j, name) for j, name in enumerate(("x", "y", "xy"))]
    for copy in rows_:
        copy.start()

    for odd_, (copies, kept, more) in enumerate(((third_e, ezk, ezr), (third_q, zk, zr))):
        for copy in copies:
            copy.wait()
        q = kept[...] + more[0].astype(f32) + more[1].astype(f32) + more[2].astype(f32)
        tail = q[2 * TQ :]
        n = TQ // 3
        tail = jnp.concatenate([tail[n * 0 : n, 32 * k : 32 * (k + 1)] for k in range(3)], axis=0)
        qt[odd_] = jnp.transpose(jnp.concatenate([q[:TQ], q[TQ : 2 * TQ], tail], axis=1))
        mine_q[odd_] = qt[odd_, pl.ds(pl.multiple_of(DC * (1 - c), 16), DC), :].astype(bf16)
        swap = remote(mine_q.at[odd_], theirs_q.at[odd_], csems, 4 + odd_, "c")
        swap.start()
        if odd_ == 1:
            line_o[...] = q[QR - 8 :]
    own = [qt[odd_, pl.ds(pl.multiple_of(DC * c, 16), DC), :] for odd_ in range(2)]

    def qkv_columns(values, owned):
        for core in range(2):

            @pl.when(c == core)
            def _():
                for odd_ in range(2):
                    for j in range(3):
                        start = DZ * j + DC * (core if owned else 1 - core) + HD * odd_
                        gq_o[:, start : start + HD] = values[odd_][:, HD * j : HD * (j + 1)]

    qkv_columns(own, True)
    for odd_ in range(2):
        remote(mine_q.at[odd_], theirs_q.at[odd_], csems, 4 + odd_, "c").wait()
    qkv_columns([theirs_q[odd_].astype(f32) for odd_ in range(2)], False)
    for copy in rows_:
        copy.wait()
    row = row_in[z]
    ada_bias_o[...] = jnp.where(c == 0, row[:, : width // 2], row[:, width // 2 :])
    home_wait(*home)


def final_kernel(out_rows, grad_rows, gq, gp, g1, g2, ada, ada_bias, line,
                 out, grad, gq_o, gp_o, g1_o, g2_o, ada_o, ada_bias_o, b_fc1, b_fc2, b_proj, b_q, b_v):
    out[...] = out_rows[...]
    grad[...] = grad_rows[...].astype(f32)
    gq_o[...] = gq[...]
    gp_o[...] = gp[...]
    g1_o[...] = g1[...]
    g2_o[...] = jnp.transpose(g2[...])
    ada_o[...] = ada[...]
    ada_bias_o[...] = ada_bias[...]
    flat = jnp.concatenate([line[k : k + 1, :] for k in range(3)], axis=1)
    n1, n = FF // 32, D // 32
    b_fc1[...] = flat[:, :n1]
    for k, ref in enumerate((b_fc2, b_proj, b_q, b_v)):
        ref[...] = flat[:, n1 + n * k : n1 + n * (k + 1)]


def one_item_per_chip(
    tokens, cotangent, timesteps, bucket_ids, head_masks, channel_masks, skip_rows,
    w_qkv, q_bias, v_bias, w_proj, proj_bias, w_fc1, fc1_bias, w_fc2, fc2_bias, ada_weight, ada_bias,
):
    b, t = lax.axis_index("bucket"), lax.axis_index("tok")
    z, c, y, x = b // 2, b % 2, t // 2, t % 2
    sds = jax.ShapeDtypeStruct

    def core_half(v, *dims):
        return lax.dynamic_index_in_dim(v.reshape(dims), c, 1, keepdims=False)

    vmem, smem = pl.BlockSpec(memory_space=pltpu.VMEM), pl.BlockSpec(memory_space=pltpu.SMEM)
    steps = -np.float32(math.log(10000.0)) * np.arange(D // 2, dtype=np.float32) / np.float32(D // 2)
    freq = jnp.asarray(np.exp(steps).reshape(1, D // 2))
    ada_cols = ada_weight.shape[1]
    front, _ = call(
        front_kernel, "front",
        (sds((L, D), bf16), sds((L, D), bf16), sds((L, D), bf16), sds((L, 3 * WC), bf16), sds((D, 3 * WC), bf16),
         sds((NF, D, FB), bf16), sds((8, D), f32), sds((L, 1), f32), sds((1, WC), f32), sds((NF, 1, FB), f32),
         sds((NF, 1, FB), f32)),
        (tokens, cotangent, timesteps, bucket_ids, skip_rows, ada_weight.T, ada_bias, head_masks, channel_masks,
         w_qkv, w_fc1, q_bias, v_bias, fc1_bias, freq),
        in_specs=[ANY, ANY, smem, smem, vmem, ANY, vmem, vmem, vmem, ANY, ANY, vmem, vmem, vmem, vmem],
        out_specs=[ANY, ANY, vmem, vmem, ANY, ANY] + [vmem] * 5,
        scratch=[vm(L, D), vm(L, D), vm(D, 3 * D), vm(D, 3 * WC), vm(D, FF), vm(NF, D, FB), vm(ada_cols, D),
                 vm(8, LANES, dtype=jnp.int32), vm(8, LANES, dtype=jnp.int32), vm(8, ada_cols, dtype=f32), vm(3, 8, ada_cols, dtype=f32),
                 vm(4, 8, ada_cols, dtype=f32), pltpu.SemaphoreType.DMA((2, 5)), pltpu.SemaphoreType.DMA((2, 4)),
                 pltpu.SemaphoreType.DMA((2, 3)), pltpu.SemaphoreType.DMA((6,))],
        peers=("c", "t0", "t1", "x", "y", "xy"), cid=10, flops=2 * L * D * 3 * WC, nbytes=50e6,
    )
    tok, g_all, shifted, qkv, wq, w1, mod, kept, hmask, chan, b1 = front
    w2 = w_fc2.reshape(4, 2, NF, FZ, D)
    wp = w_proj.reshape(4, 2, DC, D)
    (mixed, shifted2, attn), _ = call(
        functools.partial(attn_kernel, 256), "attn",
        (sds((L, WC), bf16), sds((L, D), bf16), sds((LH, D), f32)),
        (qkv, hmask, wp, proj_bias, tok, mod),
        in_specs=[vmem, vmem, ANY, vmem, ANY, vmem],
        out_specs=[ANY, vmem, vmem],
        scratch=[vm(HC, L, HD)] * 3 + [vm(L, WC), vm(L, WC), vm(2, 4, DC, D), vm(L, D),
                 pltpu.SemaphoreType.DMA((2, 4)), pltpu.SemaphoreType.DMA((4,))],
        peers=("c",), cid=11, flops=16e9, nbytes=5e6,
    )

    slot1, slot2 = sds((2, 4, G1R, LANES), bf16), sds((2, 4, G2R, LANES), bf16)
    part1, part2 = sds(slot1.shape[1:], bf16), sds(slot2.shape[1:], bf16)
    one = [part1, part1, part2, part2, part1, part2]
    rows_half = sds((LH, D), bf16)
    dma = pltpu.SemaphoreType.DMA
    own, _ = call(
        mlp_kernel, "mlp",
        one + one + [slot1, slot1, slot2, slot2] + [rows_half] * 4 + [sds((NF, 1, FB), f32), sds((1, D), f32)],
        (shifted2, g_all, kept, mod, w1, b1, chan, w2),
        in_specs=[ANY, ANY, vmem, vmem, ANY, vmem, vmem, ANY],
        out_specs=[ANY] * 16 + [vmem, vmem, ANY, ANY, vmem, vmem],
        scratch=[vm(L, D), vm(L, D), vm(L, D), vm(2, D, FB), vm(2, 4, FZ, D), vm(L, FB), vm(L, FB),
                 vm(L, D, dtype=f32), vm(L, D, dtype=f32), vm(2, LH, D), vm(4, D, TD)]
        + [vm(2, *slot1.shape)] * 2 + [vm(2, *slot2.shape)] * 2
        + [vm(2, *p.shape) for p in (part1, part2)] * 2
        + [dma((2, 8)), dma((2, 2)), dma((2,)), dma((2, 2)), dma((2, 6))],
        peers=("c", "x", "y"), cid=0,
        flops=36 * L * D * FB, nbytes=40e6,
    )
    second0, second1, slots = own[:6], own[6:12], own[12:16]
    branch, ds2, branch_r, ds2_r, sum1, sum2 = own[16:]

    slot_a, slot_b = sds((2, 4, PA, LANES), bf16), sds((2, 4, PR - PA, LANES), bf16)
    own, given = call(
        middle_kernel, "middle",
        (sds((LH, D), f32), rows_half, sds((L, WC), bf16), slot_a, slot_a, slot_b, slot_b, sds((8, D), f32),
         sds((8, D), f32)),
        (ds2, ds2_r, branch, branch_r, attn, tok, g_all, kept, mod, fc2_bias, mixed, wp),
        in_specs=[ANY] * 7 + [vmem] * 3 + [ANY] * 2,
        scratch=[vm(4, LH, D), vm(LH, D, dtype=f32), vm(2, LH, D), vm(L, WC), vm(4, DC, D), vm(L, D), vm(4, WC, TD),
                 dma((2, 4)), dma((9,))],
        peers=("c",), cid=3, jobs=[FirstSum(*slots), SecondSum(*second0)],
        flops=4 * L * D * WC, nbytes=20e6,
    )
    d_resid, out_rows, dh, *slots_p, sums_mid, sum_attn = own
    first2, result0 = given
    slot_q = vm(2, 4, QA, LANES)
    fourth = vm(4, QA, LANES)
    part_q = sds((4, QA, LANES), bf16)
    own, given = call(
        functools.partial(attn_back_kernel, 512), "attn_back",
        [sds((L, 3 * WC), bf16)] + [part_q] * 6 + [sds((8, WQ), f32)], (qkv, dh, shifted, hmask),
        in_specs=[ANY] * 3 + [vmem],
        out_specs=[ANY] * 7 + [vmem],
        scratch=[vm(L, 3 * WC), vm(L, WC), vm(L, D), vm(L, 3 * WC)] + [vm(HC // 2, L, HD)] * 4
        + [vm(HC // 2, L, HD, dtype=f32)] * 2 + [vm(4, 4, TQ, DZ, dtype=f32)] + [slot_q] * 4 + [fourth] * 4
        + [dma((2, 4)), dma((8,))],
        cid=4, ticks=True,
        jobs=[SecondThird(*second1, tick_at=1), SecondThird(*first2, slots[0], slots[2], start_at=1, tick_at=3),
              FirstSecond(*slots_p, start_at=1, tick_at=3), ThirdSum(*result0), GoHome(out_rows, tick_at=3)],
        flops=30e9, nbytes=9e6,
    )
    dqkv, *second_q, even_sums = own
    final1, final2, (sent_p, kept_p), final0, output = given[0][0], given[1][0], given[2], given[3][0], given[4][0]
    width = ada_cols + LANES
    (grad_rows, gq, gp, g1, g2, grad_ada_weight, grad_ada_bias, line), _ = call(
        end_kernel, "end",
        (sds((2, LB, D), bf16), sds((DC, 3 * TD), f32), sds((DC, TD), f32), sds((DC, FF // 4), f32),
         sds((FF // 8, TD), f32), sds((DC, ada_cols), f32), sds((1, ada_cols // 2), f32), sds((8, LANES), f32)),
        (dqkv, shifted, even_sums, sum1, sum2, sum_attn, wq, d_resid, tok, mod, sums_mid, final0, final1, final2, sent_p,
         kept_p, freq.reshape(4, 1, DC), *second_q),
        in_specs=[ANY] * 2 + [vmem] * 4 + [ANY] * 3 + [vmem] * 2 + [ANY] * 5 + [vmem] + [ANY] * 6,
        out_specs=[ANY] + [vmem] * 7,
        scratch=[vm(L, 3 * WC), vm(L, D), vm(4, 4, 8, LANES, dtype=f32), vm(4, 4, TQ, DZ, dtype=f32)] + [slot_q] * 6
        + [fourth] * 4 + [vm(3, QR, LANES), vm(QR, LANES, dtype=f32), vm(3, QR, LANES)]
        + [fourth] * 6 + [vm(3, QR, LANES), vm(QR, LANES, dtype=f32), vm(3, QR, LANES)]
        + [vm(2, DZ, TQ, dtype=f32), vm(D, 3 * WC), vm(LH, D, dtype=f32), vm(LH, D),
           vm(NF, G1R + G2R, LANES, dtype=f32)] + [vm(2, LB, D)] * 3
        + [vm(8, D, dtype=f32)] * 2 + [vm(4, 1, width, dtype=f32)] * 2
        + [vm(4, 4, 1, width, dtype=f32), vm(1, 1, ada_cols, dtype=f32), vm(4, 1, ada_cols, dtype=f32)]
        + [vm(NF * G1R, LANES)] * 2 + [vm(2, DC, TQ)] * 2 + [vm(PR, LANES, dtype=f32), vm(3, PR, LANES)]
        + [dma((2, 9)), dma((2, 5)), dma((2, 6)), dma((2, 2)), dma((2, 9)), dma((2, 3)), dma((14,))],
        peers=("c", "t0", "t1", "x", "y", "xy", "z1", "z2", "z3"), cid=5,
        flops=4 * L * D * 3 * WC, nbytes=30e6,
    )
    thin = lambda height, width: pl.BlockSpec((height, width), lambda i: (i, 0))
    tokens_spec = pl.BlockSpec((2, LB // 2, D), lambda i: (0, i, 0))
    ends = [thin(DC // 2, 3 * TD), thin(DC // 2, TD), thin(DC // 2, FF // 4)]
    bias_cols = ada_cols // 2
    finals, _ = call(
        final_kernel, "final",
        (sds((2, LB, D), bf16), sds((2, LB, D), f32), sds((DC, 3 * TD), f32), sds((DC, TD), f32), sds((DC, FF // 4), f32),
         sds((TD, FF // 8), f32), sds((DC, ada_cols), f32), sds((1, bias_cols), f32), sds((1, FF // 32), f32))
        + (sds((1, D // 32), f32),) * 4,
        (output, grad_rows, gq, gp, g1, g2, grad_ada_weight, grad_ada_bias, line),
        grid=(2,),
        in_specs=[tokens_spec, tokens_spec, *ends, full((FF // 8, TD)), thin(DC // 2, ada_cols), full((1, bias_cols)),
                  full((8, LANES))],
        out_specs=[tokens_spec, tokens_spec, *ends, full((TD, FF // 8)), thin(DC // 2, ada_cols), full((1, bias_cols)),
                   full((1, FF // 32))] + [full((1, D // 32))] * 4,
    )
    output, grad_tokens, gq, gp, g1, g2, g_ada, *lines = finals
    ada_b, b_fc1, b_fc2, b_proj, b_q, b_v = [v.reshape(-1) for v in lines]
    return (output, grad_tokens, gq, b_q, b_v, gp, b_proj, g1, b_fc1, g2.T, b_fc2, g_ada, ada_b)


def gelu_tanh(values):
    return jax.nn.gelu(values, approximate=True)


def split_heads(key_value, model_width, head_dim):
    item_count, length = (key_value.shape[0], key_value.shape[1])
    key_rows = key_value[:, :, :model_width].reshape(
        item_count, length, model_width // head_dim, head_dim
    )
    value_rows = key_value[:, :, model_width:].reshape(
        item_count, length, model_width // head_dim, head_dim
    )
    return (key_rows, value_rows)


def scores_of(queries, key_rows, score_scale):
    return (
        jnp.einsum("nqhe,nkhe->nhqk", queries, key_rows, preferred_element_type=jnp.float32)
        * score_scale
    )


def to_blocks(values, per_step):
    return values.reshape((values.shape[0] // per_step, per_step) + values.shape[1:])


def from_blocks(values):
    return values.reshape((values.shape[0] * values.shape[1],) + values.shape[2:])


def on_device(
    tokens,
    cotangent,
    timesteps,
    bucket_ids,
    head_masks,
    channel_masks,
    skip_rows,
    w_qkv,
    q_bias,
    v_bias,
    w_proj,
    proj_bias,
    w_fc1,
    fc1_bias,
    w_fc2,
    fc2_bias,
    ada_weight,
    ada_bias,
):
    item_count, local_len, model_width = tokens.shape
    row_count = item_count * local_len
    head_dim = model_width // HEADS
    score_scale = 1.0 / math.sqrt(head_dim)
    hidden_width = w_fc1.shape[1]
    ada_cols = ada_weight.shape[1]
    tok_index = lax.axis_index("tok")
    per_step = 1
    for candidate in range(1, item_count + 1):
        per_step = candidate
    condition = jax.nn.silu(step_embedding(timesteps, model_width)).astype(jnp.bfloat16)
    mod_local = jnp.dot(
        condition, ada_weight, preferred_element_type=jnp.float32
    ) + ada_bias.astype(jnp.float32)
    modulation = lax.all_gather(mod_local, "tok", axis=1, tiled=True)
    pieces = modulation.reshape(item_count, 6, 1, model_width)
    shift_a = pieces[:, 0]
    scale_a = pieces[:, 1]
    gate_a = pieces[:, 2]
    shift_m = pieces[:, 3]
    scale_m = pieces[:, 4]
    gate_m = pieces[:, 5]
    chosen = (jnp.arange(head_masks.shape[0], dtype=jnp.int32) == bucket_ids[0]).astype(jnp.float32)
    head_on = jnp.sum(chosen[:, None] * head_masks.astype(jnp.float32), axis=0)
    group_on = jnp.sum(chosen[:, None] * channel_masks.astype(jnp.float32), axis=0)
    channel_on = jnp.repeat(group_on, hidden_width // group_on.shape[0])
    positions = tok_index * local_len + jnp.arange(local_len, dtype=jnp.int32)
    skipped = jnp.any(skip_rows[:, :, None] == positions[None, None, :], axis=1)
    kept_rows = 1.0 - skipped.astype(jnp.float32)
    inputs = tokens.astype(jnp.float32)
    normed, inverse = normalize(inputs)
    shifted = (
        (normed * (1.0 + scale_a) + shift_a).astype(jnp.bfloat16).reshape(row_count, model_width)
    )
    qkv_bias = jnp.concatenate([q_bias, jnp.zeros_like(q_bias), v_bias]).astype(jnp.float32)
    projected = (jnp.dot(shifted, w_qkv, preferred_element_type=jnp.float32) + qkv_bias).astype(
        jnp.bfloat16
    )
    projected = projected.reshape(item_count, local_len, 3 * model_width)
    queries = projected[:, :, :model_width].reshape(item_count, local_len, HEADS, head_dim)
    key_value = projected[:, :, model_width:]
    all_kv = lax.all_gather(key_value, "tok", axis=1, tiled=True)

    def forward_block(packed):
        query_block, kv_block = packed
        key_rows, value_rows = split_heads(kv_block, model_width, head_dim)
        scores = scores_of(query_block, key_rows, score_scale)
        top_score = jnp.max(scores, axis=-1, keepdims=True)
        expanded = jnp.exp(scores - top_score)
        totals = jnp.sum(expanded, axis=-1, keepdims=True)
        weights_low = (expanded / totals).astype(jnp.bfloat16)
        head_out = (
            jnp.einsum(
                "nhqk,nkhe->nqhe", weights_low, value_rows, preferred_element_type=jnp.float32
            )
            * head_on[:, None]
        )
        return (head_out.astype(jnp.bfloat16), top_score + jnp.log(totals))

    mixed_heads, log_total = lax.map(
        forward_block, (to_blocks(queries, per_step), to_blocks(all_kv, per_step))
    )
    log_total = from_blocks(log_total)
    mixed = from_blocks(mixed_heads).reshape(row_count, model_width)
    attn = (
        jnp.dot(mixed, w_proj, preferred_element_type=jnp.float32) + proj_bias.astype(jnp.float32)
    ).reshape(item_count, local_len, model_width)
    resid = inputs + gate_a * attn
    normed2, inverse2 = normalize(resid)
    shifted2 = (
        (normed2 * (1.0 + scale_m) + shift_m).astype(jnp.bfloat16).reshape(row_count, model_width)
    )
    pre = jnp.dot(shifted2, w_fc1, preferred_element_type=jnp.float32) + fc1_bias.astype(
        jnp.float32
    )
    activated, gelu_pull = jax.vjp(gelu_tanh, pre)
    hidden = (activated * channel_on).astype(jnp.bfloat16)
    branch = (
        jnp.dot(hidden, w_fc2, preferred_element_type=jnp.float32) + fc2_bias.astype(jnp.float32)
    ).reshape(item_count, local_len, model_width)
    gated = kept_rows[:, :, None] * gate_m
    output = (resid + gated * branch).astype(jnp.bfloat16)
    incoming = cotangent.astype(jnp.float32)
    d_gate_m = jnp.sum(kept_rows[:, :, None] * branch * incoming, axis=1)
    d_branch = (gated * incoming).astype(jnp.bfloat16).reshape(row_count, model_width)
    grad_w_fc2 = jnp.dot(hidden.T, d_branch, preferred_element_type=jnp.float32)
    grad_fc2_bias = jnp.sum(d_branch.astype(jnp.float32), axis=0)
    d_hidden = jnp.dot(d_branch, w_fc2.T, preferred_element_type=jnp.float32)
    d_pre = gelu_pull(d_hidden * channel_on)[0].astype(jnp.bfloat16)
    grad_w_fc1 = jnp.dot(shifted2.T, d_pre, preferred_element_type=jnp.float32)
    grad_fc1_bias = jnp.sum(d_pre.astype(jnp.float32), axis=0)
    d_shifted2 = jnp.dot(d_pre, w_fc1.T, preferred_element_type=jnp.float32).reshape(
        item_count, local_len, model_width
    )
    d_shift_m = jnp.sum(d_shifted2, axis=1)
    d_scale_m = jnp.sum(d_shifted2 * normed2, axis=1)
    d_resid = incoming + normalize_back(d_shifted2 * (1.0 + scale_m), normed2, inverse2)
    d_gate_a = jnp.sum(attn * d_resid, axis=1)
    d_attn = (gate_a * d_resid).astype(jnp.bfloat16).reshape(row_count, model_width)
    grad_w_proj = jnp.dot(mixed.T, d_attn, preferred_element_type=jnp.float32)
    grad_proj_bias = jnp.sum(d_attn.astype(jnp.float32), axis=0)
    d_mixed = jnp.dot(d_attn, w_proj.T, preferred_element_type=jnp.float32).astype(jnp.bfloat16)
    d_heads = d_mixed.reshape(item_count, local_len, HEADS, head_dim) * head_on[:, None].astype(
        jnp.bfloat16
    )
    again_kv = lax.all_gather(key_value, "tok", axis=1, tiled=True)

    def backward_block(packed):
        query_block, kv_block, head_grads, totals_log = packed
        key_rows, value_rows = split_heads(kv_block, model_width, head_dim)
        scores = scores_of(query_block, key_rows, score_scale)
        probs = jnp.exp(scores - totals_log)
        d_probs = jnp.einsum(
            "nqhe,nkhe->nhqk", head_grads, value_rows, preferred_element_type=jnp.float32
        )
        row_dot = jnp.sum(probs * d_probs, axis=-1, keepdims=True)
        d_scores = (probs * (d_probs - row_dot)).astype(jnp.bfloat16)
        d_queries = (
            jnp.einsum("nhqk,nkhe->nqhe", d_scores, key_rows, preferred_element_type=jnp.float32)
            * score_scale
        )
        return (d_queries, row_dot)

    mapped = lax.map(
        backward_block,
        (
            to_blocks(queries, per_step),
            to_blocks(again_kv, per_step),
            to_blocks(d_heads, per_step),
            to_blocks(log_total, per_step),
        ),
    )
    d_queries = from_blocks(mapped[0])
    row_dot = from_blocks(mapped[1])
    queries_all, head_grads_all = (
        lax.all_gather(queries, "tok", axis=1, tiled=True),
        lax.all_gather(d_heads, "tok", axis=1, tiled=True),
    )
    totals_all, row_dot_all = (
        lax.all_gather(log_total, "tok", axis=2, tiled=True),
        lax.all_gather(row_dot, "tok", axis=2, tiled=True),
    )

    def key_block(packed):
        kv_block, query_block, head_grads, totals_log, dots = packed
        key_rows, value_rows = split_heads(kv_block, model_width, head_dim)
        scores = (
            jnp.einsum("nkhe,nqhe->nhkq", key_rows, query_block, preferred_element_type=jnp.float32)
            * score_scale
        )
        probs = jnp.exp(scores - totals_log[:, :, None, :, 0])
        d_probs = jnp.einsum(
            "nkhe,nqhe->nhkq", value_rows, head_grads, preferred_element_type=jnp.float32
        )
        d_scores = (probs * (d_probs - dots[:, :, None, :, 0])).astype(jnp.bfloat16)
        d_keys = (
            jnp.einsum("nhkq,nqhe->nkhe", d_scores, query_block, preferred_element_type=jnp.float32)
            * score_scale
        )
        d_values = jnp.einsum(
            "nhkq,nqhe->nkhe",
            probs.astype(jnp.bfloat16),
            head_grads,
            preferred_element_type=jnp.float32,
        )
        return jnp.concatenate(
            [
                d_keys.reshape(d_keys.shape[0], local_len, model_width),
                d_values.reshape(d_values.shape[0], local_len, model_width),
            ],
            axis=2,
        )

    d_kv = from_blocks(
        lax.map(
            key_block,
            (
                to_blocks(key_value, per_step),
                to_blocks(queries_all, per_step),
                to_blocks(head_grads_all, per_step),
                to_blocks(totals_all, per_step),
                to_blocks(row_dot_all, per_step),
            ),
        )
    )
    d_qkv = jnp.concatenate([d_queries.reshape(item_count, local_len, model_width), d_kv], axis=2)
    d_qkv = d_qkv.astype(jnp.bfloat16).reshape(row_count, 3 * model_width)
    grad_w_qkv = jnp.dot(shifted.T, d_qkv, preferred_element_type=jnp.float32)
    qkv_sums = jnp.sum(d_qkv.astype(jnp.float32), axis=0)
    grad_q_bias = qkv_sums[:model_width]
    grad_v_bias = qkv_sums[2 * model_width :]
    d_shifted = jnp.dot(d_qkv, w_qkv.T, preferred_element_type=jnp.float32).reshape(
        item_count, local_len, model_width
    )
    d_shift_a = jnp.sum(d_shifted, axis=1)
    d_scale_a = jnp.sum(d_shifted * normed, axis=1)
    grad_tokens = d_resid + normalize_back(d_shifted * (1.0 + scale_a), normed, inverse)
    d_modulation = jnp.concatenate(
        [d_shift_a, d_scale_a, d_gate_a, d_shift_m, d_scale_m, d_gate_m], axis=1
    )
    d_modulation = lax.psum(d_modulation, "tok")
    mod_columns = lax.dynamic_slice_in_dim(d_modulation, tok_index * ada_cols, ada_cols, 1)
    grad_ada_weight = jnp.dot(
        condition.astype(jnp.float32).T, mod_columns, precision=lax.Precision.HIGHEST
    )
    grad_ada_bias = jnp.sum(d_modulation, axis=0)
    bucket_done = (
        lax.psum_scatter(grad_w_qkv, "bucket", scatter_dimension=0, tiled=True),
        lax.psum_scatter(grad_w_proj, "bucket", scatter_dimension=0, tiled=True),
        lax.psum_scatter(grad_w_fc1, "bucket", scatter_dimension=0, tiled=True),
        lax.psum_scatter(grad_w_fc2, "bucket", scatter_dimension=0, tiled=True),
        lax.psum_scatter(grad_q_bias, "bucket", scatter_dimension=0, tiled=True),
        lax.psum_scatter(grad_v_bias, "bucket", scatter_dimension=0, tiled=True),
        lax.psum_scatter(grad_proj_bias, "bucket", scatter_dimension=0, tiled=True),
        lax.psum_scatter(grad_fc1_bias, "bucket", scatter_dimension=0, tiled=True),
        lax.psum_scatter(grad_fc2_bias, "bucket", scatter_dimension=0, tiled=True),
        lax.psum_scatter(grad_ada_weight, "bucket", scatter_dimension=0, tiled=True),
        lax.psum_scatter(grad_ada_bias, "bucket", scatter_dimension=0, tiled=True),
    )
    token_done = (
        lax.psum_scatter(bucket_done[0], "tok", scatter_dimension=1, tiled=True),
        lax.psum_scatter(bucket_done[1], "tok", scatter_dimension=1, tiled=True),
        lax.psum_scatter(bucket_done[2], "tok", scatter_dimension=1, tiled=True),
        lax.psum_scatter(bucket_done[3], "tok", scatter_dimension=1, tiled=True),
        lax.psum_scatter(bucket_done[4].reshape(1, -1), "tok", scatter_dimension=1, tiled=True),
        lax.psum_scatter(bucket_done[5].reshape(1, -1), "tok", scatter_dimension=1, tiled=True),
        lax.psum_scatter(bucket_done[6].reshape(1, -1), "tok", scatter_dimension=1, tiled=True),
        lax.psum_scatter(bucket_done[7].reshape(1, -1), "tok", scatter_dimension=1, tiled=True),
        lax.psum_scatter(bucket_done[8].reshape(1, -1), "tok", scatter_dimension=1, tiled=True),
    )
    finished = (
        token_done[0],
        token_done[1],
        token_done[2],
        token_done[3],
        token_done[4],
        token_done[5],
        token_done[6],
        token_done[7],
        token_done[8],
        bucket_done[9],
        bucket_done[10],
    )
    return (
        output,
        grad_tokens,
        finished[0],
        finished[4].reshape(-1),
        finished[5].reshape(-1),
        finished[1],
        finished[6].reshape(-1),
        finished[2],
        finished[7].reshape(-1),
        finished[3],
        finished[8].reshape(-1),
        finished[9],
        finished[10],
    )


def solution(mesh):
    planned = mesh.shape["tok"] == 4 and mesh.shape["bucket"] == 8
    return jax.shard_map(
        one_item_per_chip if planned else on_device,
        mesh=mesh,
        in_specs=(
            P("bucket", "tok", None),
            P("bucket", "tok", None),
            P("bucket"),
            P("bucket"),
            P(),
            P(),
            P("bucket", None),
            P(),
            P(),
            P(),
            P(),
            P(),
            P(),
            P(),
            P(),
            P(),
            P(None, "tok"),
            P("tok"),
        ),
        out_specs=(
            P("bucket", "tok", None),
            P("bucket", "tok", None),
            P("bucket", "tok"),
            P(("bucket", "tok")),
            P(("bucket", "tok")),
            P("bucket", "tok"),
            P(("bucket", "tok")),
            P("bucket", "tok"),
            P(("bucket", "tok")),
            P("bucket", "tok"),
            P(("bucket", "tok")),
            P("bucket", "tok"),
            P("bucket"),
        ),
        check_vma=False,
    )
```

```python
import functools
import math

import jax
import jax.numpy as jnp
import numpy as np
from jax import lax
from jax.experimental import pallas as pl
from jax.experimental.pallas import tpu as pltpu
from jax.sharding import PartitionSpec as P

HEADS = 16
EPSILON = 1e-06
LOG2E = 1.4426950408889634
GELU_K = math.sqrt(2.0 / math.pi)
GELU_C = 0.044715
LANES = 128
bf16, f32 = jnp.bfloat16, jnp.float32


def dot_nn(a, b):
    return lax.dot_general(a, b, (((1,), (0,)), ((), ())), preferred_element_type=f32)


def dot_nt(a, b):
    return lax.dot_general(a, b, (((1,), (1,)), ((), ())), preferred_element_type=f32)


def dot_tn(a, b):
    return lax.dot_general(a, b, (((0,), (0,)), ((), ())), preferred_element_type=f32)


def step_embedding(timesteps, model_width):
    half_width = model_width // 2
    frequency = jnp.exp(-math.log(10000.0) * jnp.arange(half_width, dtype=jnp.float32) / half_width)
    angles = timesteps.astype(jnp.float32)[:, None] * frequency[None, :]
    return jnp.concatenate([jnp.cos(angles), jnp.sin(angles)], axis=1)


def normalize(values):
    centred = values - jnp.mean(values, axis=-1, keepdims=True)
    inverse = lax.rsqrt(jnp.mean(centred * centred, axis=-1, keepdims=True) + EPSILON)
    return (centred * inverse, inverse)


def normalize_back(incoming, normed, inverse):
    return inverse * (
        incoming
        - jnp.mean(incoming, axis=-1, keepdims=True)
        - normed * jnp.mean(incoming * normed, axis=-1, keepdims=True)
    )


D = 1152
DC, DZ, TD = D // 8, D // 4, D // 4
HD = D // HEADS
HC = HEADS // 2
WC = D // 2
FF = 4608
NF = 3
FB = FF // 2 // NF
FZ = FB // 4
L = 1024
LH = L // 2
LB = L // 4
G1R = 3 * DC
G2R = 2 * FZ + FZ // 4
PR = 2 * DC + DC // 3
PA = 176
WQ = 3 * WC // 2
TQ = WQ // 4
QR = 512
QA = QR // 2
VMEM_LIMIT = 58 * 1024 * 1024


ANY = pl.BlockSpec(memory_space=pl.ANY)
MESH = pl.DeviceIdType.MESH


def place():
    b, t = lax.axis_index("bucket"), lax.axis_index("tok")
    return b // 2, b % 2, t // 2, t % 2


def flip(value, other):
    return (value // 2 + other // 2) % 2 * 2 + (value % 2 + other % 2) % 2


def peer(name):
    z, c, y, x = place()
    if name == "x":
        x = 1 - x
    elif name == "y":
        y = 1 - y
    elif name == "xy":
        x, y = 1 - x, 1 - y
    elif name == "c":
        c = 1 - c
    elif name in ("t0", "t1"):
        c, y, x = y, c, x if name == "t0" else 1 - x
    else:
        z = flip(z, int(name[1]))
    return (z * 2 + c, y * 2 + x)


def greet(names):
    sem = pltpu.get_barrier_semaphore()
    for name in names:
        if name == "t0":
            continue
        pl.semaphore_signal(sem, inc=1, device_id=peer(name), device_id_type=MESH)
    if "t0" in names:
        _, c, y, _ = place()

        @pl.when(c != y)
        def _():
            pl.semaphore_signal(sem, inc=1, device_id=peer("t0"), device_id_type=MESH)


def meet(names):
    wanted = len([name for name in names if name != "t0"])
    if "t0" in names:
        _, c, y, _ = place()
        wanted = wanted + (c + y) % 2
    pl.semaphore_wait(pltpu.get_barrier_semaphore(), wanted)


def remote(src, dst, sems, k, name):
    return pltpu.make_async_remote_copy(
        src_ref=src, dst_ref=dst, send_sem=sems.at[0, k], recv_sem=sems.at[1, k],
        device_id=peer(name), device_id_type=MESH,
    )


def vm(*shape, dtype=bf16):
    return pltpu.VMEM(shape, dtype)


class FirstSum:
    peers = ("x", "y")

    def __init__(self, keep_a, sent_a, keep_b, sent_b):
        self.ins = [keep_a, sent_a, keep_b, sent_b]
        shapes = [keep.shape[1:] for keep in (keep_a, keep_b)]
        self.outs = [jax.ShapeDtypeStruct(s, bf16) for s in shapes for _ in range(2)]
        self.scratch = [vm(*s) for s in shapes for _ in range(3)]
        self.scratch += [pltpu.SemaphoreType.DMA((2, 4)), pltpu.SemaphoreType.DMA((4,))]

    def plan(self, ins, outs, scratch):
        ka, sa, kb, sb = ins
        _, qa, _, qb = outs
        kav, rav, _, kbv, rbv, _, sems, local = scratch
        far = [
            remote(sa.at[1], rav, sems, 0, "x"),
            remote(sb.at[1], rbv, sems, 1, "y"),
            remote(sa.at[0], qa, sems, 2, "x"),
            remote(sb.at[0], qb, sems, 3, "y"),
        ]
        near = [
            pltpu.make_async_copy(ka.at[1], kav, local.at[0]),
            pltpu.make_async_copy(kb.at[1], kbv, local.at[1]),
        ]
        return far, near

    def finish(self, ins, outs, scratch):
        kav, rav, oav, kbv, rbv, obv, _, local = scratch
        oav[...] = (kav[...].astype(f32) + rav[...].astype(f32)).astype(bf16)
        obv[...] = (kbv[...].astype(f32) + rbv[...].astype(f32)).astype(bf16)
        return [
            pltpu.make_async_copy(oav, outs[0], local.at[2]),
            pltpu.make_async_copy(obv, outs[2], local.at[3]),
        ]


class SecondSum:
    peers = ("x", "y")

    def __init__(self, on_a, q_a, on_b, q_b, keep_a, keep_b):
        self.ins = [on_a, q_a, on_b, q_b, keep_a, keep_b]
        self.rows = [on_a.shape[1], on_b.shape[1]]
        total = sum(self.rows)
        self.outs = [jax.ShapeDtypeStruct((3, total, LANES), bf16), jax.ShapeDtypeStruct((total, LANES), f32)]
        self.scratch = [vm(4, r, LANES) for r in self.rows for _ in range(3)]
        self.scratch += [vm(3, total, LANES), vm(total, LANES, dtype=f32)]
        self.scratch += [pltpu.SemaphoreType.DMA((2, 2)), pltpu.SemaphoreType.DMA((6,))]

    def plan(self, ins, outs, scratch):
        oa, qa, ob, qb, ka, kb = ins
        kav, qav, rav, kbv, qbv, rbv, _, _, sems, local = scratch
        far = [remote(oa, rav, sems, 0, "y"), remote(ob, rbv, sems, 1, "x")]
        whole = len(ka.shape) == 4
        pairs = [(ka.at[0] if whole else ka, kav), (qa, qav), (kb.at[0] if whole else kb, kbv), (qb, qbv)]
        return far, [pltpu.make_async_copy(a, b, local.at[k]) for k, (a, b) in enumerate(pairs)]

    def finish(self, ins, outs, scratch):
        zs, zk, local = scratch[6], scratch[7], scratch[9]
        layer_sums([scratch[0:3], scratch[3:6]], zs, zk)
        return [
            pltpu.make_async_copy(zs, outs[0], local.at[4]),
            pltpu.make_async_copy(zk, outs[1], local.at[5]),
        ]


class ThirdSum:
    peers = ("z1", "z2", "z3")

    def __init__(self, sent, kept):
        self.ins = [sent, kept]
        self.outs = [jax.ShapeDtypeStruct(kept.shape, f32)]
        self.scratch = [vm(*sent.shape), vm(*kept.shape, dtype=f32)]
        self.scratch += [pltpu.SemaphoreType.DMA((2, 3)), pltpu.SemaphoreType.DMA((2,))]

    def plan(self, ins, outs, scratch):
        got, kept, sems, local = scratch
        far = [remote(ins[0].at[k], got.at[k], sems, k, f"z{k + 1}") for k in (2, 1, 0)]
        return far, [pltpu.make_async_copy(ins[1], kept, local.at[0])]

    def finish(self, ins, outs, scratch):
        got, kept, _, local = scratch
        kept[...] = kept[...] + got[0].astype(f32) + got[1].astype(f32) + got[2].astype(f32)
        return [pltpu.make_async_copy(kept, outs[0], local.at[1])]


def layer_sums(streams, zs, zk):
    start = 0
    for kv, qv, rv in streams:
        rows_ = rv.shape[1]
        for j in range(4):
            total = kv[j].astype(f32) + qv[j].astype(f32) + rv[j].astype(f32)
            if j == 0:
                zk[start : start + rows_, :] = total
            else:
                zs[j - 1, start : start + rows_, :] = total.astype(bf16)
        start += rows_


class SecondThird(SecondSum):
    peers = ("x", "y", "z1", "z2", "z3")

    def __init__(self, *args, start_at=0, tick_at=1):
        super().__init__(*args)
        self.start_at, self.tick_at = start_at, tick_at
        total = sum(self.rows)
        self.outs = [jax.ShapeDtypeStruct((total, LANES), f32)]
        self.scratch += [vm(3, total, LANES), pltpu.SemaphoreType.DMA((2, 3))]

    def third(self, scratch):
        zs, got, sems = scratch[6], scratch[10], scratch[11]
        return [remote(zs.at[k], got.at[k], sems, k, f"z{k + 1}") for k in (2, 1, 0)]

    def tick(self, ins, outs, scratch):
        for group in super().plan(ins, outs, scratch[:10]):
            for copy in group:
                copy.wait()
        layer_sums([scratch[0:3], scratch[3:6]], scratch[6], scratch[7])
        for copy in self.third(scratch):
            copy.start()

    def plan(self, ins, outs, scratch):
        return super().plan(ins, outs, scratch[:10])

    def settle(self, ins, outs, scratch):
        return self.third(scratch)

    def finish(self, ins, outs, scratch):
        kept, local, got = scratch[7], scratch[9], scratch[10]
        kept[...] = kept[...] + got[0].astype(f32) + got[1].astype(f32) + got[2].astype(f32)
        return [pltpu.make_async_copy(kept, outs[0], local.at[5])]


class FirstSecond:
    peers = ("x", "y")

    def __init__(self, keep_a, sent_a, keep_b, sent_b, start_at=0, tick_at=1):
        self.start_at, self.tick_at = start_at, tick_at
        self.ins = [keep_a, sent_a, keep_b, sent_b]
        self.rows = [keep_a.shape[2], keep_b.shape[2]]
        total = sum(self.rows)
        self.outs = [jax.ShapeDtypeStruct((3, total, LANES), bf16), jax.ShapeDtypeStruct((total, LANES), f32)]
        self.scratch = []
        for r in self.rows:
            self.scratch += [vm(2, 4, r, LANES), vm(2, 4, r, LANES), vm(4, r, LANES), vm(4, r, LANES)]
        self.scratch += [vm(3, total, LANES), vm(total, LANES, dtype=f32)]
        self.scratch += [pltpu.SemaphoreType.DMA((2, 6)), pltpu.SemaphoreType.DMA((4,))]

    def plan(self, ins, outs, scratch):
        ka, sa, kb, sb = ins
        sems, local = scratch[10:]
        far = [
            remote(sa.at[1], scratch[1].at[1], sems, 0, "x"),
            remote(sb.at[1], scratch[5].at[1], sems, 1, "y"),
            remote(sa.at[0], scratch[1].at[0], sems, 2, "x"),
            remote(sb.at[0], scratch[5].at[0], sems, 3, "y"),
        ]
        near = [pltpu.make_async_copy(k, scratch[4 * j], local.at[j]) for j, k in enumerate((ka, kb))]
        return far, near

    def second(self, scratch):
        sems = scratch[10]
        return [remote(scratch[4 * j + 2], scratch[4 * j + 3], sems, 4 + j, name) for j, name in enumerate("yx")]

    def tick(self, ins, outs, scratch):
        for group in self.plan(ins, outs, scratch):
            for copy in group:
                copy.wait()
        for j in range(2):
            kv, rv, on = scratch[4 * j : 4 * j + 3]
            on[...] = (kv[1].astype(f32) + rv[1].astype(f32)).astype(bf16)
        for copy in self.second(scratch):
            copy.start()

    def settle(self, ins, outs, scratch):
        return self.second(scratch)

    def finish(self, ins, outs, scratch):
        zs, zk, local = scratch[8], scratch[9], scratch[11]
        layer_sums([(scratch[j].at[0], scratch[j + 1].at[0], scratch[j + 3]) for j in (0, 4)], zs, zk)
        return [
            pltpu.make_async_copy(zs, outs[0], local.at[2]),
            pltpu.make_async_copy(zk, outs[1], local.at[3]),
        ]


class GoHome:
    peers = ("t0", "t1")

    def __init__(self, values, tick_at=1):
        self.tick_at = tick_at
        self.ins = [values]
        self.outs = [jax.ShapeDtypeStruct((2, LB, D), values.dtype)]
        self.scratch = [pltpu.SemaphoreType.DMA((2, 2)), pltpu.SemaphoreType.DMA]

    def plan(self, ins, outs, scratch):
        return [], []

    def tick(self, ins, outs, scratch):
        home_start(*self.copies(ins, outs, scratch))

    def copies(self, ins, outs, scratch):
        return homeward(ins[0].at[pl.ds(0, LB)], ins[0].at[pl.ds(LB, LB)], outs[0], *scratch)

    def settle(self, ins, outs, scratch):
        home_wait(*self.copies(ins, outs, scratch))
        return []

    def finish(self, ins, outs, scratch):
        return []


def homeward(first, second, dst, sems, local):
    x = place()[3]
    return (
        remote(first, dst.at[x], sems, 0, "t0"),
        pltpu.make_async_copy(first, dst.at[x], local),
        remote(second, dst.at[x], sems, 1, "t1"),
    )


def home_start(away, stay, second):
    _, c, y, _ = place()
    pl.when(c != y)(away.start)
    pl.when(c == y)(stay.start)
    second.start()


def home_wait(away, stay, second):
    _, c, y, _ = place()
    pl.when(c != y)(away.wait)
    pl.when(c == y)(stay.wait)
    second.wait()


def call(kernel, name, out_shape, args, in_specs=None, out_specs=None, scratch=(), grid=None,
         peers=(), jobs=(), cid=None, ticks=False, flops=0, nbytes=0):
    whole = pl.BlockSpec(memory_space=pltpu.VMEM)
    single = not isinstance(out_shape, (tuple, list))
    out_shape = [out_shape] if single else list(out_shape)
    in_specs = list(in_specs) if in_specs is not None else [whole] * len(args)
    out_specs = [whole] * len(out_shape) if out_specs is None else [out_specs] if single else list(out_specs)
    counts = [len(args), sum(len(j.ins) for j in jobs), len(out_shape), sum(len(j.outs) for j in jobs), len(scratch)]
    names = sorted(set(peers).union(*[j.peers for j in jobs]))

    def run(*refs):
        groups, at = [], 0
        for n in counts:
            groups.append(refs[at : at + n])
            at += n
        bound, ai, ao, asc = [], 0, 0, at
        for j in jobs:
            bound.append((
                j, groups[1][ai : ai + len(j.ins)], groups[3][ao : ao + len(j.outs)], refs[asc : asc + len(j.scratch)]
            ))
            ai, ao, asc = ai + len(j.ins), ao + len(j.outs), asc + len(j.scratch)

        def ready():
            if names:
                meet(names)
            for j, *r in bound:
                if not getattr(j, "start_at", 0):
                    j_start(j, r)

        def j_start(j, r):
            for group in j.plan(*r):
                for copy in group:
                    copy.start()

        def tick(k):
            for j, *r in bound:
                if getattr(j, "tick_at", 0) == k:
                    j.tick(*r)
            for j, *r in bound:
                if getattr(j, "start_at", 0) == k:
                    j_start(j, r)

        def end():
            last = []
            for j, *r in bound:
                far, near = (j.settle(*r), []) if hasattr(j, "tick") else j.plan(*r)
                for copy in far:
                    copy.wait()
                for copy in near:
                    copy.wait()
                copies = j.finish(*r)
                for copy in copies:
                    copy.start()
                last += copies
            for copy in last:
                copy.wait()

        if names:
            greet(names)
            kernel(*groups[0], *groups[2], *groups[4], ready=ready, **({"tick": tick} if ticks else {}))
            end()
        else:
            kernel(*groups[0], *groups[2], *groups[4])

    extra = {} if grid is None else {"grid": grid}
    params = {"collective_id": cid, "has_side_effects": True} if names else {}
    outs = pl.pallas_call(
        run,
        out_shape=out_shape + [o for j in jobs for o in j.outs],
        in_specs=in_specs + [ANY] * counts[1],
        out_specs=out_specs + [ANY] * counts[3],
        scratch_shapes=list(scratch) + [q for j in jobs for q in j.scratch],
        compiler_params=pltpu.CompilerParams(vmem_limit_bytes=VMEM_LIMIT, **params),
        cost_estimate=pl.CostEstimate(flops=int(flops), bytes_accessed=int(nbytes), transcendentals=0),
        name=name,
        **extra,
    )(*args, *[a for j in jobs for a in j.ins])
    own, rest, given = outs[: len(out_shape)], outs[len(out_shape) :], []
    for j in jobs:
        given.append(rest[: len(j.outs)])
        rest = rest[len(j.outs) :]
    return (own[0] if single else own), given


def full(shape):
    return pl.BlockSpec(shape, lambda *_: (0,) * len(shape))


def once(*shape):
    return pl.BlockSpec(shape, lambda *_: (0,) * len(shape), pipeline_mode=pl.Buffered(1))


def rows(block, width):
    return pl.BlockSpec((block, width), lambda i: (i, 0))


def arrivals(src, dst, tsems, csems, locals_, pieces=1):
    x = place()[3]
    n = LB // pieces
    moves = []
    for k in range(pieces):
        rows_ = pl.ds(n * k, n)
        here = [dst.at[pl.ds(LB * j + n * k, n)] for j in range(4)]
        moves.append((
            remote(src.at[x, rows_], here[0], tsems, 2 * k, "t0"),
            pltpu.make_async_copy(src.at[x, rows_], here[0], locals_.at[k]),
            remote(src.at[1 - x, rows_], here[1], tsems, 2 * k + 1, "t1"),
            [remote(here[j], here[2 + j], csems, 2 * k + j, "c") for j in range(2)],
        ))
    return moves


def leave(first, stay, second, onward):
    _, c, y, _ = place()
    pl.when(c != y)(first.start)
    pl.when(c == y)(stay.start)
    second.start()


def pass_on(first, stay, second, onward):
    _, c, y, _ = place()
    pl.when(c != y)(first.wait_recv)
    pl.when(c == y)(stay.wait)
    onward[0].start()
    second.wait_recv()
    onward[1].start()


def settle(first, stay, second, onward):
    _, c, y, _ = place()
    pl.when(c != y)(first.wait_send)
    second.wait_send()
    for copy in onward:
        copy.wait_send()


def column(n):
    return lax.broadcasted_iota(jnp.int32, (n, 1), 0)


def front_kernel(tokens, timesteps, bucket_ids, skips, ada_w, ada_b, head_masks, channel_masks, w_qkv, w_fc1,
                 q_bias, v_bias, b1, freq, tok_o, shifted_o, qkv_o, wq_o, w1_o, mod_o, kept_o, hmask_o, chan_o, b1_o,
                 tk, wqv, wqc, w1v, w1c, adav, ints, ints_other, m4, to_send, shares, shv, qkvv, csems, tsems, ssems, lsems, ready):
    z, c, y, x = place()
    t = 2 * y + x
    loads = [
        pltpu.make_async_copy(a, b, lsems.at[k])
        for k, (a, b) in enumerate(((ada_w, adav), (w_qkv, wqv), (w_fc1, w1v)))
    ]

    pieces = 2
    tok_moves = arrivals(tokens, tk, tsems, csems, lsems.at[pl.ds(6, pieces)], pieces)
    ready()
    for moves in tok_moves:
        leave(*moves)
    halves = [skips[:, :LANES], skips[:, LANES:]]
    ints[0:4, :] = jnp.concatenate([halves[0][0:1], halves[1][0:1], halves[0][1:2], halves[1][1:2]], axis=0)
    for k, value in enumerate((timesteps[0], timesteps[1], bucket_ids[0], 0)):
        ints[4 + k : 5 + k, :] = jnp.full((1, LANES), value, jnp.int32)
    swap = remote(ints, ints_other, csems, 2 * pieces, "c")
    swap.start()
    for load in loads:
        load.start()
    swap.wait()

    mine, other = ints[...], ints_other[...]
    r = column(8)
    steps = jnp.zeros((8, 1), f32)
    for k in range(2):
        steps = jnp.where(r == 2 * c + k, mine[4 + k : 5 + k, 0:1].astype(f32), steps)
        steps = jnp.where(r == 2 * (1 - c) + k, other[4 + k : 5 + k, 0:1].astype(f32), steps)
    angles = steps * freq[...]
    condition = jax.nn.silu(jnp.concatenate([jnp.cos(angles), jnp.sin(angles)], axis=1))
    condition = jnp.concatenate([condition, jnp.zeros_like(condition)], axis=0).astype(bf16)
    loads[0].wait()
    m4[...] = dot_nt(condition, adav[...])[:8] + ada_b[...].astype(f32).reshape(1, -1)
    moves = []
    for k in range(4):
        to = (y + k // 2) % 2 * 2 + (x + k) % 2
        row = jnp.broadcast_to(m4[pl.ds(to, 1), :], to_send.shape[1:])
        if k == 0:
            shares[t] = row
        else:
            to_send[k - 1] = row
            moves.append(remote(to_send.at[k - 1], shares.at[t], ssems, k - 1, ("x", "y", "xy")[k - 1]))
            moves[-1].start()

    group = jnp.where(c == y, mine, other)
    bucket = group[6:7, 0:1]
    skip = jnp.where(x == 0, group[0:2], group[2:4])
    for j in range(4):
        block = 2 * ((c + j // 2) % 2) + (x + j) % 2
        position = column(LB) + LB * block
        hit = jnp.where((position == skip[0:1, :]) | (position == skip[1:2, :]), 1.0, 0.0)
        kept_o[LB * j : LB * (j + 1), :] = 1.0 - jnp.max(hit, axis=1, keepdims=True)

    def chosen(masks):
        line = lax.broadcasted_iota(jnp.int32, masks.shape, 0)
        row = jnp.sum(jnp.where(line == bucket, masks[...].astype(f32), 0.0), axis=0, keepdims=True)
        return jnp.broadcast_to(row, (16, masks.shape[1])).astype(bf16)

    def spread(on, low, width):
        first = width * lax.broadcasted_iota(jnp.int32, (on.shape[1], low.shape[1]), 0)
        return dot_nn(on, jnp.where((low >= first) & (low < first + width), 1.0, 0.0).astype(bf16))[0:1, :]

    lane = lax.broadcasted_iota(jnp.int32, (1, WC), 1)
    share = sum(jnp.where(lane >= DC * k, 1, 0) for k in range(1, 4))
    hmask_o[...] = spread(chosen(head_masks), lane + DC * (share + c), HD)
    channels = chosen(channel_masks)
    lane = lax.broadcasted_iota(jnp.int32, (1, FB), 1)
    share = sum(jnp.where(lane >= FZ * k, 1, 0) for k in range(1, 4))
    for f in range(NF):
        low = lane + (4 * DZ - FZ) * share + FF // 8 * c + FZ * f
        chan_o[f] = spread(channels, low, FF // channels.shape[1])

    def half(v, k, width):
        v = v[:, 2 * width * k : 2 * width * (k + 1)]
        return jnp.where(c == 0, v[:, :width], v[:, width:])

    def line(ref):
        return ref[...].astype(f32).reshape(1, -1)

    def parity(v, odd):
        return [half(v, k, DC)[:, HD * odd : HD * (odd + 1)] for k in range(4)]

    bias = []
    for odd in range(2):
        bias += parity(line(q_bias), odd) + [jnp.zeros((1, DZ), f32)] + parity(line(v_bias), odd)
    bias = jnp.concatenate(bias, axis=1)
    b1v = [half(line(b1), k, FF // 8) for k in range(4)]
    for f in range(NF):
        b1_o[f] = jnp.concatenate([v[:, FZ * f : FZ * (f + 1)] for v in b1v], axis=1)
    loads[1].wait()
    loads[2].wait()
    for core in range(2):

        @pl.when(c == core)
        def _():
            for odd in range(2):
                for k in range(12):
                    to, start = WQ * odd + HD * k, DZ * k + DC * core + HD * odd
                    wqc[:, to : to + HD] = wqv[:, start : start + HD]
            for f in range(NF):
                for k in range(4):
                    start = 4 * DZ * k + FF // 8 * core + FZ * f
                    w1c[f, :, FZ * k : FZ * (k + 1)] = w1v[:, start : start + FZ]

    stores = [
        pltpu.make_async_copy(a, b, lsems.at[k]) for k, (a, b) in enumerate(((wqc, wq_o), (w1c, w1_o)))
    ]
    for store in stores:
        store.start()
    for copy in moves:
        copy.wait()
    share_rows = [shares[k][0:1, :] for k in range(4)]
    n, m = D // 2, 3 * D // 2
    mod = [share_rows[0][:, :D], jnp.concatenate([share_rows[0][:, D:], share_rows[1][:, :n]], axis=1),
           share_rows[1][:, n:], share_rows[2][:, :D],
           jnp.concatenate([share_rows[2][:, D:], share_rows[3][:, :n]], axis=1), share_rows[3][:, n:]]
    own_step = 0.5 * jnp.sum(jnp.where(r == t, steps, 0.0), axis=0, keepdims=True)
    mod += [jnp.broadcast_to(own_step, (1, D)), jnp.zeros((1, D), f32)]
    mod_o[...] = jnp.concatenate(mod, axis=0)
    n = LB // pieces

    def make(side, k):
        parts = [slice(LH * side + LB * j + n * k, LH * side + LB * j + n * (k + 1)) for j in range(2)]
        normed, _ = normalize(jnp.concatenate([tk[part, :] for part in parts], axis=0).astype(f32))
        shifted = (normed * (1.0 + mod[1]) + mod[0]).astype(bf16)
        made = (dot_nn(shifted, wqc[...]) + bias).astype(bf16)
        for j, part in enumerate(parts):
            shv[part, :] = shifted[n * j : n * (j + 1)]
            qkvv[part, :] = made[n * j : n * (j + 1)]

    kept_rows = []

    def keep_half(side):
        part = pl.ds(LH * side, LH)
        for k, (a, b) in enumerate(((shv, shifted_o), (qkvv, qkv_o), (tk, tok_o))):
            copy = pltpu.make_async_copy(a.at[part], b.at[part], ssems.at[side, 3 + k])
            copy.start()
            kept_rows.append(copy)

    for k in range(pieces):
        pass_on(*tok_moves[k])
        make(0, k)
    keep_half(0)
    for k in range(pieces):
        for copy in tok_moves[k][3]:
            copy.wait_recv()
        make(1, k)
    keep_half(1)
    for one in tok_moves:
        settle(*one)
    for copy in stores + kept_rows:
        copy.wait()


def attn_kernel(step, cotangent, qkv, hmask, wp, bias, tok, mod, cot_o, mixed_o, shifted2_o, attn_o,
                ck, qkvv, qh, kh, vh, mx, mo, wpv, tkv, csems, tsems, osems, lsems, ready):
    c = place()[1]
    loads = [
        pltpu.make_async_copy(wp.at[:, c], wpv.at[0], lsems.at[0]),
        pltpu.make_async_copy(wp.at[:, 1 - c], wpv.at[1], lsems.at[1]),
        pltpu.make_async_copy(tok, tkv, lsems.at[2]),
        pltpu.make_async_copy(qkv, qkvv, lsems.at[4]),
    ]
    for load in loads[::-1]:
        load.start()
    cot_moves = arrivals(cotangent, ck, tsems, osems, lsems.at[pl.ds(5, 1)])[0]
    scale = LOG2E / math.sqrt(HD)
    loads.pop().wait()
    for h in range(HC):
        for k, ref in enumerate((qh, kh, vh)):
            start = WQ * (h % 2) + DZ * k + HD * (h // 2)
            ref[h, :, :HD] = qkvv[:, start : start + HD]
        vh[h, :, HD:] = jnp.ones((L, LANES - HD), bf16)
    ready()
    leave(*cot_moves)

    def crossing(i):
        src = mx.at[pl.ds(pl.multiple_of(i * step, step), step)]
        dst = mo.at[pl.ds(pl.multiple_of((i * step + LH) % L, step), step)]
        return remote(src, dst, csems, i, "c")

    def body(i, carry):
        part = pl.ds(pl.multiple_of(i * step, step), step)
        outs = []
        for h in range(HC):
            s = dot_nt(qh[h, part, :], kh[h])
            top = jnp.max(s, axis=1, keepdims=True)
            p = jnp.exp2((s - top) * scale)
            o = dot_nn(p.astype(bf16), vh[h])
            outs.append(o[:, :HD] * (1.0 / o[:, HD : HD + 1]))
        mx[part, :] = (jnp.concatenate(outs, axis=1) * hmask[...]).astype(bf16)
        crossing(i).start()
        return carry

    lax.fori_loop(0, L // step, body, 0)
    keep = pltpu.make_async_copy(mx, mixed_o, lsems.at[3])
    keep.start()
    pass_on(*cot_moves)
    for load in loads:
        load.wait()
    for i in range(L // step):
        crossing(i).wait()
    w_mine, w_other = wpv[0].reshape(WC, D), wpv[1].reshape(WC, D)
    bias_line = bias[...].astype(f32).reshape(1, D)
    for j in range(4):
        part = slice(LB * j, LB * (j + 1))
        attn = dot_nn(mx[part, :], w_mine) + dot_nn(mo[part, :], w_other) + bias_line
        if j < 2:
            attn_o[part, :] = attn
        normed, _ = normalize(tkv[part, :].astype(f32) + mod[2:3, :] * attn)
        shifted2_o[part, :] = (normed * (1.0 + mod[4:5, :]) + mod[3:4, :]).astype(bf16)
    for copy in cot_moves[3]:
        copy.wait_recv()
    keep_cot = pltpu.make_async_copy(ck, cot_o, lsems.at[6])
    keep_cot.start()
    settle(*cot_moves)
    keep.wait()
    keep_cot.wait()


def mlp_kernel(sh2, g, kept, mod, w1, b1, chan, w2,
               on_a0, q_a0, on_b0, q_b0, keep_a0, keep_b0, on_a1, q_a1, on_b1, q_b1, keep_a1, keep_b1,
               k2a, s2a, k2b, s2b, branch_o, ds2_o, branch_r, ds2_r, sum1_o, sum2_o,
               sh2v, dbs, w1v, w2v, hid, dpre, slope, br, ds, far, tt_, ka, sa, kb, sb, ra, rb, ona, onb,
               fsems, csems, lsems, wsems, osems, ready):
    z, c, y, x = place()
    out0 = (on_a0, q_a0, on_b0, q_b0, keep_a0, keep_b0)
    out1 = (on_a1, q_a1, on_b1, q_b1, keep_a1, keep_b1)
    outs = (out0, out1)

    def weights(f):
        return [
            pltpu.make_async_copy(w1.at[f], w1v.at[f % 2], wsems.at[0, f % 2]),
            pltpu.make_async_copy(w2.at[:, c, f], w2v.at[f % 2], wsems.at[1, f % 2]),
        ]

    def first(f):
        k, out = f % 2, outs[f]
        return [
            remote(sa.at[k, 1], ra.at[k], fsems, 4 * k, "x"), remote(sb.at[k, 1], rb.at[k], fsems, 4 * k + 1, "y"),
            remote(sa.at[k, 0], out[1], fsems, 4 * k + 2, "x"), remote(sb.at[k, 0], out[3], fsems, 4 * k + 3, "y"),
        ]

    def stored(f):
        k = f % 2
        if f == NF - 1:
            pairs = ((ka.at[k], k2a), (sa.at[k], s2a), (kb.at[k], k2b), (sb.at[k], s2b))
        else:
            pairs = ((ka.at[k, 0], outs[f][4]), (kb.at[k, 0], outs[f][5]))
        return [pltpu.make_async_copy(src, dst, osems.at[k, j]) for j, (src, dst) in enumerate(pairs)]

    def onward(f):
        k = f % 2
        for copy in first(f):
            copy.wait()
        for kv, rv, on in ((ka, ra, ona), (kb, rb, onb)):
            on[k] = (kv[k, 1].astype(f32) + rv[k].astype(f32)).astype(bf16)
        copies = [
            pltpu.make_async_copy(src.at[k], dst, osems.at[k, 4 + j])
            for j, (src, dst) in enumerate(((ona, outs[f][0]), (onb, outs[f][2])))
        ]
        for copy in copies:
            copy.start()
        return copies

    loads = [pltpu.make_async_copy(src, dst, lsems.at[k]) for k, (src, dst) in enumerate(((g, dbs), (sh2, sh2v)))]
    for copy in loads + weights(0):
        copy.start()
    loads[0].wait()
    sum2 = jnp.zeros((1, D), f32)
    for j in range(4):
        part = slice(LB * j, LB * (j + 1))
        db = (dbs[part, :].astype(f32) * mod[5:6, :] * kept[part, :]).astype(bf16)
        dbs[part, :] = db
        sum2 += jnp.sum(db.astype(f32), axis=0, keepdims=True)
    sum2_o[...] = sum2
    loads[1].wait()
    crossing = [remote(far.at[j], dst, csems, j, "c") for j, dst in enumerate((branch_r, ds2_r))]
    waiting = []
    for f in range(NF):
        for copy in weights(f):
            copy.wait()
        if f + 1 < NF:
            for copy in weights(f + 1):
                copy.start()
        w1f, w2f = w1v[f % 2], w2v[f % 2].reshape(FB, D)
        on = chan[f]
        k = f % 2
        for side in (1, 0):
            part = slice(LH * side, LH * (side + 1))
            v = dot_nn(sh2v[part, :], w1f) + b1[f]
            v2 = v * v
            th = jnp.tanh(GELU_K * v * (1.0 + GELU_C * v2))
            half = 0.5 * (1.0 + th)
            hid[part, :] = (v * half * on).astype(bf16)
            slope[part, :] = (
                (half + (0.5 * GELU_K) * v * (1.0 - th * th) * (1.0 + (3.0 * GELU_C) * v2)) * on
            ).astype(bf16)
        for m in range(2):
            cut = slice(m * FB // 2, (m + 1) * FB // 2)
            p = dot_tn(hid[:, cut], dbs[...]).astype(bf16)
            for t in range(4):
                tt_[t, cut, :] = p[:, TD * t : TD * (t + 1)]
        for rz in range(4):
            zz = flip(z, rz)
            for ry in range(2):
                for rx in range(2):
                    tt = (ry + y) % 2 * 2 + (rx + x) % 2
                    o = (kb, sb)[ry]
                    block = tt_[tt, pl.ds(pl.multiple_of(zz * FZ, 16), FZ), :]
                    o[k, rx, rz, :FZ, :] = block[:, :LANES]
                    o[k, rx, rz, FZ : 2 * FZ, :] = block[:, LANES : 2 * LANES]
                    q = FZ // 4
                    o[k, rx, rz, 2 * FZ :, :] = jnp.concatenate(
                        [block[q * j : q * (j + 1), 2 * LANES :] for j in range(4)], axis=1
                    )
        if f == 0:
            ready()
        if f < NF - 1:
            for copy in first(f)[1::2]:
                copy.start()
        sum1 = jnp.zeros((1, FB), f32)
        for side in (1, 0):
            part = slice(LH * side, LH * (side + 1))
            d_pre = (dot_nt(dbs[part, :], w2f) * slope[part, :].astype(f32)).astype(bf16)
            dpre[part, :] = d_pre
            sum1 += jnp.sum(d_pre.astype(f32), axis=0, keepdims=True)
        sum1_o[f] = sum1
        for m in range(3):
            cut = slice(m * D // 3, (m + 1) * D // 3)
            p = dot_tn(sh2v[:, cut], dpre[...]).astype(bf16)
            for t in range(4):
                tt_[t, cut, :FZ] = p[:, FZ * t : FZ * (t + 1)]
        for rz in range(4):
            zz = flip(z, rz)
            for ry in range(2):
                for rx in range(2):
                    tt = (ry + y) % 2 * 2 + (rx + x) % 2
                    o = (ka, sa)[rx]
                    tails = []
                    for rc in range(2):
                        block = tt_[tt, pl.ds(pl.multiple_of(zz * DZ + (rc + c) % 2 * DC, 16), DC), :FZ]
                        o[k, ry, rz, DC * rc : DC * (rc + 1), :] = block[:, :LANES]
                        tails.append(block[:, LANES:])
                    o[k, ry, rz, 2 * DC :, :] = jnp.concatenate(tails, axis=1)
        if f < NF - 1:
            for copy in first(f)[0::2]:
                copy.start()
        for copy in stored(f):
            copy.start()
        for side in (1, 0):
            part = slice(LH * side, LH * (side + 1))
            branch, ds2 = dot_nn(hid[part, :], w2f), dot_nt(dpre[part, :], w1f)
            if f > 0:
                branch, ds2 = branch + br[part, :], ds2 + ds[part, :]
            if f < NF - 1:
                br[part, :] = branch
                ds[part, :] = ds2
            elif side == 1:
                far[0] = branch.astype(bf16)
                far[1] = ds2.astype(bf16)
                for copy in crossing:
                    copy.start()
            else:
                branch_o[...] = branch.astype(bf16)
                ds2_o[...] = ds2.astype(bf16)
        waiting += stored(f)
        if f > 0:
            waiting += onward(f - 1)
        if f == NF - 2:
            for copy in waiting:
                copy.wait()
            waiting = []
    for copy in waiting + crossing:
        copy.wait()


def middle_kernel(ds, ds_r, br, br_r, attn, tok, g, kept, mod, bias2, mixed, wp,
                  d_resid_o, out_o, dh_o, pka, psa, pkb, psb, sums_o, sum_o,
                  dsv, attnv, tokv, mixv, wpv, da, t1, csems, lsems, ready):
    z, c, y, x = place()
    n = LH // 4
    near = pl.ds(0, LH)
    loads = [
        pltpu.make_async_copy(src, dst, lsems.at[k])
        for k, (src, dst) in enumerate(
            ((tok.at[near], tokv.at[0]), (attn, attnv), (ds, dsv.at[0]), (ds_r, dsv.at[1]), (br, dsv.at[2]),
             (br_r, dsv.at[3]), (g.at[near], tokv.at[1]), (wp.at[:, c], wpv), (mixed, mixv))
        )
    ]
    for load in loads:
        load.start()
    ready()
    crossing = [remote(da.at[pl.ds(n * k, n)], da.at[pl.ds(LH + n * k, n)], csems, k, "c") for k in range(4)]
    sums = jnp.zeros((4, D), f32)
    bias_line = bias2[...].astype(f32).reshape(1, D)
    for load in loads[:7]:
        load.wait()
    for k in range(4):
        part = slice(n * k, n * (k + 1))
        gf, at = tokv[1, part, :].astype(f32), attnv[part, :]
        resid = tokv[0, part, :].astype(f32) + mod[2:3, :] * at
        normed2, inverse2 = normalize(resid)
        ds2 = dsv[0, part, :].astype(f32) + dsv[1, part, :].astype(f32)
        kb = kept[part, :] * (dsv[2, part, :].astype(f32) + dsv[3, part, :].astype(f32) + bias_line)
        out_o[part, :] = (resid + mod[5:6, :] * kb).astype(bf16)
        d_resid = gf + normalize_back(ds2 * (1.0 + mod[4:5, :]), normed2, inverse2)
        d_resid_o[part, :] = d_resid
        da[part, :] = (mod[2:3, :] * d_resid).astype(bf16)
        crossing[k].start()
        sums += jnp.concatenate(
            [jnp.sum(p, axis=0, keepdims=True) for p in (at * d_resid, ds2, ds2 * normed2, kb * gf)], axis=0
        )
    sums_o[...] = jnp.concatenate([sums, jnp.zeros((4, D), f32)], axis=0)
    for load in loads[7:]:
        load.wait()
    for copy in crossing:
        copy.wait()
    wv = wpv[...].reshape(WC, D)
    dh_o[...] = dot_nt(da[...], wv).astype(bf16)
    sum_o[...] = dot_nn(jnp.ones((16, L), bf16), da[...])[:8]
    grad = dot_tn(mixv[...], da[...]).astype(bf16)
    for t in range(4):
        t1[t] = grad[:, TD * t : TD * (t + 1)]
    for rz in range(4):
        zz = flip(z, rz)
        for ry in range(2):
            for rx in range(2):
                tt = (ry + y) % 2 * 2 + (rx + x) % 2
                a, b = (pka, psa)[rx], (pkb, psb)[ry]
                block = t1[tt, pl.ds(pl.multiple_of(zz * DC, 16), DC), :]
                a[ry, rz, :DC, :] = block[:, :LANES]
                a[ry, rz, DC:, :] = block[: PA - DC, LANES : 2 * LANES]
                b[rx, rz, : 2 * DC - PA, :] = block[PA - DC :, LANES : 2 * LANES]
                q = DC // 3
                tails = [block[q * k : q * (k + 1), 2 * LANES :] for k in range(3)]
                tails.append(jnp.zeros((q, 32), bf16))
                b[rx, rz, 2 * DC - PA :, :] = jnp.concatenate(tails, axis=1)


def qkv_slots(dqkv, shifted, extra, t1, ka, sa, kb, sb):
    z, _, y, x = place()
    grad = dot_tn(dqkv, shifted)
    for t in range(4):
        for zz in range(4):
            t1[t, zz] = grad[TQ * t : TQ * (t + 1), DZ * zz : DZ * (zz + 1)]
    q = TQ // 3
    for rz in range(4):
        zz = flip(z, rz)
        for ry in range(2):
            for rx in range(2):
                tt = (ry + y) % 2 * 2 + (rx + x) % 2
                block = t1[tt, zz]
                tails = [block[q * k : q * (k + 1), 2 * LANES :] for k in range(3)] + [jnp.zeros((q, 32), f32)]
                more = jnp.zeros((8, LANES), f32) if extra is None else extra[zz, tt]
                slot = [block[:, :LANES], block[:, LANES : 2 * LANES], jnp.concatenate(tails, axis=1), more]
                slot = jnp.concatenate(slot, axis=0).astype(bf16)
                (ka, sa)[rx][ry, rz] = slot[:QA]
                (kb, sb)[ry][rx, rz] = slot[QA:]


def column_sums(dqkv):
    return dot_nn(jnp.ones((16, L), bf16), dqkv)[:8]


def attn_back_kernel(step, qkv, dh, shifted, hmask, out, on_a, q_a, on_b, q_b, keep_a, keep_b, sums_o,
                     qkvv, dhv, shv, outv, qh, kh, vh, doh, dk, dv, t1, ka, sa, kb, sb, ra, rb, ona, onb,
                     fsems, lsems, ready, tick):
    loads = [
        pltpu.make_async_copy(a, b, lsems.at[k])
        for k, (a, b) in enumerate(((qkv, qkvv), (dh, dhv), (shifted, shv)))
    ]
    for load in loads:
        load.start()
    ready()
    for load in loads:
        load.wait()
    scale = LOG2E / math.sqrt(HD)
    first = [
        remote(sa.at[1], ra, fsems, 0, "x"), remote(sb.at[1], rb, fsems, 1, "y"),
        remote(sa.at[0], q_a, fsems, 2, "x"), remote(sb.at[0], q_b, fsems, 3, "y"),
    ]
    stores = [pltpu.make_async_copy(a, b, lsems.at[3 + k]) for k, (a, b) in enumerate(((ka.at[0], keep_a), (kb.at[0], keep_b)))]
    for odd in range(2):
        base = WQ * odd
        for j in range(HC // 2):
            for k, ref in enumerate((qh, kh, vh)):
                start = base + DZ * k + HD * j
                ref[j] = qkvv[:, start : start + HD]
            cut = slice(HD * (2 * j + odd), HD * (2 * j + odd + 1))
            doh[j] = (dhv[:, cut].astype(f32) * hmask[:, cut]).astype(bf16)
        dk[...] = jnp.zeros_like(dk)
        dv[...] = jnp.zeros_like(dv)

        def body(i, carry):
            part = pl.ds(pl.multiple_of(i * step, step), step)
            outs = []
            for j in range(HC // 2):
                q, do = qh[j, part, :], doh[j, part, :]
                s = dot_nt(kh[j], q)
                top = jnp.max(s, axis=0, keepdims=True)
                p = jnp.exp2((s - top) * scale)
                p = p * (1.0 / jnp.sum(p, axis=0, keepdims=True))
                dp = dot_nt(vh[j], do)
                row_dot = jnp.sum(p * dp, axis=0, keepdims=True)
                ds = (p * (dp - row_dot)).astype(bf16)
                dv[j] += dot_nn(p.astype(bf16), do)
                dk[j] += dot_nn(ds, q)
                outs.append(dot_tn(ds, kh[j]))
            outv[part, base : base + DZ] = (jnp.concatenate(outs, axis=1) * (1.0 / math.sqrt(HD))).astype(bf16)
            return carry

        half = L // step // 2
        lax.fori_loop(0, half, body, 0)
        tick(1 + 2 * odd)
        lax.fori_loop(half, 2 * half, body, 0)
        for j in range(HC // 2):
            start = base + DZ + HD * j
            outv[:, start : start + HD] = (dk[j] * (1.0 / math.sqrt(HD))).astype(bf16)
            outv[:, start + DZ : start + DZ + HD] = dv[j].astype(bf16)
        if odd == 0:
            sums_o[...] = column_sums(outv[:, :WQ])
            qkv_slots(outv[:, :WQ], shv[...], None, t1, ka, sa, kb, sb)
            for copy in first + stores:
                copy.start()
            tick(2)
    keep = pltpu.make_async_copy(outv, out, lsems.at[5])
    keep.start()
    for copy in first:
        copy.wait()
    for kv, rv, on in ((ka, ra, ona), (kb, rb, onb)):
        on[...] = (kv[1].astype(f32) + rv[...].astype(f32)).astype(bf16)
    onward = [pltpu.make_async_copy(a, b, lsems.at[6 + k]) for k, (a, b) in enumerate(((ona, on_a), (onb, on_b)))]
    for copy in onward:
        copy.start()
    for copy in stores + onward + [keep]:
        copy.wait()


def end_kernel(dqkv, shifted, even_sums, sum1, sum2, sum_attn, wq, d_resid, tok, mod, sums_mid, f0, f1, f2, sent_p, kept_p, freq,
               on_a, q_a, on_b, q_b, keep_a, keep_b,
               grad, gq_o, gp_o, g1_o, g2_o, ada_o, ada_bias_o, line_o,
               dqv, shv, extra, t1, ka, sa, kb, sb, ra, rb, ona, onb, r2a, r2b, zs, zk, zr,
               eqa, era, eka, eqb, erb, ekb, ezs, ezk, ezr, qt, wqv, dres, tokv, fv, far, got, gb,
               item, item_r, out_shares, square, every, row_out, row_in, mine, theirs, mine_q, theirs_q, pk, pr,
               qsems, esems, csems, tsems, ssems, psems, lsems, ready):
    z, c, y, x = place()
    t, b = 2 * y + x, 2 * z + c
    second_e = [remote(on_a, era, esems, 0, "y"), remote(on_b, erb, esems, 1, "x")]
    third_p = [remote(sent_p.at[k], pr.at[k], psems, k, f"z{k + 1}") for k in (2, 1, 0)]
    pairs = ((dqkv, dqv), (shifted, shv), (wq, wqv), (d_resid, dres), (tok.at[pl.ds(0, LH)], tokv),
             (keep_a, eka), (q_a, eqa), (keep_b, ekb), (q_b, eqb), (f0, fv.at[0]), (f1, fv.at[1]), (f2, fv.at[2]),
             (kept_p, pk))
    loads = [pltpu.make_async_copy(src, dst, lsems.at[k]) for k, (src, dst) in enumerate(pairs)]
    for copy in loads:
        copy.start()
    loads[0].wait()
    loads[1].wait()
    ready()
    for copy in second_e + third_p:
        copy.start()

    odd = dqv[:, WQ:]
    odd_sums = column_sums(odd)
    for zs_ in range(4):
        for ts in range(4):
            start, n = FF // 32 * ts, FF // 32
            pieces = []
            for f in range(NF):
                low, high = max(start, FZ * f), min(start + n, FZ * (f + 1))
                if low < high:
                    pieces.append(sum1[f][:, FZ * zs_ + low - FZ * f : FZ * zs_ + high - FZ * f])
            n = D // 32
            for total in (sum2[...], sum_attn[0:1, :]):
                at = DZ * zs_ + n * ts
                pieces.append(jnp.where(c == 0, total[:, at : at + n], total[:, at + DC : at + DC + n]))
            total = (even_sums, odd_sums)[ts // 2][0:1, :]
            at = HD * zs_ + n * (ts % 2)
            pieces += [total[:, at : at + n], total[:, 2 * DZ + at : 2 * DZ + at + n]]
            flat = jnp.concatenate(pieces + [jnp.zeros((1, 3 * LANES - DZ), f32)], axis=1)
            lines = [flat[:, LANES * k : LANES * (k + 1)] for k in range(3)] + [jnp.zeros((5, LANES), f32)]
            extra[zs_, ts] = jnp.concatenate(lines, axis=0)
    qkv_slots(odd, shv[...], extra, t1, ka, sa, kb, sb)
    first_q = [
        remote(sa.at[1], ra.at[1], qsems, 0, "x"), remote(sb.at[1], rb.at[1], qsems, 1, "y"),
        remote(sa.at[0], ra.at[0], qsems, 2, "x"), remote(sb.at[0], rb.at[0], qsems, 3, "y"),
    ]
    for copy in first_q:
        copy.start()

    loads[2].wait()
    crossing = [remote(far.at[k], got.at[k], csems, k, "c") for k in range(2)]
    d_far = dot_nt(dqv[LH:, :], wqv[...])
    for k in range(2):
        far[k] = d_far[LB * k : LB * (k + 1)].astype(bf16)
        crossing[k].start()

    for copy in second_e:
        copy.wait()
    for k in (5, 6, 7, 8):
        loads[k].wait()
    layer_sums([(eka, eqa, era), (ekb, eqb, erb)], ezs, ezk)
    third_e = [remote(ezs.at[k], ezr.at[k], esems, 2 + k, f"z{k + 1}") for k in (2, 1, 0)]
    for copy in third_e:
        copy.start()
    d_near = dot_nt(dqv[:LH, :], wqv[...])
    loads[3].wait()
    loads[4].wait()
    token_sums = jnp.zeros((2, D), f32)
    for k in range(2):
        part = slice(LB * k, LB * (k + 1))
        crossing[k].wait()
        total = d_near[part] + got[k].astype(f32)
        normed, inverse = normalize(tokv[part, :].astype(f32))
        back = dres[part, :] + normalize_back(total * (1.0 + mod[1:2, :]), normed, inverse)
        gb[k] = back.astype(bf16)
        token_sums += jnp.concatenate(
            [jnp.sum(v, axis=0, keepdims=True) for v in (total, total * normed)], axis=0
        )
    item[...] = jnp.concatenate([token_sums, sums_mid[0:4, :], mod[6:8, :]], axis=0)
    over = remote(item, item_r, csems, 2, "c")
    over.start()

    for copy in first_q:
        copy.wait()
    for kv, rv, on in ((ka, ra, ona), (kb, rb, onb)):
        on[...] = (kv[1].astype(f32) + rv[1].astype(f32)).astype(bf16)
    second_q = [remote(ona, r2a, qsems, 4, "y"), remote(onb, r2b, qsems, 5, "x")]
    for copy in second_q:
        copy.start()
    over.wait()
    v = item[...] + item_r[...]
    n = D // 2
    stamp = v[6:7, :LANES]
    pieces = ([v[0:1], v[1:2, :n]], [v[1:2, n:], v[2:3]], [v[3:4], v[4:5, :n]], [v[4:5, n:], v[5:6]])
    for j in range(4):
        out_shares[j] = jnp.concatenate(pieces[j] + [stamp], axis=1)
    square[t] = out_shares[t]
    meeting = [
        remote(out_shares.at[(y + j // 2) % 2 * 2 + (x + j) % 2], square.at[t], ssems, j - 1, ("x", "y", "xy")[j - 1])
        for j in (1, 2, 3)
    ]
    for copy in meeting:
        copy.start()

    def first_columns(pairs, own):
        for core in range(2):

            @pl.when(c == core)
            def _():
                for f, pair in enumerate(pairs):
                    start = FF // 8 * (core if own else 1 - core) + FZ * f
                    g1_o[:, start : start + FZ] = jnp.concatenate(pair, axis=1)

    for k in (9, 10, 11, 12):
        loads[k].wait()
    for f in range(NF):
        mine[G1R * f : G1R * (f + 1), :] = fv[f, :G1R, :].astype(bf16)
    swap = remote(mine, theirs, csems, 3, "c")
    swap.start()
    first_columns([[fv[f, :DC, :], fv[f, 2 * DC : 3 * DC, : FZ - LANES]] for f in range(NF)], True)
    for copy in second_q:
        copy.wait()
    layer_sums([(ka.at[0], ra.at[0], r2a), (kb.at[0], rb.at[0], r2b)], zs, zk)
    third_q = [remote(zs.at[k], zr.at[k], qsems, 6 + k, f"z{k + 1}") for k in (2, 1, 0)]
    for copy in third_q:
        copy.start()
    home = homeward(gb.at[0], gb.at[1], grad, tsems, lsems.at[len(pairs)])
    home_start(*home)
    for copy in meeting:
        copy.wait()
    spread_z = [remote(square, every.at[z], ssems, 2 + k, f"z{k}") for k in (1, 2, 3)]
    every[z] = square[...]
    for copy in spread_z:
        copy.start()
    for f in range(NF):
        part = fv[f, G1R:, :]
        tail = part[2 * FZ :]
        tail = jnp.concatenate([tail[:, 32 * k : 32 * (k + 1)] for k in range(4)], axis=0)
        g2_o[FZ * f : FZ * (f + 1), :] = jnp.concatenate([part[:FZ], part[FZ : 2 * FZ], tail], axis=1)
    for copy in third_p:
        copy.wait()
    part = pk[...] + pr[0].astype(f32) + pr[1].astype(f32) + pr[2].astype(f32)
    tail = part[2 * DC :]
    tail = jnp.concatenate([tail[:, 32 * k : 32 * (k + 1)] for k in range(3)], axis=0)
    gp_o[...] = jnp.concatenate([part[:DC], part[DC : 2 * DC], tail], axis=1)
    swap.wait()
    first_columns(
        [
            [theirs[G1R * f + DC : G1R * f + 2 * DC, :].astype(f32),
             theirs[G1R * f + 2 * DC : G1R * (f + 1), FZ - LANES :].astype(f32)]
            for f in range(NF)
        ],
        False,
    )

    for copy in spread_z:
        copy.wait()
    columns = jnp.concatenate([every[i, j] for i in range(4) for j in range(4)], axis=0)
    width = 3 * D // 2
    angles = columns[:, width : width + 1] * freq[b % 4]
    cond = jax.nn.silu(jnp.where(b < 4, jnp.cos(angles), jnp.sin(angles))).astype(bf16).astype(f32)
    columns = columns[:, :width]
    ada_o[...] = lax.dot_general(
        cond, columns, (((0,), (0,)), ((), ())), precision=lax.Precision.HIGHEST, preferred_element_type=f32
    )
    row = jnp.sum(columns, axis=0, keepdims=True)
    row_out[0] = row
    row_in[t] = row
    rows_ = [remote(row_out.at[0], row_in.at[t], ssems, 6 + j, name) for j, name in enumerate(("x", "y", "xy"))]
    for copy in rows_:
        copy.start()

    for odd_, (copies, kept, more) in enumerate(((third_e, ezk, ezr), (third_q, zk, zr))):
        for copy in copies:
            copy.wait()
        q = kept[...] + more[0].astype(f32) + more[1].astype(f32) + more[2].astype(f32)
        tail = q[2 * TQ :]
        n = TQ // 3
        tail = jnp.concatenate([tail[n * 0 : n, 32 * k : 32 * (k + 1)] for k in range(3)], axis=0)
        qt[odd_] = jnp.transpose(jnp.concatenate([q[:TQ], q[TQ : 2 * TQ], tail], axis=1))
        mine_q[odd_] = qt[odd_, pl.ds(pl.multiple_of(DC * (1 - c), 16), DC), :].astype(bf16)
        swap = remote(mine_q.at[odd_], theirs_q.at[odd_], csems, 4 + odd_, "c")
        swap.start()
        if odd_ == 1:
            line_o[...] = q[QR - 8 :]
    own = [qt[odd_, pl.ds(pl.multiple_of(DC * c, 16), DC), :] for odd_ in range(2)]

    def qkv_columns(values, owned):
        for core in range(2):

            @pl.when(c == core)
            def _():
                for odd_ in range(2):
                    for j in range(3):
                        start = DZ * j + DC * (core if owned else 1 - core) + HD * odd_
                        gq_o[:, start : start + HD] = values[odd_][:, HD * j : HD * (j + 1)]

    qkv_columns(own, True)
    for odd_ in range(2):
        remote(mine_q.at[odd_], theirs_q.at[odd_], csems, 4 + odd_, "c").wait()
    qkv_columns([theirs_q[odd_].astype(f32) for odd_ in range(2)], False)
    for copy in rows_:
        copy.wait()
    row = row_in[z]
    ada_bias_o[...] = jnp.where(c == 0, row[:, : width // 2], row[:, width // 2 :])
    home_wait(*home)


def final_kernel(out_rows, grad_rows, gq, gp, g1, g2, ada, ada_bias, line,
                 out, grad, gq_o, gp_o, g1_o, g2_o, ada_o, ada_bias_o, b_fc1, b_fc2, b_proj, b_q, b_v):
    out[...] = out_rows[...]
    grad[...] = grad_rows[...].astype(f32)
    gq_o[...] = gq[...]
    gp_o[...] = gp[...]
    g1_o[...] = g1[...]
    g2_o[...] = jnp.transpose(g2[...])
    ada_o[...] = ada[...]
    ada_bias_o[...] = ada_bias[...].reshape(-1)
    flat = jnp.concatenate([line[k : k + 1, :] for k in range(3)], axis=1)
    n1, n = FF // 32, D // 32
    b_fc1[...] = flat[:, :n1].reshape(-1)
    for k, ref in enumerate((b_fc2, b_proj, b_q, b_v)):
        ref[...] = flat[:, n1 + n * k : n1 + n * (k + 1)].reshape(-1)


def one_item_per_chip(
    tokens, cotangent, timesteps, bucket_ids, head_masks, channel_masks, skip_rows,
    w_qkv, q_bias, v_bias, w_proj, proj_bias, w_fc1, fc1_bias, w_fc2, fc2_bias, ada_weight, ada_bias,
):
    b, t = lax.axis_index("bucket"), lax.axis_index("tok")
    z, c, y, x = b // 2, b % 2, t // 2, t % 2
    sds = jax.ShapeDtypeStruct

    def core_half(v, *dims):
        return lax.dynamic_index_in_dim(v.reshape(dims), c, 1, keepdims=False)

    vmem, smem = pl.BlockSpec(memory_space=pltpu.VMEM), pl.BlockSpec(memory_space=pltpu.SMEM)
    steps = -np.float32(math.log(10000.0)) * np.arange(D // 2, dtype=np.float32) / np.float32(D // 2)
    freq = jnp.asarray(np.exp(steps).reshape(1, D // 2))
    ada_cols = ada_weight.shape[1]
    front, _ = call(
        front_kernel, "front",
        (sds((L, D), bf16), sds((L, D), bf16), sds((L, 3 * WC), bf16), sds((D, 3 * WC), bf16), sds((NF, D, FB), bf16), sds((8, D), f32), sds((L, 1), f32), sds((1, WC), f32), sds((NF, 1, FB), f32),
         sds((NF, 1, FB), f32)),
        (tokens, timesteps, bucket_ids, skip_rows, ada_weight.T, ada_bias, head_masks, channel_masks,
         w_qkv, w_fc1, q_bias, v_bias, fc1_bias, freq),
        in_specs=[ANY, smem, smem, vmem, ANY, vmem, vmem, vmem, ANY, ANY, vmem, vmem, vmem, vmem],
        out_specs=[ANY] * 5 + [vmem] * 5,
        scratch=[vm(L, D), vm(D, 3 * D), vm(D, 3 * WC), vm(D, FF), vm(NF, D, FB), vm(ada_cols, D),
                 vm(8, LANES, dtype=jnp.int32), vm(8, LANES, dtype=jnp.int32), vm(8, ada_cols, dtype=f32), vm(3, 8, ada_cols, dtype=f32),
                 vm(4, 8, ada_cols, dtype=f32), vm(L, D), vm(L, 3 * WC), pltpu.SemaphoreType.DMA((2, 5)),
                 pltpu.SemaphoreType.DMA((2, 4)), pltpu.SemaphoreType.DMA((2, 6)), pltpu.SemaphoreType.DMA((8,))],
        peers=("c", "t0", "t1", "x", "y", "xy"), cid=10, flops=2 * L * D * 3 * WC, nbytes=50e6,
    )
    tok, shifted, qkv, wq, w1, mod, kept, hmask, chan, b1 = front
    w2 = w_fc2.reshape(4, 2, NF, FZ, D)
    wp = w_proj.reshape(4, 2, DC, D)
    (g_all, mixed, shifted2, attn), _ = call(
        functools.partial(attn_kernel, 512), "attn",
        (sds((L, D), bf16), sds((L, WC), bf16), sds((L, D), bf16), sds((LH, D), f32)),
        (cotangent, qkv, hmask, wp, proj_bias, tok, mod),
        in_specs=[ANY, ANY, vmem, ANY, vmem, ANY, vmem],
        out_specs=[ANY, ANY, vmem, vmem],
        scratch=[vm(L, D), vm(L, 3 * WC)] + [vm(HC, L, HD)] * 2 + [vm(HC, L, LANES)] + [vm(L, WC), vm(L, WC), vm(2, 4, DC, D), vm(L, D),
                 pltpu.SemaphoreType.DMA((2, 4)), pltpu.SemaphoreType.DMA((2, 2)), pltpu.SemaphoreType.DMA((2, 2)),
                 pltpu.SemaphoreType.DMA((7,))],
        peers=("c", "t0", "t1"), cid=11, flops=16e9, nbytes=5e6,
    )

    slot1, slot2 = sds((2, 4, G1R, LANES), bf16), sds((2, 4, G2R, LANES), bf16)
    part1, part2 = sds(slot1.shape[1:], bf16), sds(slot2.shape[1:], bf16)
    one = [part1, part1, part2, part2, part1, part2]
    rows_half = sds((LH, D), bf16)
    dma = pltpu.SemaphoreType.DMA
    own, _ = call(
        mlp_kernel, "mlp",
        one + one + [slot1, slot1, slot2, slot2] + [rows_half] * 4 + [sds((NF, 1, FB), f32), sds((1, D), f32)],
        (shifted2, g_all, kept, mod, w1, b1, chan, w2),
        in_specs=[ANY, ANY, vmem, vmem, ANY, vmem, vmem, ANY],
        out_specs=[ANY] * 16 + [vmem, vmem, ANY, ANY, vmem, vmem],
        scratch=[vm(L, D), vm(L, D), vm(2, D, FB), vm(2, 4, FZ, D), vm(L, FB), vm(L, FB),
                 vm(L, FB), vm(L, D, dtype=f32), vm(L, D, dtype=f32), vm(2, LH, D), vm(4, D, TD)]
        + [vm(2, *slot1.shape)] * 2 + [vm(2, *slot2.shape)] * 2
        + [vm(2, *p.shape) for p in (part1, part2)] * 2
        + [dma((2, 8)), dma((2, 2)), dma((2,)), dma((2, 2)), dma((2, 6))],
        peers=("c", "x", "y"), cid=0,
        flops=36 * L * D * FB, nbytes=40e6,
    )
    second0, second1, slots = own[:6], own[6:12], own[12:16]
    branch, ds2, branch_r, ds2_r, sum1, sum2 = own[16:]

    slot_a, slot_b = sds((2, 4, PA, LANES), bf16), sds((2, 4, PR - PA, LANES), bf16)
    own, given = call(
        middle_kernel, "middle",
        (sds((LH, D), f32), rows_half, sds((L, WC), bf16), slot_a, slot_a, slot_b, slot_b, sds((8, D), f32),
         sds((8, D), f32)),
        (ds2, ds2_r, branch, branch_r, attn, tok, g_all, kept, mod, fc2_bias, mixed, wp),
        in_specs=[ANY] * 7 + [vmem] * 3 + [ANY] * 2,
        scratch=[vm(4, LH, D), vm(LH, D, dtype=f32), vm(2, LH, D), vm(L, WC), vm(4, DC, D), vm(L, D), vm(4, WC, TD),
                 dma((2, 4)), dma((9,))],
        peers=("c",), cid=3, jobs=[FirstSum(*slots), SecondSum(*second0)],
        flops=4 * L * D * WC, nbytes=20e6,
    )
    d_resid, out_rows, dh, *slots_p, sums_mid, sum_attn = own
    first2, result0 = given
    slot_q = vm(2, 4, QA, LANES)
    fourth = vm(4, QA, LANES)
    part_q = sds((4, QA, LANES), bf16)
    own, given = call(
        functools.partial(attn_back_kernel, 512), "attn_back",
        [sds((L, 3 * WC), bf16)] + [part_q] * 6 + [sds((8, WQ), f32)], (qkv, dh, shifted, hmask),
        in_specs=[ANY] * 3 + [vmem],
        out_specs=[ANY] * 7 + [vmem],
        scratch=[vm(L, 3 * WC), vm(L, WC), vm(L, D), vm(L, 3 * WC)] + [vm(HC // 2, L, HD)] * 4
        + [vm(HC // 2, L, HD, dtype=f32)] * 2 + [vm(4, 4, TQ, DZ, dtype=f32)] + [slot_q] * 4 + [fourth] * 4
        + [dma((2, 4)), dma((8,))],
        cid=4, ticks=True,
        jobs=[SecondThird(*second1, tick_at=1), SecondThird(*first2, slots[0], slots[2], start_at=1, tick_at=3),
              FirstSecond(*slots_p, start_at=1, tick_at=3), ThirdSum(*result0), GoHome(out_rows, tick_at=3)],
        flops=30e9, nbytes=9e6,
    )
    dqkv, *second_q, even_sums = own
    final1, final2, (sent_p, kept_p), final0, output = given[0][0], given[1][0], given[2], given[3][0], given[4][0]
    width = ada_cols + LANES
    (grad_rows, gq, gp, g1, g2, grad_ada_weight, grad_ada_bias, line), _ = call(
        end_kernel, "end",
        (sds((2, LB, D), bf16), sds((DC, 3 * TD), f32), sds((DC, TD), f32), sds((DC, FF // 4), f32),
         sds((FF // 8, TD), f32), sds((DC, ada_cols), f32), sds((1, ada_cols // 2), f32), sds((8, LANES), f32)),
        (dqkv, shifted, even_sums, sum1, sum2, sum_attn, wq, d_resid, tok, mod, sums_mid, final0, final1, final2, sent_p,
         kept_p, freq.reshape(4, 1, DC), *second_q),
        in_specs=[ANY] * 2 + [vmem] * 4 + [ANY] * 3 + [vmem] * 2 + [ANY] * 5 + [vmem] + [ANY] * 6,
        out_specs=[ANY] + [vmem] * 7,
        scratch=[vm(L, 3 * WC), vm(L, D), vm(4, 4, 8, LANES, dtype=f32), vm(4, 4, TQ, DZ, dtype=f32)] + [slot_q] * 6
        + [fourth] * 4 + [vm(3, QR, LANES), vm(QR, LANES, dtype=f32), vm(3, QR, LANES)]
        + [fourth] * 6 + [vm(3, QR, LANES), vm(QR, LANES, dtype=f32), vm(3, QR, LANES)]
        + [vm(2, DZ, TQ, dtype=f32), vm(D, 3 * WC), vm(LH, D, dtype=f32), vm(LH, D),
           vm(NF, G1R + G2R, LANES, dtype=f32)] + [vm(2, LB, D)] * 3
        + [vm(8, D, dtype=f32)] * 2 + [vm(4, 1, width, dtype=f32)] * 2
        + [vm(4, 4, 1, width, dtype=f32), vm(1, 1, ada_cols, dtype=f32), vm(4, 1, ada_cols, dtype=f32)]
        + [vm(NF * G1R, LANES)] * 2 + [vm(2, DC, TQ)] * 2 + [vm(PR, LANES, dtype=f32), vm(3, PR, LANES)]
        + [dma((2, 9)), dma((2, 5)), dma((2, 6)), dma((2, 2)), dma((2, 9)), dma((2, 3)), dma((14,))],
        peers=("c", "t0", "t1", "x", "y", "xy", "z1", "z2", "z3"), cid=5,
        flops=4 * L * D * 3 * WC, nbytes=30e6,
    )
    thin = lambda height, width: pl.BlockSpec((height, width), lambda i: (i, 0))
    tokens_spec = pl.BlockSpec((2, LB // 2, D), lambda i: (0, i, 0))
    ends = [thin(DC // 2, 3 * TD), thin(DC // 2, TD), thin(DC // 2, FF // 4)]
    bias_cols = ada_cols // 2
    finals, _ = call(
        final_kernel, "final",
        (sds((2, LB, D), bf16), sds((2, LB, D), f32), sds((DC, 3 * TD), f32), sds((DC, TD), f32), sds((DC, FF // 4), f32),
         sds((TD, FF // 8), f32), sds((DC, ada_cols), f32), sds((bias_cols,), f32), sds((FF // 32,), f32))
        + (sds((D // 32,), f32),) * 4,
        (output, grad_rows, gq, gp, g1, g2, grad_ada_weight, grad_ada_bias, line),
        grid=(2,),
        in_specs=[tokens_spec, tokens_spec, *ends, full((FF // 8, TD)), thin(DC // 2, ada_cols), full((1, bias_cols)),
                  full((8, LANES))],
        out_specs=[tokens_spec, tokens_spec, *ends, full((TD, FF // 8)), thin(DC // 2, ada_cols), full((bias_cols,)),
                   full((FF // 32,))] + [full((D // 32,))] * 4,
    )
    output, grad_tokens, gq, gp, g1, g2, g_ada, ada_b, b_fc1, b_fc2, b_proj, b_q, b_v = finals
    return (output, grad_tokens, gq, b_q, b_v, gp, b_proj, g1, b_fc1, g2.T, b_fc2, g_ada, ada_b)


def gelu_tanh(values):
    return jax.nn.gelu(values, approximate=True)


def split_heads(key_value, model_width, head_dim):
    item_count, length = (key_value.shape[0], key_value.shape[1])
    key_rows = key_value[:, :, :model_width].reshape(
        item_count, length, model_width // head_dim, head_dim
    )
    value_rows = key_value[:, :, model_width:].reshape(
        item_count, length, model_width // head_dim, head_dim
    )
    return (key_rows, value_rows)


def scores_of(queries, key_rows, score_scale):
    return (
        jnp.einsum("nqhe,nkhe->nhqk", queries, key_rows, preferred_element_type=jnp.float32)
        * score_scale
    )


def to_blocks(values, per_step):
    return values.reshape((values.shape[0] // per_step, per_step) + values.shape[1:])


def from_blocks(values):
    return values.reshape((values.shape[0] * values.shape[1],) + values.shape[2:])


def on_device(
    tokens,
    cotangent,
    timesteps,
    bucket_ids,
    head_masks,
    channel_masks,
    skip_rows,
    w_qkv,
    q_bias,
    v_bias,
    w_proj,
    proj_bias,
    w_fc1,
    fc1_bias,
    w_fc2,
    fc2_bias,
    ada_weight,
    ada_bias,
):
    item_count, local_len, model_width = tokens.shape
    row_count = item_count * local_len
    head_dim = model_width // HEADS
    score_scale = 1.0 / math.sqrt(head_dim)
    hidden_width = w_fc1.shape[1]
    ada_cols = ada_weight.shape[1]
    tok_index = lax.axis_index("tok")
    per_step = 1
    for candidate in range(1, item_count + 1):
        per_step = candidate
    condition = jax.nn.silu(step_embedding(timesteps, model_width)).astype(jnp.bfloat16)
    mod_local = jnp.dot(
        condition, ada_weight, preferred_element_type=jnp.float32
    ) + ada_bias.astype(jnp.float32)
    modulation = lax.all_gather(mod_local, "tok", axis=1, tiled=True)
    pieces = modulation.reshape(item_count, 6, 1, model_width)
    shift_a = pieces[:, 0]
    scale_a = pieces[:, 1]
    gate_a = pieces[:, 2]
    shift_m = pieces[:, 3]
    scale_m = pieces[:, 4]
    gate_m = pieces[:, 5]
    chosen = (jnp.arange(head_masks.shape[0], dtype=jnp.int32) == bucket_ids[0]).astype(jnp.float32)
    head_on = jnp.sum(chosen[:, None] * head_masks.astype(jnp.float32), axis=0)
    group_on = jnp.sum(chosen[:, None] * channel_masks.astype(jnp.float32), axis=0)
    channel_on = jnp.repeat(group_on, hidden_width // group_on.shape[0])
    positions = tok_index * local_len + jnp.arange(local_len, dtype=jnp.int32)
    skipped = jnp.any(skip_rows[:, :, None] == positions[None, None, :], axis=1)
    kept_rows = 1.0 - skipped.astype(jnp.float32)
    inputs = tokens.astype(jnp.float32)
    normed, inverse = normalize(inputs)
    shifted = (
        (normed * (1.0 + scale_a) + shift_a).astype(jnp.bfloat16).reshape(row_count, model_width)
    )
    qkv_bias = jnp.concatenate([q_bias, jnp.zeros_like(q_bias), v_bias]).astype(jnp.float32)
    projected = (jnp.dot(shifted, w_qkv, preferred_element_type=jnp.float32) + qkv_bias).astype(
        jnp.bfloat16
    )
    projected = projected.reshape(item_count, local_len, 3 * model_width)
    queries = projected[:, :, :model_width].reshape(item_count, local_len, HEADS, head_dim)
    key_value = projected[:, :, model_width:]
    all_kv = lax.all_gather(key_value, "tok", axis=1, tiled=True)

    def forward_block(packed):
        query_block, kv_block = packed
        key_rows, value_rows = split_heads(kv_block, model_width, head_dim)
        scores = scores_of(query_block, key_rows, score_scale)
        top_score = jnp.max(scores, axis=-1, keepdims=True)
        expanded = jnp.exp(scores - top_score)
        totals = jnp.sum(expanded, axis=-1, keepdims=True)
        weights_low = (expanded / totals).astype(jnp.bfloat16)
        head_out = (
            jnp.einsum(
                "nhqk,nkhe->nqhe", weights_low, value_rows, preferred_element_type=jnp.float32
            )
            * head_on[:, None]
        )
        return (head_out.astype(jnp.bfloat16), top_score + jnp.log(totals))

    mixed_heads, log_total = lax.map(
        forward_block, (to_blocks(queries, per_step), to_blocks(all_kv, per_step))
    )
    log_total = from_blocks(log_total)
    mixed = from_blocks(mixed_heads).reshape(row_count, model_width)
    attn = (
        jnp.dot(mixed, w_proj, preferred_element_type=jnp.float32) + proj_bias.astype(jnp.float32)
    ).reshape(item_count, local_len, model_width)
    resid = inputs + gate_a * attn
    normed2, inverse2 = normalize(resid)
    shifted2 = (
        (normed2 * (1.0 + scale_m) + shift_m).astype(jnp.bfloat16).reshape(row_count, model_width)
    )
    pre = jnp.dot(shifted2, w_fc1, preferred_element_type=jnp.float32) + fc1_bias.astype(
        jnp.float32
    )
    activated, gelu_pull = jax.vjp(gelu_tanh, pre)
    hidden = (activated * channel_on).astype(jnp.bfloat16)
    branch = (
        jnp.dot(hidden, w_fc2, preferred_element_type=jnp.float32) + fc2_bias.astype(jnp.float32)
    ).reshape(item_count, local_len, model_width)
    gated = kept_rows[:, :, None] * gate_m
    output = (resid + gated * branch).astype(jnp.bfloat16)
    incoming = cotangent.astype(jnp.float32)
    d_gate_m = jnp.sum(kept_rows[:, :, None] * branch * incoming, axis=1)
    d_branch = (gated * incoming).astype(jnp.bfloat16).reshape(row_count, model_width)
    grad_w_fc2 = jnp.dot(hidden.T, d_branch, preferred_element_type=jnp.float32)
    grad_fc2_bias = jnp.sum(d_branch.astype(jnp.float32), axis=0)
    d_hidden = jnp.dot(d_branch, w_fc2.T, preferred_element_type=jnp.float32)
    d_pre = gelu_pull(d_hidden * channel_on)[0].astype(jnp.bfloat16)
    grad_w_fc1 = jnp.dot(shifted2.T, d_pre, preferred_element_type=jnp.float32)
    grad_fc1_bias = jnp.sum(d_pre.astype(jnp.float32), axis=0)
    d_shifted2 = jnp.dot(d_pre, w_fc1.T, preferred_element_type=jnp.float32).reshape(
        item_count, local_len, model_width
    )
    d_shift_m = jnp.sum(d_shifted2, axis=1)
    d_scale_m = jnp.sum(d_shifted2 * normed2, axis=1)
    d_resid = incoming + normalize_back(d_shifted2 * (1.0 + scale_m), normed2, inverse2)
    d_gate_a = jnp.sum(attn * d_resid, axis=1)
    d_attn = (gate_a * d_resid).astype(jnp.bfloat16).reshape(row_count, model_width)
    grad_w_proj = jnp.dot(mixed.T, d_attn, preferred_element_type=jnp.float32)
    grad_proj_bias = jnp.sum(d_attn.astype(jnp.float32), axis=0)
    d_mixed = jnp.dot(d_attn, w_proj.T, preferred_element_type=jnp.float32).astype(jnp.bfloat16)
    d_heads = d_mixed.reshape(item_count, local_len, HEADS, head_dim) * head_on[:, None].astype(
        jnp.bfloat16
    )
    again_kv = lax.all_gather(key_value, "tok", axis=1, tiled=True)

    def backward_block(packed):
        query_block, kv_block, head_grads, totals_log = packed
        key_rows, value_rows = split_heads(kv_block, model_width, head_dim)
        scores = scores_of(query_block, key_rows, score_scale)
        probs = jnp.exp(scores - totals_log)
        d_probs = jnp.einsum(
            "nqhe,nkhe->nhqk", head_grads, value_rows, preferred_element_type=jnp.float32
        )
        row_dot = jnp.sum(probs * d_probs, axis=-1, keepdims=True)
        d_scores = (probs * (d_probs - row_dot)).astype(jnp.bfloat16)
        d_queries = (
            jnp.einsum("nhqk,nkhe->nqhe", d_scores, key_rows, preferred_element_type=jnp.float32)
            * score_scale
        )
        return (d_queries, row_dot)

    mapped = lax.map(
        backward_block,
        (
            to_blocks(queries, per_step),
            to_blocks(again_kv, per_step),
            to_blocks(d_heads, per_step),
            to_blocks(log_total, per_step),
        ),
    )
    d_queries = from_blocks(mapped[0])
    row_dot = from_blocks(mapped[1])
    queries_all, head_grads_all = (
        lax.all_gather(queries, "tok", axis=1, tiled=True),
        lax.all_gather(d_heads, "tok", axis=1, tiled=True),
    )
    totals_all, row_dot_all = (
        lax.all_gather(log_total, "tok", axis=2, tiled=True),
        lax.all_gather(row_dot, "tok", axis=2, tiled=True),
    )

    def key_block(packed):
        kv_block, query_block, head_grads, totals_log, dots = packed
        key_rows, value_rows = split_heads(kv_block, model_width, head_dim)
        scores = (
            jnp.einsum("nkhe,nqhe->nhkq", key_rows, query_block, preferred_element_type=jnp.float32)
            * score_scale
        )
        probs = jnp.exp(scores - totals_log[:, :, None, :, 0])
        d_probs = jnp.einsum(
            "nkhe,nqhe->nhkq", value_rows, head_grads, preferred_element_type=jnp.float32
        )
        d_scores = (probs * (d_probs - dots[:, :, None, :, 0])).astype(jnp.bfloat16)
        d_keys = (
            jnp.einsum("nhkq,nqhe->nkhe", d_scores, query_block, preferred_element_type=jnp.float32)
            * score_scale
        )
        d_values = jnp.einsum(
            "nhkq,nqhe->nkhe",
            probs.astype(jnp.bfloat16),
            head_grads,
            preferred_element_type=jnp.float32,
        )
        return jnp.concatenate(
            [
                d_keys.reshape(d_keys.shape[0], local_len, model_width),
                d_values.reshape(d_values.shape[0], local_len, model_width),
            ],
            axis=2,
        )

    d_kv = from_blocks(
        lax.map(
            key_block,
            (
                to_blocks(key_value, per_step),
                to_blocks(queries_all, per_step),
                to_blocks(head_grads_all, per_step),
                to_blocks(totals_all, per_step),
                to_blocks(row_dot_all, per_step),
            ),
        )
    )
    d_qkv = jnp.concatenate([d_queries.reshape(item_count, local_len, model_width), d_kv], axis=2)
    d_qkv = d_qkv.astype(jnp.bfloat16).reshape(row_count, 3 * model_width)
    grad_w_qkv = jnp.dot(shifted.T, d_qkv, preferred_element_type=jnp.float32)
    qkv_sums = jnp.sum(d_qkv.astype(jnp.float32), axis=0)
    grad_q_bias = qkv_sums[:model_width]
    grad_v_bias = qkv_sums[2 * model_width :]
    d_shifted = jnp.dot(d_qkv, w_qkv.T, preferred_element_type=jnp.float32).reshape(
        item_count, local_len, model_width
    )
    d_shift_a = jnp.sum(d_shifted, axis=1)
    d_scale_a = jnp.sum(d_shifted * normed, axis=1)
    grad_tokens = d_resid + normalize_back(d_shifted * (1.0 + scale_a), normed, inverse)
    d_modulation = jnp.concatenate(
        [d_shift_a, d_scale_a, d_gate_a, d_shift_m, d_scale_m, d_gate_m], axis=1
    )
    d_modulation = lax.psum(d_modulation, "tok")
    mod_columns = lax.dynamic_slice_in_dim(d_modulation, tok_index * ada_cols, ada_cols, 1)
    grad_ada_weight = jnp.dot(
        condition.astype(jnp.float32).T, mod_columns, precision=lax.Precision.HIGHEST
    )
    grad_ada_bias = jnp.sum(d_modulation, axis=0)
    bucket_done = (
        lax.psum_scatter(grad_w_qkv, "bucket", scatter_dimension=0, tiled=True),
        lax.psum_scatter(grad_w_proj, "bucket", scatter_dimension=0, tiled=True),
        lax.psum_scatter(grad_w_fc1, "bucket", scatter_dimension=0, tiled=True),
        lax.psum_scatter(grad_w_fc2, "bucket", scatter_dimension=0, tiled=True),
        lax.psum_scatter(grad_q_bias, "bucket", scatter_dimension=0, tiled=True),
        lax.psum_scatter(grad_v_bias, "bucket", scatter_dimension=0, tiled=True),
        lax.psum_scatter(grad_proj_bias, "bucket", scatter_dimension=0, tiled=True),
        lax.psum_scatter(grad_fc1_bias, "bucket", scatter_dimension=0, tiled=True),
        lax.psum_scatter(grad_fc2_bias, "bucket", scatter_dimension=0, tiled=True),
        lax.psum_scatter(grad_ada_weight, "bucket", scatter_dimension=0, tiled=True),
        lax.psum_scatter(grad_ada_bias, "bucket", scatter_dimension=0, tiled=True),
    )
    token_done = (
        lax.psum_scatter(bucket_done[0], "tok", scatter_dimension=1, tiled=True),
        lax.psum_scatter(bucket_done[1], "tok", scatter_dimension=1, tiled=True),
        lax.psum_scatter(bucket_done[2], "tok", scatter_dimension=1, tiled=True),
        lax.psum_scatter(bucket_done[3], "tok", scatter_dimension=1, tiled=True),
        lax.psum_scatter(bucket_done[4].reshape(1, -1), "tok", scatter_dimension=1, tiled=True),
        lax.psum_scatter(bucket_done[5].reshape(1, -1), "tok", scatter_dimension=1, tiled=True),
        lax.psum_scatter(bucket_done[6].reshape(1, -1), "tok", scatter_dimension=1, tiled=True),
        lax.psum_scatter(bucket_done[7].reshape(1, -1), "tok", scatter_dimension=1, tiled=True),
        lax.psum_scatter(bucket_done[8].reshape(1, -1), "tok", scatter_dimension=1, tiled=True),
    )
    finished = (
        token_done[0],
        token_done[1],
        token_done[2],
        token_done[3],
        token_done[4],
        token_done[5],
        token_done[6],
        token_done[7],
        token_done[8],
        bucket_done[9],
        bucket_done[10],
    )
    return (
        output,
        grad_tokens,
        finished[0],
        finished[4].reshape(-1),
        finished[5].reshape(-1),
        finished[1],
        finished[6].reshape(-1),
        finished[2],
        finished[7].reshape(-1),
        finished[3],
        finished[8].reshape(-1),
        finished[9],
        finished[10],
    )


def solution(mesh):
    planned = mesh.shape["tok"] == 4 and mesh.shape["bucket"] == 8
    return jax.shard_map(
        one_item_per_chip if planned else on_device,
        mesh=mesh,
        in_specs=(
            P("bucket", "tok", None),
            P("bucket", "tok", None),
            P("bucket"),
            P("bucket"),
            P(),
            P(),
            P("bucket", None),
            P(),
            P(),
            P(),
            P(),
            P(),
            P(),
            P(),
            P(),
            P(),
            P(None, "tok"),
            P("tok"),
        ),
        out_specs=(
            P("bucket", "tok", None),
            P("bucket", "tok", None),
            P("bucket", "tok"),
            P(("bucket", "tok")),
            P(("bucket", "tok")),
            P("bucket", "tok"),
            P(("bucket", "tok")),
            P("bucket", "tok"),
            P(("bucket", "tok")),
            P("bucket", "tok"),
            P(("bucket", "tok")),
            P("bucket", "tok"),
            P("bucket"),
        ),
        check_vma=False,
    )
```

```python
import functools
import math
import types

import jax
import jax.numpy as jnp
import numpy as np
from jax import lax
from jax.experimental import pallas as pl
from jax.experimental.pallas import tpu as pltpu
from jax.sharding import PartitionSpec as P

HEADS = 16
EPSILON = 1e-06
LOG2E = 1.4426950408889634
GELU_K = math.sqrt(2.0 / math.pi)
GELU_C = 0.044715
LANES = 128
bf16, f32 = jnp.bfloat16, jnp.float32


def dot_nn(a, b):
    return lax.dot_general(a, b, (((1,), (0,)), ((), ())), preferred_element_type=f32)


def dot_nt(a, b):
    return lax.dot_general(a, b, (((1,), (1,)), ((), ())), preferred_element_type=f32)


def dot_tn(a, b):
    return lax.dot_general(a, b, (((0,), (0,)), ((), ())), preferred_element_type=f32)


def step_embedding(timesteps, model_width):
    half_width = model_width // 2
    frequency = jnp.exp(-math.log(10000.0) * jnp.arange(half_width, dtype=jnp.float32) / half_width)
    angles = timesteps.astype(jnp.float32)[:, None] * frequency[None, :]
    return jnp.concatenate([jnp.cos(angles), jnp.sin(angles)], axis=1)


def normalize(values):
    centred = values - jnp.mean(values, axis=-1, keepdims=True)
    inverse = lax.rsqrt(jnp.mean(centred * centred, axis=-1, keepdims=True) + EPSILON)
    return (centred * inverse, inverse)


def normalize_back(incoming, normed, inverse):
    return inverse * (
        incoming
        - jnp.mean(incoming, axis=-1, keepdims=True)
        - normed * jnp.mean(incoming * normed, axis=-1, keepdims=True)
    )


D = 1152
DC, DZ, TD = D // 8, D // 4, D // 4
HD = D // HEADS
HC = HEADS // 2
WC = D // 2
FF = 4608
NF = 3
FB = FF // 2 // NF
FZ = FB // 4
L = 1024
LH = L // 2
LB = L // 4
G1R = 3 * DC
G2R = 2 * FZ + FZ // 4
GC = 96
GA, GB = G1R - GC, G2R - GC
PR = 2 * DC + DC // 3
PA = 176
WQ = 3 * WC // 2
TQ = WQ // 4
QR = 512
QA = QR // 2
VMEM_LIMIT = 58 * 1024 * 1024


ANY = pl.BlockSpec(memory_space=pl.ANY)
MESH = pl.DeviceIdType.MESH


def place():
    b, t = lax.axis_index("bucket"), lax.axis_index("tok")
    return b // 2, b % 2, t // 2, t % 2


def flip(value, other):
    return (value // 2 + other // 2) % 2 * 2 + (value % 2 + other % 2) % 2


def peer(name):
    z, c, y, x = place()
    if name == "x":
        x = 1 - x
    elif name == "y":
        y = 1 - y
    elif name == "xy":
        x, y = 1 - x, 1 - y
    elif name == "c":
        c = 1 - c
    elif name in ("t0", "t1"):
        c, y, x = y, c, x if name == "t0" else 1 - x
    else:
        z = flip(z, int(name[1]))
    return (z * 2 + c, y * 2 + x)


def greet(names):
    sem = pltpu.get_barrier_semaphore()
    for name in names:
        if name == "t0":
            continue
        pl.semaphore_signal(sem, inc=1, device_id=peer(name), device_id_type=MESH)
    if "t0" in names:
        _, c, y, _ = place()

        @pl.when(c != y)
        def _():
            pl.semaphore_signal(sem, inc=1, device_id=peer("t0"), device_id_type=MESH)


def meet(names):
    wanted = len([name for name in names if name != "t0"])
    if "t0" in names:
        _, c, y, _ = place()
        wanted = wanted + (c + y) % 2
    pl.semaphore_wait(pltpu.get_barrier_semaphore(), wanted)


def remote(src, dst, sems, k, name):
    return pltpu.make_async_remote_copy(
        src_ref=src, dst_ref=dst, send_sem=sems.at[0, k], recv_sem=sems.at[1, k],
        device_id=peer(name), device_id_type=MESH,
    )


def vm(*shape, dtype=bf16):
    return pltpu.VMEM(shape, dtype)


class Job:
    start_at = tick_at = 0

    def bind(self, scratch):
        return types.SimpleNamespace(**dict(zip(self.spec, scratch)))

    @property
    def scratch(self):
        return list(self.spec.values())


def sds(shape, dtype=bf16):
    return jax.ShapeDtypeStruct(shape, dtype)


def upto(sources, targets, sems):
    return [pltpu.make_async_copy(a, b, sems.at[k]) for k, (a, b) in enumerate(zip(sources, targets))]


def dma(*shape):
    return pltpu.SemaphoreType.DMA(shape)


def total_of(*parts):
    total = parts[0].astype(f32)
    for part in parts[1:]:
        total = total + part.astype(f32)
    return total


class FirstSum(Job):
    def __init__(self, keep_a, sent_a, keep_b, sent_b, third=None):
        self.third = third is not None
        self.peers = ("x", "y", "z1", "z2", "z3") if self.third else ("x", "y")
        self.ins = [keep_a, sent_a, keep_b, sent_b] + ([third] if self.third else [])
        a, b = keep_a.shape[1:], keep_b.shape[1:]
        self.outs = [sds(a), sds(a), sds(b), sds(b)]
        self.spec = dict(ka=vm(*a), ra=vm(*a), oa=vm(*a), kb=vm(*b), rb=vm(*b), ob=vm(*b), sems=dma(2, 7), local=dma(7))
        if self.third:
            c = third.shape[1:]
            self.outs += [sds(c[1:]), sds(c[1:])]
            self.spec.update(kc=vm(*c), rc=vm(3, *c))

    def plan(self, ins, outs, scratch):
        v = self.bind(scratch)
        far = [
            remote(ins[1].at[1], v.ra, v.sems, 0, "x"), remote(ins[3].at[1], v.rb, v.sems, 1, "y"),
            remote(ins[1].at[0], outs[1], v.sems, 2, "x"), remote(ins[3].at[0], outs[3], v.sems, 3, "y"),
        ]
        near = upto([ins[0].at[1], ins[2].at[1]], [v.ka, v.kb], v.local)
        if self.third:
            far += [remote(ins[4].at[k], v.rc.at[k - 1], v.sems, 3 + k, f"z{k}") for k in (3, 2, 1)]
            near.append(pltpu.make_async_copy(ins[4].at[0], v.kc, v.local.at[2]))
        return far, near

    def finish(self, ins, outs, scratch):
        v = self.bind(scratch)
        v.oa[...] = total_of(v.ka[...], v.ra[...]).astype(bf16)
        v.ob[...] = total_of(v.kb[...], v.rb[...]).astype(bf16)
        pairs = [(v.oa, outs[0]), (v.ob, outs[2])]
        if self.third:
            v.kc[...] = total_of(v.kc[...], v.rc[0], v.rc[1], v.rc[2]).astype(bf16)
            pairs += [(v.kc.at[0], outs[4]), (v.kc.at[1], outs[5])]
        return [pltpu.make_async_copy(a, b, v.local.at[3 + k]) for k, (a, b) in enumerate(pairs)]


def layer_sums(streams, zs, zk):
    start = 0
    for kv, qv, rv in streams:
        end = start + rv.shape[1]
        for j in range(4):
            total = total_of(kv[j], qv[j], rv[j])
            if j == 0:
                zk[start:end, :] = total
            else:
                zs[j - 1, start:end, :] = total.astype(bf16)
        start = end


class SecondSum(Job):
    peers = ("x", "y")

    def __init__(self, on_a, q_a, on_b, q_b, keep_a, keep_b, keep_c=None, sent_c=None, start_at=0):
        self.start_at = start_at
        self.third = keep_c is not None
        self.ins = [on_a, q_a, on_b, q_b, keep_a, keep_b] + ([keep_c, sent_c] if self.third else [])
        a, b = on_a.shape, on_b.shape
        rows_ = a[1] + b[1]
        self.outs = [sds((3, rows_, LANES)), sds((rows_, LANES), f32)]
        self.spec = dict(ka=vm(*a), qa=vm(*a), ra=vm(*a), kb=vm(*b), qb=vm(*b), rb=vm(*b), zs=vm(3, rows_, LANES),
                         zk=vm(rows_, LANES, dtype=f32), sems=dma(2, 3), local=dma(9))
        if self.third:
            c = keep_c.shape
            self.outs += [sds(c[1:]), sds(c[1:])]
            self.spec.update(kc=vm(*c), rc=vm(*c))

    def plan(self, ins, outs, scratch):
        v = self.bind(scratch)
        whole = [k.at[0] if len(k.shape) == 4 else k for k in ins[4:6]]
        far = [remote(ins[0], v.ra, v.sems, 0, "y"), remote(ins[2], v.rb, v.sems, 1, "x")]
        near = upto([whole[0], ins[1], whole[1], ins[3]], [v.ka, v.qa, v.kb, v.qb], v.local)
        if self.third:
            far.append(remote(ins[7], v.rc, v.sems, 2, "x"))
            near.append(pltpu.make_async_copy(ins[6], v.kc, v.local.at[4]))
        return far, near

    def add(self, v):
        layer_sums([(v.ka, v.qa, v.ra), (v.kb, v.qb, v.rb)], v.zs, v.zk)
        if self.third:
            v.kc[...] = total_of(v.kc[...], v.rc[...]).astype(bf16)

    def finish(self, ins, outs, scratch):
        v = self.bind(scratch)
        self.add(v)
        pairs = [(v.zs, outs[0]), (v.zk, outs[1])]
        if self.third:
            pairs += [(v.kc.at[0], outs[2]), (v.kc.at[1], outs[3])]
        return [pltpu.make_async_copy(a, b, v.local.at[5 + k]) for k, (a, b) in enumerate(pairs)]


class ThirdSum(Job):
    def __init__(self, sent, kept, keep_c=None, sent_c=None):
        self.third = keep_c is not None
        self.peers = ("z1", "z2", "z3", "y") if self.third else ("z1", "z2", "z3")
        self.ins = [sent, kept] + ([keep_c, sent_c] if self.third else [])
        self.outs = [sds(kept.shape, f32)]
        self.spec = dict(got=vm(*sent.shape), kept=vm(*kept.shape, dtype=f32), sems=dma(2, 4), local=dma(4))
        if self.third:
            self.outs.append(sds(keep_c.shape, f32))
            self.spec.update(kc=vm(*keep_c.shape), rc=vm(*keep_c.shape), fc=vm(*keep_c.shape, dtype=f32))

    def plan(self, ins, outs, scratch):
        v = self.bind(scratch)
        far = [remote(ins[0].at[k], v.got.at[k], v.sems, k, f"z{k + 1}") for k in (2, 1, 0)]
        near = [pltpu.make_async_copy(ins[1], v.kept, v.local.at[0])]
        if self.third:
            far.append(remote(ins[3], v.rc, v.sems, 3, "y"))
            near.append(pltpu.make_async_copy(ins[2], v.kc, v.local.at[1]))
        return far, near

    def finish(self, ins, outs, scratch):
        v = self.bind(scratch)
        v.kept[...] = total_of(v.kept[...], v.got[0], v.got[1], v.got[2])
        pairs = [(v.kept, outs[0])]
        if self.third:
            v.fc[...] = total_of(v.kc[...], v.rc[...])
            pairs.append((v.fc, outs[1]))
        return [pltpu.make_async_copy(a, b, v.local.at[2 + k]) for k, (a, b) in enumerate(pairs)]


class SecondThird(SecondSum):
    peers = ("x", "y", "z1", "z2", "z3")

    def __init__(self, *args, start_at=0, tick_at=1):
        super().__init__(*args, start_at=start_at)
        self.tick_at = tick_at
        kept, c = self.outs[1], self.spec["kc"].shape[1:]
        self.outs = [kept, sds(c, f32)]
        self.spec.update(got=vm(3, *kept.shape), sems3=dma(2, 4), rc3=vm(*c), fc=vm(*c, dtype=f32))

    def next_copies(self, v):
        far = [remote(v.zs.at[k], v.got.at[k], v.sems3, k, f"z{k + 1}") for k in (2, 1, 0)]
        return far + [remote(v.kc.at[1], v.rc3, v.sems3, 3, "y")]

    def tick(self, ins, outs, scratch):
        v = self.bind(scratch)
        for group in self.plan(ins, outs, scratch):
            for copy in group:
                copy.wait()
        self.add(v)
        for copy in self.next_copies(v):
            copy.start()

    def settle(self, ins, outs, scratch):
        return self.next_copies(self.bind(scratch))

    def finish(self, ins, outs, scratch):
        v = self.bind(scratch)
        v.zk[...] = total_of(v.zk[...], v.got[0], v.got[1], v.got[2])
        v.fc[...] = total_of(v.kc[0], v.rc3[...])
        return upto([v.zk, v.fc], outs, v.local)


class FirstSecond(Job):
    peers = ("x", "y")

    def __init__(self, keep_a, sent_a, keep_b, sent_b, start_at=0, tick_at=1):
        self.start_at, self.tick_at = start_at, tick_at
        self.ins = [keep_a, sent_a, keep_b, sent_b]
        a, b = keep_a.shape, keep_b.shape
        rows_ = a[2] + b[2]
        self.outs = [sds((3, rows_, LANES)), sds((rows_, LANES), f32)]
        self.spec = dict(ka=vm(*a), ra=vm(*a), oa=vm(*a[1:]), ra2=vm(*a[1:]), kb=vm(*b), rb=vm(*b), ob=vm(*b[1:]),
                         rb2=vm(*b[1:]), zs=vm(3, rows_, LANES), zk=vm(rows_, LANES, dtype=f32), sems=dma(2, 6), local=dma(4))

    def plan(self, ins, outs, scratch):
        v = self.bind(scratch)
        far = [
            remote(ins[1].at[1], v.ra.at[1], v.sems, 0, "x"), remote(ins[3].at[1], v.rb.at[1], v.sems, 1, "y"),
            remote(ins[1].at[0], v.ra.at[0], v.sems, 2, "x"), remote(ins[3].at[0], v.rb.at[0], v.sems, 3, "y"),
        ]
        return far, upto([ins[0], ins[2]], [v.ka, v.kb], v.local)

    def next_copies(self, v):
        return [remote(v.oa, v.ra2, v.sems, 4, "y"), remote(v.ob, v.rb2, v.sems, 5, "x")]

    def tick(self, ins, outs, scratch):
        v = self.bind(scratch)
        for group in self.plan(ins, outs, scratch):
            for copy in group:
                copy.wait()
        v.oa[...] = total_of(v.ka[1], v.ra[1]).astype(bf16)
        v.ob[...] = total_of(v.kb[1], v.rb[1]).astype(bf16)
        for copy in self.next_copies(v):
            copy.start()

    def settle(self, ins, outs, scratch):
        return self.next_copies(self.bind(scratch))

    def finish(self, ins, outs, scratch):
        v = self.bind(scratch)
        layer_sums([(v.ka.at[0], v.ra.at[0], v.ra2), (v.kb.at[0], v.rb.at[0], v.rb2)], v.zs, v.zk)
        return [pltpu.make_async_copy(a, b, v.local.at[2 + k]) for k, (a, b) in enumerate(((v.zs, outs[0]), (v.zk, outs[1])))]


class GoHome(Job):
    peers = ("t0", "t1")

    def __init__(self, values, tick_at=1):
        self.tick_at = tick_at
        self.ins = [values]
        self.outs = [jax.ShapeDtypeStruct((2, LB, D), values.dtype)]
        self.spec = dict(sems=dma(2, 2), local=pltpu.SemaphoreType.DMA)

    def plan(self, ins, outs, scratch):
        return [], []

    def tick(self, ins, outs, scratch):
        home_start(*self.copies(ins, outs, scratch))

    def copies(self, ins, outs, scratch):
        return homeward(ins[0].at[pl.ds(0, LB)], ins[0].at[pl.ds(LB, LB)], outs[0], *scratch)

    def settle(self, ins, outs, scratch):
        home_wait(*self.copies(ins, outs, scratch))
        return []

    def finish(self, ins, outs, scratch):
        return []


def homeward(first, second, dst, sems, local):
    x = place()[3]
    return (
        remote(first, dst.at[x], sems, 0, "t0"),
        pltpu.make_async_copy(first, dst.at[x], local),
        remote(second, dst.at[x], sems, 1, "t1"),
    )


def home_start(away, stay, second):
    _, c, y, _ = place()
    pl.when(c != y)(away.start)
    pl.when(c == y)(stay.start)
    second.start()


def home_wait(away, stay, second):
    _, c, y, _ = place()
    pl.when(c != y)(away.wait)
    pl.when(c == y)(stay.wait)
    second.wait()


def call(kernel, name, out_shape, args, in_specs=None, out_specs=None, scratch=(), grid=None,
         peers=(), jobs=(), cid=None, ticks=False, flops=0, nbytes=0):
    whole = pl.BlockSpec(memory_space=pltpu.VMEM)
    single = not isinstance(out_shape, (tuple, list))
    out_shape = [out_shape] if single else list(out_shape)
    in_specs = list(in_specs) if in_specs is not None else [whole] * len(args)
    out_specs = [whole] * len(out_shape) if out_specs is None else [out_specs] if single else list(out_specs)
    counts = [len(args), sum(len(j.ins) for j in jobs), len(out_shape), sum(len(j.outs) for j in jobs), len(scratch)]
    names = sorted(set(peers).union(*[j.peers for j in jobs]))

    def run(*refs):
        groups, at = [], 0
        for n in counts:
            groups.append(refs[at : at + n])
            at += n
        bound, ai, ao, asc = [], 0, 0, at
        for j in jobs:
            bound.append((
                j, groups[1][ai : ai + len(j.ins)], groups[3][ao : ao + len(j.outs)], refs[asc : asc + len(j.scratch)]
            ))
            ai, ao, asc = ai + len(j.ins), ao + len(j.outs), asc + len(j.scratch)

        def ready():
            if names:
                meet(names)
            for j, *r in bound:
                if not j.start_at:
                    j_start(j, r)

        def j_start(j, r):
            for group in j.plan(*r):
                for copy in group:
                    copy.start()

        def tick(k):
            for j, *r in bound:
                if j.tick_at == k:
                    j.tick(*r)
            for j, *r in bound:
                if j.start_at == k:
                    j_start(j, r)

        def end():
            last = []
            for j, *r in bound:
                far, near = (j.settle(*r), []) if j.tick_at else j.plan(*r)
                for copy in far:
                    copy.wait()
                for copy in near:
                    copy.wait()
                copies = j.finish(*r)
                for copy in copies:
                    copy.start()
                last += copies
            for copy in last:
                copy.wait()

        if names:
            greet(names)
            kernel(*groups[0], *groups[2], *groups[4], ready=ready, **({"tick": tick} if ticks else {}))
            end()
        else:
            kernel(*groups[0], *groups[2], *groups[4])

    extra = {} if grid is None else {"grid": grid}
    params = {"collective_id": cid, "has_side_effects": True} if names else {}
    outs = pl.pallas_call(
        run,
        out_shape=out_shape + [o for j in jobs for o in j.outs],
        in_specs=in_specs + [ANY] * counts[1],
        out_specs=out_specs + [ANY] * counts[3],
        scratch_shapes=list(scratch) + [q for j in jobs for q in j.scratch],
        compiler_params=pltpu.CompilerParams(vmem_limit_bytes=VMEM_LIMIT, **params),
        cost_estimate=pl.CostEstimate(flops=int(flops), bytes_accessed=int(nbytes), transcendentals=0),
        name=name,
        **extra,
    )(*args, *[a for j in jobs for a in j.ins])
    own, rest, given = outs[: len(out_shape)], outs[len(out_shape) :], []
    for j in jobs:
        given.append(rest[: len(j.outs)])
        rest = rest[len(j.outs) :]
    return (own[0] if single else own), given


def full(shape):
    return pl.BlockSpec(shape, lambda *_: (0,) * len(shape))


def once(*shape):
    return pl.BlockSpec(shape, lambda *_: (0,) * len(shape), pipeline_mode=pl.Buffered(1))


def rows(block, width):
    return pl.BlockSpec((block, width), lambda i: (i, 0))


def arrivals(src, dst, tsems, csems, locals_, pieces=1):
    x = place()[3]
    n = LB // pieces
    moves = []
    for k in range(pieces):
        rows_ = pl.ds(n * k, n)
        here = [dst.at[pl.ds(LB * j + n * k, n)] for j in range(4)]
        moves.append((
            remote(src.at[x, rows_], here[0], tsems, 2 * k, "t0"),
            pltpu.make_async_copy(src.at[x, rows_], here[0], locals_.at[k]),
            remote(src.at[1 - x, rows_], here[1], tsems, 2 * k + 1, "t1"),
            [remote(here[j], here[2 + j], csems, 2 * k + j, "c") for j in range(2)],
        ))
    return moves


def leave(first, stay, second, onward):
    _, c, y, _ = place()
    pl.when(c != y)(first.start)
    pl.when(c == y)(stay.start)
    second.start()


def pass_on(first, stay, second, onward):
    _, c, y, _ = place()
    pl.when(c != y)(first.wait_recv)
    pl.when(c == y)(stay.wait)
    onward[0].start()
    second.wait_recv()
    onward[1].start()


def settle(first, stay, second, onward):
    _, c, y, _ = place()
    pl.when(c != y)(first.wait_send)
    second.wait_send()
    for copy in onward:
        copy.wait_send()


def column(n):
    return lax.broadcasted_iota(jnp.int32, (n, 1), 0)


def front_kernel(tokens, timesteps, bucket_ids, skips, ada_w, ada_b, head_masks, channel_masks, w_qkv, w_fc1,
                 q_bias, v_bias, b1, freq, tok_o, shifted_o, qkv_o, wq_o, w1_o, mod_o, kept_o, hmask_o, chan_o, b1_o,
                 tk, wqv, wqc, w1v, w1c, adav, ints, ints_other, m4, to_send, shares, shv, qkvv, csems, tsems, ssems, lsems, ready):
    z, c, y, x = place()
    t = 2 * y + x
    loads = [
        pltpu.make_async_copy(a, b, lsems.at[k])
        for k, (a, b) in enumerate(((ada_w, adav), (w_qkv, wqv), (w_fc1, w1v)))
    ]

    pieces = 2
    tok_moves = arrivals(tokens, tk, tsems, csems, lsems.at[pl.ds(6, pieces)], pieces)
    ready()
    for moves in tok_moves:
        leave(*moves)
    halves = [skips[:, :LANES], skips[:, LANES:]]
    ints[0:4, :] = jnp.concatenate([halves[0][0:1], halves[1][0:1], halves[0][1:2], halves[1][1:2]], axis=0)
    for k, value in enumerate((timesteps[0], timesteps[1], bucket_ids[0], 0)):
        ints[4 + k : 5 + k, :] = jnp.full((1, LANES), value, jnp.int32)
    swap = remote(ints, ints_other, csems, 2 * pieces, "c")
    swap.start()
    for load in loads:
        load.start()
    swap.wait()

    mine, other = ints[...], ints_other[...]
    r = column(8)
    steps = jnp.zeros((8, 1), f32)
    for k in range(2):
        steps = jnp.where(r == 2 * c + k, mine[4 + k : 5 + k, 0:1].astype(f32), steps)
        steps = jnp.where(r == 2 * (1 - c) + k, other[4 + k : 5 + k, 0:1].astype(f32), steps)
    angles = steps * freq[...]
    condition = jax.nn.silu(jnp.concatenate([jnp.cos(angles), jnp.sin(angles)], axis=1))
    condition = jnp.concatenate([condition, jnp.zeros_like(condition)], axis=0).astype(bf16)
    loads[0].wait()
    m4[...] = dot_nt(condition, adav[...])[:8] + ada_b[...].astype(f32).reshape(1, -1)
    moves = []
    for k in range(4):
        to = (y + k // 2) % 2 * 2 + (x + k) % 2
        row = jnp.broadcast_to(m4[pl.ds(to, 1), :], to_send.shape[1:])
        if k == 0:
            shares[t] = row
        else:
            to_send[k - 1] = row
            moves.append(remote(to_send.at[k - 1], shares.at[t], ssems, k - 1, ("x", "y", "xy")[k - 1]))
            moves[-1].start()

    group = jnp.where(c == y, mine, other)
    bucket = group[6:7, 0:1]
    skip = jnp.where(x == 0, group[0:2], group[2:4])
    for j in range(4):
        block = 2 * ((c + j // 2) % 2) + (x + j) % 2
        position = column(LB) + LB * block
        hit = jnp.where((position == skip[0:1, :]) | (position == skip[1:2, :]), 1.0, 0.0)
        kept_o[LB * j : LB * (j + 1), :] = 1.0 - jnp.max(hit, axis=1, keepdims=True)

    def chosen(masks):
        line = lax.broadcasted_iota(jnp.int32, masks.shape, 0)
        row = jnp.sum(jnp.where(line == bucket, masks[...].astype(f32), 0.0), axis=0, keepdims=True)
        return jnp.broadcast_to(row, (16, masks.shape[1])).astype(bf16)

    def spread(on, low, width):
        first = width * lax.broadcasted_iota(jnp.int32, (on.shape[1], low.shape[1]), 0)
        return dot_nn(on, jnp.where((low >= first) & (low < first + width), 1.0, 0.0).astype(bf16))[0:1, :]

    lane = lax.broadcasted_iota(jnp.int32, (1, WC), 1)
    share = sum(jnp.where(lane >= DC * k, 1, 0) for k in range(1, 4))
    hmask_o[...] = spread(chosen(head_masks), lane + DC * (share + c), HD)
    channels = chosen(channel_masks)
    lane = lax.broadcasted_iota(jnp.int32, (1, FB), 1)
    share = sum(jnp.where(lane >= FZ * k, 1, 0) for k in range(1, 4))
    for f in range(NF):
        low = lane + (4 * DZ - FZ) * share + FF // 8 * c + FZ * f
        chan_o[f] = spread(channels, low, FF // channels.shape[1])

    def half(v, k, width):
        v = v[:, 2 * width * k : 2 * width * (k + 1)]
        return jnp.where(c == 0, v[:, :width], v[:, width:])

    def line(ref):
        return ref[...].astype(f32).reshape(1, -1)

    def parity(v, odd):
        return [half(v, k, DC)[:, HD * odd : HD * (odd + 1)] for k in range(4)]

    bias = []
    for odd in range(2):
        bias += parity(line(q_bias), odd) + [jnp.zeros((1, DZ), f32)] + parity(line(v_bias), odd)
    bias = jnp.concatenate(bias, axis=1)
    b1v = [half(line(b1), k, FF // 8) for k in range(4)]
    for f in range(NF):
        b1_o[f] = jnp.concatenate([v[:, FZ * f : FZ * (f + 1)] for v in b1v], axis=1)
    loads[1].wait()
    loads[2].wait()
    for core in range(2):

        @pl.when(c == core)
        def _():
            for odd in range(2):
                for k in range(12):
                    to, start = WQ * odd + HD * k, DZ * k + DC * core + HD * odd
                    wqc[:, to : to + HD] = wqv[:, start : start + HD]
            for f in range(NF):
                for k in range(4):
                    start = 4 * DZ * k + FF // 8 * core + FZ * f
                    w1c[f, :, FZ * k : FZ * (k + 1)] = w1v[:, start : start + FZ]

    stores = [
        pltpu.make_async_copy(a, b, lsems.at[k]) for k, (a, b) in enumerate(((wqc, wq_o), (w1c, w1_o)))
    ]
    for store in stores:
        store.start()
    for copy in moves:
        copy.wait()
    share_rows = [shares[k][0:1, :] for k in range(4)]
    n, m = D // 2, 3 * D // 2
    mod = [share_rows[0][:, :D], jnp.concatenate([share_rows[0][:, D:], share_rows[1][:, :n]], axis=1),
           share_rows[1][:, n:], share_rows[2][:, :D],
           jnp.concatenate([share_rows[2][:, D:], share_rows[3][:, :n]], axis=1), share_rows[3][:, n:]]
    own_step = 0.5 * jnp.sum(jnp.where(r == t, steps, 0.0), axis=0, keepdims=True)
    mod += [jnp.broadcast_to(own_step, (1, D)), jnp.zeros((1, D), f32)]
    mod_o[...] = jnp.concatenate(mod, axis=0)
    n = LB // pieces

    def make(side, k):
        parts = [slice(LH * side + LB * j + n * k, LH * side + LB * j + n * (k + 1)) for j in range(2)]
        normed, _ = normalize(jnp.concatenate([tk[part, :] for part in parts], axis=0).astype(f32))
        shifted = (normed * (1.0 + mod[1]) + mod[0]).astype(bf16)
        made = (dot_nn(shifted, wqc[...]) + bias).astype(bf16)
        for j, part in enumerate(parts):
            shv[part, :] = shifted[n * j : n * (j + 1)]
            qkvv[part, :] = made[n * j : n * (j + 1)]

    kept_rows = []

    def keep_half(side):
        part = pl.ds(LH * side, LH)
        for k, (a, b) in enumerate(((shv, shifted_o), (qkvv, qkv_o), (tk, tok_o))):
            copy = pltpu.make_async_copy(a.at[part], b.at[part], ssems.at[side, 3 + k])
            copy.start()
            kept_rows.append(copy)

    for k in range(pieces):
        pass_on(*tok_moves[k])
        make(0, k)
    keep_half(0)
    for k in range(pieces):
        for copy in tok_moves[k][3]:
            copy.wait_recv()
        make(1, k)
    keep_half(1)
    for one in tok_moves:
        settle(*one)
    for copy in stores + kept_rows:
        copy.wait()


def attn_kernel(step, cotangent, qkv, hmask, wp, bias, tok, mod, cot_o, mixed_o, shifted2_o, attn_o,
                ck, qkvv, qh, kh, vh, mx, mo, wpv, tkv, csems, tsems, osems, lsems, ready):
    c = place()[1]
    loads = [
        pltpu.make_async_copy(wp.at[:, c], wpv.at[0], lsems.at[0]),
        pltpu.make_async_copy(wp.at[:, 1 - c], wpv.at[1], lsems.at[1]),
        pltpu.make_async_copy(tok, tkv, lsems.at[2]),
        pltpu.make_async_copy(qkv, qkvv, lsems.at[4]),
    ]
    for load in loads[::-1]:
        load.start()
    cot_moves = arrivals(cotangent, ck, tsems, osems, lsems.at[pl.ds(5, 1)])[0]
    scale = LOG2E / math.sqrt(HD)
    loads.pop().wait()
    for h in range(HC):
        for k, ref in enumerate((qh, kh, vh)):
            start = WQ * (h % 2) + DZ * k + HD * (h // 2)
            ref[h, :, :HD] = qkvv[:, start : start + HD]
        vh[h, :, HD:] = jnp.ones((L, LANES - HD), bf16)
    ready()
    leave(*cot_moves)

    def crossing(i):
        src = mx.at[pl.ds(pl.multiple_of(i * step, step), step)]
        dst = mo.at[pl.ds(pl.multiple_of((i * step + LH) % L, step), step)]
        return remote(src, dst, csems, i, "c")

    def body(i, carry):
        part = pl.ds(pl.multiple_of(i * step, step), step)
        outs = []
        for h in range(HC):
            s = dot_nt(qh[h, part, :], kh[h])
            top = jnp.max(s, axis=1, keepdims=True)
            p = jnp.exp2((s - top) * scale)
            o = dot_nn(p.astype(bf16), vh[h])
            outs.append(o[:, :HD] * (1.0 / o[:, HD : HD + 1]))
        mx[part, :] = (jnp.concatenate(outs, axis=1) * hmask[...]).astype(bf16)
        crossing(i).start()
        return carry

    lax.fori_loop(0, L // step, body, 0)
    keep = pltpu.make_async_copy(mx, mixed_o, lsems.at[3])
    keep.start()
    pass_on(*cot_moves)
    for load in loads:
        load.wait()
    for i in range(L // step):
        crossing(i).wait()
    w_mine, w_other = wpv[0].reshape(WC, D), wpv[1].reshape(WC, D)
    bias_line = bias[...].astype(f32).reshape(1, D)
    for j in range(4):
        part = slice(LB * j, LB * (j + 1))
        attn = dot_nn(mx[part, :], w_mine) + dot_nn(mo[part, :], w_other) + bias_line
        if j < 2:
            attn_o[part, :] = attn
        normed, _ = normalize(tkv[part, :].astype(f32) + mod[2:3, :] * attn)
        shifted2_o[part, :] = (normed * (1.0 + mod[4:5, :]) + mod[3:4, :]).astype(bf16)
    for copy in cot_moves[3]:
        copy.wait_recv()
    keep_cot = pltpu.make_async_copy(ck, cot_o, lsems.at[6])
    keep_cot.start()
    settle(*cot_moves)
    keep.wait()
    keep_cot.wait()


def mlp_kernel(sh2, g, kept, mod, w1, b1, chan, w2,
               on_a0, q_a0, on_b0, q_b0, keep_a0, keep_b0, keep_c0, send_c0,
               on_a1, q_a1, on_b1, q_b1, keep_a1, keep_b1, keep_c1, send_c1,
               k2a, s2a, k2b, s2b, c2, branch_o, ds2_o, branch_r, ds2_r, sum1_o, sum2_o,
               sh2v, dbs, w1v, w2v, hid, dpre, slope, br, ds, far, tt_, ka, sa, kb, sb, cz, cr, ra, rb, ona, onb,
               fsems, csems, lsems, wsems, osems, ready):
    z, c, y, x = place()
    out0 = (on_a0, q_a0, on_b0, q_b0, keep_a0, keep_b0, keep_c0, send_c0)
    out1 = (on_a1, q_a1, on_b1, q_b1, keep_a1, keep_b1, keep_c1, send_c1)
    outs = (out0, out1)

    def weights(f):
        return [
            pltpu.make_async_copy(w1.at[f], w1v.at[f % 2], wsems.at[0, f % 2]),
            pltpu.make_async_copy(w2.at[:, c, f], w2v.at[f % 2], wsems.at[1, f % 2]),
        ]

    def first(f):
        k, out = f % 2, outs[f]
        return [
            remote(sa.at[k, 1], ra.at[k], fsems, 10 * k, "x"), remote(sb.at[k, 1], rb.at[k], fsems, 10 * k + 1, "y"),
            remote(sa.at[k, 0], out[1], fsems, 10 * k + 2, "x"), remote(sb.at[k, 0], out[3], fsems, 10 * k + 3, "y"),
        ] + [
            remote(cz.at[k, j, :, :, pl.ds(GC * half, GC)], cr.at[k, j - 1, :, :, pl.ds(GC * half, GC)], fsems,
                   10 * k + 3 + 3 * half + j, f"z{j}")
            for half in range(2) for j in (3, 2, 1)
        ]

    def stored(f):
        k = f % 2
        if f == NF - 1:
            pairs = ((ka.at[k], k2a), (sa.at[k], s2a), (kb.at[k], k2b), (sb.at[k], s2b), (cz.at[k], c2))
        else:
            pairs = ((ka.at[k, 0], outs[f][4]), (kb.at[k, 0], outs[f][5]))
        return [pltpu.make_async_copy(src, dst, osems.at[k, j]) for j, (src, dst) in enumerate(pairs)]

    def onward(f):
        k = f % 2
        for copy in first(f):
            copy.wait()
        for kv, rv, on in ((ka, ra, ona), (kb, rb, onb)):
            on[k] = total_of(kv[k, 1], rv[k]).astype(bf16)
        cz[k, 0] = total_of(cz[k, 0], cr[k, 0], cr[k, 1], cr[k, 2]).astype(bf16)
        pairs = (
            (ona.at[k], outs[f][0]), (onb.at[k], outs[f][2]), (cz.at[k, 0, 0], outs[f][6]), (cz.at[k, 0, 1], outs[f][7])
        )
        copies = [pltpu.make_async_copy(src, dst, osems.at[k, 5 + j]) for j, (src, dst) in enumerate(pairs)]
        for copy in copies:
            copy.start()
        return copies

    loads = [pltpu.make_async_copy(src, dst, lsems.at[k]) for k, (src, dst) in enumerate(((g, dbs), (sh2, sh2v)))]
    for copy in loads + weights(0):
        copy.start()
    loads[0].wait()
    sum2 = jnp.zeros((1, D), f32)
    for j in range(4):
        part = slice(LB * j, LB * (j + 1))
        db = (dbs[part, :].astype(f32) * mod[5:6, :] * kept[part, :]).astype(bf16)
        dbs[part, :] = db
        sum2 += jnp.sum(db.astype(f32), axis=0, keepdims=True)
    sum2_o[...] = sum2
    loads[1].wait()
    crossing = [remote(far.at[j], dst, csems, j, "c") for j, dst in enumerate((branch_r, ds2_r))]
    waiting = []
    for f in range(NF):
        for copy in weights(f):
            copy.wait()
        if f + 1 < NF:
            for copy in weights(f + 1):
                copy.start()
        w1f, w2f = w1v[f % 2], w2v[f % 2].reshape(FB, D)
        on = chan[f]
        k = f % 2
        for side in (1, 0):
            part = slice(LH * side, LH * (side + 1))
            v = dot_nn(sh2v[part, :], w1f) + b1[f]
            v2 = v * v
            th = jnp.tanh(GELU_K * v * (1.0 + GELU_C * v2))
            half = 0.5 * (1.0 + th)
            hid[part, :] = (v * half * on).astype(bf16)
            slope[part, :] = (
                (half + (0.5 * GELU_K) * v * (1.0 - th * th) * (1.0 + (3.0 * GELU_C) * v2)) * on
            ).astype(bf16)
        for m in range(2):
            cut = slice(m * FB // 2, (m + 1) * FB // 2)
            p = dot_tn(hid[:, cut], dbs[...]).astype(bf16)
            for t in range(4):
                tt_[t, cut, :] = p[:, TD * t : TD * (t + 1)]
        for rz in range(4):
            zz = flip(z, rz)
            for ry in range(2):
                for rx in range(2):
                    tt = (ry + y) % 2 * 2 + (rx + x) % 2
                    o = (kb, sb)[ry]
                    block = tt_[tt, pl.ds(pl.multiple_of(zz * FZ, 16), FZ), :]
                    o[k, rx, rz, :FZ, :] = block[:, :LANES]
                    o[k, rx, rz, FZ:, :] = block[: GB - FZ, LANES : 2 * LANES]
                    q = FZ // 4
                    cz[k, rz, rx, ry, GC : GC + 2 * FZ - GB, :] = block[GB - FZ :, LANES : 2 * LANES]
                    cz[k, rz, rx, ry, GC + 2 * FZ - GB :, :] = jnp.concatenate(
                        [block[q * j : q * (j + 1), 2 * LANES :] for j in range(4)], axis=1
                    )
        if f == 0:
            ready()
        if f < NF - 1:
            for copy in first(f)[1:4:2] + first(f)[7:]:
                copy.start()
        sum1 = jnp.zeros((1, FB), f32)
        for side in (1, 0):
            part = slice(LH * side, LH * (side + 1))
            d_pre = (dot_nt(dbs[part, :], w2f) * slope[part, :].astype(f32)).astype(bf16)
            dpre[part, :] = d_pre
            sum1 += jnp.sum(d_pre.astype(f32), axis=0, keepdims=True)
        sum1_o[f] = sum1
        for m in range(3):
            cut = slice(m * D // 3, (m + 1) * D // 3)
            p = dot_tn(sh2v[:, cut], dpre[...]).astype(bf16)
            for t in range(4):
                tt_[t, cut, :FZ] = p[:, FZ * t : FZ * (t + 1)]
        for rz in range(4):
            zz = flip(z, rz)
            for ry in range(2):
                for rx in range(2):
                    tt = (ry + y) % 2 * 2 + (rx + x) % 2
                    o = (ka, sa)[rx]
                    tails = []
                    for rc in range(2):
                        block = tt_[tt, pl.ds(pl.multiple_of(zz * DZ + (rc + c) % 2 * DC, 16), DC), :FZ]
                        o[k, ry, rz, DC * rc : DC * (rc + 1), :] = block[:, :LANES]
                        tails.append(block[:, LANES:])
                    tail = jnp.concatenate(tails, axis=1)
                    o[k, ry, rz, 2 * DC :, :] = tail[: GA - 2 * DC]
                    cz[k, rz, rx, ry, :GC, :] = tail[GA - 2 * DC :]
        if f < NF - 1:
            for copy in first(f)[0:4:2] + first(f)[4:7]:
                copy.start()
        for copy in stored(f):
            copy.start()
        for side in (1, 0):
            part = slice(LH * side, LH * (side + 1))
            branch, ds2 = dot_nn(hid[part, :], w2f), dot_nt(dpre[part, :], w1f)
            if f > 0:
                branch, ds2 = branch + br[part, :], ds2 + ds[part, :]
            if f < NF - 1:
                br[part, :] = branch
                ds[part, :] = ds2
            elif side == 1:
                far[0] = branch.astype(bf16)
                far[1] = ds2.astype(bf16)
                for copy in crossing:
                    copy.start()
            else:
                branch_o[...] = branch.astype(bf16)
                ds2_o[...] = ds2.astype(bf16)
        waiting += stored(f)
        if f > 0:
            waiting += onward(f - 1)
        if f == NF - 2:
            for copy in waiting:
                copy.wait()
            waiting = []
    for copy in waiting + crossing:
        copy.wait()


def middle_kernel(ds, ds_r, br, br_r, attn, tok, g, kept, mod, bias2, mixed, wp,
                  d_resid_o, out_o, dh_o, pka, psa, pkb, psb, sums_o, sum_o,
                  dsv, attnv, tokv, mixv, wpv, da, t1, csems, lsems, ready):
    z, c, y, x = place()
    n = LH // 4
    near = pl.ds(0, LH)
    loads = [
        pltpu.make_async_copy(src, dst, lsems.at[k])
        for k, (src, dst) in enumerate(
            ((tok.at[near], tokv.at[0]), (attn, attnv), (ds, dsv.at[0]), (ds_r, dsv.at[1]), (br, dsv.at[2]),
             (br_r, dsv.at[3]), (g.at[near], tokv.at[1]), (wp.at[:, c], wpv), (mixed, mixv))
        )
    ]
    for load in loads:
        load.start()
    ready()
    crossing = [remote(da.at[pl.ds(n * k, n)], da.at[pl.ds(LH + n * k, n)], csems, k, "c") for k in range(4)]
    sums = jnp.zeros((4, D), f32)
    bias_line = bias2[...].astype(f32).reshape(1, D)
    for load in loads[:7]:
        load.wait()
    for k in range(4):
        part = slice(n * k, n * (k + 1))
        gf, at = tokv[1, part, :].astype(f32), attnv[part, :]
        resid = tokv[0, part, :].astype(f32) + mod[2:3, :] * at
        normed2, inverse2 = normalize(resid)
        ds2 = dsv[0, part, :].astype(f32) + dsv[1, part, :].astype(f32)
        kb = kept[part, :] * (dsv[2, part, :].astype(f32) + dsv[3, part, :].astype(f32) + bias_line)
        out_o[part, :] = (resid + mod[5:6, :] * kb).astype(bf16)
        d_resid = gf + normalize_back(ds2 * (1.0 + mod[4:5, :]), normed2, inverse2)
        d_resid_o[part, :] = d_resid
        da[part, :] = (mod[2:3, :] * d_resid).astype(bf16)
        crossing[k].start()
        sums += jnp.concatenate(
            [jnp.sum(p, axis=0, keepdims=True) for p in (at * d_resid, ds2, ds2 * normed2, kb * gf)], axis=0
        )
    sums_o[...] = jnp.concatenate([sums, jnp.zeros((4, D), f32)], axis=0)
    for load in loads[7:]:
        load.wait()
    for copy in crossing:
        copy.wait()
    wv = wpv[...].reshape(WC, D)
    dh_o[...] = dot_nt(da[...], wv).astype(bf16)
    sum_o[...] = dot_nn(jnp.ones((16, L), bf16), da[...])[:8]
    grad = dot_tn(mixv[...], da[...]).astype(bf16)
    for t in range(4):
        t1[t] = grad[:, TD * t : TD * (t + 1)]
    for rz in range(4):
        zz = flip(z, rz)
        for ry in range(2):
            for rx in range(2):
                tt = (ry + y) % 2 * 2 + (rx + x) % 2
                a, b = (pka, psa)[rx], (pkb, psb)[ry]
                block = t1[tt, pl.ds(pl.multiple_of(zz * DC, 16), DC), :]
                a[ry, rz, :DC, :] = block[:, :LANES]
                a[ry, rz, DC:, :] = block[: PA - DC, LANES : 2 * LANES]
                b[rx, rz, : 2 * DC - PA, :] = block[PA - DC :, LANES : 2 * LANES]
                q = DC // 3
                tails = [block[q * k : q * (k + 1), 2 * LANES :] for k in range(3)]
                tails.append(jnp.zeros((q, 32), bf16))
                b[rx, rz, 2 * DC - PA :, :] = jnp.concatenate(tails, axis=1)


def qkv_slots(dqkv, shifted, extra, t1, ka, sa, kb, sb):
    z, _, y, x = place()
    grad = dot_tn(dqkv, shifted)
    for t in range(4):
        for zz in range(4):
            t1[t, zz] = grad[TQ * t : TQ * (t + 1), DZ * zz : DZ * (zz + 1)]
    q = TQ // 3
    for rz in range(4):
        zz = flip(z, rz)
        for ry in range(2):
            for rx in range(2):
                tt = (ry + y) % 2 * 2 + (rx + x) % 2
                block = t1[tt, zz]
                tails = [block[q * k : q * (k + 1), 2 * LANES :] for k in range(3)] + [jnp.zeros((q, 32), f32)]
                more = jnp.zeros((8, LANES), f32) if extra is None else extra[zz, tt]
                slot = [block[:, :LANES], block[:, LANES : 2 * LANES], jnp.concatenate(tails, axis=1), more]
                slot = jnp.concatenate(slot, axis=0).astype(bf16)
                (ka, sa)[rx][ry, rz] = slot[:QA]
                (kb, sb)[ry][rx, rz] = slot[QA:]


def column_sums(dqkv):
    return dot_nn(jnp.ones((16, L), bf16), dqkv)[:8]


def attn_back_kernel(step, qkv, dh, shifted, hmask, out, on_a, q_a, on_b, q_b, keep_a, keep_b, sums_o,
                     qkvv, dhv, shv, outv, qh, kh, vh, doh, dk, dv, t1, ka, sa, kb, sb, ra, rb, ona, onb,
                     fsems, lsems, ready, tick):
    loads = [
        pltpu.make_async_copy(a, b, lsems.at[k])
        for k, (a, b) in enumerate(((qkv, qkvv), (dh, dhv), (shifted, shv)))
    ]
    for load in loads:
        load.start()
    ready()
    for load in loads:
        load.wait()
    scale = LOG2E / math.sqrt(HD)
    first = [
        remote(sa.at[1], ra, fsems, 0, "x"), remote(sb.at[1], rb, fsems, 1, "y"),
        remote(sa.at[0], q_a, fsems, 2, "x"), remote(sb.at[0], q_b, fsems, 3, "y"),
    ]
    stores = [pltpu.make_async_copy(a, b, lsems.at[3 + k]) for k, (a, b) in enumerate(((ka.at[0], keep_a), (kb.at[0], keep_b)))]
    for odd in range(2):
        base = WQ * odd
        for j in range(HC // 2):
            for k, ref in enumerate((qh, kh, vh)):
                start = base + DZ * k + HD * j
                ref[j] = qkvv[:, start : start + HD]
            cut = slice(HD * (2 * j + odd), HD * (2 * j + odd + 1))
            doh[j] = (dhv[:, cut].astype(f32) * hmask[:, cut]).astype(bf16)
        dk[...] = jnp.zeros_like(dk)
        dv[...] = jnp.zeros_like(dv)

        def body(i, carry):
            part = pl.ds(pl.multiple_of(i * step, step), step)
            outs = []
            for j in range(HC // 2):
                q, do = qh[j, part, :], doh[j, part, :]
                s = dot_nt(kh[j], q)
                top = jnp.max(s, axis=0, keepdims=True)
                p = jnp.exp2((s - top) * scale)
                p = p * (1.0 / jnp.sum(p, axis=0, keepdims=True))
                dp = dot_nt(vh[j], do)
                row_dot = jnp.sum(p * dp, axis=0, keepdims=True)
                ds = (p * (dp - row_dot)).astype(bf16)
                dv[j] += dot_nn(p.astype(bf16), do)
                dk[j] += dot_nn(ds, q)
                outs.append(dot_tn(ds, kh[j]))
            outv[part, base : base + DZ] = (jnp.concatenate(outs, axis=1) * (1.0 / math.sqrt(HD))).astype(bf16)
            return carry

        half = L // step // 2
        lax.fori_loop(0, half, body, 0)
        tick(1 + 2 * odd)
        lax.fori_loop(half, 2 * half, body, 0)
        for j in range(HC // 2):
            start = base + DZ + HD * j
            outv[:, start : start + HD] = (dk[j] * (1.0 / math.sqrt(HD))).astype(bf16)
            outv[:, start + DZ : start + DZ + HD] = dv[j].astype(bf16)
        if odd == 0:
            sums_o[...] = column_sums(outv[:, :WQ])
            qkv_slots(outv[:, :WQ], shv[...], None, t1, ka, sa, kb, sb)
            for copy in first + stores:
                copy.start()
            tick(2)
    keep = pltpu.make_async_copy(outv, out, lsems.at[5])
    keep.start()
    for copy in first:
        copy.wait()
    for kv, rv, on in ((ka, ra, ona), (kb, rb, onb)):
        on[...] = (kv[1].astype(f32) + rv[...].astype(f32)).astype(bf16)
    onward = [pltpu.make_async_copy(a, b, lsems.at[6 + k]) for k, (a, b) in enumerate(((ona, on_a), (onb, on_b)))]
    for copy in onward:
        copy.start()
    for copy in stores + onward + [keep]:
        copy.wait()


def end_kernel(dqkv, shifted, even_sums, sum1, sum2, sum_attn, wq, d_resid, tok, mod, sums_mid, f0, c0, f1, c1, f2, c2, sent_p, kept_p, freq,
               on_a, q_a, on_b, q_b, keep_a, keep_b,
               grad, gq_o, gp_o, g1_o, g2_o, ada_o, ada_bias_o, line_o,
               dqv, shv, extra, t1, ka, sa, kb, sb, ra, rb, ona, onb, r2a, r2b, zs, zk, zr,
               eqa, era, eka, eqb, erb, ekb, ezs, ezk, ezr, qt, wqv, dres, tokv, fv, far, got, gb,
               item, item_r, out_shares, square, every, row_out, row_in, mine, theirs, mine_q, theirs_q, pk, pr,
               qsems, esems, csems, tsems, ssems, psems, lsems, ready):
    z, c, y, x = place()
    t, b = 2 * y + x, 2 * z + c
    second_e = [remote(on_a, era, esems, 0, "y"), remote(on_b, erb, esems, 1, "x")]
    third_p = [remote(sent_p.at[k], pr.at[k], psems, k, f"z{k + 1}") for k in (2, 1, 0)]
    pairs = ((dqkv, dqv), (shifted, shv), (wq, wqv), (d_resid, dres), (tok.at[pl.ds(0, LH)], tokv),
             (keep_a, eka), (q_a, eqa), (keep_b, ekb), (q_b, eqb), (kept_p, pk))
    for f, (two, one) in enumerate(((f0, c0), (f1, c1), (f2, c2))):
        pairs += ((two.at[pl.ds(0, GA)], fv.at[f, pl.ds(0, GA)]), (one.at[pl.ds(0, GC)], fv.at[f, pl.ds(GA, GC)]),
                  (two.at[pl.ds(GA, GB)], fv.at[f, pl.ds(G1R, GB)]), (one.at[pl.ds(GC, GC)], fv.at[f, pl.ds(G1R + GB, GC)]))
    loads = [pltpu.make_async_copy(src, dst, lsems.at[k]) for k, (src, dst) in enumerate(pairs)]
    for copy in loads:
        copy.start()
    loads[0].wait()
    loads[1].wait()
    ready()
    for copy in second_e + third_p:
        copy.start()

    odd = dqv[:, WQ:]
    odd_sums = column_sums(odd)
    for zs_ in range(4):
        for ts in range(4):
            start, n = FF // 32 * ts, FF // 32
            pieces = []
            for f in range(NF):
                low, high = max(start, FZ * f), min(start + n, FZ * (f + 1))
                if low < high:
                    pieces.append(sum1[f][:, FZ * zs_ + low - FZ * f : FZ * zs_ + high - FZ * f])
            n = D // 32
            for total in (sum2[...], sum_attn[0:1, :]):
                at = DZ * zs_ + n * ts
                pieces.append(jnp.where(c == 0, total[:, at : at + n], total[:, at + DC : at + DC + n]))
            total = (even_sums, odd_sums)[ts // 2][0:1, :]
            at = HD * zs_ + n * (ts % 2)
            pieces += [total[:, at : at + n], total[:, 2 * DZ + at : 2 * DZ + at + n]]
            flat = jnp.concatenate(pieces + [jnp.zeros((1, 3 * LANES - DZ), f32)], axis=1)
            lines = [flat[:, LANES * k : LANES * (k + 1)] for k in range(3)] + [jnp.zeros((5, LANES), f32)]
            extra[zs_, ts] = jnp.concatenate(lines, axis=0)
    qkv_slots(odd, shv[...], extra, t1, ka, sa, kb, sb)
    first_q = [
        remote(sa.at[1], ra.at[1], qsems, 0, "x"), remote(sb.at[1], rb.at[1], qsems, 1, "y"),
        remote(sa.at[0], ra.at[0], qsems, 2, "x"), remote(sb.at[0], rb.at[0], qsems, 3, "y"),
    ]
    for copy in first_q:
        copy.start()

    loads[2].wait()
    crossing = [remote(far.at[k], got.at[k], csems, k, "c") for k in range(2)]
    d_far = dot_nt(dqv[LH:, :], wqv[...])
    for k in range(2):
        far[k] = d_far[LB * k : LB * (k + 1)].astype(bf16)
        crossing[k].start()

    for copy in second_e:
        copy.wait()
    for k in (5, 6, 7, 8):
        loads[k].wait()
    layer_sums([(eka, eqa, era), (ekb, eqb, erb)], ezs, ezk)
    third_e = [remote(ezs.at[k], ezr.at[k], esems, 2 + k, f"z{k + 1}") for k in (2, 1, 0)]
    for copy in third_e:
        copy.start()
    d_near = dot_nt(dqv[:LH, :], wqv[...])
    loads[3].wait()
    loads[4].wait()
    token_sums = jnp.zeros((2, D), f32)
    for k in range(2):
        part = slice(LB * k, LB * (k + 1))
        crossing[k].wait()
        total = d_near[part] + got[k].astype(f32)
        normed, inverse = normalize(tokv[part, :].astype(f32))
        back = dres[part, :] + normalize_back(total * (1.0 + mod[1:2, :]), normed, inverse)
        gb[k] = back.astype(bf16)
        token_sums += jnp.concatenate(
            [jnp.sum(v, axis=0, keepdims=True) for v in (total, total * normed)], axis=0
        )
    item[...] = jnp.concatenate([token_sums, sums_mid[0:4, :], mod[6:8, :]], axis=0)
    over = remote(item, item_r, csems, 2, "c")
    over.start()

    for copy in first_q:
        copy.wait()
    for kv, rv, on in ((ka, ra, ona), (kb, rb, onb)):
        on[...] = (kv[1].astype(f32) + rv[1].astype(f32)).astype(bf16)
    second_q = [remote(ona, r2a, qsems, 4, "y"), remote(onb, r2b, qsems, 5, "x")]
    for copy in second_q:
        copy.start()
    over.wait()
    v = item[...] + item_r[...]
    n = D // 2
    stamp = v[6:7, :LANES]
    pieces = ([v[0:1], v[1:2, :n]], [v[1:2, n:], v[2:3]], [v[3:4], v[4:5, :n]], [v[4:5, n:], v[5:6]])
    for j in range(4):
        out_shares[j] = jnp.concatenate(pieces[j] + [stamp], axis=1)
    square[t] = out_shares[t]
    meeting = [
        remote(out_shares.at[(y + j // 2) % 2 * 2 + (x + j) % 2], square.at[t], ssems, j - 1, ("x", "y", "xy")[j - 1])
        for j in (1, 2, 3)
    ]
    for copy in meeting:
        copy.start()

    def first_columns(pairs, own):
        for core in range(2):

            @pl.when(c == core)
            def _():
                for f, pair in enumerate(pairs):
                    start = FF // 8 * (core if own else 1 - core) + FZ * f
                    g1_o[:, start : start + FZ] = jnp.concatenate(pair, axis=1)

    for load in loads[9:]:
        load.wait()
    for f in range(NF):
        mine[G1R * f : G1R * (f + 1), :] = fv[f, :G1R, :].astype(bf16)
    swap = remote(mine, theirs, csems, 3, "c")
    swap.start()
    first_columns([[fv[f, :DC, :], fv[f, 2 * DC : 3 * DC, : FZ - LANES]] for f in range(NF)], True)
    for copy in second_q:
        copy.wait()
    layer_sums([(ka.at[0], ra.at[0], r2a), (kb.at[0], rb.at[0], r2b)], zs, zk)
    third_q = [remote(zs.at[k], zr.at[k], qsems, 6 + k, f"z{k + 1}") for k in (2, 1, 0)]
    for copy in third_q:
        copy.start()
    home = homeward(gb.at[0], gb.at[1], grad, tsems, lsems.at[len(pairs)])
    home_start(*home)
    for copy in meeting:
        copy.wait()
    spread_z = [remote(square, every.at[z], ssems, 2 + k, f"z{k}") for k in (1, 2, 3)]
    every[z] = square[...]
    for copy in spread_z:
        copy.start()
    for f in range(NF):
        part = fv[f, G1R:, :]
        tail = part[2 * FZ :]
        tail = jnp.concatenate([tail[:, 32 * k : 32 * (k + 1)] for k in range(4)], axis=0)
        g2_o[FZ * f : FZ * (f + 1), :] = jnp.concatenate([part[:FZ], part[FZ : 2 * FZ], tail], axis=1)
    for copy in third_p:
        copy.wait()
    part = pk[...] + pr[0].astype(f32) + pr[1].astype(f32) + pr[2].astype(f32)
    tail = part[2 * DC :]
    tail = jnp.concatenate([tail[:, 32 * k : 32 * (k + 1)] for k in range(3)], axis=0)
    gp_o[...] = jnp.concatenate([part[:DC], part[DC : 2 * DC], tail], axis=1)
    swap.wait()
    first_columns(
        [
            [theirs[G1R * f + DC : G1R * f + 2 * DC, :].astype(f32),
             theirs[G1R * f + 2 * DC : G1R * (f + 1), FZ - LANES :].astype(f32)]
            for f in range(NF)
        ],
        False,
    )

    for copy in spread_z:
        copy.wait()
    columns = jnp.concatenate([every[i, j] for i in range(4) for j in range(4)], axis=0)
    width = 3 * D // 2
    angles = columns[:, width : width + 1] * freq[b % 4]
    cond = jax.nn.silu(jnp.where(b < 4, jnp.cos(angles), jnp.sin(angles))).astype(bf16).astype(f32)
    columns = columns[:, :width]
    ada_o[...] = lax.dot_general(
        cond, columns, (((0,), (0,)), ((), ())), precision=lax.Precision.HIGHEST, preferred_element_type=f32
    )
    row = jnp.sum(columns, axis=0, keepdims=True)
    row_out[0] = row
    row_in[t] = row
    rows_ = [remote(row_out.at[0], row_in.at[t], ssems, 6 + j, name) for j, name in enumerate(("x", "y", "xy"))]
    for copy in rows_:
        copy.start()

    for odd_, (copies, kept, more) in enumerate(((third_e, ezk, ezr), (third_q, zk, zr))):
        for copy in copies:
            copy.wait()
        q = total_of(kept[...], more[0], more[1], more[2])
        tail = q[2 * TQ :]
        n = TQ // 3
        tail = jnp.concatenate([tail[n * 0 : n, 32 * k : 32 * (k + 1)] for k in range(3)], axis=0)
        qt[odd_] = jnp.transpose(jnp.concatenate([q[:TQ], q[TQ : 2 * TQ], tail], axis=1))
        mine_q[odd_] = qt[odd_, pl.ds(pl.multiple_of(DC * (1 - c), 16), DC), :].astype(bf16)
        swap = remote(mine_q.at[odd_], theirs_q.at[odd_], csems, 4 + odd_, "c")
        swap.start()
        if odd_ == 1:
            line_o[...] = q[QR - 8 :]
    own = [qt[odd_, pl.ds(pl.multiple_of(DC * c, 16), DC), :] for odd_ in range(2)]

    def qkv_columns(values, owned):
        for core in range(2):

            @pl.when(c == core)
            def _():
                for odd_ in range(2):
                    for j in range(3):
                        start = DZ * j + DC * (core if owned else 1 - core) + HD * odd_
                        gq_o[:, start : start + HD] = values[odd_][:, HD * j : HD * (j + 1)]

    qkv_columns(own, True)
    for odd_ in range(2):
        remote(mine_q.at[odd_], theirs_q.at[odd_], csems, 4 + odd_, "c").wait()
    qkv_columns([theirs_q[odd_].astype(f32) for odd_ in range(2)], False)
    for copy in rows_:
        copy.wait()
    row = row_in[z]
    ada_bias_o[...] = jnp.where(c == 0, row[:, : width // 2], row[:, width // 2 :])
    home_wait(*home)


def final_kernel(out_rows, grad_rows, gq, gp, g1, g2, ada, ada_bias, line,
                 out, grad, gq_o, gp_o, g1_o, g2_o, ada_o, ada_bias_o, b_fc1, b_fc2, b_proj, b_q, b_v):
    out[...] = out_rows[...]
    grad[...] = grad_rows[...].astype(f32)
    gq_o[...] = gq[...]
    gp_o[...] = gp[...]
    g1_o[...] = g1[...]
    g2_o[...] = jnp.transpose(g2[...])
    ada_o[...] = ada[...]
    ada_bias_o[...] = ada_bias[...].reshape(-1)
    flat = jnp.concatenate([line[k : k + 1, :] for k in range(3)], axis=1)
    n1, n = FF // 32, D // 32
    b_fc1[...] = flat[:, :n1].reshape(-1)
    for k, ref in enumerate((b_fc2, b_proj, b_q, b_v)):
        ref[...] = flat[:, n1 + n * k : n1 + n * (k + 1)].reshape(-1)


def one_item_per_chip(
    tokens, cotangent, timesteps, bucket_ids, head_masks, channel_masks, skip_rows,
    w_qkv, q_bias, v_bias, w_proj, proj_bias, w_fc1, fc1_bias, w_fc2, fc2_bias, ada_weight, ada_bias,
):
    b, t = lax.axis_index("bucket"), lax.axis_index("tok")
    z, c, y, x = b // 2, b % 2, t // 2, t % 2

    def core_half(v, *dims):
        return lax.dynamic_index_in_dim(v.reshape(dims), c, 1, keepdims=False)

    vmem, smem = pl.BlockSpec(memory_space=pltpu.VMEM), pl.BlockSpec(memory_space=pltpu.SMEM)
    steps = -np.float32(math.log(10000.0)) * np.arange(D // 2, dtype=np.float32) / np.float32(D // 2)
    freq = jnp.asarray(np.exp(steps).reshape(1, D // 2))
    ada_cols = ada_weight.shape[1]
    front, _ = call(
        front_kernel, "front",
        (sds((L, D), bf16), sds((L, D), bf16), sds((L, 3 * WC), bf16), sds((D, 3 * WC), bf16), sds((NF, D, FB), bf16), sds((8, D), f32), sds((L, 1), f32), sds((1, WC), f32), sds((NF, 1, FB), f32),
         sds((NF, 1, FB), f32)),
        (tokens, timesteps, bucket_ids, skip_rows, ada_weight.T, ada_bias, head_masks, channel_masks,
         w_qkv, w_fc1, q_bias, v_bias, fc1_bias, freq),
        in_specs=[ANY, smem, smem, vmem, ANY, vmem, vmem, vmem, ANY, ANY, vmem, vmem, vmem, vmem],
        out_specs=[ANY] * 5 + [vmem] * 5,
        scratch=[vm(L, D), vm(D, 3 * D), vm(D, 3 * WC), vm(D, FF), vm(NF, D, FB), vm(ada_cols, D),
                 vm(8, LANES, dtype=jnp.int32), vm(8, LANES, dtype=jnp.int32), vm(8, ada_cols, dtype=f32), vm(3, 8, ada_cols, dtype=f32),
                 vm(4, 8, ada_cols, dtype=f32), vm(L, D), vm(L, 3 * WC), pltpu.SemaphoreType.DMA((2, 5)),
                 pltpu.SemaphoreType.DMA((2, 4)), pltpu.SemaphoreType.DMA((2, 6)), pltpu.SemaphoreType.DMA((8,))],
        peers=("c", "t0", "t1", "x", "y", "xy"), cid=10, flops=2 * L * D * 3 * WC, nbytes=50e6,
    )
    tok, shifted, qkv, wq, w1, mod, kept, hmask, chan, b1 = front
    w2 = w_fc2.reshape(4, 2, NF, FZ, D)
    wp = w_proj.reshape(4, 2, DC, D)
    (g_all, mixed, shifted2, attn), _ = call(
        functools.partial(attn_kernel, 512), "attn",
        (sds((L, D), bf16), sds((L, WC), bf16), sds((L, D), bf16), sds((LH, D), f32)),
        (cotangent, qkv, hmask, wp, proj_bias, tok, mod),
        in_specs=[ANY, ANY, vmem, ANY, vmem, ANY, vmem],
        out_specs=[ANY, ANY, vmem, vmem],
        scratch=[vm(L, D), vm(L, 3 * WC)] + [vm(HC, L, HD)] * 2 + [vm(HC, L, LANES)] + [vm(L, WC), vm(L, WC), vm(2, 4, DC, D), vm(L, D),
                 pltpu.SemaphoreType.DMA((2, 4)), pltpu.SemaphoreType.DMA((2, 2)), pltpu.SemaphoreType.DMA((2, 2)),
                 pltpu.SemaphoreType.DMA((7,))],
        peers=("c", "t0", "t1"), cid=11, flops=16e9, nbytes=5e6,
    )

    slot1, slot2, slot3 = sds((2, 4, GA, LANES)), sds((2, 4, GB, LANES)), sds((4, 2, 2, 2 * GC, LANES))
    part1, part2, part3 = sds(slot1.shape[1:]), sds(slot2.shape[1:]), sds(slot3.shape[2:])
    one = [part1, part1, part2, part2, part1, part2, part3, part3]
    rows_half = sds((LH, D), bf16)
    own, _ = call(
        mlp_kernel, "mlp",
        one + one + [slot1, slot1, slot2, slot2, slot3] + [rows_half] * 4 + [sds((NF, 1, FB), f32), sds((1, D), f32)],
        (shifted2, g_all, kept, mod, w1, b1, chan, w2),
        in_specs=[ANY, ANY, vmem, vmem, ANY, vmem, vmem, ANY],
        out_specs=[ANY] * 21 + [vmem, vmem, ANY, ANY, vmem, vmem],
        scratch=[vm(L, D), vm(L, D), vm(2, D, FB), vm(2, 4, FZ, D), vm(L, FB), vm(L, FB),
                 vm(L, FB), vm(L, D, dtype=f32), vm(L, D, dtype=f32), vm(2, LH, D), vm(4, D, TD)]
        + [vm(2, *slot1.shape)] * 2 + [vm(2, *slot2.shape)] * 2 + [vm(2, *slot3.shape), vm(2, 3, *slot3.shape[1:])]
        + [vm(2, *p.shape) for p in (part1, part2)] * 2
        + [dma(2, 20), dma(2, 2), dma(2), dma(2, 2), dma(2, 9)],
        peers=("c", "x", "y", "z1", "z2", "z3"), cid=0,
        flops=36 * L * D * FB, nbytes=40e6,
    )
    second0, second1, slots = own[:8], own[8:16], own[16:21]
    branch, ds2, branch_r, ds2_r, sum1, sum2 = own[21:]

    slot_a, slot_b = sds((2, 4, PA, LANES), bf16), sds((2, 4, PR - PA, LANES), bf16)
    own, given = call(
        middle_kernel, "middle",
        (sds((LH, D), f32), rows_half, sds((L, WC), bf16), slot_a, slot_a, slot_b, slot_b, sds((8, D), f32),
         sds((8, D), f32)),
        (ds2, ds2_r, branch, branch_r, attn, tok, g_all, kept, mod, fc2_bias, mixed, wp),
        in_specs=[ANY] * 7 + [vmem] * 3 + [ANY] * 2,
        scratch=[vm(4, LH, D), vm(LH, D, dtype=f32), vm(2, LH, D), vm(L, WC), vm(4, DC, D), vm(L, D), vm(4, WC, TD),
                 dma(2, 4), dma(9)],
        peers=("c",), cid=3, jobs=[FirstSum(*slots), SecondSum(*second0)],
        flops=4 * L * D * WC, nbytes=20e6,
    )
    d_resid, out_rows, dh, *slots_p, sums_mid, sum_attn = own
    first2, result0 = given
    slot_q = vm(2, 4, QA, LANES)
    fourth = vm(4, QA, LANES)
    part_q = sds((4, QA, LANES), bf16)
    own, given = call(
        functools.partial(attn_back_kernel, 512), "attn_back",
        [sds((L, 3 * WC), bf16)] + [part_q] * 6 + [sds((8, WQ), f32)], (qkv, dh, shifted, hmask),
        in_specs=[ANY] * 3 + [vmem],
        out_specs=[ANY] * 7 + [vmem],
        scratch=[vm(L, 3 * WC), vm(L, WC), vm(L, D), vm(L, 3 * WC)] + [vm(HC // 2, L, HD)] * 4
        + [vm(HC // 2, L, HD, dtype=f32)] * 2 + [vm(4, 4, TQ, DZ, dtype=f32)] + [slot_q] * 4 + [fourth] * 4
        + [dma(2, 4), dma(8)],
        cid=4, ticks=True,
        jobs=[SecondThird(*second1, tick_at=1), SecondThird(*first2[:4], slots[0], slots[2], *first2[4:], start_at=1, tick_at=3),
              FirstSecond(*slots_p, start_at=1, tick_at=3), ThirdSum(*result0), GoHome(out_rows, tick_at=3)],
        flops=30e9, nbytes=9e6,
    )
    dqkv, *second_q, even_sums = own
    final1, final2, (sent_p, kept_p), final0, (output,) = given
    width = ada_cols + LANES
    (grad_rows, gq, gp, g1, g2, grad_ada_weight, grad_ada_bias, line), _ = call(
        end_kernel, "end",
        (sds((2, LB, D), bf16), sds((DC, 3 * TD), f32), sds((DC, TD), f32), sds((DC, FF // 4), f32),
         sds((FF // 8, TD), f32), sds((DC, ada_cols), f32), sds((1, ada_cols // 2), f32), sds((8, LANES), f32)),
        (dqkv, shifted, even_sums, sum1, sum2, sum_attn, wq, d_resid, tok, mod, sums_mid, *final0, *final1, *final2, sent_p,
         kept_p, freq.reshape(4, 1, DC), *second_q),
        in_specs=[ANY] * 2 + [vmem] * 4 + [ANY] * 3 + [vmem] * 2 + [ANY] * 8 + [vmem] + [ANY] * 6,
        out_specs=[ANY] + [vmem] * 7,
        scratch=[vm(L, 3 * WC), vm(L, D), vm(4, 4, 8, LANES, dtype=f32), vm(4, 4, TQ, DZ, dtype=f32)]
        + [slot_q] * 6 + [fourth] * 4 + [vm(3, QR, LANES), vm(QR, LANES, dtype=f32), vm(3, QR, LANES)]
        + [fourth] * 6 + [vm(3, QR, LANES), vm(QR, LANES, dtype=f32), vm(3, QR, LANES)]
        + [vm(2, DZ, TQ, dtype=f32), vm(D, 3 * WC), vm(LH, D, dtype=f32), vm(LH, D),
           vm(NF, G1R + G2R, LANES, dtype=f32)] + [vm(2, LB, D)] * 3
        + [vm(8, D, dtype=f32)] * 2 + [vm(4, 1, width, dtype=f32)] * 2
        + [vm(4, 4, 1, width, dtype=f32), vm(1, 1, ada_cols, dtype=f32), vm(4, 1, ada_cols, dtype=f32)]
        + [vm(NF * G1R, LANES)] * 2 + [vm(2, DC, TQ)] * 2 + [vm(PR, LANES, dtype=f32), vm(3, PR, LANES)]
        + [dma(2, 9), dma(2, 5), dma(2, 6), dma(2, 2), dma(2, 9), dma(2, 3), dma(23)],
        peers=("c", "t0", "t1", "x", "y", "xy", "z1", "z2", "z3"), cid=5,
        flops=4 * L * D * 3 * WC, nbytes=30e6,
    )
    thin = lambda height, width: pl.BlockSpec((height, width), lambda i: (i, 0))
    tokens_spec = pl.BlockSpec((2, LB // 2, D), lambda i: (0, i, 0))
    ends = [thin(DC // 2, 3 * TD), thin(DC // 2, TD), thin(DC // 2, FF // 4)]
    bias_cols = ada_cols // 2
    finals, _ = call(
        final_kernel, "final",
        (sds((2, LB, D), bf16), sds((2, LB, D), f32), sds((DC, 3 * TD), f32), sds((DC, TD), f32), sds((DC, FF // 4), f32),
         sds((TD, FF // 8), f32), sds((DC, ada_cols), f32), sds((bias_cols,), f32), sds((FF // 32,), f32))
        + (sds((D // 32,), f32),) * 4,
        (output, grad_rows, gq, gp, g1, g2, grad_ada_weight, grad_ada_bias, line),
        grid=(2,),
        in_specs=[tokens_spec, tokens_spec, *ends, full((FF // 8, TD)), thin(DC // 2, ada_cols), full((1, bias_cols)),
                  full((8, LANES))],
        out_specs=[tokens_spec, tokens_spec, *ends, full((TD, FF // 8)), thin(DC // 2, ada_cols), full((bias_cols,)),
                   full((FF // 32,))] + [full((D // 32,))] * 4,
    )
    output, grad_tokens, gq, gp, g1, g2, g_ada, ada_b, b_fc1, b_fc2, b_proj, b_q, b_v = finals
    return (output, grad_tokens, gq, b_q, b_v, gp, b_proj, g1, b_fc1, g2.T, b_fc2, g_ada, ada_b)


def gelu_tanh(values):
    return jax.nn.gelu(values, approximate=True)


def split_heads(key_value, model_width, head_dim):
    item_count, length = (key_value.shape[0], key_value.shape[1])
    key_rows = key_value[:, :, :model_width].reshape(
        item_count, length, model_width // head_dim, head_dim
    )
    value_rows = key_value[:, :, model_width:].reshape(
        item_count, length, model_width // head_dim, head_dim
    )
    return (key_rows, value_rows)


def scores_of(queries, key_rows, score_scale):
    return (
        jnp.einsum("nqhe,nkhe->nhqk", queries, key_rows, preferred_element_type=jnp.float32)
        * score_scale
    )


def to_blocks(values, per_step):
    return values.reshape((values.shape[0] // per_step, per_step) + values.shape[1:])


def from_blocks(values):
    return values.reshape((values.shape[0] * values.shape[1],) + values.shape[2:])


def on_device(
    tokens,
    cotangent,
    timesteps,
    bucket_ids,
    head_masks,
    channel_masks,
    skip_rows,
    w_qkv,
    q_bias,
    v_bias,
    w_proj,
    proj_bias,
    w_fc1,
    fc1_bias,
    w_fc2,
    fc2_bias,
    ada_weight,
    ada_bias,
):
    item_count, local_len, model_width = tokens.shape
    row_count = item_count * local_len
    head_dim = model_width // HEADS
    score_scale = 1.0 / math.sqrt(head_dim)
    hidden_width = w_fc1.shape[1]
    ada_cols = ada_weight.shape[1]
    tok_index = lax.axis_index("tok")
    per_step = 1
    for candidate in range(1, item_count + 1):
        per_step = candidate
    condition = jax.nn.silu(step_embedding(timesteps, model_width)).astype(jnp.bfloat16)
    mod_local = jnp.dot(
        condition, ada_weight, preferred_element_type=jnp.float32
    ) + ada_bias.astype(jnp.float32)
    modulation = lax.all_gather(mod_local, "tok", axis=1, tiled=True)
    pieces = modulation.reshape(item_count, 6, 1, model_width)
    shift_a = pieces[:, 0]
    scale_a = pieces[:, 1]
    gate_a = pieces[:, 2]
    shift_m = pieces[:, 3]
    scale_m = pieces[:, 4]
    gate_m = pieces[:, 5]
    chosen = (jnp.arange(head_masks.shape[0], dtype=jnp.int32) == bucket_ids[0]).astype(jnp.float32)
    head_on = jnp.sum(chosen[:, None] * head_masks.astype(jnp.float32), axis=0)
    group_on = jnp.sum(chosen[:, None] * channel_masks.astype(jnp.float32), axis=0)
    channel_on = jnp.repeat(group_on, hidden_width // group_on.shape[0])
    positions = tok_index * local_len + jnp.arange(local_len, dtype=jnp.int32)
    skipped = jnp.any(skip_rows[:, :, None] == positions[None, None, :], axis=1)
    kept_rows = 1.0 - skipped.astype(jnp.float32)
    inputs = tokens.astype(jnp.float32)
    normed, inverse = normalize(inputs)
    shifted = (
        (normed * (1.0 + scale_a) + shift_a).astype(jnp.bfloat16).reshape(row_count, model_width)
    )
    qkv_bias = jnp.concatenate([q_bias, jnp.zeros_like(q_bias), v_bias]).astype(jnp.float32)
    projected = (jnp.dot(shifted, w_qkv, preferred_element_type=jnp.float32) + qkv_bias).astype(
        jnp.bfloat16
    )
    projected = projected.reshape(item_count, local_len, 3 * model_width)
    queries = projected[:, :, :model_width].reshape(item_count, local_len, HEADS, head_dim)
    key_value = projected[:, :, model_width:]
    all_kv = lax.all_gather(key_value, "tok", axis=1, tiled=True)

    def forward_block(packed):
        query_block, kv_block = packed
        key_rows, value_rows = split_heads(kv_block, model_width, head_dim)
        scores = scores_of(query_block, key_rows, score_scale)
        top_score = jnp.max(scores, axis=-1, keepdims=True)
        expanded = jnp.exp(scores - top_score)
        totals = jnp.sum(expanded, axis=-1, keepdims=True)
        weights_low = (expanded / totals).astype(jnp.bfloat16)
        head_out = (
            jnp.einsum(
                "nhqk,nkhe->nqhe", weights_low, value_rows, preferred_element_type=jnp.float32
            )
            * head_on[:, None]
        )
        return (head_out.astype(jnp.bfloat16), top_score + jnp.log(totals))

    mixed_heads, log_total = lax.map(
        forward_block, (to_blocks(queries, per_step), to_blocks(all_kv, per_step))
    )
    log_total = from_blocks(log_total)
    mixed = from_blocks(mixed_heads).reshape(row_count, model_width)
    attn = (
        jnp.dot(mixed, w_proj, preferred_element_type=jnp.float32) + proj_bias.astype(jnp.float32)
    ).reshape(item_count, local_len, model_width)
    resid = inputs + gate_a * attn
    normed2, inverse2 = normalize(resid)
    shifted2 = (
        (normed2 * (1.0 + scale_m) + shift_m).astype(jnp.bfloat16).reshape(row_count, model_width)
    )
    pre = jnp.dot(shifted2, w_fc1, preferred_element_type=jnp.float32) + fc1_bias.astype(
        jnp.float32
    )
    activated, gelu_pull = jax.vjp(gelu_tanh, pre)
    hidden = (activated * channel_on).astype(jnp.bfloat16)
    branch = (
        jnp.dot(hidden, w_fc2, preferred_element_type=jnp.float32) + fc2_bias.astype(jnp.float32)
    ).reshape(item_count, local_len, model_width)
    gated = kept_rows[:, :, None] * gate_m
    output = (resid + gated * branch).astype(jnp.bfloat16)
    incoming = cotangent.astype(jnp.float32)
    d_gate_m = jnp.sum(kept_rows[:, :, None] * branch * incoming, axis=1)
    d_branch = (gated * incoming).astype(jnp.bfloat16).reshape(row_count, model_width)
    grad_w_fc2 = jnp.dot(hidden.T, d_branch, preferred_element_type=jnp.float32)
    grad_fc2_bias = jnp.sum(d_branch.astype(jnp.float32), axis=0)
    d_hidden = jnp.dot(d_branch, w_fc2.T, preferred_element_type=jnp.float32)
    d_pre = gelu_pull(d_hidden * channel_on)[0].astype(jnp.bfloat16)
    grad_w_fc1 = jnp.dot(shifted2.T, d_pre, preferred_element_type=jnp.float32)
    grad_fc1_bias = jnp.sum(d_pre.astype(jnp.float32), axis=0)
    d_shifted2 = jnp.dot(d_pre, w_fc1.T, preferred_element_type=jnp.float32).reshape(
        item_count, local_len, model_width
    )
    d_shift_m = jnp.sum(d_shifted2, axis=1)
    d_scale_m = jnp.sum(d_shifted2 * normed2, axis=1)
    d_resid = incoming + normalize_back(d_shifted2 * (1.0 + scale_m), normed2, inverse2)
    d_gate_a = jnp.sum(attn * d_resid, axis=1)
    d_attn = (gate_a * d_resid).astype(jnp.bfloat16).reshape(row_count, model_width)
    grad_w_proj = jnp.dot(mixed.T, d_attn, preferred_element_type=jnp.float32)
    grad_proj_bias = jnp.sum(d_attn.astype(jnp.float32), axis=0)
    d_mixed = jnp.dot(d_attn, w_proj.T, preferred_element_type=jnp.float32).astype(jnp.bfloat16)
    d_heads = d_mixed.reshape(item_count, local_len, HEADS, head_dim) * head_on[:, None].astype(
        jnp.bfloat16
    )
    again_kv = lax.all_gather(key_value, "tok", axis=1, tiled=True)

    def backward_block(packed):
        query_block, kv_block, head_grads, totals_log = packed
        key_rows, value_rows = split_heads(kv_block, model_width, head_dim)
        scores = scores_of(query_block, key_rows, score_scale)
        probs = jnp.exp(scores - totals_log)
        d_probs = jnp.einsum(
            "nqhe,nkhe->nhqk", head_grads, value_rows, preferred_element_type=jnp.float32
        )
        row_dot = jnp.sum(probs * d_probs, axis=-1, keepdims=True)
        d_scores = (probs * (d_probs - row_dot)).astype(jnp.bfloat16)
        d_queries = (
            jnp.einsum("nhqk,nkhe->nqhe", d_scores, key_rows, preferred_element_type=jnp.float32)
            * score_scale
        )
        return (d_queries, row_dot)

    mapped = lax.map(
        backward_block,
        (
            to_blocks(queries, per_step),
            to_blocks(again_kv, per_step),
            to_blocks(d_heads, per_step),
            to_blocks(log_total, per_step),
        ),
    )
    d_queries = from_blocks(mapped[0])
    row_dot = from_blocks(mapped[1])
    queries_all, head_grads_all = (
        lax.all_gather(queries, "tok", axis=1, tiled=True),
        lax.all_gather(d_heads, "tok", axis=1, tiled=True),
    )
    totals_all, row_dot_all = (
        lax.all_gather(log_total, "tok", axis=2, tiled=True),
        lax.all_gather(row_dot, "tok", axis=2, tiled=True),
    )

    def key_block(packed):
        kv_block, query_block, head_grads, totals_log, dots = packed
        key_rows, value_rows = split_heads(kv_block, model_width, head_dim)
        scores = (
            jnp.einsum("nkhe,nqhe->nhkq", key_rows, query_block, preferred_element_type=jnp.float32)
            * score_scale
        )
        probs = jnp.exp(scores - totals_log[:, :, None, :, 0])
        d_probs = jnp.einsum(
            "nkhe,nqhe->nhkq", value_rows, head_grads, preferred_element_type=jnp.float32
        )
        d_scores = (probs * (d_probs - dots[:, :, None, :, 0])).astype(jnp.bfloat16)
        d_keys = (
            jnp.einsum("nhkq,nqhe->nkhe", d_scores, query_block, preferred_element_type=jnp.float32)
            * score_scale
        )
        d_values = jnp.einsum(
            "nhkq,nqhe->nkhe",
            probs.astype(jnp.bfloat16),
            head_grads,
            preferred_element_type=jnp.float32,
        )
        return jnp.concatenate(
            [
                d_keys.reshape(d_keys.shape[0], local_len, model_width),
                d_values.reshape(d_values.shape[0], local_len, model_width),
            ],
            axis=2,
        )

    d_kv = from_blocks(
        lax.map(
            key_block,
            (
                to_blocks(key_value, per_step),
                to_blocks(queries_all, per_step),
                to_blocks(head_grads_all, per_step),
                to_blocks(totals_all, per_step),
                to_blocks(row_dot_all, per_step),
            ),
        )
    )
    d_qkv = jnp.concatenate([d_queries.reshape(item_count, local_len, model_width), d_kv], axis=2)
    d_qkv = d_qkv.astype(jnp.bfloat16).reshape(row_count, 3 * model_width)
    grad_w_qkv = jnp.dot(shifted.T, d_qkv, preferred_element_type=jnp.float32)
    qkv_sums = jnp.sum(d_qkv.astype(jnp.float32), axis=0)
    grad_q_bias = qkv_sums[:model_width]
    grad_v_bias = qkv_sums[2 * model_width :]
    d_shifted = jnp.dot(d_qkv, w_qkv.T, preferred_element_type=jnp.float32).reshape(
        item_count, local_len, model_width
    )
    d_shift_a = jnp.sum(d_shifted, axis=1)
    d_scale_a = jnp.sum(d_shifted * normed, axis=1)
    grad_tokens = d_resid + normalize_back(d_shifted * (1.0 + scale_a), normed, inverse)
    d_modulation = jnp.concatenate(
        [d_shift_a, d_scale_a, d_gate_a, d_shift_m, d_scale_m, d_gate_m], axis=1
    )
    d_modulation = lax.psum(d_modulation, "tok")
    mod_columns = lax.dynamic_slice_in_dim(d_modulation, tok_index * ada_cols, ada_cols, 1)
    grad_ada_weight = jnp.dot(
        condition.astype(jnp.float32).T, mod_columns, precision=lax.Precision.HIGHEST
    )
    grad_ada_bias = jnp.sum(d_modulation, axis=0)
    bucket_done = (
        lax.psum_scatter(grad_w_qkv, "bucket", scatter_dimension=0, tiled=True),
        lax.psum_scatter(grad_w_proj, "bucket", scatter_dimension=0, tiled=True),
        lax.psum_scatter(grad_w_fc1, "bucket", scatter_dimension=0, tiled=True),
        lax.psum_scatter(grad_w_fc2, "bucket", scatter_dimension=0, tiled=True),
        lax.psum_scatter(grad_q_bias, "bucket", scatter_dimension=0, tiled=True),
        lax.psum_scatter(grad_v_bias, "bucket", scatter_dimension=0, tiled=True),
        lax.psum_scatter(grad_proj_bias, "bucket", scatter_dimension=0, tiled=True),
        lax.psum_scatter(grad_fc1_bias, "bucket", scatter_dimension=0, tiled=True),
        lax.psum_scatter(grad_fc2_bias, "bucket", scatter_dimension=0, tiled=True),
        lax.psum_scatter(grad_ada_weight, "bucket", scatter_dimension=0, tiled=True),
        lax.psum_scatter(grad_ada_bias, "bucket", scatter_dimension=0, tiled=True),
    )
    token_done = (
        lax.psum_scatter(bucket_done[0], "tok", scatter_dimension=1, tiled=True),
        lax.psum_scatter(bucket_done[1], "tok", scatter_dimension=1, tiled=True),
        lax.psum_scatter(bucket_done[2], "tok", scatter_dimension=1, tiled=True),
        lax.psum_scatter(bucket_done[3], "tok", scatter_dimension=1, tiled=True),
        lax.psum_scatter(bucket_done[4].reshape(1, -1), "tok", scatter_dimension=1, tiled=True),
        lax.psum_scatter(bucket_done[5].reshape(1, -1), "tok", scatter_dimension=1, tiled=True),
        lax.psum_scatter(bucket_done[6].reshape(1, -1), "tok", scatter_dimension=1, tiled=True),
        lax.psum_scatter(bucket_done[7].reshape(1, -1), "tok", scatter_dimension=1, tiled=True),
        lax.psum_scatter(bucket_done[8].reshape(1, -1), "tok", scatter_dimension=1, tiled=True),
    )
    finished = (
        token_done[0],
        token_done[1],
        token_done[2],
        token_done[3],
        token_done[4],
        token_done[5],
        token_done[6],
        token_done[7],
        token_done[8],
        bucket_done[9],
        bucket_done[10],
    )
    return (
        output,
        grad_tokens,
        finished[0],
        finished[4].reshape(-1),
        finished[5].reshape(-1),
        finished[1],
        finished[6].reshape(-1),
        finished[2],
        finished[7].reshape(-1),
        finished[3],
        finished[8].reshape(-1),
        finished[9],
        finished[10],
    )


def solution(mesh):
    planned = mesh.shape["tok"] == 4 and mesh.shape["bucket"] == 8
    return jax.shard_map(
        one_item_per_chip if planned else on_device,
        mesh=mesh,
        in_specs=(
            P("bucket", "tok", None),
            P("bucket", "tok", None),
            P("bucket"),
            P("bucket"),
            P(),
            P(),
            P("bucket", None),
            P(),
            P(),
            P(),
            P(),
            P(),
            P(),
            P(),
            P(),
            P(),
            P(None, "tok"),
            P("tok"),
        ),
        out_specs=(
            P("bucket", "tok", None),
            P("bucket", "tok", None),
            P("bucket", "tok"),
            P(("bucket", "tok")),
            P(("bucket", "tok")),
            P("bucket", "tok"),
            P(("bucket", "tok")),
            P("bucket", "tok"),
            P(("bucket", "tok")),
            P("bucket", "tok"),
            P(("bucket", "tok")),
            P("bucket", "tok"),
            P("bucket"),
        ),
        check_vma=False,
    )
```

```python
import functools
import math
import types

import jax
import jax.numpy as jnp
import numpy as np
from jax import lax
from jax.experimental import pallas as pl
from jax.experimental.pallas import tpu as pltpu
from jax.sharding import PartitionSpec as P

HEADS = 16
EPSILON = 1e-06
LOG2E = 1.4426950408889634
GELU_K = math.sqrt(2.0 / math.pi)
GELU_C = 0.044715
LANES = 128
bf16, f32 = jnp.bfloat16, jnp.float32


def dot_nn(a, b):
    return lax.dot_general(a, b, (((1,), (0,)), ((), ())), preferred_element_type=f32)


def dot_nt(a, b):
    return lax.dot_general(a, b, (((1,), (1,)), ((), ())), preferred_element_type=f32)


def dot_tn(a, b):
    return lax.dot_general(a, b, (((0,), (0,)), ((), ())), preferred_element_type=f32)


def step_embedding(timesteps, model_width):
    half_width = model_width // 2
    frequency = jnp.exp(-math.log(10000.0) * jnp.arange(half_width, dtype=jnp.float32) / half_width)
    angles = timesteps.astype(jnp.float32)[:, None] * frequency[None, :]
    return jnp.concatenate([jnp.cos(angles), jnp.sin(angles)], axis=1)


def normalize(values):
    centred = values - jnp.mean(values, axis=-1, keepdims=True)
    inverse = lax.rsqrt(jnp.mean(centred * centred, axis=-1, keepdims=True) + EPSILON)
    return (centred * inverse, inverse)


def normalize_back(incoming, normed, inverse):
    return inverse * (
        incoming
        - jnp.mean(incoming, axis=-1, keepdims=True)
        - normed * jnp.mean(incoming * normed, axis=-1, keepdims=True)
    )


D = 1152
DC, DZ, TD = D // 8, D // 4, D // 4
HD = D // HEADS
HC = HEADS // 2
WC = D // 2
FF = 4608
NF = 3
FB = FF // 2 // NF
FZ = FB // 4
L = 1024
LH = L // 2
LB = L // 4
G1R = 3 * DC
G2R = 2 * FZ + FZ // 4
GC = 96
GA, GB = G1R - GC, G2R - GC
PR = 2 * DC + DC // 3
PA = 176
WQ = 3 * WC // 2
TQ = WQ // 4
QR = 512
QA = QR // 2
VMEM_LIMIT = 60 * 1024 * 1024


ANY = pl.BlockSpec(memory_space=pl.ANY)
MESH = pl.DeviceIdType.MESH


def place():
    b, t = lax.axis_index("bucket"), lax.axis_index("tok")
    return b // 2, b % 2, t // 2, t % 2


def flip(value, other):
    return (value // 2 + other // 2) % 2 * 2 + (value % 2 + other % 2) % 2


def peer(name):
    z, c, y, x = place()
    if name == "x":
        x = 1 - x
    elif name == "y":
        y = 1 - y
    elif name == "xy":
        x, y = 1 - x, 1 - y
    elif name == "c":
        c = 1 - c
    elif name in ("t0", "t1"):
        c, y, x = y, c, x if name == "t0" else 1 - x
    else:
        z = flip(z, int(name[1]))
    return (z * 2 + c, y * 2 + x)


def greet(names):
    sem = pltpu.get_barrier_semaphore()
    for name in names:
        if name == "t0":
            continue
        pl.semaphore_signal(sem, inc=1, device_id=peer(name), device_id_type=MESH)
    if "t0" in names:
        _, c, y, _ = place()

        @pl.when(c != y)
        def _():
            pl.semaphore_signal(sem, inc=1, device_id=peer("t0"), device_id_type=MESH)


def meet(names):
    wanted = len([name for name in names if name != "t0"])
    if "t0" in names:
        _, c, y, _ = place()
        wanted = wanted + (c + y) % 2
    pl.semaphore_wait(pltpu.get_barrier_semaphore(), wanted)


def remote(src, dst, sems, k, name):
    return pltpu.make_async_remote_copy(
        src_ref=src, dst_ref=dst, send_sem=sems.at[0, k], recv_sem=sems.at[1, k],
        device_id=peer(name), device_id_type=MESH,
    )


def vm(*shape, dtype=bf16):
    return pltpu.VMEM(shape, dtype)


class Job:
    start_at = tick_at = 0

    def bind(self, scratch):
        return types.SimpleNamespace(**dict(zip(self.spec, scratch)))

    @property
    def scratch(self):
        return list(self.spec.values())


def sds(shape, dtype=bf16):
    return jax.ShapeDtypeStruct(shape, dtype)


def upto(sources, targets, sems):
    return [pltpu.make_async_copy(a, b, sems.at[k]) for k, (a, b) in enumerate(zip(sources, targets))]


def dma(*shape):
    return pltpu.SemaphoreType.DMA(shape)


def total_of(*parts):
    total = parts[0].astype(f32)
    for part in parts[1:]:
        total = total + part.astype(f32)
    return total


class FirstSum(Job):
    def __init__(self, keep_a, sent_a, keep_b, sent_b, third=None):
        self.third = third is not None
        self.peers = ("x", "y", "z1", "z2", "z3") if self.third else ("x", "y")
        self.ins = [keep_a, sent_a, keep_b, sent_b] + ([third] if self.third else [])
        a, b = keep_a.shape[1:], keep_b.shape[1:]
        self.outs = [sds(a), sds(a), sds(b), sds(b)]
        self.spec = dict(ka=vm(*a), ra=vm(*a), oa=vm(*a), kb=vm(*b), rb=vm(*b), ob=vm(*b), sems=dma(2, 7), local=dma(7))
        if self.third:
            c = third.shape[1:]
            self.outs += [sds(c[1:]), sds(c[1:])]
            self.spec.update(kc=vm(*c), rc=vm(3, *c))

    def plan(self, ins, outs, scratch):
        v = self.bind(scratch)
        far = [
            remote(ins[1].at[1], v.ra, v.sems, 0, "x"), remote(ins[3].at[1], v.rb, v.sems, 1, "y"),
            remote(ins[1].at[0], outs[1], v.sems, 2, "x"), remote(ins[3].at[0], outs[3], v.sems, 3, "y"),
        ]
        near = upto([ins[0].at[1], ins[2].at[1]], [v.ka, v.kb], v.local)
        if self.third:
            far += [remote(ins[4].at[k], v.rc.at[k - 1], v.sems, 3 + k, f"z{k}") for k in (3, 2, 1)]
            near.append(pltpu.make_async_copy(ins[4].at[0], v.kc, v.local.at[2]))
        return far, near

    def finish(self, ins, outs, scratch):
        v = self.bind(scratch)
        v.oa[...] = total_of(v.ka[...], v.ra[...]).astype(bf16)
        v.ob[...] = total_of(v.kb[...], v.rb[...]).astype(bf16)
        pairs = [(v.oa, outs[0]), (v.ob, outs[2])]
        if self.third:
            v.kc[...] = total_of(v.kc[...], v.rc[0], v.rc[1], v.rc[2]).astype(bf16)
            pairs += [(v.kc.at[0], outs[4]), (v.kc.at[1], outs[5])]
        return [pltpu.make_async_copy(a, b, v.local.at[3 + k]) for k, (a, b) in enumerate(pairs)]


def layer_sums(streams, zs, zk):
    start = 0
    for kv, qv, rv in streams:
        end = start + rv.shape[1]
        for j in range(4):
            total = total_of(kv[j], qv[j], rv[j])
            if j == 0:
                zk[start:end, :] = total
            else:
                zs[j - 1, start:end, :] = total.astype(bf16)
        start = end


class SecondSum(Job):
    peers = ("x", "y")

    def __init__(self, on_a, q_a, on_b, q_b, keep_a, keep_b, keep_c=None, sent_c=None, start_at=0):
        self.start_at = start_at
        self.third = keep_c is not None
        self.ins = [on_a, q_a, on_b, q_b, keep_a, keep_b] + ([keep_c, sent_c] if self.third else [])
        a, b = on_a.shape, on_b.shape
        rows_ = a[1] + b[1]
        self.outs = [sds((3, rows_, LANES)), sds((rows_, LANES), f32)]
        self.spec = dict(ka=vm(*a), qa=vm(*a), ra=vm(*a), kb=vm(*b), qb=vm(*b), rb=vm(*b), zs=vm(3, rows_, LANES),
                         zk=vm(rows_, LANES, dtype=f32), sems=dma(2, 3), local=dma(9))
        if self.third:
            c = keep_c.shape
            self.outs += [sds(c[1:]), sds(c[1:])]
            self.spec.update(kc=vm(*c), rc=vm(*c))

    def plan(self, ins, outs, scratch):
        v = self.bind(scratch)
        whole = [k.at[0] if len(k.shape) == 4 else k for k in ins[4:6]]
        far = [remote(ins[0], v.ra, v.sems, 0, "y"), remote(ins[2], v.rb, v.sems, 1, "x")]
        near = upto([whole[0], ins[1], whole[1], ins[3]], [v.ka, v.qa, v.kb, v.qb], v.local)
        if self.third:
            far.append(remote(ins[7], v.rc, v.sems, 2, "x"))
            near.append(pltpu.make_async_copy(ins[6], v.kc, v.local.at[4]))
        return far, near

    def add(self, v):
        layer_sums([(v.ka, v.qa, v.ra), (v.kb, v.qb, v.rb)], v.zs, v.zk)
        if self.third:
            v.kc[...] = total_of(v.kc[...], v.rc[...]).astype(bf16)

    def finish(self, ins, outs, scratch):
        v = self.bind(scratch)
        self.add(v)
        pairs = [(v.zs, outs[0]), (v.zk, outs[1])]
        if self.third:
            pairs += [(v.kc.at[0], outs[2]), (v.kc.at[1], outs[3])]
        return [pltpu.make_async_copy(a, b, v.local.at[5 + k]) for k, (a, b) in enumerate(pairs)]


class ThirdSum(Job):
    def __init__(self, sent, kept, keep_c=None, sent_c=None):
        self.third = keep_c is not None
        self.peers = ("z1", "z2", "z3", "y") if self.third else ("z1", "z2", "z3")
        self.ins = [sent, kept] + ([keep_c, sent_c] if self.third else [])
        self.outs = [sds(kept.shape, f32)]
        self.spec = dict(got=vm(*sent.shape), kept=vm(*kept.shape, dtype=f32), sems=dma(2, 4), local=dma(4))
        if self.third:
            self.outs.append(sds(keep_c.shape, f32))
            self.spec.update(kc=vm(*keep_c.shape), rc=vm(*keep_c.shape), fc=vm(*keep_c.shape, dtype=f32))

    def plan(self, ins, outs, scratch):
        v = self.bind(scratch)
        far = [remote(ins[0].at[k], v.got.at[k], v.sems, k, f"z{k + 1}") for k in (2, 1, 0)]
        near = [pltpu.make_async_copy(ins[1], v.kept, v.local.at[0])]
        if self.third:
            far.append(remote(ins[3], v.rc, v.sems, 3, "y"))
            near.append(pltpu.make_async_copy(ins[2], v.kc, v.local.at[1]))
        return far, near

    def finish(self, ins, outs, scratch):
        v = self.bind(scratch)
        v.kept[...] = total_of(v.kept[...], v.got[0], v.got[1], v.got[2])
        pairs = [(v.kept, outs[0])]
        if self.third:
            v.fc[...] = total_of(v.kc[...], v.rc[...])
            pairs.append((v.fc, outs[1]))
        return [pltpu.make_async_copy(a, b, v.local.at[2 + k]) for k, (a, b) in enumerate(pairs)]


class SecondThird(SecondSum):
    peers = ("x", "y", "z1", "z2", "z3")

    def __init__(self, *args, start_at=0, tick_at=1):
        super().__init__(*args, start_at=start_at)
        self.tick_at = tick_at
        kept, c = self.outs[1], self.spec["kc"].shape[1:]
        self.outs = [kept, sds(c, f32)]
        self.spec.update(got=vm(3, *kept.shape), sems3=dma(2, 4), rc3=vm(*c), fc=vm(*c, dtype=f32))

    def next_copies(self, v):
        far = [remote(v.zs.at[k], v.got.at[k], v.sems3, k, f"z{k + 1}") for k in (2, 1, 0)]
        return far + [remote(v.kc.at[1], v.rc3, v.sems3, 3, "y")]

    def tick(self, ins, outs, scratch):
        v = self.bind(scratch)
        for group in self.plan(ins, outs, scratch):
            for copy in group:
                copy.wait()
        self.add(v)
        for copy in self.next_copies(v):
            copy.start()

    def settle(self, ins, outs, scratch):
        return self.next_copies(self.bind(scratch))

    def finish(self, ins, outs, scratch):
        v = self.bind(scratch)
        v.zk[...] = total_of(v.zk[...], v.got[0], v.got[1], v.got[2])
        v.fc[...] = total_of(v.kc[0], v.rc3[...])
        return upto([v.zk, v.fc], outs, v.local)


class FirstSecond(Job):
    peers = ("x", "y")

    def __init__(self, keep_a, sent_a, keep_b, sent_b, start_at=0, tick_at=1):
        self.start_at, self.tick_at = start_at, tick_at
        self.ins = [keep_a, sent_a, keep_b, sent_b]
        a, b = keep_a.shape, keep_b.shape
        rows_ = a[2] + b[2]
        self.outs = [sds((3, rows_, LANES)), sds((rows_, LANES), f32)]
        self.spec = dict(ka=vm(*a), ra=vm(*a), oa=vm(*a[1:]), ra2=vm(*a[1:]), kb=vm(*b), rb=vm(*b), ob=vm(*b[1:]),
                         rb2=vm(*b[1:]), zs=vm(3, rows_, LANES), zk=vm(rows_, LANES, dtype=f32), sems=dma(2, 6), local=dma(4))

    def plan(self, ins, outs, scratch):
        v = self.bind(scratch)
        far = [
            remote(ins[1].at[1], v.ra.at[1], v.sems, 0, "x"), remote(ins[3].at[1], v.rb.at[1], v.sems, 1, "y"),
            remote(ins[1].at[0], v.ra.at[0], v.sems, 2, "x"), remote(ins[3].at[0], v.rb.at[0], v.sems, 3, "y"),
        ]
        return far, upto([ins[0], ins[2]], [v.ka, v.kb], v.local)

    def next_copies(self, v):
        return [remote(v.oa, v.ra2, v.sems, 4, "y"), remote(v.ob, v.rb2, v.sems, 5, "x")]

    def tick(self, ins, outs, scratch):
        v = self.bind(scratch)
        for group in self.plan(ins, outs, scratch):
            for copy in group:
                copy.wait()
        v.oa[...] = total_of(v.ka[1], v.ra[1]).astype(bf16)
        v.ob[...] = total_of(v.kb[1], v.rb[1]).astype(bf16)
        for copy in self.next_copies(v):
            copy.start()

    def settle(self, ins, outs, scratch):
        return self.next_copies(self.bind(scratch))

    def finish(self, ins, outs, scratch):
        v = self.bind(scratch)
        layer_sums([(v.ka.at[0], v.ra.at[0], v.ra2), (v.kb.at[0], v.rb.at[0], v.rb2)], v.zs, v.zk)
        return [pltpu.make_async_copy(a, b, v.local.at[2 + k]) for k, (a, b) in enumerate(((v.zs, outs[0]), (v.zk, outs[1])))]


class GoHome(Job):
    peers = ("t0", "t1")

    def __init__(self, values, tick_at=1):
        self.tick_at = tick_at
        self.ins = [values]
        self.outs = [sds((2, LB, D), values.dtype)]
        self.spec = dict(sems=dma(2, 2), local=pltpu.SemaphoreType.DMA)

    def copies(self, ins, outs, scratch):
        return homeward(ins[0].at[pl.ds(0, LB)], ins[0].at[pl.ds(LB, LB)], outs[0], *scratch)

    def plan(self, ins, outs, scratch):
        home_start(*self.copies(ins, outs, scratch)[:2])
        return [], []

    def tick(self, ins, outs, scratch):
        self.copies(ins, outs, scratch)[2].start()

    def settle(self, ins, outs, scratch):
        home_wait(*self.copies(ins, outs, scratch))
        return []

    def finish(self, ins, outs, scratch):
        return []


def homeward(first, second, dst, sems, local):
    x = place()[3]
    return (
        remote(first, dst.at[x], sems, 0, "t0"),
        pltpu.make_async_copy(first, dst.at[x], local),
        remote(second, dst.at[x], sems, 1, "t1"),
    )


def home_start(away, stay, second=None):
    _, c, y, _ = place()
    pl.when(c != y)(away.start)
    pl.when(c == y)(stay.start)
    if second is not None:
        second.start()


def home_wait(away, stay, second):
    _, c, y, _ = place()
    pl.when(c != y)(away.wait)
    pl.when(c == y)(stay.wait)
    second.wait()


def call(kernel, name, out_shape, args, in_specs=None, out_specs=None, scratch=(), grid=None,
         peers=(), jobs=(), cid=None, ticks=False, flops=0, nbytes=0):
    whole = pl.BlockSpec(memory_space=pltpu.VMEM)
    single = not isinstance(out_shape, (tuple, list))
    out_shape = [out_shape] if single else list(out_shape)
    in_specs = list(in_specs) if in_specs is not None else [whole] * len(args)
    out_specs = [whole] * len(out_shape) if out_specs is None else [out_specs] if single else list(out_specs)
    counts = [len(args), sum(len(j.ins) for j in jobs), len(out_shape), sum(len(j.outs) for j in jobs), len(scratch)]
    names = sorted(set(peers).union(*[j.peers for j in jobs]))

    def run(*refs):
        groups, at = [], 0
        for n in counts:
            groups.append(refs[at : at + n])
            at += n
        bound, ai, ao, asc = [], 0, 0, at
        for j in jobs:
            bound.append((
                j, groups[1][ai : ai + len(j.ins)], groups[3][ao : ao + len(j.outs)], refs[asc : asc + len(j.scratch)]
            ))
            ai, ao, asc = ai + len(j.ins), ao + len(j.outs), asc + len(j.scratch)

        def ready():
            if names:
                meet(names)
            for j, *r in bound:
                if not j.start_at:
                    j_start(j, r)

        def j_start(j, r):
            for group in j.plan(*r):
                for copy in group:
                    copy.start()

        def tick(k):
            for j, *r in bound:
                if j.tick_at == k:
                    j.tick(*r)
            for j, *r in bound:
                if j.start_at == k:
                    j_start(j, r)

        def end():
            last = []
            for j, *r in bound:
                far, near = (j.settle(*r), []) if j.tick_at else j.plan(*r)
                for copy in far:
                    copy.wait()
                for copy in near:
                    copy.wait()
                copies = j.finish(*r)
                for copy in copies:
                    copy.start()
                last += copies
            for copy in last:
                copy.wait()

        if names:
            greet(names)
            kernel(*groups[0], *groups[2], *groups[4], ready=ready, **({"tick": tick} if ticks else {}))
            end()
        else:
            kernel(*groups[0], *groups[2], *groups[4])

    extra = {} if grid is None else {"grid": grid}
    params = {"collective_id": cid, "has_side_effects": True} if names else {}
    outs = pl.pallas_call(
        run,
        out_shape=out_shape + [o for j in jobs for o in j.outs],
        in_specs=in_specs + [ANY] * counts[1],
        out_specs=out_specs + [ANY] * counts[3],
        scratch_shapes=list(scratch) + [q for j in jobs for q in j.scratch],
        compiler_params=pltpu.CompilerParams(vmem_limit_bytes=VMEM_LIMIT, **params),
        cost_estimate=pl.CostEstimate(flops=int(flops), bytes_accessed=int(nbytes), transcendentals=0),
        name=name,
        **extra,
    )(*args, *[a for j in jobs for a in j.ins])
    own, rest, given = outs[: len(out_shape)], outs[len(out_shape) :], []
    for j in jobs:
        given.append(rest[: len(j.outs)])
        rest = rest[len(j.outs) :]
    return (own[0] if single else own), given


def full(shape):
    return pl.BlockSpec(shape, lambda *_: (0,) * len(shape))


def once(*shape):
    return pl.BlockSpec(shape, lambda *_: (0,) * len(shape), pipeline_mode=pl.Buffered(1))


def rows(block, width):
    return pl.BlockSpec((block, width), lambda i: (i, 0))


def arrivals(src, dst, tsems, csems, locals_, pieces=1):
    x = place()[3]
    n = LB // pieces
    moves = []
    for k in range(pieces):
        rows_ = pl.ds(n * k, n)
        here = [dst.at[pl.ds(LB * j + n * k, n)] for j in range(4)]
        moves.append((
            remote(src.at[x, rows_], here[0], tsems, 2 * k, "t0"),
            pltpu.make_async_copy(src.at[x, rows_], here[0], locals_.at[k]),
            remote(src.at[1 - x, rows_], here[1], tsems, 2 * k + 1, "t1"),
            [remote(here[j], here[2 + j], csems, 2 * k + j, "c") for j in range(2)],
        ))
    return moves


def leave(first, stay, second, onward):
    _, c, y, _ = place()
    pl.when(c != y)(first.start)
    pl.when(c == y)(stay.start)
    second.start()


def pass_on(first, stay, second, onward):
    _, c, y, _ = place()
    pl.when(c != y)(first.wait_recv)
    pl.when(c == y)(stay.wait)
    onward[0].start()
    second.wait_recv()
    onward[1].start()


def settle(first, stay, second, onward):
    _, c, y, _ = place()
    pl.when(c != y)(first.wait_send)
    second.wait_send()
    for copy in onward:
        copy.wait_send()


def column(n):
    return lax.broadcasted_iota(jnp.int32, (n, 1), 0)


def front_kernel(tokens, timesteps, bucket_ids, skips, ada_w, ada_b, head_masks, channel_masks, w_qkv, w_fc1,
                 q_bias, v_bias, b1, freq, tok_o, shifted_o, qkv_o, wq_o, w1_o, mod_o, kept_o, hmask_o, chan_o, b1_o,
                 tk, wqv, wqc, w1v, w1c, adav, ints, ints_other, m4, to_send, shares, shv, qkvv, csems, tsems, ssems, lsems, ready):
    z, c, y, x = place()
    t = 2 * y + x
    loads = [
        pltpu.make_async_copy(a, b, lsems.at[k])
        for k, (a, b) in enumerate(((ada_w, adav), (w_qkv, wqv), (w_fc1, w1v)))
    ]

    pieces = 2
    tok_moves = arrivals(tokens, tk, tsems, csems, lsems.at[pl.ds(6, pieces)], pieces)
    ready()
    for moves in tok_moves:
        leave(*moves)
    halves = [skips[:, :LANES], skips[:, LANES:]]
    ints[0:4, :] = jnp.concatenate([halves[0][0:1], halves[1][0:1], halves[0][1:2], halves[1][1:2]], axis=0)
    for k, value in enumerate((timesteps[0], timesteps[1], bucket_ids[0], 0)):
        ints[4 + k : 5 + k, :] = jnp.full((1, LANES), value, jnp.int32)
    swap = remote(ints, ints_other, csems, 2 * pieces, "c")
    swap.start()
    for load in loads:
        load.start()
    swap.wait()

    mine, other = ints[...], ints_other[...]
    r = column(8)
    steps = jnp.zeros((8, 1), f32)
    for k in range(2):
        steps = jnp.where(r == 2 * c + k, mine[4 + k : 5 + k, 0:1].astype(f32), steps)
        steps = jnp.where(r == 2 * (1 - c) + k, other[4 + k : 5 + k, 0:1].astype(f32), steps)
    angles = steps * freq[...]
    condition = jax.nn.silu(jnp.concatenate([jnp.cos(angles), jnp.sin(angles)], axis=1))
    condition = jnp.concatenate([condition, jnp.zeros_like(condition)], axis=0).astype(bf16)
    loads[0].wait()
    m4[...] = dot_nt(condition, adav[...])[:8] + ada_b[...].astype(f32).reshape(1, -1)
    moves = []
    for k in range(4):
        to = (y + k // 2) % 2 * 2 + (x + k) % 2
        row = jnp.broadcast_to(m4[pl.ds(to, 1), :], to_send.shape[1:])
        if k == 0:
            shares[t] = row
        else:
            to_send[k - 1] = row
            moves.append(remote(to_send.at[k - 1], shares.at[t], ssems, k - 1, ("x", "y", "xy")[k - 1]))
            moves[-1].start()

    group = jnp.where(c == y, mine, other)
    bucket = group[6:7, 0:1]
    skip = jnp.where(x == 0, group[0:2], group[2:4])
    for j in range(4):
        block = 2 * ((c + j // 2) % 2) + (x + j) % 2
        position = column(LB) + LB * block
        hit = jnp.where((position == skip[0:1, :]) | (position == skip[1:2, :]), 1.0, 0.0)
        kept_o[LB * j : LB * (j + 1), :] = 1.0 - jnp.max(hit, axis=1, keepdims=True)

    def chosen(masks):
        line = lax.broadcasted_iota(jnp.int32, masks.shape, 0)
        row = jnp.sum(jnp.where(line == bucket, masks[...].astype(f32), 0.0), axis=0, keepdims=True)
        return jnp.broadcast_to(row, (16, masks.shape[1])).astype(bf16)

    def spread(on, low, width):
        first = width * lax.broadcasted_iota(jnp.int32, (on.shape[1], low.shape[1]), 0)
        return dot_nn(on, jnp.where((low >= first) & (low < first + width), 1.0, 0.0).astype(bf16))[0:1, :]

    lane = lax.broadcasted_iota(jnp.int32, (1, WC), 1)
    share = sum(jnp.where(lane >= DC * k, 1, 0) for k in range(1, 4))
    hmask_o[...] = spread(chosen(head_masks), lane + DC * (share + c), HD)
    channels = chosen(channel_masks)
    lane = lax.broadcasted_iota(jnp.int32, (1, FB), 1)
    share = sum(jnp.where(lane >= FZ * k, 1, 0) for k in range(1, 4))
    for f in range(NF):
        low = lane + (4 * DZ - FZ) * share + FF // 8 * c + FZ * f
        chan_o[f] = spread(channels, low, FF // channels.shape[1])

    def half(v, k, width):
        v = v[:, 2 * width * k : 2 * width * (k + 1)]
        return jnp.where(c == 0, v[:, :width], v[:, width:])

    def line(ref):
        return ref[...].astype(f32).reshape(1, -1)

    def parity(v, odd):
        return [half(v, k, DC)[:, HD * odd : HD * (odd + 1)] for k in range(4)]

    bias = []
    for odd in range(2):
        bias += parity(line(q_bias), odd) + [jnp.zeros((1, DZ), f32)] + parity(line(v_bias), odd)
    bias = jnp.concatenate(bias, axis=1)
    b1v = [half(line(b1), k, FF // 8) for k in range(4)]
    for f in range(NF):
        b1_o[f] = jnp.concatenate([v[:, FZ * f : FZ * (f + 1)] for v in b1v], axis=1)
    loads[1].wait()
    loads[2].wait()
    for core in range(2):

        @pl.when(c == core)
        def _():
            for odd in range(2):
                for k in range(12):
                    to, start = WQ * odd + HD * k, DZ * k + DC * core + HD * odd
                    wqc[:, to : to + HD] = wqv[:, start : start + HD]
            for f in range(NF):
                for k in range(4):
                    start = 4 * DZ * k + FF // 8 * core + FZ * f
                    w1c[f, :, FZ * k : FZ * (k + 1)] = w1v[:, start : start + FZ]

    stores = [
        pltpu.make_async_copy(a, b, lsems.at[k]) for k, (a, b) in enumerate(((wqc, wq_o), (w1c, w1_o)))
    ]
    for store in stores:
        store.start()
    for copy in moves:
        copy.wait()
    share_rows = [shares[k][0:1, :] for k in range(4)]
    n, m = D // 2, 3 * D // 2
    mod = [share_rows[0][:, :D], jnp.concatenate([share_rows[0][:, D:], share_rows[1][:, :n]], axis=1),
           share_rows[1][:, n:], share_rows[2][:, :D],
           jnp.concatenate([share_rows[2][:, D:], share_rows[3][:, :n]], axis=1), share_rows[3][:, n:]]
    own_step = 0.5 * jnp.sum(jnp.where(r == t, steps, 0.0), axis=0, keepdims=True)
    mod += [jnp.broadcast_to(own_step, (1, D)), jnp.zeros((1, D), f32)]
    mod_o[...] = jnp.concatenate(mod, axis=0)
    n = LB // pieces

    def make(side, k):
        parts = [slice(LH * side + LB * j + n * k, LH * side + LB * j + n * (k + 1)) for j in range(2)]
        normed, _ = normalize(jnp.concatenate([tk[part, :] for part in parts], axis=0).astype(f32))
        shifted = (normed * (1.0 + mod[1]) + mod[0]).astype(bf16)
        made = (dot_nn(shifted, wqc[...]) + bias).astype(bf16)
        for j, part in enumerate(parts):
            shv[part, :] = shifted[n * j : n * (j + 1)]
            qkvv[part, :] = made[n * j : n * (j + 1)]

    kept_rows = []

    def keep_half(side):
        part = pl.ds(LH * side, LH)
        for k, (a, b) in enumerate(((shv, shifted_o), (qkvv, qkv_o), (tk, tok_o))):
            copy = pltpu.make_async_copy(a.at[part], b.at[part], ssems.at[side, 3 + k])
            copy.start()
            kept_rows.append(copy)

    for k in range(pieces):
        pass_on(*tok_moves[k])
        make(0, k)
        if k == pieces - 1:
            keep_half(0)
        for copy in tok_moves[k][3]:
            copy.wait_recv()
        make(1, k)
    keep_half(1)
    for one in tok_moves:
        settle(*one)
    for copy in stores + kept_rows:
        copy.wait()


def attn_kernel(step, cotangent, qkv, hmask, wp, bias, tok, mod, cot_o, mixed_o, shifted2_o, attn_o,
                ck, qkvv, qh, kh, vh, mx, mo, wpv, tkv, sh2v, attnv, csems, tsems, osems, lsems, ssems, ready):
    c = place()[1]
    loads = [
        pltpu.make_async_copy(wp.at[:, c], wpv.at[0], lsems.at[0]),
        pltpu.make_async_copy(wp.at[:, 1 - c], wpv.at[1], lsems.at[1]),
        pltpu.make_async_copy(tok, tkv, lsems.at[2]),
        pltpu.make_async_copy(qkv, qkvv, lsems.at[4]),
    ]
    for load in loads[::-1]:
        load.start()
    cot_moves = arrivals(cotangent, ck, tsems, osems, lsems.at[pl.ds(5, 1)])[0]
    scale = LOG2E / math.sqrt(HD)
    loads.pop().wait()
    for h in range(HC):
        for k, ref in enumerate((qh, kh, vh)):
            start = WQ * (h % 2) + DZ * k + HD * (h // 2)
            ref[h, :, :HD] = qkvv[:, start : start + HD]
        vh[h, :, HD:] = jnp.ones((L, LANES - HD), bf16)
    ready()
    leave(*cot_moves)

    def crossing(i):
        src = mx.at[pl.ds(pl.multiple_of(i * step, step), step)]
        dst = mo.at[pl.ds(pl.multiple_of((i * step + LH) % L, step), step)]
        return remote(src, dst, csems, i, "c")

    def body(i, carry):
        part = pl.ds(pl.multiple_of(i * step, step), step)
        outs = []
        for h in range(HC):
            s = dot_nt(qh[h, part, :], kh[h])
            top = jnp.max(s, axis=1, keepdims=True)
            p = jnp.exp2((s - top) * scale)
            o = dot_nn(p.astype(bf16), vh[h])
            outs.append(o[:, :HD] * (1.0 / o[:, HD : HD + 1]))
        mx[part, :] = (jnp.concatenate(outs, axis=1) * hmask[...]).astype(bf16)
        crossing(i).start()
        return carry

    lax.fori_loop(0, L // step, body, 0)
    keep = pltpu.make_async_copy(mx, mixed_o, lsems.at[3])
    keep.start()
    pass_on(*cot_moves)
    for load in loads:
        load.wait()
    for i in range(L // step):
        crossing(i).wait()
    w_mine, w_other = wpv[0].reshape(WC, D), wpv[1].reshape(WC, D)
    bias_line = bias[...].astype(f32).reshape(1, D)
    stores = []
    for j in range(4):
        part = slice(LB * j, LB * (j + 1))
        attn = dot_nn(mx[part, :], w_mine) + dot_nn(mo[part, :], w_other) + bias_line
        if j < 2:
            attnv[part, :] = attn
        normed, _ = normalize(tkv[part, :].astype(f32) + mod[2:3, :] * attn)
        sh2v[part, :] = (normed * (1.0 + mod[4:5, :]) + mod[3:4, :]).astype(bf16)
        made = [(sh2v, shifted2_o)] + [(attnv, attn_o)] * (j < 2)
        for k, (a, b) in enumerate(made):
            stores.append(pltpu.make_async_copy(a.at[pl.ds(LB * j, LB)], b.at[pl.ds(LB * j, LB)], ssems.at[k, j]))
            stores[-1].start()
    for copy in cot_moves[3]:
        copy.wait_recv()
    keep_cot = pltpu.make_async_copy(ck, cot_o, lsems.at[6])
    keep_cot.start()
    settle(*cot_moves)
    for copy in stores + [keep, keep_cot]:
        copy.wait()


def mlp_kernel(sh2, g, kept, mod, w1, b1, chan, w2,
               on_a0, q_a0, on_b0, q_b0, keep_a0, keep_b0, keep_c0, send_c0,
               on_a1, q_a1, on_b1, q_b1, keep_a1, keep_b1, keep_c1, send_c1,
               k2a, s2a, k2b, s2b, c2, branch_o, ds2_o, branch_r, ds2_r, sum1_o, sum2_o,
               sh2v, dbs, w1v, w2v, hid, dpre, slope, br, ds, far, tt_, ka, sa, kb, sb, cz, cr, ra, rb, ona, onb,
               fsems, csems, lsems, wsems, osems, ready):
    z, c, y, x = place()
    out0 = (on_a0, q_a0, on_b0, q_b0, keep_a0, keep_b0, keep_c0, send_c0)
    out1 = (on_a1, q_a1, on_b1, q_b1, keep_a1, keep_b1, keep_c1, send_c1)
    outs = (out0, out1)

    def weights(f):
        return [
            pltpu.make_async_copy(w1.at[f], w1v.at[f % 2], wsems.at[0, f % 2]),
            pltpu.make_async_copy(w2.at[:, c, f], w2v.at[f % 2], wsems.at[1, f % 2]),
        ]

    def first(f):
        k, out = f % 2, outs[f]
        return [
            remote(sa.at[k, 1], ra.at[k], fsems, 10 * k, "x"), remote(sb.at[k, 1], rb.at[k], fsems, 10 * k + 1, "y"),
            remote(sa.at[k, 0], out[1], fsems, 10 * k + 2, "x"), remote(sb.at[k, 0], out[3], fsems, 10 * k + 3, "y"),
        ] + [
            remote(cz.at[k, j, :, :, pl.ds(GC * half, GC)], cr.at[k, j - 1, :, :, pl.ds(GC * half, GC)], fsems,
                   10 * k + 3 + 3 * half + j, f"z{j}")
            for half in range(2) for j in (3, 2, 1)
        ]

    def stored(f):
        k = f % 2
        if f == NF - 1:
            pairs = ((ka.at[k], k2a), (sa.at[k], s2a), (kb.at[k], k2b), (sb.at[k], s2b), (cz.at[k], c2))
        else:
            pairs = ((ka.at[k, 0], outs[f][4]), (kb.at[k, 0], outs[f][5]))
        return [pltpu.make_async_copy(src, dst, osems.at[k, j]) for j, (src, dst) in enumerate(pairs)]

    def onward(f):
        k = f % 2
        for copy in first(f):
            copy.wait()
        for kv, rv, on in ((ka, ra, ona), (kb, rb, onb)):
            on[k] = total_of(kv[k, 1], rv[k]).astype(bf16)
        cz[k, 0] = total_of(cz[k, 0], cr[k, 0], cr[k, 1], cr[k, 2]).astype(bf16)
        pairs = (
            (ona.at[k], outs[f][0]), (onb.at[k], outs[f][2]), (cz.at[k, 0, 0], outs[f][6]), (cz.at[k, 0, 1], outs[f][7])
        )
        copies = [pltpu.make_async_copy(src, dst, osems.at[k, 5 + j]) for j, (src, dst) in enumerate(pairs)]
        for copy in copies:
            copy.start()
        return copies

    loads = [pltpu.make_async_copy(src, dst, lsems.at[k]) for k, (src, dst) in enumerate(((g, dbs), (sh2, sh2v)))]
    for copy in loads + weights(0):
        copy.start()
    loads[0].wait()
    sum2 = jnp.zeros((1, D), f32)
    for j in range(4):
        part = slice(LB * j, LB * (j + 1))
        db = (dbs[part, :].astype(f32) * mod[5:6, :] * kept[part, :]).astype(bf16)
        dbs[part, :] = db
        sum2 += jnp.sum(db.astype(f32), axis=0, keepdims=True)
    sum2_o[...] = sum2
    loads[1].wait()
    crossing = [remote(far.at[j], dst, csems, j, "c") for j, dst in enumerate((branch_r, ds2_r))]
    waiting = []
    for f in range(NF):
        for copy in weights(f):
            copy.wait()
        if f + 1 < NF:
            for copy in weights(f + 1):
                copy.start()
        w1f, w2f = w1v[f % 2], w2v[f % 2].reshape(FB, D)
        on = chan[f]
        k = f % 2
        for side in (1, 0):
            part = slice(LH * side, LH * (side + 1))
            v = dot_nn(sh2v[part, :], w1f) + b1[f]
            v2 = v * v
            th = jnp.tanh(GELU_K * v * (1.0 + GELU_C * v2))
            half = 0.5 * (1.0 + th)
            hid[part, :] = (v * half * on).astype(bf16)
            slope[part, :] = (
                (half + (0.5 * GELU_K) * v * (1.0 - th * th) * (1.0 + (3.0 * GELU_C) * v2)) * on
            ).astype(bf16)
        p = dot_tn(hid[...], dbs[...]).astype(bf16)
        for t in range(4):
            tt_[t, :FB, :] = p[:, TD * t : TD * (t + 1)]
        for rz in range(4):
            zz = flip(z, rz)
            for ry in range(2):
                for rx in range(2):
                    tt = (ry + y) % 2 * 2 + (rx + x) % 2
                    o = (kb, sb)[ry]
                    block = tt_[tt, pl.ds(pl.multiple_of(zz * FZ, 16), FZ), :]
                    o[k, rx, rz, :FZ, :] = block[:, :LANES]
                    o[k, rx, rz, FZ:, :] = block[: GB - FZ, LANES : 2 * LANES]
                    q = FZ // 4
                    cz[k, rz, rx, ry, GC : GC + 2 * FZ - GB, :] = block[GB - FZ :, LANES : 2 * LANES]
                    cz[k, rz, rx, ry, GC + 2 * FZ - GB :, :] = jnp.concatenate(
                        [block[q * j : q * (j + 1), 2 * LANES :] for j in range(4)], axis=1
                    )
        if f == 0:
            ready()
        if f < NF - 1:
            for copy in first(f)[1:4:2] + first(f)[7:]:
                copy.start()
        sum1 = jnp.zeros((1, FB), f32)
        for side in (1, 0):
            part = slice(LH * side, LH * (side + 1))
            d_pre = (dot_nt(dbs[part, :], w2f) * slope[part, :].astype(f32)).astype(bf16)
            dpre[part, :] = d_pre
            sum1 += jnp.sum(d_pre.astype(f32), axis=0, keepdims=True)
        sum1_o[f] = sum1
        p = dot_tn(sh2v[...], dpre[...]).astype(bf16)
        for t in range(4):
            tt_[t, :, :FZ] = p[:, FZ * t : FZ * (t + 1)]
        for rz in range(4):
            zz = flip(z, rz)
            for ry in range(2):
                for rx in range(2):
                    tt = (ry + y) % 2 * 2 + (rx + x) % 2
                    o = (ka, sa)[rx]
                    tails = []
                    for rc in range(2):
                        block = tt_[tt, pl.ds(pl.multiple_of(zz * DZ + (rc + c) % 2 * DC, 16), DC), :FZ]
                        o[k, ry, rz, DC * rc : DC * (rc + 1), :] = block[:, :LANES]
                        tails.append(block[:, LANES:])
                    tail = jnp.concatenate(tails, axis=1)
                    o[k, ry, rz, 2 * DC :, :] = tail[: GA - 2 * DC]
                    cz[k, rz, rx, ry, :GC, :] = tail[GA - 2 * DC :]
        if f < NF - 1:
            for copy in first(f)[0:4:2] + first(f)[4:7]:
                copy.start()
        for copy in stored(f):
            copy.start()
        for side in (1, 0):
            part = slice(LH * side, LH * (side + 1))
            branch, ds2 = dot_nn(hid[part, :], w2f), dot_nt(dpre[part, :], w1f)
            if f > 0:
                branch, ds2 = branch + br[part, :], ds2 + ds[part, :]
            if f < NF - 1:
                br[part, :] = branch
                ds[part, :] = ds2
            elif side == 1:
                far[0] = branch.astype(bf16)
                far[1] = ds2.astype(bf16)
                for copy in crossing:
                    copy.start()
            else:
                branch_o[...] = branch.astype(bf16)
                ds2_o[...] = ds2.astype(bf16)
        waiting += stored(f)
        if f > 0:
            waiting += onward(f - 1)
        if f == NF - 2:
            for copy in waiting:
                copy.wait()
            waiting = []
    for copy in waiting + crossing:
        copy.wait()


def middle_kernel(ds, ds_r, br, br_r, attn, tok, g, kept, mod, bias2, mixed, wp,
                  d_resid_o, out_o, dh_o, pka, psa, pkb, psb, sums_o, sum_o,
                  dsv, attnv, tokv, mixv, wpv, da, t1, csems, lsems, bsems, ready):
    z, c, y, x = place()
    n = LH // 4
    pairs = ((tok, tokv.at[0]), (attn, attnv), (ds, dsv.at[0]), (ds_r, dsv.at[1]), (br, dsv.at[2]), (br_r, dsv.at[3]),
             (g, tokv.at[1]))
    blocks = [
        [
            pltpu.make_async_copy(src.at[pl.ds(n * k, n)], dst.at[pl.ds(n * k, n)], bsems.at[k, j])
            for j, (src, dst) in enumerate(pairs)
        ]
        for k in range(4)
    ]
    loads = [pltpu.make_async_copy(src, dst, lsems.at[k]) for k, (src, dst) in enumerate(((wp.at[:, c], wpv), (mixed, mixv)))]
    for load in sum(blocks, []) + loads:
        load.start()
    ready()
    crossing = [remote(da.at[pl.ds(n * k, n)], da.at[pl.ds(LH + n * k, n)], csems, k, "c") for k in range(4)]
    sums = jnp.zeros((4, D), f32)
    bias_line = bias2[...].astype(f32).reshape(1, D)
    for k in range(4):
        for load in blocks[k]:
            load.wait()
        part = slice(n * k, n * (k + 1))
        gf, at = tokv[1, part, :].astype(f32), attnv[part, :]
        resid = tokv[0, part, :].astype(f32) + mod[2:3, :] * at
        normed2, inverse2 = normalize(resid)
        ds2 = dsv[0, part, :].astype(f32) + dsv[1, part, :].astype(f32)
        kb = kept[part, :] * (dsv[2, part, :].astype(f32) + dsv[3, part, :].astype(f32) + bias_line)
        out_o[part, :] = (resid + mod[5:6, :] * kb).astype(bf16)
        d_resid = gf + normalize_back(ds2 * (1.0 + mod[4:5, :]), normed2, inverse2)
        d_resid_o[part, :] = d_resid
        da[part, :] = (mod[2:3, :] * d_resid).astype(bf16)
        crossing[k].start()
        sums += jnp.concatenate(
            [jnp.sum(p, axis=0, keepdims=True) for p in (at * d_resid, ds2, ds2 * normed2, kb * gf)], axis=0
        )
    sums_o[...] = jnp.concatenate([sums, jnp.zeros((4, D), f32)], axis=0)
    for load in loads:
        load.wait()
    for copy in crossing:
        copy.wait()
    wv = wpv[...].reshape(WC, D)
    dh_o[...] = dot_nt(da[...], wv).astype(bf16)
    sum_o[...] = dot_nn(jnp.ones((16, L), bf16), da[...])[:8]
    grad = dot_tn(mixv[...], da[...]).astype(bf16)
    for t in range(4):
        t1[t] = grad[:, TD * t : TD * (t + 1)]
    for rz in range(4):
        zz = flip(z, rz)
        for ry in range(2):
            for rx in range(2):
                tt = (ry + y) % 2 * 2 + (rx + x) % 2
                a, b = (pka, psa)[rx], (pkb, psb)[ry]
                block = t1[tt, pl.ds(pl.multiple_of(zz * DC, 16), DC), :]
                a[ry, rz, :DC, :] = block[:, :LANES]
                a[ry, rz, DC:, :] = block[: PA - DC, LANES : 2 * LANES]
                b[rx, rz, : 2 * DC - PA, :] = block[PA - DC :, LANES : 2 * LANES]
                q = DC // 3
                tails = [block[q * k : q * (k + 1), 2 * LANES :] for k in range(3)]
                tails.append(jnp.zeros((q, 32), bf16))
                b[rx, rz, 2 * DC - PA :, :] = jnp.concatenate(tails, axis=1)


def qkv_slots(grad, extra, t1, ka, sa, kb, sb):
    z, _, y, x = place()
    for t in range(4):
        for zz in range(4):
            t1[t, zz] = grad[TQ * t : TQ * (t + 1), DZ * zz : DZ * (zz + 1)]
    q = TQ // 3
    for rz in range(4):
        zz = flip(z, rz)
        for ry in range(2):
            for rx in range(2):
                tt = (ry + y) % 2 * 2 + (rx + x) % 2
                block = t1[tt, zz]
                tails = [block[q * k : q * (k + 1), 2 * LANES :] for k in range(3)] + [jnp.zeros((q, 32), f32)]
                more = jnp.zeros((8, LANES), f32) if extra is None else extra[zz, tt]
                slot = [block[:, :LANES], block[:, LANES : 2 * LANES], jnp.concatenate(tails, axis=1), more]
                slot = jnp.concatenate(slot, axis=0).astype(bf16)
                (ka, sa)[rx][ry, rz] = slot[:QA]
                (kb, sb)[ry][rx, rz] = slot[QA:]


def column_sums(dqkv):
    return dot_nn(jnp.ones((16, L), bf16), dqkv)[:8]


def attn_back_kernel(step, qkv, dh, shifted, hmask, out, on_a, q_a, on_b, q_b, keep_a, keep_b, sums_o,
                     qkvv, dhv, shv, outv, qh, kh, vh, doh, dk, dv, t1, ka, sa, kb, sb, ra, rb, ona, onb,
                     fsems, lsems, ready, tick):
    loads = [
        pltpu.make_async_copy(a, b, lsems.at[k])
        for k, (a, b) in enumerate(((qkv, qkvv), (dh, dhv), (shifted, shv)))
    ]
    for load in loads:
        load.start()
    ready()
    for load in loads:
        load.wait()
    scale = LOG2E / math.sqrt(HD)
    first = [
        remote(sa.at[1], ra, fsems, 0, "x"), remote(sb.at[1], rb, fsems, 1, "y"),
        remote(sa.at[0], q_a, fsems, 2, "x"), remote(sb.at[0], q_b, fsems, 3, "y"),
    ]
    stores = [pltpu.make_async_copy(a, b, lsems.at[3 + k]) for k, (a, b) in enumerate(((ka.at[0], keep_a), (kb.at[0], keep_b)))]
    for odd in range(2):
        base = WQ * odd
        for j in range(HC // 2):
            for k, ref in enumerate((qh, kh, vh)):
                start = base + DZ * k + HD * j
                ref[j] = qkvv[:, start : start + HD]
            cut = slice(HD * (2 * j + odd), HD * (2 * j + odd + 1))
            doh[j] = (dhv[:, cut].astype(f32) * hmask[:, cut]).astype(bf16)
        dk[...] = jnp.zeros_like(dk)
        dv[...] = jnp.zeros_like(dv)

        def body(i, carry):
            part = pl.ds(pl.multiple_of(i * step, step), step)
            outs = []
            for j in range(HC // 2):
                q, do = qh[j, part, :], doh[j, part, :]
                s = dot_nt(kh[j], q)
                top = jnp.max(s, axis=0, keepdims=True)
                p = jnp.exp2((s - top) * scale)
                p = p * (1.0 / jnp.sum(p, axis=0, keepdims=True))
                dp = dot_nt(vh[j], do)
                row_dot = jnp.sum(p * dp, axis=0, keepdims=True)
                ds = (p * (dp - row_dot)).astype(bf16)
                dv[j] += dot_nn(p.astype(bf16), do)
                dk[j] += dot_nn(ds, q)
                outs.append(dot_tn(ds, kh[j]))
            outv[part, base : base + DZ] = (jnp.concatenate(outs, axis=1) * (1.0 / math.sqrt(HD))).astype(bf16)
            return carry

        half = L // step // 2
        lax.fori_loop(0, half, body, 0)
        tick(1 + 2 * odd)
        lax.fori_loop(half, 2 * half, body, 0)
        for j in range(HC // 2):
            start = base + DZ + HD * j
            outv[:, start : start + HD] = (dk[j] * (1.0 / math.sqrt(HD))).astype(bf16)
            outv[:, start + DZ : start + DZ + HD] = dv[j].astype(bf16)
        if odd == 0:
            sums_o[...] = column_sums(outv[:, :WQ])
            qkv_slots(dot_tn(outv[:, :WQ], shv[...]), None, t1, ka, sa, kb, sb)
            for copy in first + stores:
                copy.start()
            tick(2)
    keep = pltpu.make_async_copy(outv, out, lsems.at[5])
    keep.start()
    for copy in first:
        copy.wait()
    for kv, rv, on in ((ka, ra, ona), (kb, rb, onb)):
        on[...] = (kv[1].astype(f32) + rv[...].astype(f32)).astype(bf16)
    onward = [pltpu.make_async_copy(a, b, lsems.at[6 + k]) for k, (a, b) in enumerate(((ona, on_a), (onb, on_b)))]
    for copy in onward:
        copy.start()
    for copy in stores + onward + [keep]:
        copy.wait()


def end_kernel(dqkv, shifted, even_sums, sum1, sum2, sum_attn, wq, d_resid, tok, mod, sums_mid, f0, c0, f1, c1, f2, c2, sent_p, kept_p, freq,
               on_a, q_a, on_b, q_b, keep_a, keep_b,
               grad, gq_o, gp_out, g1_out, g2_out, ada_out, ada_bias_o, line_o,
               dqv, shv, extra, t1, ka, sa, kb, sb, ra, rb, ona, onb, r2a, r2b, zs, zk, zr,
               eqa, era, eka, eqb, erb, ekb, ezs, ezk, ezr, qt, wqv, dres, tokv, fv, far, got, gb,
               item, item_r, out_shares, square, every, row_out, row_in, mine, theirs, mine_q, theirs_q, pk, pr, gp_o, g1_o, g2_o, ada_o,
               qsems, esems, csems, tsems, ssems, psems, lsems, xsems, ready):
    z, c, y, x = place()
    t, b = 2 * y + x, 2 * z + c
    second_e = [remote(on_a, era, esems, 0, "y"), remote(on_b, erb, esems, 1, "x")]
    third_p = [remote(sent_p.at[k], pr.at[k], psems, k, f"z{k + 1}") for k in (2, 1, 0)]
    pairs = ((dqkv, dqv), (shifted, shv), (wq, wqv), (d_resid, dres), (tok.at[pl.ds(0, LH)], tokv),
             (keep_a, eka), (q_a, eqa), (keep_b, ekb), (q_b, eqb), (kept_p, pk))
    for f, (two, one) in enumerate(((f0, c0), (f1, c1), (f2, c2))):
        pairs += ((two.at[pl.ds(0, GA)], fv.at[f, pl.ds(0, GA)]), (one.at[pl.ds(0, GC)], fv.at[f, pl.ds(GA, GC)]),
                  (two.at[pl.ds(GA, GB)], fv.at[f, pl.ds(G1R, GB)]), (one.at[pl.ds(GC, GC)], fv.at[f, pl.ds(G1R + GB, GC)]))
    loads = [pltpu.make_async_copy(src, dst, lsems.at[k]) for k, (src, dst) in enumerate(pairs)]
    for copy in loads:
        copy.start()
    loads[0].wait()
    loads[1].wait()
    ready()
    for copy in second_e + third_p:
        copy.start()

    odd = dqv[:, WQ:]
    grad_odd = dot_tn(odd, shv[...])
    odd_sums = column_sums(odd)
    for zs_ in range(4):
        for ts in range(4):
            start, n = FF // 32 * ts, FF // 32
            pieces = []
            for f in range(NF):
                low, high = max(start, FZ * f), min(start + n, FZ * (f + 1))
                if low < high:
                    pieces.append(sum1[f][:, FZ * zs_ + low - FZ * f : FZ * zs_ + high - FZ * f])
            n = D // 32
            for total in (sum2[...], sum_attn[0:1, :]):
                at = DZ * zs_ + n * ts
                pieces.append(jnp.where(c == 0, total[:, at : at + n], total[:, at + DC : at + DC + n]))
            total = (even_sums, odd_sums)[ts // 2][0:1, :]
            at = HD * zs_ + n * (ts % 2)
            pieces += [total[:, at : at + n], total[:, 2 * DZ + at : 2 * DZ + at + n]]
            flat = jnp.concatenate(pieces + [jnp.zeros((1, 3 * LANES - DZ), f32)], axis=1)
            lines = [flat[:, LANES * k : LANES * (k + 1)] for k in range(3)] + [jnp.zeros((5, LANES), f32)]
            extra[zs_, ts] = jnp.concatenate(lines, axis=0)
    qkv_slots(grad_odd, extra, t1, ka, sa, kb, sb)
    first_q = [
        remote(sa.at[1], ra.at[1], qsems, 0, "x"), remote(sb.at[1], rb.at[1], qsems, 1, "y"),
        remote(sa.at[0], ra.at[0], qsems, 2, "x"), remote(sb.at[0], rb.at[0], qsems, 3, "y"),
    ]
    for copy in first_q:
        copy.start()

    loads[2].wait()
    crossing = [remote(far.at[k], got.at[k], csems, k, "c") for k in range(2)]
    d_far = dot_nt(dqv[LH:, :], wqv[...])
    for k in range(2):
        far[k] = d_far[LB * k : LB * (k + 1)].astype(bf16)
        crossing[k].start()

    for copy in second_e:
        copy.wait()
    for k in (5, 6, 7, 8):
        loads[k].wait()
    layer_sums([(eka, eqa, era), (ekb, eqb, erb)], ezs, ezk)
    third_e = [remote(ezs.at[k], ezr.at[k], esems, 2 + k, f"z{k + 1}") for k in (2, 1, 0)]
    for copy in third_e:
        copy.start()
    d_near = dot_nt(dqv[:LH, :], wqv[...])
    loads[3].wait()
    loads[4].wait()
    token_sums = jnp.zeros((2, D), f32)
    for k in range(2):
        part = slice(LB * k, LB * (k + 1))
        crossing[k].wait()
        total = d_near[part] + got[k].astype(f32)
        normed, inverse = normalize(tokv[part, :].astype(f32))
        back = dres[part, :] + normalize_back(total * (1.0 + mod[1:2, :]), normed, inverse)
        gb[k] = back.astype(bf16)
        token_sums += jnp.concatenate(
            [jnp.sum(v, axis=0, keepdims=True) for v in (total, total * normed)], axis=0
        )
    item[...] = jnp.concatenate([token_sums, sums_mid[0:4, :], mod[6:8, :]], axis=0)
    over = remote(item, item_r, csems, 2, "c")
    over.start()

    for copy in first_q:
        copy.wait()
    for kv, rv, on in ((ka, ra, ona), (kb, rb, onb)):
        on[...] = (kv[1].astype(f32) + rv[1].astype(f32)).astype(bf16)
    second_q = [remote(ona, r2a, qsems, 4, "y"), remote(onb, r2b, qsems, 5, "x")]
    for copy in second_q:
        copy.start()
    over.wait()
    v = item[...] + item_r[...]
    n = D // 2
    stamp = v[6:7, :LANES]
    pieces = ([v[0:1], v[1:2, :n]], [v[1:2, n:], v[2:3]], [v[3:4], v[4:5, :n]], [v[4:5, n:], v[5:6]])
    for j in range(4):
        out_shares[j] = jnp.concatenate(pieces[j] + [stamp], axis=1)
    square[t] = out_shares[t]
    meeting = [
        remote(out_shares.at[(y + j // 2) % 2 * 2 + (x + j) % 2], square.at[t], ssems, j - 1, ("x", "y", "xy")[j - 1])
        for j in (1, 2, 3)
    ]
    for copy in meeting:
        copy.start()

    def first_columns(pairs, own):
        for core in range(2):

            @pl.when(c == core)
            def _():
                for f, pair in enumerate(pairs):
                    start = FF // 8 * (core if own else 1 - core) + FZ * f
                    g1_o[:, start : start + FZ] = jnp.concatenate(pair, axis=1)

    for load in loads[9:]:
        load.wait()
    for f in range(NF):
        mine[G1R * f : G1R * (f + 1), :] = fv[f, :G1R, :].astype(bf16)
    swap = remote(mine, theirs, csems, 3, "c")
    swap.start()
    first_columns([[fv[f, :DC, :], fv[f, 2 * DC : 3 * DC, : FZ - LANES]] for f in range(NF)], True)
    for copy in second_q:
        copy.wait()
    layer_sums([(ka.at[0], ra.at[0], r2a), (kb.at[0], rb.at[0], r2b)], zs, zk)
    third_q = [remote(zs.at[k], zr.at[k], qsems, 6 + k, f"z{k + 1}") for k in (2, 1, 0)]
    for copy in third_q:
        copy.start()
    home = homeward(gb.at[0], gb.at[1], grad, tsems, lsems.at[len(pairs)])
    home_start(*home)
    for copy in meeting:
        copy.wait()
    spread_z = [remote(square, every.at[z], ssems, 2 + k, f"z{k}") for k in (1, 2, 3)]
    every[z] = square[...]
    for copy in spread_z:
        copy.start()
    for f in range(NF):
        part = fv[f, G1R:, :]
        tail = part[2 * FZ :]
        tail = jnp.concatenate([tail[:, 32 * k : 32 * (k + 1)] for k in range(4)], axis=0)
        g2_o[FZ * f : FZ * (f + 1), :] = jnp.concatenate([part[:FZ], part[FZ : 2 * FZ], tail], axis=1)
    for copy in third_p:
        copy.wait()
    part = pk[...] + pr[0].astype(f32) + pr[1].astype(f32) + pr[2].astype(f32)
    tail = part[2 * DC :]
    tail = jnp.concatenate([tail[:, 32 * k : 32 * (k + 1)] for k in range(3)], axis=0)
    gp_o[...] = jnp.concatenate([part[:DC], part[DC : 2 * DC], tail], axis=1)
    swap.wait()
    first_columns(
        [
            [theirs[G1R * f + DC : G1R * f + 2 * DC, :].astype(f32),
             theirs[G1R * f + 2 * DC : G1R * (f + 1), FZ - LANES :].astype(f32)]
            for f in range(NF)
        ],
        False,
    )

    stores = upto([gp_o, g1_o, g2_o, ada_o], [gp_out, g1_out, g2_out, ada_out], xsems)
    for copy in stores[:3]:
        copy.start()

    for copy in spread_z:
        copy.wait()
    columns = jnp.concatenate([every[i, j] for i in range(4) for j in range(4)], axis=0)
    width = 3 * D // 2
    angles = columns[:, width : width + 1] * freq[b % 4]
    cond = jax.nn.silu(jnp.where(b < 4, jnp.cos(angles), jnp.sin(angles))).astype(bf16).astype(f32)
    columns = columns[:, :width]
    ada_o[...] = lax.dot_general(
        cond, columns, (((0,), (0,)), ((), ())), precision=lax.Precision.HIGHEST, preferred_element_type=f32
    )
    stores[3].start()
    row = jnp.sum(columns, axis=0, keepdims=True)
    row_out[0] = row
    row_in[t] = row
    rows_ = [remote(row_out.at[0], row_in.at[t], ssems, 6 + j, name) for j, name in enumerate(("x", "y", "xy"))]
    for copy in rows_:
        copy.start()

    for odd_, (copies, kept, more) in enumerate(((third_e, ezk, ezr), (third_q, zk, zr))):
        for copy in copies:
            copy.wait()
        q = total_of(kept[...], more[0], more[1], more[2])
        tail = q[2 * TQ :]
        n = TQ // 3
        tail = jnp.concatenate([tail[n * 0 : n, 32 * k : 32 * (k + 1)] for k in range(3)], axis=0)
        qt[odd_] = jnp.transpose(jnp.concatenate([q[:TQ], q[TQ : 2 * TQ], tail], axis=1))
        mine_q[odd_] = qt[odd_, pl.ds(pl.multiple_of(DC * (1 - c), 16), DC), :].astype(bf16)
        swap = remote(mine_q.at[odd_], theirs_q.at[odd_], csems, 4 + odd_, "c")
        swap.start()
        if odd_ == 1:
            line_o[...] = q[QR - 8 :]
    own = [qt[odd_, pl.ds(pl.multiple_of(DC * c, 16), DC), :] for odd_ in range(2)]

    def qkv_columns(values, owned):
        for core in range(2):

            @pl.when(c == core)
            def _():
                for odd_ in range(2):
                    for j in range(3):
                        start = DZ * j + DC * (core if owned else 1 - core) + HD * odd_
                        gq_o[:, start : start + HD] = values[odd_][:, HD * j : HD * (j + 1)]

    qkv_columns(own, True)
    for odd_ in range(2):
        remote(mine_q.at[odd_], theirs_q.at[odd_], csems, 4 + odd_, "c").wait()
    qkv_columns([theirs_q[odd_].astype(f32) for odd_ in range(2)], False)
    for copy in rows_:
        copy.wait()
    row = row_in[z]
    ada_bias_o[...] = jnp.where(c == 0, row[:, : width // 2], row[:, width // 2 :])
    home_wait(*home)
    for copy in stores:
        copy.wait()


def final_kernel(out_rows, grad_rows, gq, gp, g1, g2, ada, ada_bias, line,
                 out, grad, gq_o, gp_o, g1_o, g2_o, ada_o, ada_bias_o, b_fc1, b_fc2, b_proj, b_q, b_v):
    out[...] = out_rows[...]
    grad[...] = grad_rows[...].astype(f32)
    gq_o[...] = gq[...]
    gp_o[...] = gp[...]
    g1_o[...] = g1[...]
    g2_o[...] = jnp.transpose(g2[...])
    ada_o[...] = ada[...]
    ada_bias_o[...] = ada_bias[...].reshape(-1)
    flat = jnp.concatenate([line[k : k + 1, :] for k in range(3)], axis=1)
    n1, n = FF // 32, D // 32
    b_fc1[...] = flat[:, :n1].reshape(-1)
    for k, ref in enumerate((b_fc2, b_proj, b_q, b_v)):
        ref[...] = flat[:, n1 + n * k : n1 + n * (k + 1)].reshape(-1)


def one_item_per_chip(
    tokens, cotangent, timesteps, bucket_ids, head_masks, channel_masks, skip_rows,
    w_qkv, q_bias, v_bias, w_proj, proj_bias, w_fc1, fc1_bias, w_fc2, fc2_bias, ada_weight, ada_bias,
):
    b, t = lax.axis_index("bucket"), lax.axis_index("tok")
    z, c, y, x = b // 2, b % 2, t // 2, t % 2

    def core_half(v, *dims):
        return lax.dynamic_index_in_dim(v.reshape(dims), c, 1, keepdims=False)

    vmem, smem = pl.BlockSpec(memory_space=pltpu.VMEM), pl.BlockSpec(memory_space=pltpu.SMEM)
    steps = -np.float32(math.log(10000.0)) * np.arange(D // 2, dtype=np.float32) / np.float32(D // 2)
    freq = jnp.asarray(np.exp(steps).reshape(1, D // 2))
    ada_cols = ada_weight.shape[1]
    front, _ = call(
        front_kernel, "front",
        (sds((L, D), bf16), sds((L, D), bf16), sds((L, 3 * WC), bf16), sds((D, 3 * WC), bf16), sds((NF, D, FB), bf16), sds((8, D), f32), sds((L, 1), f32), sds((1, WC), f32), sds((NF, 1, FB), f32),
         sds((NF, 1, FB), f32)),
        (tokens, timesteps, bucket_ids, skip_rows, ada_weight.T, ada_bias, head_masks, channel_masks,
         w_qkv, w_fc1, q_bias, v_bias, fc1_bias, freq),
        in_specs=[ANY, smem, smem, vmem, ANY, vmem, vmem, vmem, ANY, ANY, vmem, vmem, vmem, vmem],
        out_specs=[ANY] * 5 + [vmem] * 5,
        scratch=[vm(L, D), vm(D, 3 * D), vm(D, 3 * WC), vm(D, FF), vm(NF, D, FB), vm(ada_cols, D),
                 vm(8, LANES, dtype=jnp.int32), vm(8, LANES, dtype=jnp.int32), vm(8, ada_cols, dtype=f32), vm(3, 8, ada_cols, dtype=f32),
                 vm(4, 8, ada_cols, dtype=f32), vm(L, D), vm(L, 3 * WC), pltpu.SemaphoreType.DMA((2, 5)),
                 pltpu.SemaphoreType.DMA((2, 4)), pltpu.SemaphoreType.DMA((2, 6)), pltpu.SemaphoreType.DMA((8,))],
        peers=("c", "t0", "t1", "x", "y", "xy"), cid=10, flops=2 * L * D * 3 * WC, nbytes=50e6,
    )
    tok, shifted, qkv, wq, w1, mod, kept, hmask, chan, b1 = front
    w2 = w_fc2.reshape(4, 2, NF, FZ, D)
    wp = w_proj.reshape(4, 2, DC, D)
    (g_all, mixed, shifted2, attn), _ = call(
        functools.partial(attn_kernel, 512), "attn",
        (sds((L, D), bf16), sds((L, WC), bf16), sds((L, D), bf16), sds((LH, D), f32)),
        (cotangent, qkv, hmask, wp, proj_bias, tok, mod),
        in_specs=[ANY, ANY, vmem, ANY, vmem, ANY, vmem],
        out_specs=[ANY] * 4,
        scratch=[vm(L, D), vm(L, 3 * WC)] + [vm(HC, L, HD)] * 2 + [vm(HC, L, LANES)] + [vm(L, WC), vm(L, WC), vm(2, 4, DC, D), vm(L, D), vm(L, D),
                 vm(LH, D, dtype=f32),
                 pltpu.SemaphoreType.DMA((2, 4)), pltpu.SemaphoreType.DMA((2, 2)), pltpu.SemaphoreType.DMA((2, 2)),
                 pltpu.SemaphoreType.DMA((7,)), dma(2, 4)],
        peers=("c", "t0", "t1"), cid=11, flops=16e9, nbytes=5e6,
    )

    slot1, slot2, slot3 = sds((2, 4, GA, LANES)), sds((2, 4, GB, LANES)), sds((4, 2, 2, 2 * GC, LANES))
    part1, part2, part3 = sds(slot1.shape[1:]), sds(slot2.shape[1:]), sds(slot3.shape[2:])
    one = [part1, part1, part2, part2, part1, part2, part3, part3]
    rows_half = sds((LH, D), bf16)
    own, _ = call(
        mlp_kernel, "mlp",
        one + one + [slot1, slot1, slot2, slot2, slot3] + [rows_half] * 4 + [sds((NF, 1, FB), f32), sds((1, D), f32)],
        (shifted2, g_all, kept, mod, w1, b1, chan, w2),
        in_specs=[ANY, ANY, vmem, vmem, ANY, vmem, vmem, ANY],
        out_specs=[ANY] * 21 + [vmem, vmem, ANY, ANY, vmem, vmem],
        scratch=[vm(L, D), vm(L, D), vm(2, D, FB), vm(2, 4, FZ, D), vm(L, FB), vm(L, FB),
                 vm(L, FB), vm(L, D, dtype=f32), vm(L, D, dtype=f32), vm(2, LH, D), vm(4, D, TD)]
        + [vm(2, *slot1.shape)] * 2 + [vm(2, *slot2.shape)] * 2 + [vm(2, *slot3.shape), vm(2, 3, *slot3.shape[1:])]
        + [vm(2, *p.shape) for p in (part1, part2)] * 2
        + [dma(2, 20), dma(2, 2), dma(2), dma(2, 2), dma(2, 9)],
        peers=("c", "x", "y", "z1", "z2", "z3"), cid=0,
        flops=36 * L * D * FB, nbytes=40e6,
    )
    second0, second1, slots = own[:8], own[8:16], own[16:21]
    branch, ds2, branch_r, ds2_r, sum1, sum2 = own[21:]

    slot_a, slot_b = sds((2, 4, PA, LANES), bf16), sds((2, 4, PR - PA, LANES), bf16)
    own, given = call(
        middle_kernel, "middle",
        (sds((LH, D), f32), rows_half, sds((L, WC), bf16), slot_a, slot_a, slot_b, slot_b, sds((8, D), f32),
         sds((8, D), f32)),
        (ds2, ds2_r, branch, branch_r, attn, tok, g_all, kept, mod, fc2_bias, mixed, wp),
        in_specs=[ANY] * 7 + [vmem] * 3 + [ANY] * 2,
        scratch=[vm(4, LH, D), vm(LH, D, dtype=f32), vm(2, LH, D), vm(L, WC), vm(4, DC, D), vm(L, D), vm(4, WC, TD),
                 dma(2, 4), dma(2), dma(4, 7)],
        peers=("c",), cid=3, jobs=[FirstSum(*slots), SecondSum(*second0)],
        flops=4 * L * D * WC, nbytes=20e6,
    )
    d_resid, out_rows, dh, *slots_p, sums_mid, sum_attn = own
    first2, result0 = given
    slot_q = vm(2, 4, QA, LANES)
    fourth = vm(4, QA, LANES)
    part_q = sds((4, QA, LANES), bf16)
    own, given = call(
        functools.partial(attn_back_kernel, 512), "attn_back",
        [sds((L, 3 * WC), bf16)] + [part_q] * 6 + [sds((8, WQ), f32)], (qkv, dh, shifted, hmask),
        in_specs=[ANY] * 3 + [vmem],
        out_specs=[ANY] * 7 + [vmem],
        scratch=[vm(L, 3 * WC), vm(L, WC), vm(L, D), vm(L, 3 * WC)] + [vm(HC // 2, L, HD)] * 4
        + [vm(HC // 2, L, HD, dtype=f32)] * 2 + [vm(4, 4, TQ, DZ, dtype=f32)] + [slot_q] * 4 + [fourth] * 4
        + [dma(2, 4), dma(8)],
        cid=4, ticks=True,
        jobs=[SecondThird(*second1, tick_at=1), SecondThird(*first2[:4], slots[0], slots[2], *first2[4:], start_at=1, tick_at=2),
              FirstSecond(*slots_p, start_at=1, tick_at=3), ThirdSum(*result0), GoHome(out_rows, tick_at=2)],
        flops=30e9, nbytes=9e6,
    )
    dqkv, *second_q, even_sums = own
    final1, final2, (sent_p, kept_p), final0, (output,) = given
    width = ada_cols + LANES
    (grad_rows, gq, gp, g1, g2, grad_ada_weight, grad_ada_bias, line), _ = call(
        end_kernel, "end",
        (sds((2, LB, D), bf16), sds((DC, 3 * TD), f32), sds((DC, TD), f32), sds((DC, FF // 4), f32),
         sds((FF // 8, TD), f32), sds((DC, ada_cols), f32), sds((1, ada_cols // 2), f32), sds((8, LANES), f32)),
        (dqkv, shifted, even_sums, sum1, sum2, sum_attn, wq, d_resid, tok, mod, sums_mid, *final0, *final1, *final2, sent_p,
         kept_p, freq.reshape(4, 1, DC), *second_q),
        in_specs=[ANY] * 2 + [vmem] * 4 + [ANY] * 3 + [vmem] * 2 + [ANY] * 8 + [vmem] + [ANY] * 6,
        out_specs=[ANY, vmem] + [ANY] * 4 + [vmem] * 2,
        scratch=[vm(L, 3 * WC), vm(L, D), vm(4, 4, 8, LANES, dtype=f32), vm(4, 4, TQ, DZ, dtype=f32)]
        + [slot_q] * 6 + [fourth] * 4 + [vm(3, QR, LANES), vm(QR, LANES, dtype=f32), vm(3, QR, LANES)]
        + [fourth] * 6 + [vm(3, QR, LANES), vm(QR, LANES, dtype=f32), vm(3, QR, LANES)]
        + [vm(2, DZ, TQ, dtype=f32), vm(D, 3 * WC), vm(LH, D, dtype=f32), vm(LH, D),
           vm(NF, G1R + G2R, LANES, dtype=f32)] + [vm(2, LB, D)] * 3
        + [vm(8, D, dtype=f32)] * 2 + [vm(4, 1, width, dtype=f32)] * 2
        + [vm(4, 4, 1, width, dtype=f32), vm(1, 1, ada_cols, dtype=f32), vm(4, 1, ada_cols, dtype=f32)]
        + [vm(NF * G1R, LANES)] * 2 + [vm(2, DC, TQ)] * 2 + [vm(PR, LANES, dtype=f32), vm(3, PR, LANES)]
        + [vm(*v, dtype=f32) for v in ((DC, TD), (DC, FF // 4), (FF // 8, TD), (DC, ada_cols))]
        + [dma(2, 9), dma(2, 5), dma(2, 6), dma(2, 2), dma(2, 9), dma(2, 3), dma(23), dma(4)],
        peers=("c", "t0", "t1", "x", "y", "xy", "z1", "z2", "z3"), cid=5,
        flops=4 * L * D * 3 * WC, nbytes=30e6,
    )
    thin = lambda height, width: pl.BlockSpec((height, width), lambda i: (i, 0))
    tokens_spec = pl.BlockSpec((2, LB // 2, D), lambda i: (0, i, 0))
    ends = [thin(DC // 2, 3 * TD), thin(DC // 2, TD), thin(DC // 2, FF // 4)]
    bias_cols = ada_cols // 2
    finals, _ = call(
        final_kernel, "final",
        (sds((2, LB, D), bf16), sds((2, LB, D), f32), sds((DC, 3 * TD), f32), sds((DC, TD), f32), sds((DC, FF // 4), f32),
         sds((TD, FF // 8), f32), sds((DC, ada_cols), f32), sds((bias_cols,), f32), sds((FF // 32,), f32))
        + (sds((D // 32,), f32),) * 4,
        (output, grad_rows, gq, gp, g1, g2, grad_ada_weight, grad_ada_bias, line),
        grid=(2,),
        in_specs=[tokens_spec, tokens_spec, *ends, full((FF // 8, TD)), thin(DC // 2, ada_cols), full((1, bias_cols)),
                  full((8, LANES))],
        out_specs=[tokens_spec, tokens_spec, *ends, full((TD, FF // 8)), thin(DC // 2, ada_cols), full((bias_cols,)),
                   full((FF // 32,))] + [full((D // 32,))] * 4,
    )
    output, grad_tokens, gq, gp, g1, g2, g_ada, ada_b, b_fc1, b_fc2, b_proj, b_q, b_v = finals
    return (output, grad_tokens, gq, b_q, b_v, gp, b_proj, g1, b_fc1, g2.T, b_fc2, g_ada, ada_b)


def gelu_tanh(values):
    return jax.nn.gelu(values, approximate=True)


def split_heads(key_value, model_width, head_dim):
    item_count, length = (key_value.shape[0], key_value.shape[1])
    key_rows = key_value[:, :, :model_width].reshape(
        item_count, length, model_width // head_dim, head_dim
    )
    value_rows = key_value[:, :, model_width:].reshape(
        item_count, length, model_width // head_dim, head_dim
    )
    return (key_rows, value_rows)


def scores_of(queries, key_rows, score_scale):
    return (
        jnp.einsum("nqhe,nkhe->nhqk", queries, key_rows, preferred_element_type=jnp.float32)
        * score_scale
    )


def to_blocks(values, per_step):
    return values.reshape((values.shape[0] // per_step, per_step) + values.shape[1:])


def from_blocks(values):
    return values.reshape((values.shape[0] * values.shape[1],) + values.shape[2:])


def on_device(
    tokens,
    cotangent,
    timesteps,
    bucket_ids,
    head_masks,
    channel_masks,
    skip_rows,
    w_qkv,
    q_bias,
    v_bias,
    w_proj,
    proj_bias,
    w_fc1,
    fc1_bias,
    w_fc2,
    fc2_bias,
    ada_weight,
    ada_bias,
):
    item_count, local_len, model_width = tokens.shape
    row_count = item_count * local_len
    head_dim = model_width // HEADS
    score_scale = 1.0 / math.sqrt(head_dim)
    hidden_width = w_fc1.shape[1]
    ada_cols = ada_weight.shape[1]
    tok_index = lax.axis_index("tok")
    per_step = 1
    for candidate in range(1, item_count + 1):
        per_step = candidate
    condition = jax.nn.silu(step_embedding(timesteps, model_width)).astype(jnp.bfloat16)
    mod_local = jnp.dot(
        condition, ada_weight, preferred_element_type=jnp.float32
    ) + ada_bias.astype(jnp.float32)
    modulation = lax.all_gather(mod_local, "tok", axis=1, tiled=True)
    pieces = modulation.reshape(item_count, 6, 1, model_width)
    shift_a = pieces[:, 0]
    scale_a = pieces[:, 1]
    gate_a = pieces[:, 2]
    shift_m = pieces[:, 3]
    scale_m = pieces[:, 4]
    gate_m = pieces[:, 5]
    chosen = (jnp.arange(head_masks.shape[0], dtype=jnp.int32) == bucket_ids[0]).astype(jnp.float32)
    head_on = jnp.sum(chosen[:, None] * head_masks.astype(jnp.float32), axis=0)
    group_on = jnp.sum(chosen[:, None] * channel_masks.astype(jnp.float32), axis=0)
    channel_on = jnp.repeat(group_on, hidden_width // group_on.shape[0])
    positions = tok_index * local_len + jnp.arange(local_len, dtype=jnp.int32)
    skipped = jnp.any(skip_rows[:, :, None] == positions[None, None, :], axis=1)
    kept_rows = 1.0 - skipped.astype(jnp.float32)
    inputs = tokens.astype(jnp.float32)
    normed, inverse = normalize(inputs)
    shifted = (
        (normed * (1.0 + scale_a) + shift_a).astype(jnp.bfloat16).reshape(row_count, model_width)
    )
    qkv_bias = jnp.concatenate([q_bias, jnp.zeros_like(q_bias), v_bias]).astype(jnp.float32)
    projected = (jnp.dot(shifted, w_qkv, preferred_element_type=jnp.float32) + qkv_bias).astype(
        jnp.bfloat16
    )
    projected = projected.reshape(item_count, local_len, 3 * model_width)
    queries = projected[:, :, :model_width].reshape(item_count, local_len, HEADS, head_dim)
    key_value = projected[:, :, model_width:]
    all_kv = lax.all_gather(key_value, "tok", axis=1, tiled=True)

    def forward_block(packed):
        query_block, kv_block = packed
        key_rows, value_rows = split_heads(kv_block, model_width, head_dim)
        scores = scores_of(query_block, key_rows, score_scale)
        top_score = jnp.max(scores, axis=-1, keepdims=True)
        expanded = jnp.exp(scores - top_score)
        totals = jnp.sum(expanded, axis=-1, keepdims=True)
        weights_low = (expanded / totals).astype(jnp.bfloat16)
        head_out = (
            jnp.einsum(
                "nhqk,nkhe->nqhe", weights_low, value_rows, preferred_element_type=jnp.float32
            )
            * head_on[:, None]
        )
        return (head_out.astype(jnp.bfloat16), top_score + jnp.log(totals))

    mixed_heads, log_total = lax.map(
        forward_block, (to_blocks(queries, per_step), to_blocks(all_kv, per_step))
    )
    log_total = from_blocks(log_total)
    mixed = from_blocks(mixed_heads).reshape(row_count, model_width)
    attn = (
        jnp.dot(mixed, w_proj, preferred_element_type=jnp.float32) + proj_bias.astype(jnp.float32)
    ).reshape(item_count, local_len, model_width)
    resid = inputs + gate_a * attn
    normed2, inverse2 = normalize(resid)
    shifted2 = (
        (normed2 * (1.0 + scale_m) + shift_m).astype(jnp.bfloat16).reshape(row_count, model_width)
    )
    pre = jnp.dot(shifted2, w_fc1, preferred_element_type=jnp.float32) + fc1_bias.astype(
        jnp.float32
    )
    activated, gelu_pull = jax.vjp(gelu_tanh, pre)
    hidden = (activated * channel_on).astype(jnp.bfloat16)
    branch = (
        jnp.dot(hidden, w_fc2, preferred_element_type=jnp.float32) + fc2_bias.astype(jnp.float32)
    ).reshape(item_count, local_len, model_width)
    gated = kept_rows[:, :, None] * gate_m
    output = (resid + gated * branch).astype(jnp.bfloat16)
    incoming = cotangent.astype(jnp.float32)
    d_gate_m = jnp.sum(kept_rows[:, :, None] * branch * incoming, axis=1)
    d_branch = (gated * incoming).astype(jnp.bfloat16).reshape(row_count, model_width)
    grad_w_fc2 = jnp.dot(hidden.T, d_branch, preferred_element_type=jnp.float32)
    grad_fc2_bias = jnp.sum(d_branch.astype(jnp.float32), axis=0)
    d_hidden = jnp.dot(d_branch, w_fc2.T, preferred_element_type=jnp.float32)
    d_pre = gelu_pull(d_hidden * channel_on)[0].astype(jnp.bfloat16)
    grad_w_fc1 = jnp.dot(shifted2.T, d_pre, preferred_element_type=jnp.float32)
    grad_fc1_bias = jnp.sum(d_pre.astype(jnp.float32), axis=0)
    d_shifted2 = jnp.dot(d_pre, w_fc1.T, preferred_element_type=jnp.float32).reshape(
        item_count, local_len, model_width
    )
    d_shift_m = jnp.sum(d_shifted2, axis=1)
    d_scale_m = jnp.sum(d_shifted2 * normed2, axis=1)
    d_resid = incoming + normalize_back(d_shifted2 * (1.0 + scale_m), normed2, inverse2)
    d_gate_a = jnp.sum(attn * d_resid, axis=1)
    d_attn = (gate_a * d_resid).astype(jnp.bfloat16).reshape(row_count, model_width)
    grad_w_proj = jnp.dot(mixed.T, d_attn, preferred_element_type=jnp.float32)
    grad_proj_bias = jnp.sum(d_attn.astype(jnp.float32), axis=0)
    d_mixed = jnp.dot(d_attn, w_proj.T, preferred_element_type=jnp.float32).astype(jnp.bfloat16)
    d_heads = d_mixed.reshape(item_count, local_len, HEADS, head_dim) * head_on[:, None].astype(
        jnp.bfloat16
    )
    again_kv = lax.all_gather(key_value, "tok", axis=1, tiled=True)

    def backward_block(packed):
        query_block, kv_block, head_grads, totals_log = packed
        key_rows, value_rows = split_heads(kv_block, model_width, head_dim)
        scores = scores_of(query_block, key_rows, score_scale)
        probs = jnp.exp(scores - totals_log)
        d_probs = jnp.einsum(
            "nqhe,nkhe->nhqk", head_grads, value_rows, preferred_element_type=jnp.float32
        )
        row_dot = jnp.sum(probs * d_probs, axis=-1, keepdims=True)
        d_scores = (probs * (d_probs - row_dot)).astype(jnp.bfloat16)
        d_queries = (
            jnp.einsum("nhqk,nkhe->nqhe", d_scores, key_rows, preferred_element_type=jnp.float32)
            * score_scale
        )
        return (d_queries, row_dot)

    mapped = lax.map(
        backward_block,
        (
            to_blocks(queries, per_step),
            to_blocks(again_kv, per_step),
            to_blocks(d_heads, per_step),
            to_blocks(log_total, per_step),
        ),
    )
    d_queries = from_blocks(mapped[0])
    row_dot = from_blocks(mapped[1])
    queries_all, head_grads_all = (
        lax.all_gather(queries, "tok", axis=1, tiled=True),
        lax.all_gather(d_heads, "tok", axis=1, tiled=True),
    )
    totals_all, row_dot_all = (
        lax.all_gather(log_total, "tok", axis=2, tiled=True),
        lax.all_gather(row_dot, "tok", axis=2, tiled=True),
    )

    def key_block(packed):
        kv_block, query_block, head_grads, totals_log, dots = packed
        key_rows, value_rows = split_heads(kv_block, model_width, head_dim)
        scores = (
            jnp.einsum("nkhe,nqhe->nhkq", key_rows, query_block, preferred_element_type=jnp.float32)
            * score_scale
        )
        probs = jnp.exp(scores - totals_log[:, :, None, :, 0])
        d_probs = jnp.einsum(
            "nkhe,nqhe->nhkq", value_rows, head_grads, preferred_element_type=jnp.float32
        )
        d_scores = (probs * (d_probs - dots[:, :, None, :, 0])).astype(jnp.bfloat16)
        d_keys = (
            jnp.einsum("nhkq,nqhe->nkhe", d_scores, query_block, preferred_element_type=jnp.float32)
            * score_scale
        )
        d_values = jnp.einsum(
            "nhkq,nqhe->nkhe",
            probs.astype(jnp.bfloat16),
            head_grads,
            preferred_element_type=jnp.float32,
        )
        return jnp.concatenate(
            [
                d_keys.reshape(d_keys.shape[0], local_len, model_width),
                d_values.reshape(d_values.shape[0], local_len, model_width),
            ],
            axis=2,
        )

    d_kv = from_blocks(
        lax.map(
            key_block,
            (
                to_blocks(key_value, per_step),
                to_blocks(queries_all, per_step),
                to_blocks(head_grads_all, per_step),
                to_blocks(totals_all, per_step),
                to_blocks(row_dot_all, per_step),
            ),
        )
    )
    d_qkv = jnp.concatenate([d_queries.reshape(item_count, local_len, model_width), d_kv], axis=2)
    d_qkv = d_qkv.astype(jnp.bfloat16).reshape(row_count, 3 * model_width)
    grad_w_qkv = jnp.dot(shifted.T, d_qkv, preferred_element_type=jnp.float32)
    qkv_sums = jnp.sum(d_qkv.astype(jnp.float32), axis=0)
    grad_q_bias = qkv_sums[:model_width]
    grad_v_bias = qkv_sums[2 * model_width :]
    d_shifted = jnp.dot(d_qkv, w_qkv.T, preferred_element_type=jnp.float32).reshape(
        item_count, local_len, model_width
    )
    d_shift_a = jnp.sum(d_shifted, axis=1)
    d_scale_a = jnp.sum(d_shifted * normed, axis=1)
    grad_tokens = d_resid + normalize_back(d_shifted * (1.0 + scale_a), normed, inverse)
    d_modulation = jnp.concatenate(
        [d_shift_a, d_scale_a, d_gate_a, d_shift_m, d_scale_m, d_gate_m], axis=1
    )
    d_modulation = lax.psum(d_modulation, "tok")
    mod_columns = lax.dynamic_slice_in_dim(d_modulation, tok_index * ada_cols, ada_cols, 1)
    grad_ada_weight = jnp.dot(
        condition.astype(jnp.float32).T, mod_columns, precision=lax.Precision.HIGHEST
    )
    grad_ada_bias = jnp.sum(d_modulation, axis=0)
    bucket_done = (
        lax.psum_scatter(grad_w_qkv, "bucket", scatter_dimension=0, tiled=True),
        lax.psum_scatter(grad_w_proj, "bucket", scatter_dimension=0, tiled=True),
        lax.psum_scatter(grad_w_fc1, "bucket", scatter_dimension=0, tiled=True),
        lax.psum_scatter(grad_w_fc2, "bucket", scatter_dimension=0, tiled=True),
        lax.psum_scatter(grad_q_bias, "bucket", scatter_dimension=0, tiled=True),
        lax.psum_scatter(grad_v_bias, "bucket", scatter_dimension=0, tiled=True),
        lax.psum_scatter(grad_proj_bias, "bucket", scatter_dimension=0, tiled=True),
        lax.psum_scatter(grad_fc1_bias, "bucket", scatter_dimension=0, tiled=True),
        lax.psum_scatter(grad_fc2_bias, "bucket", scatter_dimension=0, tiled=True),
        lax.psum_scatter(grad_ada_weight, "bucket", scatter_dimension=0, tiled=True),
        lax.psum_scatter(grad_ada_bias, "bucket", scatter_dimension=0, tiled=True),
    )
    token_done = (
        lax.psum_scatter(bucket_done[0], "tok", scatter_dimension=1, tiled=True),
        lax.psum_scatter(bucket_done[1], "tok", scatter_dimension=1, tiled=True),
        lax.psum_scatter(bucket_done[2], "tok", scatter_dimension=1, tiled=True),
        lax.psum_scatter(bucket_done[3], "tok", scatter_dimension=1, tiled=True),
        lax.psum_scatter(bucket_done[4].reshape(1, -1), "tok", scatter_dimension=1, tiled=True),
        lax.psum_scatter(bucket_done[5].reshape(1, -1), "tok", scatter_dimension=1, tiled=True),
        lax.psum_scatter(bucket_done[6].reshape(1, -1), "tok", scatter_dimension=1, tiled=True),
        lax.psum_scatter(bucket_done[7].reshape(1, -1), "tok", scatter_dimension=1, tiled=True),
        lax.psum_scatter(bucket_done[8].reshape(1, -1), "tok", scatter_dimension=1, tiled=True),
    )
    finished = (
        token_done[0],
        token_done[1],
        token_done[2],
        token_done[3],
        token_done[4],
        token_done[5],
        token_done[6],
        token_done[7],
        token_done[8],
        bucket_done[9],
        bucket_done[10],
    )
    return (
        output,
        grad_tokens,
        finished[0],
        finished[4].reshape(-1),
        finished[5].reshape(-1),
        finished[1],
        finished[6].reshape(-1),
        finished[2],
        finished[7].reshape(-1),
        finished[3],
        finished[8].reshape(-1),
        finished[9],
        finished[10],
    )


def solution(mesh):
    planned = mesh.shape["tok"] == 4 and mesh.shape["bucket"] == 8
    return jax.shard_map(
        one_item_per_chip if planned else on_device,
        mesh=mesh,
        in_specs=(
            P("bucket", "tok", None),
            P("bucket", "tok", None),
            P("bucket"),
            P("bucket"),
            P(),
            P(),
            P("bucket", None),
            P(),
            P(),
            P(),
            P(),
            P(),
            P(),
            P(),
            P(),
            P(),
            P(None, "tok"),
            P("tok"),
        ),
        out_specs=(
            P("bucket", "tok", None),
            P("bucket", "tok", None),
            P("bucket", "tok"),
            P(("bucket", "tok")),
            P(("bucket", "tok")),
            P("bucket", "tok"),
            P(("bucket", "tok")),
            P("bucket", "tok"),
            P(("bucket", "tok")),
            P("bucket", "tok"),
            P(("bucket", "tok")),
            P("bucket", "tok"),
            P("bucket"),
        ),
        check_vma=False,
    )
```

```python
import functools
import math
import types

import jax
import jax.numpy as jnp
import numpy as np
from jax import lax
from jax.experimental import pallas as pl
from jax.experimental.pallas import tpu as pltpu
from jax.sharding import PartitionSpec as P

HEADS = 16
EPSILON = 1e-06
LOG2E = 1.4426950408889634
GELU_K = math.sqrt(2.0 / math.pi)
GELU_C = 0.044715
LANES = 128
bf16, f32 = jnp.bfloat16, jnp.float32


def dot_nn(a, b):
    return lax.dot_general(a, b, (((1,), (0,)), ((), ())), preferred_element_type=f32)


def dot_nt(a, b):
    return lax.dot_general(a, b, (((1,), (1,)), ((), ())), preferred_element_type=f32)


def dot_tn(a, b):
    return lax.dot_general(a, b, (((0,), (0,)), ((), ())), preferred_element_type=f32)


def step_embedding(timesteps, model_width):
    half_width = model_width // 2
    frequency = jnp.exp(-math.log(10000.0) * jnp.arange(half_width, dtype=jnp.float32) / half_width)
    angles = timesteps.astype(jnp.float32)[:, None] * frequency[None, :]
    return jnp.concatenate([jnp.cos(angles), jnp.sin(angles)], axis=1)


def normalize(values):
    centred = values - jnp.mean(values, axis=-1, keepdims=True)
    inverse = lax.rsqrt(jnp.mean(centred * centred, axis=-1, keepdims=True) + EPSILON)
    return (centred * inverse, inverse)


def normalize_back(incoming, normed, inverse):
    return inverse * (
        incoming
        - jnp.mean(incoming, axis=-1, keepdims=True)
        - normed * jnp.mean(incoming * normed, axis=-1, keepdims=True)
    )


D = 1152
DC, DZ, TD = D // 8, D // 4, D // 4
HD = D // HEADS
HC = HEADS // 2
WC = D // 2
FF = 4608
NF = 3
FB = FF // 2 // NF
FZ = FB // 4
L = 1024
LH = L // 2
LB = L // 4
G1R = 3 * DC
G2R = 2 * FZ + FZ // 4
GC = 96
GA, GB = G1R - GC, G2R - GC
PR = 2 * DC + DC // 3
PA = 176
WQ = 3 * WC // 2
TQ = WQ // 4
QR = 512
QA = QR // 2
VMEM_LIMIT = 60 * 1024 * 1024


ANY = pl.BlockSpec(memory_space=pl.ANY)
MESH = pl.DeviceIdType.MESH


def place():
    b, t = lax.axis_index("bucket"), lax.axis_index("tok")
    return b // 2, b % 2, t // 2, t % 2


def flip(value, other):
    return (value // 2 + other // 2) % 2 * 2 + (value % 2 + other % 2) % 2


def peer(name):
    z, c, y, x = place()
    if name == "x":
        x = 1 - x
    elif name == "y":
        y = 1 - y
    elif name == "xy":
        x, y = 1 - x, 1 - y
    elif name == "c":
        c = 1 - c
    elif name in ("t0", "t1"):
        c, y, x = y, c, x if name == "t0" else 1 - x
    else:
        z = flip(z, int(name[1]))
    return (z * 2 + c, y * 2 + x)


def greet(names):
    sem = pltpu.get_barrier_semaphore()
    for name in names:
        if name == "t0":
            continue
        pl.semaphore_signal(sem, inc=1, device_id=peer(name), device_id_type=MESH)
    if "t0" in names:
        _, c, y, _ = place()

        @pl.when(c != y)
        def _():
            pl.semaphore_signal(sem, inc=1, device_id=peer("t0"), device_id_type=MESH)


def meet(names):
    wanted = len([name for name in names if name != "t0"])
    if "t0" in names:
        _, c, y, _ = place()
        wanted = wanted + (c + y) % 2
    pl.semaphore_wait(pltpu.get_barrier_semaphore(), wanted)


def remote(src, dst, sems, k, name):
    return pltpu.make_async_remote_copy(
        src_ref=src, dst_ref=dst, send_sem=sems.at[0, k], recv_sem=sems.at[1, k],
        device_id=peer(name), device_id_type=MESH,
    )


def vm(*shape, dtype=bf16):
    return pltpu.VMEM(shape, dtype)


class Job:
    start_at = tick_at = 0

    def bind(self, scratch):
        return types.SimpleNamespace(**dict(zip(self.spec, scratch)))

    @property
    def scratch(self):
        return list(self.spec.values())


def sds(shape, dtype=bf16):
    return jax.ShapeDtypeStruct(shape, dtype)


def upto(sources, targets, sems):
    return [pltpu.make_async_copy(a, b, sems.at[k]) for k, (a, b) in enumerate(zip(sources, targets))]


def dma(*shape):
    return pltpu.SemaphoreType.DMA(shape)


def total_of(*parts):
    total = parts[0].astype(f32)
    for part in parts[1:]:
        total = total + part.astype(f32)
    return total


class FirstSum(Job):
    def __init__(self, keep_a, sent_a, keep_b, sent_b, third=None):
        self.third = third is not None
        self.peers = ("x", "y", "z1", "z2", "z3") if self.third else ("x", "y")
        self.ins = [keep_a, sent_a, keep_b, sent_b] + ([third] if self.third else [])
        a, b = keep_a.shape[1:], keep_b.shape[1:]
        self.outs = [sds(a), sds(a), sds(b), sds(b)]
        self.spec = dict(ka=vm(*a), ra=vm(*a), oa=vm(*a), kb=vm(*b), rb=vm(*b), ob=vm(*b), sems=dma(2, 7), local=dma(7))
        if self.third:
            c = third.shape[1:]
            self.outs += [sds(c[1:]), sds(c[1:])]
            self.spec.update(kc=vm(*c), rc=vm(3, *c))

    def plan(self, ins, outs, scratch):
        v = self.bind(scratch)
        far = [
            remote(ins[1].at[1], v.ra, v.sems, 0, "x"), remote(ins[3].at[1], v.rb, v.sems, 1, "y"),
            remote(ins[1].at[0], outs[1], v.sems, 2, "x"), remote(ins[3].at[0], outs[3], v.sems, 3, "y"),
        ]
        near = upto([ins[0].at[1], ins[2].at[1]], [v.ka, v.kb], v.local)
        if self.third:
            far += [remote(ins[4].at[k], v.rc.at[k - 1], v.sems, 3 + k, f"z{k}") for k in (3, 2, 1)]
            near.append(pltpu.make_async_copy(ins[4].at[0], v.kc, v.local.at[2]))
        return far, near

    def finish(self, ins, outs, scratch):
        v = self.bind(scratch)
        v.oa[...] = total_of(v.ka[...], v.ra[...]).astype(bf16)
        v.ob[...] = total_of(v.kb[...], v.rb[...]).astype(bf16)
        pairs = [(v.oa, outs[0]), (v.ob, outs[2])]
        if self.third:
            v.kc[...] = total_of(v.kc[...], v.rc[0], v.rc[1], v.rc[2]).astype(bf16)
            pairs += [(v.kc.at[0], outs[4]), (v.kc.at[1], outs[5])]
        return [pltpu.make_async_copy(a, b, v.local.at[3 + k]) for k, (a, b) in enumerate(pairs)]


def layer_sums(streams, zs, zk):
    start = 0
    for kv, qv, rv in streams:
        end = start + rv.shape[1]
        for j in range(4):
            total = total_of(kv[j], qv[j], rv[j])
            if j == 0:
                zk[start:end, :] = total
            else:
                zs[j - 1, start:end, :] = total.astype(bf16)
        start = end


class SecondSum(Job):
    peers = ("x", "y")

    def __init__(self, on_a, q_a, on_b, q_b, keep_a, keep_b, keep_c=None, sent_c=None, start_at=0):
        self.start_at = start_at
        self.third = keep_c is not None
        self.ins = [on_a, q_a, on_b, q_b, keep_a, keep_b] + ([keep_c, sent_c] if self.third else [])
        a, b = on_a.shape, on_b.shape
        rows_ = a[1] + b[1]
        self.outs = [sds((3, rows_, LANES)), sds((rows_, LANES), f32)]
        self.spec = dict(ka=vm(*a), qa=vm(*a), ra=vm(*a), kb=vm(*b), qb=vm(*b), rb=vm(*b), zs=vm(3, rows_, LANES),
                         zk=vm(rows_, LANES, dtype=f32), sems=dma(2, 3), local=dma(9))
        if self.third:
            c = keep_c.shape
            self.outs += [sds(c[1:]), sds(c[1:])]
            self.spec.update(kc=vm(*c), rc=vm(*c))

    def plan(self, ins, outs, scratch):
        v = self.bind(scratch)
        whole = [k.at[0] if len(k.shape) == 4 else k for k in ins[4:6]]
        far = [remote(ins[0], v.ra, v.sems, 0, "y"), remote(ins[2], v.rb, v.sems, 1, "x")]
        near = upto([whole[0], ins[1], whole[1], ins[3]], [v.ka, v.qa, v.kb, v.qb], v.local)
        if self.third:
            far.append(remote(ins[7], v.rc, v.sems, 2, "x"))
            near.append(pltpu.make_async_copy(ins[6], v.kc, v.local.at[4]))
        return far, near

    def add(self, v):
        layer_sums([(v.ka, v.qa, v.ra), (v.kb, v.qb, v.rb)], v.zs, v.zk)
        if self.third:
            v.kc[...] = total_of(v.kc[...], v.rc[...]).astype(bf16)

    def finish(self, ins, outs, scratch):
        v = self.bind(scratch)
        self.add(v)
        pairs = [(v.zs, outs[0]), (v.zk, outs[1])]
        if self.third:
            pairs += [(v.kc.at[0], outs[2]), (v.kc.at[1], outs[3])]
        return [pltpu.make_async_copy(a, b, v.local.at[5 + k]) for k, (a, b) in enumerate(pairs)]


class ThirdSum(Job):
    def __init__(self, sent, kept, keep_c=None, sent_c=None):
        self.third = keep_c is not None
        self.peers = ("z1", "z2", "z3", "y") if self.third else ("z1", "z2", "z3")
        self.ins = [sent, kept] + ([keep_c, sent_c] if self.third else [])
        self.outs = [sds(kept.shape, f32)]
        self.spec = dict(got=vm(*sent.shape), kept=vm(*kept.shape, dtype=f32), sems=dma(2, 4), local=dma(4))
        if self.third:
            self.outs.append(sds(keep_c.shape, f32))
            self.spec.update(kc=vm(*keep_c.shape), rc=vm(*keep_c.shape), fc=vm(*keep_c.shape, dtype=f32))

    def plan(self, ins, outs, scratch):
        v = self.bind(scratch)
        far = [remote(ins[0].at[k], v.got.at[k], v.sems, k, f"z{k + 1}") for k in (2, 1, 0)]
        near = [pltpu.make_async_copy(ins[1], v.kept, v.local.at[0])]
        if self.third:
            far.append(remote(ins[3], v.rc, v.sems, 3, "y"))
            near.append(pltpu.make_async_copy(ins[2], v.kc, v.local.at[1]))
        return far, near

    def finish(self, ins, outs, scratch):
        v = self.bind(scratch)
        v.kept[...] = total_of(v.kept[...], v.got[0], v.got[1], v.got[2])
        pairs = [(v.kept, outs[0])]
        if self.third:
            v.fc[...] = total_of(v.kc[...], v.rc[...])
            pairs.append((v.fc, outs[1]))
        return [pltpu.make_async_copy(a, b, v.local.at[2 + k]) for k, (a, b) in enumerate(pairs)]


class SecondThird(SecondSum):
    peers = ("x", "y", "z1", "z2", "z3")

    def __init__(self, *args, start_at=0, tick_at=1):
        super().__init__(*args, start_at=start_at)
        self.tick_at = tick_at
        kept, c = self.outs[1], self.spec["kc"].shape[1:]
        self.outs = [kept, sds(c, f32)]
        self.spec.update(got=vm(3, *kept.shape), sems3=dma(2, 4), rc3=vm(*c), fc=vm(*c, dtype=f32))

    def next_copies(self, v):
        far = [remote(v.zs.at[k], v.got.at[k], v.sems3, k, f"z{k + 1}") for k in (2, 1, 0)]
        return far + [remote(v.kc.at[1], v.rc3, v.sems3, 3, "y")]

    def tick(self, ins, outs, scratch):
        v = self.bind(scratch)
        for group in self.plan(ins, outs, scratch):
            for copy in group:
                copy.wait()
        self.add(v)
        for copy in self.next_copies(v):
            copy.start()

    def settle(self, ins, outs, scratch):
        return self.next_copies(self.bind(scratch))

    def finish(self, ins, outs, scratch):
        v = self.bind(scratch)
        v.zk[...] = total_of(v.zk[...], v.got[0], v.got[1], v.got[2])
        v.fc[...] = total_of(v.kc[0], v.rc3[...])
        return upto([v.zk, v.fc], outs, v.local)


class FirstSecond(Job):
    peers = ("x", "y")

    def __init__(self, keep_a, sent_a, keep_b, sent_b, start_at=0, tick_at=1):
        self.start_at, self.tick_at = start_at, tick_at
        self.ins = [keep_a, sent_a, keep_b, sent_b]
        a, b = keep_a.shape, keep_b.shape
        rows_ = a[2] + b[2]
        self.outs = [sds((3, rows_, LANES)), sds((rows_, LANES), f32)]
        self.spec = dict(ka=vm(*a), ra=vm(*a), oa=vm(*a[1:]), ra2=vm(*a[1:]), kb=vm(*b), rb=vm(*b), ob=vm(*b[1:]),
                         rb2=vm(*b[1:]), zs=vm(3, rows_, LANES), zk=vm(rows_, LANES, dtype=f32), sems=dma(2, 6), local=dma(4))

    def plan(self, ins, outs, scratch):
        v = self.bind(scratch)
        far = [
            remote(ins[1].at[1], v.ra.at[1], v.sems, 0, "x"), remote(ins[3].at[1], v.rb.at[1], v.sems, 1, "y"),
            remote(ins[1].at[0], v.ra.at[0], v.sems, 2, "x"), remote(ins[3].at[0], v.rb.at[0], v.sems, 3, "y"),
        ]
        return far, upto([ins[0], ins[2]], [v.ka, v.kb], v.local)

    def next_copies(self, v):
        return [remote(v.oa, v.ra2, v.sems, 4, "y"), remote(v.ob, v.rb2, v.sems, 5, "x")]

    def tick(self, ins, outs, scratch):
        v = self.bind(scratch)
        for group in self.plan(ins, outs, scratch):
            for copy in group:
                copy.wait()
        v.oa[...] = total_of(v.ka[1], v.ra[1]).astype(bf16)
        v.ob[...] = total_of(v.kb[1], v.rb[1]).astype(bf16)
        for copy in self.next_copies(v):
            copy.start()

    def settle(self, ins, outs, scratch):
        return self.next_copies(self.bind(scratch))

    def finish(self, ins, outs, scratch):
        v = self.bind(scratch)
        layer_sums([(v.ka.at[0], v.ra.at[0], v.ra2), (v.kb.at[0], v.rb.at[0], v.rb2)], v.zs, v.zk)
        return [pltpu.make_async_copy(a, b, v.local.at[2 + k]) for k, (a, b) in enumerate(((v.zs, outs[0]), (v.zk, outs[1])))]


class GoHome(Job):
    peers = ("t0", "t1")

    def __init__(self, values, tick_at=1):
        self.tick_at = tick_at
        self.ins = [values]
        self.outs = [sds((2, LB, D), values.dtype)]
        self.spec = dict(sems=dma(2, 2), local=pltpu.SemaphoreType.DMA)

    def copies(self, ins, outs, scratch):
        return homeward(ins[0].at[pl.ds(0, LB)], ins[0].at[pl.ds(LB, LB)], outs[0], *scratch)

    def plan(self, ins, outs, scratch):
        home_start(*self.copies(ins, outs, scratch)[:2])
        return [], []

    def tick(self, ins, outs, scratch):
        self.copies(ins, outs, scratch)[2].start()

    def settle(self, ins, outs, scratch):
        home_wait(*self.copies(ins, outs, scratch))
        return []

    def finish(self, ins, outs, scratch):
        return []


def homeward(first, second, dst, sems, local):
    x = place()[3]
    return (
        remote(first, dst.at[x], sems, 0, "t0"),
        pltpu.make_async_copy(first, dst.at[x], local),
        remote(second, dst.at[x], sems, 1, "t1"),
    )


def home_start(away, stay, second=None):
    _, c, y, _ = place()
    pl.when(c != y)(away.start)
    pl.when(c == y)(stay.start)
    if second is not None:
        second.start()


def home_wait(away, stay, second):
    _, c, y, _ = place()
    pl.when(c != y)(away.wait)
    pl.when(c == y)(stay.wait)
    second.wait()


def call(kernel, name, out_shape, args, in_specs=None, out_specs=None, scratch=(), grid=None,
         peers=(), jobs=(), cid=None, ticks=False, flops=0, nbytes=0):
    whole = pl.BlockSpec(memory_space=pltpu.VMEM)
    single = not isinstance(out_shape, (tuple, list))
    out_shape = [out_shape] if single else list(out_shape)
    in_specs = list(in_specs) if in_specs is not None else [whole] * len(args)
    out_specs = [whole] * len(out_shape) if out_specs is None else [out_specs] if single else list(out_specs)
    counts = [len(args), sum(len(j.ins) for j in jobs), len(out_shape), sum(len(j.outs) for j in jobs), len(scratch)]
    names = sorted(set(peers).union(*[j.peers for j in jobs]))

    def run(*refs):
        groups, at = [], 0
        for n in counts:
            groups.append(refs[at : at + n])
            at += n
        bound, ai, ao, asc = [], 0, 0, at
        for j in jobs:
            bound.append((
                j, groups[1][ai : ai + len(j.ins)], groups[3][ao : ao + len(j.outs)], refs[asc : asc + len(j.scratch)]
            ))
            ai, ao, asc = ai + len(j.ins), ao + len(j.outs), asc + len(j.scratch)

        def ready():
            if names:
                meet(names)
            for j, *r in bound:
                if not j.start_at:
                    j_start(j, r)

        def j_start(j, r):
            for group in j.plan(*r):
                for copy in group:
                    copy.start()

        def tick(k):
            for j, *r in bound:
                if j.tick_at == k:
                    j.tick(*r)
            for j, *r in bound:
                if j.start_at == k:
                    j_start(j, r)

        def end():
            last = []
            for j, *r in bound:
                far, near = (j.settle(*r), []) if j.tick_at else j.plan(*r)
                for copy in far:
                    copy.wait()
                for copy in near:
                    copy.wait()
                copies = j.finish(*r)
                for copy in copies:
                    copy.start()
                last += copies
            for copy in last:
                copy.wait()

        if names:
            greet(names)
            kernel(*groups[0], *groups[2], *groups[4], ready=ready, **({"tick": tick} if ticks else {}))
            end()
        else:
            kernel(*groups[0], *groups[2], *groups[4])

    extra = {} if grid is None else {"grid": grid}
    params = {"collective_id": cid, "has_side_effects": True} if names else {}
    outs = pl.pallas_call(
        run,
        out_shape=out_shape + [o for j in jobs for o in j.outs],
        in_specs=in_specs + [ANY] * counts[1],
        out_specs=out_specs + [ANY] * counts[3],
        scratch_shapes=list(scratch) + [q for j in jobs for q in j.scratch],
        compiler_params=pltpu.CompilerParams(vmem_limit_bytes=VMEM_LIMIT, **params),
        cost_estimate=pl.CostEstimate(flops=int(flops), bytes_accessed=int(nbytes), transcendentals=0),
        name=name,
        **extra,
    )(*args, *[a for j in jobs for a in j.ins])
    own, rest, given = outs[: len(out_shape)], outs[len(out_shape) :], []
    for j in jobs:
        given.append(rest[: len(j.outs)])
        rest = rest[len(j.outs) :]
    return (own[0] if single else own), given


def full(shape):
    return pl.BlockSpec(shape, lambda *_: (0,) * len(shape))


def once(*shape):
    return pl.BlockSpec(shape, lambda *_: (0,) * len(shape), pipeline_mode=pl.Buffered(1))


def rows(block, width):
    return pl.BlockSpec((block, width), lambda i: (i, 0))


def arrivals(src, dst, tsems, csems, locals_, pieces=1):
    x = place()[3]
    n = LB // pieces
    moves = []
    for k in range(pieces):
        rows_ = pl.ds(n * k, n)
        here = [dst.at[pl.ds(LB * j + n * k, n)] for j in range(4)]
        moves.append((
            remote(src.at[x, rows_], here[0], tsems, 2 * k, "t0"),
            pltpu.make_async_copy(src.at[x, rows_], here[0], locals_.at[k]),
            remote(src.at[1 - x, rows_], here[1], tsems, 2 * k + 1, "t1"),
            [remote(here[j], here[2 + j], csems, 2 * k + j, "c") for j in range(2)],
        ))
    return moves


def leave(first, stay, second, onward):
    _, c, y, _ = place()
    pl.when(c != y)(first.start)
    pl.when(c == y)(stay.start)
    second.start()


def pass_on(first, stay, second, onward):
    _, c, y, _ = place()
    pl.when(c != y)(first.wait_recv)
    pl.when(c == y)(stay.wait)
    onward[0].start()
    second.wait_recv()
    onward[1].start()


def settle(first, stay, second, onward):
    _, c, y, _ = place()
    pl.when(c != y)(first.wait_send)
    second.wait_send()
    for copy in onward:
        copy.wait_send()


def column(n):
    return lax.broadcasted_iota(jnp.int32, (n, 1), 0)


def front_kernel(tokens, timesteps, bucket_ids, skips, ada_w, ada_b, head_masks, channel_masks, w_qkv, w_fc1,
                 q_bias, v_bias, b1, freq, tok_o, shifted_o, qkv_o, wq_o, w1_o, mod_o, kept_o, hmask_o, chan_o, b1_o,
                 tk, wqv, wqc, w1v, w1c, adav, ints, ints_other, m4, to_send, shares, shv, qkvv, csems, tsems, ssems, lsems, ready):
    z, c, y, x = place()
    t = 2 * y + x
    loads = [
        pltpu.make_async_copy(a, b, lsems.at[k])
        for k, (a, b) in enumerate(((ada_w, adav), (w_qkv, wqv), (w_fc1, w1v)))
    ]

    pieces = 2
    tok_moves = arrivals(tokens, tk, tsems, csems, lsems.at[pl.ds(6, pieces)], pieces)
    for load in loads:
        load.start()
    ready()
    leave(*tok_moves[0])
    halves = [skips[:, :LANES], skips[:, LANES:]]
    ints[0:4, :] = jnp.concatenate([halves[0][0:1], halves[1][0:1], halves[0][1:2], halves[1][1:2]], axis=0)
    for k, value in enumerate((timesteps[0], timesteps[1], bucket_ids[0], 0)):
        ints[4 + k : 5 + k, :] = jnp.full((1, LANES), value, jnp.int32)
    swap = remote(ints, ints_other, csems, 2 * pieces, "c")
    swap.start()

    loads[1].wait()
    for core in range(2):

        @pl.when(c == core)
        def _():
            for odd in range(2):
                for k in range(12):
                    to, start = WQ * odd + HD * k, DZ * k + DC * core + HD * odd
                    wqc[:, to : to + HD] = wqv[:, start : start + HD]

    swap.wait()

    mine, other = ints[...], ints_other[...]
    r = column(8)
    steps = jnp.zeros((8, 1), f32)
    for k in range(2):
        steps = jnp.where(r == 2 * c + k, mine[4 + k : 5 + k, 0:1].astype(f32), steps)
        steps = jnp.where(r == 2 * (1 - c) + k, other[4 + k : 5 + k, 0:1].astype(f32), steps)
    angles = steps * freq[...]
    condition = jax.nn.silu(jnp.concatenate([jnp.cos(angles), jnp.sin(angles)], axis=1))
    condition = jnp.concatenate([condition, jnp.zeros_like(condition)], axis=0).astype(bf16)
    loads[0].wait()
    m4[...] = dot_nt(condition, adav[...])[:8] + ada_b[...].astype(f32).reshape(1, -1)
    moves = []
    for k in range(4):
        to = (y + k // 2) % 2 * 2 + (x + k) % 2
        row = jnp.broadcast_to(m4[pl.ds(to, 1), :], to_send.shape[1:])
        if k == 0:
            shares[t] = row
        else:
            to_send[k - 1] = row
            moves.append(remote(to_send.at[k - 1], shares.at[t], ssems, k - 1, ("x", "y", "xy")[k - 1]))
            moves[-1].start()

    leave(*tok_moves[1])

    group = jnp.where(c == y, mine, other)
    bucket = group[6:7, 0:1]
    skip = jnp.where(x == 0, group[0:2], group[2:4])
    for j in range(4):
        block = 2 * ((c + j // 2) % 2) + (x + j) % 2
        position = column(LB) + LB * block
        hit = jnp.where((position == skip[0:1, :]) | (position == skip[1:2, :]), 1.0, 0.0)
        kept_o[LB * j : LB * (j + 1), :] = 1.0 - jnp.max(hit, axis=1, keepdims=True)

    def chosen(masks):
        line = lax.broadcasted_iota(jnp.int32, masks.shape, 0)
        row = jnp.sum(jnp.where(line == bucket, masks[...].astype(f32), 0.0), axis=0, keepdims=True)
        return jnp.broadcast_to(row, (16, masks.shape[1])).astype(bf16)

    def spread(on, low, width):
        first = width * lax.broadcasted_iota(jnp.int32, (on.shape[1], low.shape[1]), 0)
        return dot_nn(on, jnp.where((low >= first) & (low < first + width), 1.0, 0.0).astype(bf16))[0:1, :]

    lane = lax.broadcasted_iota(jnp.int32, (1, WC), 1)
    share = sum(jnp.where(lane >= DC * k, 1, 0) for k in range(1, 4))
    hmask_o[...] = spread(chosen(head_masks), lane + DC * (share + c), HD)
    channels = chosen(channel_masks)
    lane = lax.broadcasted_iota(jnp.int32, (1, FB), 1)
    share = sum(jnp.where(lane >= FZ * k, 1, 0) for k in range(1, 4))
    for f in range(NF):
        low = lane + (4 * DZ - FZ) * share + FF // 8 * c + FZ * f
        chan_o[f] = spread(channels, low, FF // channels.shape[1])

    def half(v, k, width):
        v = v[:, 2 * width * k : 2 * width * (k + 1)]
        return jnp.where(c == 0, v[:, :width], v[:, width:])

    def line(ref):
        return ref[...].astype(f32).reshape(1, -1)

    def parity(v, odd):
        return [half(v, k, DC)[:, HD * odd : HD * (odd + 1)] for k in range(4)]

    bias = []
    for odd in range(2):
        bias += parity(line(q_bias), odd) + [jnp.zeros((1, DZ), f32)] + parity(line(v_bias), odd)
    bias = jnp.concatenate(bias, axis=1)
    b1v = [half(line(b1), k, FF // 8) for k in range(4)]
    for f in range(NF):
        b1_o[f] = jnp.concatenate([v[:, FZ * f : FZ * (f + 1)] for v in b1v], axis=1)
    loads[2].wait()
    for core in range(2):

        @pl.when(c == core)
        def _():
            for f in range(NF):
                for k in range(4):
                    start = 4 * DZ * k + FF // 8 * core + FZ * f
                    w1c[f, :, FZ * k : FZ * (k + 1)] = w1v[:, start : start + FZ]

    stores = [
        pltpu.make_async_copy(a, b, lsems.at[k]) for k, (a, b) in enumerate(((wqc, wq_o), (w1c, w1_o)))
    ]
    for store in stores:
        store.start()
    for copy in moves:
        copy.wait()
    share_rows = [shares[k][0:1, :] for k in range(4)]
    n, m = D // 2, 3 * D // 2
    mod = [share_rows[0][:, :D], jnp.concatenate([share_rows[0][:, D:], share_rows[1][:, :n]], axis=1),
           share_rows[1][:, n:], share_rows[2][:, :D],
           jnp.concatenate([share_rows[2][:, D:], share_rows[3][:, :n]], axis=1), share_rows[3][:, n:]]
    own_step = 0.5 * jnp.sum(jnp.where(r == t, steps, 0.0), axis=0, keepdims=True)
    mod += [jnp.broadcast_to(own_step, (1, D)), jnp.zeros((1, D), f32)]
    mod_o[...] = jnp.concatenate(mod, axis=0)
    n = LB // pieces

    def make(side, k):
        parts = [slice(LH * side + LB * j + n * k, LH * side + LB * j + n * (k + 1)) for j in range(2)]
        normed, _ = normalize(jnp.concatenate([tk[part, :] for part in parts], axis=0).astype(f32))
        shifted = (normed * (1.0 + mod[1]) + mod[0]).astype(bf16)
        made = (dot_nn(shifted, wqc[...]) + bias).astype(bf16)
        for j, part in enumerate(parts):
            shv[part, :] = shifted[n * j : n * (j + 1)]
            qkvv[part, :] = made[n * j : n * (j + 1)]

    kept_rows = []

    def keep_half(side):
        part = pl.ds(LH * side, LH)
        for k, (a, b) in enumerate(((shv, shifted_o), (qkvv, qkv_o), (tk, tok_o))):
            copy = pltpu.make_async_copy(a.at[part], b.at[part], ssems.at[side, 3 + k])
            copy.start()
            kept_rows.append(copy)

    pass_on(*tok_moves[0])
    make(0, 0)
    pass_on(*tok_moves[1])
    for side, k in ((1, 0), (0, 1), (1, 1)):
        if side == 1:
            for copy in tok_moves[k][3]:
                copy.wait_recv()
        make(side, k)
        if k == 1:
            keep_half(side)
    for one in tok_moves:
        settle(*one)
    for copy in stores + kept_rows:
        copy.wait()


def attn_kernel(step, cotangent, qkv, hmask, wp, bias, tok, mod, cot_o, mixed_o, shifted2_o, attn_o,
                ck, qkvv, qh, kh, vh, mx, mo, wpv, tkv, sh2v, attnv, csems, tsems, osems, lsems, ssems, ready):
    c = place()[1]
    loads = [
        pltpu.make_async_copy(wp.at[:, c], wpv.at[0], lsems.at[0]),
        pltpu.make_async_copy(wp.at[:, 1 - c], wpv.at[1], lsems.at[1]),
        pltpu.make_async_copy(tok, tkv, lsems.at[2]),
        pltpu.make_async_copy(qkv, qkvv, lsems.at[4]),
    ]
    for load in loads[::-1]:
        load.start()
    cot_moves = arrivals(cotangent, ck, tsems, osems, lsems.at[pl.ds(5, 1)])[0]
    scale = LOG2E / math.sqrt(HD)
    loads.pop().wait()
    for h in range(HC):
        for k, ref in enumerate((qh, kh, vh)):
            start = WQ * (h % 2) + DZ * k + HD * (h // 2)
            ref[h, :, :HD] = qkvv[:, start : start + HD]
        vh[h, :, HD:] = jnp.ones((L, LANES - HD), bf16)
    ready()
    leave(*cot_moves)

    def crossing(i):
        src = mx.at[pl.ds(pl.multiple_of(i * step, step), step)]
        dst = mo.at[pl.ds(pl.multiple_of((i * step + LH) % L, step), step)]
        return remote(src, dst, csems, i, "c")

    def body(i, carry):
        part = pl.ds(pl.multiple_of(i * step, step), step)
        outs = []
        for h in range(HC):
            s = dot_nt(qh[h, part, :], kh[h])
            top = jnp.max(s, axis=1, keepdims=True)
            p = jnp.exp2((s - top) * scale)
            o = dot_nn(p.astype(bf16), vh[h])
            outs.append(o[:, :HD] * (1.0 / o[:, HD : HD + 1]))
        mx[part, :] = (jnp.concatenate(outs, axis=1) * hmask[...]).astype(bf16)
        crossing(i).start()
        return carry

    lax.fori_loop(0, L // step, body, 0)
    keep = pltpu.make_async_copy(mx, mixed_o, lsems.at[3])
    keep.start()
    pass_on(*cot_moves)
    for load in loads:
        load.wait()
    for i in range(L // step):
        crossing(i).wait()
    w_mine, w_other = wpv[0].reshape(WC, D), wpv[1].reshape(WC, D)
    bias_line = bias[...].astype(f32).reshape(1, D)
    stores = []
    for j in range(4):
        part = slice(LB * j, LB * (j + 1))
        attn = dot_nn(mx[part, :], w_mine) + dot_nn(mo[part, :], w_other) + bias_line
        if j < 2:
            attnv[part, :] = attn
        normed, _ = normalize(tkv[part, :].astype(f32) + mod[2:3, :] * attn)
        sh2v[part, :] = (normed * (1.0 + mod[4:5, :]) + mod[3:4, :]).astype(bf16)
        made = [(sh2v, shifted2_o)] + [(attnv, attn_o)] * (j < 2)
        for k, (a, b) in enumerate(made):
            stores.append(pltpu.make_async_copy(a.at[pl.ds(LB * j, LB)], b.at[pl.ds(LB * j, LB)], ssems.at[k, j]))
            stores[-1].start()
    for copy in cot_moves[3]:
        copy.wait_recv()
    keep_cot = pltpu.make_async_copy(ck, cot_o, lsems.at[6])
    keep_cot.start()
    settle(*cot_moves)
    for copy in stores + [keep, keep_cot]:
        copy.wait()


def mlp_kernel(sh2, g, kept, mod, w1, b1, chan, w2,
               on_a0, q_a0, on_b0, q_b0, keep_a0, keep_b0, keep_c0, send_c0,
               on_a1, q_a1, on_b1, q_b1, keep_a1, keep_b1, keep_c1, send_c1,
               k2a, s2a, k2b, s2b, c2, branch_o, ds2_o, branch_r, ds2_r, sum1_o, sum2_o,
               sh2v, dbs, w1v, w2v, hid, dpre, slope, br, ds, far, near, tt_, ka, sa, kb, sb, cz, cr, ra, rb, ona, onb,
               fsems, csems, lsems, wsems, osems, ready):
    z, c, y, x = place()
    out0 = (on_a0, q_a0, on_b0, q_b0, keep_a0, keep_b0, keep_c0, send_c0)
    out1 = (on_a1, q_a1, on_b1, q_b1, keep_a1, keep_b1, keep_c1, send_c1)
    outs = (out0, out1)

    def weights(f):
        return [
            pltpu.make_async_copy(w1.at[f], w1v.at[f % 2], wsems.at[0, f % 2]),
            pltpu.make_async_copy(w2.at[:, c, f], w2v.at[f % 2], wsems.at[1, f % 2]),
        ]

    def first(f):
        k, out = f % 2, outs[f]
        return [
            remote(sa.at[k, 1], ra.at[k], fsems, 10 * k, "x"), remote(sb.at[k, 1], rb.at[k], fsems, 10 * k + 1, "y"),
            remote(sa.at[k, 0], out[1], fsems, 10 * k + 2, "x"), remote(sb.at[k, 0], out[3], fsems, 10 * k + 3, "y"),
        ] + [
            remote(cz.at[k, j, :, :, pl.ds(GC * half, GC)], cr.at[k, j - 1, :, :, pl.ds(GC * half, GC)], fsems,
                   10 * k + 3 + 3 * half + j, f"z{j}")
            for half in range(2) for j in (3, 2, 1)
        ]

    def stored(f):
        k = f % 2
        if f == NF - 1:
            pairs = ((ka.at[k], k2a), (sa.at[k], s2a), (kb.at[k], k2b), (sb.at[k], s2b), (cz.at[k], c2))
        else:
            pairs = ((ka.at[k, 0], outs[f][4]), (kb.at[k, 0], outs[f][5]))
        return [pltpu.make_async_copy(src, dst, osems.at[k, j]) for j, (src, dst) in enumerate(pairs)]

    def onward(f):
        k = f % 2
        for copy in first(f):
            copy.wait()
        for kv, rv, on in ((ka, ra, ona), (kb, rb, onb)):
            on[k] = total_of(kv[k, 1], rv[k]).astype(bf16)
        cz[k, 0] = total_of(cz[k, 0], cr[k, 0], cr[k, 1], cr[k, 2]).astype(bf16)
        pairs = (
            (ona.at[k], outs[f][0]), (onb.at[k], outs[f][2]), (cz.at[k, 0, 0], outs[f][6]), (cz.at[k, 0, 1], outs[f][7])
        )
        copies = [pltpu.make_async_copy(src, dst, osems.at[k, 5 + j]) for j, (src, dst) in enumerate(pairs)]
        for copy in copies:
            copy.start()
        return copies

    loads = [pltpu.make_async_copy(src, dst, lsems.at[k]) for k, (src, dst) in enumerate(((g, dbs), (sh2, sh2v)))]
    for copy in loads + weights(0):
        copy.start()
    loads[0].wait()
    sum2 = jnp.zeros((1, D), f32)
    for j in range(4):
        part = slice(LB * j, LB * (j + 1))
        db = (dbs[part, :].astype(f32) * mod[5:6, :] * kept[part, :]).astype(bf16)
        dbs[part, :] = db
        sum2 += jnp.sum(db.astype(f32), axis=0, keepdims=True)
    sum2_o[...] = sum2
    loads[1].wait()
    crossing = [remote(far.at[j], dst, csems, j, "c") for j, dst in enumerate((branch_r, ds2_r))]
    waiting = []
    for f in range(NF):
        for copy in weights(f):
            copy.wait()
        if f + 1 < NF:
            for copy in weights(f + 1):
                copy.start()
        w1f, w2f = w1v[f % 2], w2v[f % 2].reshape(FB, D)
        on = chan[f]
        k = f % 2
        for side in (1, 0):
            part = slice(LH * side, LH * (side + 1))
            v = dot_nn(sh2v[part, :], w1f) + b1[f]
            v2 = v * v
            th = jnp.tanh(GELU_K * v * (1.0 + GELU_C * v2))
            half = 0.5 * (1.0 + th)
            hid[part, :] = (v * half * on).astype(bf16)
            slope[part, :] = (
                (half + (0.5 * GELU_K) * v * (1.0 - th * th) * (1.0 + (3.0 * GELU_C) * v2)) * on
            ).astype(bf16)
        p = dot_tn(hid[...], dbs[...]).astype(bf16)
        for t in range(4):
            tt_[t, :FB, :] = p[:, TD * t : TD * (t + 1)]
        for rz in range(4):
            zz = flip(z, rz)
            for ry in range(2):
                for rx in range(2):
                    tt = (ry + y) % 2 * 2 + (rx + x) % 2
                    o = (kb, sb)[ry]
                    block = tt_[tt, pl.ds(pl.multiple_of(zz * FZ, 16), FZ), :]
                    o[k, rx, rz, :FZ, :] = block[:, :LANES]
                    o[k, rx, rz, FZ:, :] = block[: GB - FZ, LANES : 2 * LANES]
                    q = FZ // 4
                    cz[k, rz, rx, ry, GC : GC + 2 * FZ - GB, :] = block[GB - FZ :, LANES : 2 * LANES]
                    cz[k, rz, rx, ry, GC + 2 * FZ - GB :, :] = jnp.concatenate(
                        [block[q * j : q * (j + 1), 2 * LANES :] for j in range(4)], axis=1
                    )
        if f == 0:
            ready()
        if f < NF - 1:
            for copy in first(f)[1:4:2] + first(f)[7:]:
                copy.start()
        sum1 = jnp.zeros((1, FB), f32)
        for side in (1, 0):
            part = slice(LH * side, LH * (side + 1))
            d_pre = (dot_nt(dbs[part, :], w2f) * slope[part, :].astype(f32)).astype(bf16)
            dpre[part, :] = d_pre
            sum1 += jnp.sum(d_pre.astype(f32), axis=0, keepdims=True)
        sum1_o[f] = sum1
        p = dot_tn(sh2v[...], dpre[...]).astype(bf16)
        for t in range(4):
            tt_[t, :, :FZ] = p[:, FZ * t : FZ * (t + 1)]
        for rz in range(4):
            zz = flip(z, rz)
            for ry in range(2):
                for rx in range(2):
                    tt = (ry + y) % 2 * 2 + (rx + x) % 2
                    o = (ka, sa)[rx]
                    tails = []
                    for rc in range(2):
                        block = tt_[tt, pl.ds(pl.multiple_of(zz * DZ + (rc + c) % 2 * DC, 16), DC), :FZ]
                        o[k, ry, rz, DC * rc : DC * (rc + 1), :] = block[:, :LANES]
                        tails.append(block[:, LANES:])
                    tail = jnp.concatenate(tails, axis=1)
                    o[k, ry, rz, 2 * DC :, :] = tail[: GA - 2 * DC]
                    cz[k, rz, rx, ry, :GC, :] = tail[GA - 2 * DC :]
        if f < NF - 1:
            for copy in first(f)[0:4:2] + first(f)[4:7]:
                copy.start()
        for copy in stored(f):
            copy.start()
        for side in (1, 0):
            part = slice(LH * side, LH * (side + 1))
            branch, ds2 = dot_nn(hid[part, :], w2f), dot_nt(dpre[part, :], w1f)
            if f > 0:
                branch, ds2 = branch + br[part, :], ds2 + ds[part, :]
            if f < NF - 1:
                br[part, :] = branch
                ds[part, :] = ds2
            elif side == 1:
                far[0] = branch.astype(bf16)
                far[1] = ds2.astype(bf16)
                for copy in crossing:
                    copy.start()
            else:
                near[0] = branch.astype(bf16)
                near[1] = ds2.astype(bf16)
                waiting += upto([near.at[0], near.at[1]], [branch_o, ds2_o], lsems)
                for copy in waiting[-2:]:
                    copy.start()
        waiting += stored(f)
        if f > 0:
            waiting += onward(f - 1)
        if f == NF - 2:
            for copy in waiting:
                copy.wait()
            waiting = []
    for copy in waiting + crossing:
        copy.wait()


def middle_kernel(ds, ds_r, br, br_r, attn, tok, g, kept, mod, bias2, mixed, wp,
                  d_resid_out, out_out, dh_out, pka_out, psa_out, pkb_out, psb_out, sums_o, sum_o,
                  d_resid_o, out_o, dh_o, pka, psa, pkb, psb, dsv, attnv, tokv, mixv, wpv, da, t1, csems, lsems, bsems, ssems, ready):
    z, c, y, x = place()
    n = LH // 4
    pairs = ((tok, tokv.at[0]), (attn, attnv), (ds, dsv.at[0]), (ds_r, dsv.at[1]), (br, dsv.at[2]), (br_r, dsv.at[3]),
             (g, tokv.at[1]))
    blocks = [
        [
            pltpu.make_async_copy(src.at[pl.ds(n * k, n)], dst.at[pl.ds(n * k, n)], bsems.at[k, j])
            for j, (src, dst) in enumerate(pairs)
        ]
        for k in range(4)
    ]
    loads = [pltpu.make_async_copy(src, dst, lsems.at[k]) for k, (src, dst) in enumerate(((wp.at[:, c], wpv), (mixed, mixv)))]
    for load in sum(blocks, []) + loads:
        load.start()
    ready()
    crossing = [remote(da.at[pl.ds(n * k, n)], da.at[pl.ds(LH + n * k, n)], csems, k, "c") for k in range(4)]
    sums = jnp.zeros((4, D), f32)
    bias_line = bias2[...].astype(f32).reshape(1, D)
    for k in range(4):
        for load in blocks[k]:
            load.wait()
        part = slice(n * k, n * (k + 1))
        gf, at = tokv[1, part, :].astype(f32), attnv[part, :]
        resid = tokv[0, part, :].astype(f32) + mod[2:3, :] * at
        normed2, inverse2 = normalize(resid)
        ds2 = dsv[0, part, :].astype(f32) + dsv[1, part, :].astype(f32)
        kb = kept[part, :] * (dsv[2, part, :].astype(f32) + dsv[3, part, :].astype(f32) + bias_line)
        out_o[part, :] = (resid + mod[5:6, :] * kb).astype(bf16)
        d_resid = gf + normalize_back(ds2 * (1.0 + mod[4:5, :]), normed2, inverse2)
        d_resid_o[part, :] = d_resid
        da[part, :] = (mod[2:3, :] * d_resid).astype(bf16)
        crossing[k].start()
        sums += jnp.concatenate(
            [jnp.sum(p, axis=0, keepdims=True) for p in (at * d_resid, ds2, ds2 * normed2, kb * gf)], axis=0
        )
    sums_o[...] = jnp.concatenate([sums, jnp.zeros((4, D), f32)], axis=0)
    for load in loads:
        load.wait()
    for copy in crossing:
        copy.wait()
    wv = wpv[...].reshape(WC, D)
    dh_o[...] = dot_nt(da[...], wv).astype(bf16)
    stores = upto(
        [d_resid_o, out_o, dh_o, pka, psa, pkb, psb],
        [d_resid_out, out_out, dh_out, pka_out, psa_out, pkb_out, psb_out], ssems,
    )
    for copy in stores[:3]:
        copy.start()
    sum_o[...] = dot_nn(jnp.ones((16, L), bf16), da[...])[:8]
    grad = dot_tn(mixv[...], da[...]).astype(bf16)
    for t in range(4):
        t1[t] = grad[:, TD * t : TD * (t + 1)]
    for rz in range(4):
        zz = flip(z, rz)
        for ry in range(2):
            for rx in range(2):
                tt = (ry + y) % 2 * 2 + (rx + x) % 2
                a, b = (pka, psa)[rx], (pkb, psb)[ry]
                block = t1[tt, pl.ds(pl.multiple_of(zz * DC, 16), DC), :]
                a[ry, rz, :DC, :] = block[:, :LANES]
                a[ry, rz, DC:, :] = block[: PA - DC, LANES : 2 * LANES]
                b[rx, rz, : 2 * DC - PA, :] = block[PA - DC :, LANES : 2 * LANES]
                q = DC // 3
                tails = [block[q * k : q * (k + 1), 2 * LANES :] for k in range(3)]
                tails.append(jnp.zeros((q, 32), bf16))
                b[rx, rz, 2 * DC - PA :, :] = jnp.concatenate(tails, axis=1)
    for copy in stores[3:]:
        copy.start()
    for copy in stores:
        copy.wait()


def qkv_slots(grad, extra, t1, ka, sa, kb, sb, copies):
    z, _, y, x = place()
    for t in range(4):
        for zz in range(4):
            t1[t, zz] = grad[TQ * t : TQ * (t + 1), DZ * zz : DZ * (zz + 1)]
    q = TQ // 3
    for ry, rx, ready_now in ((1, 1, copies[:2]), (0, 1, copies[2:3]), (1, 0, copies[3:]), (0, 0, ())):
        tt = (ry + y) % 2 * 2 + (rx + x) % 2
        for rz in range(4):
            zz = flip(z, rz)
            block = t1[tt, zz]
            tails = [block[q * k : q * (k + 1), 2 * LANES :] for k in range(3)] + [jnp.zeros((q, 32), f32)]
            more = jnp.zeros((8, LANES), f32) if extra is None else extra[zz, tt]
            slot = [block[:, :LANES], block[:, LANES : 2 * LANES], jnp.concatenate(tails, axis=1), more]
            slot = jnp.concatenate(slot, axis=0).astype(bf16)
            (ka, sa)[rx][ry, rz] = slot[:QA]
            (kb, sb)[ry][rx, rz] = slot[QA:]
        for copy in ready_now:
            copy.start()


def column_sums(dqkv):
    return dot_nn(jnp.ones((16, L), bf16), dqkv)[:8]


def attn_back_kernel(step, qkv, dh, shifted, hmask, out, on_a, q_a, on_b, q_b, keep_a, keep_b, sums_o,
                     qkvv, dhv, shv, outv, qh, kh, vh, doh, dk, dv, t1, ka, sa, kb, sb, ra, rb, ona, onb,
                     fsems, lsems, ready, tick):
    loads = [
        pltpu.make_async_copy(a, b, lsems.at[k])
        for k, (a, b) in enumerate(((qkv, qkvv), (dh, dhv), (shifted, shv)))
    ]
    for load in loads:
        load.start()
    ready()
    for load in loads:
        load.wait()
    scale = LOG2E / math.sqrt(HD)
    first = [
        remote(sa.at[1], ra, fsems, 0, "x"), remote(sb.at[1], rb, fsems, 1, "y"),
        remote(sa.at[0], q_a, fsems, 2, "x"), remote(sb.at[0], q_b, fsems, 3, "y"),
    ]
    stores = [pltpu.make_async_copy(a, b, lsems.at[3 + k]) for k, (a, b) in enumerate(((ka.at[0], keep_a), (kb.at[0], keep_b)))]
    for odd in range(2):
        base = WQ * odd
        for j in range(HC // 2):
            for k, ref in enumerate((qh, kh, vh)):
                start = base + DZ * k + HD * j
                ref[j] = qkvv[:, start : start + HD]
            cut = slice(HD * (2 * j + odd), HD * (2 * j + odd + 1))
            doh[j] = (dhv[:, cut].astype(f32) * hmask[:, cut]).astype(bf16)
        dk[...] = jnp.zeros_like(dk)
        dv[...] = jnp.zeros_like(dv)

        def body(i, carry):
            part = pl.ds(pl.multiple_of(i * step, step), step)
            outs = []
            for j in range(HC // 2):
                q, do = qh[j, part, :], doh[j, part, :]
                s = dot_nt(kh[j], q)
                top = jnp.max(s, axis=0, keepdims=True)
                p = jnp.exp2((s - top) * scale)
                p = p * (1.0 / jnp.sum(p, axis=0, keepdims=True))
                dp = dot_nt(vh[j], do)
                row_dot = jnp.sum(p * dp, axis=0, keepdims=True)
                ds = (p * (dp - row_dot)).astype(bf16)
                dv[j] += dot_nn(p.astype(bf16), do)
                dk[j] += dot_nn(ds, q)
                outs.append(dot_tn(ds, kh[j]))
            outv[part, base : base + DZ] = (jnp.concatenate(outs, axis=1) * (1.0 / math.sqrt(HD))).astype(bf16)
            return carry

        half = L // step // 2
        lax.fori_loop(0, half, body, 0)
        tick(1 + 2 * odd)
        lax.fori_loop(half, 2 * half, body, 0)
        for j in range(HC // 2):
            start = base + DZ + HD * j
            outv[:, start : start + HD] = (dk[j] * (1.0 / math.sqrt(HD))).astype(bf16)
            outv[:, start + DZ : start + DZ + HD] = dv[j].astype(bf16)
        if odd == 0:
            sums_o[...] = column_sums(outv[:, :WQ])
            qkv_slots(dot_tn(outv[:, :WQ], shv[...]), None, t1, ka, sa, kb, sb, first)
            for copy in stores:
                copy.start()
            tick(2)
    keep = pltpu.make_async_copy(outv, out, lsems.at[5])
    keep.start()
    for copy in first:
        copy.wait()
    for kv, rv, on in ((ka, ra, ona), (kb, rb, onb)):
        on[...] = (kv[1].astype(f32) + rv[...].astype(f32)).astype(bf16)
    onward = [pltpu.make_async_copy(a, b, lsems.at[6 + k]) for k, (a, b) in enumerate(((ona, on_a), (onb, on_b)))]
    for copy in onward:
        copy.start()
    for copy in stores + onward + [keep]:
        copy.wait()


def end_kernel(dqkv, shifted, even_sums, sum1, sum2, sum_attn, wq, d_resid, tok, mod, sums_mid, f0, c0, f1, c1, f2, c2, sent_p, kept_p, freq,
               on_a, q_a, on_b, q_b, keep_a, keep_b,
               grad, gq_o, gp_out, g1_out, g2_out, ada_out, ada_bias_o, line_o,
               dqv, shv, extra, t1, ka, sa, kb, sb, ra, rb, ona, onb, r2a, r2b, zs, zk, zr,
               eqa, era, eka, eqb, erb, ekb, ezs, ezk, ezr, qt, wqv, dres, tokv, fv, far, got, gb,
               item, item_r, out_shares, square, every, row_out, row_in, mine, theirs, mine_q, theirs_q, pk, pr, gp_o, g1_o, g2_o, ada_o,
               qsems, esems, csems, tsems, ssems, psems, lsems, xsems, ready):
    z, c, y, x = place()
    t, b = 2 * y + x, 2 * z + c
    second_e = [remote(on_a, era, esems, 0, "y"), remote(on_b, erb, esems, 1, "x")]
    third_p = [remote(sent_p.at[k], pr.at[k], psems, k, f"z{k + 1}") for k in (2, 1, 0)]
    pairs = ((dqkv, dqv), (shifted, shv), (wq, wqv), (d_resid, dres), (tok.at[pl.ds(0, LH)], tokv),
             (keep_a, eka), (q_a, eqa), (keep_b, ekb), (q_b, eqb), (kept_p, pk))
    for f, (two, one) in enumerate(((f0, c0), (f1, c1), (f2, c2))):
        pairs += ((two.at[pl.ds(0, GA)], fv.at[f, pl.ds(0, GA)]), (one.at[pl.ds(0, GC)], fv.at[f, pl.ds(GA, GC)]),
                  (two.at[pl.ds(GA, GB)], fv.at[f, pl.ds(G1R, GB)]), (one.at[pl.ds(GC, GC)], fv.at[f, pl.ds(G1R + GB, GC)]))
    loads = [pltpu.make_async_copy(src, dst, lsems.at[k]) for k, (src, dst) in enumerate(pairs)]
    for copy in loads:
        copy.start()
    loads[0].wait()
    loads[1].wait()
    ready()
    for copy in second_e + third_p:
        copy.start()

    odd = dqv[:, WQ:]
    grad_odd = dot_tn(odd, shv[...])
    odd_sums = column_sums(odd)
    for zs_ in range(4):
        for ts in range(4):
            start, n = FF // 32 * ts, FF // 32
            pieces = []
            for f in range(NF):
                low, high = max(start, FZ * f), min(start + n, FZ * (f + 1))
                if low < high:
                    pieces.append(sum1[f][:, FZ * zs_ + low - FZ * f : FZ * zs_ + high - FZ * f])
            n = D // 32
            for total in (sum2[...], sum_attn[0:1, :]):
                at = DZ * zs_ + n * ts
                pieces.append(jnp.where(c == 0, total[:, at : at + n], total[:, at + DC : at + DC + n]))
            total = (even_sums, odd_sums)[ts // 2][0:1, :]
            at = HD * zs_ + n * (ts % 2)
            pieces += [total[:, at : at + n], total[:, 2 * DZ + at : 2 * DZ + at + n]]
            flat = jnp.concatenate(pieces + [jnp.zeros((1, 3 * LANES - DZ), f32)], axis=1)
            lines = [flat[:, LANES * k : LANES * (k + 1)] for k in range(3)] + [jnp.zeros((5, LANES), f32)]
            extra[zs_, ts] = jnp.concatenate(lines, axis=0)
    first_q = [
        remote(sa.at[1], ra.at[1], qsems, 0, "x"), remote(sb.at[1], rb.at[1], qsems, 1, "y"),
        remote(sa.at[0], ra.at[0], qsems, 2, "x"), remote(sb.at[0], rb.at[0], qsems, 3, "y"),
    ]
    qkv_slots(grad_odd, extra, t1, ka, sa, kb, sb, first_q)

    loads[2].wait()
    crossing = [remote(far.at[k], got.at[k], csems, k, "c") for k in range(2)]
    d_far = dot_nt(dqv[LH:, :], wqv[...])
    for k in range(2):
        far[k] = d_far[LB * k : LB * (k + 1)].astype(bf16)
        crossing[k].start()

    for copy in second_e:
        copy.wait()
    for k in (5, 6, 7, 8):
        loads[k].wait()
    layer_sums([(eka, eqa, era), (ekb, eqb, erb)], ezs, ezk)
    third_e = [remote(ezs.at[k], ezr.at[k], esems, 2 + k, f"z{k + 1}") for k in (2, 1, 0)]
    for copy in third_e:
        copy.start()
    d_near = dot_nt(dqv[:LH, :], wqv[...])
    loads[3].wait()
    loads[4].wait()
    token_sums = jnp.zeros((2, D), f32)
    for k in range(2):
        part = slice(LB * k, LB * (k + 1))
        crossing[k].wait()
        total = d_near[part] + got[k].astype(f32)
        normed, inverse = normalize(tokv[part, :].astype(f32))
        back = dres[part, :] + normalize_back(total * (1.0 + mod[1:2, :]), normed, inverse)
        gb[k] = back.astype(bf16)
        token_sums += jnp.concatenate(
            [jnp.sum(v, axis=0, keepdims=True) for v in (total, total * normed)], axis=0
        )
    item[...] = jnp.concatenate([token_sums, sums_mid[0:4, :], mod[6:8, :]], axis=0)
    over = remote(item, item_r, csems, 2, "c")
    over.start()

    for copy in first_q:
        copy.wait()
    for kv, rv, on in ((ka, ra, ona), (kb, rb, onb)):
        on[...] = (kv[1].astype(f32) + rv[1].astype(f32)).astype(bf16)
    second_q = [remote(ona, r2a, qsems, 4, "y"), remote(onb, r2b, qsems, 5, "x")]
    for copy in second_q:
        copy.start()
    over.wait()
    v = item[...] + item_r[...]
    n = D // 2
    stamp = v[6:7, :LANES]
    pieces = ([v[0:1], v[1:2, :n]], [v[1:2, n:], v[2:3]], [v[3:4], v[4:5, :n]], [v[4:5, n:], v[5:6]])
    for j in range(4):
        out_shares[j] = jnp.concatenate(pieces[j] + [stamp], axis=1)
    square[t] = out_shares[t]
    meeting = [
        remote(out_shares.at[(y + j // 2) % 2 * 2 + (x + j) % 2], square.at[t], ssems, j - 1, ("x", "y", "xy")[j - 1])
        for j in (1, 2, 3)
    ]
    for copy in meeting:
        copy.start()

    def first_columns(pairs, own):
        for core in range(2):

            @pl.when(c == core)
            def _():
                for f, pair in enumerate(pairs):
                    start = FF // 8 * (core if own else 1 - core) + FZ * f
                    g1_o[:, start : start + FZ] = jnp.concatenate(pair, axis=1)

    for load in loads[9:]:
        load.wait()
    for f in range(NF):
        mine[G1R * f : G1R * (f + 1), :] = fv[f, :G1R, :].astype(bf16)
    swap = remote(mine, theirs, csems, 3, "c")
    swap.start()
    first_columns([[fv[f, :DC, :], fv[f, 2 * DC : 3 * DC, : FZ - LANES]] for f in range(NF)], True)
    for copy in second_q:
        copy.wait()
    layer_sums([(ka.at[0], ra.at[0], r2a), (kb.at[0], rb.at[0], r2b)], zs, zk)
    third_q = [remote(zs.at[k], zr.at[k], qsems, 6 + k, f"z{k + 1}") for k in (2, 1, 0)]
    for copy in third_q:
        copy.start()
    home = homeward(gb.at[0], gb.at[1], grad, tsems, lsems.at[len(pairs)])
    home_start(*home)
    for copy in meeting:
        copy.wait()
    spread_z = [remote(square, every.at[z], ssems, 2 + k, f"z{k}") for k in (1, 2, 3)]
    every[z] = square[...]
    for copy in spread_z:
        copy.start()
    for f in range(NF):
        part = fv[f, G1R:, :]
        tail = part[2 * FZ :]
        tail = jnp.concatenate([tail[:, 32 * k : 32 * (k + 1)] for k in range(4)], axis=0)
        g2_o[FZ * f : FZ * (f + 1), :] = jnp.concatenate([part[:FZ], part[FZ : 2 * FZ], tail], axis=1)
    for copy in third_p:
        copy.wait()
    part = pk[...] + pr[0].astype(f32) + pr[1].astype(f32) + pr[2].astype(f32)
    tail = part[2 * DC :]
    tail = jnp.concatenate([tail[:, 32 * k : 32 * (k + 1)] for k in range(3)], axis=0)
    gp_o[...] = jnp.concatenate([part[:DC], part[DC : 2 * DC], tail], axis=1)
    swap.wait()
    first_columns(
        [
            [theirs[G1R * f + DC : G1R * f + 2 * DC, :].astype(f32),
             theirs[G1R * f + 2 * DC : G1R * (f + 1), FZ - LANES :].astype(f32)]
            for f in range(NF)
        ],
        False,
    )

    stores = upto([gp_o, g1_o, g2_o, ada_o], [gp_out, g1_out, g2_out, ada_out], xsems)
    for copy in stores[:3]:
        copy.start()

    for copy in spread_z:
        copy.wait()
    columns = jnp.concatenate([every[i, j] for i in range(4) for j in range(4)], axis=0)
    width = 3 * D // 2
    angles = columns[:, width : width + 1] * freq[b % 4]
    cond = jax.nn.silu(jnp.where(b < 4, jnp.cos(angles), jnp.sin(angles))).astype(bf16).astype(f32)
    columns = columns[:, :width]
    ada_o[...] = lax.dot_general(
        cond, columns, (((0,), (0,)), ((), ())), precision=lax.Precision.HIGHEST, preferred_element_type=f32
    )
    stores[3].start()
    row = jnp.sum(columns, axis=0, keepdims=True)
    row_out[0] = row
    row_in[t] = row
    rows_ = [remote(row_out.at[0], row_in.at[t], ssems, 6 + j, name) for j, name in enumerate(("x", "y", "xy"))]
    for copy in rows_:
        copy.start()

    for odd_, (copies, kept, more) in enumerate(((third_e, ezk, ezr), (third_q, zk, zr))):
        for copy in copies:
            copy.wait()
        q = total_of(kept[...], more[0], more[1], more[2])
        tail = q[2 * TQ :]
        n = TQ // 3
        tail = jnp.concatenate([tail[n * 0 : n, 32 * k : 32 * (k + 1)] for k in range(3)], axis=0)
        qt[odd_] = jnp.transpose(jnp.concatenate([q[:TQ], q[TQ : 2 * TQ], tail], axis=1))
        mine_q[odd_] = qt[odd_, pl.ds(pl.multiple_of(DC * (1 - c), 16), DC), :].astype(bf16)
        swap = remote(mine_q.at[odd_], theirs_q.at[odd_], csems, 4 + odd_, "c")
        swap.start()
        if odd_ == 1:
            line_o[...] = q[QR - 8 :]
    own = [qt[odd_, pl.ds(pl.multiple_of(DC * c, 16), DC), :] for odd_ in range(2)]

    def qkv_columns(values, owned):
        for core in range(2):

            @pl.when(c == core)
            def _():
                for odd_ in range(2):
                    for j in range(3):
                        start = DZ * j + DC * (core if owned else 1 - core) + HD * odd_
                        gq_o[:, start : start + HD] = values[odd_][:, HD * j : HD * (j + 1)]

    qkv_columns(own, True)
    for odd_ in range(2):
        remote(mine_q.at[odd_], theirs_q.at[odd_], csems, 4 + odd_, "c").wait()
    qkv_columns([theirs_q[odd_].astype(f32) for odd_ in range(2)], False)
    for copy in rows_:
        copy.wait()
    row = row_in[z]
    ada_bias_o[...] = jnp.where(c == 0, row[:, : width // 2], row[:, width // 2 :])
    home_wait(*home)
    for copy in stores:
        copy.wait()


def final_kernel(out_rows, grad_rows, gq, gp, g1, g2, ada, ada_bias, line,
                 out, grad, gq_o, gp_o, g1_o, g2_o, ada_o, ada_bias_o, b_fc1, b_fc2, b_proj, b_q, b_v):
    out[...] = out_rows[...]
    grad[...] = grad_rows[...].astype(f32)
    gq_o[...] = gq[...]
    gp_o[...] = gp[...]
    g1_o[...] = g1[...]
    g2_o[...] = jnp.transpose(g2[...])
    ada_o[...] = ada[...]
    ada_bias_o[...] = ada_bias[...].reshape(-1)
    flat = jnp.concatenate([line[k : k + 1, :] for k in range(3)], axis=1)
    n1, n = FF // 32, D // 32
    b_fc1[...] = flat[:, :n1].reshape(-1)
    for k, ref in enumerate((b_fc2, b_proj, b_q, b_v)):
        ref[...] = flat[:, n1 + n * k : n1 + n * (k + 1)].reshape(-1)


def one_item_per_chip(
    tokens, cotangent, timesteps, bucket_ids, head_masks, channel_masks, skip_rows,
    w_qkv, q_bias, v_bias, w_proj, proj_bias, w_fc1, fc1_bias, w_fc2, fc2_bias, ada_weight, ada_bias,
):
    b, t = lax.axis_index("bucket"), lax.axis_index("tok")
    z, c, y, x = b // 2, b % 2, t // 2, t % 2

    def core_half(v, *dims):
        return lax.dynamic_index_in_dim(v.reshape(dims), c, 1, keepdims=False)

    vmem, smem = pl.BlockSpec(memory_space=pltpu.VMEM), pl.BlockSpec(memory_space=pltpu.SMEM)
    steps = -np.float32(math.log(10000.0)) * np.arange(D // 2, dtype=np.float32) / np.float32(D // 2)
    freq = jnp.asarray(np.exp(steps).reshape(1, D // 2))
    ada_cols = ada_weight.shape[1]
    front, _ = call(
        front_kernel, "front",
        (sds((L, D), bf16), sds((L, D), bf16), sds((L, 3 * WC), bf16), sds((D, 3 * WC), bf16), sds((NF, D, FB), bf16), sds((8, D), f32), sds((L, 1), f32), sds((1, WC), f32), sds((NF, 1, FB), f32),
         sds((NF, 1, FB), f32)),
        (tokens, timesteps, bucket_ids, skip_rows, ada_weight.T, ada_bias, head_masks, channel_masks,
         w_qkv, w_fc1, q_bias, v_bias, fc1_bias, freq),
        in_specs=[ANY, smem, smem, vmem, ANY, vmem, vmem, vmem, ANY, ANY, vmem, vmem, vmem, vmem],
        out_specs=[ANY] * 5 + [vmem] * 5,
        scratch=[vm(L, D), vm(D, 3 * D), vm(D, 3 * WC), vm(D, FF), vm(NF, D, FB), vm(ada_cols, D),
                 vm(8, LANES, dtype=jnp.int32), vm(8, LANES, dtype=jnp.int32), vm(8, ada_cols, dtype=f32), vm(3, 8, ada_cols, dtype=f32),
                 vm(4, 8, ada_cols, dtype=f32), vm(L, D), vm(L, 3 * WC), pltpu.SemaphoreType.DMA((2, 5)),
                 pltpu.SemaphoreType.DMA((2, 4)), pltpu.SemaphoreType.DMA((2, 6)), pltpu.SemaphoreType.DMA((8,))],
        peers=("c", "t0", "t1", "x", "y", "xy"), cid=10, flops=2 * L * D * 3 * WC, nbytes=50e6,
    )
    tok, shifted, qkv, wq, w1, mod, kept, hmask, chan, b1 = front
    w2 = w_fc2.reshape(4, 2, NF, FZ, D)
    wp = w_proj.reshape(4, 2, DC, D)
    (g_all, mixed, shifted2, attn), _ = call(
        functools.partial(attn_kernel, 512), "attn",
        (sds((L, D), bf16), sds((L, WC), bf16), sds((L, D), bf16), sds((LH, D), f32)),
        (cotangent, qkv, hmask, wp, proj_bias, tok, mod),
        in_specs=[ANY, ANY, vmem, ANY, vmem, ANY, vmem],
        out_specs=[ANY] * 4,
        scratch=[vm(L, D), vm(L, 3 * WC)] + [vm(HC, L, HD)] * 2 + [vm(HC, L, LANES)] + [vm(L, WC), vm(L, WC), vm(2, 4, DC, D), vm(L, D), vm(L, D),
                 vm(LH, D, dtype=f32),
                 pltpu.SemaphoreType.DMA((2, 4)), pltpu.SemaphoreType.DMA((2, 2)), pltpu.SemaphoreType.DMA((2, 2)),
                 pltpu.SemaphoreType.DMA((7,)), dma(2, 4)],
        peers=("c", "t0", "t1"), cid=11, flops=16e9, nbytes=5e6,
    )

    slot1, slot2, slot3 = sds((2, 4, GA, LANES)), sds((2, 4, GB, LANES)), sds((4, 2, 2, 2 * GC, LANES))
    part1, part2, part3 = sds(slot1.shape[1:]), sds(slot2.shape[1:]), sds(slot3.shape[2:])
    one = [part1, part1, part2, part2, part1, part2, part3, part3]
    rows_half = sds((LH, D), bf16)
    own, _ = call(
        mlp_kernel, "mlp",
        one + one + [slot1, slot1, slot2, slot2, slot3] + [rows_half] * 4 + [sds((NF, 1, FB), f32), sds((1, D), f32)],
        (shifted2, g_all, kept, mod, w1, b1, chan, w2),
        in_specs=[ANY, ANY, vmem, vmem, ANY, vmem, vmem, ANY],
        out_specs=[ANY] * 25 + [vmem, vmem],
        scratch=[vm(L, D), vm(L, D), vm(2, D, FB), vm(2, 4, FZ, D), vm(L, FB), vm(L, FB),
                 vm(L, FB), vm(L, D, dtype=f32), vm(L, D, dtype=f32), vm(2, LH, D), vm(2, LH, D), vm(4, D, TD)]
        + [vm(2, *slot1.shape)] * 2 + [vm(2, *slot2.shape)] * 2 + [vm(2, *slot3.shape), vm(2, 3, *slot3.shape[1:])]
        + [vm(2, *p.shape) for p in (part1, part2)] * 2
        + [dma(2, 20), dma(2, 2), dma(2), dma(2, 2), dma(2, 9)],
        peers=("c", "x", "y", "z1", "z2", "z3"), cid=0,
        flops=36 * L * D * FB, nbytes=40e6,
    )
    second0, second1, slots = own[:8], own[8:16], own[16:21]
    branch, ds2, branch_r, ds2_r, sum1, sum2 = own[21:]

    slot_a, slot_b = sds((2, 4, PA, LANES), bf16), sds((2, 4, PR - PA, LANES), bf16)
    own, given = call(
        middle_kernel, "middle",
        (sds((LH, D), f32), rows_half, sds((L, WC), bf16), slot_a, slot_a, slot_b, slot_b, sds((8, D), f32),
         sds((8, D), f32)),
        (ds2, ds2_r, branch, branch_r, attn, tok, g_all, kept, mod, fc2_bias, mixed, wp),
        in_specs=[ANY] * 7 + [vmem] * 3 + [ANY] * 2,
        out_specs=[ANY] * 7 + [vmem] * 2,
        scratch=[vm(LH, D, dtype=f32), vm(LH, D), vm(L, WC)] + [vm(*v.shape) for v in (slot_a, slot_a, slot_b, slot_b)]
        + [vm(4, LH, D), vm(LH, D, dtype=f32), vm(2, LH, D), vm(L, WC), vm(4, DC, D), vm(L, D), vm(4, WC, TD),
                 dma(2, 4), dma(2), dma(4, 7), dma(7)],
        peers=("c",), cid=3, jobs=[FirstSum(*slots), SecondSum(*second0)],
        flops=4 * L * D * WC, nbytes=20e6,
    )
    d_resid, out_rows, dh, *slots_p, sums_mid, sum_attn = own
    first2, result0 = given
    slot_q = vm(2, 4, QA, LANES)
    fourth = vm(4, QA, LANES)
    part_q = sds((4, QA, LANES), bf16)
    own, given = call(
        functools.partial(attn_back_kernel, 512), "attn_back",
        [sds((L, 3 * WC), bf16)] + [part_q] * 6 + [sds((8, WQ), f32)], (qkv, dh, shifted, hmask),
        in_specs=[ANY] * 3 + [vmem],
        out_specs=[ANY] * 7 + [vmem],
        scratch=[vm(L, 3 * WC), vm(L, WC), vm(L, D), vm(L, 3 * WC)] + [vm(HC // 2, L, HD)] * 4
        + [vm(HC // 2, L, HD, dtype=f32)] * 2 + [vm(4, 4, TQ, DZ, dtype=f32)] + [slot_q] * 4 + [fourth] * 4
        + [dma(2, 4), dma(8)],
        cid=4, ticks=True,
        jobs=[SecondThird(*second1, tick_at=1), SecondThird(*first2[:4], slots[0], slots[2], *first2[4:], start_at=1, tick_at=2),
              FirstSecond(*slots_p, start_at=1, tick_at=2), ThirdSum(*result0), GoHome(out_rows, tick_at=2)],
        flops=30e9, nbytes=9e6,
    )
    dqkv, *second_q, even_sums = own
    final1, final2, (sent_p, kept_p), final0, (output,) = given
    width = ada_cols + LANES
    (grad_rows, gq, gp, g1, g2, grad_ada_weight, grad_ada_bias, line), _ = call(
        end_kernel, "end",
        (sds((2, LB, D), bf16), sds((DC, 3 * TD), f32), sds((DC, TD), f32), sds((DC, FF // 4), f32),
         sds((FF // 8, TD), f32), sds((DC, ada_cols), f32), sds((1, ada_cols // 2), f32), sds((8, LANES), f32)),
        (dqkv, shifted, even_sums, sum1, sum2, sum_attn, wq, d_resid, tok, mod, sums_mid, *final0, *final1, *final2, sent_p,
         kept_p, freq.reshape(4, 1, DC), *second_q),
        in_specs=[ANY] * 2 + [vmem] * 4 + [ANY] * 3 + [vmem] * 2 + [ANY] * 8 + [vmem] + [ANY] * 6,
        out_specs=[ANY, vmem] + [ANY] * 4 + [vmem] * 2,
        scratch=[vm(L, 3 * WC), vm(L, D), vm(4, 4, 8, LANES, dtype=f32), vm(4, 4, TQ, DZ, dtype=f32)]
        + [slot_q] * 6 + [fourth] * 4 + [vm(3, QR, LANES), vm(QR, LANES, dtype=f32), vm(3, QR, LANES)]
        + [fourth] * 6 + [vm(3, QR, LANES), vm(QR, LANES, dtype=f32), vm(3, QR, LANES)]
        + [vm(2, DZ, TQ, dtype=f32), vm(D, 3 * WC), vm(LH, D, dtype=f32), vm(LH, D),
           vm(NF, G1R + G2R, LANES, dtype=f32)] + [vm(2, LB, D)] * 3
        + [vm(8, D, dtype=f32)] * 2 + [vm(4, 1, width, dtype=f32)] * 2
        + [vm(4, 4, 1, width, dtype=f32), vm(1, 1, ada_cols, dtype=f32), vm(4, 1, ada_cols, dtype=f32)]
        + [vm(NF * G1R, LANES)] * 2 + [vm(2, DC, TQ)] * 2 + [vm(PR, LANES, dtype=f32), vm(3, PR, LANES)]
        + [vm(*v, dtype=f32) for v in ((DC, TD), (DC, FF // 4), (FF // 8, TD), (DC, ada_cols))]
        + [dma(2, 9), dma(2, 5), dma(2, 6), dma(2, 2), dma(2, 9), dma(2, 3), dma(23), dma(4)],
        peers=("c", "t0", "t1", "x", "y", "xy", "z1", "z2", "z3"), cid=5,
        flops=4 * L * D * 3 * WC, nbytes=30e6,
    )
    thin = lambda height, width: pl.BlockSpec((height, width), lambda i: (i, 0))
    tokens_spec = pl.BlockSpec((2, LB // 2, D), lambda i: (0, i, 0))
    ends = [thin(DC // 2, 3 * TD), thin(DC // 2, TD), thin(DC // 2, FF // 4)]
    bias_cols = ada_cols // 2
    finals, _ = call(
        final_kernel, "final",
        (sds((2, LB, D), bf16), sds((2, LB, D), f32), sds((DC, 3 * TD), f32), sds((DC, TD), f32), sds((DC, FF // 4), f32),
         sds((TD, FF // 8), f32), sds((DC, ada_cols), f32), sds((bias_cols,), f32), sds((FF // 32,), f32))
        + (sds((D // 32,), f32),) * 4,
        (output, grad_rows, gq, gp, g1, g2, grad_ada_weight, grad_ada_bias, line),
        grid=(2,),
        in_specs=[tokens_spec, tokens_spec, *ends, full((FF // 8, TD)), thin(DC // 2, ada_cols), full((1, bias_cols)),
                  full((8, LANES))],
        out_specs=[tokens_spec, tokens_spec, *ends, full((TD, FF // 8)), thin(DC // 2, ada_cols), full((bias_cols,)),
                   full((FF // 32,))] + [full((D // 32,))] * 4,
    )
    output, grad_tokens, gq, gp, g1, g2, g_ada, ada_b, b_fc1, b_fc2, b_proj, b_q, b_v = finals
    return (output, grad_tokens, gq, b_q, b_v, gp, b_proj, g1, b_fc1, g2.T, b_fc2, g_ada, ada_b)


def gelu_tanh(values):
    return jax.nn.gelu(values, approximate=True)


def split_heads(key_value, model_width, head_dim):
    item_count, length = (key_value.shape[0], key_value.shape[1])
    key_rows = key_value[:, :, :model_width].reshape(
        item_count, length, model_width // head_dim, head_dim
    )
    value_rows = key_value[:, :, model_width:].reshape(
        item_count, length, model_width // head_dim, head_dim
    )
    return (key_rows, value_rows)


def scores_of(queries, key_rows, score_scale):
    return (
        jnp.einsum("nqhe,nkhe->nhqk", queries, key_rows, preferred_element_type=jnp.float32)
        * score_scale
    )


def to_blocks(values, per_step):
    return values.reshape((values.shape[0] // per_step, per_step) + values.shape[1:])


def from_blocks(values):
    return values.reshape((values.shape[0] * values.shape[1],) + values.shape[2:])


def on_device(
    tokens,
    cotangent,
    timesteps,
    bucket_ids,
    head_masks,
    channel_masks,
    skip_rows,
    w_qkv,
    q_bias,
    v_bias,
    w_proj,
    proj_bias,
    w_fc1,
    fc1_bias,
    w_fc2,
    fc2_bias,
    ada_weight,
    ada_bias,
):
    item_count, local_len, model_width = tokens.shape
    row_count = item_count * local_len
    head_dim = model_width // HEADS
    score_scale = 1.0 / math.sqrt(head_dim)
    hidden_width = w_fc1.shape[1]
    ada_cols = ada_weight.shape[1]
    tok_index = lax.axis_index("tok")
    per_step = 1
    for candidate in range(1, item_count + 1):
        per_step = candidate
    condition = jax.nn.silu(step_embedding(timesteps, model_width)).astype(jnp.bfloat16)
    mod_local = jnp.dot(
        condition, ada_weight, preferred_element_type=jnp.float32
    ) + ada_bias.astype(jnp.float32)
    modulation = lax.all_gather(mod_local, "tok", axis=1, tiled=True)
    pieces = modulation.reshape(item_count, 6, 1, model_width)
    shift_a = pieces[:, 0]
    scale_a = pieces[:, 1]
    gate_a = pieces[:, 2]
    shift_m = pieces[:, 3]
    scale_m = pieces[:, 4]
    gate_m = pieces[:, 5]
    chosen = (jnp.arange(head_masks.shape[0], dtype=jnp.int32) == bucket_ids[0]).astype(jnp.float32)
    head_on = jnp.sum(chosen[:, None] * head_masks.astype(jnp.float32), axis=0)
    group_on = jnp.sum(chosen[:, None] * channel_masks.astype(jnp.float32), axis=0)
    channel_on = jnp.repeat(group_on, hidden_width // group_on.shape[0])
    positions = tok_index * local_len + jnp.arange(local_len, dtype=jnp.int32)
    skipped = jnp.any(skip_rows[:, :, None] == positions[None, None, :], axis=1)
    kept_rows = 1.0 - skipped.astype(jnp.float32)
    inputs = tokens.astype(jnp.float32)
    normed, inverse = normalize(inputs)
    shifted = (
        (normed * (1.0 + scale_a) + shift_a).astype(jnp.bfloat16).reshape(row_count, model_width)
    )
    qkv_bias = jnp.concatenate([q_bias, jnp.zeros_like(q_bias), v_bias]).astype(jnp.float32)
    projected = (jnp.dot(shifted, w_qkv, preferred_element_type=jnp.float32) + qkv_bias).astype(
        jnp.bfloat16
    )
    projected = projected.reshape(item_count, local_len, 3 * model_width)
    queries = projected[:, :, :model_width].reshape(item_count, local_len, HEADS, head_dim)
    key_value = projected[:, :, model_width:]
    all_kv = lax.all_gather(key_value, "tok", axis=1, tiled=True)

    def forward_block(packed):
        query_block, kv_block = packed
        key_rows, value_rows = split_heads(kv_block, model_width, head_dim)
        scores = scores_of(query_block, key_rows, score_scale)
        top_score = jnp.max(scores, axis=-1, keepdims=True)
        expanded = jnp.exp(scores - top_score)
        totals = jnp.sum(expanded, axis=-1, keepdims=True)
        weights_low = (expanded / totals).astype(jnp.bfloat16)
        head_out = (
            jnp.einsum(
                "nhqk,nkhe->nqhe", weights_low, value_rows, preferred_element_type=jnp.float32
            )
            * head_on[:, None]
        )
        return (head_out.astype(jnp.bfloat16), top_score + jnp.log(totals))

    mixed_heads, log_total = lax.map(
        forward_block, (to_blocks(queries, per_step), to_blocks(all_kv, per_step))
    )
    log_total = from_blocks(log_total)
    mixed = from_blocks(mixed_heads).reshape(row_count, model_width)
    attn = (
        jnp.dot(mixed, w_proj, preferred_element_type=jnp.float32) + proj_bias.astype(jnp.float32)
    ).reshape(item_count, local_len, model_width)
    resid = inputs + gate_a * attn
    normed2, inverse2 = normalize(resid)
    shifted2 = (
        (normed2 * (1.0 + scale_m) + shift_m).astype(jnp.bfloat16).reshape(row_count, model_width)
    )
    pre = jnp.dot(shifted2, w_fc1, preferred_element_type=jnp.float32) + fc1_bias.astype(
        jnp.float32
    )
    activated, gelu_pull = jax.vjp(gelu_tanh, pre)
    hidden = (activated * channel_on).astype(jnp.bfloat16)
    branch = (
        jnp.dot(hidden, w_fc2, preferred_element_type=jnp.float32) + fc2_bias.astype(jnp.float32)
    ).reshape(item_count, local_len, model_width)
    gated = kept_rows[:, :, None] * gate_m
    output = (resid + gated * branch).astype(jnp.bfloat16)
    incoming = cotangent.astype(jnp.float32)
    d_gate_m = jnp.sum(kept_rows[:, :, None] * branch * incoming, axis=1)
    d_branch = (gated * incoming).astype(jnp.bfloat16).reshape(row_count, model_width)
    grad_w_fc2 = jnp.dot(hidden.T, d_branch, preferred_element_type=jnp.float32)
    grad_fc2_bias = jnp.sum(d_branch.astype(jnp.float32), axis=0)
    d_hidden = jnp.dot(d_branch, w_fc2.T, preferred_element_type=jnp.float32)
    d_pre = gelu_pull(d_hidden * channel_on)[0].astype(jnp.bfloat16)
    grad_w_fc1 = jnp.dot(shifted2.T, d_pre, preferred_element_type=jnp.float32)
    grad_fc1_bias = jnp.sum(d_pre.astype(jnp.float32), axis=0)
    d_shifted2 = jnp.dot(d_pre, w_fc1.T, preferred_element_type=jnp.float32).reshape(
        item_count, local_len, model_width
    )
    d_shift_m = jnp.sum(d_shifted2, axis=1)
    d_scale_m = jnp.sum(d_shifted2 * normed2, axis=1)
    d_resid = incoming + normalize_back(d_shifted2 * (1.0 + scale_m), normed2, inverse2)
    d_gate_a = jnp.sum(attn * d_resid, axis=1)
    d_attn = (gate_a * d_resid).astype(jnp.bfloat16).reshape(row_count, model_width)
    grad_w_proj = jnp.dot(mixed.T, d_attn, preferred_element_type=jnp.float32)
    grad_proj_bias = jnp.sum(d_attn.astype(jnp.float32), axis=0)
    d_mixed = jnp.dot(d_attn, w_proj.T, preferred_element_type=jnp.float32).astype(jnp.bfloat16)
    d_heads = d_mixed.reshape(item_count, local_len, HEADS, head_dim) * head_on[:, None].astype(
        jnp.bfloat16
    )
    again_kv = lax.all_gather(key_value, "tok", axis=1, tiled=True)

    def backward_block(packed):
        query_block, kv_block, head_grads, totals_log = packed
        key_rows, value_rows = split_heads(kv_block, model_width, head_dim)
        scores = scores_of(query_block, key_rows, score_scale)
        probs = jnp.exp(scores - totals_log)
        d_probs = jnp.einsum(
            "nqhe,nkhe->nhqk", head_grads, value_rows, preferred_element_type=jnp.float32
        )
        row_dot = jnp.sum(probs * d_probs, axis=-1, keepdims=True)
        d_scores = (probs * (d_probs - row_dot)).astype(jnp.bfloat16)
        d_queries = (
            jnp.einsum("nhqk,nkhe->nqhe", d_scores, key_rows, preferred_element_type=jnp.float32)
            * score_scale
        )
        return (d_queries, row_dot)

    mapped = lax.map(
        backward_block,
        (
            to_blocks(queries, per_step),
            to_blocks(again_kv, per_step),
            to_blocks(d_heads, per_step),
            to_blocks(log_total, per_step),
        ),
    )
    d_queries = from_blocks(mapped[0])
    row_dot = from_blocks(mapped[1])
    queries_all, head_grads_all = (
        lax.all_gather(queries, "tok", axis=1, tiled=True),
        lax.all_gather(d_heads, "tok", axis=1, tiled=True),
    )
    totals_all, row_dot_all = (
        lax.all_gather(log_total, "tok", axis=2, tiled=True),
        lax.all_gather(row_dot, "tok", axis=2, tiled=True),
    )

    def key_block(packed):
        kv_block, query_block, head_grads, totals_log, dots = packed
        key_rows, value_rows = split_heads(kv_block, model_width, head_dim)
        scores = (
            jnp.einsum("nkhe,nqhe->nhkq", key_rows, query_block, preferred_element_type=jnp.float32)
            * score_scale
        )
        probs = jnp.exp(scores - totals_log[:, :, None, :, 0])
        d_probs = jnp.einsum(
            "nkhe,nqhe->nhkq", value_rows, head_grads, preferred_element_type=jnp.float32
        )
        d_scores = (probs * (d_probs - dots[:, :, None, :, 0])).astype(jnp.bfloat16)
        d_keys = (
            jnp.einsum("nhkq,nqhe->nkhe", d_scores, query_block, preferred_element_type=jnp.float32)
            * score_scale
        )
        d_values = jnp.einsum(
            "nhkq,nqhe->nkhe",
            probs.astype(jnp.bfloat16),
            head_grads,
            preferred_element_type=jnp.float32,
        )
        return jnp.concatenate(
            [
                d_keys.reshape(d_keys.shape[0], local_len, model_width),
                d_values.reshape(d_values.shape[0], local_len, model_width),
            ],
            axis=2,
        )

    d_kv = from_blocks(
        lax.map(
            key_block,
            (
                to_blocks(key_value, per_step),
                to_blocks(queries_all, per_step),
                to_blocks(head_grads_all, per_step),
                to_blocks(totals_all, per_step),
                to_blocks(row_dot_all, per_step),
            ),
        )
    )
    d_qkv = jnp.concatenate([d_queries.reshape(item_count, local_len, model_width), d_kv], axis=2)
    d_qkv = d_qkv.astype(jnp.bfloat16).reshape(row_count, 3 * model_width)
    grad_w_qkv = jnp.dot(shifted.T, d_qkv, preferred_element_type=jnp.float32)
    qkv_sums = jnp.sum(d_qkv.astype(jnp.float32), axis=0)
    grad_q_bias = qkv_sums[:model_width]
    grad_v_bias = qkv_sums[2 * model_width :]
    d_shifted = jnp.dot(d_qkv, w_qkv.T, preferred_element_type=jnp.float32).reshape(
        item_count, local_len, model_width
    )
    d_shift_a = jnp.sum(d_shifted, axis=1)
    d_scale_a = jnp.sum(d_shifted * normed, axis=1)
    grad_tokens = d_resid + normalize_back(d_shifted * (1.0 + scale_a), normed, inverse)
    d_modulation = jnp.concatenate(
        [d_shift_a, d_scale_a, d_gate_a, d_shift_m, d_scale_m, d_gate_m], axis=1
    )
    d_modulation = lax.psum(d_modulation, "tok")
    mod_columns = lax.dynamic_slice_in_dim(d_modulation, tok_index * ada_cols, ada_cols, 1)
    grad_ada_weight = jnp.dot(
        condition.astype(jnp.float32).T, mod_columns, precision=lax.Precision.HIGHEST
    )
    grad_ada_bias = jnp.sum(d_modulation, axis=0)
    bucket_done = (
        lax.psum_scatter(grad_w_qkv, "bucket", scatter_dimension=0, tiled=True),
        lax.psum_scatter(grad_w_proj, "bucket", scatter_dimension=0, tiled=True),
        lax.psum_scatter(grad_w_fc1, "bucket", scatter_dimension=0, tiled=True),
        lax.psum_scatter(grad_w_fc2, "bucket", scatter_dimension=0, tiled=True),
        lax.psum_scatter(grad_q_bias, "bucket", scatter_dimension=0, tiled=True),
        lax.psum_scatter(grad_v_bias, "bucket", scatter_dimension=0, tiled=True),
        lax.psum_scatter(grad_proj_bias, "bucket", scatter_dimension=0, tiled=True),
        lax.psum_scatter(grad_fc1_bias, "bucket", scatter_dimension=0, tiled=True),
        lax.psum_scatter(grad_fc2_bias, "bucket", scatter_dimension=0, tiled=True),
        lax.psum_scatter(grad_ada_weight, "bucket", scatter_dimension=0, tiled=True),
        lax.psum_scatter(grad_ada_bias, "bucket", scatter_dimension=0, tiled=True),
    )
    token_done = (
        lax.psum_scatter(bucket_done[0], "tok", scatter_dimension=1, tiled=True),
        lax.psum_scatter(bucket_done[1], "tok", scatter_dimension=1, tiled=True),
        lax.psum_scatter(bucket_done[2], "tok", scatter_dimension=1, tiled=True),
        lax.psum_scatter(bucket_done[3], "tok", scatter_dimension=1, tiled=True),
        lax.psum_scatter(bucket_done[4].reshape(1, -1), "tok", scatter_dimension=1, tiled=True),
        lax.psum_scatter(bucket_done[5].reshape(1, -1), "tok", scatter_dimension=1, tiled=True),
        lax.psum_scatter(bucket_done[6].reshape(1, -1), "tok", scatter_dimension=1, tiled=True),
        lax.psum_scatter(bucket_done[7].reshape(1, -1), "tok", scatter_dimension=1, tiled=True),
        lax.psum_scatter(bucket_done[8].reshape(1, -1), "tok", scatter_dimension=1, tiled=True),
    )
    finished = (
        token_done[0],
        token_done[1],
        token_done[2],
        token_done[3],
        token_done[4],
        token_done[5],
        token_done[6],
        token_done[7],
        token_done[8],
        bucket_done[9],
        bucket_done[10],
    )
    return (
        output,
        grad_tokens,
        finished[0],
        finished[4].reshape(-1),
        finished[5].reshape(-1),
        finished[1],
        finished[6].reshape(-1),
        finished[2],
        finished[7].reshape(-1),
        finished[3],
        finished[8].reshape(-1),
        finished[9],
        finished[10],
    )


def solution(mesh):
    planned = mesh.shape["tok"] == 4 and mesh.shape["bucket"] == 8
    return jax.shard_map(
        one_item_per_chip if planned else on_device,
        mesh=mesh,
        in_specs=(
            P("bucket", "tok", None),
            P("bucket", "tok", None),
            P("bucket"),
            P("bucket"),
            P(),
            P(),
            P("bucket", None),
            P(),
            P(),
            P(),
            P(),
            P(),
            P(),
            P(),
            P(),
            P(),
            P(None, "tok"),
            P("tok"),
        ),
        out_specs=(
            P("bucket", "tok", None),
            P("bucket", "tok", None),
            P("bucket", "tok"),
            P(("bucket", "tok")),
            P(("bucket", "tok")),
            P("bucket", "tok"),
            P(("bucket", "tok")),
            P("bucket", "tok"),
            P(("bucket", "tok")),
            P("bucket", "tok"),
            P(("bucket", "tok")),
            P("bucket", "tok"),
            P("bucket"),
        ),
        check_vma=False,
    )
```

```python
import functools
import math
import types

import jax
import jax.numpy as jnp
import numpy as np
from jax import lax
from jax.experimental import pallas as pl
from jax.experimental.pallas import tpu as pltpu
from jax.sharding import PartitionSpec as P

HEADS = 16
EPSILON = 1e-06
LOG2E = 1.4426950408889634
GELU_K = math.sqrt(2.0 / math.pi)
GELU_C = 0.044715
LANES = 128
bf16, f32 = jnp.bfloat16, jnp.float32


def dot_nn(a, b):
    return lax.dot_general(a, b, (((1,), (0,)), ((), ())), preferred_element_type=f32)


def dot_nt(a, b):
    return lax.dot_general(a, b, (((1,), (1,)), ((), ())), preferred_element_type=f32)


def dot_tn(a, b):
    return lax.dot_general(a, b, (((0,), (0,)), ((), ())), preferred_element_type=f32)


def step_embedding(timesteps, model_width):
    half_width = model_width // 2
    frequency = jnp.exp(-math.log(10000.0) * jnp.arange(half_width, dtype=jnp.float32) / half_width)
    angles = timesteps.astype(jnp.float32)[:, None] * frequency[None, :]
    return jnp.concatenate([jnp.cos(angles), jnp.sin(angles)], axis=1)


def normalize(values):
    centred = values - jnp.mean(values, axis=-1, keepdims=True)
    inverse = lax.rsqrt(jnp.mean(centred * centred, axis=-1, keepdims=True) + EPSILON)
    return (centred * inverse, inverse)


def normalize_back(incoming, normed, inverse):
    return inverse * (
        incoming
        - jnp.mean(incoming, axis=-1, keepdims=True)
        - normed * jnp.mean(incoming * normed, axis=-1, keepdims=True)
    )


D = 1152
DC, DZ, TD = D // 8, D // 4, D // 4
HD = D // HEADS
HC = HEADS // 2
WC = D // 2
FF = 4608
NF = 3
FB = FF // 2 // NF
FZ = FB // 4
L = 1024
LH = L // 2
LB = L // 4
G1R = 3 * DC
G2R = 2 * FZ + FZ // 4
GC = 96
GA, GB = G1R - GC, G2R - GC
PR = 2 * DC + DC // 3
PA = 176
WQ = 3 * WC // 2
TQ = WQ // 4
QR = 512
QA = QR // 2
VMEM_LIMIT = 60 * 1024 * 1024


ANY = pl.BlockSpec(memory_space=pl.ANY)
MESH = pl.DeviceIdType.MESH


def place():
    b, t = lax.axis_index("bucket"), lax.axis_index("tok")
    return b // 2, b % 2, t // 2, t % 2


def flip(value, other):
    return (value // 2 + other // 2) % 2 * 2 + (value % 2 + other % 2) % 2


def peer(name):
    z, c, y, x = place()
    if name == "x":
        x = 1 - x
    elif name == "y":
        y = 1 - y
    elif name == "xy":
        x, y = 1 - x, 1 - y
    elif name == "c":
        c = 1 - c
    elif name in ("t0", "t1"):
        c, y, x = y, c, x if name == "t0" else 1 - x
    else:
        z = flip(z, int(name[1]))
    return (z * 2 + c, y * 2 + x)


def greet(names):
    sem = pltpu.get_barrier_semaphore()
    for name in names:
        if name == "t0":
            continue
        pl.semaphore_signal(sem, inc=1, device_id=peer(name), device_id_type=MESH)
    if "t0" in names:
        _, c, y, _ = place()

        @pl.when(c != y)
        def _():
            pl.semaphore_signal(sem, inc=1, device_id=peer("t0"), device_id_type=MESH)


def meet(names):
    wanted = len([name for name in names if name != "t0"])
    if "t0" in names:
        _, c, y, _ = place()
        wanted = wanted + (c + y) % 2
    pl.semaphore_wait(pltpu.get_barrier_semaphore(), wanted)


def remote(src, dst, sems, k, name):
    return pltpu.make_async_remote_copy(
        src_ref=src, dst_ref=dst, send_sem=sems.at[0, k], recv_sem=sems.at[1, k],
        device_id=peer(name), device_id_type=MESH,
    )


def vm(*shape, dtype=bf16):
    return pltpu.VMEM(shape, dtype)


class Job:
    start_at = tick_at = 0

    def bind(self, scratch):
        return types.SimpleNamespace(**dict(zip(self.spec, scratch)))

    @property
    def scratch(self):
        return list(self.spec.values())


def sds(shape, dtype=bf16):
    return jax.ShapeDtypeStruct(shape, dtype)


def upto(sources, targets, sems):
    return [pltpu.make_async_copy(a, b, sems.at[k]) for k, (a, b) in enumerate(zip(sources, targets))]


def dma(*shape):
    return pltpu.SemaphoreType.DMA(shape)


def total_of(*parts):
    total = parts[0].astype(f32)
    for part in parts[1:]:
        total = total + part.astype(f32)
    return total


class FirstSum(Job):
    def __init__(self, keep_a, sent_a, keep_b, sent_b, third=None):
        self.third = third is not None
        self.peers = ("x", "y", "z1", "z2", "z3") if self.third else ("x", "y")
        self.ins = [keep_a, sent_a, keep_b, sent_b] + ([third] if self.third else [])
        a, b = keep_a.shape[1:], keep_b.shape[1:]
        self.outs = [sds(a), sds(a), sds(b), sds(b)]
        self.spec = dict(ka=vm(*a), ra=vm(*a), oa=vm(*a), kb=vm(*b), rb=vm(*b), ob=vm(*b), sems=dma(2, 7), local=dma(7))
        if self.third:
            c = third.shape[1:]
            self.outs += [sds(c[1:]), sds(c[1:])]
            self.spec.update(kc=vm(*c), rc=vm(3, *c))

    def plan(self, ins, outs, scratch):
        v = self.bind(scratch)
        far = [
            remote(ins[1].at[1], v.ra, v.sems, 0, "x"), remote(ins[3].at[1], v.rb, v.sems, 1, "y"),
            remote(ins[1].at[0], outs[1], v.sems, 2, "x"), remote(ins[3].at[0], outs[3], v.sems, 3, "y"),
        ]
        near = upto([ins[0].at[1], ins[2].at[1]], [v.ka, v.kb], v.local)
        if self.third:
            far += [remote(ins[4].at[k], v.rc.at[k - 1], v.sems, 3 + k, f"z{k}") for k in (3, 2, 1)]
            near.append(pltpu.make_async_copy(ins[4].at[0], v.kc, v.local.at[2]))
        return far, near

    def finish(self, ins, outs, scratch):
        v = self.bind(scratch)
        v.oa[...] = total_of(v.ka[...], v.ra[...]).astype(bf16)
        v.ob[...] = total_of(v.kb[...], v.rb[...]).astype(bf16)
        pairs = [(v.oa, outs[0]), (v.ob, outs[2])]
        if self.third:
            v.kc[...] = total_of(v.kc[...], v.rc[0], v.rc[1], v.rc[2]).astype(bf16)
            pairs += [(v.kc.at[0], outs[4]), (v.kc.at[1], outs[5])]
        return [pltpu.make_async_copy(a, b, v.local.at[3 + k]) for k, (a, b) in enumerate(pairs)]


def layer_sums(streams, zs, zk):
    start = 0
    for kv, qv, rv in streams:
        end = start + rv.shape[1]
        for j in range(4):
            total = total_of(kv[j], qv[j], rv[j])
            if j == 0:
                zk[start:end, :] = total
            else:
                zs[j - 1, start:end, :] = total.astype(bf16)
        start = end


class SecondSum(Job):
    peers = ("x", "y")

    def __init__(self, on_a, q_a, on_b, q_b, keep_a, keep_b, keep_c=None, sent_c=None, start_at=0):
        self.start_at = start_at
        self.third = keep_c is not None
        self.ins = [on_a, q_a, on_b, q_b, keep_a, keep_b] + ([keep_c, sent_c] if self.third else [])
        a, b = on_a.shape, on_b.shape
        rows_ = a[1] + b[1]
        self.outs = [sds((3, rows_, LANES)), sds((rows_, LANES), f32)]
        self.spec = dict(ka=vm(*a), qa=vm(*a), ra=vm(*a), kb=vm(*b), qb=vm(*b), rb=vm(*b), zs=vm(3, rows_, LANES),
                         zk=vm(rows_, LANES, dtype=f32), sems=dma(2, 3), local=dma(9))
        if self.third:
            c = keep_c.shape
            self.outs += [sds(c[1:]), sds(c[1:])]
            self.spec.update(kc=vm(*c), rc=vm(*c))

    def plan(self, ins, outs, scratch):
        v = self.bind(scratch)
        whole = [k.at[0] if len(k.shape) == 4 else k for k in ins[4:6]]
        far = [remote(ins[0], v.ra, v.sems, 0, "y"), remote(ins[2], v.rb, v.sems, 1, "x")]
        near = upto([whole[0], ins[1], whole[1], ins[3]], [v.ka, v.qa, v.kb, v.qb], v.local)
        if self.third:
            far.append(remote(ins[7], v.rc, v.sems, 2, "x"))
            near.append(pltpu.make_async_copy(ins[6], v.kc, v.local.at[4]))
        return far, near

    def add(self, v):
        layer_sums([(v.ka, v.qa, v.ra), (v.kb, v.qb, v.rb)], v.zs, v.zk)
        if self.third:
            v.kc[...] = total_of(v.kc[...], v.rc[...]).astype(bf16)

    def finish(self, ins, outs, scratch):
        v = self.bind(scratch)
        self.add(v)
        pairs = [(v.zs, outs[0]), (v.zk, outs[1])]
        if self.third:
            pairs += [(v.kc.at[0], outs[2]), (v.kc.at[1], outs[3])]
        return [pltpu.make_async_copy(a, b, v.local.at[5 + k]) for k, (a, b) in enumerate(pairs)]


class ThirdSum(Job):
    def __init__(self, sent, kept, keep_c=None, sent_c=None):
        self.third = keep_c is not None
        self.peers = ("z1", "z2", "z3", "y") if self.third else ("z1", "z2", "z3")
        self.ins = [sent, kept] + ([keep_c, sent_c] if self.third else [])
        self.outs = [sds(kept.shape, f32)]
        self.spec = dict(got=vm(*sent.shape), kept=vm(*kept.shape, dtype=f32), sems=dma(2, 4), local=dma(4))
        if self.third:
            self.outs.append(sds(keep_c.shape, f32))
            self.spec.update(kc=vm(*keep_c.shape), rc=vm(*keep_c.shape), fc=vm(*keep_c.shape, dtype=f32))

    def plan(self, ins, outs, scratch):
        v = self.bind(scratch)
        far = [remote(ins[0].at[k], v.got.at[k], v.sems, k, f"z{k + 1}") for k in (2, 1, 0)]
        near = [pltpu.make_async_copy(ins[1], v.kept, v.local.at[0])]
        if self.third:
            far.append(remote(ins[3], v.rc, v.sems, 3, "y"))
            near.append(pltpu.make_async_copy(ins[2], v.kc, v.local.at[1]))
        return far, near

    def finish(self, ins, outs, scratch):
        v = self.bind(scratch)
        v.kept[...] = total_of(v.kept[...], v.got[0], v.got[1], v.got[2])
        pairs = [(v.kept, outs[0])]
        if self.third:
            v.fc[...] = total_of(v.kc[...], v.rc[...])
            pairs.append((v.fc, outs[1]))
        return [pltpu.make_async_copy(a, b, v.local.at[2 + k]) for k, (a, b) in enumerate(pairs)]


class SecondThird(SecondSum):
    peers = ("x", "y", "z1", "z2", "z3")

    def __init__(self, *args, start_at=0, tick_at=1):
        super().__init__(*args, start_at=start_at)
        self.tick_at = tick_at
        kept, c = self.outs[1], self.spec["kc"].shape[1:]
        self.outs = [kept, sds(c, f32)]
        self.spec.update(got=vm(3, *kept.shape), sems3=dma(2, 4), rc3=vm(*c), fc=vm(*c, dtype=f32))

    def next_copies(self, v):
        far = [remote(v.zs.at[k], v.got.at[k], v.sems3, k, f"z{k + 1}") for k in (2, 1, 0)]
        return far + [remote(v.kc.at[1], v.rc3, v.sems3, 3, "y")]

    def tick(self, ins, outs, scratch):
        v = self.bind(scratch)
        for group in self.plan(ins, outs, scratch):
            for copy in group:
                copy.wait()
        self.add(v)
        for copy in self.next_copies(v):
            copy.start()

    def settle(self, ins, outs, scratch):
        return self.next_copies(self.bind(scratch))

    def finish(self, ins, outs, scratch):
        v = self.bind(scratch)
        v.zk[...] = total_of(v.zk[...], v.got[0], v.got[1], v.got[2])
        v.fc[...] = total_of(v.kc[0], v.rc3[...])
        return upto([v.zk, v.fc], outs, v.local)


class FirstSecond(Job):
    peers = ("x", "y")

    def __init__(self, keep_a, sent_a, keep_b, sent_b, start_at=0, tick_at=1):
        self.start_at, self.tick_at = start_at, tick_at
        self.ins = [keep_a, sent_a, keep_b, sent_b]
        a, b = keep_a.shape, keep_b.shape
        rows_ = a[2] + b[2]
        self.outs = [sds((3, rows_, LANES)), sds((rows_, LANES), f32)]
        self.spec = dict(ka=vm(*a), ra=vm(*a), oa=vm(*a[1:]), ra2=vm(*a[1:]), kb=vm(*b), rb=vm(*b), ob=vm(*b[1:]),
                         rb2=vm(*b[1:]), zs=vm(3, rows_, LANES), zk=vm(rows_, LANES, dtype=f32), sems=dma(2, 6), local=dma(4))

    def plan(self, ins, outs, scratch):
        v = self.bind(scratch)
        far = [
            remote(ins[1].at[1], v.ra.at[1], v.sems, 0, "x"), remote(ins[3].at[1], v.rb.at[1], v.sems, 1, "y"),
            remote(ins[1].at[0], v.ra.at[0], v.sems, 2, "x"), remote(ins[3].at[0], v.rb.at[0], v.sems, 3, "y"),
        ]
        return far, upto([ins[0], ins[2]], [v.ka, v.kb], v.local)

    def next_copies(self, v):
        return [remote(v.oa, v.ra2, v.sems, 4, "y"), remote(v.ob, v.rb2, v.sems, 5, "x")]

    def tick(self, ins, outs, scratch):
        v = self.bind(scratch)
        for group in self.plan(ins, outs, scratch):
            for copy in group:
                copy.wait()
        v.oa[...] = total_of(v.ka[1], v.ra[1]).astype(bf16)
        v.ob[...] = total_of(v.kb[1], v.rb[1]).astype(bf16)
        for copy in self.next_copies(v):
            copy.start()

    def settle(self, ins, outs, scratch):
        return self.next_copies(self.bind(scratch))

    def finish(self, ins, outs, scratch):
        v = self.bind(scratch)
        layer_sums([(v.ka.at[0], v.ra.at[0], v.ra2), (v.kb.at[0], v.rb.at[0], v.rb2)], v.zs, v.zk)
        return [pltpu.make_async_copy(a, b, v.local.at[2 + k]) for k, (a, b) in enumerate(((v.zs, outs[0]), (v.zk, outs[1])))]


class GoHome(Job):
    peers = ("t0", "t1")

    def __init__(self, values, tick_at=1):
        self.tick_at = tick_at
        self.ins = [values]
        self.outs = [sds((2, LB, D), values.dtype)]
        self.spec = dict(sems=dma(2, 2), local=pltpu.SemaphoreType.DMA)

    def copies(self, ins, outs, scratch):
        return homeward(ins[0].at[pl.ds(0, LB)], ins[0].at[pl.ds(LB, LB)], outs[0], *scratch)

    def plan(self, ins, outs, scratch):
        home_start(*self.copies(ins, outs, scratch)[:2])
        return [], []

    def tick(self, ins, outs, scratch):
        self.copies(ins, outs, scratch)[2].start()

    def settle(self, ins, outs, scratch):
        home_wait(*self.copies(ins, outs, scratch))
        return []

    def finish(self, ins, outs, scratch):
        return []


def homeward(first, second, dst, sems, local):
    x = place()[3]
    return (
        remote(first, dst.at[x], sems, 0, "t0"),
        pltpu.make_async_copy(first, dst.at[x], local),
        remote(second, dst.at[x], sems, 1, "t1"),
    )


def home_start(away, stay, second=None):
    _, c, y, _ = place()
    pl.when(c != y)(away.start)
    pl.when(c == y)(stay.start)
    if second is not None:
        second.start()


def home_wait(away, stay, second):
    _, c, y, _ = place()
    pl.when(c != y)(away.wait)
    pl.when(c == y)(stay.wait)
    second.wait()


def call(kernel, name, out_shape, args, in_specs=None, out_specs=None, scratch=(), grid=None,
         peers=(), jobs=(), cid=None, ticks=False, flops=0, nbytes=0):
    whole = pl.BlockSpec(memory_space=pltpu.VMEM)
    single = not isinstance(out_shape, (tuple, list))
    out_shape = [out_shape] if single else list(out_shape)
    in_specs = list(in_specs) if in_specs is not None else [whole] * len(args)
    out_specs = [whole] * len(out_shape) if out_specs is None else [out_specs] if single else list(out_specs)
    counts = [len(args), sum(len(j.ins) for j in jobs), len(out_shape), sum(len(j.outs) for j in jobs), len(scratch)]
    names = sorted(set(peers).union(*[j.peers for j in jobs]))

    def run(*refs):
        groups, at = [], 0
        for n in counts:
            groups.append(refs[at : at + n])
            at += n
        bound, ai, ao, asc = [], 0, 0, at
        for j in jobs:
            bound.append((
                j, groups[1][ai : ai + len(j.ins)], groups[3][ao : ao + len(j.outs)], refs[asc : asc + len(j.scratch)]
            ))
            ai, ao, asc = ai + len(j.ins), ao + len(j.outs), asc + len(j.scratch)

        def ready():
            if names:
                meet(names)
            for j, *r in bound:
                if not j.start_at:
                    j_start(j, r)

        def j_start(j, r):
            for group in j.plan(*r):
                for copy in group:
                    copy.start()

        def tick(k):
            for j, *r in bound:
                if j.tick_at == k:
                    j.tick(*r)
            for j, *r in bound:
                if j.start_at == k:
                    j_start(j, r)

        def end():
            last = []
            for j, *r in bound:
                far, near = (j.settle(*r), []) if j.tick_at else j.plan(*r)
                for copy in far:
                    copy.wait()
                for copy in near:
                    copy.wait()
                copies = j.finish(*r)
                for copy in copies:
                    copy.start()
                last += copies
            for copy in last:
                copy.wait()

        if names:
            greet(names)
            kernel(*groups[0], *groups[2], *groups[4], ready=ready, **({"tick": tick} if ticks else {}))
            end()
        else:
            kernel(*groups[0], *groups[2], *groups[4])

    extra = {} if grid is None else {"grid": grid}
    params = {"collective_id": cid, "has_side_effects": True} if names else {}
    outs = pl.pallas_call(
        run,
        out_shape=out_shape + [o for j in jobs for o in j.outs],
        in_specs=in_specs + [ANY] * counts[1],
        out_specs=out_specs + [ANY] * counts[3],
        scratch_shapes=list(scratch) + [q for j in jobs for q in j.scratch],
        compiler_params=pltpu.CompilerParams(vmem_limit_bytes=VMEM_LIMIT, **params),
        cost_estimate=pl.CostEstimate(flops=int(flops), bytes_accessed=int(nbytes), transcendentals=0),
        name=name,
        **extra,
    )(*args, *[a for j in jobs for a in j.ins])
    own, rest, given = outs[: len(out_shape)], outs[len(out_shape) :], []
    for j in jobs:
        given.append(rest[: len(j.outs)])
        rest = rest[len(j.outs) :]
    return (own[0] if single else own), given


def full(shape):
    return pl.BlockSpec(shape, lambda *_: (0,) * len(shape))


def once(*shape):
    return pl.BlockSpec(shape, lambda *_: (0,) * len(shape), pipeline_mode=pl.Buffered(1))


def rows(block, width):
    return pl.BlockSpec((block, width), lambda i: (i, 0))


def arrivals(src, dst, tsems, csems, locals_, pieces=1):
    x = place()[3]
    n = LB // pieces
    moves = []
    for k in range(pieces):
        rows_ = pl.ds(n * k, n)
        here = [dst.at[pl.ds(LB * j + n * k, n)] for j in range(4)]
        moves.append((
            remote(src.at[x, rows_], here[0], tsems, 2 * k, "t0"),
            pltpu.make_async_copy(src.at[x, rows_], here[0], locals_.at[k]),
            remote(src.at[1 - x, rows_], here[1], tsems, 2 * k + 1, "t1"),
            [remote(here[j], here[2 + j], csems, 2 * k + j, "c") for j in range(2)],
        ))
    return moves


def leave(first, stay, second, onward):
    _, c, y, _ = place()
    pl.when(c != y)(first.start)
    pl.when(c == y)(stay.start)
    second.start()


def pass_on(first, stay, second, onward):
    _, c, y, _ = place()
    pl.when(c != y)(first.wait_recv)
    pl.when(c == y)(stay.wait)
    onward[0].start()
    second.wait_recv()
    onward[1].start()


def settle(first, stay, second, onward):
    _, c, y, _ = place()
    pl.when(c != y)(first.wait_send)
    second.wait_send()
    for copy in onward:
        copy.wait_send()


def column(n):
    return lax.broadcasted_iota(jnp.int32, (n, 1), 0)


def front_kernel(tokens, timesteps, bucket_ids, skips, ada_w, ada_b, head_masks, channel_masks, w_qkv, w_fc1,
                 q_bias, v_bias, b1, freq, tok_o, shifted_o, qkv_o, wq_o, w1_o, mod_o, kept_o, hmask_o, chan_o, b1_o,
                 tk, wqv, wqc, w1v, w1c, adav, ints, ints_other, m4, to_send, shares, shv, qkvv, csems, tsems, ssems, lsems, ready):
    z, c, y, x = place()
    t = 2 * y + x
    loads = [
        pltpu.make_async_copy(a, b, lsems.at[k])
        for k, (a, b) in enumerate(((ada_w, adav), (w_qkv, wqv), (w_fc1, w1v)))
    ]

    pieces = 2
    tok_moves = arrivals(tokens, tk, tsems, csems, lsems.at[pl.ds(6, pieces)], pieces)
    for load in loads:
        load.start()
    ready()
    leave(*tok_moves[0])
    halves = [skips[:, :LANES], skips[:, LANES:]]
    ints[0:4, :] = jnp.concatenate([halves[0][0:1], halves[1][0:1], halves[0][1:2], halves[1][1:2]], axis=0)
    for k, value in enumerate((timesteps[0], timesteps[1], bucket_ids[0], 0)):
        ints[4 + k : 5 + k, :] = jnp.full((1, LANES), value, jnp.int32)
    swap = remote(ints, ints_other, csems, 2 * pieces, "c")
    swap.start()

    loads[1].wait()
    for core in range(2):

        @pl.when(c == core)
        def _():
            for odd in range(2):
                for k in range(12):
                    to, start = WQ * odd + HD * k, DZ * k + DC * core + HD * odd
                    wqc[:, to : to + HD] = wqv[:, start : start + HD]

    swap.wait()

    mine, other = ints[...], ints_other[...]
    r = column(8)
    steps = jnp.zeros((8, 1), f32)
    for k in range(2):
        steps = jnp.where(r == 2 * c + k, mine[4 + k : 5 + k, 0:1].astype(f32), steps)
        steps = jnp.where(r == 2 * (1 - c) + k, other[4 + k : 5 + k, 0:1].astype(f32), steps)
    angles = steps * freq[...]
    condition = jax.nn.silu(jnp.concatenate([jnp.cos(angles), jnp.sin(angles)], axis=1))
    condition = jnp.concatenate([condition, jnp.zeros_like(condition)], axis=0).astype(bf16)
    loads[0].wait()
    m4[...] = dot_nt(condition, adav[...])[:8] + ada_b[...].astype(f32).reshape(1, -1)
    moves = []
    for k in range(4):
        to = (y + k // 2) % 2 * 2 + (x + k) % 2
        row = jnp.broadcast_to(m4[pl.ds(to, 1), :], to_send.shape[1:])
        if k == 0:
            shares[t] = row
        else:
            to_send[k - 1] = row
            moves.append(remote(to_send.at[k - 1], shares.at[t], ssems, k - 1, ("x", "y", "xy")[k - 1]))
            moves[-1].start()

    leave(*tok_moves[1])

    group = jnp.where(c == y, mine, other)
    bucket = group[6:7, 0:1]
    skip = jnp.where(x == 0, group[0:2], group[2:4])
    for j in range(4):
        block = 2 * ((c + j // 2) % 2) + (x + j) % 2
        position = column(LB) + LB * block
        hit = jnp.where((position == skip[0:1, :]) | (position == skip[1:2, :]), 1.0, 0.0)
        kept_o[LB * j : LB * (j + 1), :] = 1.0 - jnp.max(hit, axis=1, keepdims=True)

    def chosen(masks):
        line = lax.broadcasted_iota(jnp.int32, masks.shape, 0)
        row = jnp.sum(jnp.where(line == bucket, masks[...].astype(f32), 0.0), axis=0, keepdims=True)
        return jnp.broadcast_to(row, (16, masks.shape[1])).astype(bf16)

    def spread(on, low, width):
        first = width * lax.broadcasted_iota(jnp.int32, (on.shape[1], low.shape[1]), 0)
        return dot_nn(on, jnp.where((low >= first) & (low < first + width), 1.0, 0.0).astype(bf16))[0:1, :]

    lane = lax.broadcasted_iota(jnp.int32, (1, WC), 1)
    share = sum(jnp.where(lane >= DC * k, 1, 0) for k in range(1, 4))
    hmask_o[...] = spread(chosen(head_masks), lane + DC * (share + c), HD)
    channels = chosen(channel_masks)
    lane = lax.broadcasted_iota(jnp.int32, (1, FB), 1)
    share = sum(jnp.where(lane >= FZ * k, 1, 0) for k in range(1, 4))
    for f in range(NF):
        low = lane + (4 * DZ - FZ) * share + FF // 8 * c + FZ * f
        chan_o[f] = spread(channels, low, FF // channels.shape[1])

    def half(v, k, width):
        v = v[:, 2 * width * k : 2 * width * (k + 1)]
        return jnp.where(c == 0, v[:, :width], v[:, width:])

    def line(ref):
        return ref[...].astype(f32).reshape(1, -1)

    def parity(v, odd):
        return [half(v, k, DC)[:, HD * odd : HD * (odd + 1)] for k in range(4)]

    bias = []
    for odd in range(2):
        bias += parity(line(q_bias), odd) + [jnp.zeros((1, DZ), f32)] + parity(line(v_bias), odd)
    bias = jnp.concatenate(bias, axis=1)
    b1v = [half(line(b1), k, FF // 8) for k in range(4)]
    for f in range(NF):
        b1_o[f] = jnp.concatenate([v[:, FZ * f : FZ * (f + 1)] for v in b1v], axis=1)
    loads[2].wait()
    for core in range(2):

        @pl.when(c == core)
        def _():
            for f in range(NF):
                for k in range(4):
                    start = 4 * DZ * k + FF // 8 * core + FZ * f
                    w1c[f, :, FZ * k : FZ * (k + 1)] = w1v[:, start : start + FZ]

    stores = [
        pltpu.make_async_copy(a, b, lsems.at[k]) for k, (a, b) in enumerate(((wqc, wq_o), (w1c, w1_o)))
    ]
    for store in stores:
        store.start()
    for copy in moves:
        copy.wait()
    share_rows = [shares[k][0:1, :] for k in range(4)]
    n, m = D // 2, 3 * D // 2
    mod = [share_rows[0][:, :D], jnp.concatenate([share_rows[0][:, D:], share_rows[1][:, :n]], axis=1),
           share_rows[1][:, n:], share_rows[2][:, :D],
           jnp.concatenate([share_rows[2][:, D:], share_rows[3][:, :n]], axis=1), share_rows[3][:, n:]]
    own_step = 0.5 * jnp.sum(jnp.where(r == t, steps, 0.0), axis=0, keepdims=True)
    mod += [jnp.broadcast_to(own_step, (1, D)), jnp.zeros((1, D), f32)]
    mod_o[...] = jnp.concatenate(mod, axis=0)
    n = LB // pieces

    def make(side, k):
        parts = [slice(LH * side + LB * j + n * k, LH * side + LB * j + n * (k + 1)) for j in range(2)]
        normed, _ = normalize(jnp.concatenate([tk[part, :] for part in parts], axis=0).astype(f32))
        shifted = (normed * (1.0 + mod[1]) + mod[0]).astype(bf16)
        made = (dot_nn(shifted, wqc[...]) + bias).astype(bf16)
        for j, part in enumerate(parts):
            shv[part, :] = shifted[n * j : n * (j + 1)]
            qkvv[part, :] = made[n * j : n * (j + 1)]

    kept_rows = []

    def keep_half(side):
        part = pl.ds(LH * side, LH)
        for k, (a, b) in enumerate(((shv, shifted_o), (qkvv, qkv_o), (tk, tok_o))):
            copy = pltpu.make_async_copy(a.at[part], b.at[part], ssems.at[side, 3 + k])
            copy.start()
            kept_rows.append(copy)

    pass_on(*tok_moves[0])
    make(0, 0)
    pass_on(*tok_moves[1])
    for side, k in ((1, 0), (0, 1), (1, 1)):
        if side == 1:
            for copy in tok_moves[k][3]:
                copy.wait_recv()
        make(side, k)
        if k == 1:
            keep_half(side)
    for one in tok_moves:
        settle(*one)
    for copy in stores + kept_rows:
        copy.wait()


def attn_kernel(step, cotangent, qkv, hmask, wp, bias, tok, mod, cot_o, mixed_o, shifted2_o, attn_o,
                ck, qkvv, qh, kh, vh, mx, mo, wpv, tkv, sh2v, attnv, csems, tsems, osems, lsems, ssems, ready):
    c = place()[1]
    loads = [
        pltpu.make_async_copy(wp.at[:, c], wpv.at[0], lsems.at[0]),
        pltpu.make_async_copy(wp.at[:, 1 - c], wpv.at[1], lsems.at[1]),
        pltpu.make_async_copy(tok, tkv, lsems.at[2]),
        pltpu.make_async_copy(qkv, qkvv, lsems.at[4]),
    ]
    for load in loads[::-1]:
        load.start()
    cot_moves = arrivals(cotangent, ck, tsems, osems, lsems.at[pl.ds(5, 1)])[0]
    scale = LOG2E / math.sqrt(HD)
    loads.pop().wait()
    for h in range(HC):
        for k, ref in enumerate((qh, kh, vh)):
            start = WQ * (h % 2) + DZ * k + HD * (h // 2)
            ref[h, :, :HD] = qkvv[:, start : start + HD]
        vh[h, :, HD:] = jnp.ones((L, LANES - HD), bf16)
    ready()
    leave(*cot_moves)

    def crossing(i):
        src = mx.at[pl.ds(pl.multiple_of(i * step, step), step)]
        dst = mo.at[pl.ds(pl.multiple_of((i * step + LH) % L, step), step)]
        return remote(src, dst, csems, i, "c")

    def body(i, carry):
        part = pl.ds(pl.multiple_of(i * step, step), step)
        outs = []
        for h in range(HC):
            s = dot_nt(qh[h, part, :], kh[h])
            top = jnp.max(s, axis=1, keepdims=True)
            p = jnp.exp2((s - top) * scale)
            o = dot_nn(p.astype(bf16), vh[h])
            outs.append(o[:, :HD] * (1.0 / o[:, HD : HD + 1]))
        mx[part, :] = (jnp.concatenate(outs, axis=1) * hmask[...]).astype(bf16)
        crossing(i).start()
        return carry

    lax.fori_loop(0, L // step, body, 0)
    keep = pltpu.make_async_copy(mx, mixed_o, lsems.at[3])
    keep.start()
    pass_on(*cot_moves)
    for load in loads:
        load.wait()
    for i in range(L // step):
        crossing(i).wait()
    w_mine, w_other = wpv[0].reshape(WC, D), wpv[1].reshape(WC, D)
    bias_line = bias[...].astype(f32).reshape(1, D)
    stores = []
    for j in range(4):
        part = slice(LB * j, LB * (j + 1))
        attn = dot_nn(mx[part, :], w_mine) + dot_nn(mo[part, :], w_other) + bias_line
        if j < 2:
            attnv[part, :] = attn
        normed, _ = normalize(tkv[part, :].astype(f32) + mod[2:3, :] * attn)
        sh2v[part, :] = (normed * (1.0 + mod[4:5, :]) + mod[3:4, :]).astype(bf16)
        made = [(sh2v, shifted2_o)] + [(attnv, attn_o)] * (j < 2)
        for k, (a, b) in enumerate(made):
            stores.append(pltpu.make_async_copy(a.at[pl.ds(LB * j, LB)], b.at[pl.ds(LB * j, LB)], ssems.at[k, j]))
            stores[-1].start()
    for copy in cot_moves[3]:
        copy.wait_recv()
    keep_cot = pltpu.make_async_copy(ck, cot_o, lsems.at[6])
    keep_cot.start()
    settle(*cot_moves)
    for copy in stores + [keep, keep_cot]:
        copy.wait()


def mlp_kernel(sh2, g, kept, mod, w1, b1, chan, w2,
               on_a0, q_a0, on_b0, q_b0, keep_a0, keep_b0, keep_c0, send_c0,
               on_a1, q_a1, on_b1, q_b1, keep_a1, keep_b1, keep_c1, send_c1,
               k2a, s2a, k2b, s2b, c2, branch_o, ds2_o, branch_r, ds2_r, sum1_o, sum2_o,
               sh2v, dbs, w1v, w2v, hid, dpre, slope, br, ds, far, near, tt_, ka, sa, kb, sb, cz, cr, ra, rb, ona, onb,
               fsems, csems, lsems, wsems, osems, ready):
    z, c, y, x = place()
    out0 = (on_a0, q_a0, on_b0, q_b0, keep_a0, keep_b0, keep_c0, send_c0)
    out1 = (on_a1, q_a1, on_b1, q_b1, keep_a1, keep_b1, keep_c1, send_c1)
    outs = (out0, out1)

    def weights(f):
        return [
            pltpu.make_async_copy(w1.at[f], w1v.at[f % 2], wsems.at[0, f % 2]),
            pltpu.make_async_copy(w2.at[:, c, f], w2v.at[f % 2], wsems.at[1, f % 2]),
        ]

    def first(f):
        k, out = f % 2, outs[f]
        return [
            remote(sa.at[k, 1], ra.at[k], fsems, 10 * k, "x"), remote(sb.at[k, 1], rb.at[k], fsems, 10 * k + 1, "y"),
            remote(sa.at[k, 0], out[1], fsems, 10 * k + 2, "x"), remote(sb.at[k, 0], out[3], fsems, 10 * k + 3, "y"),
        ] + [
            remote(cz.at[k, j, :, :, pl.ds(GC * half, GC)], cr.at[k, j - 1, :, :, pl.ds(GC * half, GC)], fsems,
                   10 * k + 3 + 3 * half + j, f"z{j}")
            for half in range(2) for j in (3, 2, 1)
        ]

    def stored(f):
        k = f % 2
        if f == NF - 1:
            pairs = ((ka.at[k], k2a), (sa.at[k], s2a), (kb.at[k], k2b), (sb.at[k], s2b), (cz.at[k], c2))
        else:
            pairs = ((ka.at[k, 0], outs[f][4]), (kb.at[k, 0], outs[f][5]))
        return [pltpu.make_async_copy(src, dst, osems.at[k, j]) for j, (src, dst) in enumerate(pairs)]

    def onward(f):
        k = f % 2
        for copy in first(f):
            copy.wait()
        for kv, rv, on in ((ka, ra, ona), (kb, rb, onb)):
            on[k] = total_of(kv[k, 1], rv[k]).astype(bf16)
        cz[k, 0] = total_of(cz[k, 0], cr[k, 0], cr[k, 1], cr[k, 2]).astype(bf16)
        pairs = (
            (ona.at[k], outs[f][0]), (onb.at[k], outs[f][2]), (cz.at[k, 0, 0], outs[f][6]), (cz.at[k, 0, 1], outs[f][7])
        )
        copies = [pltpu.make_async_copy(src, dst, osems.at[k, 5 + j]) for j, (src, dst) in enumerate(pairs)]
        for copy in copies:
            copy.start()
        return copies

    loads = [pltpu.make_async_copy(src, dst, lsems.at[k]) for k, (src, dst) in enumerate(((g, dbs), (sh2, sh2v)))]
    for copy in loads + weights(0):
        copy.start()
    loads[0].wait()
    sum2 = jnp.zeros((1, D), f32)
    for j in range(4):
        part = slice(LB * j, LB * (j + 1))
        db = (dbs[part, :].astype(f32) * mod[5:6, :] * kept[part, :]).astype(bf16)
        dbs[part, :] = db
        sum2 += jnp.sum(db.astype(f32), axis=0, keepdims=True)
    sum2_o[...] = sum2
    loads[1].wait()
    crossing = [remote(far.at[j], dst, csems, j, "c") for j, dst in enumerate((branch_r, ds2_r))]
    waiting = []
    for f in range(NF):
        for copy in weights(f):
            copy.wait()
        if f + 1 < NF:
            for copy in weights(f + 1):
                copy.start()
        w1f, w2f = w1v[f % 2], w2v[f % 2].reshape(FB, D)
        on = chan[f]
        k = f % 2
        for side in (1, 0):
            part = slice(LH * side, LH * (side + 1))
            v = dot_nn(sh2v[part, :], w1f) + b1[f]
            v2 = v * v
            th = jnp.tanh(GELU_K * v * (1.0 + GELU_C * v2))
            half = 0.5 * (1.0 + th)
            hid[part, :] = (v * half * on).astype(bf16)
            slope[part, :] = (
                (half + (0.5 * GELU_K) * v * (1.0 - th * th) * (1.0 + (3.0 * GELU_C) * v2)) * on
            ).astype(bf16)
        p = dot_tn(hid[...], dbs[...]).astype(bf16)
        for t in range(4):
            tt_[t, :FB, :] = p[:, TD * t : TD * (t + 1)]
        if f == 0:
            ready()
        for ry, rx in ((1, 1), (1, 0), (0, 1), (0, 0)):
            for rz in range(4):
                zz = flip(z, rz)
                if True:
                    tt = (ry + y) % 2 * 2 + (rx + x) % 2
                    o = (kb, sb)[ry]
                    block = tt_[tt, pl.ds(pl.multiple_of(zz * FZ, 16), FZ), :]
                    o[k, rx, rz, :FZ, :] = block[:, :LANES]
                    o[k, rx, rz, FZ:, :] = block[: GB - FZ, LANES : 2 * LANES]
                    q = FZ // 4
                    cz[k, rz, rx, ry, GC : GC + 2 * FZ - GB, :] = block[GB - FZ :, LANES : 2 * LANES]
                    cz[k, rz, rx, ry, GC + 2 * FZ - GB :, :] = jnp.concatenate(
                        [block[q * j : q * (j + 1), 2 * LANES :] for j in range(4)], axis=1
                    )
            if f < NF - 1 and ry == 1:
                first(f)[1 if rx == 1 else 3].start()
        if f < NF - 1:
            for copy in first(f)[7:]:
                copy.start()
        sum1 = jnp.zeros((1, FB), f32)
        for side in (1, 0):
            part = slice(LH * side, LH * (side + 1))
            d_pre = (dot_nt(dbs[part, :], w2f) * slope[part, :].astype(f32)).astype(bf16)
            dpre[part, :] = d_pre
            sum1 += jnp.sum(d_pre.astype(f32), axis=0, keepdims=True)
        sum1_o[f] = sum1
        p = dot_tn(sh2v[...], dpre[...]).astype(bf16)
        for t in range(4):
            tt_[t, :, :FZ] = p[:, FZ * t : FZ * (t + 1)]
        for ry, rx in ((1, 1), (0, 1), (1, 0), (0, 0)):
            for rz in range(4):
                zz = flip(z, rz)
                if True:
                    tt = (ry + y) % 2 * 2 + (rx + x) % 2
                    o = (ka, sa)[rx]
                    tails = []
                    for rc in range(2):
                        block = tt_[tt, pl.ds(pl.multiple_of(zz * DZ + (rc + c) % 2 * DC, 16), DC), :FZ]
                        o[k, ry, rz, DC * rc : DC * (rc + 1), :] = block[:, :LANES]
                        tails.append(block[:, LANES:])
                    tail = jnp.concatenate(tails, axis=1)
                    o[k, ry, rz, 2 * DC :, :] = tail[: GA - 2 * DC]
                    cz[k, rz, rx, ry, :GC, :] = tail[GA - 2 * DC :]
            if f < NF - 1 and rx == 1:
                first(f)[0 if ry == 1 else 2].start()
        if f < NF - 1:
            for copy in first(f)[4:7]:
                copy.start()
        for copy in stored(f):
            copy.start()
        for side in (1, 0):
            part = slice(LH * side, LH * (side + 1))
            branch, ds2 = dot_nn(hid[part, :], w2f), dot_nt(dpre[part, :], w1f)
            if f > 0:
                branch, ds2 = branch + br[part, :], ds2 + ds[part, :]
            if f < NF - 1:
                br[part, :] = branch
                ds[part, :] = ds2
            elif side == 1:
                far[0] = branch.astype(bf16)
                far[1] = ds2.astype(bf16)
                for copy in crossing:
                    copy.start()
            else:
                near[0] = branch.astype(bf16)
                near[1] = ds2.astype(bf16)
                waiting += upto([near.at[0], near.at[1]], [branch_o, ds2_o], lsems)
                for copy in waiting[-2:]:
                    copy.start()
        waiting += stored(f)
        if f > 0:
            waiting += onward(f - 1)
        if f == NF - 2:
            for copy in waiting:
                copy.wait()
            waiting = []
    for copy in waiting + crossing:
        copy.wait()


def middle_kernel(ds, ds_r, br, br_r, attn, tok, g, kept, mod, bias2, mixed, wp,
                  d_resid_out, out_out, dh_out, pka_out, psa_out, pkb_out, psb_out, sums_o, sum_o,
                  d_resid_o, out_o, dh_o, pka, psa, pkb, psb, dsv, attnv, tokv, mixv, wpv, da, t1, csems, lsems, bsems, ssems, ready):
    z, c, y, x = place()
    n = LH // 4
    pairs = ((tok, tokv.at[0]), (attn, attnv), (ds, dsv.at[0]), (ds_r, dsv.at[1]), (br, dsv.at[2]), (br_r, dsv.at[3]),
             (g, tokv.at[1]))
    blocks = [
        [
            pltpu.make_async_copy(src.at[pl.ds(n * k, n)], dst.at[pl.ds(n * k, n)], bsems.at[k, j])
            for j, (src, dst) in enumerate(pairs)
        ]
        for k in range(4)
    ]
    loads = [pltpu.make_async_copy(src, dst, lsems.at[k]) for k, (src, dst) in enumerate(((wp.at[:, c], wpv), (mixed, mixv)))]
    for load in sum(blocks, []) + loads:
        load.start()
    ready()
    crossing = [remote(da.at[pl.ds(n * k, n)], da.at[pl.ds(LH + n * k, n)], csems, k, "c") for k in range(4)]
    sums = jnp.zeros((4, D), f32)
    bias_line = bias2[...].astype(f32).reshape(1, D)
    for k in range(4):
        for load in blocks[k]:
            load.wait()
        part = slice(n * k, n * (k + 1))
        gf, at = tokv[1, part, :].astype(f32), attnv[part, :]
        resid = tokv[0, part, :].astype(f32) + mod[2:3, :] * at
        normed2, inverse2 = normalize(resid)
        ds2 = dsv[0, part, :].astype(f32) + dsv[1, part, :].astype(f32)
        kb = kept[part, :] * (dsv[2, part, :].astype(f32) + dsv[3, part, :].astype(f32) + bias_line)
        out_o[part, :] = (resid + mod[5:6, :] * kb).astype(bf16)
        d_resid = gf + normalize_back(ds2 * (1.0 + mod[4:5, :]), normed2, inverse2)
        d_resid_o[part, :] = d_resid
        da[part, :] = (mod[2:3, :] * d_resid).astype(bf16)
        crossing[k].start()
        sums += jnp.concatenate(
            [jnp.sum(p, axis=0, keepdims=True) for p in (at * d_resid, ds2, ds2 * normed2, kb * gf)], axis=0
        )
    sums_o[...] = jnp.concatenate([sums, jnp.zeros((4, D), f32)], axis=0)
    for load in loads:
        load.wait()
    for copy in crossing:
        copy.wait()
    wv = wpv[...].reshape(WC, D)
    dh_o[...] = dot_nt(da[...], wv).astype(bf16)
    stores = upto(
        [d_resid_o, out_o, dh_o, pka, psa, pkb, psb],
        [d_resid_out, out_out, dh_out, pka_out, psa_out, pkb_out, psb_out], ssems,
    )
    for copy in stores[:3]:
        copy.start()
    sum_o[...] = dot_nn(jnp.ones((16, L), bf16), da[...])[:8]
    grad = dot_tn(mixv[...], da[...]).astype(bf16)
    for t in range(4):
        t1[t] = grad[:, TD * t : TD * (t + 1)]
    for rz in range(4):
        zz = flip(z, rz)
        for ry in range(2):
            for rx in range(2):
                tt = (ry + y) % 2 * 2 + (rx + x) % 2
                a, b = (pka, psa)[rx], (pkb, psb)[ry]
                block = t1[tt, pl.ds(pl.multiple_of(zz * DC, 16), DC), :]
                a[ry, rz, :DC, :] = block[:, :LANES]
                a[ry, rz, DC:, :] = block[: PA - DC, LANES : 2 * LANES]
                b[rx, rz, : 2 * DC - PA, :] = block[PA - DC :, LANES : 2 * LANES]
                q = DC // 3
                tails = [block[q * k : q * (k + 1), 2 * LANES :] for k in range(3)]
                tails.append(jnp.zeros((q, 32), bf16))
                b[rx, rz, 2 * DC - PA :, :] = jnp.concatenate(tails, axis=1)
    for copy in stores[3:]:
        copy.start()
    for copy in stores:
        copy.wait()


def qkv_slots(grad, extra, t1, ka, sa, kb, sb, copies):
    z, _, y, x = place()
    for t in range(4):
        for zz in range(4):
            t1[t, zz] = grad[TQ * t : TQ * (t + 1), DZ * zz : DZ * (zz + 1)]
    q = TQ // 3
    for ry, rx, ready_now in ((1, 1, copies[:2]), (0, 1, copies[2:3]), (1, 0, copies[3:]), (0, 0, ())):
        tt = (ry + y) % 2 * 2 + (rx + x) % 2
        for rz in range(4):
            zz = flip(z, rz)
            block = t1[tt, zz]
            tails = [block[q * k : q * (k + 1), 2 * LANES :] for k in range(3)] + [jnp.zeros((q, 32), f32)]
            more = jnp.zeros((8, LANES), f32) if extra is None else extra[zz, tt]
            slot = [block[:, :LANES], block[:, LANES : 2 * LANES], jnp.concatenate(tails, axis=1), more]
            slot = jnp.concatenate(slot, axis=0).astype(bf16)
            (ka, sa)[rx][ry, rz] = slot[:QA]
            (kb, sb)[ry][rx, rz] = slot[QA:]
        for copy in ready_now:
            copy.start()


def column_sums(dqkv):
    return dot_nn(jnp.ones((16, L), bf16), dqkv)[:8]


def attn_back_kernel(step, qkv, dh, shifted, hmask, out, on_a, q_a, on_b, q_b, keep_a, keep_b, sums_o,
                     qkvv, dhv, shv, outv, qh, kh, vh, doh, dk, dv, t1, ka, sa, kb, sb, ra, rb, ona, onb,
                     fsems, lsems, ready, tick):
    loads = [
        pltpu.make_async_copy(a, b, lsems.at[k])
        for k, (a, b) in enumerate(((qkv, qkvv), (dh, dhv), (shifted, shv)))
    ]
    for load in loads:
        load.start()
    ready()
    for load in loads:
        load.wait()
    scale = LOG2E / math.sqrt(HD)
    first = [
        remote(sa.at[1], ra, fsems, 0, "x"), remote(sb.at[1], rb, fsems, 1, "y"),
        remote(sa.at[0], q_a, fsems, 2, "x"), remote(sb.at[0], q_b, fsems, 3, "y"),
    ]
    stores = [pltpu.make_async_copy(a, b, lsems.at[3 + k]) for k, (a, b) in enumerate(((ka.at[0], keep_a), (kb.at[0], keep_b)))]
    for odd in range(2):
        base = WQ * odd
        for j in range(HC // 2):
            for k, ref in enumerate((qh, kh, vh)):
                start = base + DZ * k + HD * j
                ref[j] = qkvv[:, start : start + HD]
            cut = slice(HD * (2 * j + odd), HD * (2 * j + odd + 1))
            doh[j] = (dhv[:, cut].astype(f32) * hmask[:, cut]).astype(bf16)
        dk[...] = jnp.zeros_like(dk)
        dv[...] = jnp.zeros_like(dv)

        def body(i, carry):
            part = pl.ds(pl.multiple_of(i * step, step), step)
            outs = []
            for j in range(HC // 2):
                q, do = qh[j, part, :], doh[j, part, :]
                s = dot_nt(kh[j], q)
                top = jnp.max(s, axis=0, keepdims=True)
                p = jnp.exp2((s - top) * scale)
                p = p * (1.0 / jnp.sum(p, axis=0, keepdims=True))
                dp = dot_nt(vh[j], do)
                row_dot = jnp.sum(p * dp, axis=0, keepdims=True)
                ds = (p * (dp - row_dot)).astype(bf16)
                dv[j] += dot_nn(p.astype(bf16), do)
                dk[j] += dot_nn(ds, q)
                outs.append(dot_tn(ds, kh[j]))
            outv[part, base : base + DZ] = (jnp.concatenate(outs, axis=1) * (1.0 / math.sqrt(HD))).astype(bf16)
            return carry

        half = L // step // 2
        lax.fori_loop(0, half, body, 0)
        tick(1 + 2 * odd)
        lax.fori_loop(half, 2 * half, body, 0)
        for j in range(HC // 2):
            start = base + DZ + HD * j
            outv[:, start : start + HD] = (dk[j] * (1.0 / math.sqrt(HD))).astype(bf16)
            outv[:, start + DZ : start + DZ + HD] = dv[j].astype(bf16)
        if odd == 0:
            sums_o[...] = column_sums(outv[:, :WQ])
            qkv_slots(dot_tn(outv[:, :WQ], shv[...]), None, t1, ka, sa, kb, sb, first)
            for copy in stores:
                copy.start()
            tick(2)
    keep = pltpu.make_async_copy(outv, out, lsems.at[5])
    keep.start()
    for copy in first:
        copy.wait()
    for kv, rv, on in ((ka, ra, ona), (kb, rb, onb)):
        on[...] = (kv[1].astype(f32) + rv[...].astype(f32)).astype(bf16)
    onward = [pltpu.make_async_copy(a, b, lsems.at[6 + k]) for k, (a, b) in enumerate(((ona, on_a), (onb, on_b)))]
    for copy in onward:
        copy.start()
    for copy in stores + onward + [keep]:
        copy.wait()


def end_kernel(dqkv, shifted, even_sums, sum1, sum2, sum_attn, wq, d_resid, tok, mod, sums_mid, f0, c0, f1, c1, f2, c2, sent_p, kept_p, freq,
               on_a, q_a, on_b, q_b, keep_a, keep_b,
               grad, gq_o, gp_out, g1_out, g2_out, ada_out, ada_bias_o, line_o,
               dqv, shv, extra, t1, ka, sa, kb, sb, ra, rb, ona, onb, r2a, r2b, zs, zk, zr,
               eqa, era, eka, eqb, erb, ekb, ezs, ezk, ezr, qt, wqv, dres, tokv, fv, far, got, gb,
               item, item_r, out_shares, square, every, row_out, row_in, mine, theirs, mine_q, theirs_q, pk, pr, gp_o, g1_o, g2_o, ada_o,
               qsems, esems, csems, tsems, ssems, psems, lsems, xsems, ready):
    z, c, y, x = place()
    t, b = 2 * y + x, 2 * z + c
    second_e = [remote(on_a, era, esems, 0, "y"), remote(on_b, erb, esems, 1, "x")]
    third_p = [remote(sent_p.at[k], pr.at[k], psems, k, f"z{k + 1}") for k in (2, 1, 0)]
    pairs = ((dqkv, dqv), (shifted, shv), (wq, wqv), (d_resid, dres), (tok.at[pl.ds(0, LH)], tokv),
             (keep_a, eka), (q_a, eqa), (keep_b, ekb), (q_b, eqb), (kept_p, pk))
    for f, (two, one) in enumerate(((f0, c0), (f1, c1), (f2, c2))):
        pairs += ((two.at[pl.ds(0, GA)], fv.at[f, pl.ds(0, GA)]), (one.at[pl.ds(0, GC)], fv.at[f, pl.ds(GA, GC)]),
                  (two.at[pl.ds(GA, GB)], fv.at[f, pl.ds(G1R, GB)]), (one.at[pl.ds(GC, GC)], fv.at[f, pl.ds(G1R + GB, GC)]))
    loads = [pltpu.make_async_copy(src, dst, lsems.at[k]) for k, (src, dst) in enumerate(pairs)]
    for copy in loads:
        copy.start()
    loads[0].wait()
    loads[1].wait()
    ready()
    for copy in second_e + third_p:
        copy.start()

    odd = dqv[:, WQ:]
    grad_odd = dot_tn(odd, shv[...])
    odd_sums = column_sums(odd)
    for zs_ in range(4):
        for ts in range(4):
            start, n = FF // 32 * ts, FF // 32
            pieces = []
            for f in range(NF):
                low, high = max(start, FZ * f), min(start + n, FZ * (f + 1))
                if low < high:
                    pieces.append(sum1[f][:, FZ * zs_ + low - FZ * f : FZ * zs_ + high - FZ * f])
            n = D // 32
            for total in (sum2[...], sum_attn[0:1, :]):
                at = DZ * zs_ + n * ts
                pieces.append(jnp.where(c == 0, total[:, at : at + n], total[:, at + DC : at + DC + n]))
            total = (even_sums, odd_sums)[ts // 2][0:1, :]
            at = HD * zs_ + n * (ts % 2)
            pieces += [total[:, at : at + n], total[:, 2 * DZ + at : 2 * DZ + at + n]]
            flat = jnp.concatenate(pieces + [jnp.zeros((1, 3 * LANES - DZ), f32)], axis=1)
            lines = [flat[:, LANES * k : LANES * (k + 1)] for k in range(3)] + [jnp.zeros((5, LANES), f32)]
            extra[zs_, ts] = jnp.concatenate(lines, axis=0)
    first_q = [
        remote(sa.at[1], ra.at[1], qsems, 0, "x"), remote(sb.at[1], rb.at[1], qsems, 1, "y"),
        remote(sa.at[0], ra.at[0], qsems, 2, "x"), remote(sb.at[0], rb.at[0], qsems, 3, "y"),
    ]
    qkv_slots(grad_odd, extra, t1, ka, sa, kb, sb, first_q)

    loads[2].wait()
    crossing = [remote(far.at[k], got.at[k], csems, k, "c") for k in range(2)]
    d_far = dot_nt(dqv[LH:, :], wqv[...])
    for k in range(2):
        far[k] = d_far[LB * k : LB * (k + 1)].astype(bf16)
        crossing[k].start()

    for copy in second_e:
        copy.wait()
    for k in (5, 6, 7, 8):
        loads[k].wait()
    layer_sums([(eka, eqa, era), (ekb, eqb, erb)], ezs, ezk)
    third_e = [remote(ezs.at[k], ezr.at[k], esems, 2 + k, f"z{k + 1}") for k in (2, 1, 0)]
    for copy in third_e:
        copy.start()
    d_near = dot_nt(dqv[:LH, :], wqv[...])
    loads[3].wait()
    loads[4].wait()
    token_sums = jnp.zeros((2, D), f32)
    for k in range(2):
        part = slice(LB * k, LB * (k + 1))
        crossing[k].wait()
        total = d_near[part] + got[k].astype(f32)
        normed, inverse = normalize(tokv[part, :].astype(f32))
        back = dres[part, :] + normalize_back(total * (1.0 + mod[1:2, :]), normed, inverse)
        gb[k] = back.astype(bf16)
        token_sums += jnp.concatenate(
            [jnp.sum(v, axis=0, keepdims=True) for v in (total, total * normed)], axis=0
        )
    item[...] = jnp.concatenate([token_sums, sums_mid[0:4, :], mod[6:8, :]], axis=0)
    over = remote(item, item_r, csems, 2, "c")
    over.start()

    for copy in first_q:
        copy.wait()
    for kv, rv, on in ((ka, ra, ona), (kb, rb, onb)):
        on[...] = (kv[1].astype(f32) + rv[1].astype(f32)).astype(bf16)
    second_q = [remote(ona, r2a, qsems, 4, "y"), remote(onb, r2b, qsems, 5, "x")]
    for copy in second_q:
        copy.start()
    over.wait()
    v = item[...] + item_r[...]
    n = D // 2
    stamp = v[6:7, :LANES]
    pieces = ([v[0:1], v[1:2, :n]], [v[1:2, n:], v[2:3]], [v[3:4], v[4:5, :n]], [v[4:5, n:], v[5:6]])
    for j in range(4):
        out_shares[j] = jnp.concatenate(pieces[j] + [stamp], axis=1)
    square[t] = out_shares[t]
    meeting = [
        remote(out_shares.at[(y + j // 2) % 2 * 2 + (x + j) % 2], square.at[t], ssems, j - 1, ("x", "y", "xy")[j - 1])
        for j in (1, 2, 3)
    ]
    for copy in meeting:
        copy.start()

    def first_columns(pairs, own):
        for core in range(2):

            @pl.when(c == core)
            def _():
                for f, pair in enumerate(pairs):
                    start = FF // 8 * (core if own else 1 - core) + FZ * f
                    g1_o[:, start : start + FZ] = jnp.concatenate(pair, axis=1)

    for load in loads[9:]:
        load.wait()
    for f in range(NF):
        mine[G1R * f : G1R * (f + 1), :] = fv[f, :G1R, :].astype(bf16)
    swap = remote(mine, theirs, csems, 3, "c")
    swap.start()
    first_columns([[fv[f, :DC, :], fv[f, 2 * DC : 3 * DC, : FZ - LANES]] for f in range(NF)], True)
    for copy in second_q:
        copy.wait()
    layer_sums([(ka.at[0], ra.at[0], r2a), (kb.at[0], rb.at[0], r2b)], zs, zk)
    third_q = [remote(zs.at[k], zr.at[k], qsems, 6 + k, f"z{k + 1}") for k in (2, 1, 0)]
    for copy in third_q:
        copy.start()
    home = homeward(gb.at[0], gb.at[1], grad, tsems, lsems.at[len(pairs)])
    home_start(*home)
    for copy in meeting:
        copy.wait()
    spread_z = [remote(square, every.at[z], ssems, 2 + k, f"z{k}") for k in (1, 2, 3)]
    every[z] = square[...]
    for copy in spread_z:
        copy.start()
    for f in range(NF):
        part = fv[f, G1R:, :]
        tail = part[2 * FZ :]
        tail = jnp.concatenate([tail[:, 32 * k : 32 * (k + 1)] for k in range(4)], axis=0)
        g2_o[FZ * f : FZ * (f + 1), :] = jnp.concatenate([part[:FZ], part[FZ : 2 * FZ], tail], axis=1)
    for copy in third_p:
        copy.wait()
    part = pk[...] + pr[0].astype(f32) + pr[1].astype(f32) + pr[2].astype(f32)
    tail = part[2 * DC :]
    tail = jnp.concatenate([tail[:, 32 * k : 32 * (k + 1)] for k in range(3)], axis=0)
    gp_o[...] = jnp.concatenate([part[:DC], part[DC : 2 * DC], tail], axis=1)
    swap.wait()
    first_columns(
        [
            [theirs[G1R * f + DC : G1R * f + 2 * DC, :].astype(f32),
             theirs[G1R * f + 2 * DC : G1R * (f + 1), FZ - LANES :].astype(f32)]
            for f in range(NF)
        ],
        False,
    )

    stores = upto([gp_o, g1_o, g2_o, ada_o], [gp_out, g1_out, g2_out, ada_out], xsems)
    for copy in stores[:3]:
        copy.start()

    for copy in spread_z:
        copy.wait()
    columns = jnp.concatenate([every[i, j] for i in range(4) for j in range(4)], axis=0)
    width = 3 * D // 2
    angles = columns[:, width : width + 1] * freq[b % 4]
    cond = jax.nn.silu(jnp.where(b < 4, jnp.cos(angles), jnp.sin(angles))).astype(bf16).astype(f32)
    columns = columns[:, :width]
    ada_o[...] = lax.dot_general(
        cond, columns, (((0,), (0,)), ((), ())), precision=lax.Precision.HIGHEST, preferred_element_type=f32
    )
    stores[3].start()
    row = jnp.sum(columns, axis=0, keepdims=True)
    row_out[0] = row
    row_in[t] = row
    rows_ = [remote(row_out.at[0], row_in.at[t], ssems, 6 + j, name) for j, name in enumerate(("x", "y", "xy"))]
    for copy in rows_:
        copy.start()

    for odd_, (copies, kept, more) in enumerate(((third_e, ezk, ezr), (third_q, zk, zr))):
        for copy in copies:
            copy.wait()
        q = total_of(kept[...], more[0], more[1], more[2])
        tail = q[2 * TQ :]
        n = TQ // 3
        tail = jnp.concatenate([tail[n * 0 : n, 32 * k : 32 * (k + 1)] for k in range(3)], axis=0)
        qt[odd_] = jnp.transpose(jnp.concatenate([q[:TQ], q[TQ : 2 * TQ], tail], axis=1))
        mine_q[odd_] = qt[odd_, pl.ds(pl.multiple_of(DC * (1 - c), 16), DC), :].astype(bf16)
        swap = remote(mine_q.at[odd_], theirs_q.at[odd_], csems, 4 + odd_, "c")
        swap.start()
        if odd_ == 1:
            line_o[...] = q[QR - 8 :]
    own = [qt[odd_, pl.ds(pl.multiple_of(DC * c, 16), DC), :] for odd_ in range(2)]

    def qkv_columns(values, owned):
        for core in range(2):

            @pl.when(c == core)
            def _():
                for odd_ in range(2):
                    for j in range(3):
                        start = DZ * j + DC * (core if owned else 1 - core) + HD * odd_
                        gq_o[:, start : start + HD] = values[odd_][:, HD * j : HD * (j + 1)]

    qkv_columns(own, True)
    for odd_ in range(2):
        remote(mine_q.at[odd_], theirs_q.at[odd_], csems, 4 + odd_, "c").wait()
    qkv_columns([theirs_q[odd_].astype(f32) for odd_ in range(2)], False)
    for copy in rows_:
        copy.wait()
    row = row_in[z]
    ada_bias_o[...] = jnp.where(c == 0, row[:, : width // 2], row[:, width // 2 :])
    home_wait(*home)
    for copy in stores:
        copy.wait()


def final_kernel(out_rows, grad_rows, gq, gp, g1, g2, ada, ada_bias, line,
                 out, grad, gq_o, gp_o, g1_o, g2_o, ada_o, ada_bias_o, b_fc1, b_fc2, b_proj, b_q, b_v):
    out[...] = out_rows[...]
    grad[...] = grad_rows[...].astype(f32)
    gq_o[...] = gq[...]
    gp_o[...] = gp[...]
    g1_o[...] = g1[...]
    g2_o[...] = jnp.transpose(g2[...])
    ada_o[...] = ada[...]
    ada_bias_o[...] = ada_bias[...].reshape(-1)
    flat = jnp.concatenate([line[k : k + 1, :] for k in range(3)], axis=1)
    n1, n = FF // 32, D // 32
    b_fc1[...] = flat[:, :n1].reshape(-1)
    for k, ref in enumerate((b_fc2, b_proj, b_q, b_v)):
        ref[...] = flat[:, n1 + n * k : n1 + n * (k + 1)].reshape(-1)


def one_item_per_chip(
    tokens, cotangent, timesteps, bucket_ids, head_masks, channel_masks, skip_rows,
    w_qkv, q_bias, v_bias, w_proj, proj_bias, w_fc1, fc1_bias, w_fc2, fc2_bias, ada_weight, ada_bias,
):
    b, t = lax.axis_index("bucket"), lax.axis_index("tok")
    z, c, y, x = b // 2, b % 2, t // 2, t % 2

    def core_half(v, *dims):
        return lax.dynamic_index_in_dim(v.reshape(dims), c, 1, keepdims=False)

    vmem, smem = pl.BlockSpec(memory_space=pltpu.VMEM), pl.BlockSpec(memory_space=pltpu.SMEM)
    steps = -np.float32(math.log(10000.0)) * np.arange(D // 2, dtype=np.float32) / np.float32(D // 2)
    freq = jnp.asarray(np.exp(steps).reshape(1, D // 2))
    ada_cols = ada_weight.shape[1]
    front, _ = call(
        front_kernel, "front",
        (sds((L, D), bf16), sds((L, D), bf16), sds((L, 3 * WC), bf16), sds((D, 3 * WC), bf16), sds((NF, D, FB), bf16), sds((8, D), f32), sds((L, 1), f32), sds((1, WC), f32), sds((NF, 1, FB), f32),
         sds((NF, 1, FB), f32)),
        (tokens, timesteps, bucket_ids, skip_rows, ada_weight.T, ada_bias, head_masks, channel_masks,
         w_qkv, w_fc1, q_bias, v_bias, fc1_bias, freq),
        in_specs=[ANY, smem, smem, vmem, ANY, vmem, vmem, vmem, ANY, ANY, vmem, vmem, vmem, vmem],
        out_specs=[ANY] * 5 + [vmem] * 5,
        scratch=[vm(L, D), vm(D, 3 * D), vm(D, 3 * WC), vm(D, FF), vm(NF, D, FB), vm(ada_cols, D),
                 vm(8, LANES, dtype=jnp.int32), vm(8, LANES, dtype=jnp.int32), vm(8, ada_cols, dtype=f32), vm(3, 8, ada_cols, dtype=f32),
                 vm(4, 8, ada_cols, dtype=f32), vm(L, D), vm(L, 3 * WC), pltpu.SemaphoreType.DMA((2, 5)),
                 pltpu.SemaphoreType.DMA((2, 4)), pltpu.SemaphoreType.DMA((2, 6)), pltpu.SemaphoreType.DMA((8,))],
        peers=("c", "t0", "t1", "x", "y", "xy"), cid=10, flops=2 * L * D * 3 * WC, nbytes=50e6,
    )
    tok, shifted, qkv, wq, w1, mod, kept, hmask, chan, b1 = front
    w2 = w_fc2.reshape(4, 2, NF, FZ, D)
    wp = w_proj.reshape(4, 2, DC, D)
    (g_all, mixed, shifted2, attn), _ = call(
        functools.partial(attn_kernel, 512), "attn",
        (sds((L, D), bf16), sds((L, WC), bf16), sds((L, D), bf16), sds((LH, D), f32)),
        (cotangent, qkv, hmask, wp, proj_bias, tok, mod),
        in_specs=[ANY, ANY, vmem, ANY, vmem, ANY, vmem],
        out_specs=[ANY] * 4,
        scratch=[vm(L, D), vm(L, 3 * WC)] + [vm(HC, L, HD)] * 2 + [vm(HC, L, LANES)] + [vm(L, WC), vm(L, WC), vm(2, 4, DC, D), vm(L, D), vm(L, D),
                 vm(LH, D, dtype=f32),
                 pltpu.SemaphoreType.DMA((2, 4)), pltpu.SemaphoreType.DMA((2, 2)), pltpu.SemaphoreType.DMA((2, 2)),
                 pltpu.SemaphoreType.DMA((7,)), dma(2, 4)],
        peers=("c", "t0", "t1"), cid=11, flops=16e9, nbytes=5e6,
    )

    slot1, slot2, slot3 = sds((2, 4, GA, LANES)), sds((2, 4, GB, LANES)), sds((4, 2, 2, 2 * GC, LANES))
    part1, part2, part3 = sds(slot1.shape[1:]), sds(slot2.shape[1:]), sds(slot3.shape[2:])
    one = [part1, part1, part2, part2, part1, part2, part3, part3]
    rows_half = sds((LH, D), bf16)
    own, _ = call(
        mlp_kernel, "mlp",
        one + one + [slot1, slot1, slot2, slot2, slot3] + [rows_half] * 4 + [sds((NF, 1, FB), f32), sds((1, D), f32)],
        (shifted2, g_all, kept, mod, w1, b1, chan, w2),
        in_specs=[ANY, ANY, vmem, vmem, ANY, vmem, vmem, ANY],
        out_specs=[ANY] * 25 + [vmem, vmem],
        scratch=[vm(L, D), vm(L, D), vm(2, D, FB), vm(2, 4, FZ, D), vm(L, FB), vm(L, FB),
                 vm(L, FB), vm(L, D, dtype=f32), vm(L, D, dtype=f32), vm(2, LH, D), vm(2, LH, D), vm(4, D, TD)]
        + [vm(2, *slot1.shape)] * 2 + [vm(2, *slot2.shape)] * 2 + [vm(2, *slot3.shape), vm(2, 3, *slot3.shape[1:])]
        + [vm(2, *p.shape) for p in (part1, part2)] * 2
        + [dma(2, 20), dma(2, 2), dma(2), dma(2, 2), dma(2, 9)],
        peers=("c", "x", "y", "z1", "z2", "z3"), cid=0,
        flops=36 * L * D * FB, nbytes=40e6,
    )
    second0, second1, slots = own[:8], own[8:16], own[16:21]
    branch, ds2, branch_r, ds2_r, sum1, sum2 = own[21:]

    slot_a, slot_b = sds((2, 4, PA, LANES), bf16), sds((2, 4, PR - PA, LANES), bf16)
    own, given = call(
        middle_kernel, "middle",
        (sds((LH, D), f32), rows_half, sds((L, WC), bf16), slot_a, slot_a, slot_b, slot_b, sds((8, D), f32),
         sds((8, D), f32)),
        (ds2, ds2_r, branch, branch_r, attn, tok, g_all, kept, mod, fc2_bias, mixed, wp),
        in_specs=[ANY] * 7 + [vmem] * 3 + [ANY] * 2,
        out_specs=[ANY] * 7 + [vmem] * 2,
        scratch=[vm(LH, D, dtype=f32), vm(LH, D), vm(L, WC)] + [vm(*v.shape) for v in (slot_a, slot_a, slot_b, slot_b)]
        + [vm(4, LH, D), vm(LH, D, dtype=f32), vm(2, LH, D), vm(L, WC), vm(4, DC, D), vm(L, D), vm(4, WC, TD),
                 dma(2, 4), dma(2), dma(4, 7), dma(7)],
        peers=("c",), cid=3, jobs=[FirstSum(*slots), SecondSum(*second0)],
        flops=4 * L * D * WC, nbytes=20e6,
    )
    d_resid, out_rows, dh, *slots_p, sums_mid, sum_attn = own
    first2, result0 = given
    slot_q = vm(2, 4, QA, LANES)
    fourth = vm(4, QA, LANES)
    part_q = sds((4, QA, LANES), bf16)
    own, given = call(
        functools.partial(attn_back_kernel, 512), "attn_back",
        [sds((L, 3 * WC), bf16)] + [part_q] * 6 + [sds((8, WQ), f32)], (qkv, dh, shifted, hmask),
        in_specs=[ANY] * 3 + [vmem],
        out_specs=[ANY] * 7 + [vmem],
        scratch=[vm(L, 3 * WC), vm(L, WC), vm(L, D), vm(L, 3 * WC)] + [vm(HC // 2, L, HD)] * 4
        + [vm(HC // 2, L, HD, dtype=f32)] * 2 + [vm(4, 4, TQ, DZ, dtype=f32)] + [slot_q] * 4 + [fourth] * 4
        + [dma(2, 4), dma(8)],
        cid=4, ticks=True,
        jobs=[SecondThird(*second1, tick_at=1), SecondThird(*first2[:4], slots[0], slots[2], *first2[4:], start_at=1, tick_at=2),
              FirstSecond(*slots_p, start_at=1, tick_at=2), ThirdSum(*result0), GoHome(out_rows, tick_at=2)],
        flops=30e9, nbytes=9e6,
    )
    dqkv, *second_q, even_sums = own
    final1, final2, (sent_p, kept_p), final0, (output,) = given
    width = ada_cols + LANES
    (grad_rows, gq, gp, g1, g2, grad_ada_weight, grad_ada_bias, line), _ = call(
        end_kernel, "end",
        (sds((2, LB, D), bf16), sds((DC, 3 * TD), f32), sds((DC, TD), f32), sds((DC, FF // 4), f32),
         sds((FF // 8, TD), f32), sds((DC, ada_cols), f32), sds((1, ada_cols // 2), f32), sds((8, LANES), f32)),
        (dqkv, shifted, even_sums, sum1, sum2, sum_attn, wq, d_resid, tok, mod, sums_mid, *final0, *final1, *final2, sent_p,
         kept_p, freq.reshape(4, 1, DC), *second_q),
        in_specs=[ANY] * 2 + [vmem] * 4 + [ANY] * 3 + [vmem] * 2 + [ANY] * 8 + [vmem] + [ANY] * 6,
        out_specs=[ANY, vmem] + [ANY] * 4 + [vmem] * 2,
        scratch=[vm(L, 3 * WC), vm(L, D), vm(4, 4, 8, LANES, dtype=f32), vm(4, 4, TQ, DZ, dtype=f32)]
        + [slot_q] * 6 + [fourth] * 4 + [vm(3, QR, LANES), vm(QR, LANES, dtype=f32), vm(3, QR, LANES)]
        + [fourth] * 6 + [vm(3, QR, LANES), vm(QR, LANES, dtype=f32), vm(3, QR, LANES)]
        + [vm(2, DZ, TQ, dtype=f32), vm(D, 3 * WC), vm(LH, D, dtype=f32), vm(LH, D),
           vm(NF, G1R + G2R, LANES, dtype=f32)] + [vm(2, LB, D)] * 3
        + [vm(8, D, dtype=f32)] * 2 + [vm(4, 1, width, dtype=f32)] * 2
        + [vm(4, 4, 1, width, dtype=f32), vm(1, 1, ada_cols, dtype=f32), vm(4, 1, ada_cols, dtype=f32)]
        + [vm(NF * G1R, LANES)] * 2 + [vm(2, DC, TQ)] * 2 + [vm(PR, LANES, dtype=f32), vm(3, PR, LANES)]
        + [vm(*v, dtype=f32) for v in ((DC, TD), (DC, FF // 4), (FF // 8, TD), (DC, ada_cols))]
        + [dma(2, 9), dma(2, 5), dma(2, 6), dma(2, 2), dma(2, 9), dma(2, 3), dma(23), dma(4)],
        peers=("c", "t0", "t1", "x", "y", "xy", "z1", "z2", "z3"), cid=5,
        flops=4 * L * D * 3 * WC, nbytes=30e6,
    )
    thin = lambda height, width: pl.BlockSpec((height, width), lambda i: (i, 0))
    tokens_spec = pl.BlockSpec((2, LB // 2, D), lambda i: (0, i, 0))
    ends = [thin(DC // 2, 3 * TD), thin(DC // 2, TD), thin(DC // 2, FF // 4)]
    bias_cols = ada_cols // 2
    finals, _ = call(
        final_kernel, "final",
        (sds((2, LB, D), bf16), sds((2, LB, D), f32), sds((DC, 3 * TD), f32), sds((DC, TD), f32), sds((DC, FF // 4), f32),
         sds((TD, FF // 8), f32), sds((DC, ada_cols), f32), sds((bias_cols,), f32), sds((FF // 32,), f32))
        + (sds((D // 32,), f32),) * 4,
        (output, grad_rows, gq, gp, g1, g2, grad_ada_weight, grad_ada_bias, line),
        grid=(2,),
        in_specs=[tokens_spec, tokens_spec, *ends, full((FF // 8, TD)), thin(DC // 2, ada_cols), full((1, bias_cols)),
                  full((8, LANES))],
        out_specs=[tokens_spec, tokens_spec, *ends, full((TD, FF // 8)), thin(DC // 2, ada_cols), full((bias_cols,)),
                   full((FF // 32,))] + [full((D // 32,))] * 4,
    )
    output, grad_tokens, gq, gp, g1, g2, g_ada, ada_b, b_fc1, b_fc2, b_proj, b_q, b_v = finals
    return (output, grad_tokens, gq, b_q, b_v, gp, b_proj, g1, b_fc1, g2.T, b_fc2, g_ada, ada_b)


def gelu_tanh(values):
    return jax.nn.gelu(values, approximate=True)


def split_heads(key_value, model_width, head_dim):
    item_count, length = (key_value.shape[0], key_value.shape[1])
    key_rows = key_value[:, :, :model_width].reshape(
        item_count, length, model_width // head_dim, head_dim
    )
    value_rows = key_value[:, :, model_width:].reshape(
        item_count, length, model_width // head_dim, head_dim
    )
    return (key_rows, value_rows)


def scores_of(queries, key_rows, score_scale):
    return (
        jnp.einsum("nqhe,nkhe->nhqk", queries, key_rows, preferred_element_type=jnp.float32)
        * score_scale
    )


def to_blocks(values, per_step):
    return values.reshape((values.shape[0] // per_step, per_step) + values.shape[1:])


def from_blocks(values):
    return values.reshape((values.shape[0] * values.shape[1],) + values.shape[2:])


def on_device(
    tokens,
    cotangent,
    timesteps,
    bucket_ids,
    head_masks,
    channel_masks,
    skip_rows,
    w_qkv,
    q_bias,
    v_bias,
    w_proj,
    proj_bias,
    w_fc1,
    fc1_bias,
    w_fc2,
    fc2_bias,
    ada_weight,
    ada_bias,
):
    item_count, local_len, model_width = tokens.shape
    row_count = item_count * local_len
    head_dim = model_width // HEADS
    score_scale = 1.0 / math.sqrt(head_dim)
    hidden_width = w_fc1.shape[1]
    ada_cols = ada_weight.shape[1]
    tok_index = lax.axis_index("tok")
    per_step = 1
    for candidate in range(1, item_count + 1):
        per_step = candidate
    condition = jax.nn.silu(step_embedding(timesteps, model_width)).astype(jnp.bfloat16)
    mod_local = jnp.dot(
        condition, ada_weight, preferred_element_type=jnp.float32
    ) + ada_bias.astype(jnp.float32)
    modulation = lax.all_gather(mod_local, "tok", axis=1, tiled=True)
    pieces = modulation.reshape(item_count, 6, 1, model_width)
    shift_a = pieces[:, 0]
    scale_a = pieces[:, 1]
    gate_a = pieces[:, 2]
    shift_m = pieces[:, 3]
    scale_m = pieces[:, 4]
    gate_m = pieces[:, 5]
    chosen = (jnp.arange(head_masks.shape[0], dtype=jnp.int32) == bucket_ids[0]).astype(jnp.float32)
    head_on = jnp.sum(chosen[:, None] * head_masks.astype(jnp.float32), axis=0)
    group_on = jnp.sum(chosen[:, None] * channel_masks.astype(jnp.float32), axis=0)
    channel_on = jnp.repeat(group_on, hidden_width // group_on.shape[0])
    positions = tok_index * local_len + jnp.arange(local_len, dtype=jnp.int32)
    skipped = jnp.any(skip_rows[:, :, None] == positions[None, None, :], axis=1)
    kept_rows = 1.0 - skipped.astype(jnp.float32)
    inputs = tokens.astype(jnp.float32)
    normed, inverse = normalize(inputs)
    shifted = (
        (normed * (1.0 + scale_a) + shift_a).astype(jnp.bfloat16).reshape(row_count, model_width)
    )
    qkv_bias = jnp.concatenate([q_bias, jnp.zeros_like(q_bias), v_bias]).astype(jnp.float32)
    projected = (jnp.dot(shifted, w_qkv, preferred_element_type=jnp.float32) + qkv_bias).astype(
        jnp.bfloat16
    )
    projected = projected.reshape(item_count, local_len, 3 * model_width)
    queries = projected[:, :, :model_width].reshape(item_count, local_len, HEADS, head_dim)
    key_value = projected[:, :, model_width:]
    all_kv = lax.all_gather(key_value, "tok", axis=1, tiled=True)

    def forward_block(packed):
        query_block, kv_block = packed
        key_rows, value_rows = split_heads(kv_block, model_width, head_dim)
        scores = scores_of(query_block, key_rows, score_scale)
        top_score = jnp.max(scores, axis=-1, keepdims=True)
        expanded = jnp.exp(scores - top_score)
        totals = jnp.sum(expanded, axis=-1, keepdims=True)
        weights_low = (expanded / totals).astype(jnp.bfloat16)
        head_out = (
            jnp.einsum(
                "nhqk,nkhe->nqhe", weights_low, value_rows, preferred_element_type=jnp.float32
            )
            * head_on[:, None]
        )
        return (head_out.astype(jnp.bfloat16), top_score + jnp.log(totals))

    mixed_heads, log_total = lax.map(
        forward_block, (to_blocks(queries, per_step), to_blocks(all_kv, per_step))
    )
    log_total = from_blocks(log_total)
    mixed = from_blocks(mixed_heads).reshape(row_count, model_width)
    attn = (
        jnp.dot(mixed, w_proj, preferred_element_type=jnp.float32) + proj_bias.astype(jnp.float32)
    ).reshape(item_count, local_len, model_width)
    resid = inputs + gate_a * attn
    normed2, inverse2 = normalize(resid)
    shifted2 = (
        (normed2 * (1.0 + scale_m) + shift_m).astype(jnp.bfloat16).reshape(row_count, model_width)
    )
    pre = jnp.dot(shifted2, w_fc1, preferred_element_type=jnp.float32) + fc1_bias.astype(
        jnp.float32
    )
    activated, gelu_pull = jax.vjp(gelu_tanh, pre)
    hidden = (activated * channel_on).astype(jnp.bfloat16)
    branch = (
        jnp.dot(hidden, w_fc2, preferred_element_type=jnp.float32) + fc2_bias.astype(jnp.float32)
    ).reshape(item_count, local_len, model_width)
    gated = kept_rows[:, :, None] * gate_m
    output = (resid + gated * branch).astype(jnp.bfloat16)
    incoming = cotangent.astype(jnp.float32)
    d_gate_m = jnp.sum(kept_rows[:, :, None] * branch * incoming, axis=1)
    d_branch = (gated * incoming).astype(jnp.bfloat16).reshape(row_count, model_width)
    grad_w_fc2 = jnp.dot(hidden.T, d_branch, preferred_element_type=jnp.float32)
    grad_fc2_bias = jnp.sum(d_branch.astype(jnp.float32), axis=0)
    d_hidden = jnp.dot(d_branch, w_fc2.T, preferred_element_type=jnp.float32)
    d_pre = gelu_pull(d_hidden * channel_on)[0].astype(jnp.bfloat16)
    grad_w_fc1 = jnp.dot(shifted2.T, d_pre, preferred_element_type=jnp.float32)
    grad_fc1_bias = jnp.sum(d_pre.astype(jnp.float32), axis=0)
    d_shifted2 = jnp.dot(d_pre, w_fc1.T, preferred_element_type=jnp.float32).reshape(
        item_count, local_len, model_width
    )
    d_shift_m = jnp.sum(d_shifted2, axis=1)
    d_scale_m = jnp.sum(d_shifted2 * normed2, axis=1)
    d_resid = incoming + normalize_back(d_shifted2 * (1.0 + scale_m), normed2, inverse2)
    d_gate_a = jnp.sum(attn * d_resid, axis=1)
    d_attn = (gate_a * d_resid).astype(jnp.bfloat16).reshape(row_count, model_width)
    grad_w_proj = jnp.dot(mixed.T, d_attn, preferred_element_type=jnp.float32)
    grad_proj_bias = jnp.sum(d_attn.astype(jnp.float32), axis=0)
    d_mixed = jnp.dot(d_attn, w_proj.T, preferred_element_type=jnp.float32).astype(jnp.bfloat16)
    d_heads = d_mixed.reshape(item_count, local_len, HEADS, head_dim) * head_on[:, None].astype(
        jnp.bfloat16
    )
    again_kv = lax.all_gather(key_value, "tok", axis=1, tiled=True)

    def backward_block(packed):
        query_block, kv_block, head_grads, totals_log = packed
        key_rows, value_rows = split_heads(kv_block, model_width, head_dim)
        scores = scores_of(query_block, key_rows, score_scale)
        probs = jnp.exp(scores - totals_log)
        d_probs = jnp.einsum(
            "nqhe,nkhe->nhqk", head_grads, value_rows, preferred_element_type=jnp.float32
        )
        row_dot = jnp.sum(probs * d_probs, axis=-1, keepdims=True)
        d_scores = (probs * (d_probs - row_dot)).astype(jnp.bfloat16)
        d_queries = (
            jnp.einsum("nhqk,nkhe->nqhe", d_scores, key_rows, preferred_element_type=jnp.float32)
            * score_scale
        )
        return (d_queries, row_dot)

    mapped = lax.map(
        backward_block,
        (
            to_blocks(queries, per_step),
            to_blocks(again_kv, per_step),
            to_blocks(d_heads, per_step),
            to_blocks(log_total, per_step),
        ),
    )
    d_queries = from_blocks(mapped[0])
    row_dot = from_blocks(mapped[1])
    queries_all, head_grads_all = (
        lax.all_gather(queries, "tok", axis=1, tiled=True),
        lax.all_gather(d_heads, "tok", axis=1, tiled=True),
    )
    totals_all, row_dot_all = (
        lax.all_gather(log_total, "tok", axis=2, tiled=True),
        lax.all_gather(row_dot, "tok", axis=2, tiled=True),
    )

    def key_block(packed):
        kv_block, query_block, head_grads, totals_log, dots = packed
        key_rows, value_rows = split_heads(kv_block, model_width, head_dim)
        scores = (
            jnp.einsum("nkhe,nqhe->nhkq", key_rows, query_block, preferred_element_type=jnp.float32)
            * score_scale
        )
        probs = jnp.exp(scores - totals_log[:, :, None, :, 0])
        d_probs = jnp.einsum(
            "nkhe,nqhe->nhkq", value_rows, head_grads, preferred_element_type=jnp.float32
        )
        d_scores = (probs * (d_probs - dots[:, :, None, :, 0])).astype(jnp.bfloat16)
        d_keys = (
            jnp.einsum("nhkq,nqhe->nkhe", d_scores, query_block, preferred_element_type=jnp.float32)
            * score_scale
        )
        d_values = jnp.einsum(
            "nhkq,nqhe->nkhe",
            probs.astype(jnp.bfloat16),
            head_grads,
            preferred_element_type=jnp.float32,
        )
        return jnp.concatenate(
            [
                d_keys.reshape(d_keys.shape[0], local_len, model_width),
                d_values.reshape(d_values.shape[0], local_len, model_width),
            ],
            axis=2,
        )

    d_kv = from_blocks(
        lax.map(
            key_block,
            (
                to_blocks(key_value, per_step),
                to_blocks(queries_all, per_step),
                to_blocks(head_grads_all, per_step),
                to_blocks(totals_all, per_step),
                to_blocks(row_dot_all, per_step),
            ),
        )
    )
    d_qkv = jnp.concatenate([d_queries.reshape(item_count, local_len, model_width), d_kv], axis=2)
    d_qkv = d_qkv.astype(jnp.bfloat16).reshape(row_count, 3 * model_width)
    grad_w_qkv = jnp.dot(shifted.T, d_qkv, preferred_element_type=jnp.float32)
    qkv_sums = jnp.sum(d_qkv.astype(jnp.float32), axis=0)
    grad_q_bias = qkv_sums[:model_width]
    grad_v_bias = qkv_sums[2 * model_width :]
    d_shifted = jnp.dot(d_qkv, w_qkv.T, preferred_element_type=jnp.float32).reshape(
        item_count, local_len, model_width
    )
    d_shift_a = jnp.sum(d_shifted, axis=1)
    d_scale_a = jnp.sum(d_shifted * normed, axis=1)
    grad_tokens = d_resid + normalize_back(d_shifted * (1.0 + scale_a), normed, inverse)
    d_modulation = jnp.concatenate(
        [d_shift_a, d_scale_a, d_gate_a, d_shift_m, d_scale_m, d_gate_m], axis=1
    )
    d_modulation = lax.psum(d_modulation, "tok")
    mod_columns = lax.dynamic_slice_in_dim(d_modulation, tok_index * ada_cols, ada_cols, 1)
    grad_ada_weight = jnp.dot(
        condition.astype(jnp.float32).T, mod_columns, precision=lax.Precision.HIGHEST
    )
    grad_ada_bias = jnp.sum(d_modulation, axis=0)
    bucket_done = (
        lax.psum_scatter(grad_w_qkv, "bucket", scatter_dimension=0, tiled=True),
        lax.psum_scatter(grad_w_proj, "bucket", scatter_dimension=0, tiled=True),
        lax.psum_scatter(grad_w_fc1, "bucket", scatter_dimension=0, tiled=True),
        lax.psum_scatter(grad_w_fc2, "bucket", scatter_dimension=0, tiled=True),
        lax.psum_scatter(grad_q_bias, "bucket", scatter_dimension=0, tiled=True),
        lax.psum_scatter(grad_v_bias, "bucket", scatter_dimension=0, tiled=True),
        lax.psum_scatter(grad_proj_bias, "bucket", scatter_dimension=0, tiled=True),
        lax.psum_scatter(grad_fc1_bias, "bucket", scatter_dimension=0, tiled=True),
        lax.psum_scatter(grad_fc2_bias, "bucket", scatter_dimension=0, tiled=True),
        lax.psum_scatter(grad_ada_weight, "bucket", scatter_dimension=0, tiled=True),
        lax.psum_scatter(grad_ada_bias, "bucket", scatter_dimension=0, tiled=True),
    )
    token_done = (
        lax.psum_scatter(bucket_done[0], "tok", scatter_dimension=1, tiled=True),
        lax.psum_scatter(bucket_done[1], "tok", scatter_dimension=1, tiled=True),
        lax.psum_scatter(bucket_done[2], "tok", scatter_dimension=1, tiled=True),
        lax.psum_scatter(bucket_done[3], "tok", scatter_dimension=1, tiled=True),
        lax.psum_scatter(bucket_done[4].reshape(1, -1), "tok", scatter_dimension=1, tiled=True),
        lax.psum_scatter(bucket_done[5].reshape(1, -1), "tok", scatter_dimension=1, tiled=True),
        lax.psum_scatter(bucket_done[6].reshape(1, -1), "tok", scatter_dimension=1, tiled=True),
        lax.psum_scatter(bucket_done[7].reshape(1, -1), "tok", scatter_dimension=1, tiled=True),
        lax.psum_scatter(bucket_done[8].reshape(1, -1), "tok", scatter_dimension=1, tiled=True),
    )
    finished = (
        token_done[0],
        token_done[1],
        token_done[2],
        token_done[3],
        token_done[4],
        token_done[5],
        token_done[6],
        token_done[7],
        token_done[8],
        bucket_done[9],
        bucket_done[10],
    )
    return (
        output,
        grad_tokens,
        finished[0],
        finished[4].reshape(-1),
        finished[5].reshape(-1),
        finished[1],
        finished[6].reshape(-1),
        finished[2],
        finished[7].reshape(-1),
        finished[3],
        finished[8].reshape(-1),
        finished[9],
        finished[10],
    )


def solution(mesh):
    planned = mesh.shape["tok"] == 4 and mesh.shape["bucket"] == 8
    return jax.shard_map(
        one_item_per_chip if planned else on_device,
        mesh=mesh,
        in_specs=(
            P("bucket", "tok", None),
            P("bucket", "tok", None),
            P("bucket"),
            P("bucket"),
            P(),
            P(),
            P("bucket", None),
            P(),
            P(),
            P(),
            P(),
            P(),
            P(),
            P(),
            P(),
            P(),
            P(None, "tok"),
            P("tok"),
        ),
        out_specs=(
            P("bucket", "tok", None),
            P("bucket", "tok", None),
            P("bucket", "tok"),
            P(("bucket", "tok")),
            P(("bucket", "tok")),
            P("bucket", "tok"),
            P(("bucket", "tok")),
            P("bucket", "tok"),
            P(("bucket", "tok")),
            P("bucket", "tok"),
            P(("bucket", "tok")),
            P("bucket", "tok"),
            P("bucket"),
        ),
        check_vma=False,
    )
```
